32 devices in a mesh: row: 8 (over z, core), col: 4 (over y, x).
Axes of the slice: x: 2, y: 2, z: 4, core: 2. Of those that a mesh axis runs over, the one named last changes fastest.
Arguments:
- tokens_in: bfloat16 [8192, 2048], P(('row', 'col')), may hold values from -6 to 6
- cotangent: bfloat16 [8192, 2048], P(('row', 'col')), may hold values from -6 to 6
- target: int32 [8192], P(('row', 'col')), may hold values from 0 to 8191, as said below
- sequence_lengths: int32 [8, 2], P('row'), may hold values from 341 to 683, as said below
- sequence_adapter: int32 [8, 2], P('row'), may hold values from 0 to 7, as said below
- norm_gains: bfloat16 [2, 2048], replicated, may hold values from 0.5 to 1.5
- weight_in: bfloat16 [2048, 8240], P('row', 'col'), may hold values from -0.125 to 0.125
- conv_values: bfloat16 [5, 3072], P(None, 'col'), may hold values from -3 to 3
- conv_states: bfloat16 [5, 512], P(None, 'col'), may hold values from -3 to 3
- scan_params: float32 [3, 48], P(None, 'col'), may hold values from -4 to 2.8
- weight_mix: bfloat16 [4096, 2048], P('col', 'row'), may hold values from -3 to 3
- weight_feed: bfloat16 [2048, 8192], P('row', 'col'), may hold values from -0.125 to 0.125
- weight_down: bfloat16 [4096, 2048], P('col', 'row'), may hold values from -0.09375 to 0.09375
- in_lower: bfloat16 [2048, 128], P('row'), may hold values from -0.125 to 0.125
- in_raise: bfloat16 [128, 8240], P('row', 'col'), may hold values from -0.75 to 0.75
- mix_lower: bfloat16 [4096, 128], P('col', 'row'), may hold values from -0.001953125 to 0.001953125
- mix_raise: bfloat16 [128, 2048], P(None, 'row'), may hold values from -0.75 to 0.75
- feed_lower: bfloat16 [2048, 128], P('row'), may hold values from -0.125 to 0.125
- feed_raise: bfloat16 [128, 8192], P('row', 'col'), may hold values from -0.75 to 0.75
- down_lower: bfloat16 [4096, 128], P('col', 'row'), may hold values from -0.09375 to 0.09375
- down_raise: bfloat16 [128, 2048], P(None, 'row'), may hold values from -0.75 to 0.75
Outputs:
- block_out: bfloat16 [8192, 2048], P(('row', 'col'))
- input_grad: bfloat16 [8192, 2048], P(('row', 'col'))
- grad_in_lower: float32 [2048, 128], P(('row', 'col'))
- grad_in_raise: float32 [128, 8240], P('row', 'col')
- grad_mix_lower: float32 [4096, 128], P('col', 'row')
- grad_mix_raise: float32 [128, 2048], P(None, ('row', 'col'))
- grad_feed_lower: float32 [2048, 128], P(('row', 'col'))
- grad_feed_raise: float32 [128, 8192], P('row', 'col')
- grad_down_lower: float32 [4096, 128], P('col', 'row')
- grad_down_raise: float32 [128, 2048], P(None, ('row', 'col'))
The draws below stay inside these ranges and needn't reach their ends.
Inputs may be any that keep to these rules, and one draw needn't show every extreme that they name: `target`: A permutation of the packed positions; packed position p lies on device p // 256; the 256 rows of one device go to every device in equal shares of 8 rows. `sequence_lengths`: each row sums to 1024. `sequence_adapter`: neighbouring sequences of a group use different adapters; every adapter is that of the first sequence of some group.
All inputs are finite; a program needn't handle non-finite values.
Results may differ from the reference program's by a relative error of at most 0.024.
Values may be sent and summed in bfloat16 or wider, within the bound.
No kernel may reach another device: no remote copies, remote signals or barrier semaphores. Data moves between devices by JAX's collectives and lax.ppermute only.
A program may use at most 256 MiB of HBM per device.

```python
import math
import jax
import jax.numpy as jnp
from jax import lax

D = 2048
NH = 48
HP = 64
NSTATE = 256
KCONV = 4
QUERY_HEADS = 8
KEY_VALUE_HEADS = 2
HEAD_SIZE = 128
FF = 4096
RANK = 16
NADAPT = 8
TOK_DEV = 256
SSD_BLOCK = 256
ATT_BLOCK = 512
DSSM = 3072
UNIT_IN = 1030
UNIT_OUT = 512
UNIT_FF = 512
PROJ_IN = 8240
PROJ_OUT = 4096
ADAPT_COLS = 128
GROUP = 1024
GROUPS = 8
SEQS = 2
LEAST = 341
TOKENS = 8192
PEER_ROWS = 8


def draw_target(key, part):
    base_key = jax.random.fold_in(key, 7)
    source_key, dest_key = jax.random.split(base_key)
    device_count = TOKENS // TOK_DEV
    source_order = jax.vmap(lambda sub_key: jax.random.permutation(sub_key, TOK_DEV))(jax.random.split(source_key, device_count))
    dest_order = jax.vmap(lambda sub_key: jax.random.permutation(sub_key, TOK_DEV))(jax.random.split(dest_key, device_count))
    rank_index = jnp.arange(TOK_DEV, dtype=jnp.int32)
    dest_device = rank_index // PEER_ROWS
    slot_index = jnp.arange(device_count, dtype=jnp.int32)[:, None] * PEER_ROWS + (rank_index % PEER_ROWS)[None, :]
    final_slot = dest_order[jnp.broadcast_to(dest_device[None, :], slot_index.shape), slot_index]
    packed = (dest_device[None, :] * TOK_DEV + final_slot).astype(jnp.int32)
    row_index = jnp.broadcast_to(jnp.arange(device_count, dtype=jnp.int32)[:, None], (device_count, TOK_DEV))
    target = jnp.zeros((device_count, TOK_DEV), jnp.int32).at[row_index, source_order].set(packed)
    return target.reshape(TOKENS)


def draw_sequence_lengths(key, part):
    spare_tokens = GROUP - SEQS * LEAST
    cut_points = jax.random.randint(jax.random.fold_in(key, 3), (GROUPS, SEQS - 1), 0, spare_tokens + 1)
    cut_points = jnp.sort(cut_points, axis=1).astype(jnp.int32)
    extreme_group = jax.random.randint(jax.random.fold_in(key, 4), (), 0, GROUPS)
    extreme_cut = (jax.random.randint(jax.random.fold_in(key, 6), (), 0, 2) * spare_tokens).astype(jnp.int32)
    group_index = jnp.arange(GROUPS, dtype=jnp.int32)[:, None]
    cut_points = jnp.where(group_index == extreme_group, extreme_cut, cut_points).astype(jnp.int32)
    edge_points = jnp.concatenate([jnp.zeros((GROUPS, 1), jnp.int32), cut_points, jnp.full((GROUPS, 1), spare_tokens, jnp.int32)], axis=1)
    return (LEAST + edge_points[:, 1:] - edge_points[:, :-1]).astype(jnp.int32)


def draw_sequence_adapter(key, part):
    first_key, step_key = jax.random.split(jax.random.fold_in(key, 11))
    first_choice = (jax.random.permutation(first_key, GROUPS) % NADAPT).astype(jnp.int32)[:, None]
    step_choice = jax.random.randint(step_key, (GROUPS, SEQS - 1), 1, NADAPT).astype(jnp.int32)
    running = jnp.cumsum(jnp.concatenate([first_choice, step_choice], axis=1), axis=1)
    return (running % NADAPT).astype(jnp.int32)


def draw_scan_params(key, part):
    key_list = jax.random.split(jax.random.fold_in(key, 5), 3)
    step_bias = jax.random.uniform(key_list[0], (NH,), jnp.float32, -3.5, 0.5)
    rate_log = jax.random.uniform(key_list[1], (NH,), jnp.float32, -3.0, 2.8)
    skip_gain = jax.random.uniform(key_list[2], (NH,), jnp.float32, 0.5, 1.5)
    return jnp.stack([step_bias, rate_log, skip_gain])


def draw_weight_mix(key, part):
    noise_draw = jax.random.normal(jax.random.fold_in(key, 9), (PROJ_OUT, D), jnp.float32)
    row_index = jnp.arange(PROJ_OUT, dtype=jnp.int32) % UNIT_OUT
    scan_scale = 0.16 * 16.0 / (NSTATE * math.sqrt(DSSM))
    attend_scale = 6.0 / math.sqrt(QUERY_HEADS * HEAD_SIZE)
    row_scale = jnp.where(row_index < DSSM // QUERY_HEADS, scan_scale, attend_scale)
    return jnp.clip(noise_draw * row_scale[:, None], -3.0, 3.0).astype(jnp.bfloat16)


def shard_levels(key, dims, shards, least, high):
    level, own = 1.0, jax.random.fold_in(key, 6)
    for axis_at, blocks in shards:
        heights = jnp.exp(jax.random.uniform(jax.random.fold_in(own, axis_at), (blocks,), jnp.float32, least / len(shards), high / len(shards)))
        level = level * jnp.repeat(heights, dims[axis_at] // blocks).reshape([-1 if axis == axis_at else 1 for axis in range(len(dims))])
    return level


def noise(rng, shape, width, reach, shards=(), held_as=jnp.bfloat16):
    drawn = width * jax.random.normal(rng, shape, jnp.float32)
    if shards:
        drawn = drawn * shard_levels(rng, shape, shards, -0.22, 0.18)
    return jnp.clip(drawn, -reach, reach).astype(held_as)


def setup_inputs(seed: int = 0) -> dict:
    streams_of = jax.random.split(jax.random.key(seed), 22)
    tokens_in = noise(streams_of[0], (TOKENS, D), 1.0, 6.0, ((0, 32),))
    cotangent = noise(streams_of[1], (TOKENS, D), 1.0, 6.0, ((0, 32),))
    target = draw_target(jax.random.fold_in(streams_of[21], 71), 0)
    sequence_lengths = draw_sequence_lengths(jax.random.fold_in(streams_of[21], 71), 0)
    sequence_adapter = draw_sequence_adapter(jax.random.fold_in(streams_of[21], 71), 0)
    norm_gains = jnp.clip(1.0 + 0.1 * jax.random.normal(streams_of[5], (2, D), jnp.float32), 0.5, 1.5).astype(jnp.bfloat16)
    weight_in = noise(streams_of[6], (D, PROJ_IN), D ** -0.5, 0.125, ((0, 8), (1, 4)))
    conv_values = noise(streams_of[7], (KCONV + 1, DSSM), 0.5, 3.0, ((1, 4),))
    conv_states = noise(streams_of[8], (KCONV + 1, 2 * NSTATE), 0.5, 3.0, ((1, 4),))
    scan_params = draw_scan_params(jax.random.fold_in(streams_of[21], 71), 0)
    weight_mix = draw_weight_mix(jax.random.fold_in(streams_of[21], 71), 0)
    weight_feed = noise(streams_of[11], (D, 2 * FF), D ** -0.5, 0.125, ((0, 8), (1, 4)))
    weight_down = noise(streams_of[12], (FF, D), FF ** -0.5, 0.09375, ((0, 4), (1, 8)))
    in_lower = noise(streams_of[13], (D, ADAPT_COLS), D ** -0.5, 0.125, ((0, 8),))
    in_raise = noise(streams_of[14], (ADAPT_COLS, PROJ_IN), (4 * RANK) ** -0.5, 0.75, ((0, 8), (1, 4)))
    mix_lower = noise(streams_of[15], (PROJ_OUT, ADAPT_COLS), (PROJ_OUT * NSTATE * 8) ** -0.5, 0.001953125, ((0, 4), (1, 8)))
    mix_raise = noise(streams_of[16], (ADAPT_COLS, D), (4 * RANK) ** -0.5, 0.75, ((1, 8),))
    feed_lower = noise(streams_of[17], (D, ADAPT_COLS), D ** -0.5, 0.125, ((0, 8),))
    feed_raise = noise(streams_of[18], (ADAPT_COLS, 2 * FF), (4 * RANK) ** -0.5, 0.75, ((0, 8), (1, 4)))
    down_lower = noise(streams_of[19], (FF, ADAPT_COLS), FF ** -0.5, 0.09375, ((0, 4), (1, 8)))
    down_raise = noise(streams_of[20], (ADAPT_COLS, D), (4 * RANK) ** -0.5, 0.75, ((1, 8),))
    return dict(tokens_in=tokens_in, cotangent=cotangent, target=target, sequence_lengths=sequence_lengths, sequence_adapter=sequence_adapter, norm_gains=norm_gains, weight_in=weight_in, conv_values=conv_values, conv_states=conv_states, scan_params=scan_params, weight_mix=weight_mix, weight_feed=weight_feed, weight_down=weight_down, in_lower=in_lower, in_raise=in_raise, mix_lower=mix_lower, mix_raise=mix_raise, feed_lower=feed_lower, feed_raise=feed_raise, down_lower=down_lower, down_raise=down_raise)


EPSILON = 1e-05
ROPE_BASE = 10000.0
NEGATIVE = -1e+30
PRECISE = lax.Precision.HIGHEST

@jax.custom_vjp
def low(v):
    return lax.optimization_barrier(v.astype(jnp.bfloat16)).astype(jnp.float32)

@jax.custom_vjp
def low_back(v):
    return v

def low_keep(v):
    return (low(v), None)

def low_pass(kept, grad):
    return (grad,)

def back_keep(v):
    return (v, None)

def back_low(kept, grad):
    return (low(grad),)
low.defvjp(low_keep, low_pass)
low_back.defvjp(back_keep, back_low)

def matmul(left, right):
    return jnp.dot(left, right, precision=PRECISE)

def rms_norm(values, gain):
    return values * lax.rsqrt(lax.optimization_barrier(jnp.mean(values * values, axis=-1, keepdims=True)) + EPSILON) * gain

def sequence_tables(lengths, adapters, sequence_length):
    sequence_count = lengths.shape[0]
    boundary = jnp.cumsum(lengths).astype(jnp.int32)
    token_index = jnp.arange(sequence_length, dtype=jnp.int32)
    passed = (token_index[:, None] >= boundary[None, :]).astype(jnp.int32)
    segment = lax.optimization_barrier(jnp.sum(passed, axis=1)).astype(jnp.int32)
    segment_start = lax.optimization_barrier(jnp.sum(passed * lengths[None, :], axis=1)).astype(jnp.int32)
    position = (token_index - segment_start).astype(jnp.int32)
    member = (segment[:, None] == jnp.arange(sequence_count, dtype=jnp.int32)[None, :]).astype(jnp.int32)
    chosen = lax.optimization_barrier(jnp.sum(member * adapters[None, :], axis=1)).astype(jnp.int32)
    column = (jnp.arange(NADAPT * RANK, dtype=jnp.int32) // RANK).astype(jnp.int32)
    selector = (chosen[:, None] == column[None, :]).astype(jnp.float32)
    return (segment, position, selector)

def causal_conv(channels, tap_table, position):
    running = tap_table[KCONV] + channels * tap_table[0]
    for lag_step in range(1, KCONV):
        shifted = jnp.concatenate([jnp.zeros((lag_step, channels.shape[1]), jnp.float32), channels[:-lag_step]], axis=0)
        running = running + jnp.where((position >= lag_step)[:, None], shifted, 0.0) * tap_table[lag_step]
    return jax.nn.silu(running)

def rotate(vectors, position):
    half_width = HEAD_SIZE // 2
    frequency = ROPE_BASE ** (-2.0 * jnp.arange(half_width, dtype=jnp.float32) / HEAD_SIZE)
    angle_table = position.astype(jnp.float32)[:, None] * frequency[None, :]
    cosine = jnp.cos(angle_table)[:, None, :]
    sine_part = jnp.sin(angle_table)[:, None, :]
    leading = vectors[..., :half_width]
    trailing = vectors[..., half_width:]
    return jnp.concatenate([leading * cosine - trailing * sine_part, trailing * cosine + leading * sine_part], axis=-1)

def state_scan(inputs, step_size, log_decay, write_vectors, read_vectors, segment):
    sequence_length, head_count = step_size.shape
    block_count = sequence_length // SSD_BLOCK
    previous = jnp.concatenate([jnp.full((1,), -1, jnp.int32), segment[:-1]])
    first_previous = previous.reshape(block_count, SSD_BLOCK)[:, 0]
    inner_index = jnp.arange(SSD_BLOCK, dtype=jnp.int32)
    lower_mask = inner_index[:, None] >= inner_index[None, :]

    def scan_step(carry_state, block_data):
        block_inputs, block_steps, block_decay, block_write, block_read, block_segment, block_previous = block_data
        cumulative = jnp.cumsum(block_decay, axis=0)
        intersection = jnp.dot(block_read, block_write.T, precision=PRECISE)
        allowed = lower_mask & (block_segment[:, None] == block_segment[None, :])
        difference = cumulative[:, None, :] - cumulative[None, :, :]
        decay_table = jnp.exp(jnp.where(allowed[:, :, None], difference, NEGATIVE))
        weights = low(intersection[:, :, None] * decay_table * block_steps[None, :, :])
        within = jnp.einsum('tsh,shp->thp', weights, block_inputs, precision=PRECISE)
        carried = (block_segment == block_previous).astype(jnp.float32)
        read_scaled = low(block_read[:, None, :] * (jnp.exp(cumulative) * carried[:, None])[:, :, None])
        across = jnp.einsum('thn,hpn->thp', read_scaled, low(carry_state), precision=PRECISE)
        tail_factor = jnp.exp(cumulative[-1][None, :] - cumulative) * block_steps * (block_segment == block_segment[-1]).astype(jnp.float32)[:, None]
        write_scaled = low(block_write[:, None, :] * tail_factor[:, :, None])
        fresh_state = jnp.einsum('shp,shn->hpn', block_inputs, write_scaled, precision=PRECISE)
        through = jnp.exp(cumulative[-1]) * (block_segment[-1] == block_previous).astype(jnp.float32)
        return (carry_state * through[:, None, None] + fresh_state, within + across)
    sliced = (inputs.reshape(block_count, SSD_BLOCK, head_count, HP), step_size.reshape(block_count, SSD_BLOCK, head_count), log_decay.reshape(block_count, SSD_BLOCK, head_count), write_vectors.reshape(block_count, SSD_BLOCK, NSTATE), read_vectors.reshape(block_count, SSD_BLOCK, NSTATE), segment.reshape(block_count, SSD_BLOCK), first_previous)
    zero_state = jnp.zeros((head_count, HP, NSTATE), jnp.float32)
    _, outputs = lax.scan(jax.checkpoint(scan_step), zero_state, sliced)
    return outputs.reshape(sequence_length, head_count, HP)

def attention(query, key_rows, value_rows, segment):
    sequence_length, unit_count = (query.shape[0], query.shape[1])
    block_count = sequence_length // ATT_BLOCK
    token_index = jnp.arange(sequence_length, dtype=jnp.int32)
    score_scale = 1.0 / math.sqrt(HEAD_SIZE)

    def score_block(block_data):
        query_block, segment_block, token_block = block_data
        score = jnp.einsum('qud,kud->uqk', query_block, key_rows, precision=PRECISE) * score_scale
        allowed = (segment_block[:, None] == segment[None, :]) & (token_index[None, :] <= token_block[:, None])
        score = jnp.where(allowed[None], score, NEGATIVE)
        row_max = lax.optimization_barrier(jnp.max(score, axis=2, keepdims=True))
        exponent = jnp.exp(score - row_max)
        weights = low(exponent / lax.optimization_barrier(jnp.sum(exponent, axis=2, keepdims=True)))
        return jnp.einsum('uqk,kud->qud', weights, value_rows, precision=PRECISE)
    attended = lax.map(jax.checkpoint(score_block), (query.reshape(block_count, ATT_BLOCK, unit_count, HEAD_SIZE), segment.reshape(block_count, ATT_BLOCK), token_index.reshape(block_count, ATT_BLOCK)))
    return attended.reshape(sequence_length, unit_count, HEAD_SIZE)

def mixer_branch(blocks, state_values, paired_values, conv_values, scan_params, unit_index_list, segment, position):
    sequence_length, unit_count = (blocks.shape[0], blocks.shape[1])
    gate_width = DSSM // QUERY_HEADS
    per_unit = NH // QUERY_HEADS
    head_count = unit_count * per_unit
    gate_values = blocks[:, :, :gate_width].reshape(sequence_length, head_count, HP)
    conv_input = blocks[:, :, gate_width:2 * gate_width].reshape(sequence_length, unit_count * gate_width)
    query = blocks[:, :, 2 * gate_width:2 * gate_width + HEAD_SIZE]
    step_raw = blocks[:, :, blocks.shape[2] - per_unit:].reshape(sequence_length, head_count)
    scan_input = low(causal_conv(conv_input, conv_values, position)).reshape(sequence_length, head_count, HP)
    step_size = jax.nn.softplus(step_raw + scan_params[0][None, :])
    log_decay = -step_size * jnp.exp(scan_params[1])[None, :]
    scanned = state_scan(scan_input, step_size, log_decay, state_values[:, :NSTATE], state_values[:, NSTATE:], segment)
    scan_output = (scanned + scan_params[2][None, :, None] * scan_input) * jax.nn.silu(gate_values)
    heads_for_keys = paired_values[:, :KEY_VALUE_HEADS * HEAD_SIZE].reshape(sequence_length, KEY_VALUE_HEADS, HEAD_SIZE)
    heads_for_values = paired_values[:, KEY_VALUE_HEADS * HEAD_SIZE:].reshape(sequence_length, KEY_VALUE_HEADS, HEAD_SIZE)
    head_selection = (unit_index_list[:, None] // (QUERY_HEADS // KEY_VALUE_HEADS) == jnp.arange(KEY_VALUE_HEADS, dtype=jnp.int32)[None, :]).astype(jnp.float32)
    key_rows = jnp.einsum('gjd,uj->gud', heads_for_keys, head_selection, precision=PRECISE)
    value_rows = jnp.einsum('gjd,uj->gud', heads_for_values, head_selection, precision=PRECISE)
    attended = attention(low(rotate(query, position)), low(rotate(key_rows, position)), value_rows, segment)
    joined = jnp.concatenate([scan_output.reshape(sequence_length, unit_count, gate_width), attended], axis=2)
    return joined.reshape(sequence_length, unit_count * (gate_width + HEAD_SIZE))

def group_forward(inputs, adapters, frozen, segment, position, selector):
    norm_gain, weight_in, conv_values, conv_states, scan_params, weight_mix, weight_feed, weight_down = frozen
    in_lower, in_raise, mix_lower, mix_raise, feed_lower, feed_raise, down_lower, down_raise = adapters
    sequence_length = inputs.shape[0]
    gate_width = DSSM // QUERY_HEADS
    paired_width = 2 * KEY_VALUE_HEADS * HEAD_SIZE // QUERY_HEADS
    state_width = 2 * NSTATE // QUERY_HEADS
    pair_offset = 2 * gate_width + HEAD_SIZE
    state_offset = pair_offset + paired_width
    normed_one = low(rms_norm(inputs, norm_gain[0]))
    inner_in = low_back(low(selector * matmul(normed_one, in_lower)))
    projected = low_back(low(matmul(normed_one, weight_in) + matmul(inner_in, in_raise)))
    blocks = projected.reshape(sequence_length, QUERY_HEADS, UNIT_IN)
    paired_values = blocks[:, :, pair_offset:pair_offset + paired_width].reshape(sequence_length, QUERY_HEADS * paired_width)
    state_pre = blocks[:, :, state_offset:state_offset + state_width].reshape(sequence_length, QUERY_HEADS * state_width)
    state_values = low(causal_conv(state_pre, conv_states, position))
    unit_index_list = jnp.arange(QUERY_HEADS, dtype=jnp.int32)
    mixed_out = low_back(low(mixer_branch(blocks, state_values, paired_values, conv_values, scan_params, unit_index_list, segment, position)))
    inner_out = low_back(low(selector * matmul(mixed_out, mix_lower)))
    hidden = inputs + low_back(matmul(mixed_out, weight_mix) + matmul(inner_out, mix_raise))
    normed_two = low(rms_norm(hidden, norm_gain[1]))
    inner_feed = low_back(low(selector * matmul(normed_two, feed_lower)))
    gate_up = low_back(low(matmul(normed_two, weight_feed) + matmul(inner_feed, feed_raise))).reshape(sequence_length, QUERY_HEADS, 2 * UNIT_FF)
    activated = low_back(low(jax.nn.silu(gate_up[:, :, :UNIT_FF]) * gate_up[:, :, UNIT_FF:])).reshape(sequence_length, FF)
    inner_down = low_back(low(selector * matmul(activated, down_lower)))
    return hidden + low_back(matmul(activated, weight_down) + matmul(inner_down, down_raise))

def reference(tokens_in, cotangent, target, sequence_lengths, sequence_adapter, norm_gains, weight_in, conv_values, conv_states, scan_params, weight_mix, weight_feed, weight_down, in_lower, in_raise, mix_lower, mix_raise, feed_lower, feed_raise, down_lower, down_raise):
    arrival = jnp.argsort(target).astype(jnp.int32)
    packed_in = tokens_in.astype(jnp.float32)[arrival].reshape(GROUPS, GROUP, D)
    packed_grad = cotangent.astype(jnp.float32)[arrival].reshape(GROUPS, GROUP, D)
    frozen = tuple((weight.astype(jnp.float32) for weight in (norm_gains, weight_in, conv_values, conv_states, scan_params, weight_mix, weight_feed, weight_down)))
    adapters = tuple((factor.astype(jnp.float32) for factor in (in_lower, in_raise, mix_lower, mix_raise, feed_lower, feed_raise, down_lower, down_raise)))

    def per_group(carried, pieces):
        group_in, group_grad, lengths, chosen = pieces
        segment, position, selector = sequence_tables(lengths, chosen, GROUP)

        def forward(inputs, factors):
            return group_forward(inputs, factors, frozen, segment, position, selector)
        result, backward = jax.vjp(forward, group_in, adapters)
        grad_in, grad_factors = backward(group_grad)
        carried = tuple((running + addend for running, addend in zip(carried, grad_factors)))
        return (carried, (result, grad_in))
    zero_grads = tuple((jnp.zeros(factor.shape, jnp.float32) for factor in adapters))
    totals, (results, input_grads) = lax.scan(per_group, zero_grads, (packed_in, packed_grad, sequence_lengths, sequence_adapter))
    block_out = results.reshape(TOKENS, D)[target].astype(jnp.bfloat16)
    input_grad = input_grads.reshape(TOKENS, D)[target].astype(jnp.bfloat16)
    return (block_out, input_grad, totals[0], totals[1], totals[2], totals[3], totals[4], totals[5], totals[6], totals[7])
```

```python
import math

import jax
import jax.numpy as jnp
from jax import lax
from jax.sharding import PartitionSpec as P

NH = 48
HP = 64
NSTATE = 256
KCONV = 4
QUERY_HEADS = 8
KEY_VALUE_HEADS = 2
HEAD_SIZE = 128
RANK = 16
NADAPT = 8
SSD_BLOCK = 256
ATT_BLOCK = 512
DSSM = 3072
UNIT_IN = 1030
UNIT_FF = 512


EPSILON = 1e-05
ROPE_BASE = 10000.0
NEGATIVE = -1e30
FLOAT = jnp.float32
BFLOAT = jnp.bfloat16


def round_value(values):
    rounded = lax.optimization_barrier(values.astype(BFLOAT)).astype(FLOAT)
    return values + lax.stop_gradient(rounded - values)


def product(left, right):
    return jnp.dot(left, right, preferred_element_type=FLOAT)


def contract_last(left, right):
    return lax.dot_general(left, right, (((1,), (1,)), ((), ())), preferred_element_type=FLOAT)


def contract_first(left, right):
    return lax.dot_general(left, right, (((0,), (0,)), ((), ())), preferred_element_type=FLOAT)


def rms_norm(values, gain):
    return values * lax.rsqrt(jnp.mean(values * values, axis=-1, keepdims=True) + EPSILON) * gain


def sequence_tables(lengths, adapters, sequence_length):
    sequence_count = lengths.shape[0]
    boundary = jnp.cumsum(lengths)
    token_index = jnp.arange(sequence_length, dtype=jnp.int32)
    passed = (token_index[:, None] >= boundary[None, :]).astype(jnp.int32)
    segment = jnp.sum(passed, axis=1)
    segment_start = jnp.sum(passed * lengths[None, :], axis=1)
    position = token_index - segment_start
    member = (segment[:, None] == jnp.arange(sequence_count, dtype=jnp.int32)[None, :]).astype(
        jnp.int32
    )
    chosen = jnp.sum(member * adapters[None, :], axis=1)
    column = jnp.arange(NADAPT * RANK, dtype=jnp.int32) // RANK
    selector = (chosen[:, None] == column[None, :]).astype(FLOAT)
    return (segment, position, selector)


def causal_conv(channels, tap_table, position):
    running = tap_table[KCONV] + channels * tap_table[0]
    for lag_step in range(1, KCONV):
        shifted = jnp.concatenate(
            [jnp.zeros((lag_step, channels.shape[1]), FLOAT), channels[:-lag_step]], axis=0
        )
        running = (
            running + jnp.where((position >= lag_step)[:, None], shifted, 0.0) * tap_table[lag_step]
        )
    return jax.nn.silu(running)


def rotate(vectors, position):
    half_width = HEAD_SIZE // 2
    frequency = ROPE_BASE ** (-2.0 * jnp.arange(half_width, dtype=FLOAT) / HEAD_SIZE)
    angle_table = position.astype(FLOAT)[:, None] * frequency[None, :]
    cosine = jnp.cos(angle_table)[:, None, :]
    sine_part = jnp.sin(angle_table)[:, None, :]
    leading = vectors[..., :half_width]
    trailing = vectors[..., half_width:]
    return jnp.concatenate(
        [leading * cosine - trailing * sine_part, trailing * cosine + leading * sine_part], axis=-1
    )


def state_scan(inputs, step_size, log_decay, write_vectors, read_vectors, segment):
    sequence_length, head_count = step_size.shape
    block_count = sequence_length // SSD_BLOCK
    previous = jnp.concatenate([jnp.full((1,), -1, jnp.int32), segment[:-1]])
    first_previous = previous.reshape(block_count, SSD_BLOCK)[:, 0]
    inner_index = jnp.arange(SSD_BLOCK, dtype=jnp.int32)
    lower_mask = inner_index[:, None] >= inner_index[None, :]

    def scan_step(carry_state, block_data):
        (
            block_inputs,
            block_steps,
            block_decay,
            block_write,
            block_read,
            block_segment,
            block_previous,
        ) = block_data
        cumulative = jnp.cumsum(block_decay, axis=0)
        intersection = contract_last(block_read, block_write)
        allowed = lower_mask & (block_segment[:, None] == block_segment[None, :])
        difference = cumulative[:, None, :] - cumulative[None, :, :]
        decay_table = jnp.exp(jnp.where(allowed[:, :, None], difference, NEGATIVE))
        weights = round_value(intersection[:, :, None] * decay_table * block_steps[None, :, :])
        within = jnp.einsum("tsh,shp->thp", weights, block_inputs)
        carried = (block_segment == block_previous).astype(FLOAT)
        read_scaled = round_value(
            block_read[:, None, :] * (jnp.exp(cumulative) * carried[:, None])[:, :, None]
        )
        across = jnp.einsum("thn,hpn->thp", read_scaled, round_value(carry_state))
        tail_factor = (
            jnp.exp(cumulative[-1][None, :] - cumulative)
            * block_steps
            * (block_segment == block_segment[-1]).astype(FLOAT)[:, None]
        )
        write_scaled = round_value(block_write[:, None, :] * tail_factor[:, :, None])
        fresh_state = jnp.einsum("shp,shn->hpn", block_inputs, write_scaled)
        through = jnp.exp(cumulative[-1]) * (block_segment[-1] == block_previous).astype(FLOAT)
        return (carry_state * through[:, None, None] + fresh_state, within + across)

    sliced = (
        inputs.reshape(block_count, SSD_BLOCK, head_count, HP),
        step_size.reshape(block_count, SSD_BLOCK, head_count),
        log_decay.reshape(block_count, SSD_BLOCK, head_count),
        write_vectors.reshape(block_count, SSD_BLOCK, NSTATE),
        read_vectors.reshape(block_count, SSD_BLOCK, NSTATE),
        segment.reshape(block_count, SSD_BLOCK),
        first_previous,
    )
    zero_state = jnp.zeros((head_count, HP, NSTATE), FLOAT)
    _, outputs = lax.scan(jax.checkpoint(scan_step), zero_state, sliced)
    return outputs.reshape(sequence_length, head_count, HP)


def attention(query, key_rows, value_rows, segment):
    sequence_length, unit_count = (query.shape[0], query.shape[1])
    block_count = sequence_length // ATT_BLOCK
    token_index = jnp.arange(sequence_length, dtype=jnp.int32)
    score_scale = 1.0 / math.sqrt(HEAD_SIZE)

    def score_block(block_data):
        query_block, segment_block, token_block = block_data
        score = jnp.einsum("qud,kud->uqk", query_block, key_rows) * score_scale
        allowed = (segment_block[:, None] == segment[None, :]) & (
            token_index[None, :] <= token_block[:, None]
        )
        score = jnp.where(allowed[None], score, NEGATIVE)
        row_max = jnp.max(score, axis=2, keepdims=True)
        exponent = jnp.exp(score - row_max)
        weights = round_value(exponent / jnp.sum(exponent, axis=2, keepdims=True))
        return jnp.einsum("uqk,kud->qud", weights, value_rows)

    attended = lax.map(
        jax.checkpoint(score_block),
        (
            query.reshape(block_count, ATT_BLOCK, unit_count, HEAD_SIZE),
            segment.reshape(block_count, ATT_BLOCK),
            token_index.reshape(block_count, ATT_BLOCK),
        ),
    )
    return attended.reshape(sequence_length, unit_count, HEAD_SIZE)


def mixer_branch(gate_in, conv_in, query_in, step_in, state_values, key_in, value_in, conv_values, scan_params, segment, position):
    rows = gate_in.shape[0]
    head_count = step_in.shape[1]
    unit_count = head_count * QUERY_HEADS // NH
    scan_input = round_value(causal_conv(conv_in, conv_values, position)).reshape(rows, head_count, HP)
    step_size = jax.nn.softplus(step_in + scan_params[0][None, :])
    log_decay = -step_size * jnp.exp(scan_params[1])[None, :]
    scanned = state_scan(
        scan_input, step_size, log_decay, state_values[:, :NSTATE], state_values[:, NSTATE:], segment
    )
    scan_output = (scanned + scan_params[2][None, :, None] * scan_input) * jax.nn.silu(
        gate_in.reshape(rows, head_count, HP)
    )
    attended = attention(
        round_value(rotate(query_in.reshape(rows, unit_count, HEAD_SIZE), position)),
        jnp.broadcast_to(round_value(rotate(key_in[:, None, :], position)), (rows, unit_count, HEAD_SIZE)),
        jnp.broadcast_to(value_in[:, None, :], (rows, unit_count, HEAD_SIZE)),
        segment,
    )
    return jnp.concatenate(
        [scan_output.reshape(rows, head_count * HP), attended.reshape(rows, unit_count * HEAD_SIZE)], axis=1
    )


GATE_WIDTH = DSSM // QUERY_HEADS
PAIR_WIDTH = 2 * KEY_VALUE_HEADS * HEAD_SIZE // QUERY_HEADS
STATE_WIDTH = 2 * NSTATE // QUERY_HEADS
STEP_WIDTH = NH // QUERY_HEADS
LANES = 128
ALL_AXES = ("row", "col")


def pad_columns(values, width):
    return jnp.pad(values, ((0, 0), (0, width - values.shape[1])))


def align_units(values, units):
    cuts = [0, GATE_WIDTH, 2 * GATE_WIDTH, 2 * GATE_WIDTH + HEAD_SIZE]
    cuts += [cuts[-1] + PAIR_WIDTH, cuts[-1] + PAIR_WIDTH + STATE_WIDTH, UNIT_IN]
    parts = [
        values[:, unit * UNIT_IN + low : unit * UNIT_IN + high]
        for low, high in zip(cuts[:-1], cuts[1:])
        for unit in range(units)
    ]
    joined = jnp.concatenate(parts, axis=1)
    return pad_columns(joined, -(-joined.shape[1] // LANES) * LANES)


def restore_units(values, units):
    widths = [GATE_WIDTH, GATE_WIDTH, HEAD_SIZE, PAIR_WIDTH, STATE_WIDTH, STEP_WIDTH]
    parts = []
    for unit in range(units):
        start = 0
        for width in widths:
            parts.append(values[:, start + unit * width : start + (unit + 1) * width])
            start += units * width
    return jnp.concatenate(parts, axis=1)


def split_halves(values, units, first, axis):
    block = values.shape[axis] // units
    take = lambda low, high: lax.slice_in_dim(values, low, high, axis=axis)
    parts = [take(unit * block, unit * block + first) for unit in range(units)]
    parts += [take(unit * block + first, (unit + 1) * block) for unit in range(units)]
    return jnp.concatenate(parts, axis=axis)


def join_halves(values, units, first, axis):
    block = values.shape[axis] // units
    rest = block - first
    take = lambda low, high: lax.slice_in_dim(values, low, high, axis=axis)
    parts = []
    for unit in range(units):
        parts.append(take(unit * first, (unit + 1) * first))
        parts.append(take(units * first + unit * rest, units * first + (unit + 1) * rest))
    return jnp.concatenate(parts, axis=axis)


def flip(values, mask):
    return lax.ppermute(values, "col", [(i, i ^ mask) for i in range(4)])


def gather_blocks(own):
    col = lax.axis_index("col")
    half = own.shape[-1] // 2
    near = flip(own, 1)
    far = flip(own, 2)
    corner = jnp.concatenate([flip(far[..., :half], 1), flip(near[..., half:], 2)], axis=-1)
    return [(col, own), (col ^ 1, near), (col ^ 2, far), (col ^ 3, corner)]


def reduce_blocks(piece):
    col = lax.axis_index("col")
    wide = lambda values: values.astype(FLOAT)
    send = lambda values, mask: flip(values.astype(BFLOAT), mask)
    corner_a = send(piece(col ^ 3, 0), 1)
    corner_b = send(piece(col ^ 3, 1), 2)
    near_a = send(piece(col ^ 1, 0), 1)
    far_b = send(piece(col ^ 2, 1), 2)
    far_a = send(piece(col ^ 2, 0) + wide(corner_a), 2)
    near_b = send(piece(col ^ 1, 1) + wide(corner_b), 1)
    first = piece(col, 0) + wide(near_a) + wide(far_a)
    second = piece(col, 1) + wide(far_b) + wide(near_b)
    return first, second


def rows_of(values, block, rows):
    return lax.dynamic_slice_in_dim(values, block * rows, rows, 0)


def spread_project(own, wide, narrow_factor, selector):
    rows = own.shape[0]
    width = narrow_factor.shape[1]

    def project(values, chosen):
        both = product(values, wide)
        narrow = (chosen * both[:, width:]).astype(BFLOAT)
        return (both[:, :width] + product(narrow, narrow_factor)).astype(BFLOAT), narrow

    if lax.axis_size("col") != 4:
        return project(lax.all_gather(own, "col", axis=0, tiled=True), selector)
    total = rows * 4
    result = jnp.zeros((total, width), BFLOAT)
    narrow_result = jnp.zeros((total, LANES), BFLOAT)
    for block, values in gather_blocks(own):
        part, narrow = project(values, rows_of(selector, block, rows))
        result = lax.dynamic_update_slice_in_dim(result, part, block * rows, 0)
        narrow_result = lax.dynamic_update_slice_in_dim(narrow_result, narrow, block * rows, 0)
    return result, narrow_result


def collect_project(values, wide, narrow_factor, own_selector):
    rows = own_selector.shape[0]
    width = narrow_factor.shape[1]
    model = wide.shape[0]
    weight = wide[:, :width]
    if lax.axis_size("col") != 4:
        partial = jnp.concatenate(
            [contract_last(values, weight), contract_last(values, narrow_factor)], axis=1
        ).astype(BFLOAT)
        summed = lax.psum_scatter(partial, "col", scatter_dimension=0, tiled=True).astype(FLOAT)
        base, narrow = summed[:, :model], summed[:, model:]
    else:
        half = model // 2

        def piece(block, side):
            taken = rows_of(values, block, rows)
            if side:
                return contract_last(taken, weight[half:])
            return jnp.concatenate(
                [contract_last(taken, weight[:half]), contract_last(taken, narrow_factor)], axis=1
            )

        first, second = reduce_blocks(piece)
        base = jnp.concatenate([first[:, :half], second], axis=1)
        narrow = first[:, half:]
    inner = (own_selector * narrow).astype(BFLOAT)
    return base + contract_last(inner, wide[:, width:]), inner


def local(
    tokens_in,
    cotangent,
    target,
    sequence_lengths,
    sequence_adapter,
    norm_gains,
    weight_in,
    conv_values,
    conv_states,
    scan_params,
    weight_mix,
    weight_feed,
    weight_down,
    in_lower,
    in_raise,
    mix_lower,
    mix_raise,
    feed_lower,
    feed_raise,
    down_lower,
    down_raise,
):
    cols = lax.axis_size("col")
    rows_axis = lax.axis_size("row")
    col = lax.axis_index("col")
    devices = cols * rows_axis
    rows = tokens_in.shape[0]
    model = tokens_in.shape[1]
    total = rows * cols
    units = QUERY_HEADS // cols
    heads = units * STEP_WIDTH
    peer = rows // devices
    lengths, adapters = sequence_lengths[0], sequence_adapter[0]
    sequences = lengths.shape[0]

    gather = lambda values: lax.all_gather(values, "row", axis=0, tiled=True)
    wide_in = gather(jnp.concatenate([align_units(weight_in, units), in_lower], axis=1))
    small_parts = [
        align_units(in_raise, units),
        split_halves(mix_lower, units, GATE_WIDTH, 0).T,
        split_halves(feed_raise, units, UNIT_FF, 1),
        down_lower.T,
    ]
    small_cuts = [0]
    for part in small_parts:
        small_cuts.append(small_cuts[-1] + part.shape[1])
    small = gather(jnp.concatenate(small_parts, axis=1))
    narrow_in, narrow_mix, narrow_feed, narrow_down = [
        small[:, low:high] for low, high in zip(small_cuts[:-1], small_cuts[1:])
    ]
    wide_mix = gather(
        jnp.concatenate([split_halves(weight_mix, units, GATE_WIDTH, 0), mix_raise], axis=0).T
    )
    wide_feed = gather(
        jnp.concatenate([split_halves(weight_feed, units, UNIT_FF, 1), feed_lower], axis=1)
    )
    wide_down = gather(jnp.concatenate([weight_down, down_raise], axis=0).T)

    destination = target // rows
    index = jnp.arange(rows, dtype=jnp.int32)
    same = (destination[:, None] == destination[None, :]) & (index[None, :] < index[:, None])
    place_sent = destination * peer + jnp.sum(same.astype(jnp.int32), axis=1)
    send_matrix = (index[:, None] == place_sent[None, :]).astype(BFLOAT)
    notes = jnp.concatenate([(target % rows)[:, None], jnp.broadcast_to(adapters[None, :], (rows, sequences))], axis=1)
    notes = pad_columns(notes.astype(BFLOAT), LANES)
    exchange = lambda values: lax.all_to_all(values, ALL_AXES, split_axis=0, concat_axis=0, tiled=True)
    arrived = exchange(product(send_matrix, jnp.concatenate([tokens_in, notes], axis=1)).astype(BFLOAT))
    arrived_grad = exchange(product(send_matrix, cotangent).astype(BFLOAT))
    arrived_slot = arrived[:, model].astype(jnp.int32)
    place_matrix = (index[:, None] == arrived_slot[None, :]).astype(BFLOAT)
    source_adapters = arrived[::peer, model + 1 : model + 1 + sequences].astype(jnp.int32)
    own_input = product(place_matrix, arrived[:, :model])
    branch_two = product(place_matrix, arrived_grad).astype(BFLOAT)
    own_upstream = branch_two.astype(FLOAT)

    segment, position, selector = sequence_tables(lengths, adapters, total)
    own_selector = rows_of(selector, col, rows)
    own_segment = rows_of(segment, col, rows)
    norm_gain = norm_gains.astype(FLOAT)

    def compact_grad(narrow, values):
        parts = [
            lax.dynamic_slice_in_dim(narrow, adapters[at] * RANK, RANK, 1)
            * (own_segment == at).astype(BFLOAT)[:, None]
            for at in range(sequences)
        ]
        grad = contract_first(jnp.concatenate(parts, axis=1), values).astype(BFLOAT)
        kept = sequences * RANK
        grad = grad.reshape(kept, devices, model // devices).transpose(1, 0, 2)
        return pad_columns(grad.reshape(devices, kept * model // devices), model)

    def expand_grad(dealt):
        kept = sequences * RANK
        dealt = dealt[:, : kept * model // devices].reshape(devices * kept, model // devices)
        adapter_row = (source_adapters[:, :, None] * RANK + jnp.arange(RANK, dtype=jnp.int32)).reshape(-1)
        chosen = (jnp.arange(NADAPT * RANK, dtype=jnp.int32)[:, None] == adapter_row[None, :]).astype(BFLOAT)
        return product(chosen, dealt)

    def send_back(values, grads):
        back = product(place_matrix.T, values.astype(BFLOAT)).astype(BFLOAT).reshape(devices, peer, model)
        joined = jnp.concatenate([back] + [grad[:, None, :] for grad in grads], axis=1)
        dealt = exchange(joined)
        returned = product(send_matrix.T, dealt[:, :peer].reshape(rows, model)).astype(BFLOAT)
        return returned, [expand_grad(dealt[:, peer + at]) for at in range(len(grads))]

    normed_one, norm_one_back = jax.vjp(lambda values: rms_norm(values, norm_gain[0]), own_input)
    normed_one = normed_one.astype(BFLOAT)
    projected, inner_in = spread_project(normed_one, wide_in, narrow_in, selector)
    cuts = [0]
    for width in (GATE_WIDTH, GATE_WIDTH, HEAD_SIZE, PAIR_WIDTH, STATE_WIDTH, STEP_WIDTH):
        cuts.append(cuts[-1] + units * width)
    gate_in, conv_in, query_in, pair_own, state_own, step_in = [
        projected[:, low:high] for low, high in zip(cuts[:-1], cuts[1:])
    ]
    conv_state_float = conv_states.astype(FLOAT)
    state_post, state_back = jax.vjp(
        lambda values: causal_conv(values, conv_state_float, position), state_own.astype(FLOAT)
    )
    shared = jnp.concatenate([pair_own, state_post.astype(BFLOAT)], axis=1)
    if cols == 4:
        held = jnp.zeros((cols,) + shared.shape, BFLOAT)
        for block, values in gather_blocks(shared):
            held = lax.dynamic_update_index_in_dim(held, values, block, 0)
    else:
        held = lax.all_gather(shared, "col", axis=0)
    pair_width = units * PAIR_WIDTH
    state_full = jnp.concatenate([held[at, :, pair_width:] for at in range(cols)], axis=1)
    pair_full = jnp.concatenate([held[at, :, :pair_width] for at in range(cols)], axis=1)
    key_head = col * units // (QUERY_HEADS // KEY_VALUE_HEADS)
    pick = lambda start: lax.select_n(
        key_head,
        *[pair_full[:, start + at * HEAD_SIZE : start + (at + 1) * HEAD_SIZE] for at in range(KEY_VALUE_HEADS)],
    )
    keys, values = pick(0), pick(KEY_VALUE_HEADS * HEAD_SIZE)
    conv_value_float = conv_values.astype(FLOAT)

    def mix_local(*parts):
        return mixer_branch(*parts, conv_value_float, scan_params, segment, position)

    mixed_float, mixer_back = jax.vjp(
        mix_local, *[part.astype(FLOAT) for part in (gate_in, conv_in, query_in, step_in, state_full, keys, values)]
    )
    mixed_out = mixed_float.astype(BFLOAT)
    branch_sum, inner_out = collect_project(mixed_out, wide_mix, narrow_mix, own_selector)
    hidden = own_input + branch_sum
    normed_two, norm_two_back = jax.vjp(lambda values: rms_norm(values, norm_gain[1]), hidden)
    normed_two = normed_two.astype(BFLOAT)
    gate_up, inner_feed = spread_project(normed_two, wide_feed, narrow_feed, selector)
    act_grad, narrow_two = spread_project(branch_two, wide_down, narrow_down, selector)
    half_feed = units * UNIT_FF

    def swiglu(gate_part, up_part):
        return jax.nn.silu(gate_part) * up_part

    activated, swiglu_back = jax.vjp(
        swiglu, gate_up[:, :half_feed].astype(FLOAT), gate_up[:, half_feed:].astype(FLOAT)
    )
    activated = activated.astype(BFLOAT)
    feed_grad = jnp.concatenate(swiglu_back(act_grad.astype(FLOAT)), axis=1).astype(BFLOAT)
    normed_two_grad, narrow_three = collect_project(feed_grad, wide_feed, narrow_feed, own_selector)
    (hidden_from_norm,) = norm_two_back(normed_two_grad)
    hidden_grad = own_upstream + hidden_from_norm
    branch_one = hidden_grad.astype(BFLOAT)
    mixed_grad, narrow_one = spread_project(branch_one, wide_mix, narrow_mix, selector)

    down_sum, inner_down = collect_project(activated, wide_down, narrow_down, own_selector)
    block_out, (grad_down_raise, grad_feed_lower, grad_mix_raise) = send_back(
        hidden + down_sum,
        [
            compact_grad(inner_down, branch_two),
            compact_grad(narrow_three, normed_two),
            compact_grad(inner_out, branch_one),
        ],
    )

    def sum_rows(values):
        return lax.psum_scatter(values.astype(BFLOAT), "row", scatter_dimension=0, tiled=True).astype(FLOAT)

    early = sum_rows(
        jnp.concatenate(
            [
                contract_first(narrow_one, mixed_out),
                contract_first(inner_feed, feed_grad),
                contract_first(narrow_two, activated),
            ],
            axis=1,
        )
    )
    early_cuts = [cut - small_cuts[1] for cut in small_cuts[1:]]
    mix_lower_part, feed_raise_part, down_lower_part = [
        early[:, low:high] for low, high in zip(early_cuts[:-1], early_cuts[1:])
    ]
    grad_mix_lower = join_halves(mix_lower_part, units, GATE_WIDTH, 1).T
    grad_feed_raise = join_halves(feed_raise_part, units, UNIT_FF, 1)
    grad_down_lower = down_lower_part.T

    gate_grad, conv_grad, query_grad, step_grad, state_grad, key_grad, value_grad = mixer_back(
        mixed_grad.astype(FLOAT)
    )
    mine = [(key_head == at).astype(FLOAT) for at in range(KEY_VALUE_HEADS)]
    pair_grad = jnp.concatenate([grad * here for grad in (key_grad, value_grad) for here in mine], axis=1)
    state_width = units * STATE_WIDTH
    stacked = jnp.stack(
        [
            jnp.concatenate(
                [
                    pair_grad[:, at * pair_width : (at + 1) * pair_width],
                    state_grad[:, at * state_width : (at + 1) * state_width],
                ],
                axis=1,
            )
            for at in range(cols)
        ]
    )
    if cols == 4:
        part = total // 2
        shared_grad = jnp.concatenate(
            reduce_blocks(
                lambda block, side: lax.dynamic_index_in_dim(stacked, block, 0, False)[
                    side * part : (side + 1) * part
                ]
            ),
            axis=0,
        )
    else:
        shared_grad = lax.psum_scatter(
            stacked.astype(BFLOAT).reshape(cols * total, -1), "col", scatter_dimension=0, tiled=True
        ).astype(FLOAT)
    (state_pre_grad,) = state_back(shared_grad[:, pair_width:])
    projected_grad = jnp.concatenate(
        [gate_grad, conv_grad, query_grad, shared_grad[:, :pair_width], state_pre_grad, step_grad], axis=1
    ).astype(BFLOAT)
    projected_grad = pad_columns(projected_grad, narrow_in.shape[1])
    grad_in_raise = restore_units(sum_rows(contract_first(inner_in, projected_grad)), units)
    normed_one_grad, narrow_four = collect_project(projected_grad, wide_in, narrow_in, own_selector)
    (input_from_norm,) = norm_one_back(normed_one_grad)
    input_grad, (grad_in_lower,) = send_back(
        hidden_grad + input_from_norm, [compact_grad(narrow_four, normed_one)]
    )
    return (
        block_out,
        input_grad,
        grad_in_lower.T,
        grad_in_raise,
        grad_mix_lower,
        grad_mix_raise,
        grad_feed_lower.T,
        grad_feed_raise,
        grad_down_lower,
        grad_down_raise,
    )


def solution(mesh):
    in_specs = (
        P(("row", "col"), None),
        P(("row", "col"), None),
        P(("row", "col")),
        P("row", None),
        P("row", None),
        P(),
        P("row", "col"),
        P(None, "col"),
        P(None, "col"),
        P(None, "col"),
        P("col", "row"),
        P("row", "col"),
        P("col", "row"),
        P("row", None),
        P("row", "col"),
        P("col", "row"),
        P(None, "row"),
        P("row", None),
        P("row", "col"),
        P("col", "row"),
        P(None, "row"),
    )
    out_specs = (
        P(("row", "col"), None),
        P(("row", "col"), None),
        P(("row", "col"), None),
        P("row", "col"),
        P("col", "row"),
        P(None, ("row", "col")),
        P(("row", "col"), None),
        P("row", "col"),
        P("col", "row"),
        P(None, ("row", "col")),
    )
    return jax.shard_map(local, mesh=mesh, in_specs=in_specs, out_specs=out_specs, check_vma=False)
```

```python
import math

import jax
import jax.numpy as jnp
from jax import lax
from jax.experimental import pallas as pl
from jax.experimental.pallas import tpu as pltpu
from jax.sharding import PartitionSpec as P

NH = 48
HP = 64
NSTATE = 256
KCONV = 4
QUERY_HEADS = 8
KEY_VALUE_HEADS = 2
HEAD_SIZE = 128
RANK = 16
NADAPT = 8
SSD_BLOCK = 256
DSSM = 3072
UNIT_IN = 1030
UNIT_FF = 512


EPSILON = 1e-05
ROPE_BASE = 10000.0
NEGATIVE = -1e30
FLOAT = jnp.float32
BFLOAT = jnp.bfloat16


def product(left, right):
    return jnp.dot(left, right, preferred_element_type=FLOAT)


def contract_last(left, right):
    return lax.dot_general(left, right, (((1,), (1,)), ((), ())), preferred_element_type=FLOAT)


def contract_first(left, right):
    return lax.dot_general(left, right, (((0,), (0,)), ((), ())), preferred_element_type=FLOAT)


def rms_norm(values, gain):
    return values * lax.rsqrt(jnp.mean(values * values, axis=-1, keepdims=True) + EPSILON) * gain


def sequence_tables(lengths, adapters, sequence_length):
    sequence_count = lengths.shape[0]
    boundary = jnp.cumsum(lengths)
    token_index = jnp.arange(sequence_length, dtype=jnp.int32)
    passed = (token_index[:, None] >= boundary[None, :]).astype(jnp.int32)
    segment = jnp.sum(passed, axis=1)
    segment_start = jnp.sum(passed * lengths[None, :], axis=1)
    position = token_index - segment_start
    member = (segment[:, None] == jnp.arange(sequence_count, dtype=jnp.int32)[None, :]).astype(
        jnp.int32
    )
    chosen = jnp.sum(member * adapters[None, :], axis=1)
    column = jnp.arange(NADAPT * RANK, dtype=jnp.int32) // RANK
    selector = (chosen[:, None] == column[None, :]).astype(FLOAT)
    return (segment, position, selector)


def causal_conv(channels, tap_table, position):
    running = tap_table[KCONV] + channels * tap_table[0]
    for lag_step in range(1, KCONV):
        shifted = jnp.concatenate(
            [jnp.zeros((lag_step, channels.shape[1]), FLOAT), channels[:-lag_step]], axis=0
        )
        running = (
            running + jnp.where((position >= lag_step)[:, None], shifted, 0.0) * tap_table[lag_step]
        )
    return jax.nn.silu(running)


VMEM_BYTES = 56 * 1024 * 1024
LANES = 128


def whole(shape):
    return pl.BlockSpec(shape, lambda *_: (0,) * len(shape))


def dot(left, right, contract):
    return lax.dot_general(left, right, ((contract[:1], contract[1:]), ((), ())), preferred_element_type=FLOAT)


def parts_of(values, count):
    parts = []
    for _ in range(count):
        part = values.astype(BFLOAT)
        parts.append(part)
        values = values - part.astype(FLOAT)
    return parts


def running_sum(values, triangle, contract):
    width = values.shape[1]
    split = dot(triangle, jnp.concatenate(parts_of(values, 3), axis=1), contract)
    return split[:, :width] + split[:, width : 2 * width] + split[:, 2 * width :]


def head_spread(values, expand):
    return dot(jnp.concatenate(parts_of(values, 2), axis=1), expand, (1, 0))


def head_sum(values, expand):
    high, low = parts_of(values, 2)
    single = expand[:LANES]
    return dot(high, single, (1, 1)) + dot(low, single, (1, 1))


def silu_parts(values):
    gate = 1.0 / (1.0 + jnp.exp(-values))
    return values * gate, gate


def expand_table(channels):
    row = lax.broadcasted_iota(jnp.int32, (2 * LANES, channels), 0) % LANES
    channel = lax.broadcasted_iota(jnp.int32, (2 * LANES, channels), 1) // HP
    return (row == channel).astype(BFLOAT)


def scan_block(gate_ref, conv_ref, before_ref, step_ref, write_ref, read_ref, meta_ref, segment_ref, taps_ref, head_ref):
    rows = SSD_BLOCK
    channels = conv_ref.shape[1]
    meta = meta_ref[...]
    current = conv_ref[...].astype(FLOAT)
    window = jnp.concatenate([before_ref[8:16, :].astype(FLOAT), current], axis=0)
    summed = taps_ref[KCONV : KCONV + 1, :] + current * taps_ref[0:1, :]
    for lag in range(1, KCONV):
        shifted = window[8 - lag : 8 - lag + rows]
        summed = summed + jnp.where(meta[:, 1:2] >= lag, shifted, 0.0) * taps_ref[lag : lag + 1, :]
    activated, conv_gate = silu_parts(summed)
    inputs = activated.astype(BFLOAT)
    wide_inputs = inputs.astype(FLOAT)
    raw = step_ref[...].astype(FLOAT) + head_ref[0:1, :]
    steps = jnp.maximum(raw, 0.0) + jnp.log1p(jnp.exp(-jnp.abs(raw)))
    row = lax.broadcasted_iota(jnp.int32, (rows, rows), 0)
    column = lax.broadcasted_iota(jnp.int32, (rows, rows), 1)
    triangle = (row >= column).astype(BFLOAT)
    total = running_sum(steps * head_ref[1:2, :], triangle, (1, 0))
    entered = jnp.exp(total) * meta[:, 3:4]
    leaving = jnp.exp(total[rows - 1 : rows] - total) * meta[:, 4:5]
    expand = expand_table(channels)
    spread = head_spread(jnp.concatenate([steps, entered, leaving * steps], axis=0), expand)
    blocked = jnp.where((row >= column) & (meta[:, 0:1] == segment_ref[0:1, :]), 0.0, NEGATIVE)
    crossing = dot(read_ref[...], write_ref[...], (1, 1))
    return dict(
        summed=summed,
        conv_gate=conv_gate,
        wide_inputs=wide_inputs,
        raw=raw,
        steps=steps,
        triangle=triangle,
        total=total,
        total_rows=total.T,
        leaving=leaving,
        expand=expand,
        steps_wide=spread[:rows],
        entered_wide=spread[rows : 2 * rows],
        tail_wide=spread[2 * rows :],
        stepped=(wide_inputs * spread[:rows]).astype(BFLOAT),
        tailed=(wide_inputs * spread[2 * rows :]).astype(BFLOAT),
        blocked=blocked,
        crossing=crossing,
    )


def decay_of(block, head):
    return jnp.exp(
        block["total"][:, head : head + 1] - block["total_rows"][head : head + 1, :] + block["blocked"]
    )


def scan_forward_kernel(
    gate_ref, conv_ref, before_ref, step_ref, write_ref, read_ref, meta_ref, segment_ref, taps_ref, head_ref,
    skip_ref, out_ref, scanned_ref, states_ref, state,
):
    @pl.when(pl.program_id(0) == 0)
    def _():
        state[...] = jnp.zeros_like(state)

    block = scan_block(
        gate_ref, conv_ref, before_ref, step_ref, write_ref, read_ref, meta_ref, segment_ref, taps_ref, head_ref
    )
    heads = conv_ref.shape[1] // HP
    carried = state[...].astype(BFLOAT)
    states_ref[0] = carried
    across = dot(read_ref[...], carried, (1, 0)) * block["entered_wide"]
    within = []
    for head in range(heads):
        weights = (block["crossing"] * decay_of(block, head)).astype(BFLOAT)
        within.append(dot(weights, block["stepped"][:, head * HP : (head + 1) * HP], (1, 0)))
    scanned = across + jnp.concatenate(within, axis=1)
    scanned_ref[...] = scanned
    gated, _ = silu_parts(gate_ref[...].astype(FLOAT))
    out_ref[...] = ((scanned + skip_ref[0:1, :] * block["wide_inputs"]) * gated).astype(BFLOAT)
    state[...] = state[...] * block["entered_wide"][SSD_BLOCK - 1 : SSD_BLOCK, :] + dot(
        write_ref[...], block["tailed"], (0, 0)
    )


def scan_backward_kernel(
    gate_ref, conv_ref, before_ref, step_ref, write_ref, read_ref, meta_ref, segment_ref, taps_ref, head_ref,
    skip_ref, scanned_ref, states_ref, grad_ref, query_grad_ref, out_ref, shared_ref, state_grad, later,
):
    @pl.when(pl.program_id(0) == 0)
    def _():
        state_grad[...] = jnp.zeros_like(state_grad)
        later[...] = jnp.zeros_like(later)

    block = scan_block(
        gate_ref, conv_ref, before_ref, step_ref, write_ref, read_ref, meta_ref, segment_ref, taps_ref, head_ref
    )
    rows = SSD_BLOCK
    channels = conv_ref.shape[1]
    heads = channels // HP
    meta = meta_ref[...]
    read, write = read_ref[...], write_ref[...]
    inputs = block["wide_inputs"]
    scanned = scanned_ref[...]
    skip = skip_ref[0:1, :]
    gate_values = gate_ref[...].astype(FLOAT)
    gated, gate = silu_parts(gate_values)
    grad = grad_ref[...].astype(FLOAT)
    gate_grad = grad * (scanned + skip * inputs) * (gate * (1.0 + gate_values * (1.0 - gate)))
    out_grad = grad * gated
    inputs_grad = skip * out_grad
    rounded = out_grad.astype(BFLOAT)
    wide_rounded = rounded.astype(FLOAT)
    carried = states_ref[0]
    after = state_grad[...]
    after_rounded = after.astype(BFLOAT)

    from_state = dot(write, after_rounded, (1, 0))
    entering = (wide_rounded * block["entered_wide"]).astype(BFLOAT)
    write_grad = dot(block["tailed"], after_rounded, (1, 1))
    read_grad = dot(entering, carried, (1, 1))
    last_entered = block["entered_wide"][rows - 1 : rows, :]
    through = jnp.sum(after * carried.astype(FLOAT), axis=0, keepdims=True) * last_entered
    state_grad[...] = after * last_entered + dot(read, entering, (0, 0))

    crossing_grad = jnp.zeros((rows, rows), FLOAT)
    pulled = []
    for head in range(heads):
        span = slice(head * HP, (head + 1) * HP)
        decay = decay_of(block, head)
        weights = (block["crossing"] * decay).astype(BFLOAT)
        pulled.append(dot(weights, rounded[:, span], (0, 0)))
        crossing_grad = crossing_grad + dot(rounded[:, span], block["stepped"][:, span], (1, 1)) * decay
    pulled = jnp.concatenate(pulled, axis=1)
    crossing_rounded = crossing_grad.astype(BFLOAT)
    read_grad = read_grad + dot(crossing_rounded, write, (1, 0))
    write_grad = write_grad + dot(crossing_rounded, read, (0, 0))
    shared_ref[:, :NSTATE] = write_grad.astype(BFLOAT)
    shared_ref[:, NSTATE:] = read_grad.astype(BFLOAT)

    inputs_grad = inputs_grad + block["steps_wide"] * pulled + block["tail_wide"] * from_state
    sums = head_sum(
        jnp.concatenate(
            [
                wide_rounded * scanned - block["stepped"].astype(FLOAT) * pulled,
                inputs * pulled,
                inputs * from_state,
                jnp.broadcast_to(through, (8, channels)),
            ],
            axis=0,
        ),
        block["expand"],
    )
    leaving_grad = sums[2 * rows : 3 * rows] * block["leaving"]
    leaving_total = leaving_grad * block["steps"]
    last = sums[3 * rows : 3 * rows + 1] + jnp.sum(leaving_total, axis=0, keepdims=True)
    total_grad = sums[:rows] - leaving_total
    total_grad = total_grad + jnp.where(
        lax.broadcasted_iota(jnp.int32, total_grad.shape, 0) == rows - 1, last, 0.0
    )
    decay_grad = running_sum(total_grad, block["triangle"], (0, 0))
    steps_grad = sums[rows : 2 * rows] + leaving_grad + decay_grad * head_ref[1:2, :]
    raw_grad = steps_grad / (1.0 + jnp.exp(-block["raw"]))
    raw_grad = jnp.where(lax.broadcasted_iota(jnp.int32, raw_grad.shape, 1) < heads, raw_grad, 0.0)

    summed, conv_gate = block["summed"], block["conv_gate"]
    summed_grad = inputs_grad * (conv_gate * (1.0 + summed * (1.0 - conv_gate)))
    window = jnp.concatenate([summed_grad, later[...]], axis=0)
    conv_grad = summed_grad * taps_ref[0:1, :]
    for lag in range(1, KCONV):
        conv_grad = conv_grad + jnp.where(meta[:, 2:3] >= lag, window[lag : lag + rows], 0.0) * taps_ref[lag : lag + 1, :]
    later[...] = summed_grad[:8]

    out_ref[:, :channels] = gate_grad.astype(BFLOAT)
    out_ref[:, channels : 2 * channels] = conv_grad.astype(BFLOAT)
    query_width = query_grad_ref.shape[1]
    out_ref[:, 2 * channels : 2 * channels + query_width] = query_grad_ref[...]
    rest = out_ref.shape[1] - LANES
    out_ref[:, 2 * channels + query_width : rest] = jnp.zeros((rows, rest - 2 * channels - query_width), BFLOAT)
    out_ref[:, rest:] = raw_grad.astype(BFLOAT)


def scan_specs(tokens, channels, width, order):
    half = SSD_BLOCK // 16
    return [
        pl.BlockSpec((SSD_BLOCK, channels), lambda i: (order(i), 0)),
        pl.BlockSpec((SSD_BLOCK, channels), lambda i: (order(i), 1)),
        pl.BlockSpec((16, channels), lambda i: (jnp.maximum(order(i) * half - 1, 0), 1)),
        pl.BlockSpec((SSD_BLOCK, LANES), lambda i: (order(i), width // LANES - 1)),
        pl.BlockSpec((SSD_BLOCK, NSTATE), lambda i: (order(i), 0)),
        pl.BlockSpec((SSD_BLOCK, NSTATE), lambda i: (order(i), 1)),
        pl.BlockSpec((SSD_BLOCK, LANES), lambda i: (order(i), 0)),
        pl.BlockSpec((8, SSD_BLOCK), lambda i: (0, order(i))),
        whole((8, channels)),
        whole((8, LANES)),
        whole((8, channels)),
    ]


def scan_cost(tokens, channels, factor):
    heads = channels // HP
    return pl.CostEstimate(
        flops=factor * 2 * tokens * SSD_BLOCK * (3 * channels + NSTATE),
        bytes_accessed=factor * tokens * channels * 12,
        transcendentals=tokens * SSD_BLOCK * heads,
    )


def scan_forward(projected, states, tables):
    tokens, width = projected.shape
    channels = tables["taps"].shape[1]
    blocks = tokens // SSD_BLOCK
    order = lambda i: i
    return pl.pallas_call(
        scan_forward_kernel,
        grid=(blocks,),
        in_specs=scan_specs(tokens, channels, width, order),
        out_specs=[
            pl.BlockSpec((SSD_BLOCK, channels), lambda i: (i, 0)),
            pl.BlockSpec((SSD_BLOCK, channels), lambda i: (i, 0)),
            pl.BlockSpec((1, NSTATE, channels), lambda i: (i, 0, 0)),
        ],
        out_shape=[
            jax.ShapeDtypeStruct((tokens, channels), BFLOAT),
            jax.ShapeDtypeStruct((tokens, channels), FLOAT),
            jax.ShapeDtypeStruct((blocks, NSTATE, channels), BFLOAT),
        ],
        scratch_shapes=[pltpu.VMEM((NSTATE, channels), FLOAT)],
        compiler_params=pltpu.CompilerParams(vmem_limit_bytes=VMEM_BYTES),
        cost_estimate=scan_cost(tokens, channels, 1),
        name="scan_forward",
    )(
        projected, projected, projected, projected, states, states,
        tables["meta"], tables["segment_row"], tables["taps"], tables["head"], tables["skip"],
    )


def scan_backward(projected, states, tables, scanned, carried, mixed_grad, query_grad):
    tokens, width = projected.shape
    channels = tables["taps"].shape[1]
    blocks = tokens // SSD_BLOCK
    order = lambda i: blocks - 1 - i
    back = lambda i: (blocks - 1 - i, 0)
    return pl.pallas_call(
        scan_backward_kernel,
        grid=(blocks,),
        in_specs=scan_specs(tokens, channels, width, order)
        + [
            pl.BlockSpec((SSD_BLOCK, channels), back),
            pl.BlockSpec((1, NSTATE, channels), lambda i: (blocks - 1 - i, 0, 0)),
            pl.BlockSpec((SSD_BLOCK, channels), back),
            pl.BlockSpec((SSD_BLOCK, query_grad.shape[1]), back),
        ],
        out_specs=[
            pl.BlockSpec((SSD_BLOCK, width), back),
            pl.BlockSpec((SSD_BLOCK, 2 * NSTATE), back),
        ],
        out_shape=[
            jax.ShapeDtypeStruct((tokens, width), BFLOAT),
            jax.ShapeDtypeStruct((tokens, 2 * NSTATE), BFLOAT),
        ],
        scratch_shapes=[pltpu.VMEM((NSTATE, channels), FLOAT), pltpu.VMEM((8, channels), FLOAT)],
        compiler_params=pltpu.CompilerParams(vmem_limit_bytes=VMEM_BYTES),
        cost_estimate=scan_cost(tokens, channels, 2),
        name="scan_backward",
    )(
        projected, projected, projected, projected, states, states,
        tables["meta"], tables["segment_row"], tables["taps"], tables["head"], tables["skip"],
        scanned, carried, mixed_grad, query_grad,
    )


def turned(values, cosine, sine):
    return (values * cosine + pltpu.roll(values, HEAD_SIZE // 2, 1) * sine).astype(BFLOAT)


def turned_back(values, cosine, sine):
    return values * cosine + pltpu.roll(values * sine, HEAD_SIZE // 2, 1)


ATT_ROWS = 256


def attention_mask(meta_ref, segment_ref, start, extent):
    row = start + lax.broadcasted_iota(jnp.int32, (ATT_ROWS, extent), 0)
    column = lax.broadcasted_iota(jnp.int32, (ATT_ROWS, extent), 1)
    return (row >= column) & (meta_ref[start : start + ATT_ROWS, 0:1] == segment_ref[0:1, :extent])


def probabilities(query, keys, allowed):
    score = dot(query, keys, (1, 1)) * (1.0 / math.sqrt(HEAD_SIZE))
    score = jnp.where(allowed, score, NEGATIVE)
    exponent = jnp.exp(score - jnp.max(score, axis=1, keepdims=True))
    return exponent / jnp.sum(exponent, axis=1, keepdims=True)


def attention_forward_kernel(query_ref, key_ref, value_ref, cosine_ref, sine_ref, meta_ref, segment_ref, out_ref, keys):
    tokens = key_ref.shape[0]
    keys[...] = turned(key_ref[...].astype(FLOAT), cosine_ref[...], sine_ref[...])
    for start in range(0, tokens, ATT_ROWS):
        extent = start + ATT_ROWS
        here = slice(start, extent)
        allowed = attention_mask(meta_ref, segment_ref, start, extent)
        for unit in range(query_ref.shape[1] // HEAD_SIZE):
            span = slice(unit * HEAD_SIZE, (unit + 1) * HEAD_SIZE)
            query = turned(query_ref[here, span].astype(FLOAT), cosine_ref[here], sine_ref[here])
            weights = probabilities(query, keys[:extent], allowed).astype(BFLOAT)
            out_ref[here, span] = dot(weights, value_ref[:extent], (1, 0)).astype(BFLOAT)


def attention_backward_kernel(
    query_ref, key_ref, value_ref, cosine_ref, sine_ref, meta_ref, segment_ref, grad_ref,
    query_grad_ref, key_grad_ref, value_grad_ref, keys, key_sum, value_sum,
):
    tokens = key_ref.shape[0]
    scale = 1.0 / math.sqrt(HEAD_SIZE)
    keys[...] = turned(key_ref[...].astype(FLOAT), cosine_ref[...], sine_ref[...])
    key_sum[...] = jnp.zeros_like(key_sum)
    value_sum[...] = jnp.zeros_like(value_sum)
    for start in range(0, tokens, ATT_ROWS):
        extent = start + ATT_ROWS
        here = slice(start, extent)
        allowed = attention_mask(meta_ref, segment_ref, start, extent)
        for unit in range(query_ref.shape[1] // HEAD_SIZE):
            span = slice(unit * HEAD_SIZE, (unit + 1) * HEAD_SIZE)
            query = turned(query_ref[here, span].astype(FLOAT), cosine_ref[here], sine_ref[here])
            weights = probabilities(query, keys[:extent], allowed)
            grad = grad_ref[here, span]
            weights_grad = dot(grad, value_ref[:extent], (1, 1))
            value_sum[:extent] += dot(weights.astype(BFLOAT), grad, (0, 0))
            mean_grad = jnp.sum(weights * weights_grad, axis=1, keepdims=True)
            score_grad = (weights * (weights_grad - mean_grad) * scale).astype(BFLOAT)
            query_grad = dot(score_grad, keys[:extent], (1, 0))
            key_sum[:extent] += dot(score_grad, query, (0, 0))
            query_grad_ref[here, span] = turned_back(query_grad, cosine_ref[here], sine_ref[here]).astype(BFLOAT)
    key_grad_ref[...] = turned_back(key_sum[...], cosine_ref[...], sine_ref[...]).astype(BFLOAT)
    value_grad_ref[...] = value_sum[...].astype(BFLOAT)


def attention_cost(tokens, width, factor):
    return pl.CostEstimate(
        flops=factor * 2 * tokens * tokens * width,
        bytes_accessed=factor * tokens * width * 8,
        transcendentals=tokens * tokens * width // (2 * HEAD_SIZE),
    )


def attention_specs(projected, channels, units):
    tokens = projected.shape[0]
    query_width = units * HEAD_SIZE
    narrow = whole((tokens, HEAD_SIZE))
    return [
        pl.BlockSpec((tokens, query_width), lambda *_: (0, 2 * channels // query_width)),
        narrow,
        narrow,
        narrow,
        narrow,
        whole((tokens, LANES)),
        whole((8, tokens)),
    ]


def attention_forward(projected, keys, values, tables):
    tokens = projected.shape[0]
    channels = tables["taps"].shape[1]
    units = channels // (DSSM // QUERY_HEADS)
    width = units * HEAD_SIZE
    return pl.pallas_call(
        attention_forward_kernel,
        grid=(1,),
        in_specs=attention_specs(projected, channels, units),
        out_specs=whole((tokens, width)),
        out_shape=jax.ShapeDtypeStruct((tokens, width), BFLOAT),
        scratch_shapes=[pltpu.VMEM((tokens, HEAD_SIZE), BFLOAT)],
        compiler_params=pltpu.CompilerParams(vmem_limit_bytes=VMEM_BYTES),
        cost_estimate=attention_cost(tokens, width, 1),
        name="attention_forward",
    )(projected, keys, values, tables["cosine"], tables["sine"], tables["meta"], tables["segment_row"])


def attention_backward(projected, keys, values, tables, mixed_grad):
    tokens = projected.shape[0]
    channels = tables["taps"].shape[1]
    units = channels // (DSSM // QUERY_HEADS)
    width = units * HEAD_SIZE
    narrow = whole((tokens, HEAD_SIZE))
    return pl.pallas_call(
        attention_backward_kernel,
        grid=(1,),
        in_specs=attention_specs(projected, channels, units)
        + [pl.BlockSpec((tokens, width), lambda *_: (0, channels // width))],
        out_specs=[whole((tokens, width)), narrow, narrow],
        out_shape=[
            jax.ShapeDtypeStruct((tokens, width), BFLOAT),
            jax.ShapeDtypeStruct((tokens, HEAD_SIZE), BFLOAT),
            jax.ShapeDtypeStruct((tokens, HEAD_SIZE), BFLOAT),
        ],
        scratch_shapes=[
            pltpu.VMEM((tokens, HEAD_SIZE), BFLOAT),
            pltpu.VMEM((tokens, HEAD_SIZE), FLOAT),
            pltpu.VMEM((tokens, HEAD_SIZE), FLOAT),
        ],
        compiler_params=pltpu.CompilerParams(vmem_limit_bytes=VMEM_BYTES),
        cost_estimate=attention_cost(tokens, width, 3),
        name="attention_backward",
    )(
        projected, keys, values, tables["cosine"], tables["sine"], tables["meta"], tables["segment_row"], mixed_grad
    )


def mixer_tables(lengths, segment, position, conv_values, scan_params):
    tokens = segment.shape[0]
    block = jnp.arange(tokens, dtype=jnp.int32) // SSD_BLOCK
    previous = jnp.concatenate([jnp.full((1,), -1, jnp.int32), segment[:-1]])
    first_previous = jnp.repeat(previous[::SSD_BLOCK], SSD_BLOCK)
    last_segment = jnp.repeat(segment[SSD_BLOCK - 1 :: SSD_BLOCK], SSD_BLOCK)
    length = jnp.sum(
        jnp.where(segment[:, None] == jnp.arange(lengths.shape[0], dtype=jnp.int32)[None, :], lengths[None, :], 0),
        axis=1,
    )
    columns = [
        segment,
        position,
        length - 1 - position,
        segment == first_previous,
        segment == last_segment,
    ]
    meta = jnp.stack([column.astype(FLOAT) for column in columns], axis=1)
    half_width = HEAD_SIZE // 2
    frequency = ROPE_BASE ** (-2.0 * jnp.arange(half_width, dtype=FLOAT) / HEAD_SIZE)
    angle = position.astype(FLOAT)[:, None] * frequency[None, :]
    cosine, sine = jnp.cos(angle), jnp.sin(angle)
    heads = scan_params.shape[1]
    head = jnp.stack([scan_params[0], -jnp.exp(scan_params[1]), scan_params[2]])
    return dict(
        meta=jnp.pad(meta, ((0, 0), (0, LANES - meta.shape[1]))),
        segment_row=jnp.broadcast_to(segment.astype(FLOAT)[None, :], (8, tokens)),
        taps=jnp.pad(conv_values.astype(FLOAT), ((0, 3), (0, 0))),
        head=jnp.pad(head, ((0, 5), (0, LANES - heads))),
        skip=jnp.broadcast_to(jnp.repeat(scan_params[2], HP)[None, :], (8, heads * HP)),
        cosine=jnp.concatenate([cosine, cosine], axis=1),
        sine=jnp.concatenate([-sine, sine], axis=1),
    )


GATE_WIDTH = DSSM // QUERY_HEADS
PAIR_WIDTH = 2 * KEY_VALUE_HEADS * HEAD_SIZE // QUERY_HEADS
STATE_WIDTH = 2 * NSTATE // QUERY_HEADS
STEP_WIDTH = NH // QUERY_HEADS
ALL_AXES = ("row", "col")


def pad_columns(values, width):
    return jnp.pad(values, ((0, 0), (0, width - values.shape[1])))


def align_units(values, units):
    cuts = [0, GATE_WIDTH, 2 * GATE_WIDTH, 2 * GATE_WIDTH + HEAD_SIZE]
    cuts += [cuts[-1] + PAIR_WIDTH, cuts[-1] + PAIR_WIDTH + STATE_WIDTH, UNIT_IN]
    parts = [
        values[:, unit * UNIT_IN + low : unit * UNIT_IN + high]
        for low, high in zip(cuts[:-1], cuts[1:])
        for unit in range(units)
    ]
    joined = jnp.concatenate(parts, axis=1)
    return pad_columns(joined, -(-joined.shape[1] // LANES) * LANES)


def restore_units(values, units):
    widths = [GATE_WIDTH, GATE_WIDTH, HEAD_SIZE, PAIR_WIDTH, STATE_WIDTH, STEP_WIDTH]
    parts = []
    for unit in range(units):
        start = 0
        for width in widths:
            parts.append(values[:, start + unit * width : start + (unit + 1) * width])
            start += units * width
    return jnp.concatenate(parts, axis=1)


def split_halves(values, units, first, axis):
    block = values.shape[axis] // units
    take = lambda low, high: lax.slice_in_dim(values, low, high, axis=axis)
    parts = [take(unit * block, unit * block + first) for unit in range(units)]
    parts += [take(unit * block + first, (unit + 1) * block) for unit in range(units)]
    return jnp.concatenate(parts, axis=axis)


def join_halves(values, units, first, axis):
    block = values.shape[axis] // units
    rest = block - first
    take = lambda low, high: lax.slice_in_dim(values, low, high, axis=axis)
    parts = []
    for unit in range(units):
        parts.append(take(unit * first, (unit + 1) * first))
        parts.append(take(units * first + unit * rest, units * first + (unit + 1) * rest))
    return jnp.concatenate(parts, axis=axis)


def flip(values, mask):
    return lax.ppermute(values, "col", [(i, i ^ mask) for i in range(4)])


def gather_blocks(own):
    col = lax.axis_index("col")
    half = own.shape[-1] // 2
    near = flip(own, 1)
    far = flip(own, 2)
    corner = jnp.concatenate([flip(far[..., :half], 1), flip(near[..., half:], 2)], axis=-1)
    return [(col, own), (col ^ 1, near), (col ^ 2, far), (col ^ 3, corner)]


def reduce_blocks(piece):
    col = lax.axis_index("col")
    wide = lambda values: values.astype(FLOAT)
    send = lambda values, mask: flip(values.astype(BFLOAT), mask)
    corner_a = send(piece(col ^ 3, 0), 1)
    corner_b = send(piece(col ^ 3, 1), 2)
    near_a = send(piece(col ^ 1, 0), 1)
    far_b = send(piece(col ^ 2, 1), 2)
    far_a = send(piece(col ^ 2, 0) + wide(corner_a), 2)
    near_b = send(piece(col ^ 1, 1) + wide(corner_b), 1)
    first = piece(col, 0) + wide(near_a) + wide(far_a)
    second = piece(col, 1) + wide(far_b) + wide(near_b)
    return first, second


def rows_of(values, block, rows):
    return lax.dynamic_slice_in_dim(values, block * rows, rows, 0)


def spread_project(own, wide, narrow_factor, selector):
    rows = own.shape[0]
    width = narrow_factor.shape[1]

    def project(values, chosen):
        both = product(values, wide)
        narrow = (chosen * both[:, width:]).astype(BFLOAT)
        return (both[:, :width] + product(narrow, narrow_factor)).astype(BFLOAT), narrow

    if lax.axis_size("col") != 4:
        return project(lax.all_gather(own, "col", axis=0, tiled=True), selector)
    total = rows * 4
    result = jnp.zeros((total, width), BFLOAT)
    narrow_result = jnp.zeros((total, LANES), BFLOAT)
    for block, values in gather_blocks(own):
        part, narrow = project(values, rows_of(selector, block, rows))
        result = lax.dynamic_update_slice_in_dim(result, part, block * rows, 0)
        narrow_result = lax.dynamic_update_slice_in_dim(narrow_result, narrow, block * rows, 0)
    return result, narrow_result


def collect_project(values, wide, narrow_factor, own_selector):
    rows = own_selector.shape[0]
    width = narrow_factor.shape[1]
    model = wide.shape[0]
    weight = wide[:, :width]
    if lax.axis_size("col") != 4:
        partial = jnp.concatenate(
            [contract_last(values, weight), contract_last(values, narrow_factor)], axis=1
        ).astype(BFLOAT)
        summed = lax.psum_scatter(partial, "col", scatter_dimension=0, tiled=True).astype(FLOAT)
        base, narrow = summed[:, :model], summed[:, model:]
    else:
        half = model // 2

        def piece(block, side):
            taken = rows_of(values, block, rows)
            if side:
                return contract_last(taken, weight[half:])
            return jnp.concatenate(
                [contract_last(taken, weight[:half]), contract_last(taken, narrow_factor)], axis=1
            )

        first, second = reduce_blocks(piece)
        base = jnp.concatenate([first[:, :half], second], axis=1)
        narrow = first[:, half:]
    inner = (own_selector * narrow).astype(BFLOAT)
    return base + contract_last(inner, wide[:, width:]), inner


def local(
    tokens_in,
    cotangent,
    target,
    sequence_lengths,
    sequence_adapter,
    norm_gains,
    weight_in,
    conv_values,
    conv_states,
    scan_params,
    weight_mix,
    weight_feed,
    weight_down,
    in_lower,
    in_raise,
    mix_lower,
    mix_raise,
    feed_lower,
    feed_raise,
    down_lower,
    down_raise,
):
    cols = lax.axis_size("col")
    rows_axis = lax.axis_size("row")
    col = lax.axis_index("col")
    devices = cols * rows_axis
    rows = tokens_in.shape[0]
    model = tokens_in.shape[1]
    total = rows * cols
    units = QUERY_HEADS // cols
    heads = units * STEP_WIDTH
    peer = rows // devices
    lengths, adapters = sequence_lengths[0], sequence_adapter[0]
    sequences = lengths.shape[0]

    gather = lambda values: lax.all_gather(values, "row", axis=0, tiled=True)
    wide_in = gather(jnp.concatenate([align_units(weight_in, units), in_lower], axis=1))
    small_parts = [
        align_units(in_raise, units),
        split_halves(mix_lower, units, GATE_WIDTH, 0).T,
        split_halves(feed_raise, units, UNIT_FF, 1),
        down_lower.T,
    ]
    small_cuts = [0]
    for part in small_parts:
        small_cuts.append(small_cuts[-1] + part.shape[1])
    small = gather(jnp.concatenate(small_parts, axis=1))
    narrow_in, narrow_mix, narrow_feed, narrow_down = [
        small[:, low:high] for low, high in zip(small_cuts[:-1], small_cuts[1:])
    ]
    wide_mix = gather(
        jnp.concatenate([split_halves(weight_mix, units, GATE_WIDTH, 0), mix_raise], axis=0).T
    )
    wide_feed = gather(
        jnp.concatenate([split_halves(weight_feed, units, UNIT_FF, 1), feed_lower], axis=1)
    )
    wide_down = gather(jnp.concatenate([weight_down, down_raise], axis=0).T)

    destination = target // rows
    index = jnp.arange(rows, dtype=jnp.int32)
    same = (destination[:, None] == destination[None, :]) & (index[None, :] < index[:, None])
    place_sent = destination * peer + jnp.sum(same.astype(jnp.int32), axis=1)
    send_matrix = (index[:, None] == place_sent[None, :]).astype(BFLOAT)
    notes = jnp.concatenate([(target % rows)[:, None], jnp.broadcast_to(adapters[None, :], (rows, sequences))], axis=1)
    notes = pad_columns(notes.astype(BFLOAT), LANES)
    exchange = lambda values: lax.all_to_all(values, ALL_AXES, split_axis=0, concat_axis=0, tiled=True)
    arrived = exchange(product(send_matrix, jnp.concatenate([tokens_in, notes], axis=1)).astype(BFLOAT))
    arrived_grad = exchange(product(send_matrix, cotangent).astype(BFLOAT))
    arrived_slot = arrived[:, model].astype(jnp.int32)
    place_matrix = (index[:, None] == arrived_slot[None, :]).astype(BFLOAT)
    source_adapters = arrived[::peer, model + 1 : model + 1 + sequences].astype(jnp.int32)
    own_input = product(place_matrix, arrived[:, :model])
    branch_two = product(place_matrix, arrived_grad).astype(BFLOAT)
    own_upstream = branch_two.astype(FLOAT)

    segment, position, selector = sequence_tables(lengths, adapters, total)
    own_selector = rows_of(selector, col, rows)
    own_segment = rows_of(segment, col, rows)
    norm_gain = norm_gains.astype(FLOAT)

    def compact_grad(narrow, values):
        parts = [
            lax.dynamic_slice_in_dim(narrow, adapters[at] * RANK, RANK, 1)
            * (own_segment == at).astype(BFLOAT)[:, None]
            for at in range(sequences)
        ]
        grad = contract_first(jnp.concatenate(parts, axis=1), values).astype(BFLOAT)
        kept = sequences * RANK
        grad = grad.reshape(kept, devices, model // devices).transpose(1, 0, 2)
        return pad_columns(grad.reshape(devices, kept * model // devices), model)

    def expand_grad(dealt):
        kept = sequences * RANK
        dealt = dealt[:, : kept * model // devices].reshape(devices * kept, model // devices)
        adapter_row = (source_adapters[:, :, None] * RANK + jnp.arange(RANK, dtype=jnp.int32)).reshape(-1)
        chosen = (jnp.arange(NADAPT * RANK, dtype=jnp.int32)[:, None] == adapter_row[None, :]).astype(BFLOAT)
        return product(chosen, dealt)

    def send_back(values, grads):
        back = product(place_matrix.T, values.astype(BFLOAT)).astype(BFLOAT).reshape(devices, peer, model)
        joined = jnp.concatenate([back] + [grad[:, None, :] for grad in grads], axis=1)
        dealt = exchange(joined)
        returned = product(send_matrix.T, dealt[:, :peer].reshape(rows, model)).astype(BFLOAT)
        return returned, [expand_grad(dealt[:, peer + at]) for at in range(len(grads))]

    normed_one, norm_one_back = jax.vjp(lambda values: rms_norm(values, norm_gain[0]), own_input)
    normed_one = normed_one.astype(BFLOAT)
    projected, inner_in = spread_project(normed_one, wide_in, narrow_in, selector)
    cuts = [0]
    for width in (GATE_WIDTH, GATE_WIDTH, HEAD_SIZE, PAIR_WIDTH, STATE_WIDTH, STEP_WIDTH):
        cuts.append(cuts[-1] + units * width)
    gate_in, conv_in, query_in, pair_own, state_own, step_in = [
        projected[:, low:high] for low, high in zip(cuts[:-1], cuts[1:])
    ]
    conv_state_float = conv_states.astype(FLOAT)
    state_post, state_back = jax.vjp(
        lambda values: causal_conv(values, conv_state_float, position), state_own.astype(FLOAT)
    )
    shared = jnp.concatenate([pair_own, state_post.astype(BFLOAT)], axis=1)
    if cols == 4:
        held = jnp.zeros((cols,) + shared.shape, BFLOAT)
        for block, values in gather_blocks(shared):
            held = lax.dynamic_update_index_in_dim(held, values, block, 0)
    else:
        held = lax.all_gather(shared, "col", axis=0)
    pair_width = units * PAIR_WIDTH
    state_full = jnp.concatenate([held[at, :, pair_width:] for at in range(cols)], axis=1)
    pair_full = jnp.concatenate([held[at, :, :pair_width] for at in range(cols)], axis=1)
    key_head = col * units // (QUERY_HEADS // KEY_VALUE_HEADS)
    pick = lambda start: lax.select_n(
        key_head,
        *[pair_full[:, start + at * HEAD_SIZE : start + (at + 1) * HEAD_SIZE] for at in range(KEY_VALUE_HEADS)],
    )
    keys, values = pick(0), pick(KEY_VALUE_HEADS * HEAD_SIZE)
    tables = mixer_tables(lengths, segment, position, conv_values, scan_params)
    scan_out, scanned, carried = scan_forward(projected, state_full, tables)
    attended = attention_forward(projected, keys, values, tables)
    mixed_out = jnp.concatenate([scan_out, attended], axis=1)
    branch_sum, inner_out = collect_project(mixed_out, wide_mix, narrow_mix, own_selector)
    hidden = own_input + branch_sum
    normed_two, norm_two_back = jax.vjp(lambda values: rms_norm(values, norm_gain[1]), hidden)
    normed_two = normed_two.astype(BFLOAT)
    gate_up, inner_feed = spread_project(normed_two, wide_feed, narrow_feed, selector)
    act_grad, narrow_two = spread_project(branch_two, wide_down, narrow_down, selector)
    half_feed = units * UNIT_FF

    def swiglu(gate_part, up_part):
        return jax.nn.silu(gate_part) * up_part

    activated, swiglu_back = jax.vjp(
        swiglu, gate_up[:, :half_feed].astype(FLOAT), gate_up[:, half_feed:].astype(FLOAT)
    )
    activated = activated.astype(BFLOAT)
    feed_grad = jnp.concatenate(swiglu_back(act_grad.astype(FLOAT)), axis=1).astype(BFLOAT)
    normed_two_grad, narrow_three = collect_project(feed_grad, wide_feed, narrow_feed, own_selector)
    (hidden_from_norm,) = norm_two_back(normed_two_grad)
    hidden_grad = own_upstream + hidden_from_norm
    branch_one = hidden_grad.astype(BFLOAT)
    mixed_grad, narrow_one = spread_project(branch_one, wide_mix, narrow_mix, selector)

    down_sum, inner_down = collect_project(activated, wide_down, narrow_down, own_selector)
    block_out, (grad_down_raise, grad_feed_lower, grad_mix_raise) = send_back(
        hidden + down_sum,
        [
            compact_grad(inner_down, branch_two),
            compact_grad(narrow_three, normed_two),
            compact_grad(inner_out, branch_one),
        ],
    )

    def sum_rows(values):
        return lax.psum_scatter(values.astype(BFLOAT), "row", scatter_dimension=0, tiled=True).astype(FLOAT)

    early = sum_rows(
        jnp.concatenate(
            [
                contract_first(narrow_one, mixed_out),
                contract_first(inner_feed, feed_grad),
                contract_first(narrow_two, activated),
            ],
            axis=1,
        )
    )
    early_cuts = [cut - small_cuts[1] for cut in small_cuts[1:]]
    mix_lower_part, feed_raise_part, down_lower_part = [
        early[:, low:high] for low, high in zip(early_cuts[:-1], early_cuts[1:])
    ]
    grad_mix_lower = join_halves(mix_lower_part, units, GATE_WIDTH, 1).T
    grad_feed_raise = join_halves(feed_raise_part, units, UNIT_FF, 1)
    grad_down_lower = down_lower_part.T

    query_grad, key_grad, value_grad = attention_backward(projected, keys, values, tables, mixed_grad)
    projected_grad, state_grad = scan_backward(
        projected, state_full, tables, scanned, carried, mixed_grad, query_grad
    )
    mine = [(key_head == at).astype(BFLOAT) for at in range(KEY_VALUE_HEADS)]
    pair_grad = jnp.concatenate([grad * here for grad in (key_grad, value_grad) for here in mine], axis=1)
    state_width = units * STATE_WIDTH
    stacked = jnp.stack(
        [
            jnp.concatenate(
                [
                    pair_grad[:, at * pair_width : (at + 1) * pair_width],
                    state_grad[:, at * state_width : (at + 1) * state_width],
                ],
                axis=1,
            )
            for at in range(cols)
        ]
    )
    if cols == 4:
        part = total // 2
        shared_grad = jnp.concatenate(
            reduce_blocks(
                lambda block, side: lax.dynamic_index_in_dim(stacked, block, 0, False)[
                    side * part : (side + 1) * part
                ]
            ),
            axis=0,
        )
    else:
        shared_grad = lax.psum_scatter(
            stacked.astype(BFLOAT).reshape(cols * total, -1), "col", scatter_dimension=0, tiled=True
        ).astype(FLOAT)
    (state_pre_grad,) = state_back(shared_grad[:, pair_width:])
    shared_back = jnp.concatenate([shared_grad[:, :pair_width], state_pre_grad], axis=1).astype(BFLOAT)
    projected_grad = lax.dynamic_update_slice(projected_grad, shared_back, (0, cuts[3]))
    grad_in_raise = restore_units(sum_rows(contract_first(inner_in, projected_grad)), units)
    normed_one_grad, narrow_four = collect_project(projected_grad, wide_in, narrow_in, own_selector)
    (input_from_norm,) = norm_one_back(normed_one_grad)
    input_grad, (grad_in_lower,) = send_back(
        hidden_grad + input_from_norm, [compact_grad(narrow_four, normed_one)]
    )
    return (
        block_out,
        input_grad,
        grad_in_lower.T,
        grad_in_raise,
        grad_mix_lower,
        grad_mix_raise,
        grad_feed_lower.T,
        grad_feed_raise,
        grad_down_lower,
        grad_down_raise,
    )


def solution(mesh):
    in_specs = (
        P(("row", "col"), None),
        P(("row", "col"), None),
        P(("row", "col")),
        P("row", None),
        P("row", None),
        P(),
        P("row", "col"),
        P(None, "col"),
        P(None, "col"),
        P(None, "col"),
        P("col", "row"),
        P("row", "col"),
        P("col", "row"),
        P("row", None),
        P("row", "col"),
        P("col", "row"),
        P(None, "row"),
        P("row", None),
        P("row", "col"),
        P("col", "row"),
        P(None, "row"),
    )
    out_specs = (
        P(("row", "col"), None),
        P(("row", "col"), None),
        P(("row", "col"), None),
        P("row", "col"),
        P("col", "row"),
        P(None, ("row", "col")),
        P(("row", "col"), None),
        P("row", "col"),
        P("col", "row"),
        P(None, ("row", "col")),
    )
    return jax.shard_map(local, mesh=mesh, in_specs=in_specs, out_specs=out_specs, check_vma=False)
```

```python
import functools
import math

import jax
import jax.numpy as jnp
from jax import lax
from jax.experimental import pallas as pl
from jax.experimental.pallas import tpu as pltpu
from jax.sharding import PartitionSpec as P

NH = 48
HP = 64
NSTATE = 256
KCONV = 4
QUERY_HEADS = 8
KEY_VALUE_HEADS = 2
HEAD_SIZE = 128
RANK = 16
NADAPT = 8
SSD_BLOCK = 256
DSSM = 3072
UNIT_IN = 1030
UNIT_FF = 512


EPSILON = 1e-05
ROPE_BASE = 10000.0
NEGATIVE = -1e30
FLOAT = jnp.float32
BFLOAT = jnp.bfloat16


def product(left, right):
    return jnp.dot(left, right, preferred_element_type=FLOAT)


def contract_last(left, right):
    return lax.dot_general(left, right, (((1,), (1,)), ((), ())), preferred_element_type=FLOAT)


def contract_first(left, right):
    return lax.dot_general(left, right, (((0,), (0,)), ((), ())), preferred_element_type=FLOAT)


def rms_norm(values, gain):
    return values * lax.rsqrt(jnp.mean(values * values, axis=-1, keepdims=True) + EPSILON) * gain


def sequence_tables(lengths, adapters, sequence_length):
    sequence_count = lengths.shape[0]
    boundary = jnp.cumsum(lengths)
    token_index = jnp.arange(sequence_length, dtype=jnp.int32)
    passed = (token_index[:, None] >= boundary[None, :]).astype(jnp.int32)
    segment = jnp.sum(passed, axis=1)
    segment_start = jnp.sum(passed * lengths[None, :], axis=1)
    position = token_index - segment_start
    member = (segment[:, None] == jnp.arange(sequence_count, dtype=jnp.int32)[None, :]).astype(
        jnp.int32
    )
    chosen = jnp.sum(member * adapters[None, :], axis=1)
    column = jnp.arange(NADAPT * RANK, dtype=jnp.int32) // RANK
    selector = (chosen[:, None] == column[None, :]).astype(FLOAT)
    return (segment, position, selector)


SCAN_BYTES = 32 * 1024 * 1024
DENSE_BYTES = 16 * 1024 * 1024
LANES = 128


def whole(shape):
    return pl.BlockSpec(shape, lambda *_: (0,) * len(shape))


def dot(left, right, contract):
    return lax.dot_general(left, right, ((contract[:1], contract[1:]), ((), ())), preferred_element_type=FLOAT)


def parts_of(values, count):
    parts = []
    for _ in range(count):
        part = values.astype(BFLOAT)
        parts.append(part)
        values = values - part.astype(FLOAT)
    return parts


def running_sum(values, triangle, contract):
    width = values.shape[1]
    split = dot(triangle, jnp.concatenate(parts_of(values, 3), axis=1), contract)
    return split[:, :width] + split[:, width : 2 * width] + split[:, 2 * width :]


def head_spread(values, expand):
    return dot(jnp.concatenate(parts_of(values, 2), axis=1), expand, (1, 0))


def head_sum(values, expand):
    high, low = parts_of(values, 2)
    single = expand[:LANES]
    return dot(high, single, (1, 1)) + dot(low, single, (1, 1))


def silu_parts(values):
    gate = 1.0 / (1.0 + jnp.exp(-values))
    return values * gate, gate


def expand_table(channels):
    row = lax.broadcasted_iota(jnp.int32, (2 * LANES, channels), 0) % LANES
    channel = lax.broadcasted_iota(jnp.int32, (2 * LANES, channels), 1) // HP
    return (row == channel).astype(BFLOAT)


def conv_sum(current_ref, before_ref, taps_ref, meta):
    rows = SSD_BLOCK
    current = current_ref[...].astype(FLOAT)
    window = jnp.concatenate([before_ref[...].astype(FLOAT)[8:16], current], axis=0)
    summed = taps_ref[KCONV : KCONV + 1, :] + current * taps_ref[0:1, :]
    for lag in range(1, KCONV):
        shifted = window[8 - lag : 8 - lag + rows]
        summed = summed + jnp.where(meta[:, 1:2] >= lag, shifted, 0.0) * taps_ref[lag : lag + 1, :]
    return summed


def conv_back(summed_grad, later, taps_ref, meta):
    rows = SSD_BLOCK
    window = jnp.concatenate([summed_grad, later[...]], axis=0)
    grad = summed_grad * taps_ref[0:1, :]
    for lag in range(1, KCONV):
        grad = grad + jnp.where(meta[:, 2:3] >= lag, window[lag : lag + rows], 0.0) * taps_ref[lag : lag + 1, :]
    later[...] = summed_grad[:8]
    return grad


def silu_slope(values, gate):
    return gate * (1.0 + values * (1.0 - gate))


def scan_block(
    conv_ref, before_ref, state_ref, state_before_ref, step_ref, meta_ref, segment_ref, taps_ref, state_taps_ref, head_ref
):
    rows = SSD_BLOCK
    channels = conv_ref.shape[1]
    meta = meta_ref[...]
    summed = conv_sum(conv_ref, before_ref, taps_ref, meta)
    activated, conv_gate = silu_parts(summed)
    wide_inputs = activated.astype(BFLOAT).astype(FLOAT)
    state_summed = conv_sum(state_ref, state_before_ref, state_taps_ref, meta)
    state_values, state_gate = silu_parts(state_summed)
    write = state_values[:, :NSTATE].astype(BFLOAT)
    read = state_values[:, NSTATE:].astype(BFLOAT)
    raw = step_ref[...].astype(FLOAT) + head_ref[0:1, :]
    steps = jnp.maximum(raw, 0.0) + jnp.log1p(jnp.exp(-jnp.abs(raw)))
    row = lax.broadcasted_iota(jnp.int32, (rows, rows), 0)
    column = lax.broadcasted_iota(jnp.int32, (rows, rows), 1)
    triangle = (row >= column).astype(BFLOAT)
    total = running_sum(steps * head_ref[1:2, :], triangle, (1, 0))
    entered = jnp.exp(total) * meta[:, 3:4]
    leaving = jnp.exp(total[rows - 1 : rows] - total) * meta[:, 4:5]
    expand = expand_table(channels)
    spread = head_spread(jnp.concatenate([steps, entered, leaving * steps], axis=0), expand)
    blocked = jnp.where((row >= column) & (meta[:, 0:1] == segment_ref[0:1, :]), 0.0, NEGATIVE)
    return dict(
        summed=summed,
        conv_gate=conv_gate,
        state_summed=state_summed,
        state_gate=state_gate,
        write=write,
        read=read,
        wide_inputs=wide_inputs,
        raw=raw,
        steps=steps,
        triangle=triangle,
        total=total,
        total_rows=total.T,
        leaving=leaving,
        expand=expand,
        steps_wide=spread[:rows],
        entered_wide=spread[rows : 2 * rows],
        tail_wide=spread[2 * rows :],
        stepped=(wide_inputs * spread[:rows]).astype(BFLOAT),
        tailed=(wide_inputs * spread[2 * rows :]).astype(BFLOAT),
        blocked=blocked,
        crossing=dot(read, write, (1, 1)),
    )


def decay_of(block, head):
    return jnp.exp(
        block["total"][:, head : head + 1] - block["total_rows"][head : head + 1, :] + block["blocked"]
    )


def scan_forward_kernel(
    gate_ref, conv_ref, before_ref, state_ref, state_before_ref, step_ref, meta_ref, segment_ref, taps_ref,
    state_taps_ref, head_ref, skip_ref, mixed_ref, out_ref, scanned_ref, states_ref, state,
):
    del mixed_ref

    @pl.when(pl.program_id(0) == 0)
    def _():
        state[...] = jnp.zeros_like(state)

    block = scan_block(
        conv_ref, before_ref, state_ref, state_before_ref, step_ref, meta_ref, segment_ref, taps_ref, state_taps_ref,
        head_ref,
    )
    heads = conv_ref.shape[1] // HP
    carried = state[...].astype(BFLOAT)
    states_ref[0] = carried
    across = dot(block["read"], carried, (1, 0)) * block["entered_wide"]
    within = []
    for head in range(heads):
        weights = (block["crossing"] * decay_of(block, head)).astype(BFLOAT)
        within.append(dot(weights, block["stepped"][:, head * HP : (head + 1) * HP], (1, 0)))
    scanned = across + jnp.concatenate(within, axis=1)
    scanned_ref[...] = scanned
    gated, _ = silu_parts(gate_ref[...].astype(FLOAT))
    out_ref[...] = ((scanned + skip_ref[0:1, :] * block["wide_inputs"]) * gated).astype(BFLOAT)
    state[...] = state[...] * block["entered_wide"][SSD_BLOCK - 1 : SSD_BLOCK, :] + dot(
        block["write"], block["tailed"], (0, 0)
    )


def scan_backward_kernel(
    gate_ref, conv_ref, before_ref, state_ref, state_before_ref, step_ref, meta_ref, segment_ref, taps_ref,
    state_taps_ref, head_ref, skip_ref, scanned_ref, states_ref, grad_ref, query_grad_ref, key_grad_ref,
    value_grad_ref, out_ref, state_grad, later, state_later,
):
    @pl.when(pl.program_id(0) == 0)
    def _():
        state_grad[...] = jnp.zeros_like(state_grad)
        later[...] = jnp.zeros_like(later)
        state_later[...] = jnp.zeros_like(state_later)

    block = scan_block(
        conv_ref, before_ref, state_ref, state_before_ref, step_ref, meta_ref, segment_ref, taps_ref, state_taps_ref,
        head_ref,
    )
    rows = SSD_BLOCK
    channels = conv_ref.shape[1]
    heads = channels // HP
    meta = meta_ref[...]
    read, write = block["read"], block["write"]
    inputs = block["wide_inputs"]
    scanned = scanned_ref[...]
    skip = skip_ref[0:1, :]
    gate_values = gate_ref[...].astype(FLOAT)
    gated, gate = silu_parts(gate_values)
    grad = grad_ref[...].astype(FLOAT)
    gate_grad = grad * (scanned + skip * inputs) * silu_slope(gate_values, gate)
    out_grad = grad * gated
    inputs_grad = skip * out_grad
    rounded = out_grad.astype(BFLOAT)
    wide_rounded = rounded.astype(FLOAT)
    carried = states_ref[0]
    after = state_grad[...]
    after_rounded = after.astype(BFLOAT)

    from_state = dot(write, after_rounded, (1, 0))
    entering = (wide_rounded * block["entered_wide"]).astype(BFLOAT)
    write_grad = dot(block["tailed"], after_rounded, (1, 1))
    read_grad = dot(entering, carried, (1, 1))
    last_entered = block["entered_wide"][rows - 1 : rows, :]
    through = jnp.sum(after * carried.astype(FLOAT), axis=0, keepdims=True) * last_entered
    state_grad[...] = after * last_entered + dot(read, entering, (0, 0))

    crossing_grad = jnp.zeros((rows, rows), FLOAT)
    pulled = []
    for head in range(heads):
        span = slice(head * HP, (head + 1) * HP)
        decay = decay_of(block, head)
        weights = (block["crossing"] * decay).astype(BFLOAT)
        pulled.append(dot(weights, rounded[:, span], (0, 0)))
        crossing_grad = crossing_grad + dot(rounded[:, span], block["stepped"][:, span], (1, 1)) * decay
    pulled = jnp.concatenate(pulled, axis=1)
    crossing_rounded = crossing_grad.astype(BFLOAT)
    read_grad = read_grad + dot(crossing_rounded, write, (1, 0))
    write_grad = write_grad + dot(crossing_rounded, read, (0, 0))

    inputs_grad = inputs_grad + block["steps_wide"] * pulled + block["tail_wide"] * from_state
    sums = head_sum(
        jnp.concatenate(
            [
                wide_rounded * scanned - block["stepped"].astype(FLOAT) * pulled,
                inputs * pulled,
                inputs * from_state,
                jnp.broadcast_to(through, (8, channels)),
            ],
            axis=0,
        ),
        block["expand"],
    )
    leaving_grad = sums[2 * rows : 3 * rows] * block["leaving"]
    leaving_total = leaving_grad * block["steps"]
    last = sums[3 * rows : 3 * rows + 1] + jnp.sum(leaving_total, axis=0, keepdims=True)
    total_grad = sums[:rows] - leaving_total
    total_grad = total_grad + jnp.where(
        lax.broadcasted_iota(jnp.int32, total_grad.shape, 0) == rows - 1, last, 0.0
    )
    decay_grad = running_sum(total_grad, block["triangle"], (0, 0))
    steps_grad = sums[rows : 2 * rows] + leaving_grad + decay_grad * head_ref[1:2, :]
    raw_grad = steps_grad / (1.0 + jnp.exp(-block["raw"]))
    raw_grad = jnp.where(lax.broadcasted_iota(jnp.int32, raw_grad.shape, 1) < heads, raw_grad, 0.0)

    state_slope = silu_slope(block["state_summed"], block["state_gate"])
    state_pre = conv_back(
        jnp.concatenate([write_grad, read_grad], axis=1) * state_slope, state_later, state_taps_ref, meta
    )
    conv_pre = conv_back(inputs_grad * silu_slope(block["summed"], block["conv_gate"]), later, taps_ref, meta)
    start = 0
    for values in (
        state_pre, key_grad_ref[...], value_grad_ref[...], gate_grad, conv_pre, query_grad_ref[...], raw_grad
    ):
        out_ref[:, start : start + values.shape[1]] = values.astype(BFLOAT)
        start += values.shape[1]


STATES = 2 * NSTATE
PAIR = 2 * HEAD_SIZE


def scan_specs(channels, order):
    half = SSD_BLOCK // 16
    before = lambda i: jnp.maximum(order(i) * half - 1, 0)
    gate_at = (STATES + PAIR) // channels
    step_at = (STATES + PAIR + 2 * channels + channels * QUERY_HEADS // DSSM * HEAD_SIZE) // LANES
    return [
        pl.BlockSpec((SSD_BLOCK, channels), lambda i: (order(i), gate_at)),
        pl.BlockSpec((SSD_BLOCK, channels), lambda i: (order(i), gate_at + 1)),
        pl.BlockSpec((16, channels), lambda i: (before(i), gate_at + 1)),
        pl.BlockSpec((SSD_BLOCK, STATES), lambda i: (order(i), 0)),
        pl.BlockSpec((16, STATES), lambda i: (before(i), 0)),
        pl.BlockSpec((SSD_BLOCK, LANES), lambda i: (order(i), step_at)),
        pl.BlockSpec((SSD_BLOCK, LANES), lambda i: (order(i), 0)),
        pl.BlockSpec((8, SSD_BLOCK), lambda i: (0, order(i))),
        whole((8, channels)),
        whole((8, STATES)),
        whole((8, LANES)),
        whole((8, channels)),
    ]


def scan_operands(projected, tables):
    return [projected] * 6 + [
        tables[name] for name in ("meta", "segment_row", "taps", "state_taps", "head", "skip")
    ]


def scan_cost(tokens, channels, factor):
    heads = channels // HP
    return pl.CostEstimate(
        flops=factor * 2 * tokens * SSD_BLOCK * (3 * channels + NSTATE),
        bytes_accessed=factor * tokens * channels * 12,
        transcendentals=tokens * SSD_BLOCK * heads,
    )


def scan_forward(projected, tables, mixed):
    tokens = projected.shape[0]
    channels = tables["taps"].shape[1]
    blocks = tokens // SSD_BLOCK
    return pl.pallas_call(
        scan_forward_kernel,
        grid=(blocks,),
        in_specs=scan_specs(channels, lambda i: i) + [pl.BlockSpec(memory_space=pl.ANY)],
        out_specs=[
            pl.BlockSpec((SSD_BLOCK, channels), lambda i: (i, 0)),
            pl.BlockSpec((SSD_BLOCK, channels), lambda i: (i, 0)),
            pl.BlockSpec((1, NSTATE, channels), lambda i: (i, 0, 0)),
        ],
        out_shape=[
            jax.ShapeDtypeStruct(mixed.shape, BFLOAT),
            jax.ShapeDtypeStruct((tokens, channels), FLOAT),
            jax.ShapeDtypeStruct((blocks, NSTATE, channels), BFLOAT),
        ],
        scratch_shapes=[pltpu.VMEM((NSTATE, channels), FLOAT)],
        input_output_aliases={12: 0},
        compiler_params=pltpu.CompilerParams(vmem_limit_bytes=SCAN_BYTES),
        cost_estimate=scan_cost(tokens, channels, 1),
        name="scan_forward",
    )(*scan_operands(projected, tables), mixed)


def scan_backward(projected, tables, scanned, carried, mixed_grad, query_grad, key_grad, value_grad):
    tokens, width = projected.shape
    channels = tables["taps"].shape[1]
    blocks = tokens // SSD_BLOCK
    back = lambda i: (blocks - 1 - i, 0)
    return pl.pallas_call(
        scan_backward_kernel,
        grid=(blocks,),
        in_specs=scan_specs(channels, lambda i: blocks - 1 - i)
        + [
            pl.BlockSpec((SSD_BLOCK, channels), back),
            pl.BlockSpec((1, NSTATE, channels), lambda i: (blocks - 1 - i, 0, 0)),
            pl.BlockSpec((SSD_BLOCK, channels), back),
            pl.BlockSpec((SSD_BLOCK, query_grad.shape[1]), back),
            pl.BlockSpec((SSD_BLOCK, HEAD_SIZE), back),
            pl.BlockSpec((SSD_BLOCK, HEAD_SIZE), back),
        ],
        out_specs=pl.BlockSpec((SSD_BLOCK, width), back),
        out_shape=jax.ShapeDtypeStruct((tokens, width), BFLOAT),
        scratch_shapes=[
            pltpu.VMEM((NSTATE, channels), FLOAT),
            pltpu.VMEM((8, channels), FLOAT),
            pltpu.VMEM((8, STATES), FLOAT),
        ],
        compiler_params=pltpu.CompilerParams(vmem_limit_bytes=SCAN_BYTES),
        cost_estimate=scan_cost(tokens, channels, 2),
        name="scan_backward",
    )(*scan_operands(projected, tables), scanned, carried, mixed_grad, query_grad, key_grad, value_grad)


def turned(values, cosine, sine):
    return (values * cosine + pltpu.roll(values, HEAD_SIZE // 2, 1) * sine).astype(BFLOAT)


def turned_back(values, cosine, sine):
    return values * cosine + pltpu.roll(values * sine, HEAD_SIZE // 2, 1)


ATT_ROWS = 256


def attention_mask(meta_ref, segment_ref, start, extent):
    row = start + lax.broadcasted_iota(jnp.int32, (ATT_ROWS, extent), 0)
    column = lax.broadcasted_iota(jnp.int32, (ATT_ROWS, extent), 1)
    return (row >= column) & (meta_ref[start : start + ATT_ROWS, 0:1] == segment_ref[0:1, :extent])


def probabilities(query, keys, allowed):
    score = dot(query, keys, (1, 1)) * (1.0 / math.sqrt(HEAD_SIZE))
    score = jnp.where(allowed, score, NEGATIVE)
    exponent = jnp.exp(score - jnp.max(score, axis=1, keepdims=True))
    return exponent / jnp.sum(exponent, axis=1, keepdims=True)


def attention_forward_kernel(query_ref, key_ref, value_ref, cosine_ref, sine_ref, meta_ref, segment_ref, out_ref, keys):
    tokens = key_ref.shape[0]
    keys[...] = turned(key_ref[...].astype(FLOAT), cosine_ref[...], sine_ref[...])
    for start in range(0, tokens, ATT_ROWS):
        extent = start + ATT_ROWS
        here = slice(start, extent)
        allowed = attention_mask(meta_ref, segment_ref, start, extent)
        for unit in range(query_ref.shape[1] // HEAD_SIZE):
            span = slice(unit * HEAD_SIZE, (unit + 1) * HEAD_SIZE)
            query = turned(query_ref[here, span].astype(FLOAT), cosine_ref[here], sine_ref[here])
            weights = probabilities(query, keys[:extent], allowed).astype(BFLOAT)
            out_ref[here, span] = dot(weights, value_ref[:extent], (1, 0)).astype(BFLOAT)


def attention_backward_kernel(
    query_ref, key_ref, value_ref, cosine_ref, sine_ref, meta_ref, segment_ref, grad_ref,
    query_grad_ref, key_grad_ref, value_grad_ref, keys, key_sum, value_sum,
):
    tokens = key_ref.shape[0]
    scale = 1.0 / math.sqrt(HEAD_SIZE)
    keys[...] = turned(key_ref[...].astype(FLOAT), cosine_ref[...], sine_ref[...])
    key_sum[...] = jnp.zeros_like(key_sum)
    value_sum[...] = jnp.zeros_like(value_sum)
    for start in range(0, tokens, ATT_ROWS):
        extent = start + ATT_ROWS
        here = slice(start, extent)
        allowed = attention_mask(meta_ref, segment_ref, start, extent)
        for unit in range(query_ref.shape[1] // HEAD_SIZE):
            span = slice(unit * HEAD_SIZE, (unit + 1) * HEAD_SIZE)
            query = turned(query_ref[here, span].astype(FLOAT), cosine_ref[here], sine_ref[here])
            weights = probabilities(query, keys[:extent], allowed)
            grad = grad_ref[here, span]
            weights_grad = dot(grad, value_ref[:extent], (1, 1))
            value_sum[:extent] += dot(weights.astype(BFLOAT), grad, (0, 0))
            mean_grad = jnp.sum(weights * weights_grad, axis=1, keepdims=True)
            score_grad = (weights * (weights_grad - mean_grad) * scale).astype(BFLOAT)
            query_grad = dot(score_grad, keys[:extent], (1, 0))
            key_sum[:extent] += dot(score_grad, query, (0, 0))
            query_grad_ref[here, span] = turned_back(query_grad, cosine_ref[here], sine_ref[here]).astype(BFLOAT)
    key_grad_ref[...] = turned_back(key_sum[...], cosine_ref[...], sine_ref[...]).astype(BFLOAT)
    value_grad_ref[...] = value_sum[...].astype(BFLOAT)


def attention_cost(tokens, width, factor):
    return pl.CostEstimate(
        flops=factor * 2 * tokens * tokens * width,
        bytes_accessed=factor * tokens * width * 8,
        transcendentals=tokens * tokens * width // (2 * HEAD_SIZE),
    )


def attention_specs(tokens, channels):
    width = channels * QUERY_HEADS // DSSM * HEAD_SIZE
    narrow = whole((tokens, HEAD_SIZE))
    return [
        pl.BlockSpec((tokens, width), lambda *_: (0, (STATES + PAIR + 2 * channels) // width)),
        pl.BlockSpec((tokens, HEAD_SIZE), lambda *_: (0, STATES // HEAD_SIZE)),
        pl.BlockSpec((tokens, HEAD_SIZE), lambda *_: (0, STATES // HEAD_SIZE + 1)),
        narrow,
        narrow,
        whole((tokens, LANES)),
        whole((8, tokens)),
    ]


def attention_operands(projected, tables):
    return [projected] * 3 + [tables[name] for name in ("cosine", "sine", "meta", "segment_row")]


def attention_forward(projected, tables):
    tokens = projected.shape[0]
    channels = tables["taps"].shape[1]
    width = channels * QUERY_HEADS // DSSM * HEAD_SIZE
    return pl.pallas_call(
        attention_forward_kernel,
        grid=(1,),
        in_specs=attention_specs(tokens, channels),
        out_specs=pl.BlockSpec((tokens, width), lambda *_: (0, channels // width)),
        out_shape=jax.ShapeDtypeStruct((tokens, channels + width), BFLOAT),
        scratch_shapes=[pltpu.VMEM((tokens, HEAD_SIZE), BFLOAT)],
        compiler_params=pltpu.CompilerParams(vmem_limit_bytes=SCAN_BYTES),
        cost_estimate=attention_cost(tokens, width, 1),
        name="attention_forward",
    )(*attention_operands(projected, tables))


def attention_backward(projected, tables, mixed_grad):
    tokens = projected.shape[0]
    channels = tables["taps"].shape[1]
    width = channels * QUERY_HEADS // DSSM * HEAD_SIZE
    narrow = whole((tokens, HEAD_SIZE))
    return pl.pallas_call(
        attention_backward_kernel,
        grid=(1,),
        in_specs=attention_specs(tokens, channels)
        + [pl.BlockSpec((tokens, width), lambda *_: (0, channels // width))],
        out_specs=[whole((tokens, width)), narrow, narrow],
        out_shape=[
            jax.ShapeDtypeStruct((tokens, width), BFLOAT),
            jax.ShapeDtypeStruct((tokens, HEAD_SIZE), BFLOAT),
            jax.ShapeDtypeStruct((tokens, HEAD_SIZE), BFLOAT),
        ],
        scratch_shapes=[
            pltpu.VMEM((tokens, HEAD_SIZE), BFLOAT),
            pltpu.VMEM((tokens, HEAD_SIZE), FLOAT),
            pltpu.VMEM((tokens, HEAD_SIZE), FLOAT),
        ],
        compiler_params=pltpu.CompilerParams(vmem_limit_bytes=SCAN_BYTES),
        cost_estimate=attention_cost(tokens, width, 3),
        name="attention_backward",
    )(*attention_operands(projected, tables), mixed_grad)


def mixer_tables(lengths, segment, position, conv_values, conv_states, scan_params):
    tokens = segment.shape[0]
    block = jnp.arange(tokens, dtype=jnp.int32) // SSD_BLOCK
    previous = jnp.concatenate([jnp.full((1,), -1, jnp.int32), segment[:-1]])
    first_previous = jnp.repeat(previous[::SSD_BLOCK], SSD_BLOCK)
    last_segment = jnp.repeat(segment[SSD_BLOCK - 1 :: SSD_BLOCK], SSD_BLOCK)
    length = jnp.sum(
        jnp.where(segment[:, None] == jnp.arange(lengths.shape[0], dtype=jnp.int32)[None, :], lengths[None, :], 0),
        axis=1,
    )
    columns = [
        segment,
        position,
        length - 1 - position,
        segment == first_previous,
        segment == last_segment,
    ]
    meta = jnp.stack([column.astype(FLOAT) for column in columns], axis=1)
    half_width = HEAD_SIZE // 2
    frequency = ROPE_BASE ** (-2.0 * jnp.arange(half_width, dtype=FLOAT) / HEAD_SIZE)
    angle = position.astype(FLOAT)[:, None] * frequency[None, :]
    cosine, sine = jnp.cos(angle), jnp.sin(angle)
    heads = scan_params.shape[1]
    head = jnp.stack([scan_params[0], -jnp.exp(scan_params[1]), scan_params[2]])
    return dict(
        meta=jnp.pad(meta, ((0, 0), (0, LANES - meta.shape[1]))),
        segment_row=jnp.broadcast_to(segment.astype(FLOAT)[None, :], (8, tokens)),
        taps=jnp.pad(conv_values.astype(FLOAT), ((0, 3), (0, 0))),
        state_taps=jnp.pad(conv_states.astype(FLOAT), ((0, 3), (0, 0))),
        head=jnp.pad(head, ((0, 5), (0, LANES - heads))),
        skip=jnp.broadcast_to(jnp.repeat(scan_params[2], HP)[None, :], (8, heads * HP)),
        cosine=jnp.concatenate([cosine, cosine], axis=1),
        sine=jnp.concatenate([-sine, sine], axis=1),
    )


HALVES = 2


def matrix_rows(values):
    return values.reshape(values.shape[0] * values.shape[1], values.shape[2])


def cut_tiles(width, tile):
    return [(low, min(low + tile, width)) for low in range(0, width, tile)]


def spread_kernel(mask, count, left_ref, right_ref, chosen_ref, *rest):
    weights, (out_ref, narrow_ref, out_tile, narrow, sems) = rest[:count], rest[-5:]
    rows = left_ref.shape[0]
    shards = weights[0].shape[0]
    depth = shards // HALVES
    start = pl.multiple_of((lax.axis_index("col") ^ mask) * rows, rows)
    here = pl.ds(start, rows)

    def through(ref, low, high):
        return dot(left_ref[...], matrix_rows(ref[:depth, :rows, low:high]), (1, 0)) + dot(
            right_ref[...], matrix_rows(ref[depth:, :rows, low:high]), (1, 0)
        )

    lower = weights[-1].shape[2] - LANES
    narrow[...] = (chosen_ref[here, :] * through(weights[-1], lower, lower + LANES)).astype(BFLOAT)
    copies = [pltpu.make_async_copy(narrow, narrow_ref.at[here, :], sems.at[0])]
    copies[0].start()
    column = 0
    for ref in weights:
        for low, high in cut_tiles(ref.shape[2] - (LANES if ref is weights[-1] else 0), 512):
            span = slice(column, column + high - low)
            column += high - low
            raised = matrix_rows(ref[:, rows : rows + NADAPT * RANK // shards, low:high])
            out_tile[:, span] = (through(ref, low, high) + dot(narrow[...], raised, (1, 0))).astype(BFLOAT)
            copies.append(
                pltpu.make_async_copy(out_tile.at[:, span], out_ref.at[here, span], sems.at[len(copies)])
            )
            copies[-1].start()
    for copy in copies:
        copy.wait()


def weights_width(gathered):
    return sum(part.shape[2] for part in gathered) - LANES


def spread_block(mask, halves, gathered, selector, held):
    rows, half = halves[0].shape
    width = weights_width(gathered)
    total = selector.shape[0]
    fast, free = pl.BlockSpec(memory_space=pltpu.VMEM), pl.BlockSpec(memory_space=pl.ANY)
    operands = [*halves, selector, *gathered]
    in_specs = [fast] * len(operands)
    aliases = {}
    if held is not None:
        aliases = {len(operands): 0, len(operands) + 1: 1}
        operands += list(held)
        in_specs += [free] * 2
    copies = 1 + sum(-(-part.shape[2] // 512) for part in gathered)
    return pl.pallas_call(
        functools.partial(spread_kernel, mask, len(gathered)),
        in_specs=in_specs,
        out_specs=[free] * 2,
        out_shape=[
            jax.ShapeDtypeStruct((total, width), BFLOAT),
            jax.ShapeDtypeStruct((total, LANES), BFLOAT),
        ],
        scratch_shapes=[
            pltpu.VMEM((rows, width), BFLOAT),
            pltpu.VMEM((rows, LANES), BFLOAT),
            pltpu.SemaphoreType.DMA((copies,)),
        ],
        input_output_aliases=aliases,
        compiler_params=pltpu.CompilerParams(vmem_limit_bytes=DENSE_BYTES),
        cost_estimate=pl.CostEstimate(
            flops=4 * rows * half * (width + LANES), bytes_accessed=2 * rows * (2 * half + width), transcendentals=0
        ),
        name="spread_block",
    )(*operands)


def collect_kernel(masks, count, values_ref, *refs):
    weights, outs = refs[:count], refs[count:]
    rows = values_ref.shape[0] // 4
    shards = weights[0].shape[0]
    half = shards // HALVES * rows
    width = values_ref.shape[1]
    starts, column = [], 0
    for ref in weights:
        high = min(column + ref.shape[2], width)
        starts.append((column, high))
        column = high
    for at, mask in enumerate(masks):
        here = pl.ds(pl.multiple_of((lax.axis_index("col") ^ mask) * rows, rows), rows)
        first, second = outs[2 * at], outs[2 * at + 1]

        def through(cut):
            total = None
            for (low, high), ref in zip(starts, weights):
                part = dot(values_ref[here, low:high], cut(ref, high - low), (1, 1))
                total = part if total is None else total + part
            return total

        for shard in range(shards):
            out_ref = first if shard < shards // HALVES else second
            column = shard * rows % half
            out_ref[:, column : column + rows] = through(lambda ref, wide: ref[shard, :rows, :wide]).astype(
                out_ref.dtype
            )
        first[:, half:] = through(
            lambda ref, wide: matrix_rows(ref[:, rows : rows + NADAPT * RANK // shards, :wide])
        ).astype(first.dtype)


def collect_blocks(masks, values, gathered, types):
    rows = values.shape[0] // 4
    half = gathered[0].shape[0] // HALVES * rows
    fast = pl.BlockSpec(memory_space=pltpu.VMEM)
    out_shape = []
    for pair in types:
        out_shape.append(jax.ShapeDtypeStruct((rows, half + LANES), pair[0]))
        out_shape.append(jax.ShapeDtypeStruct((rows, half), pair[1]))
    outs = pl.pallas_call(
        functools.partial(collect_kernel, masks, len(gathered)),
        in_specs=[fast] * (1 + len(gathered)),
        out_specs=[fast] * len(out_shape),
        out_shape=out_shape,
        compiler_params=pltpu.CompilerParams(vmem_limit_bytes=DENSE_BYTES),
        cost_estimate=pl.CostEstimate(
            flops=4 * len(masks) * rows * half * values.shape[1],
            bytes_accessed=2 * len(masks) * rows * (values.shape[1] + 4 * half),
            transcendentals=0,
        ),
        name="collect_blocks",
    )(values, *gathered)
    return [tuple(outs[2 * at : 2 * at + 2]) for at in range(len(masks))]


def root_mean(values):
    return lax.rsqrt(jnp.mean(values * values, axis=1, keepdims=True) + EPSILON)


def finish_kernel(kind, first_own, first_near, first_far, second_own, second_near, second_far, lower_ref, chosen_ref,
                  *refs):
    half = second_own.shape[1]
    wide = lambda ref: ref[...].astype(FLOAT)
    first = wide(first_own) + wide(first_near) + wide(first_far)
    second = wide(second_own) + wide(second_near) + wide(second_far)
    inner = (chosen_ref[...] * first[:, half:]).astype(BFLOAT)
    shards, tall, _ = lower_ref.shape
    rows = tall - NADAPT * RANK // shards
    summed = jnp.concatenate([first[:, :half], second], axis=1) + dot(
        inner, matrix_rows(lower_ref[:, :rows, :]), (1, 1)
    )
    if kind == "output":
        residual_ref, out_ref, inner_ref = refs
        inner_ref[...] = inner
        out_ref[...] = (residual_ref[...] + summed).astype(BFLOAT)
        return
    if kind == "forward":
        residual_ref, gain_ref, out_ref, inner_ref, left_ref, right_ref = refs
        hidden = residual_ref[...] + summed
        normed = (hidden * root_mean(hidden) * gain_ref[0:1, :]).astype(BFLOAT)
        out_ref[...] = hidden
    else:
        values_ref, upstream_ref, gain_ref = refs[:3]
        values = values_ref[...]
        scale = root_mean(values)
        weighted = summed * gain_ref[0:1, :]
        mean = jnp.mean(weighted * values, axis=1, keepdims=True)
        hidden = upstream_ref[...].astype(FLOAT) + scale * weighted - values * (scale * scale * scale * mean)
        normed = hidden.astype(BFLOAT)
        if kind == "input":
            out_ref, inner_ref = refs[3:]
            inner_ref[...] = inner
            out_ref[...] = normed
            return
        out_ref, inner_ref, left_ref, right_ref = refs[3:]
        out_ref[...] = hidden
    inner_ref[...] = inner
    left_ref[...] = normed[:, :half]
    right_ref[...] = normed[:, half:]


def finish(kind, parts, gathered, own_selector, *operands):
    rows = own_selector.shape[0]
    half = parts[3].shape[1]
    shards, tall, full = gathered[-1].shape
    model = HALVES * half
    result = BFLOAT if kind in ("output", "input") else FLOAT
    out_shape = [jax.ShapeDtypeStruct((rows, model), result), jax.ShapeDtypeStruct((rows, LANES), BFLOAT)]
    if kind in ("forward", "backward"):
        out_shape += [jax.ShapeDtypeStruct((rows, half), BFLOAT)] * 2
    given = [*parts, gathered[-1], own_selector, *operands]
    in_specs = [whole(value.shape) for value in given]
    in_specs[6] = pl.BlockSpec((shards, tall, LANES), lambda *_: (0, 0, full // LANES - 1))
    return pl.pallas_call(
        functools.partial(finish_kernel, kind),
        grid=(1,),
        in_specs=in_specs,
        out_specs=[whole(shape.shape) for shape in out_shape],
        out_shape=out_shape,
        compiler_params=pltpu.CompilerParams(vmem_limit_bytes=DENSE_BYTES),
        cost_estimate=pl.CostEstimate(
            flops=2 * rows * model * LANES, bytes_accessed=rows * model * 20, transcendentals=0
        ),
        name="finish_" + kind,
    )(*given)


def send_kernel(target_column, target_row, tokens_ref, adapter_ref, sent_ref, matrix_ref):
    rows = tokens_ref.shape[0]
    model = tokens_ref.shape[1]
    peer = adapter_ref.shape[0]
    column, row = target_column[:, 0:1], target_row[0:1, :]
    earlier = lax.broadcasted_iota(jnp.int32, (rows, rows), 0) < lax.broadcasted_iota(jnp.int32, (rows, rows), 1)
    same = jnp.where((column // rows == row // rows) & earlier, 1.0, 0.0)
    place = (row // rows) * peer + jnp.sum(same, axis=0, keepdims=True).astype(jnp.int32)
    matrix = (lax.broadcasted_iota(jnp.int32, (rows, rows), 0) == place).astype(BFLOAT)
    matrix_ref[...] = matrix
    sent_ref[:, :model] = dot(matrix, tokens_ref[...], (1, 0)).astype(BFLOAT)
    lane = lax.broadcasted_iota(jnp.int32, (rows, LANES), 1)
    slots = jnp.where(lane == 0, column % rows, 0).astype(FLOAT).astype(BFLOAT)
    notes = dot(matrix, slots, (1, 0))
    sent_ref[:, model:] = jnp.where(lane == 0, notes, adapter_ref[0:1, :]).astype(BFLOAT)


def send_tokens(target, tokens, adapters, peer):
    rows, model = tokens.shape
    notes = jnp.pad(adapters.astype(FLOAT), (1, LANES - 1 - adapters.shape[0]))
    return pl.pallas_call(
        send_kernel,
        in_specs=[pl.BlockSpec(memory_space=pltpu.VMEM)] * 4,
        out_specs=[pl.BlockSpec(memory_space=pltpu.VMEM)] * 2,
        out_shape=[
            jax.ShapeDtypeStruct((rows, model + LANES), BFLOAT),
            jax.ShapeDtypeStruct((rows, rows), BFLOAT),
        ],
        compiler_params=pltpu.CompilerParams(vmem_limit_bytes=DENSE_BYTES),
        name="send_tokens",
    )(
        jnp.broadcast_to(target[:, None], (rows, LANES)),
        jnp.broadcast_to(target[None, :], (8, rows)),
        tokens,
        jnp.broadcast_to(notes[None, :], (peer, LANES)),
    )


def arrive_kernel(arrived_ref, gain_ref, own_ref, matrix_ref, left_ref, right_ref):
    rows, model = own_ref.shape
    slots = arrived_ref[:, model:].astype(FLOAT).T[0:1, :]
    row = lax.broadcasted_iota(jnp.int32, (rows, rows), 0).astype(FLOAT)
    matrix = (row == slots).astype(BFLOAT)
    matrix_ref[...] = matrix
    own = dot(matrix, arrived_ref[:, :model], (1, 0))
    own_ref[...] = own
    normed = (own * root_mean(own) * gain_ref[0:1, :]).astype(BFLOAT)
    left_ref[...] = normed[:, : model // HALVES]
    right_ref[...] = normed[:, model // HALVES :]


def arrive_tokens(arrived, gain):
    rows, model = arrived.shape[0], arrived.shape[1] - LANES
    return pl.pallas_call(
        arrive_kernel,
        in_specs=[pl.BlockSpec(memory_space=pltpu.VMEM)] * 2,
        out_specs=[pl.BlockSpec(memory_space=pltpu.VMEM)] * 4,
        out_shape=[
            jax.ShapeDtypeStruct((rows, model), FLOAT),
            jax.ShapeDtypeStruct((rows, rows), BFLOAT),
            jax.ShapeDtypeStruct((rows, model // HALVES), BFLOAT),
            jax.ShapeDtypeStruct((rows, model // HALVES), BFLOAT),
        ],
        compiler_params=pltpu.CompilerParams(vmem_limit_bytes=DENSE_BYTES),
        name="arrive_tokens",
    )(arrived, gain)


GATE_WIDTH = DSSM // QUERY_HEADS
PAIR_WIDTH = 2 * KEY_VALUE_HEADS * HEAD_SIZE // QUERY_HEADS
STATE_WIDTH = 2 * NSTATE // QUERY_HEADS
STEP_WIDTH = NH // QUERY_HEADS
ALL_AXES = ("row", "col")


def pad_columns(values, width):
    return jnp.pad(values, ((0, 0), (0, width - values.shape[1])))


def after(values, *earlier):
    return lax.optimization_barrier((values, *earlier))[0]


def unit_parts(values, units):
    cuts = [0]
    for width in (GATE_WIDTH, GATE_WIDTH, HEAD_SIZE, PAIR_WIDTH, STATE_WIDTH, STEP_WIDTH):
        cuts.append(cuts[-1] + width)
    return [
        jnp.concatenate(
            [values[:, unit * UNIT_IN + low : unit * UNIT_IN + high] for unit in range(units)], axis=1
        )
        for low, high in zip(cuts[:-1], cuts[1:])
    ]


def restore_units(parts, units):
    ordered = []
    for unit in range(units):
        for part in parts:
            width = part.shape[1] // units
            ordered.append(part[:, unit * width : (unit + 1) * width])
    return jnp.concatenate(ordered, axis=1)


def split_halves(values, units, first, axis):
    block = values.shape[axis] // units
    take = lambda low, high: lax.slice_in_dim(values, low, high, axis=axis)
    parts = [take(unit * block, unit * block + first) for unit in range(units)]
    parts += [take(unit * block + first, (unit + 1) * block) for unit in range(units)]
    return jnp.concatenate(parts, axis=axis)


def join_halves(values, units, first, axis):
    block = values.shape[axis] // units
    rest = block - first
    take = lambda low, high: lax.slice_in_dim(values, low, high, axis=axis)
    parts = []
    for unit in range(units):
        parts.append(take(unit * first, (unit + 1) * first))
        parts.append(take(units * first + unit * rest, units * first + (unit + 1) * rest))
    return jnp.concatenate(parts, axis=axis)


def quick(rows):
    return lax.axis_size("col") == 4 and lax.axis_size("row") == 8 and rows == 256


def flip(values, mask):
    return lax.ppermute(values, "col", [(i, i ^ mask) for i in range(4)])


def gather_blocks(halves):
    left, right = halves
    far_left, near_right = flip(left, 2), flip(right, 1)
    near_left, far_right = flip(left, 1), flip(right, 2)
    corner_left, corner_right = flip(far_left, 1), flip(near_right, 2)
    return [
        (0, (left, right)),
        (1, (near_left, near_right)),
        (2, (far_left, far_right)),
        (3, (corner_left, corner_right)),
    ]


def rows_of(values, block, rows):
    return lax.dynamic_slice_in_dim(values, block * rows, rows, 0)


def spread_project(halves, gathered, selector):
    rows = halves[0].shape[0]
    if quick(rows):
        held = None
        for mask, values in gather_blocks(halves):
            held = spread_block(mask, values, gathered, selector, held)
        return held
    wide, narrow_factor = gathered
    width = narrow_factor.shape[1]
    both = product(lax.all_gather(jnp.concatenate(halves, axis=1), "col", axis=0, tiled=True), wide)
    narrow = (selector * both[:, width:]).astype(BFLOAT)
    return (both[:, :width] + product(narrow, narrow_factor)).astype(BFLOAT), narrow


def collect_project(values, gathered, kind, own_selector, *operands):
    rows, model = own_selector.shape[0], operands[0].shape[1]
    if quick(rows):
        wide = lambda part: part.astype(FLOAT)
        (corner,) = collect_blocks([3], values, gathered, [(BFLOAT, BFLOAT)])
        corner_first, corner_second = flip(corner[0], 1), flip(corner[1], 2)
        near, far = collect_blocks([1, 2], values, gathered, [(BFLOAT, FLOAT), (FLOAT, BFLOAT)])
        near_first, far_second = flip(near[0], 1), flip(far[1], 2)
        (own,) = collect_blocks([0], values, gathered, [(FLOAT, FLOAT)])
        far_first = flip((far[0] + wide(corner_first)).astype(BFLOAT), 2)
        near_second = flip((near[1] + wide(corner_second)).astype(BFLOAT), 1)
        parts = [own[0], near_first, far_first, own[1], far_second, near_second]
        return finish(kind, parts, gathered, own_selector, *operands)
    wide, narrow_factor = gathered
    width = narrow_factor.shape[1]
    partial = jnp.concatenate(
        [contract_last(values, wide[:, :width]), contract_last(values, narrow_factor)], axis=1
    ).astype(BFLOAT)
    summed = lax.psum_scatter(partial, "col", scatter_dimension=0, tiled=True).astype(FLOAT)
    inner = (own_selector * summed[:, model:]).astype(BFLOAT)
    summed = summed[:, :model] + contract_last(inner, wide[:, width:])
    if kind == "output":
        return (operands[0] + summed).astype(BFLOAT), inner
    if kind == "forward":
        residual, gain = operands
        hidden = residual + summed
        return hidden, inner, *cut_halves(rms_norm(hidden, gain[0]).astype(BFLOAT))
    values, upstream, gain = operands
    _, back = jax.vjp(lambda given: rms_norm(given, gain[0]), values)
    hidden = upstream.astype(FLOAT) + back(summed)[0]
    if kind == "input":
        return hidden.astype(BFLOAT), inner
    return hidden, inner, *cut_halves(hidden.astype(BFLOAT))


def cut_halves(values):
    half = values.shape[1] // HALVES
    return values[:, :half], values[:, half:]


def local(
    tokens_in,
    cotangent,
    target,
    sequence_lengths,
    sequence_adapter,
    norm_gains,
    weight_in,
    conv_values,
    conv_states,
    scan_params,
    weight_mix,
    weight_feed,
    weight_down,
    in_lower,
    in_raise,
    mix_lower,
    mix_raise,
    feed_lower,
    feed_raise,
    down_lower,
    down_raise,
):
    cols = lax.axis_size("col")
    rows_axis = lax.axis_size("row")
    col = lax.axis_index("col")
    devices = cols * rows_axis
    rows = tokens_in.shape[0]
    model = tokens_in.shape[1]
    total = rows * cols
    units = QUERY_HEADS // cols
    channels = units * GATE_WIDTH
    peer = rows // devices
    lengths, adapters = sequence_lengths[0], sequence_adapter[0]
    sequences = lengths.shape[0]
    fast = quick(rows)
    key_head = col * units // (QUERY_HEADS // KEY_VALUE_HEADS)
    exchange = lambda values: lax.all_to_all(values, ALL_AXES, split_axis=0, concat_axis=0, tiled=True)

    sent, send_matrix = send_tokens(target, tokens_in, adapters, peer)
    arrived = exchange(sent)

    def gather_weight(weight, lower, raised):
        top = jnp.concatenate([weight, lower], axis=1)
        if fast:
            bottom = pad_columns(raised, top.shape[1])
            return (lax.all_gather(jnp.concatenate([top, bottom], axis=0), "row", axis=0),)
        wide = lax.all_gather(top, "row", axis=0, tiled=True)
        return wide, lax.all_gather(raised, "row", axis=0, tiled=True)

    depth = weight_in.shape[0]
    height = depth + in_raise.shape[0]
    given = after(jnp.concatenate([weight_in, in_raise], axis=0), send_matrix)
    gates, convs, queries, pairs, states, steps = unit_parts(given, units)
    pair_width, state_width = pairs.shape[1], states.shape[1]
    taps = jnp.concatenate([jnp.zeros((KCONV + 1, pair_width), BFLOAT), conv_states], axis=1)
    taps = jnp.pad(taps, ((0, 16 - KCONV - 1), (0, 0)))
    shared = jnp.concatenate([jnp.concatenate([pairs, states], axis=1), taps], axis=0)
    if fast:
        shared = lax.all_gather(shared, "row", axis=0)
        held = jnp.zeros((cols,) + shared.shape, BFLOAT)
        near, far = flip(shared, 1), flip(shared, 2)
        for block, values in ((col, shared), (col ^ 1, near), (col ^ 2, far)):
            held = lax.dynamic_update_index_in_dim(held, values, block, 0)
        split = shared.shape[0] // 2
        corner = jnp.concatenate([flip(near[:split], 2), flip(far[split:], 1)], axis=0)
        held = lax.dynamic_update_index_in_dim(held, corner, col ^ 3, 0)
    else:
        held = lax.all_gather(shared, "col", axis=0)
    all_pairs = jnp.concatenate([held[at, ..., :height, :pair_width] for at in range(cols)], axis=-1)
    pick = lambda start: lax.select_n(
        key_head,
        *[all_pairs[..., start + at * HEAD_SIZE : start + (at + 1) * HEAD_SIZE] for at in range(KEY_VALUE_HEADS)],
    )
    shared_columns = jnp.concatenate(
        [held[at, ..., :height, pair_width:] for at in range(cols)]
        + [pick(0), pick(KEY_VALUE_HEADS * HEAD_SIZE)],
        axis=-1,
    )
    tap_rows = held[:, 0] if fast else held
    all_taps = jnp.concatenate(
        [tap_rows[at, height : height + KCONV + 1, pair_width:] for at in range(cols)], axis=1
    )
    own_columns = [gates, convs, queries, pad_columns(steps, LANES)]
    if fast:
        own_columns = jnp.concatenate(own_columns, axis=1)
        weights_in = (shared_columns, *gather_weight(own_columns[:depth], in_lower, own_columns[depth:]))
    else:
        columns = jnp.concatenate([shared_columns, *own_columns], axis=1)
        weights_in = gather_weight(columns[:depth], in_lower, columns[depth:])
    weights_mix = gather_weight(
        after(split_halves(weight_mix, units, GATE_WIDTH, 0).T, send_matrix),
        mix_raise.T,
        split_halves(mix_lower, units, GATE_WIDTH, 0).T,
    )
    weights_feed = gather_weight(
        after(split_halves(weight_feed, units, UNIT_FF, 1), arrived),
        feed_lower,
        split_halves(feed_raise, units, UNIT_FF, 1),
    )

    gains = jnp.broadcast_to(norm_gains.astype(FLOAT)[:, None, :], (2, 8, model))
    own_input, place_matrix, *normed_one = arrive_tokens(arrived.reshape(rows, model + LANES), gains[0])
    source_adapters = arrived.reshape(rows, model + LANES)[::peer, model + 1 : model + 1 + sequences].astype(jnp.int32)
    segment, position, selector = sequence_tables(lengths, adapters, total)
    own_selector = rows_of(selector, col, rows)
    own_segment = rows_of(segment, col, rows)
    tables = mixer_tables(lengths, segment, position, conv_values, all_taps, scan_params)

    def compact_grad(narrow, values):
        parts = [
            lax.dynamic_slice_in_dim(narrow, adapters[at] * RANK, RANK, 1)
            * (own_segment == at).astype(BFLOAT)[:, None]
            for at in range(sequences)
        ]
        grad = contract_first(jnp.concatenate(parts, axis=1), values).astype(BFLOAT)
        kept = sequences * RANK
        grad = grad.reshape(kept, devices, model // devices).transpose(1, 0, 2)
        return grad.reshape(devices, peer, kept * model // devices // peer)

    def expand_grad(dealt):
        kept = sequences * RANK
        dealt = dealt.reshape(devices * kept, model // devices)
        adapter_row = (source_adapters[:, :, None] * RANK + jnp.arange(RANK, dtype=jnp.int32)).reshape(-1)
        chosen = (jnp.arange(NADAPT * RANK, dtype=jnp.int32)[:, None] == adapter_row[None, :]).astype(BFLOAT)
        return product(chosen, dealt)

    def send_back(values, grads):
        back = contract_first(place_matrix, values).astype(BFLOAT).reshape(devices, peer, model)
        return exchange(jnp.concatenate([back, *grads], axis=2))

    def take_back(dealt, count):
        returned = contract_first(send_matrix, dealt[:, :, :model].reshape(rows, model)).astype(BFLOAT)
        width = (dealt.shape[2] - model) // max(count, 1)
        return returned, [
            expand_grad(dealt[:, :, model + at * width : model + (at + 1) * width]) for at in range(count)
        ]

    projected, inner_in = spread_project(normed_one, weights_in, selector)

    sent_grad = product(send_matrix, cotangent).astype(BFLOAT).reshape(devices, peer, model)
    arrived_grad = exchange(after(sent_grad, normed_one[0])).reshape(rows, model)
    branch_two = product(place_matrix, arrived_grad).astype(BFLOAT)
    weights_down = gather_weight(after(weight_down.T, normed_one[0]), down_raise.T, down_lower.T)

    mixed_out = attention_forward(projected, tables)
    mixed_out, scanned, carried = scan_forward(projected, tables, mixed_out)
    hidden, inner_out, *normed_two = collect_project(mixed_out, weights_mix, "forward", own_selector, own_input, gains[1])
    gate_up, inner_feed = spread_project(normed_two, weights_feed, selector)
    act_grad, narrow_two = spread_project(cut_halves(after(branch_two, projected)), weights_down, selector)
    half_feed = units * UNIT_FF
    gate_part, up_part = gate_up[:, :half_feed].astype(FLOAT), gate_up[:, half_feed:].astype(FLOAT)
    gate = jax.nn.sigmoid(gate_part)
    silu = gate_part * gate
    activated = (silu * up_part).astype(BFLOAT)
    wide_grad = act_grad.astype(FLOAT)
    feed_grad = jnp.concatenate(
        [wide_grad * up_part * (gate * (1.0 + gate_part * (1.0 - gate))), wide_grad * silu], axis=1
    ).astype(BFLOAT)
    hidden_grad, narrow_three, *branch_one = collect_project(
        feed_grad, weights_feed, "backward", own_selector, hidden, branch_two, gains[1]
    )
    mixed_grad, narrow_one = spread_project(branch_one, weights_mix, selector)

    block_out, inner_down = collect_project(
        after(activated, mixed_grad), weights_down, "output", own_selector, hidden
    )
    query_grad, key_grad, value_grad = attention_backward(projected, tables, mixed_grad)
    projected_grad = scan_backward(
        projected, tables, scanned, carried, mixed_grad, query_grad, key_grad, value_grad
    )
    dealt_out = send_back(
        block_out,
        [
            compact_grad(inner_down, branch_two),
            compact_grad(narrow_three, jnp.concatenate(normed_two, axis=1)),
            compact_grad(inner_out, jnp.concatenate(branch_one, axis=1)),
        ],
    )

    def sum_rows(values):
        return lax.psum_scatter(values.astype(BFLOAT), "row", scatter_dimension=0, tiled=True).astype(FLOAT)

    early_parts = [
        contract_first(narrow_one, mixed_out),
        contract_first(inner_feed, feed_grad),
        contract_first(narrow_two, activated),
    ]
    early = sum_rows(jnp.concatenate(early_parts, axis=1))
    early_cuts = [0, early_parts[0].shape[1]]
    early_cuts.append(early_cuts[1] + early_parts[1].shape[1])
    grad_mix_lower = join_halves(early[:, : early_cuts[1]], units, GATE_WIDTH, 1).T
    grad_feed_raise = join_halves(early[:, early_cuts[1] : early_cuts[2]], units, UNIT_FF, 1)
    grad_down_lower = early[:, early_cuts[2] :].T

    raise_grad = contract_first(inner_in, projected_grad)
    key_columns = raise_grad[:, STATES : STATES + HEAD_SIZE]
    value_columns = raise_grad[:, STATES + HEAD_SIZE : STATES + PAIR]
    mine = [(key_head == at).astype(FLOAT) for at in range(KEY_VALUE_HEADS)]
    pair_grad = jnp.concatenate([part * here for part in (key_columns, value_columns) for here in mine], axis=1)
    stacked = jnp.stack(
        [
            jnp.concatenate(
                [
                    pair_grad[:, at * pair_width : (at + 1) * pair_width],
                    raise_grad[:, at * state_width : (at + 1) * state_width],
                ],
                axis=1,
            )
            for at in range(cols)
        ]
    )
    if fast:
        to_send = stacked.astype(BFLOAT)
        piece = lambda block: lax.dynamic_index_in_dim(to_send, block, 0, False)
        near_sum = lambda block: lax.dynamic_index_in_dim(stacked, block, 0, False)
        pair_sums = flip(jnp.stack([piece(col ^ 1), piece(col ^ 3)]), 1).astype(FLOAT)
        far_sum = (near_sum(col ^ 2) + pair_sums[1]).astype(BFLOAT)
        shared_sum = near_sum(col) + pair_sums[0] + flip(far_sum, 2).astype(FLOAT)
    else:
        shared_sum = lax.psum_scatter(
            stacked.astype(BFLOAT).reshape(cols * NADAPT * RANK, -1), "col", scatter_dimension=0, tiled=True
        ).astype(FLOAT)
    late = sum_rows(jnp.concatenate([shared_sum, raise_grad[:, STATES + PAIR :]], axis=1))
    shared_width = pair_width + state_width
    cuts = [shared_width]
    for width in (channels, channels, units * HEAD_SIZE, units * STEP_WIDTH):
        cuts.append(cuts[-1] + width)
    gate_columns, conv_columns, query_columns, step_columns = [
        late[:, low:high] for low, high in zip(cuts[:-1], cuts[1:])
    ]
    grad_in_raise = restore_units(
        [
            gate_columns,
            conv_columns,
            query_columns,
            late[:, :pair_width],
            late[:, pair_width:shared_width],
            step_columns,
        ],
        units,
    )

    input_grad, narrow_four = collect_project(
        after(projected_grad, dealt_out), weights_in, "input", own_selector, own_input, hidden_grad, gains[0]
    )
    dealt_grad = send_back(input_grad, [compact_grad(narrow_four, jnp.concatenate(normed_one, axis=1))])
    returned_out, (grad_down_raise, grad_feed_lower, grad_mix_raise) = take_back(dealt_out, 3)
    returned_grad, (grad_in_lower,) = take_back(dealt_grad, 1)
    return (
        returned_out,
        returned_grad,
        grad_in_lower.T,
        grad_in_raise,
        grad_mix_lower,
        grad_mix_raise,
        grad_feed_lower.T,
        grad_feed_raise,
        grad_down_lower,
        grad_down_raise,
    )


def solution(mesh):
    in_specs = (
        P(("row", "col"), None),
        P(("row", "col"), None),
        P(("row", "col")),
        P("row", None),
        P("row", None),
        P(),
        P("row", "col"),
        P(None, "col"),
        P(None, "col"),
        P(None, "col"),
        P("col", "row"),
        P("row", "col"),
        P("col", "row"),
        P("row", None),
        P("row", "col"),
        P("col", "row"),
        P(None, "row"),
        P("row", None),
        P("row", "col"),
        P("col", "row"),
        P(None, "row"),
    )
    out_specs = (
        P(("row", "col"), None),
        P(("row", "col"), None),
        P(("row", "col"), None),
        P("row", "col"),
        P("col", "row"),
        P(None, ("row", "col")),
        P(("row", "col"), None),
        P("row", "col"),
        P("col", "row"),
        P(None, ("row", "col")),
    )
    return jax.shard_map(local, mesh=mesh, in_specs=in_specs, out_specs=out_specs, check_vma=False)
```

```python
import functools
import math

import jax
import jax.numpy as jnp
from jax import lax
from jax.experimental import pallas as pl
from jax.experimental.pallas import tpu as pltpu
from jax.sharding import PartitionSpec as P

NH = 48
HP = 64
NSTATE = 256
KCONV = 4
QUERY_HEADS = 8
KEY_VALUE_HEADS = 2
HEAD_SIZE = 128
RANK = 16
NADAPT = 8
SSD_BLOCK = 256
DSSM = 3072
UNIT_IN = 1030
UNIT_FF = 512


EPSILON = 1e-05
ROPE_BASE = 10000.0
NEGATIVE = -1e30
FLOAT = jnp.float32
BFLOAT = jnp.bfloat16


def product(left, right):
    return jnp.dot(left, right, preferred_element_type=FLOAT)


def contract_last(left, right):
    return lax.dot_general(left, right, (((1,), (1,)), ((), ())), preferred_element_type=FLOAT)


def contract_first(left, right):
    return lax.dot_general(left, right, (((0,), (0,)), ((), ())), preferred_element_type=FLOAT)


def rms_norm(values, gain):
    return values * lax.rsqrt(jnp.mean(values * values, axis=-1, keepdims=True) + EPSILON) * gain


def sequence_tables(lengths, adapters, sequence_length):
    sequence_count = lengths.shape[0]
    boundary = jnp.cumsum(lengths)
    token_index = jnp.arange(sequence_length, dtype=jnp.int32)
    passed = (token_index[:, None] >= boundary[None, :]).astype(jnp.int32)
    segment = jnp.sum(passed, axis=1)
    segment_start = jnp.sum(passed * lengths[None, :], axis=1)
    position = token_index - segment_start
    member = (segment[:, None] == jnp.arange(sequence_count, dtype=jnp.int32)[None, :]).astype(
        jnp.int32
    )
    chosen = jnp.sum(member * adapters[None, :], axis=1)
    column = jnp.arange(NADAPT * RANK, dtype=jnp.int32) // RANK
    selector = (chosen[:, None] == column[None, :]).astype(FLOAT)
    return (segment, position, selector)


SCAN_BYTES = 32 * 1024 * 1024
DENSE_BYTES = 16 * 1024 * 1024
LANES = 128


def whole(shape):
    return pl.BlockSpec(shape, lambda *_: (0,) * len(shape))


def dot(left, right, contract):
    return lax.dot_general(left, right, ((contract[:1], contract[1:]), ((), ())), preferred_element_type=FLOAT)


def parts_of(values, count):
    parts = []
    for _ in range(count):
        part = values.astype(BFLOAT)
        parts.append(part)
        values = values - part.astype(FLOAT)
    return parts


def running_sum(values, triangle, contract):
    width = values.shape[1]
    split = dot(triangle, jnp.concatenate(parts_of(values, 3), axis=1), contract)
    return split[:, :width] + split[:, width : 2 * width] + split[:, 2 * width :]


def head_spread(values, expand):
    return dot(jnp.concatenate(parts_of(values, 2), axis=1), expand, (1, 0))


def head_sum(values, expand):
    high, low = parts_of(values, 2)
    single = expand[:LANES]
    return dot(high, single, (1, 1)) + dot(low, single, (1, 1))


def silu_parts(values):
    gate = 1.0 / (1.0 + jnp.exp(-values))
    return values * gate, gate


def expand_table(channels):
    row = lax.broadcasted_iota(jnp.int32, (2 * LANES, channels), 0) % LANES
    channel = lax.broadcasted_iota(jnp.int32, (2 * LANES, channels), 1) // HP
    return (row == channel).astype(BFLOAT)


def conv_sum(current_ref, before_ref, taps_ref, meta):
    rows = SSD_BLOCK
    current = current_ref[...].astype(FLOAT)
    window = jnp.concatenate([before_ref[...].astype(FLOAT)[8:16], current], axis=0)
    summed = taps_ref[KCONV : KCONV + 1, :] + current * taps_ref[0:1, :]
    for lag in range(1, KCONV):
        shifted = window[8 - lag : 8 - lag + rows]
        summed = summed + jnp.where(meta[:, 1:2] >= lag, shifted, 0.0) * taps_ref[lag : lag + 1, :]
    return summed


def conv_back(summed_grad, later, taps_ref, meta):
    rows = SSD_BLOCK
    window = jnp.concatenate([summed_grad, later[...]], axis=0)
    grad = summed_grad * taps_ref[0:1, :]
    for lag in range(1, KCONV):
        grad = grad + jnp.where(meta[:, 2:3] >= lag, window[lag : lag + rows], 0.0) * taps_ref[lag : lag + 1, :]
    later[...] = summed_grad[:8]
    return grad


def silu_slope(values, gate):
    return gate * (1.0 + values * (1.0 - gate))


def scan_block(
    conv_ref, before_ref, state_ref, state_before_ref, step_ref, meta_ref, segment_ref, taps_ref, state_taps_ref, head_ref,
    turned_over,
):
    rows = SSD_BLOCK
    channels = conv_ref.shape[1]
    meta = meta_ref[...]
    summed = conv_sum(conv_ref, before_ref, taps_ref, meta)
    activated, conv_gate = silu_parts(summed)
    wide_inputs = activated.astype(BFLOAT).astype(FLOAT)
    state_summed = conv_sum(state_ref, state_before_ref, state_taps_ref, meta)
    state_values, state_gate = silu_parts(state_summed)
    write = state_values[:, :NSTATE].astype(BFLOAT)
    read = state_values[:, NSTATE:].astype(BFLOAT)
    raw = step_ref[...].astype(FLOAT) + head_ref[0:1, :]
    steps = jnp.maximum(raw, 0.0) + jnp.log1p(jnp.exp(-jnp.abs(raw)))
    row = lax.broadcasted_iota(jnp.int32, (rows, rows), 0)
    column = lax.broadcasted_iota(jnp.int32, (rows, rows), 1)
    triangle = (row >= column).astype(BFLOAT)
    total = running_sum(steps * head_ref[1:2, :], triangle, (1, 0))
    entered = jnp.exp(total) * meta[:, 3:4]
    leaving = jnp.exp(total[rows - 1 : rows] - total) * meta[:, 4:5]
    expand = expand_table(channels)
    spread = head_spread(jnp.concatenate([steps, entered, leaving * steps], axis=0), expand)
    ordered = row <= column if turned_over else row >= column
    blocked = jnp.where(ordered & (meta[:, 0:1] == segment_ref[0:1, :]), 0.0, NEGATIVE)
    return dict(
        summed=summed,
        conv_gate=conv_gate,
        state_summed=state_summed,
        state_gate=state_gate,
        write=write,
        read=read,
        wide_inputs=wide_inputs,
        raw=raw,
        steps=steps,
        triangle=triangle,
        total=total,
        total_rows=total.T,
        leaving=leaving,
        expand=expand,
        steps_wide=spread[:rows],
        entered_wide=spread[rows : 2 * rows],
        tail_wide=spread[2 * rows :],
        stepped=(wide_inputs * spread[:rows]).astype(BFLOAT),
        tailed=(wide_inputs * spread[2 * rows :]).astype(BFLOAT),
        blocked=blocked,
        crossing=dot(write, read, (1, 1)) if turned_over else dot(read, write, (1, 1)),
    )


def decay_of(block, head):
    difference = block["total"][:, head : head + 1] - block["total_rows"][head : head + 1, :]
    return jnp.exp(difference + block["blocked"])


def turned_decay_of(block, head):
    difference = block["total_rows"][head : head + 1, :] - block["total"][:, head : head + 1]
    return jnp.exp(difference + block["blocked"])


def scan_forward_kernel(
    gate_ref, conv_ref, before_ref, state_ref, state_before_ref, step_ref, meta_ref, segment_ref, taps_ref,
    state_taps_ref, head_ref, skip_ref, mixed_ref, out_ref, scanned_ref, states_ref, state,
):
    del mixed_ref

    @pl.when(pl.program_id(0) == 0)
    def _():
        state[...] = jnp.zeros_like(state)

    block = scan_block(
        conv_ref, before_ref, state_ref, state_before_ref, step_ref, meta_ref, segment_ref, taps_ref, state_taps_ref,
        head_ref, False,
    )
    heads = conv_ref.shape[1] // HP
    carried = state[...].astype(BFLOAT)
    states_ref[0] = carried
    across = dot(block["read"], carried, (1, 0)) * block["entered_wide"]
    within = []
    for head in range(heads):
        weights = (block["crossing"] * decay_of(block, head)).astype(BFLOAT)
        within.append(dot(weights, block["stepped"][:, head * HP : (head + 1) * HP], (1, 0)))
    scanned = across + jnp.concatenate(within, axis=1)
    scanned_ref[...] = scanned
    gated, _ = silu_parts(gate_ref[...].astype(FLOAT))
    out_ref[...] = ((scanned + skip_ref[0:1, :] * block["wide_inputs"]) * gated).astype(BFLOAT)
    state[...] = state[...] * block["entered_wide"][SSD_BLOCK - 1 : SSD_BLOCK, :] + dot(
        block["write"], block["tailed"], (0, 0)
    )


def scan_backward_kernel(
    gate_ref, conv_ref, before_ref, state_ref, state_before_ref, step_ref, meta_ref, segment_ref, taps_ref,
    state_taps_ref, head_ref, skip_ref, scanned_ref, states_ref, grad_ref, out_ref, state_grad, later, state_later,
):
    @pl.when(pl.program_id(0) == 0)
    def _():
        state_grad[...] = jnp.zeros_like(state_grad)
        later[...] = jnp.zeros_like(later)
        state_later[...] = jnp.zeros_like(state_later)

    block = scan_block(
        conv_ref, before_ref, state_ref, state_before_ref, step_ref, meta_ref, segment_ref, taps_ref, state_taps_ref,
        head_ref, True,
    )
    rows = SSD_BLOCK
    channels = conv_ref.shape[1]
    heads = channels // HP
    meta = meta_ref[...]
    read, write = block["read"], block["write"]
    inputs = block["wide_inputs"]
    scanned = scanned_ref[...]
    skip = skip_ref[0:1, :]
    gate_values = gate_ref[...].astype(FLOAT)
    gated, gate = silu_parts(gate_values)
    grad = grad_ref[...].astype(FLOAT)
    gate_grad = grad * (scanned + skip * inputs) * silu_slope(gate_values, gate)
    out_grad = grad * gated
    inputs_grad = skip * out_grad
    rounded = out_grad.astype(BFLOAT)
    wide_rounded = rounded.astype(FLOAT)
    carried = states_ref[0]
    after = state_grad[...]
    after_rounded = after.astype(BFLOAT)

    from_state = dot(write, after_rounded, (1, 0))
    entering = (wide_rounded * block["entered_wide"]).astype(BFLOAT)
    write_grad = dot(block["tailed"], after_rounded, (1, 1))
    read_grad = dot(entering, carried, (1, 1))
    last_entered = block["entered_wide"][rows - 1 : rows, :]
    through = jnp.sum(after * carried.astype(FLOAT), axis=0, keepdims=True) * last_entered
    state_grad[...] = after * last_entered + dot(read, entering, (0, 0))

    crossing_grad = jnp.zeros((rows, rows), FLOAT)
    pulled = []
    for head in range(heads):
        span = slice(head * HP, (head + 1) * HP)
        decay = turned_decay_of(block, head)
        weights = (block["crossing"] * decay).astype(BFLOAT)
        pulled.append(dot(weights, rounded[:, span], (1, 0)))
        crossing_grad = crossing_grad + dot(block["stepped"][:, span], rounded[:, span], (1, 1)) * decay
    pulled = jnp.concatenate(pulled, axis=1)
    crossing_rounded = crossing_grad.astype(BFLOAT)
    read_grad = read_grad + dot(crossing_rounded, write, (0, 0))
    write_grad = write_grad + dot(crossing_rounded, read, (1, 0))

    inputs_grad = inputs_grad + block["steps_wide"] * pulled + block["tail_wide"] * from_state
    sums = head_sum(
        jnp.concatenate(
            [
                wide_rounded * scanned - block["stepped"].astype(FLOAT) * pulled,
                inputs * pulled,
                inputs * from_state,
                jnp.broadcast_to(through, (8, channels)),
            ],
            axis=0,
        ),
        block["expand"],
    )
    leaving_grad = sums[2 * rows : 3 * rows] * block["leaving"]
    leaving_total = leaving_grad * block["steps"]
    last = sums[3 * rows : 3 * rows + 1] + jnp.sum(leaving_total, axis=0, keepdims=True)
    total_grad = sums[:rows] - leaving_total
    total_grad = total_grad + jnp.where(
        lax.broadcasted_iota(jnp.int32, total_grad.shape, 0) == rows - 1, last, 0.0
    )
    decay_grad = running_sum(total_grad, block["triangle"], (0, 0))
    steps_grad = sums[rows : 2 * rows] + leaving_grad + decay_grad * head_ref[1:2, :]
    raw_grad = steps_grad / (1.0 + jnp.exp(-block["raw"]))
    raw_grad = jnp.where(lax.broadcasted_iota(jnp.int32, raw_grad.shape, 1) < heads, raw_grad, 0.0)

    state_slope = silu_slope(block["state_summed"], block["state_gate"])
    state_pre = conv_back(
        jnp.concatenate([write_grad, read_grad], axis=1) * state_slope, state_later, state_taps_ref, meta
    )
    conv_pre = conv_back(inputs_grad * silu_slope(block["summed"], block["conv_gate"]), later, taps_ref, meta)
    out_ref[:, : 2 * NSTATE] = state_pre.astype(BFLOAT)
    start = 2 * NSTATE + 2 * HEAD_SIZE
    out_ref[:, start : start + channels] = gate_grad.astype(BFLOAT)
    out_ref[:, start + channels : start + 2 * channels] = conv_pre.astype(BFLOAT)
    out_ref[:, out_ref.shape[1] - LANES :] = raw_grad.astype(BFLOAT)


STATES = 2 * NSTATE
PAIR = 2 * HEAD_SIZE


def scan_specs(channels, order):
    half = SSD_BLOCK // 16
    before = lambda i: jnp.maximum(order(i) * half - 1, 0)
    gate_at = (STATES + PAIR) // channels
    step_at = (STATES + PAIR + 2 * channels + channels * QUERY_HEADS // DSSM * HEAD_SIZE) // LANES
    return [
        pl.BlockSpec((SSD_BLOCK, channels), lambda i: (order(i), gate_at)),
        pl.BlockSpec((SSD_BLOCK, channels), lambda i: (order(i), gate_at + 1)),
        pl.BlockSpec((16, channels), lambda i: (before(i), gate_at + 1)),
        pl.BlockSpec((SSD_BLOCK, STATES), lambda i: (order(i), 0)),
        pl.BlockSpec((16, STATES), lambda i: (before(i), 0)),
        pl.BlockSpec((SSD_BLOCK, LANES), lambda i: (order(i), step_at)),
        pl.BlockSpec((SSD_BLOCK, LANES), lambda i: (order(i), 0)),
        pl.BlockSpec((8, SSD_BLOCK), lambda i: (0, order(i))),
        whole((8, channels)),
        whole((8, STATES)),
        whole((8, LANES)),
        whole((8, channels)),
    ]


def scan_operands(projected, tables):
    return [projected] * 6 + [
        tables[name] for name in ("meta", "segment_row", "taps", "state_taps", "head", "skip")
    ]


def scan_cost(tokens, channels, factor):
    heads = channels // HP
    return pl.CostEstimate(
        flops=factor * 2 * tokens * SSD_BLOCK * (3 * channels + NSTATE),
        bytes_accessed=factor * tokens * channels * 12,
        transcendentals=tokens * SSD_BLOCK * heads,
    )


def scan_forward(projected, tables, mixed):
    tokens = projected.shape[0]
    channels = tables["taps"].shape[1]
    blocks = tokens // SSD_BLOCK
    return pl.pallas_call(
        scan_forward_kernel,
        grid=(blocks,),
        in_specs=scan_specs(channels, lambda i: i) + [pl.BlockSpec(memory_space=pl.ANY)],
        out_specs=[
            pl.BlockSpec((SSD_BLOCK, channels), lambda i: (i, 0)),
            pl.BlockSpec((SSD_BLOCK, channels), lambda i: (i, 0)),
            pl.BlockSpec((1, NSTATE, channels), lambda i: (i, 0, 0)),
        ],
        out_shape=[
            jax.ShapeDtypeStruct(mixed.shape, BFLOAT),
            jax.ShapeDtypeStruct((tokens, channels), FLOAT),
            jax.ShapeDtypeStruct((blocks, NSTATE, channels), BFLOAT),
        ],
        scratch_shapes=[pltpu.VMEM((NSTATE, channels), FLOAT)],
        input_output_aliases={12: 0},
        compiler_params=pltpu.CompilerParams(vmem_limit_bytes=SCAN_BYTES),
        cost_estimate=scan_cost(tokens, channels, 1),
        name="scan_forward",
    )(*scan_operands(projected, tables), mixed)


def scan_backward(projected, tables, scanned, carried, mixed_grad):
    tokens, width = projected.shape
    channels = tables["taps"].shape[1]
    blocks = tokens // SSD_BLOCK
    back = lambda i: (blocks - 1 - i, 0)
    return pl.pallas_call(
        scan_backward_kernel,
        grid=(blocks,),
        in_specs=scan_specs(channels, lambda i: blocks - 1 - i)
        + [
            pl.BlockSpec((SSD_BLOCK, channels), back),
            pl.BlockSpec((1, NSTATE, channels), lambda i: (blocks - 1 - i, 0, 0)),
            pl.BlockSpec((SSD_BLOCK, channels), back),
        ],
        out_specs=pl.BlockSpec((SSD_BLOCK, width), back),
        out_shape=jax.ShapeDtypeStruct((tokens, width), BFLOAT),
        scratch_shapes=[
            pltpu.VMEM((NSTATE, channels), FLOAT),
            pltpu.VMEM((8, channels), FLOAT),
            pltpu.VMEM((8, STATES), FLOAT),
        ],
        compiler_params=pltpu.CompilerParams(vmem_limit_bytes=SCAN_BYTES),
        cost_estimate=scan_cost(tokens, channels, 2),
        name="scan_backward",
    )(*scan_operands(projected, tables), scanned, carried, mixed_grad)


def turned(values, cosine, sine):
    return (values * cosine + pltpu.roll(values, HEAD_SIZE // 2, 1) * sine).astype(BFLOAT)


def turned_back(values, cosine, sine):
    return values * cosine + pltpu.roll(values * sine, HEAD_SIZE // 2, 1)


ATT_ROWS = 256


def attention_mask(meta_ref, segment_ref, start, extent):
    row = start + lax.broadcasted_iota(jnp.int32, (ATT_ROWS, extent), 0)
    column = lax.broadcasted_iota(jnp.int32, (ATT_ROWS, extent), 1)
    return (row >= column) & (meta_ref[start : start + ATT_ROWS, 0:1] == segment_ref[0:1, :extent])


def probabilities(query, keys, allowed):
    score = dot(query, keys, (1, 1)) * (1.0 / math.sqrt(HEAD_SIZE))
    score = jnp.where(allowed, score, NEGATIVE)
    exponent = jnp.exp(score - jnp.max(score, axis=1, keepdims=True))
    return exponent / jnp.sum(exponent, axis=1, keepdims=True)


def attention_forward_kernel(query_ref, key_ref, value_ref, cosine_ref, sine_ref, meta_ref, segment_ref, out_ref, keys):
    tokens = key_ref.shape[0]
    keys[...] = turned(key_ref[...].astype(FLOAT), cosine_ref[...], sine_ref[...])
    for start in range(0, tokens, ATT_ROWS):
        extent = start + ATT_ROWS
        here = slice(start, extent)
        allowed = attention_mask(meta_ref, segment_ref, start, extent)
        for unit in range(query_ref.shape[1] // HEAD_SIZE):
            span = slice(unit * HEAD_SIZE, (unit + 1) * HEAD_SIZE)
            query = turned(query_ref[here, span].astype(FLOAT), cosine_ref[here], sine_ref[here])
            weights = probabilities(query, keys[:extent], allowed).astype(BFLOAT)
            out_ref[here, span] = dot(weights, value_ref[:extent], (1, 0)).astype(BFLOAT)


def attention_backward_kernel(
    query_ref, key_ref, value_ref, cosine_ref, sine_ref, meta_ref, segment_ref, grad_ref, held_ref,
    out_ref, keys, key_sum, value_sum, query_grad_ref, shared_grad_ref, sems,
):
    del held_ref
    tokens = key_ref.shape[0]
    scale = 1.0 / math.sqrt(HEAD_SIZE)
    keys[...] = turned(key_ref[...].astype(FLOAT), cosine_ref[...], sine_ref[...])
    key_sum[...] = jnp.zeros_like(key_sum)
    value_sum[...] = jnp.zeros_like(value_sum)
    for start in range(0, tokens, ATT_ROWS):
        extent = start + ATT_ROWS
        here = slice(start, extent)
        allowed = attention_mask(meta_ref, segment_ref, start, extent)
        for unit in range(query_ref.shape[1] // HEAD_SIZE):
            span = slice(unit * HEAD_SIZE, (unit + 1) * HEAD_SIZE)
            query = turned(query_ref[here, span].astype(FLOAT), cosine_ref[here], sine_ref[here])
            weights = probabilities(query, keys[:extent], allowed)
            grad = grad_ref[here, span]
            weights_grad = dot(grad, value_ref[:extent], (1, 1))
            value_sum[:extent] += dot(weights.astype(BFLOAT), grad, (0, 0))
            mean_grad = jnp.sum(weights * weights_grad, axis=1, keepdims=True)
            score_grad = (weights * (weights_grad - mean_grad) * scale).astype(BFLOAT)
            query_grad = dot(score_grad, keys[:extent], (1, 0))
            key_sum[:extent] += dot(score_grad, query, (0, 0))
            query_grad_ref[here, span] = turned_back(query_grad, cosine_ref[here], sine_ref[here]).astype(BFLOAT)
    shared_grad_ref[:, :HEAD_SIZE] = turned_back(key_sum[...], cosine_ref[...], sine_ref[...]).astype(BFLOAT)
    shared_grad_ref[:, HEAD_SIZE:] = value_sum[...].astype(BFLOAT)
    end = out_ref.shape[1] - LANES
    width = query_grad_ref.shape[1]
    copies = [
        pltpu.make_async_copy(query_grad_ref, out_ref.at[:, end - width : end], sems.at[0]),
        pltpu.make_async_copy(shared_grad_ref, out_ref.at[:, STATES : STATES + PAIR], sems.at[1]),
    ]
    for copy in copies:
        copy.start()
    for copy in copies:
        copy.wait()


def attention_cost(tokens, width, factor):
    return pl.CostEstimate(
        flops=factor * 2 * tokens * tokens * width,
        bytes_accessed=factor * tokens * width * 8,
        transcendentals=tokens * tokens * width // (2 * HEAD_SIZE),
    )


def attention_specs(tokens, channels):
    width = channels * QUERY_HEADS // DSSM * HEAD_SIZE
    narrow = whole((tokens, HEAD_SIZE))
    return [
        pl.BlockSpec((tokens, width), lambda *_: (0, (STATES + PAIR + 2 * channels) // width)),
        pl.BlockSpec((tokens, HEAD_SIZE), lambda *_: (0, STATES // HEAD_SIZE)),
        pl.BlockSpec((tokens, HEAD_SIZE), lambda *_: (0, STATES // HEAD_SIZE + 1)),
        narrow,
        narrow,
        whole((tokens, LANES)),
        whole((8, tokens)),
    ]


def attention_operands(projected, tables):
    return [projected] * 3 + [tables[name] for name in ("cosine", "sine", "meta", "segment_row")]


def attention_forward(projected, tables):
    tokens = projected.shape[0]
    channels = tables["taps"].shape[1]
    width = channels * QUERY_HEADS // DSSM * HEAD_SIZE
    return pl.pallas_call(
        attention_forward_kernel,
        grid=(1,),
        in_specs=attention_specs(tokens, channels),
        out_specs=pl.BlockSpec((tokens, width), lambda *_: (0, channels // width)),
        out_shape=jax.ShapeDtypeStruct((tokens, channels + width), BFLOAT),
        scratch_shapes=[pltpu.VMEM((tokens, HEAD_SIZE), BFLOAT)],
        compiler_params=pltpu.CompilerParams(vmem_limit_bytes=SCAN_BYTES),
        cost_estimate=attention_cost(tokens, width, 1),
        name="attention_forward",
    )(*attention_operands(projected, tables))


def attention_backward(projected, tables, mixed_grad, projected_grad):
    tokens = projected.shape[0]
    channels = tables["taps"].shape[1]
    width = channels * QUERY_HEADS // DSSM * HEAD_SIZE
    return pl.pallas_call(
        attention_backward_kernel,
        grid=(1,),
        in_specs=attention_specs(tokens, channels)
        + [pl.BlockSpec((tokens, width), lambda *_: (0, channels // width)), pl.BlockSpec(memory_space=pl.ANY)],
        out_specs=pl.BlockSpec(memory_space=pl.ANY),
        out_shape=jax.ShapeDtypeStruct(projected_grad.shape, BFLOAT),
        scratch_shapes=[
            pltpu.VMEM((tokens, HEAD_SIZE), BFLOAT),
            pltpu.VMEM((tokens, HEAD_SIZE), FLOAT),
            pltpu.VMEM((tokens, HEAD_SIZE), FLOAT),
            pltpu.VMEM((tokens, width), BFLOAT),
            pltpu.VMEM((tokens, PAIR), BFLOAT),
            pltpu.SemaphoreType.DMA((2,)),
        ],
        input_output_aliases={8: 0},
        compiler_params=pltpu.CompilerParams(vmem_limit_bytes=SCAN_BYTES),
        cost_estimate=attention_cost(tokens, width, 3),
        name="attention_backward",
    )(*attention_operands(projected, tables), mixed_grad, projected_grad)


def mixer_tables(lengths, segment, position, conv_values, conv_states, scan_params):
    tokens = segment.shape[0]
    block = jnp.arange(tokens, dtype=jnp.int32) // SSD_BLOCK
    previous = jnp.concatenate([jnp.full((1,), -1, jnp.int32), segment[:-1]])
    first_previous = jnp.repeat(previous[::SSD_BLOCK], SSD_BLOCK)
    last_segment = jnp.repeat(segment[SSD_BLOCK - 1 :: SSD_BLOCK], SSD_BLOCK)
    length = jnp.sum(
        jnp.where(segment[:, None] == jnp.arange(lengths.shape[0], dtype=jnp.int32)[None, :], lengths[None, :], 0),
        axis=1,
    )
    columns = [
        segment,
        position,
        length - 1 - position,
        segment == first_previous,
        segment == last_segment,
    ]
    meta = jnp.stack([column.astype(FLOAT) for column in columns], axis=1)
    half_width = HEAD_SIZE // 2
    frequency = ROPE_BASE ** (-2.0 * jnp.arange(half_width, dtype=FLOAT) / HEAD_SIZE)
    angle = position.astype(FLOAT)[:, None] * frequency[None, :]
    cosine, sine = jnp.cos(angle), jnp.sin(angle)
    heads = scan_params.shape[1]
    head = jnp.stack([scan_params[0], -jnp.exp(scan_params[1]), scan_params[2]])
    return dict(
        meta=jnp.pad(meta, ((0, 0), (0, LANES - meta.shape[1]))),
        segment_row=jnp.broadcast_to(segment.astype(FLOAT)[None, :], (8, tokens)),
        taps=jnp.pad(conv_values.astype(FLOAT), ((0, 3), (0, 0))),
        state_taps=jnp.pad(conv_states.astype(FLOAT), ((0, 3), (0, 0))),
        head=jnp.pad(head, ((0, 5), (0, LANES - heads))),
        skip=jnp.broadcast_to(jnp.repeat(scan_params[2], HP)[None, :], (8, heads * HP)),
        cosine=jnp.concatenate([cosine, cosine], axis=1),
        sine=jnp.concatenate([-sine, sine], axis=1),
    )


HALVES = 2


def matrix_rows(values):
    return values.reshape(values.shape[0] * values.shape[1], values.shape[2])


def cut_tiles(width, tile):
    return [(low, min(low + tile, width)) for low in range(0, width, tile)]


def spread_kernel(mask, count, left_ref, right_ref, chosen_ref, *rest):
    weights, (out_ref, narrow_ref, out_tile, narrow, sems) = rest[:count], rest[-5:]
    rows = left_ref.shape[0]
    shards = weights[0].shape[0]
    depth = shards // HALVES
    start = pl.multiple_of((lax.axis_index("col") ^ mask) * rows, rows)
    here = pl.ds(start, rows)

    def through(ref, low, high):
        return dot(left_ref[...], matrix_rows(ref[:depth, :rows, low:high]), (1, 0)) + dot(
            right_ref[...], matrix_rows(ref[depth:, :rows, low:high]), (1, 0)
        )

    lower = weights[-1].shape[2] - LANES
    narrow[...] = (chosen_ref[here, :] * through(weights[-1], lower, lower + LANES)).astype(BFLOAT)
    copies = [pltpu.make_async_copy(narrow, narrow_ref.at[here, :], sems.at[0])]
    copies[0].start()
    column = 0
    for ref in weights:
        for low, high in cut_tiles(ref.shape[2] - (LANES if ref is weights[-1] else 0), 512):
            span = slice(column, column + high - low)
            column += high - low
            raised = matrix_rows(ref[:, rows : rows + NADAPT * RANK // shards, low:high])
            out_tile[:, span] = (through(ref, low, high) + dot(narrow[...], raised, (1, 0))).astype(BFLOAT)
            copies.append(
                pltpu.make_async_copy(out_tile.at[:, span], out_ref.at[here, span], sems.at[len(copies)])
            )
            copies[-1].start()
    for copy in copies:
        copy.wait()


def weights_width(gathered):
    return sum(part.shape[2] for part in gathered) - LANES


def spread_block(mask, halves, gathered, selector, held):
    rows, half = halves[0].shape
    width = weights_width(gathered)
    total = selector.shape[0]
    fast, free = pl.BlockSpec(memory_space=pltpu.VMEM), pl.BlockSpec(memory_space=pl.ANY)
    operands = [*halves, selector, *gathered]
    in_specs = [fast] * len(operands)
    aliases = {}
    if held is not None:
        aliases = {len(operands): 0, len(operands) + 1: 1}
        operands += list(held)
        in_specs += [free] * 2
    copies = 1 + sum(-(-part.shape[2] // 512) for part in gathered)
    return pl.pallas_call(
        functools.partial(spread_kernel, mask, len(gathered)),
        in_specs=in_specs,
        out_specs=[free] * 2,
        out_shape=[
            jax.ShapeDtypeStruct((total, width), BFLOAT),
            jax.ShapeDtypeStruct((total, LANES), BFLOAT),
        ],
        scratch_shapes=[
            pltpu.VMEM((rows, width), BFLOAT),
            pltpu.VMEM((rows, LANES), BFLOAT),
            pltpu.SemaphoreType.DMA((copies,)),
        ],
        input_output_aliases=aliases,
        compiler_params=pltpu.CompilerParams(vmem_limit_bytes=DENSE_BYTES),
        cost_estimate=pl.CostEstimate(
            flops=4 * rows * half * (width + LANES), bytes_accessed=2 * rows * (2 * half + width), transcendentals=0
        ),
        name="spread_block",
    )(*operands)


def collect_kernel(masks, count, values_ref, *refs):
    weights, outs = refs[:count], refs[count:]
    rows = values_ref.shape[0] // 4
    shards = weights[0].shape[0]
    half = shards // HALVES * rows
    width = values_ref.shape[1]
    starts, column = [], 0
    for ref in weights:
        high = min(column + ref.shape[2], width)
        starts.append((column, high))
        column = high
    for at, mask in enumerate(masks):
        here = pl.ds(pl.multiple_of((lax.axis_index("col") ^ mask) * rows, rows), rows)
        first, second = outs[2 * at], outs[2 * at + 1]

        def through(cut):
            total = None
            for (low, high), ref in zip(starts, weights):
                part = dot(values_ref[here, low:high], cut(ref, high - low), (1, 1))
                total = part if total is None else total + part
            return total

        for shard in range(shards):
            out_ref = first if shard < shards // HALVES else second
            column = shard * rows % half
            out_ref[:, column : column + rows] = through(lambda ref, wide: ref[shard, :rows, :wide]).astype(
                out_ref.dtype
            )
        first[:, half:] = through(
            lambda ref, wide: matrix_rows(ref[:, rows : rows + NADAPT * RANK // shards, :wide])
        ).astype(first.dtype)


def collect_blocks(masks, values, gathered, types):
    rows = values.shape[0] // 4
    half = gathered[0].shape[0] // HALVES * rows
    fast = pl.BlockSpec(memory_space=pltpu.VMEM)
    out_shape = []
    for pair in types:
        out_shape.append(jax.ShapeDtypeStruct((rows, half + LANES), pair[0]))
        out_shape.append(jax.ShapeDtypeStruct((rows, half), pair[1]))
    outs = pl.pallas_call(
        functools.partial(collect_kernel, masks, len(gathered)),
        in_specs=[fast] * (1 + len(gathered)),
        out_specs=[fast] * len(out_shape),
        out_shape=out_shape,
        compiler_params=pltpu.CompilerParams(vmem_limit_bytes=DENSE_BYTES),
        cost_estimate=pl.CostEstimate(
            flops=4 * len(masks) * rows * half * values.shape[1],
            bytes_accessed=2 * len(masks) * rows * (values.shape[1] + 4 * half),
            transcendentals=0,
        ),
        name="collect_blocks",
    )(values, *gathered)
    return [tuple(outs[2 * at : 2 * at + 2]) for at in range(len(masks))]


def root_mean(values):
    return lax.rsqrt(jnp.mean(values * values, axis=1, keepdims=True) + EPSILON)


def finish_kernel(kind, first_own, first_near, first_far, second_own, second_near, second_far, lower_ref, chosen_ref,
                  *refs):
    half = second_own.shape[1]
    wide = lambda ref: ref[...].astype(FLOAT)
    first = wide(first_own) + wide(first_near) + wide(first_far)
    second = wide(second_own) + wide(second_near) + wide(second_far)
    inner = (chosen_ref[...] * first[:, half:]).astype(BFLOAT)
    shards, tall, _ = lower_ref.shape
    rows = tall - NADAPT * RANK // shards
    summed = jnp.concatenate([first[:, :half], second], axis=1) + dot(
        inner, matrix_rows(lower_ref[:, :rows, :]), (1, 1)
    )
    if kind == "output":
        residual_ref, out_ref, inner_ref = refs
        inner_ref[...] = inner
        out_ref[...] = (residual_ref[...] + summed).astype(BFLOAT)
        return
    if kind == "forward":
        residual_ref, gain_ref, out_ref, inner_ref, left_ref, right_ref = refs
        hidden = residual_ref[...] + summed
        normed = (hidden * root_mean(hidden) * gain_ref[0:1, :]).astype(BFLOAT)
        out_ref[...] = hidden
    else:
        values_ref, upstream_ref, gain_ref = refs[:3]
        values = values_ref[...]
        scale = root_mean(values)
        weighted = summed * gain_ref[0:1, :]
        mean = jnp.mean(weighted * values, axis=1, keepdims=True)
        hidden = upstream_ref[...].astype(FLOAT) + scale * weighted - values * (scale * scale * scale * mean)
        normed = hidden.astype(BFLOAT)
        if kind == "input":
            out_ref, inner_ref = refs[3:]
            inner_ref[...] = inner
            out_ref[...] = normed
            return
        out_ref, inner_ref, left_ref, right_ref = refs[3:]
        out_ref[...] = hidden
    inner_ref[...] = inner
    left_ref[...] = normed[:, :half]
    right_ref[...] = normed[:, half:]


def finish(kind, parts, gathered, own_selector, *operands):
    rows = own_selector.shape[0]
    half = parts[3].shape[1]
    shards, tall, full = gathered[-1].shape
    model = HALVES * half
    result = BFLOAT if kind in ("output", "input") else FLOAT
    out_shape = [jax.ShapeDtypeStruct((rows, model), result), jax.ShapeDtypeStruct((rows, LANES), BFLOAT)]
    if kind in ("forward", "backward"):
        out_shape += [jax.ShapeDtypeStruct((rows, half), BFLOAT)] * 2
    given = [*parts, gathered[-1], own_selector, *operands]
    in_specs = [whole(value.shape) for value in given]
    in_specs[6] = pl.BlockSpec((shards, tall, LANES), lambda *_: (0, 0, full // LANES - 1))
    return pl.pallas_call(
        functools.partial(finish_kernel, kind),
        grid=(1,),
        in_specs=in_specs,
        out_specs=[whole(shape.shape) for shape in out_shape],
        out_shape=out_shape,
        compiler_params=pltpu.CompilerParams(vmem_limit_bytes=DENSE_BYTES),
        cost_estimate=pl.CostEstimate(
            flops=2 * rows * model * LANES, bytes_accessed=rows * model * 20, transcendentals=0
        ),
        name="finish_" + kind,
    )(*given)


def send_kernel(target_column, target_row, tokens_ref, adapter_ref, sent_ref, matrix_ref):
    rows = tokens_ref.shape[0]
    model = tokens_ref.shape[1]
    peer = adapter_ref.shape[0]
    column, row = target_column[:, 0:1], target_row[0:1, :]
    earlier = lax.broadcasted_iota(jnp.int32, (rows, rows), 0) < lax.broadcasted_iota(jnp.int32, (rows, rows), 1)
    same = jnp.where((column // rows == row // rows) & earlier, 1.0, 0.0)
    place = (row // rows) * peer + jnp.sum(same, axis=0, keepdims=True).astype(jnp.int32)
    matrix = (lax.broadcasted_iota(jnp.int32, (rows, rows), 0) == place).astype(BFLOAT)
    matrix_ref[...] = matrix
    sent_ref[:, :model] = dot(matrix, tokens_ref[...], (1, 0)).astype(BFLOAT)
    lane = lax.broadcasted_iota(jnp.int32, (rows, LANES), 1)
    slots = jnp.where(lane == 0, column % rows, 0).astype(FLOAT).astype(BFLOAT)
    notes = dot(matrix, slots, (1, 0))
    sent_ref[:, model:] = jnp.where(lane == 0, notes, adapter_ref[0:1, :]).astype(BFLOAT)


def send_tokens(target, tokens, adapters, peer):
    rows, model = tokens.shape
    notes = jnp.pad(adapters.astype(FLOAT), (1, LANES - 1 - adapters.shape[0]))
    return pl.pallas_call(
        send_kernel,
        in_specs=[pl.BlockSpec(memory_space=pltpu.VMEM)] * 4,
        out_specs=[pl.BlockSpec(memory_space=pltpu.VMEM)] * 2,
        out_shape=[
            jax.ShapeDtypeStruct((rows, model + LANES), BFLOAT),
            jax.ShapeDtypeStruct((rows, rows), BFLOAT),
        ],
        compiler_params=pltpu.CompilerParams(vmem_limit_bytes=DENSE_BYTES),
        name="send_tokens",
    )(
        jnp.broadcast_to(target[:, None], (rows, LANES)),
        jnp.broadcast_to(target[None, :], (8, rows)),
        tokens,
        jnp.broadcast_to(notes[None, :], (peer, LANES)),
    )


def arrive_kernel(arrived_ref, gain_ref, own_ref, matrix_ref, left_ref, right_ref):
    rows, model = own_ref.shape
    slots = arrived_ref[:, model:].astype(FLOAT).T[0:1, :]
    row = lax.broadcasted_iota(jnp.int32, (rows, rows), 0).astype(FLOAT)
    matrix = (row == slots).astype(BFLOAT)
    matrix_ref[...] = matrix
    own = dot(matrix, arrived_ref[:, :model], (1, 0))
    own_ref[...] = own
    normed = (own * root_mean(own) * gain_ref[0:1, :]).astype(BFLOAT)
    left_ref[...] = normed[:, : model // HALVES]
    right_ref[...] = normed[:, model // HALVES :]


def arrive_tokens(arrived, gain):
    rows, model = arrived.shape[0], arrived.shape[1] - LANES
    return pl.pallas_call(
        arrive_kernel,
        in_specs=[pl.BlockSpec(memory_space=pltpu.VMEM)] * 2,
        out_specs=[pl.BlockSpec(memory_space=pltpu.VMEM)] * 4,
        out_shape=[
            jax.ShapeDtypeStruct((rows, model), FLOAT),
            jax.ShapeDtypeStruct((rows, rows), BFLOAT),
            jax.ShapeDtypeStruct((rows, model // HALVES), BFLOAT),
            jax.ShapeDtypeStruct((rows, model // HALVES), BFLOAT),
        ],
        compiler_params=pltpu.CompilerParams(vmem_limit_bytes=DENSE_BYTES),
        name="arrive_tokens",
    )(arrived, gain)


GATE_WIDTH = DSSM // QUERY_HEADS
PAIR_WIDTH = 2 * KEY_VALUE_HEADS * HEAD_SIZE // QUERY_HEADS
STATE_WIDTH = 2 * NSTATE // QUERY_HEADS
STEP_WIDTH = NH // QUERY_HEADS
ALL_AXES = ("row", "col")


def pad_columns(values, width):
    return jnp.pad(values, ((0, 0), (0, width - values.shape[1])))


def after(values, *earlier):
    return lax.optimization_barrier((values, *earlier))[0]


def after_all(values, *earlier):
    return lax.optimization_barrier((*values, *earlier))[: len(values)]


def unit_parts(values, units):
    cuts = [0]
    for width in (GATE_WIDTH, GATE_WIDTH, HEAD_SIZE, PAIR_WIDTH, STATE_WIDTH, STEP_WIDTH):
        cuts.append(cuts[-1] + width)
    return [
        jnp.concatenate(
            [values[:, unit * UNIT_IN + low : unit * UNIT_IN + high] for unit in range(units)], axis=1
        )
        for low, high in zip(cuts[:-1], cuts[1:])
    ]


def restore_units(parts, units):
    ordered = []
    for unit in range(units):
        for part in parts:
            width = part.shape[1] // units
            ordered.append(part[:, unit * width : (unit + 1) * width])
    return jnp.concatenate(ordered, axis=1)


def split_halves(values, units, first, axis):
    block = values.shape[axis] // units
    take = lambda low, high: lax.slice_in_dim(values, low, high, axis=axis)
    parts = [take(unit * block, unit * block + first) for unit in range(units)]
    parts += [take(unit * block + first, (unit + 1) * block) for unit in range(units)]
    return jnp.concatenate(parts, axis=axis)


def join_halves(values, units, first, axis):
    block = values.shape[axis] // units
    rest = block - first
    take = lambda low, high: lax.slice_in_dim(values, low, high, axis=axis)
    parts = []
    for unit in range(units):
        parts.append(take(unit * first, (unit + 1) * first))
        parts.append(take(units * first + unit * rest, units * first + (unit + 1) * rest))
    return jnp.concatenate(parts, axis=axis)


def quick(rows):
    return lax.axis_size("col") == 4 and lax.axis_size("row") == 8 and rows == 256


def flip(values, mask):
    return lax.ppermute(values, "col", [(i, i ^ mask) for i in range(4)])


def gather_blocks(halves):
    left, right = halves
    far_left, near_right = flip(left, 2), flip(right, 1)
    near_left, far_right = flip(left, 1), flip(right, 2)
    corner_left, corner_right = flip(far_left, 1), flip(near_right, 2)
    return [
        (0, (left, right)),
        (1, (near_left, near_right)),
        (2, (far_left, far_right)),
        (3, (corner_left, corner_right)),
    ]


def rows_of(values, block, rows):
    return lax.dynamic_slice_in_dim(values, block * rows, rows, 0)


def spread_gathered(blocks, gathered, selector):
    held = None
    for mask, values in blocks:
        held = spread_block(mask, values, gathered, selector, held)
    return held


def spread_project(halves, gathered, selector):
    rows = halves[0].shape[0]
    if quick(rows):
        return spread_gathered(gather_blocks(halves), gathered, selector)
    wide, narrow_factor = gathered
    width = narrow_factor.shape[1]
    both = product(lax.all_gather(jnp.concatenate(halves, axis=1), "col", axis=0, tiled=True), wide)
    narrow = (selector * both[:, width:]).astype(BFLOAT)
    return (both[:, :width] + product(narrow, narrow_factor)).astype(BFLOAT), narrow


def collect_start(values, gathered, earlier=()):
    (corner,) = collect_blocks([3], values, gathered, [(BFLOAT, BFLOAT)])
    arriving = flip(corner[0], 1), flip(corner[1], 2)
    values = after(values, *earlier) if earlier else values
    near, far, own = collect_blocks([1, 2, 0], values, gathered, [(BFLOAT, FLOAT), (FLOAT, BFLOAT), (FLOAT, FLOAT)])
    return own, flip(near[0], 1), flip(far[1], 2), far[0], near[1], arriving


def collect_middle(started):
    own, near_first, far_second, far_first, near_second, arriving = started
    onward = [
        (kept + part.astype(FLOAT)).astype(BFLOAT) for kept, part in zip((far_first, near_second), arriving)
    ]
    return (own, near_first, far_second), onward


def collect_onward(onward):
    return flip(onward[0], 2), flip(onward[1], 1)


def collect_end(kept, last, kind, gathered, own_selector, *operands):
    own, near_first, far_second = kept
    parts = [own[0], near_first, last[0], own[1], far_second, last[1]]
    return finish(kind, parts, gathered, own_selector, *operands)


def collect_project(values, gathered, kind, own_selector, *operands):
    rows, model = own_selector.shape[0], operands[0].shape[1]
    if quick(rows):
        kept, onward = collect_middle(collect_start(values, gathered))
        return collect_end(kept, collect_onward(onward), kind, gathered, own_selector, *operands)
    wide, narrow_factor = gathered
    width = narrow_factor.shape[1]
    partial = jnp.concatenate(
        [contract_last(values, wide[:, :width]), contract_last(values, narrow_factor)], axis=1
    ).astype(BFLOAT)
    summed = lax.psum_scatter(partial, "col", scatter_dimension=0, tiled=True).astype(FLOAT)
    inner = (own_selector * summed[:, model:]).astype(BFLOAT)
    summed = summed[:, :model] + contract_last(inner, wide[:, width:])
    if kind == "output":
        return (operands[0] + summed).astype(BFLOAT), inner
    if kind == "forward":
        residual, gain = operands
        hidden = residual + summed
        return hidden, inner, *cut_halves(rms_norm(hidden, gain[0]).astype(BFLOAT))
    values, upstream, gain = operands
    _, back = jax.vjp(lambda given: rms_norm(given, gain[0]), values)
    hidden = upstream.astype(FLOAT) + back(summed)[0]
    if kind == "input":
        return hidden.astype(BFLOAT), inner
    return hidden, inner, *cut_halves(hidden.astype(BFLOAT))


def cut_halves(values):
    half = values.shape[1] // HALVES
    return values[:, :half], values[:, half:]


def local(
    tokens_in,
    cotangent,
    target,
    sequence_lengths,
    sequence_adapter,
    norm_gains,
    weight_in,
    conv_values,
    conv_states,
    scan_params,
    weight_mix,
    weight_feed,
    weight_down,
    in_lower,
    in_raise,
    mix_lower,
    mix_raise,
    feed_lower,
    feed_raise,
    down_lower,
    down_raise,
):
    cols = lax.axis_size("col")
    rows_axis = lax.axis_size("row")
    col = lax.axis_index("col")
    devices = cols * rows_axis
    rows = tokens_in.shape[0]
    model = tokens_in.shape[1]
    total = rows * cols
    units = QUERY_HEADS // cols
    channels = units * GATE_WIDTH
    peer = rows // devices
    lengths, adapters = sequence_lengths[0], sequence_adapter[0]
    sequences = lengths.shape[0]
    fast = quick(rows)
    key_head = col * units // (QUERY_HEADS // KEY_VALUE_HEADS)
    exchange = lambda values: lax.all_to_all(values, ALL_AXES, split_axis=0, concat_axis=0, tiled=True)

    sent, send_matrix = send_tokens(target, tokens_in, adapters, peer)
    shards = []

    def gather_weight(weight, lower, raised):
        top = jnp.concatenate([weight, lower], axis=1)
        if fast:
            bottom = pad_columns(raised, top.shape[1])
            shards.append(jnp.concatenate([top, bottom], axis=0))
            return (lax.all_gather(shards[-1], "row", axis=0),)
        wide = lax.all_gather(top, "row", axis=0, tiled=True)
        return wide, lax.all_gather(raised, "row", axis=0, tiled=True)

    depth = weight_in.shape[0]
    height = depth + in_raise.shape[0]
    given = after(jnp.concatenate([weight_in, in_raise], axis=0), send_matrix)
    gates, convs, queries, pairs, states, steps = unit_parts(given, units)
    pair_width, state_width = pairs.shape[1], states.shape[1]
    taps = jnp.concatenate([jnp.zeros((KCONV + 1, pair_width), BFLOAT), conv_states], axis=1)
    taps = jnp.pad(taps, ((0, 16 - KCONV - 1), (0, 0)))
    shared = jnp.concatenate([jnp.concatenate([pairs, states], axis=1), taps], axis=0)
    own_columns = jnp.concatenate([gates, convs, queries, pad_columns(steps, LANES)], axis=1)
    if fast:
        shared_shard = shared
        shared = lax.all_gather(shared_shard, "row", axis=0)
        weights_own = gather_weight(own_columns[:depth], in_lower, own_columns[depth:])
        sent = after(sent, shared_shard, shards[0])
    arrived = exchange(sent)
    gains = jnp.broadcast_to(norm_gains.astype(FLOAT)[:, None, :], (2, 8, model))
    if fast:
        near, far = flip(shared, 1), flip(shared, 2)
        arrived = after(arrived, near, far)
    own_input, place_matrix, *normed_one = arrive_tokens(arrived.reshape(rows, model + LANES), gains[0])
    blocks_one = gather_blocks(normed_one) if fast else normed_one
    if fast:
        held = jnp.zeros((cols,) + shared.shape, BFLOAT)
        for block, values in ((col, shared), (col ^ 1, near), (col ^ 2, far)):
            held = lax.dynamic_update_index_in_dim(held, values, block, 0)
        split = shared.shape[0] // 2
        corner = jnp.concatenate([flip(near[:split], 2), flip(far[split:], 1)], axis=0)
        held = lax.dynamic_update_index_in_dim(held, corner, col ^ 3, 0)
    else:
        held = lax.all_gather(shared, "col", axis=0)
    all_pairs = jnp.concatenate([held[at, ..., :height, :pair_width] for at in range(cols)], axis=-1)
    pick = lambda start: lax.select_n(
        key_head,
        *[all_pairs[..., start + at * HEAD_SIZE : start + (at + 1) * HEAD_SIZE] for at in range(KEY_VALUE_HEADS)],
    )
    shared_columns = jnp.concatenate(
        [held[at, ..., :height, pair_width:] for at in range(cols)]
        + [pick(0), pick(KEY_VALUE_HEADS * HEAD_SIZE)],
        axis=-1,
    )
    tap_rows = held[:, 0] if fast else held
    all_taps = jnp.concatenate(
        [tap_rows[at, height : height + KCONV + 1, pair_width:] for at in range(cols)], axis=1
    )
    if fast:
        weights_in = (shared_columns, *weights_own)
    else:
        columns = jnp.concatenate([shared_columns, own_columns], axis=1)
        weights_in = gather_weight(columns[:depth], in_lower, columns[depth:])
    weights_mix = gather_weight(
        after(split_halves(weight_mix, units, GATE_WIDTH, 0).T, sent),
        mix_raise.T,
        split_halves(mix_lower, units, GATE_WIDTH, 0).T,
    )
    weights_feed = gather_weight(
        after(split_halves(weight_feed, units, UNIT_FF, 1), arrived),
        feed_lower,
        split_halves(feed_raise, units, UNIT_FF, 1),
    )

    source_adapters = arrived.reshape(rows, model + LANES)[::peer, model + 1 : model + 1 + sequences].astype(jnp.int32)
    segment, position, selector = sequence_tables(lengths, adapters, total)
    own_selector = rows_of(selector, col, rows)
    own_segment = rows_of(segment, col, rows)
    tables = mixer_tables(lengths, segment, position, conv_values, all_taps, scan_params)

    def compact_grad(narrow, values):
        parts = [
            lax.dynamic_slice_in_dim(narrow, adapters[at] * RANK, RANK, 1)
            * (own_segment == at).astype(BFLOAT)[:, None]
            for at in range(sequences)
        ]
        grad = contract_first(jnp.concatenate(parts, axis=1), values).astype(BFLOAT)
        kept = sequences * RANK
        grad = grad.reshape(kept, devices, model // devices).transpose(1, 0, 2)
        return grad.reshape(devices, peer, kept * model // devices // peer)

    def expand_grad(dealt):
        kept = sequences * RANK
        dealt = dealt.reshape(devices * kept, model // devices)
        adapter_row = (source_adapters[:, :, None] * RANK + jnp.arange(RANK, dtype=jnp.int32)).reshape(-1)
        chosen = (jnp.arange(NADAPT * RANK, dtype=jnp.int32)[:, None] == adapter_row[None, :]).astype(BFLOAT)
        return product(chosen, dealt)

    def send_back(values, grads, earlier=()):
        back = contract_first(place_matrix, values).astype(BFLOAT).reshape(devices, peer, model)
        payload = jnp.concatenate([back, *grads], axis=2)
        payload = after(payload, *earlier) if earlier else payload
        payloads.append(payload)
        return exchange(payload)

    payloads = []

    def take_back(dealt, count):
        returned = contract_first(send_matrix, dealt[:, :, :model].reshape(rows, model)).astype(BFLOAT)
        width = (dealt.shape[2] - model) // max(count, 1)
        return returned, [
            expand_grad(dealt[:, :, model + at * width : model + (at + 1) * width]) for at in range(count)
        ]

    projected, inner_in = (spread_gathered if fast else spread_project)(blocks_one, weights_in, selector)

    sent_grad = product(send_matrix, cotangent).astype(BFLOAT).reshape(devices, peer, model)
    arrived_grad = exchange(after(sent_grad, normed_one[0])).reshape(rows, model)
    branch_two = product(place_matrix, arrived_grad).astype(BFLOAT)
    weights_down = gather_weight(after(weight_down.T, projected), down_raise.T, down_lower.T)

    mixed_out = attention_forward(projected, tables)
    mixed_out, scanned, carried = scan_forward(projected, tables, mixed_out)
    hidden, inner_out, *normed_two = collect_project(mixed_out, weights_mix, "forward", own_selector, own_input, gains[1])
    gate_up, inner_feed = spread_project(normed_two, weights_feed, selector)
    act_grad, narrow_two = spread_project(cut_halves(after(branch_two, projected)), weights_down, selector)
    half_feed = units * UNIT_FF
    gate_part, up_part = gate_up[:, :half_feed].astype(FLOAT), gate_up[:, half_feed:].astype(FLOAT)
    gate = jax.nn.sigmoid(gate_part)
    silu = gate_part * gate
    activated = (silu * up_part).astype(BFLOAT)
    wide_grad = act_grad.astype(FLOAT)
    feed_grad = jnp.concatenate(
        [wide_grad * up_part * (gate * (1.0 + gate_part * (1.0 - gate))), wide_grad * silu], axis=1
    ).astype(BFLOAT)
    hidden_grad, narrow_three, *branch_one = collect_project(
        feed_grad, weights_feed, "backward", own_selector, hidden, branch_two, gains[1]
    )
    mixed_grad, narrow_one = spread_project(branch_one, weights_mix, selector)

    if fast:
        started = collect_start(after(activated, mixed_grad), weights_down)
        projected_grad = scan_backward(
            projected, tables, scanned, carried, after(mixed_grad, started[0][0], started[3])
        )
        kept, onward = collect_middle((*started[:5], [after(part, projected_grad) for part in started[5]]))
        projected_grad = attention_backward(projected, tables, mixed_grad, after(projected_grad, *onward))
        last = collect_onward(onward)
        started_in = collect_start(projected_grad, weights_in, last)
        kept_in, onward_in = collect_middle(started_in)
        block_out, inner_down = collect_end(
            kept, last, "output", weights_down, own_selector, after(hidden, *onward_in, *kept_in[1:])
        )
    else:
        block_out, inner_down = collect_project(activated, weights_down, "output", own_selector, hidden)
        projected_grad = scan_backward(projected, tables, scanned, carried, mixed_grad)
        projected_grad = attention_backward(projected, tables, mixed_grad, projected_grad)
    dealt_out = send_back(
        block_out,
        [
            compact_grad(inner_down, branch_two),
            compact_grad(narrow_three, jnp.concatenate(normed_two, axis=1)),
            compact_grad(inner_out, jnp.concatenate(branch_one, axis=1)),
        ],
    )

    def sum_rows(values):
        return lax.psum_scatter(values.astype(BFLOAT), "row", scatter_dimension=0, tiled=True).astype(FLOAT)

    early_parts = [
        contract_first(narrow_one, mixed_out),
        contract_first(inner_feed, feed_grad),
        contract_first(narrow_two, activated),
    ]
    early = sum_rows(jnp.concatenate(early_parts, axis=1))

    raise_grad = contract_first(inner_in, projected_grad)
    key_columns = raise_grad[:, STATES : STATES + HEAD_SIZE]
    value_columns = raise_grad[:, STATES + HEAD_SIZE : STATES + PAIR]
    mine = [(key_head == at).astype(FLOAT) for at in range(KEY_VALUE_HEADS)]
    pair_grad = jnp.concatenate([part * here for part in (key_columns, value_columns) for here in mine], axis=1)
    stacked = jnp.stack(
        [
            jnp.concatenate(
                [
                    pair_grad[:, at * pair_width : (at + 1) * pair_width],
                    raise_grad[:, at * state_width : (at + 1) * state_width],
                ],
                axis=1,
            )
            for at in range(cols)
        ]
    )
    if fast:
        to_send = stacked.astype(BFLOAT)
        piece = lambda block: lax.dynamic_index_in_dim(to_send, block, 0, False)
        near_sum = lambda block: lax.dynamic_index_in_dim(stacked, block, 0, False)
        pair_sums = flip(jnp.stack([piece(col ^ 1), piece(col ^ 3)]), 1).astype(FLOAT)
        far_sum = (near_sum(col ^ 2) + pair_sums[1]).astype(BFLOAT)
        shared_sum = near_sum(col) + pair_sums[0] + flip(far_sum, 2).astype(FLOAT)
    else:
        shared_sum = lax.psum_scatter(
            stacked.astype(BFLOAT).reshape(cols * NADAPT * RANK, -1), "col", scatter_dimension=0, tiled=True
        ).astype(FLOAT)
    late = sum_rows(jnp.concatenate([shared_sum, raise_grad[:, STATES + PAIR :]], axis=1))
    if fast:
        input_grad, narrow_four = collect_end(
            kept_in,
            collect_onward(onward_in),
            "input",
            weights_in,
            own_selector,
            own_input,
            after(hidden_grad, payloads[0]),
            gains[0],
        )
    else:
        input_grad, narrow_four = collect_project(
            projected_grad, weights_in, "input", own_selector, own_input, hidden_grad, gains[0]
        )
    dealt_grad = send_back(
        input_grad, [compact_grad(narrow_four, jnp.concatenate(normed_one, axis=1))], [dealt_out]
    )
    dealt_out, early, late = after_all((dealt_out, early, late), payloads[-1])
    early_cuts = [0, early_parts[0].shape[1]]
    early_cuts.append(early_cuts[1] + early_parts[1].shape[1])
    grad_mix_lower = join_halves(early[:, : early_cuts[1]], units, GATE_WIDTH, 1).T
    grad_feed_raise = join_halves(early[:, early_cuts[1] : early_cuts[2]], units, UNIT_FF, 1)
    grad_down_lower = early[:, early_cuts[2] :].T

    shared_width = pair_width + state_width
    cuts = [shared_width]
    for width in (channels, channels, units * HEAD_SIZE, units * STEP_WIDTH):
        cuts.append(cuts[-1] + width)
    gate_columns, conv_columns, query_columns, step_columns = [
        late[:, low:high] for low, high in zip(cuts[:-1], cuts[1:])
    ]
    grad_in_raise = restore_units(
        [
            gate_columns,
            conv_columns,
            query_columns,
            late[:, :pair_width],
            late[:, pair_width:shared_width],
            step_columns,
        ],
        units,
    )

    returned_out, (grad_down_raise, grad_feed_lower, grad_mix_raise) = take_back(dealt_out, 3)
    returned_grad, (grad_in_lower,) = take_back(dealt_grad, 1)
    return (
        returned_out,
        returned_grad,
        grad_in_lower.T,
        grad_in_raise,
        grad_mix_lower,
        grad_mix_raise,
        grad_feed_lower.T,
        grad_feed_raise,
        grad_down_lower,
        grad_down_raise,
    )


def solution(mesh):
    in_specs = (
        P(("row", "col"), None),
        P(("row", "col"), None),
        P(("row", "col")),
        P("row", None),
        P("row", None),
        P(),
        P("row", "col"),
        P(None, "col"),
        P(None, "col"),
        P(None, "col"),
        P("col", "row"),
        P("row", "col"),
        P("col", "row"),
        P("row", None),
        P("row", "col"),
        P("col", "row"),
        P(None, "row"),
        P("row", None),
        P("row", "col"),
        P("col", "row"),
        P(None, "row"),
    )
    out_specs = (
        P(("row", "col"), None),
        P(("row", "col"), None),
        P(("row", "col"), None),
        P("row", "col"),
        P("col", "row"),
        P(None, ("row", "col")),
        P(("row", "col"), None),
        P("row", "col"),
        P("col", "row"),
        P(None, ("row", "col")),
    )
    return jax.shard_map(local, mesh=mesh, in_specs=in_specs, out_specs=out_specs, check_vma=False)
```

```python
import functools
import math

import jax
import jax.numpy as jnp
from jax import lax
from jax.experimental import pallas as pl
from jax.experimental.pallas import tpu as pltpu
from jax.sharding import PartitionSpec as P

NH = 48
HP = 64
NSTATE = 256
KCONV = 4
QUERY_HEADS = 8
KEY_VALUE_HEADS = 2
HEAD_SIZE = 128
RANK = 16
NADAPT = 8
SSD_BLOCK = 256
DSSM = 3072
UNIT_IN = 1030
UNIT_FF = 512


EPSILON = 1e-05
ROPE_BASE = 10000.0
NEGATIVE = -1e30
FLOAT = jnp.float32
BFLOAT = jnp.bfloat16


def product(left, right):
    return jnp.dot(left, right, preferred_element_type=FLOAT)


def contract_last(left, right):
    return lax.dot_general(left, right, (((1,), (1,)), ((), ())), preferred_element_type=FLOAT)


def contract_first(left, right):
    return lax.dot_general(left, right, (((0,), (0,)), ((), ())), preferred_element_type=FLOAT)


def rms_norm(values, gain):
    return values * lax.rsqrt(jnp.mean(values * values, axis=-1, keepdims=True) + EPSILON) * gain


def sequence_tables(lengths, adapters, sequence_length):
    sequence_count = lengths.shape[0]
    boundary = jnp.cumsum(lengths)
    token_index = jnp.arange(sequence_length, dtype=jnp.int32)
    passed = (token_index[:, None] >= boundary[None, :]).astype(jnp.int32)
    segment = jnp.sum(passed, axis=1)
    segment_start = jnp.sum(passed * lengths[None, :], axis=1)
    position = token_index - segment_start
    member = (segment[:, None] == jnp.arange(sequence_count, dtype=jnp.int32)[None, :]).astype(
        jnp.int32
    )
    chosen = jnp.sum(member * adapters[None, :], axis=1)
    column = jnp.arange(NADAPT * RANK, dtype=jnp.int32) // RANK
    selector = (chosen[:, None] == column[None, :]).astype(FLOAT)
    return (segment, position, selector)


ESTIMATE = 16
SCAN_BYTES = 32 * 1024 * 1024
DENSE_BYTES = 16 * 1024 * 1024
LANES = 128


def whole(shape):
    return pl.BlockSpec(shape, lambda *_: (0,) * len(shape))


def estimate(flops, bytes_accessed, transcendentals):
    return pl.CostEstimate(
        flops=flops // ESTIMATE,
        bytes_accessed=bytes_accessed // ESTIMATE,
        transcendentals=transcendentals // ESTIMATE,
    )


def dot(left, right, contract):
    return lax.dot_general(left, right, ((contract[:1], contract[1:]), ((), ())), preferred_element_type=FLOAT)


def parts_of(values, count):
    parts = []
    for _ in range(count):
        part = values.astype(BFLOAT)
        parts.append(part)
        values = values - part.astype(FLOAT)
    return parts


def running_sum(values, triangle, contract):
    width = values.shape[1]
    split = dot(triangle, jnp.concatenate(parts_of(values, 3), axis=1), contract)
    return split[:, :width] + split[:, width : 2 * width] + split[:, 2 * width :]


def head_spread(values, expand):
    return dot(jnp.concatenate(parts_of(values, 2), axis=1), expand, (1, 0))


def head_sum(values, expand):
    high, low = parts_of(values, 2)
    single = expand[:LANES]
    return dot(high, single, (1, 1)) + dot(low, single, (1, 1))


def silu_parts(values):
    gate = 1.0 / (1.0 + jnp.exp(-values))
    return values * gate, gate


def expand_table(channels):
    row = lax.broadcasted_iota(jnp.int32, (2 * LANES, channels), 0) % LANES
    channel = lax.broadcasted_iota(jnp.int32, (2 * LANES, channels), 1) // HP
    return (row == channel).astype(BFLOAT)


def conv_sum(current_ref, before_ref, taps_ref, meta):
    rows = SSD_BLOCK
    current = current_ref[...].astype(FLOAT)
    window = jnp.concatenate([before_ref[...].astype(FLOAT)[8:16], current], axis=0)
    summed = taps_ref[KCONV : KCONV + 1, :] + current * taps_ref[0:1, :]
    for lag in range(1, KCONV):
        shifted = window[8 - lag : 8 - lag + rows]
        summed = summed + jnp.where(meta[:, 1:2] >= lag, shifted, 0.0) * taps_ref[lag : lag + 1, :]
    return summed


def conv_back(summed_grad, later, taps_ref, meta):
    rows = SSD_BLOCK
    window = jnp.concatenate([summed_grad, later[...]], axis=0)
    grad = summed_grad * taps_ref[0:1, :]
    for lag in range(1, KCONV):
        grad = grad + jnp.where(meta[:, 2:3] >= lag, window[lag : lag + rows], 0.0) * taps_ref[lag : lag + 1, :]
    later[...] = summed_grad[:8]
    return grad


def silu_slope(values, gate):
    return gate * (1.0 + values * (1.0 - gate))


def scan_block(
    conv_ref, before_ref, state_ref, state_before_ref, step_ref, meta_ref, segment_ref, taps_ref, state_taps_ref, head_ref,
    turned_over,
):
    rows = SSD_BLOCK
    channels = conv_ref.shape[1]
    meta = meta_ref[...]
    summed = conv_sum(conv_ref, before_ref, taps_ref, meta)
    activated, conv_gate = silu_parts(summed)
    wide_inputs = activated.astype(BFLOAT).astype(FLOAT)
    state_summed = conv_sum(state_ref, state_before_ref, state_taps_ref, meta)
    state_values, state_gate = silu_parts(state_summed)
    write = state_values[:, :NSTATE].astype(BFLOAT)
    read = state_values[:, NSTATE:].astype(BFLOAT)
    raw = step_ref[...].astype(FLOAT) + head_ref[0:1, :]
    steps = jnp.maximum(raw, 0.0) + jnp.log1p(jnp.exp(-jnp.abs(raw)))
    row = lax.broadcasted_iota(jnp.int32, (rows, rows), 0)
    column = lax.broadcasted_iota(jnp.int32, (rows, rows), 1)
    triangle = (row >= column).astype(BFLOAT)
    total = running_sum(steps * head_ref[1:2, :], triangle, (1, 0))
    entered = jnp.exp(total) * meta[:, 3:4]
    leaving = jnp.exp(total[rows - 1 : rows] - total) * meta[:, 4:5]
    expand = expand_table(channels)
    spread = head_spread(jnp.concatenate([steps, entered, leaving * steps], axis=0), expand)
    ordered = row <= column if turned_over else row >= column
    blocked = jnp.where(ordered & (meta[:, 0:1] == segment_ref[0:1, :]), 0.0, NEGATIVE)
    return dict(
        summed=summed,
        conv_gate=conv_gate,
        state_summed=state_summed,
        state_gate=state_gate,
        write=write,
        read=read,
        wide_inputs=wide_inputs,
        raw=raw,
        steps=steps,
        triangle=triangle,
        total=total,
        total_rows=total.T,
        leaving=leaving,
        expand=expand,
        steps_wide=spread[:rows],
        entered_wide=spread[rows : 2 * rows],
        tail_wide=spread[2 * rows :],
        stepped=(wide_inputs * spread[:rows]).astype(BFLOAT),
        tailed=(wide_inputs * spread[2 * rows :]).astype(BFLOAT),
        blocked=blocked,
        crossing=dot(write, read, (1, 1)) if turned_over else dot(read, write, (1, 1)),
    )


def decay_of(block, head):
    difference = block["total"][:, head : head + 1] - block["total_rows"][head : head + 1, :]
    return jnp.exp(difference + block["blocked"])


def turned_decay_of(block, head):
    difference = block["total_rows"][head : head + 1, :] - block["total"][:, head : head + 1]
    return jnp.exp(difference + block["blocked"])


def scan_forward_kernel(
    gate_ref, conv_ref, before_ref, state_ref, state_before_ref, step_ref, meta_ref, segment_ref, taps_ref,
    state_taps_ref, head_ref, skip_ref, mixed_ref, out_ref, scanned_ref, states_ref, state,
):
    del mixed_ref

    @pl.when(pl.program_id(0) == 0)
    def _():
        state[...] = jnp.zeros_like(state)

    block = scan_block(
        conv_ref, before_ref, state_ref, state_before_ref, step_ref, meta_ref, segment_ref, taps_ref, state_taps_ref,
        head_ref, False,
    )
    heads = conv_ref.shape[1] // HP
    carried = state[...].astype(BFLOAT)
    states_ref[0] = carried
    across = dot(block["read"], carried, (1, 0)) * block["entered_wide"]
    within = []
    for head in range(heads):
        weights = (block["crossing"] * decay_of(block, head)).astype(BFLOAT)
        within.append(dot(weights, block["stepped"][:, head * HP : (head + 1) * HP], (1, 0)))
    scanned = across + jnp.concatenate(within, axis=1)
    scanned_ref[...] = scanned
    gated, _ = silu_parts(gate_ref[...].astype(FLOAT))
    out_ref[...] = ((scanned + skip_ref[0:1, :] * block["wide_inputs"]) * gated).astype(BFLOAT)
    state[...] = state[...] * block["entered_wide"][SSD_BLOCK - 1 : SSD_BLOCK, :] + dot(
        block["write"], block["tailed"], (0, 0)
    )


def scan_backward_kernel(
    gate_ref, conv_ref, before_ref, state_ref, state_before_ref, step_ref, meta_ref, segment_ref, taps_ref,
    state_taps_ref, head_ref, skip_ref, scanned_ref, states_ref, grad_ref, out_ref, state_grad, later, state_later,
):
    @pl.when(pl.program_id(0) == 0)
    def _():
        state_grad[...] = jnp.zeros_like(state_grad)
        later[...] = jnp.zeros_like(later)
        state_later[...] = jnp.zeros_like(state_later)

    block = scan_block(
        conv_ref, before_ref, state_ref, state_before_ref, step_ref, meta_ref, segment_ref, taps_ref, state_taps_ref,
        head_ref, True,
    )
    rows = SSD_BLOCK
    channels = conv_ref.shape[1]
    heads = channels // HP
    meta = meta_ref[...]
    read, write = block["read"], block["write"]
    inputs = block["wide_inputs"]
    scanned = scanned_ref[...]
    skip = skip_ref[0:1, :]
    gate_values = gate_ref[...].astype(FLOAT)
    gated, gate = silu_parts(gate_values)
    grad = grad_ref[...].astype(FLOAT)
    gate_grad = grad * (scanned + skip * inputs) * silu_slope(gate_values, gate)
    out_grad = grad * gated
    inputs_grad = skip * out_grad
    rounded = out_grad.astype(BFLOAT)
    wide_rounded = rounded.astype(FLOAT)
    carried = states_ref[0]
    after = state_grad[...]
    after_rounded = after.astype(BFLOAT)

    from_state = dot(write, after_rounded, (1, 0))
    entering = (wide_rounded * block["entered_wide"]).astype(BFLOAT)
    write_grad = dot(block["tailed"], after_rounded, (1, 1))
    read_grad = dot(entering, carried, (1, 1))
    last_entered = block["entered_wide"][rows - 1 : rows, :]
    through = jnp.sum(after * carried.astype(FLOAT), axis=0, keepdims=True) * last_entered
    state_grad[...] = after * last_entered + dot(read, entering, (0, 0))

    crossing_grad = jnp.zeros((rows, rows), FLOAT)
    pulled = []
    for head in range(heads):
        span = slice(head * HP, (head + 1) * HP)
        decay = turned_decay_of(block, head)
        weights = (block["crossing"] * decay).astype(BFLOAT)
        pulled.append(dot(weights, rounded[:, span], (1, 0)))
        crossing_grad = crossing_grad + dot(block["stepped"][:, span], rounded[:, span], (1, 1)) * decay
    pulled = jnp.concatenate(pulled, axis=1)
    crossing_rounded = crossing_grad.astype(BFLOAT)
    read_grad = read_grad + dot(crossing_rounded, write, (0, 0))
    write_grad = write_grad + dot(crossing_rounded, read, (1, 0))

    inputs_grad = inputs_grad + block["steps_wide"] * pulled + block["tail_wide"] * from_state
    sums = head_sum(
        jnp.concatenate(
            [
                wide_rounded * scanned - block["stepped"].astype(FLOAT) * pulled,
                inputs * pulled,
                inputs * from_state,
                jnp.broadcast_to(through, (8, channels)),
            ],
            axis=0,
        ),
        block["expand"],
    )
    leaving_grad = sums[2 * rows : 3 * rows] * block["leaving"]
    leaving_total = leaving_grad * block["steps"]
    last = sums[3 * rows : 3 * rows + 1] + jnp.sum(leaving_total, axis=0, keepdims=True)
    total_grad = sums[:rows] - leaving_total
    total_grad = total_grad + jnp.where(
        lax.broadcasted_iota(jnp.int32, total_grad.shape, 0) == rows - 1, last, 0.0
    )
    decay_grad = running_sum(total_grad, block["triangle"], (0, 0))
    steps_grad = sums[rows : 2 * rows] + leaving_grad + decay_grad * head_ref[1:2, :]
    raw_grad = steps_grad / (1.0 + jnp.exp(-block["raw"]))
    raw_grad = jnp.where(lax.broadcasted_iota(jnp.int32, raw_grad.shape, 1) < heads, raw_grad, 0.0)

    state_slope = silu_slope(block["state_summed"], block["state_gate"])
    state_pre = conv_back(
        jnp.concatenate([write_grad, read_grad], axis=1) * state_slope, state_later, state_taps_ref, meta
    )
    conv_pre = conv_back(inputs_grad * silu_slope(block["summed"], block["conv_gate"]), later, taps_ref, meta)
    out_ref[:, : 2 * NSTATE] = state_pre.astype(BFLOAT)
    start = 2 * NSTATE + 2 * HEAD_SIZE
    out_ref[:, start : start + channels] = gate_grad.astype(BFLOAT)
    out_ref[:, start + channels : start + 2 * channels] = conv_pre.astype(BFLOAT)
    out_ref[:, out_ref.shape[1] - LANES :] = raw_grad.astype(BFLOAT)


STATES = 2 * NSTATE
PAIR = 2 * HEAD_SIZE


def scan_specs(channels, order):
    half = SSD_BLOCK // 16
    before = lambda i: jnp.maximum(order(i) * half - 1, 0)
    gate_at = (STATES + PAIR) // channels
    step_at = (STATES + PAIR + 2 * channels + channels * QUERY_HEADS // DSSM * HEAD_SIZE) // LANES
    return [
        pl.BlockSpec((SSD_BLOCK, channels), lambda i: (order(i), gate_at)),
        pl.BlockSpec((SSD_BLOCK, channels), lambda i: (order(i), gate_at + 1)),
        pl.BlockSpec((16, channels), lambda i: (before(i), gate_at + 1)),
        pl.BlockSpec((SSD_BLOCK, STATES), lambda i: (order(i), 0)),
        pl.BlockSpec((16, STATES), lambda i: (before(i), 0)),
        pl.BlockSpec((SSD_BLOCK, LANES), lambda i: (order(i), step_at)),
        pl.BlockSpec((SSD_BLOCK, LANES), lambda i: (order(i), 0)),
        pl.BlockSpec((8, SSD_BLOCK), lambda i: (0, order(i))),
        whole((8, channels)),
        whole((8, STATES)),
        whole((8, LANES)),
        whole((8, channels)),
    ]


def scan_operands(projected, tables):
    return [projected] * 6 + [
        tables[name] for name in ("meta", "segment_row", "taps", "state_taps", "head", "skip")
    ]


def scan_cost(tokens, channels, factor):
    heads = channels // HP
    return estimate(
        flops=factor * 2 * tokens * SSD_BLOCK * (3 * channels + NSTATE),
        bytes_accessed=factor * tokens * channels * 12,
        transcendentals=tokens * SSD_BLOCK * heads,
    )


def scan_forward(projected, tables, mixed):
    tokens = projected.shape[0]
    channels = tables["taps"].shape[1]
    blocks = tokens // SSD_BLOCK
    return pl.pallas_call(
        scan_forward_kernel,
        grid=(blocks,),
        in_specs=scan_specs(channels, lambda i: i) + [pl.BlockSpec(memory_space=pl.ANY)],
        out_specs=[
            pl.BlockSpec((SSD_BLOCK, channels), lambda i: (i, 0)),
            pl.BlockSpec((SSD_BLOCK, channels), lambda i: (i, 0)),
            pl.BlockSpec((1, NSTATE, channels), lambda i: (i, 0, 0)),
        ],
        out_shape=[
            jax.ShapeDtypeStruct(mixed.shape, BFLOAT),
            jax.ShapeDtypeStruct((tokens, channels), FLOAT),
            jax.ShapeDtypeStruct((blocks, NSTATE, channels), BFLOAT),
        ],
        scratch_shapes=[pltpu.VMEM((NSTATE, channels), FLOAT)],
        input_output_aliases={12: 0},
        compiler_params=pltpu.CompilerParams(vmem_limit_bytes=SCAN_BYTES),
        cost_estimate=scan_cost(tokens, channels, 1),
        name="scan_forward",
    )(*scan_operands(projected, tables), mixed)


def scan_backward(projected, tables, scanned, carried, mixed_grad):
    tokens, width = projected.shape
    channels = tables["taps"].shape[1]
    blocks = tokens // SSD_BLOCK
    back = lambda i: (blocks - 1 - i, 0)
    return pl.pallas_call(
        scan_backward_kernel,
        grid=(blocks,),
        in_specs=scan_specs(channels, lambda i: blocks - 1 - i)
        + [
            pl.BlockSpec((SSD_BLOCK, channels), back),
            pl.BlockSpec((1, NSTATE, channels), lambda i: (blocks - 1 - i, 0, 0)),
            pl.BlockSpec((SSD_BLOCK, channels), back),
        ],
        out_specs=pl.BlockSpec((SSD_BLOCK, width), back),
        out_shape=jax.ShapeDtypeStruct((tokens, width), BFLOAT),
        scratch_shapes=[
            pltpu.VMEM((NSTATE, channels), FLOAT),
            pltpu.VMEM((8, channels), FLOAT),
            pltpu.VMEM((8, STATES), FLOAT),
        ],
        compiler_params=pltpu.CompilerParams(vmem_limit_bytes=SCAN_BYTES),
        cost_estimate=scan_cost(tokens, channels, 2),
        name="scan_backward",
    )(*scan_operands(projected, tables), scanned, carried, mixed_grad)


def turned(values, cosine, sine):
    return (values * cosine + pltpu.roll(values, HEAD_SIZE // 2, 1) * sine).astype(BFLOAT)


def turned_back(values, cosine, sine):
    return values * cosine + pltpu.roll(values * sine, HEAD_SIZE // 2, 1)


ATT_ROWS = 256


def attention_mask(meta_ref, segment_ref, start, extent):
    row = start + lax.broadcasted_iota(jnp.int32, (ATT_ROWS, extent), 0)
    column = lax.broadcasted_iota(jnp.int32, (ATT_ROWS, extent), 1)
    return (row >= column) & (meta_ref[start : start + ATT_ROWS, 0:1] == segment_ref[0:1, :extent])


def probabilities(query, keys, allowed):
    score = dot(query, keys, (1, 1)) * (1.0 / math.sqrt(HEAD_SIZE))
    score = jnp.where(allowed, score, NEGATIVE)
    exponent = jnp.exp(score - jnp.max(score, axis=1, keepdims=True))
    return exponent / jnp.sum(exponent, axis=1, keepdims=True)


def attention_forward_kernel(query_ref, key_ref, value_ref, cosine_ref, sine_ref, meta_ref, segment_ref, out_ref, keys):
    tokens = key_ref.shape[0]
    keys[...] = turned(key_ref[...].astype(FLOAT), cosine_ref[...], sine_ref[...])
    for start in range(0, tokens, ATT_ROWS):
        extent = start + ATT_ROWS
        here = slice(start, extent)
        allowed = attention_mask(meta_ref, segment_ref, start, extent)
        for unit in range(query_ref.shape[1] // HEAD_SIZE):
            span = slice(unit * HEAD_SIZE, (unit + 1) * HEAD_SIZE)
            query = turned(query_ref[here, span].astype(FLOAT), cosine_ref[here], sine_ref[here])
            weights = probabilities(query, keys[:extent], allowed).astype(BFLOAT)
            out_ref[here, span] = dot(weights, value_ref[:extent], (1, 0)).astype(BFLOAT)


def attention_backward_kernel(
    query_ref, key_ref, value_ref, cosine_ref, sine_ref, meta_ref, segment_ref, grad_ref, held_ref,
    out_ref, keys, key_sum, value_sum, query_grad_ref, shared_grad_ref, sems,
):
    del held_ref
    tokens = key_ref.shape[0]
    scale = 1.0 / math.sqrt(HEAD_SIZE)
    keys[...] = turned(key_ref[...].astype(FLOAT), cosine_ref[...], sine_ref[...])
    key_sum[...] = jnp.zeros_like(key_sum)
    value_sum[...] = jnp.zeros_like(value_sum)
    for start in range(0, tokens, ATT_ROWS):
        extent = start + ATT_ROWS
        here = slice(start, extent)
        allowed = attention_mask(meta_ref, segment_ref, start, extent)
        for unit in range(query_ref.shape[1] // HEAD_SIZE):
            span = slice(unit * HEAD_SIZE, (unit + 1) * HEAD_SIZE)
            query = turned(query_ref[here, span].astype(FLOAT), cosine_ref[here], sine_ref[here])
            weights = probabilities(query, keys[:extent], allowed)
            grad = grad_ref[here, span]
            weights_grad = dot(grad, value_ref[:extent], (1, 1))
            value_sum[:extent] += dot(weights.astype(BFLOAT), grad, (0, 0))
            mean_grad = jnp.sum(weights * weights_grad, axis=1, keepdims=True)
            score_grad = (weights * (weights_grad - mean_grad) * scale).astype(BFLOAT)
            query_grad = dot(score_grad, keys[:extent], (1, 0))
            key_sum[:extent] += dot(score_grad, query, (0, 0))
            query_grad_ref[here, span] = turned_back(query_grad, cosine_ref[here], sine_ref[here]).astype(BFLOAT)
    shared_grad_ref[:, :HEAD_SIZE] = turned_back(key_sum[...], cosine_ref[...], sine_ref[...]).astype(BFLOAT)
    shared_grad_ref[:, HEAD_SIZE:] = value_sum[...].astype(BFLOAT)
    end = out_ref.shape[1] - LANES
    width = query_grad_ref.shape[1]
    copies = [
        pltpu.make_async_copy(query_grad_ref, out_ref.at[:, end - width : end], sems.at[0]),
        pltpu.make_async_copy(shared_grad_ref, out_ref.at[:, STATES : STATES + PAIR], sems.at[1]),
    ]
    for copy in copies:
        copy.start()
    for copy in copies:
        copy.wait()


def attention_cost(tokens, width, factor):
    return estimate(
        flops=factor * 2 * tokens * tokens * width,
        bytes_accessed=factor * tokens * width * 8,
        transcendentals=tokens * tokens * width // (2 * HEAD_SIZE),
    )


def attention_specs(tokens, channels):
    width = channels * QUERY_HEADS // DSSM * HEAD_SIZE
    narrow = whole((tokens, HEAD_SIZE))
    return [
        pl.BlockSpec((tokens, width), lambda *_: (0, (STATES + PAIR + 2 * channels) // width)),
        pl.BlockSpec((tokens, HEAD_SIZE), lambda *_: (0, STATES // HEAD_SIZE)),
        pl.BlockSpec((tokens, HEAD_SIZE), lambda *_: (0, STATES // HEAD_SIZE + 1)),
        narrow,
        narrow,
        whole((tokens, LANES)),
        whole((8, tokens)),
    ]


def attention_operands(projected, tables):
    return [projected] * 3 + [tables[name] for name in ("cosine", "sine", "meta", "segment_row")]


def attention_forward(projected, tables):
    tokens = projected.shape[0]
    channels = tables["taps"].shape[1]
    width = channels * QUERY_HEADS // DSSM * HEAD_SIZE
    return pl.pallas_call(
        attention_forward_kernel,
        grid=(1,),
        in_specs=attention_specs(tokens, channels),
        out_specs=pl.BlockSpec((tokens, width), lambda *_: (0, channels // width)),
        out_shape=jax.ShapeDtypeStruct((tokens, channels + width), BFLOAT),
        scratch_shapes=[pltpu.VMEM((tokens, HEAD_SIZE), BFLOAT)],
        compiler_params=pltpu.CompilerParams(vmem_limit_bytes=SCAN_BYTES),
        cost_estimate=attention_cost(tokens, width, 1),
        name="attention_forward",
    )(*attention_operands(projected, tables))


def attention_backward(projected, tables, mixed_grad, projected_grad):
    tokens = projected.shape[0]
    channels = tables["taps"].shape[1]
    width = channels * QUERY_HEADS // DSSM * HEAD_SIZE
    return pl.pallas_call(
        attention_backward_kernel,
        grid=(1,),
        in_specs=attention_specs(tokens, channels)
        + [pl.BlockSpec((tokens, width), lambda *_: (0, channels // width)), pl.BlockSpec(memory_space=pl.ANY)],
        out_specs=pl.BlockSpec(memory_space=pl.ANY),
        out_shape=jax.ShapeDtypeStruct(projected_grad.shape, BFLOAT),
        scratch_shapes=[
            pltpu.VMEM((tokens, HEAD_SIZE), BFLOAT),
            pltpu.VMEM((tokens, HEAD_SIZE), FLOAT),
            pltpu.VMEM((tokens, HEAD_SIZE), FLOAT),
            pltpu.VMEM((tokens, width), BFLOAT),
            pltpu.VMEM((tokens, PAIR), BFLOAT),
            pltpu.SemaphoreType.DMA((2,)),
        ],
        input_output_aliases={8: 0},
        compiler_params=pltpu.CompilerParams(vmem_limit_bytes=SCAN_BYTES),
        cost_estimate=attention_cost(tokens, width, 3),
        name="attention_backward",
    )(*attention_operands(projected, tables), mixed_grad, projected_grad)


def mixer_tables(lengths, segment, position, conv_values, conv_states, scan_params):
    tokens = segment.shape[0]
    block = jnp.arange(tokens, dtype=jnp.int32) // SSD_BLOCK
    previous = jnp.concatenate([jnp.full((1,), -1, jnp.int32), segment[:-1]])
    first_previous = jnp.repeat(previous[::SSD_BLOCK], SSD_BLOCK)
    last_segment = jnp.repeat(segment[SSD_BLOCK - 1 :: SSD_BLOCK], SSD_BLOCK)
    length = jnp.sum(
        jnp.where(segment[:, None] == jnp.arange(lengths.shape[0], dtype=jnp.int32)[None, :], lengths[None, :], 0),
        axis=1,
    )
    columns = [
        segment,
        position,
        length - 1 - position,
        segment == first_previous,
        segment == last_segment,
    ]
    meta = jnp.stack([column.astype(FLOAT) for column in columns], axis=1)
    half_width = HEAD_SIZE // 2
    frequency = ROPE_BASE ** (-2.0 * jnp.arange(half_width, dtype=FLOAT) / HEAD_SIZE)
    angle = position.astype(FLOAT)[:, None] * frequency[None, :]
    cosine, sine = jnp.cos(angle), jnp.sin(angle)
    heads = scan_params.shape[1]
    head = jnp.stack([scan_params[0], -jnp.exp(scan_params[1]), scan_params[2]])
    return dict(
        meta=jnp.pad(meta, ((0, 0), (0, LANES - meta.shape[1]))),
        segment_row=jnp.broadcast_to(segment.astype(FLOAT)[None, :], (8, tokens)),
        taps=jnp.pad(conv_values.astype(FLOAT), ((0, 3), (0, 0))),
        state_taps=jnp.pad(conv_states.astype(FLOAT), ((0, 3), (0, 0))),
        head=jnp.pad(head, ((0, 5), (0, LANES - heads))),
        skip=jnp.broadcast_to(jnp.repeat(scan_params[2], HP)[None, :], (8, heads * HP)),
        cosine=jnp.concatenate([cosine, cosine], axis=1),
        sine=jnp.concatenate([-sine, sine], axis=1),
    )


HALVES = 2
DENSE_TILE = 1024


def matrix_rows(values):
    return values.reshape(values.shape[0] * values.shape[1], values.shape[2])


def cut_tiles(width, tile):
    return [(low, min(low + tile, width)) for low in range(0, width, tile)]


def spread_kernel(mask, count, left_ref, right_ref, chosen_ref, *rest):
    weights, (out_ref, narrow_ref, out_tile, narrow, sems) = rest[:count], rest[-5:]
    rows = left_ref.shape[0]
    shards = weights[0].shape[0]
    depth = shards // HALVES
    start = pl.multiple_of((lax.axis_index("col") ^ mask) * rows, rows)
    here = pl.ds(start, rows)

    def through(ref, low, high):
        return dot(left_ref[...], matrix_rows(ref[:depth, :rows, low:high]), (1, 0)) + dot(
            right_ref[...], matrix_rows(ref[depth:, :rows, low:high]), (1, 0)
        )

    lower = weights[-1].shape[2] - LANES
    narrow[...] = (chosen_ref[here, :] * through(weights[-1], lower, lower + LANES)).astype(BFLOAT)
    copies = [pltpu.make_async_copy(narrow, narrow_ref.at[here, :], sems.at[0])]
    copies[0].start()
    column = 0
    for ref in weights:
        for low, high in cut_tiles(ref.shape[2] - (LANES if ref is weights[-1] else 0), DENSE_TILE):
            span = slice(column, column + high - low)
            column += high - low
            raised = matrix_rows(ref[:, rows : rows + NADAPT * RANK // shards, low:high])
            out_tile[:, span] = (through(ref, low, high) + dot(narrow[...], raised, (1, 0))).astype(BFLOAT)
            copies.append(
                pltpu.make_async_copy(out_tile.at[:, span], out_ref.at[here, span], sems.at[len(copies)])
            )
            copies[-1].start()
    for copy in copies:
        copy.wait()


def weights_width(gathered):
    return sum(part.shape[2] for part in gathered) - LANES


def spread_block(mask, halves, gathered, selector, held):
    rows, half = halves[0].shape
    width = weights_width(gathered)
    total = selector.shape[0]
    fast, free = pl.BlockSpec(memory_space=pltpu.VMEM), pl.BlockSpec(memory_space=pl.ANY)
    operands = [*halves, selector, *gathered]
    in_specs = [fast] * len(operands)
    aliases = {}
    if held is not None:
        aliases = {len(operands): 0, len(operands) + 1: 1}
        operands += list(held)
        in_specs += [free] * 2
    copies = 1 + sum(-(-part.shape[2] // DENSE_TILE) for part in gathered)
    return pl.pallas_call(
        functools.partial(spread_kernel, mask, len(gathered)),
        in_specs=in_specs,
        out_specs=[free] * 2,
        out_shape=[
            jax.ShapeDtypeStruct((total, width), BFLOAT),
            jax.ShapeDtypeStruct((total, LANES), BFLOAT),
        ],
        scratch_shapes=[
            pltpu.VMEM((rows, width), BFLOAT),
            pltpu.VMEM((rows, LANES), BFLOAT),
            pltpu.SemaphoreType.DMA((copies,)),
        ],
        input_output_aliases=aliases,
        compiler_params=pltpu.CompilerParams(vmem_limit_bytes=DENSE_BYTES),
        cost_estimate=estimate(
            flops=4 * rows * half * (width + LANES), bytes_accessed=2 * rows * (2 * half + width), transcendentals=0
        ),
        name="spread_block",
    )(*operands)


def collect_kernel(masks, count, values_ref, *refs):
    weights, outs = refs[:count], refs[count:]
    rows = values_ref.shape[0] // 4
    shards = weights[0].shape[0]
    half = shards // HALVES * rows
    width = values_ref.shape[1]
    starts, column = [], 0
    for ref in weights:
        high = min(column + ref.shape[2], width)
        starts.append((column, high))
        column = high
    for at, mask in enumerate(masks):
        here = pl.ds(pl.multiple_of((lax.axis_index("col") ^ mask) * rows, rows), rows)
        first, second = outs[2 * at], outs[2 * at + 1]

        def through(cut):
            total = None
            for (low, high), ref in zip(starts, weights):
                part = dot(values_ref[here, low:high], cut(ref, high - low), (1, 1))
                total = part if total is None else total + part
            return total

        for shard in range(shards):
            out_ref = first if shard < shards // HALVES else second
            column = shard * rows % half
            out_ref[:, column : column + rows] = through(lambda ref, wide: ref[shard, :rows, :wide]).astype(
                out_ref.dtype
            )
        first[:, half:] = through(
            lambda ref, wide: matrix_rows(ref[:, rows : rows + NADAPT * RANK // shards, :wide])
        ).astype(first.dtype)


def collect_blocks(masks, values, gathered, types):
    rows = values.shape[0] // 4
    half = gathered[0].shape[0] // HALVES * rows
    fast = pl.BlockSpec(memory_space=pltpu.VMEM)
    out_shape = []
    for pair in types:
        out_shape.append(jax.ShapeDtypeStruct((rows, half + LANES), pair[0]))
        out_shape.append(jax.ShapeDtypeStruct((rows, half), pair[1]))
    outs = pl.pallas_call(
        functools.partial(collect_kernel, masks, len(gathered)),
        in_specs=[fast] * (1 + len(gathered)),
        out_specs=[fast] * len(out_shape),
        out_shape=out_shape,
        compiler_params=pltpu.CompilerParams(vmem_limit_bytes=DENSE_BYTES),
        cost_estimate=estimate(
            flops=4 * len(masks) * rows * half * values.shape[1],
            bytes_accessed=2 * len(masks) * rows * (values.shape[1] + 4 * half),
            transcendentals=0,
        ),
        name="collect_blocks",
    )(values, *gathered)
    return [tuple(outs[2 * at : 2 * at + 2]) for at in range(len(masks))]


def root_mean(values):
    return lax.rsqrt(jnp.mean(values * values, axis=1, keepdims=True) + EPSILON)


def finish_kernel(kind, first_own, first_near, first_far, second_own, second_near, second_far, lower_ref, chosen_ref,
                  *refs):
    half = second_own.shape[1]
    wide = lambda ref: ref[...].astype(FLOAT)
    first = wide(first_own) + wide(first_near) + wide(first_far)
    second = wide(second_own) + wide(second_near) + wide(second_far)
    inner = (chosen_ref[...] * first[:, half:]).astype(BFLOAT)
    summed = jnp.concatenate([first[:, :half], second], axis=1) + dot(
        inner, matrix_rows(lower_ref[...]), (1, 1)
    )
    if kind == "output":
        residual_ref, out_ref, inner_ref = refs
        inner_ref[...] = inner
        out_ref[...] = (residual_ref[...] + summed).astype(BFLOAT)
        return
    if kind == "forward":
        residual_ref, gain_ref, out_ref, inner_ref, left_ref, right_ref = refs
        hidden = residual_ref[...] + summed
        normed = (hidden * root_mean(hidden) * gain_ref[0:1, :]).astype(BFLOAT)
        out_ref[...] = hidden
    else:
        values_ref, upstream_ref, gain_ref = refs[:3]
        values = values_ref[...]
        scale = root_mean(values)
        weighted = summed * gain_ref[0:1, :]
        mean = jnp.mean(weighted * values, axis=1, keepdims=True)
        hidden = upstream_ref[...].astype(FLOAT) + scale * weighted - values * (scale * scale * scale * mean)
        normed = hidden.astype(BFLOAT)
        if kind == "input":
            out_ref, inner_ref = refs[3:]
            inner_ref[...] = inner
            out_ref[...] = normed
            return
        out_ref, inner_ref, left_ref, right_ref = refs[3:]
        out_ref[...] = hidden
    inner_ref[...] = inner
    left_ref[...] = normed[:, :half]
    right_ref[...] = normed[:, half:]


def finish(kind, parts, gathered, own_selector, *operands):
    rows = own_selector.shape[0]
    half = parts[3].shape[1]
    shards = gathered[-1].shape[0]
    model = HALVES * half
    lower = gathered[-1][:, : model // shards, -LANES:]
    result = BFLOAT if kind in ("output", "input") else FLOAT
    out_shape = [jax.ShapeDtypeStruct((rows, model), result), jax.ShapeDtypeStruct((rows, LANES), BFLOAT)]
    if kind in ("forward", "backward"):
        out_shape += [jax.ShapeDtypeStruct((rows, half), BFLOAT)] * 2
    given = [*parts, lower, own_selector, *operands]
    in_specs = [whole(value.shape) for value in given]
    return pl.pallas_call(
        functools.partial(finish_kernel, kind),
        grid=(1,),
        in_specs=in_specs,
        out_specs=[whole(shape.shape) for shape in out_shape],
        out_shape=out_shape,
        compiler_params=pltpu.CompilerParams(vmem_limit_bytes=DENSE_BYTES),
        cost_estimate=estimate(
            flops=2 * rows * model * LANES, bytes_accessed=rows * model * 20, transcendentals=0
        ),
        name="finish_" + kind,
    )(*given)


def send_kernel(target_column, target_row, tokens_ref, adapter_ref, sent_ref, matrix_ref):
    rows = tokens_ref.shape[0]
    model = tokens_ref.shape[1]
    peer = adapter_ref.shape[0]
    column, row = target_column[:, 0:1], target_row[0:1, :]
    earlier = lax.broadcasted_iota(jnp.int32, (rows, rows), 0) < lax.broadcasted_iota(jnp.int32, (rows, rows), 1)
    same = jnp.where((column // rows == row // rows) & earlier, 1.0, 0.0)
    place = (row // rows) * peer + jnp.sum(same, axis=0, keepdims=True).astype(jnp.int32)
    matrix = (lax.broadcasted_iota(jnp.int32, (rows, rows), 0) == place).astype(BFLOAT)
    matrix_ref[...] = matrix
    sent_ref[:, :model] = dot(matrix, tokens_ref[...], (1, 0)).astype(BFLOAT)
    lane = lax.broadcasted_iota(jnp.int32, (rows, LANES), 1)
    slots = jnp.where(lane == 0, column % rows, 0).astype(FLOAT).astype(BFLOAT)
    notes = dot(matrix, slots, (1, 0))
    sent_ref[:, model:] = jnp.where(lane == 0, notes, adapter_ref[0:1, :]).astype(BFLOAT)


def send_tokens(target, tokens, adapters, peer):
    rows, model = tokens.shape
    notes = jnp.pad(adapters.astype(FLOAT), (1, LANES - 1 - adapters.shape[0]))
    return pl.pallas_call(
        send_kernel,
        in_specs=[pl.BlockSpec(memory_space=pltpu.VMEM)] * 4,
        out_specs=[pl.BlockSpec(memory_space=pltpu.VMEM)] * 2,
        out_shape=[
            jax.ShapeDtypeStruct((rows, model + LANES), BFLOAT),
            jax.ShapeDtypeStruct((rows, rows), BFLOAT),
        ],
        compiler_params=pltpu.CompilerParams(vmem_limit_bytes=DENSE_BYTES),
        name="send_tokens",
    )(
        jnp.broadcast_to(target[:, None], (rows, LANES)),
        jnp.broadcast_to(target[None, :], (8, rows)),
        tokens,
        jnp.broadcast_to(notes[None, :], (peer, LANES)),
    )


def arrive_kernel(arrived_ref, gain_ref, own_ref, matrix_ref, left_ref, right_ref):
    rows, model = own_ref.shape
    slots = arrived_ref[:, model:].astype(FLOAT).T[0:1, :]
    row = lax.broadcasted_iota(jnp.int32, (rows, rows), 0).astype(FLOAT)
    matrix = (row == slots).astype(BFLOAT)
    matrix_ref[...] = matrix
    own = dot(matrix, arrived_ref[:, :model], (1, 0))
    own_ref[...] = own
    normed = (own * root_mean(own) * gain_ref[0:1, :]).astype(BFLOAT)
    left_ref[...] = normed[:, : model // HALVES]
    right_ref[...] = normed[:, model // HALVES :]


def arrive_tokens(arrived, gain):
    rows, model = arrived.shape[0], arrived.shape[1] - LANES
    return pl.pallas_call(
        arrive_kernel,
        in_specs=[pl.BlockSpec(memory_space=pltpu.VMEM)] * 2,
        out_specs=[pl.BlockSpec(memory_space=pltpu.VMEM)] * 4,
        out_shape=[
            jax.ShapeDtypeStruct((rows, model), FLOAT),
            jax.ShapeDtypeStruct((rows, rows), BFLOAT),
            jax.ShapeDtypeStruct((rows, model // HALVES), BFLOAT),
            jax.ShapeDtypeStruct((rows, model // HALVES), BFLOAT),
        ],
        compiler_params=pltpu.CompilerParams(vmem_limit_bytes=DENSE_BYTES),
        name="arrive_tokens",
    )(arrived, gain)


GATE_WIDTH = DSSM // QUERY_HEADS
PAIR_WIDTH = 2 * KEY_VALUE_HEADS * HEAD_SIZE // QUERY_HEADS
STATE_WIDTH = 2 * NSTATE // QUERY_HEADS
STEP_WIDTH = NH // QUERY_HEADS
ALL_AXES = ("row", "col")


def pad_columns(values, width):
    return jnp.pad(values, ((0, 0), (0, width - values.shape[1])))


def after(values, *earlier):
    return lax.optimization_barrier((values, *earlier))[0]


def after_all(values, *earlier):
    return lax.optimization_barrier((*values, *earlier))[: len(values)]


def unit_parts(values, units):
    cuts = [0]
    for width in (GATE_WIDTH, GATE_WIDTH, HEAD_SIZE, PAIR_WIDTH, STATE_WIDTH, STEP_WIDTH):
        cuts.append(cuts[-1] + width)
    return [
        jnp.concatenate(
            [values[:, unit * UNIT_IN + low : unit * UNIT_IN + high] for unit in range(units)], axis=1
        )
        for low, high in zip(cuts[:-1], cuts[1:])
    ]


def restore_units(parts, units):
    ordered = []
    for unit in range(units):
        for part in parts:
            width = part.shape[1] // units
            ordered.append(part[:, unit * width : (unit + 1) * width])
    return jnp.concatenate(ordered, axis=1)


def split_halves(values, units, first, axis):
    block = values.shape[axis] // units
    take = lambda low, high: lax.slice_in_dim(values, low, high, axis=axis)
    parts = [take(unit * block, unit * block + first) for unit in range(units)]
    parts += [take(unit * block + first, (unit + 1) * block) for unit in range(units)]
    return jnp.concatenate(parts, axis=axis)


def join_halves(values, units, first, axis):
    block = values.shape[axis] // units
    rest = block - first
    take = lambda low, high: lax.slice_in_dim(values, low, high, axis=axis)
    parts = []
    for unit in range(units):
        parts.append(take(unit * first, (unit + 1) * first))
        parts.append(take(units * first + unit * rest, units * first + (unit + 1) * rest))
    return jnp.concatenate(parts, axis=axis)


def quick(rows):
    return lax.axis_size("col") == 4 and lax.axis_size("row") == 8 and rows == 256


def flip(values, mask):
    return lax.ppermute(values, "col", [(i, i ^ mask) for i in range(4)])


def gather_blocks(halves):
    left, right = halves
    far_left, near_right = flip(left, 2), flip(right, 1)
    near_left, far_right = flip(left, 1), flip(right, 2)
    corner_left, corner_right = flip(far_left, 1), flip(near_right, 2)
    return [
        (0, (left, right)),
        (1, (near_left, near_right)),
        (2, (far_left, far_right)),
        (3, (corner_left, corner_right)),
    ]


def rows_of(values, block, rows):
    return lax.dynamic_slice_in_dim(values, block * rows, rows, 0)


def spread_gathered(blocks, gathered, selector):
    held = None
    for mask, values in blocks:
        held = spread_block(mask, values, gathered, selector, held)
    return held


def spread_project(halves, gathered, selector):
    rows = halves[0].shape[0]
    if quick(rows):
        return spread_gathered(gather_blocks(halves), gathered, selector)
    wide, narrow_factor = gathered
    width = narrow_factor.shape[1]
    both = product(lax.all_gather(jnp.concatenate(halves, axis=1), "col", axis=0, tiled=True), wide)
    narrow = (selector * both[:, width:]).astype(BFLOAT)
    return (both[:, :width] + product(narrow, narrow_factor)).astype(BFLOAT), narrow


def collect_start(values, gathered):
    (corner,) = collect_blocks([3], values, gathered, [(BFLOAT, BFLOAT)])
    arriving = flip(corner[0], 1), flip(corner[1], 2)
    values = after(values, corner[0])
    near, far, own = collect_blocks([1, 2, 0], values, gathered, [(BFLOAT, FLOAT), (FLOAT, BFLOAT), (FLOAT, FLOAT)])
    return own, flip(near[0], 1), flip(far[1], 2), far[0], near[1], arriving


def collect_middle(started):
    own, near_first, far_second, far_first, near_second, arriving = started
    onward = [
        (kept + part.astype(FLOAT)).astype(BFLOAT) for kept, part in zip((far_first, near_second), arriving)
    ]
    return (own, near_first, far_second), onward


def collect_onward(onward):
    return flip(onward[0], 2), flip(onward[1], 1)


def collect_end(kept, last, kind, gathered, own_selector, *operands):
    own, near_first, far_second = kept
    parts = [own[0], near_first, last[0], own[1], far_second, last[1]]
    return finish(kind, parts, gathered, own_selector, *operands)


def collect_project(values, gathered, kind, own_selector, *operands):
    rows, model = own_selector.shape[0], operands[0].shape[1]
    if quick(rows):
        kept, onward = collect_middle(collect_start(values, gathered))
        return collect_end(kept, collect_onward(onward), kind, gathered, own_selector, *operands)
    wide, narrow_factor = gathered
    width = narrow_factor.shape[1]
    partial = jnp.concatenate(
        [contract_last(values, wide[:, :width]), contract_last(values, narrow_factor)], axis=1
    ).astype(BFLOAT)
    summed = lax.psum_scatter(partial, "col", scatter_dimension=0, tiled=True).astype(FLOAT)
    inner = (own_selector * summed[:, model:]).astype(BFLOAT)
    summed = summed[:, :model] + contract_last(inner, wide[:, width:])
    if kind == "output":
        return (operands[0] + summed).astype(BFLOAT), inner
    if kind == "forward":
        residual, gain = operands
        hidden = residual + summed
        return hidden, inner, *cut_halves(rms_norm(hidden, gain[0]).astype(BFLOAT))
    values, upstream, gain = operands
    _, back = jax.vjp(lambda given: rms_norm(given, gain[0]), values)
    hidden = upstream.astype(FLOAT) + back(summed)[0]
    if kind == "input":
        return hidden.astype(BFLOAT), inner
    return hidden, inner, *cut_halves(hidden.astype(BFLOAT))


def cut_halves(values):
    half = values.shape[1] // HALVES
    return values[:, :half], values[:, half:]


def local(
    tokens_in,
    cotangent,
    target,
    sequence_lengths,
    sequence_adapter,
    norm_gains,
    weight_in,
    conv_values,
    conv_states,
    scan_params,
    weight_mix,
    weight_feed,
    weight_down,
    in_lower,
    in_raise,
    mix_lower,
    mix_raise,
    feed_lower,
    feed_raise,
    down_lower,
    down_raise,
):
    cols = lax.axis_size("col")
    rows_axis = lax.axis_size("row")
    col = lax.axis_index("col")
    devices = cols * rows_axis
    rows = tokens_in.shape[0]
    model = tokens_in.shape[1]
    total = rows * cols
    units = QUERY_HEADS // cols
    channels = units * GATE_WIDTH
    peer = rows // devices
    lengths, adapters = sequence_lengths[0], sequence_adapter[0]
    sequences = lengths.shape[0]
    fast = quick(rows)
    key_head = col * units // (QUERY_HEADS // KEY_VALUE_HEADS)
    exchange = lambda values: lax.all_to_all(values, ALL_AXES, split_axis=0, concat_axis=0, tiled=True)

    sent, send_matrix = send_tokens(target, tokens_in, adapters, peer)
    shards = []

    def gather_weight(weight, lower, raised):
        top = jnp.concatenate([weight, lower], axis=1)
        if fast:
            bottom = pad_columns(raised, top.shape[1])
            shards.append(jnp.concatenate([top, bottom], axis=0))
            return (lax.all_gather(shards[-1], "row", axis=0),)
        wide = lax.all_gather(top, "row", axis=0, tiled=True)
        return wide, lax.all_gather(raised, "row", axis=0, tiled=True)

    depth = weight_in.shape[0]
    height = depth + in_raise.shape[0]
    given = after(jnp.concatenate([weight_in, in_raise], axis=0), send_matrix)
    gates, convs, queries, pairs, states, steps = unit_parts(given, units)
    pair_width, state_width = pairs.shape[1], states.shape[1]
    taps = jnp.concatenate([jnp.zeros((KCONV + 1, pair_width), BFLOAT), conv_states], axis=1)
    taps = jnp.pad(taps, ((0, 16 - KCONV - 1), (0, 0)))
    shared = jnp.concatenate([jnp.concatenate([pairs, states], axis=1), taps], axis=0)
    own_columns = jnp.concatenate([gates, convs, queries, pad_columns(steps, LANES)], axis=1)
    if fast:
        shared_shard = shared
        shared = lax.all_gather(shared_shard, "row", axis=0)
        weights_own = gather_weight(own_columns[:depth], in_lower, own_columns[depth:])
    arrived = exchange(sent)
    gains = jnp.broadcast_to(norm_gains.astype(FLOAT)[:, None, :], (2, 8, model))
    if fast:
        near, far = flip(shared, 1), flip(shared, 2)
        arrived = after(arrived, near, far, shards[0])
    own_input, place_matrix, *normed_one = arrive_tokens(arrived.reshape(rows, model + LANES), gains[0])
    blocks_one = gather_blocks(normed_one) if fast else normed_one
    if fast:
        held = jnp.zeros((cols,) + shared.shape, BFLOAT)
        for block, values in ((col, shared), (col ^ 1, near), (col ^ 2, far)):
            held = lax.dynamic_update_index_in_dim(held, values, block, 0)
        split = shared.shape[0] // 2
        corner = jnp.concatenate([flip(near[:split], 2), flip(far[split:], 1)], axis=0)
        held = lax.dynamic_update_index_in_dim(held, corner, col ^ 3, 0)
    else:
        held = lax.all_gather(shared, "col", axis=0)
    all_pairs = jnp.concatenate([held[at, ..., :height, :pair_width] for at in range(cols)], axis=-1)
    pick = lambda start: lax.select_n(
        key_head,
        *[all_pairs[..., start + at * HEAD_SIZE : start + (at + 1) * HEAD_SIZE] for at in range(KEY_VALUE_HEADS)],
    )
    shared_columns = jnp.concatenate(
        [held[at, ..., :height, pair_width:] for at in range(cols)]
        + [pick(0), pick(KEY_VALUE_HEADS * HEAD_SIZE)],
        axis=-1,
    )
    tap_rows = held[:, 0] if fast else held
    all_taps = jnp.concatenate(
        [tap_rows[at, height : height + KCONV + 1, pair_width:] for at in range(cols)], axis=1
    )
    if fast:
        weights_in = (shared_columns, *weights_own)
    else:
        columns = jnp.concatenate([shared_columns, own_columns], axis=1)
        weights_in = gather_weight(columns[:depth], in_lower, columns[depth:])
    weights_mix = gather_weight(
        after(split_halves(weight_mix, units, GATE_WIDTH, 0).T, sent),
        mix_raise.T,
        split_halves(mix_lower, units, GATE_WIDTH, 0).T,
    )
    weights_feed = gather_weight(
        after(split_halves(weight_feed, units, UNIT_FF, 1), arrived),
        feed_lower,
        split_halves(feed_raise, units, UNIT_FF, 1),
    )

    source_adapters = arrived.reshape(rows, model + LANES)[::peer, model + 1 : model + 1 + sequences].astype(jnp.int32)
    segment, position, selector = sequence_tables(lengths, adapters, total)
    own_selector = rows_of(selector, col, rows)
    own_segment = rows_of(segment, col, rows)
    tables = mixer_tables(lengths, segment, position, conv_values, all_taps, scan_params)

    def compact_grad(narrow, values):
        parts = [
            lax.dynamic_slice_in_dim(narrow, adapters[at] * RANK, RANK, 1)
            * (own_segment == at).astype(BFLOAT)[:, None]
            for at in range(sequences)
        ]
        grad = contract_first(jnp.concatenate(parts, axis=1), values).astype(BFLOAT)
        kept = sequences * RANK
        grad = grad.reshape(kept, devices, model // devices).transpose(1, 0, 2)
        return grad.reshape(devices, peer, kept * model // devices // peer)

    def expand_grad(dealt):
        kept = sequences * RANK
        dealt = dealt.reshape(devices * kept, model // devices)
        adapter_row = (source_adapters[:, :, None] * RANK + jnp.arange(RANK, dtype=jnp.int32)).reshape(-1)
        chosen = (jnp.arange(NADAPT * RANK, dtype=jnp.int32)[:, None] == adapter_row[None, :]).astype(BFLOAT)
        return product(chosen, dealt)

    def send_back(values, grads, earlier=()):
        back = contract_first(place_matrix, values).astype(BFLOAT).reshape(devices, peer, model)
        payload = jnp.concatenate([back, *grads], axis=2)
        payload = after(payload, *earlier) if earlier else payload
        payloads.append(payload)
        return exchange(payload)

    payloads = []

    def take_back(dealt, count):
        returned = contract_first(send_matrix, dealt[:, :, :model].reshape(rows, model)).astype(BFLOAT)
        width = (dealt.shape[2] - model) // max(count, 1)
        return returned, [
            expand_grad(dealt[:, :, model + at * width : model + (at + 1) * width]) for at in range(count)
        ]

    projected, inner_in = (spread_gathered if fast else spread_project)(blocks_one, weights_in, selector)

    sent_grad = product(send_matrix, cotangent).astype(BFLOAT).reshape(devices, peer, model)
    arrived_grad = exchange(after(sent_grad, normed_one[0])).reshape(rows, model)
    branch_two = product(place_matrix, arrived_grad).astype(BFLOAT)
    weights_down = gather_weight(after(weight_down.T, projected), down_raise.T, down_lower.T)

    mixed_out = attention_forward(projected, tables)
    mixed_out, scanned, carried = scan_forward(projected, tables, mixed_out)
    hidden, inner_out, *normed_two = collect_project(mixed_out, weights_mix, "forward", own_selector, own_input, gains[1])
    gate_up, inner_feed = spread_project(normed_two, weights_feed, selector)
    act_grad, narrow_two = spread_project(cut_halves(after(branch_two, projected)), weights_down, selector)
    half_feed = units * UNIT_FF
    gate_part, up_part = gate_up[:, :half_feed].astype(FLOAT), gate_up[:, half_feed:].astype(FLOAT)
    gate = jax.nn.sigmoid(gate_part)
    silu = gate_part * gate
    activated = (silu * up_part).astype(BFLOAT)
    wide_grad = act_grad.astype(FLOAT)
    feed_grad = jnp.concatenate(
        [wide_grad * up_part * (gate * (1.0 + gate_part * (1.0 - gate))), wide_grad * silu], axis=1
    ).astype(BFLOAT)
    hidden_grad, narrow_three, *branch_one = collect_project(
        feed_grad, weights_feed, "backward", own_selector, hidden, branch_two, gains[1]
    )
    mixed_grad, narrow_one = spread_project(branch_one, weights_mix, selector)

    if fast:
        started = collect_start(after(activated, mixed_grad), weights_down)
        projected_grad = scan_backward(
            projected, tables, scanned, carried, after(mixed_grad, started[0][0], started[3])
        )
        kept, onward = collect_middle((*started[:5], [after(part, projected_grad) for part in started[5]]))
        projected_grad = attention_backward(
            projected, tables, mixed_grad, after(projected_grad, *onward, *kept[1:])
        )
        last = collect_onward(onward)
        started_in = collect_start(projected_grad, weights_in)
        kept_in, onward_in = collect_middle(started_in)
        block_out, inner_down = collect_end(
            kept, last, "output", weights_down, own_selector, after(hidden, started_in[0][0])
        )
    else:
        block_out, inner_down = collect_project(activated, weights_down, "output", own_selector, hidden)
        projected_grad = scan_backward(projected, tables, scanned, carried, mixed_grad)
        projected_grad = attention_backward(projected, tables, mixed_grad, projected_grad)
    dealt_out = send_back(
        block_out,
        [
            compact_grad(inner_down, branch_two),
            compact_grad(narrow_three, jnp.concatenate(normed_two, axis=1)),
            compact_grad(inner_out, jnp.concatenate(branch_one, axis=1)),
        ],
        [*onward_in, *kept_in[1:]] if fast else (),
    )

    def sum_rows(values):
        return lax.psum_scatter(values.astype(BFLOAT), "row", scatter_dimension=0, tiled=True).astype(FLOAT)

    early_parts = [
        contract_first(narrow_one, mixed_out),
        contract_first(inner_feed, feed_grad),
        contract_first(narrow_two, activated),
    ]
    early = sum_rows(jnp.concatenate(early_parts, axis=1))

    raise_grad = contract_first(inner_in, after(projected_grad, *onward_in) if fast else projected_grad)
    key_columns = raise_grad[:, STATES : STATES + HEAD_SIZE]
    value_columns = raise_grad[:, STATES + HEAD_SIZE : STATES + PAIR]
    mine = [(key_head == at).astype(FLOAT) for at in range(KEY_VALUE_HEADS)]
    pair_grad = jnp.concatenate([part * here for part in (key_columns, value_columns) for here in mine], axis=1)
    stacked = jnp.stack(
        [
            jnp.concatenate(
                [
                    pair_grad[:, at * pair_width : (at + 1) * pair_width],
                    raise_grad[:, at * state_width : (at + 1) * state_width],
                ],
                axis=1,
            )
            for at in range(cols)
        ]
    )
    if fast:
        to_send = stacked.astype(BFLOAT)
        piece = lambda block: lax.dynamic_index_in_dim(to_send, block, 0, False)
        near_sum = lambda block: lax.dynamic_index_in_dim(stacked, block, 0, False)
        pair_sums = flip(jnp.stack([piece(col ^ 1), piece(col ^ 3)]), 1).astype(FLOAT)
        far_sum = (near_sum(col ^ 2) + pair_sums[1]).astype(BFLOAT)
        shared_sum = near_sum(col) + pair_sums[0] + flip(far_sum, 2).astype(FLOAT)
    else:
        shared_sum = lax.psum_scatter(
            stacked.astype(BFLOAT).reshape(cols * NADAPT * RANK, -1), "col", scatter_dimension=0, tiled=True
        ).astype(FLOAT)
    late = sum_rows(jnp.concatenate([shared_sum, raise_grad[:, STATES + PAIR :]], axis=1))
    if fast:
        input_grad, narrow_four = collect_end(
            kept_in,
            collect_onward(onward_in),
            "input",
            weights_in,
            own_selector,
            own_input,
            after(hidden_grad, payloads[0]),
            gains[0],
        )
    else:
        input_grad, narrow_four = collect_project(
            projected_grad, weights_in, "input", own_selector, own_input, hidden_grad, gains[0]
        )
    dealt_grad = send_back(
        input_grad, [compact_grad(narrow_four, jnp.concatenate(normed_one, axis=1))], [dealt_out]
    )
    dealt_out, early, late = after_all((dealt_out, early, late), payloads[-1])
    early_cuts = [0, early_parts[0].shape[1]]
    early_cuts.append(early_cuts[1] + early_parts[1].shape[1])
    grad_mix_lower = join_halves(early[:, : early_cuts[1]], units, GATE_WIDTH, 1).T
    grad_feed_raise = join_halves(early[:, early_cuts[1] : early_cuts[2]], units, UNIT_FF, 1)
    grad_down_lower = early[:, early_cuts[2] :].T

    shared_width = pair_width + state_width
    cuts = [shared_width]
    for width in (channels, channels, units * HEAD_SIZE, units * STEP_WIDTH):
        cuts.append(cuts[-1] + width)
    gate_columns, conv_columns, query_columns, step_columns = [
        late[:, low:high] for low, high in zip(cuts[:-1], cuts[1:])
    ]
    grad_in_raise = restore_units(
        [
            gate_columns,
            conv_columns,
            query_columns,
            late[:, :pair_width],
            late[:, pair_width:shared_width],
            step_columns,
        ],
        units,
    )

    returned_out, (grad_down_raise, grad_feed_lower, grad_mix_raise) = take_back(dealt_out, 3)
    returned_grad, (grad_in_lower,) = take_back(dealt_grad, 1)
    return (
        returned_out,
        returned_grad,
        grad_in_lower.T,
        grad_in_raise,
        grad_mix_lower,
        grad_mix_raise,
        grad_feed_lower.T,
        grad_feed_raise,
        grad_down_lower,
        grad_down_raise,
    )


def solution(mesh):
    in_specs = (
        P(("row", "col"), None),
        P(("row", "col"), None),
        P(("row", "col")),
        P("row", None),
        P("row", None),
        P(),
        P("row", "col"),
        P(None, "col"),
        P(None, "col"),
        P(None, "col"),
        P("col", "row"),
        P("row", "col"),
        P("col", "row"),
        P("row", None),
        P("row", "col"),
        P("col", "row"),
        P(None, "row"),
        P("row", None),
        P("row", "col"),
        P("col", "row"),
        P(None, "row"),
    )
    out_specs = (
        P(("row", "col"), None),
        P(("row", "col"), None),
        P(("row", "col"), None),
        P("row", "col"),
        P("col", "row"),
        P(None, ("row", "col")),
        P(("row", "col"), None),
        P("row", "col"),
        P("col", "row"),
        P(None, ("row", "col")),
    )
    return jax.shard_map(local, mesh=mesh, in_specs=in_specs, out_specs=out_specs, check_vma=False)
```

```python
import functools
import math

import jax
import jax.numpy as jnp
from jax import lax
from jax.experimental import pallas as pl
from jax.experimental.pallas import tpu as pltpu
from jax.sharding import PartitionSpec as P

NH = 48
HP = 64
NSTATE = 256
KCONV = 4
QUERY_HEADS = 8
KEY_VALUE_HEADS = 2
HEAD_SIZE = 128
RANK = 16
NADAPT = 8
SSD_BLOCK = 256
DSSM = 3072
UNIT_IN = 1030
UNIT_FF = 512


EPSILON = 1e-05
ROPE_BASE = 10000.0
NEGATIVE = -1e30
FLOAT = jnp.float32
BFLOAT = jnp.bfloat16


def product(left, right):
    return jnp.dot(left, right, preferred_element_type=FLOAT)


def contract_last(left, right):
    return lax.dot_general(left, right, (((1,), (1,)), ((), ())), preferred_element_type=FLOAT)


def contract_first(left, right):
    return lax.dot_general(left, right, (((0,), (0,)), ((), ())), preferred_element_type=FLOAT)


def rms_norm(values, gain):
    return values * lax.rsqrt(jnp.mean(values * values, axis=-1, keepdims=True) + EPSILON) * gain


def sequence_tables(lengths, adapters, sequence_length):
    sequence_count = lengths.shape[0]
    boundary = jnp.cumsum(lengths)
    token_index = jnp.arange(sequence_length, dtype=jnp.int32)
    passed = (token_index[:, None] >= boundary[None, :]).astype(jnp.int32)
    segment = jnp.sum(passed, axis=1)
    segment_start = jnp.sum(passed * lengths[None, :], axis=1)
    position = token_index - segment_start
    member = (segment[:, None] == jnp.arange(sequence_count, dtype=jnp.int32)[None, :]).astype(
        jnp.int32
    )
    chosen = jnp.sum(member * adapters[None, :], axis=1)
    column = jnp.arange(NADAPT * RANK, dtype=jnp.int32) // RANK
    selector = (chosen[:, None] == column[None, :]).astype(FLOAT)
    return (segment, position, selector)


ESTIMATE = 16
SCAN_BYTES = 32 * 1024 * 1024
DENSE_BYTES = 16 * 1024 * 1024
LANES = 128


def whole(shape):
    return pl.BlockSpec(shape, lambda *_: (0,) * len(shape))


def estimate(flops, bytes_accessed, transcendentals):
    return pl.CostEstimate(
        flops=flops // ESTIMATE,
        bytes_accessed=bytes_accessed // ESTIMATE,
        transcendentals=transcendentals // ESTIMATE,
    )


def dot(left, right, contract):
    return lax.dot_general(left, right, ((contract[:1], contract[1:]), ((), ())), preferred_element_type=FLOAT)


def parts_of(values, count):
    parts = []
    for _ in range(count):
        part = values.astype(BFLOAT)
        parts.append(part)
        values = values - part.astype(FLOAT)
    return parts


def running_sum(values, triangle, contract):
    width = values.shape[1]
    split = dot(triangle, jnp.concatenate(parts_of(values, 3), axis=1), contract)
    return split[:, :width] + split[:, width : 2 * width] + split[:, 2 * width :]


def head_spread(values, expand):
    return dot(jnp.concatenate(parts_of(values, 2), axis=1), expand, (1, 0))


def head_sum(values, expand):
    high, low = parts_of(values, 2)
    single = expand[:LANES]
    return dot(high, single, (1, 1)) + dot(low, single, (1, 1))


def silu_parts(values):
    gate = 1.0 / (1.0 + jnp.exp(-values))
    return values * gate, gate


def expand_table(channels):
    row = lax.broadcasted_iota(jnp.int32, (2 * LANES, channels), 0) % LANES
    channel = lax.broadcasted_iota(jnp.int32, (2 * LANES, channels), 1) // HP
    return (row == channel).astype(BFLOAT)


def conv_sum(current_ref, before_ref, taps_ref, meta):
    rows = SSD_BLOCK
    current = current_ref[...].astype(FLOAT)
    window = jnp.concatenate([before_ref[...].astype(FLOAT)[8:16], current], axis=0)
    summed = taps_ref[KCONV : KCONV + 1, :] + current * taps_ref[0:1, :]
    for lag in range(1, KCONV):
        shifted = window[8 - lag : 8 - lag + rows]
        summed = summed + jnp.where(meta[:, 1:2] >= lag, shifted, 0.0) * taps_ref[lag : lag + 1, :]
    return summed


def conv_back(summed_grad, later, taps_ref, meta):
    rows = SSD_BLOCK
    window = jnp.concatenate([summed_grad, later[...]], axis=0)
    grad = summed_grad * taps_ref[0:1, :]
    for lag in range(1, KCONV):
        grad = grad + jnp.where(meta[:, 2:3] >= lag, window[lag : lag + rows], 0.0) * taps_ref[lag : lag + 1, :]
    later[...] = summed_grad[:8]
    return grad


def silu_slope(values, gate):
    return gate * (1.0 + values * (1.0 - gate))


def scan_block(
    conv_ref, before_ref, state_ref, state_before_ref, step_ref, meta_ref, segment_ref, taps_ref, state_taps_ref, head_ref,
    turned_over,
):
    rows = SSD_BLOCK
    channels = conv_ref.shape[1]
    meta = meta_ref[...]
    summed = conv_sum(conv_ref, before_ref, taps_ref, meta)
    activated, conv_gate = silu_parts(summed)
    wide_inputs = activated.astype(BFLOAT).astype(FLOAT)
    state_summed = conv_sum(state_ref, state_before_ref, state_taps_ref, meta)
    state_values, state_gate = silu_parts(state_summed)
    write = state_values[:, :NSTATE].astype(BFLOAT)
    read = state_values[:, NSTATE:].astype(BFLOAT)
    raw = step_ref[...].astype(FLOAT) + head_ref[0:1, :]
    steps = jnp.maximum(raw, 0.0) + jnp.log1p(jnp.exp(-jnp.abs(raw)))
    row = lax.broadcasted_iota(jnp.int32, (rows, rows), 0)
    column = lax.broadcasted_iota(jnp.int32, (rows, rows), 1)
    triangle = (row >= column).astype(BFLOAT)
    total = running_sum(steps * head_ref[1:2, :], triangle, (1, 0))
    entered = jnp.exp(total) * meta[:, 3:4]
    leaving = jnp.exp(total[rows - 1 : rows] - total) * meta[:, 4:5]
    expand = expand_table(channels)
    spread = head_spread(jnp.concatenate([steps, entered, leaving * steps], axis=0), expand)
    ordered = row <= column if turned_over else row >= column
    blocked = jnp.where(ordered & (meta[:, 0:1] == segment_ref[0:1, :]), 0.0, NEGATIVE)
    return dict(
        summed=summed,
        conv_gate=conv_gate,
        state_summed=state_summed,
        state_gate=state_gate,
        write=write,
        read=read,
        wide_inputs=wide_inputs,
        raw=raw,
        steps=steps,
        triangle=triangle,
        total=total,
        total_rows=total.T,
        leaving=leaving,
        expand=expand,
        steps_wide=spread[:rows],
        entered_wide=spread[rows : 2 * rows],
        tail_wide=spread[2 * rows :],
        stepped=(wide_inputs * spread[:rows]).astype(BFLOAT),
        tailed=(wide_inputs * spread[2 * rows :]).astype(BFLOAT),
        blocked=blocked,
        crossing=dot(write, read, (1, 1)) if turned_over else dot(read, write, (1, 1)),
    )


def decay_of(block, head):
    difference = block["total"][:, head : head + 1] - block["total_rows"][head : head + 1, :]
    return jnp.exp(difference + block["blocked"])


def turned_decay_of(block, head):
    difference = block["total_rows"][head : head + 1, :] - block["total"][:, head : head + 1]
    return jnp.exp(difference + block["blocked"])


def scan_forward_kernel(
    gate_ref, conv_ref, before_ref, state_ref, state_before_ref, step_ref, meta_ref, segment_ref, taps_ref,
    state_taps_ref, head_ref, skip_ref, mixed_ref, out_ref, scanned_ref, states_ref, state,
):
    del mixed_ref

    @pl.when(pl.program_id(0) == 0)
    def _():
        state[...] = jnp.zeros_like(state)

    block = scan_block(
        conv_ref, before_ref, state_ref, state_before_ref, step_ref, meta_ref, segment_ref, taps_ref, state_taps_ref,
        head_ref, False,
    )
    heads = conv_ref.shape[1] // HP
    carried = state[...].astype(BFLOAT)
    states_ref[0] = carried
    across = dot(block["read"], carried, (1, 0)) * block["entered_wide"]
    within = []
    for head in range(heads):
        weights = (block["crossing"] * decay_of(block, head)).astype(BFLOAT)
        within.append(dot(weights, block["stepped"][:, head * HP : (head + 1) * HP], (1, 0)))
    scanned = across + jnp.concatenate(within, axis=1)
    scanned_ref[...] = scanned
    gated, _ = silu_parts(gate_ref[...].astype(FLOAT))
    out_ref[...] = ((scanned + skip_ref[0:1, :] * block["wide_inputs"]) * gated).astype(BFLOAT)
    state[...] = state[...] * block["entered_wide"][SSD_BLOCK - 1 : SSD_BLOCK, :] + dot(
        block["write"], block["tailed"], (0, 0)
    )


def scan_backward_kernel(
    gate_ref, conv_ref, before_ref, state_ref, state_before_ref, step_ref, meta_ref, segment_ref, taps_ref,
    state_taps_ref, head_ref, skip_ref, scanned_ref, states_ref, grad_ref, out_ref, state_grad, later, state_later,
):
    @pl.when(pl.program_id(0) == 0)
    def _():
        state_grad[...] = jnp.zeros_like(state_grad)
        later[...] = jnp.zeros_like(later)
        state_later[...] = jnp.zeros_like(state_later)

    block = scan_block(
        conv_ref, before_ref, state_ref, state_before_ref, step_ref, meta_ref, segment_ref, taps_ref, state_taps_ref,
        head_ref, True,
    )
    rows = SSD_BLOCK
    channels = conv_ref.shape[1]
    heads = channels // HP
    meta = meta_ref[...]
    read, write = block["read"], block["write"]
    inputs = block["wide_inputs"]
    scanned = scanned_ref[...]
    skip = skip_ref[0:1, :]
    gate_values = gate_ref[...].astype(FLOAT)
    gated, gate = silu_parts(gate_values)
    grad = grad_ref[...].astype(FLOAT)
    gate_grad = grad * (scanned + skip * inputs) * silu_slope(gate_values, gate)
    out_grad = grad * gated
    inputs_grad = skip * out_grad
    rounded = out_grad.astype(BFLOAT)
    wide_rounded = rounded.astype(FLOAT)
    carried = states_ref[0]
    after = state_grad[...]
    after_rounded = after.astype(BFLOAT)

    from_state = dot(write, after_rounded, (1, 0))
    entering = (wide_rounded * block["entered_wide"]).astype(BFLOAT)
    write_grad = dot(block["tailed"], after_rounded, (1, 1))
    read_grad = dot(entering, carried, (1, 1))
    last_entered = block["entered_wide"][rows - 1 : rows, :]
    through = jnp.sum(after * carried.astype(FLOAT), axis=0, keepdims=True) * last_entered
    state_grad[...] = after * last_entered + dot(read, entering, (0, 0))

    crossing_grad = jnp.zeros((rows, rows), FLOAT)
    pulled = []
    for head in range(heads):
        span = slice(head * HP, (head + 1) * HP)
        decay = turned_decay_of(block, head)
        weights = (block["crossing"] * decay).astype(BFLOAT)
        pulled.append(dot(weights, rounded[:, span], (1, 0)))
        crossing_grad = crossing_grad + dot(block["stepped"][:, span], rounded[:, span], (1, 1)) * decay
    pulled = jnp.concatenate(pulled, axis=1)
    crossing_rounded = crossing_grad.astype(BFLOAT)
    read_grad = read_grad + dot(crossing_rounded, write, (0, 0))
    write_grad = write_grad + dot(crossing_rounded, read, (1, 0))

    inputs_grad = inputs_grad + block["steps_wide"] * pulled + block["tail_wide"] * from_state
    sums = head_sum(
        jnp.concatenate(
            [
                wide_rounded * scanned - block["stepped"].astype(FLOAT) * pulled,
                inputs * pulled,
                inputs * from_state,
                jnp.broadcast_to(through, (8, channels)),
            ],
            axis=0,
        ),
        block["expand"],
    )
    leaving_grad = sums[2 * rows : 3 * rows] * block["leaving"]
    leaving_total = leaving_grad * block["steps"]
    last = sums[3 * rows : 3 * rows + 1] + jnp.sum(leaving_total, axis=0, keepdims=True)
    total_grad = sums[:rows] - leaving_total
    total_grad = total_grad + jnp.where(
        lax.broadcasted_iota(jnp.int32, total_grad.shape, 0) == rows - 1, last, 0.0
    )
    decay_grad = running_sum(total_grad, block["triangle"], (0, 0))
    steps_grad = sums[rows : 2 * rows] + leaving_grad + decay_grad * head_ref[1:2, :]
    raw_grad = steps_grad / (1.0 + jnp.exp(-block["raw"]))
    raw_grad = jnp.where(lax.broadcasted_iota(jnp.int32, raw_grad.shape, 1) < heads, raw_grad, 0.0)

    state_slope = silu_slope(block["state_summed"], block["state_gate"])
    state_pre = conv_back(
        jnp.concatenate([write_grad, read_grad], axis=1) * state_slope, state_later, state_taps_ref, meta
    )
    conv_pre = conv_back(inputs_grad * silu_slope(block["summed"], block["conv_gate"]), later, taps_ref, meta)
    out_ref[:, : 2 * NSTATE] = state_pre.astype(BFLOAT)
    start = 2 * NSTATE + 2 * HEAD_SIZE
    out_ref[:, start : start + channels] = gate_grad.astype(BFLOAT)
    out_ref[:, start + channels : start + 2 * channels] = conv_pre.astype(BFLOAT)
    out_ref[:, out_ref.shape[1] - LANES :] = raw_grad.astype(BFLOAT)


STATES = 2 * NSTATE
PAIR = 2 * HEAD_SIZE


def scan_specs(channels, order):
    half = SSD_BLOCK // 16
    before = lambda i: jnp.maximum(order(i) * half - 1, 0)
    gate_at = (STATES + PAIR) // channels
    step_at = (STATES + PAIR + 2 * channels + channels * QUERY_HEADS // DSSM * HEAD_SIZE) // LANES
    return [
        pl.BlockSpec((SSD_BLOCK, channels), lambda i: (order(i), gate_at)),
        pl.BlockSpec((SSD_BLOCK, channels), lambda i: (order(i), gate_at + 1)),
        pl.BlockSpec((16, channels), lambda i: (before(i), gate_at + 1)),
        pl.BlockSpec((SSD_BLOCK, STATES), lambda i: (order(i), 0)),
        pl.BlockSpec((16, STATES), lambda i: (before(i), 0)),
        pl.BlockSpec((SSD_BLOCK, LANES), lambda i: (order(i), step_at)),
        pl.BlockSpec((SSD_BLOCK, LANES), lambda i: (order(i), 0)),
        pl.BlockSpec((8, SSD_BLOCK), lambda i: (0, order(i))),
        whole((8, channels)),
        whole((8, STATES)),
        whole((8, LANES)),
        whole((8, channels)),
    ]


def scan_operands(projected, tables):
    return [projected] * 6 + [
        tables[name] for name in ("meta", "segment_row", "taps", "state_taps", "head", "skip")
    ]


def scan_cost(tokens, channels, factor):
    heads = channels // HP
    return estimate(
        flops=factor * 2 * tokens * SSD_BLOCK * (3 * channels + NSTATE),
        bytes_accessed=factor * tokens * channels * 12,
        transcendentals=tokens * SSD_BLOCK * heads,
    )


def scan_forward(projected, tables, mixed):
    tokens = projected.shape[0]
    channels = tables["taps"].shape[1]
    blocks = tokens // SSD_BLOCK
    return pl.pallas_call(
        scan_forward_kernel,
        grid=(blocks,),
        in_specs=scan_specs(channels, lambda i: i) + [pl.BlockSpec(memory_space=pl.ANY)],
        out_specs=[
            pl.BlockSpec((SSD_BLOCK, channels), lambda i: (i, 0)),
            pl.BlockSpec((SSD_BLOCK, channels), lambda i: (i, 0)),
            pl.BlockSpec((1, NSTATE, channels), lambda i: (i, 0, 0)),
        ],
        out_shape=[
            jax.ShapeDtypeStruct(mixed.shape, BFLOAT),
            jax.ShapeDtypeStruct((tokens, channels), FLOAT),
            jax.ShapeDtypeStruct((blocks, NSTATE, channels), BFLOAT),
        ],
        scratch_shapes=[pltpu.VMEM((NSTATE, channels), FLOAT)],
        input_output_aliases={12: 0},
        compiler_params=pltpu.CompilerParams(vmem_limit_bytes=SCAN_BYTES),
        cost_estimate=scan_cost(tokens, channels, 1),
        name="scan_forward",
    )(*scan_operands(projected, tables), mixed)


def scan_backward(projected, tables, scanned, carried, mixed_grad):
    tokens, width = projected.shape
    channels = tables["taps"].shape[1]
    blocks = tokens // SSD_BLOCK
    back = lambda i: (blocks - 1 - i, 0)
    return pl.pallas_call(
        scan_backward_kernel,
        grid=(blocks,),
        in_specs=scan_specs(channels, lambda i: blocks - 1 - i)
        + [
            pl.BlockSpec((SSD_BLOCK, channels), back),
            pl.BlockSpec((1, NSTATE, channels), lambda i: (blocks - 1 - i, 0, 0)),
            pl.BlockSpec((SSD_BLOCK, channels), back),
        ],
        out_specs=pl.BlockSpec((SSD_BLOCK, width), back),
        out_shape=jax.ShapeDtypeStruct((tokens, width), BFLOAT),
        scratch_shapes=[
            pltpu.VMEM((NSTATE, channels), FLOAT),
            pltpu.VMEM((8, channels), FLOAT),
            pltpu.VMEM((8, STATES), FLOAT),
        ],
        compiler_params=pltpu.CompilerParams(vmem_limit_bytes=SCAN_BYTES),
        cost_estimate=scan_cost(tokens, channels, 2),
        name="scan_backward",
    )(*scan_operands(projected, tables), scanned, carried, mixed_grad)


def turned(values, cosine, sine):
    return (values * cosine + pltpu.roll(values, HEAD_SIZE // 2, 1) * sine).astype(BFLOAT)


def turned_back(values, cosine, sine):
    return values * cosine + pltpu.roll(values * sine, HEAD_SIZE // 2, 1)


ATT_ROWS = 256


def attention_mask(meta_ref, segment_ref, start, extent):
    row = start + lax.broadcasted_iota(jnp.int32, (ATT_ROWS, extent), 0)
    column = lax.broadcasted_iota(jnp.int32, (ATT_ROWS, extent), 1)
    return (row >= column) & (meta_ref[start : start + ATT_ROWS, 0:1] == segment_ref[0:1, :extent])


def probabilities(query, keys, allowed):
    score = dot(query, keys, (1, 1)) * (1.0 / math.sqrt(HEAD_SIZE))
    score = jnp.where(allowed, score, NEGATIVE)
    exponent = jnp.exp(score - jnp.max(score, axis=1, keepdims=True))
    return exponent / jnp.sum(exponent, axis=1, keepdims=True)


def attention_forward_kernel(query_ref, key_ref, value_ref, cosine_ref, sine_ref, meta_ref, segment_ref, out_ref, keys):
    tokens = key_ref.shape[0]
    keys[...] = turned(key_ref[...].astype(FLOAT), cosine_ref[...], sine_ref[...])
    for start in range(0, tokens, ATT_ROWS):
        extent = start + ATT_ROWS
        here = slice(start, extent)
        allowed = attention_mask(meta_ref, segment_ref, start, extent)
        for unit in range(query_ref.shape[1] // HEAD_SIZE):
            span = slice(unit * HEAD_SIZE, (unit + 1) * HEAD_SIZE)
            query = turned(query_ref[here, span].astype(FLOAT), cosine_ref[here], sine_ref[here])
            weights = probabilities(query, keys[:extent], allowed).astype(BFLOAT)
            out_ref[here, span] = dot(weights, value_ref[:extent], (1, 0)).astype(BFLOAT)


def attention_backward_kernel(
    query_ref, key_ref, value_ref, cosine_ref, sine_ref, meta_ref, segment_ref, grad_ref, held_ref,
    out_ref, keys, key_sum, value_sum, query_grad_ref, shared_grad_ref, sems,
):
    del held_ref
    tokens = key_ref.shape[0]
    scale = 1.0 / math.sqrt(HEAD_SIZE)
    keys[...] = turned(key_ref[...].astype(FLOAT), cosine_ref[...], sine_ref[...])
    key_sum[...] = jnp.zeros_like(key_sum)
    value_sum[...] = jnp.zeros_like(value_sum)
    for start in range(0, tokens, ATT_ROWS):
        extent = start + ATT_ROWS
        here = slice(start, extent)
        allowed = attention_mask(meta_ref, segment_ref, start, extent)
        for unit in range(query_ref.shape[1] // HEAD_SIZE):
            span = slice(unit * HEAD_SIZE, (unit + 1) * HEAD_SIZE)
            query = turned(query_ref[here, span].astype(FLOAT), cosine_ref[here], sine_ref[here])
            weights = probabilities(query, keys[:extent], allowed)
            grad = grad_ref[here, span]
            weights_grad = dot(grad, value_ref[:extent], (1, 1))
            value_sum[:extent] += dot(weights.astype(BFLOAT), grad, (0, 0))
            mean_grad = jnp.sum(weights * weights_grad, axis=1, keepdims=True)
            score_grad = (weights * (weights_grad - mean_grad) * scale).astype(BFLOAT)
            query_grad = dot(score_grad, keys[:extent], (1, 0))
            key_sum[:extent] += dot(score_grad, query, (0, 0))
            query_grad_ref[here, span] = turned_back(query_grad, cosine_ref[here], sine_ref[here]).astype(BFLOAT)
    shared_grad_ref[:, :HEAD_SIZE] = turned_back(key_sum[...], cosine_ref[...], sine_ref[...]).astype(BFLOAT)
    shared_grad_ref[:, HEAD_SIZE:] = value_sum[...].astype(BFLOAT)
    end = out_ref.shape[1] - LANES
    width = query_grad_ref.shape[1]
    copies = [
        pltpu.make_async_copy(query_grad_ref, out_ref.at[:, end - width : end], sems.at[0]),
        pltpu.make_async_copy(shared_grad_ref, out_ref.at[:, STATES : STATES + PAIR], sems.at[1]),
    ]
    for copy in copies:
        copy.start()
    for copy in copies:
        copy.wait()


def attention_cost(tokens, width, factor):
    return estimate(
        flops=factor * 2 * tokens * tokens * width,
        bytes_accessed=factor * tokens * width * 8,
        transcendentals=tokens * tokens * width // (2 * HEAD_SIZE),
    )


def attention_specs(tokens, channels):
    width = channels * QUERY_HEADS // DSSM * HEAD_SIZE
    narrow = whole((tokens, HEAD_SIZE))
    return [
        pl.BlockSpec((tokens, width), lambda *_: (0, (STATES + PAIR + 2 * channels) // width)),
        pl.BlockSpec((tokens, HEAD_SIZE), lambda *_: (0, STATES // HEAD_SIZE)),
        pl.BlockSpec((tokens, HEAD_SIZE), lambda *_: (0, STATES // HEAD_SIZE + 1)),
        narrow,
        narrow,
        whole((tokens, LANES)),
        whole((8, tokens)),
    ]


def attention_operands(projected, tables):
    return [projected] * 3 + [tables[name] for name in ("cosine", "sine", "meta", "segment_row")]


def attention_forward(projected, tables):
    tokens = projected.shape[0]
    channels = tables["taps"].shape[1]
    width = channels * QUERY_HEADS // DSSM * HEAD_SIZE
    return pl.pallas_call(
        attention_forward_kernel,
        grid=(1,),
        in_specs=attention_specs(tokens, channels),
        out_specs=pl.BlockSpec((tokens, width), lambda *_: (0, channels // width)),
        out_shape=jax.ShapeDtypeStruct((tokens, channels + width), BFLOAT),
        scratch_shapes=[pltpu.VMEM((tokens, HEAD_SIZE), BFLOAT)],
        compiler_params=pltpu.CompilerParams(vmem_limit_bytes=SCAN_BYTES),
        cost_estimate=attention_cost(tokens, width, 1),
        name="attention_forward",
    )(*attention_operands(projected, tables))


def attention_backward(projected, tables, mixed_grad, projected_grad):
    tokens = projected.shape[0]
    channels = tables["taps"].shape[1]
    width = channels * QUERY_HEADS // DSSM * HEAD_SIZE
    return pl.pallas_call(
        attention_backward_kernel,
        grid=(1,),
        in_specs=attention_specs(tokens, channels)
        + [pl.BlockSpec((tokens, width), lambda *_: (0, channels // width)), pl.BlockSpec(memory_space=pl.ANY)],
        out_specs=pl.BlockSpec(memory_space=pl.ANY),
        out_shape=jax.ShapeDtypeStruct(projected_grad.shape, BFLOAT),
        scratch_shapes=[
            pltpu.VMEM((tokens, HEAD_SIZE), BFLOAT),
            pltpu.VMEM((tokens, HEAD_SIZE), FLOAT),
            pltpu.VMEM((tokens, HEAD_SIZE), FLOAT),
            pltpu.VMEM((tokens, width), BFLOAT),
            pltpu.VMEM((tokens, PAIR), BFLOAT),
            pltpu.SemaphoreType.DMA((2,)),
        ],
        input_output_aliases={8: 0},
        compiler_params=pltpu.CompilerParams(vmem_limit_bytes=SCAN_BYTES),
        cost_estimate=attention_cost(tokens, width, 3),
        name="attention_backward",
    )(*attention_operands(projected, tables), mixed_grad, projected_grad)


def mixer_tables(lengths, segment, position, conv_values, conv_states, scan_params):
    tokens = segment.shape[0]
    block = jnp.arange(tokens, dtype=jnp.int32) // SSD_BLOCK
    previous = jnp.concatenate([jnp.full((1,), -1, jnp.int32), segment[:-1]])
    first_previous = jnp.repeat(previous[::SSD_BLOCK], SSD_BLOCK)
    last_segment = jnp.repeat(segment[SSD_BLOCK - 1 :: SSD_BLOCK], SSD_BLOCK)
    length = jnp.sum(
        jnp.where(segment[:, None] == jnp.arange(lengths.shape[0], dtype=jnp.int32)[None, :], lengths[None, :], 0),
        axis=1,
    )
    columns = [
        segment,
        position,
        length - 1 - position,
        segment == first_previous,
        segment == last_segment,
    ]
    meta = jnp.stack([column.astype(FLOAT) for column in columns], axis=1)
    half_width = HEAD_SIZE // 2
    frequency = ROPE_BASE ** (-2.0 * jnp.arange(half_width, dtype=FLOAT) / HEAD_SIZE)
    angle = position.astype(FLOAT)[:, None] * frequency[None, :]
    cosine, sine = jnp.cos(angle), jnp.sin(angle)
    heads = scan_params.shape[1]
    head = jnp.stack([scan_params[0], -jnp.exp(scan_params[1]), scan_params[2]])
    return dict(
        meta=jnp.pad(meta, ((0, 0), (0, LANES - meta.shape[1]))),
        segment_row=jnp.broadcast_to(segment.astype(FLOAT)[None, :], (8, tokens)),
        taps=jnp.pad(conv_values.astype(FLOAT), ((0, 3), (0, 0))),
        state_taps=jnp.pad(conv_states.astype(FLOAT), ((0, 3), (0, 0))),
        head=jnp.pad(head, ((0, 5), (0, LANES - heads))),
        skip=jnp.broadcast_to(jnp.repeat(scan_params[2], HP)[None, :], (8, heads * HP)),
        cosine=jnp.concatenate([cosine, cosine], axis=1),
        sine=jnp.concatenate([-sine, sine], axis=1),
    )


HALVES = 2
DENSE_TILE = 1024


def matrix_rows(values):
    return values.reshape(values.shape[0] * values.shape[1], values.shape[2])


def cut_tiles(width, tile):
    return [(low, min(low + tile, width)) for low in range(0, width, tile)]


def spread_kernel(mask, count, left_ref, right_ref, chosen_ref, *rest):
    weights, (out_ref, narrow_ref, out_tile, narrow, sems) = rest[:count], rest[-5:]
    rows = left_ref.shape[0]
    shards = weights[0].shape[0]
    depth = shards // HALVES
    start = pl.multiple_of((lax.axis_index("col") ^ mask) * rows, rows)
    here = pl.ds(start, rows)

    def through(ref, low, high):
        return dot(left_ref[...], matrix_rows(ref[:depth, :rows, low:high]), (1, 0)) + dot(
            right_ref[...], matrix_rows(ref[depth:, :rows, low:high]), (1, 0)
        )

    lower = weights[-1].shape[2] - LANES
    narrow[...] = (chosen_ref[here, :] * through(weights[-1], lower, lower + LANES)).astype(BFLOAT)
    copies = [pltpu.make_async_copy(narrow, narrow_ref.at[here, :], sems.at[0])]
    copies[0].start()
    column = 0
    for ref in weights:
        for low, high in cut_tiles(ref.shape[2] - (LANES if ref is weights[-1] else 0), DENSE_TILE):
            span = slice(column, column + high - low)
            column += high - low
            raised = matrix_rows(ref[:, rows : rows + NADAPT * RANK // shards, low:high])
            out_tile[:, span] = (through(ref, low, high) + dot(narrow[...], raised, (1, 0))).astype(BFLOAT)
            copies.append(
                pltpu.make_async_copy(out_tile.at[:, span], out_ref.at[here, span], sems.at[len(copies)])
            )
            copies[-1].start()
    for copy in copies:
        copy.wait()


def weights_width(gathered):
    return sum(part.shape[2] for part in gathered) - LANES


def spread_block(mask, halves, gathered, selector, held):
    rows, half = halves[0].shape
    width = weights_width(gathered)
    total = selector.shape[0]
    fast, free = pl.BlockSpec(memory_space=pltpu.VMEM), pl.BlockSpec(memory_space=pl.ANY)
    operands = [*halves, selector, *gathered]
    in_specs = [fast] * len(operands)
    aliases = {}
    if held is not None:
        aliases = {len(operands): 0, len(operands) + 1: 1}
        operands += list(held)
        in_specs += [free] * 2
    copies = 1 + sum(-(-part.shape[2] // DENSE_TILE) for part in gathered)
    return pl.pallas_call(
        functools.partial(spread_kernel, mask, len(gathered)),
        in_specs=in_specs,
        out_specs=[free] * 2,
        out_shape=[
            jax.ShapeDtypeStruct((total, width), BFLOAT),
            jax.ShapeDtypeStruct((total, LANES), BFLOAT),
        ],
        scratch_shapes=[
            pltpu.VMEM((rows, width), BFLOAT),
            pltpu.VMEM((rows, LANES), BFLOAT),
            pltpu.SemaphoreType.DMA((copies,)),
        ],
        input_output_aliases=aliases,
        compiler_params=pltpu.CompilerParams(vmem_limit_bytes=DENSE_BYTES),
        cost_estimate=estimate(
            flops=4 * rows * half * (width + LANES), bytes_accessed=2 * rows * (2 * half + width), transcendentals=0
        ),
        name="spread_block",
    )(*operands)


def collect_kernel(masks, count, values_ref, *refs):
    weights, outs = refs[:count], refs[count:]
    rows = values_ref.shape[0] // 4
    shards = weights[0].shape[0]
    half = shards // HALVES * rows
    width = values_ref.shape[1]
    starts, column = [], 0
    for ref in weights:
        high = min(column + ref.shape[2], width)
        starts.append((column, high))
        column = high
    for at, mask in enumerate(masks):
        here = pl.ds(pl.multiple_of((lax.axis_index("col") ^ mask) * rows, rows), rows)
        first, second = outs[2 * at], outs[2 * at + 1]

        def through(cut):
            total = None
            for (low, high), ref in zip(starts, weights):
                part = dot(values_ref[here, low:high], cut(ref, high - low), (1, 1))
                total = part if total is None else total + part
            return total

        for shard in range(shards):
            out_ref = first if shard < shards // HALVES else second
            column = shard * rows % half
            out_ref[:, column : column + rows] = through(lambda ref, wide: ref[shard, :rows, :wide]).astype(
                out_ref.dtype
            )
        first[:, half:] = through(
            lambda ref, wide: matrix_rows(ref[:, rows : rows + NADAPT * RANK // shards, :wide])
        ).astype(first.dtype)


def collect_blocks(masks, values, gathered, types):
    rows = values.shape[0] // 4
    half = gathered[0].shape[0] // HALVES * rows
    fast = pl.BlockSpec(memory_space=pltpu.VMEM)
    out_shape = []
    for pair in types:
        out_shape.append(jax.ShapeDtypeStruct((rows, half + LANES), pair[0]))
        out_shape.append(jax.ShapeDtypeStruct((rows, half), pair[1]))
    outs = pl.pallas_call(
        functools.partial(collect_kernel, masks, len(gathered)),
        in_specs=[fast] * (1 + len(gathered)),
        out_specs=[fast] * len(out_shape),
        out_shape=out_shape,
        compiler_params=pltpu.CompilerParams(vmem_limit_bytes=DENSE_BYTES),
        cost_estimate=estimate(
            flops=4 * len(masks) * rows * half * values.shape[1],
            bytes_accessed=2 * len(masks) * rows * (values.shape[1] + 4 * half),
            transcendentals=0,
        ),
        name="collect_blocks",
    )(values, *gathered)
    return [tuple(outs[2 * at : 2 * at + 2]) for at in range(len(masks))]


def root_mean(values):
    return lax.rsqrt(jnp.mean(values * values, axis=1, keepdims=True) + EPSILON)


def finish_kernel(kind, first_own, first_near, first_far, second_own, second_near, second_far, lower_ref, chosen_ref,
                  *refs):
    half = second_own.shape[1]
    wide = lambda ref: ref[...].astype(FLOAT)
    first = wide(first_own) + wide(first_near) + wide(first_far)
    second = wide(second_own) + wide(second_near) + wide(second_far)
    inner = (chosen_ref[...] * first[:, half:]).astype(BFLOAT)
    summed = jnp.concatenate([first[:, :half], second], axis=1) + dot(
        inner, matrix_rows(lower_ref[...]), (1, 1)
    )
    if kind == "output":
        residual_ref, out_ref, inner_ref = refs
        inner_ref[...] = inner
        out_ref[...] = (residual_ref[...] + summed).astype(BFLOAT)
        return
    if kind == "forward":
        residual_ref, gain_ref, out_ref, inner_ref, left_ref, right_ref = refs
        hidden = residual_ref[...] + summed
        normed = (hidden * root_mean(hidden) * gain_ref[0:1, :]).astype(BFLOAT)
        out_ref[...] = hidden
    else:
        values_ref, upstream_ref, gain_ref = refs[:3]
        values = values_ref[...]
        scale = root_mean(values)
        weighted = summed * gain_ref[0:1, :]
        mean = jnp.mean(weighted * values, axis=1, keepdims=True)
        hidden = upstream_ref[...].astype(FLOAT) + scale * weighted - values * (scale * scale * scale * mean)
        normed = hidden.astype(BFLOAT)
        if kind == "input":
            out_ref, inner_ref = refs[3:]
            inner_ref[...] = inner
            out_ref[...] = normed
            return
        out_ref, inner_ref, left_ref, right_ref = refs[3:]
        out_ref[...] = hidden
    inner_ref[...] = inner
    left_ref[...] = normed[:, :half]
    right_ref[...] = normed[:, half:]


def finish(kind, parts, gathered, own_selector, *operands):
    rows = own_selector.shape[0]
    half = parts[3].shape[1]
    shards = gathered[-1].shape[0]
    model = HALVES * half
    lower = gathered[-1][:, : model // shards, -LANES:]
    result = BFLOAT if kind in ("output", "input") else FLOAT
    out_shape = [jax.ShapeDtypeStruct((rows, model), result), jax.ShapeDtypeStruct((rows, LANES), BFLOAT)]
    if kind in ("forward", "backward"):
        out_shape += [jax.ShapeDtypeStruct((rows, half), BFLOAT)] * 2
    given = [*parts, lower, own_selector, *operands]
    in_specs = [whole(value.shape) for value in given]
    return pl.pallas_call(
        functools.partial(finish_kernel, kind),
        grid=(1,),
        in_specs=in_specs,
        out_specs=[whole(shape.shape) for shape in out_shape],
        out_shape=out_shape,
        compiler_params=pltpu.CompilerParams(vmem_limit_bytes=DENSE_BYTES),
        cost_estimate=estimate(
            flops=2 * rows * model * LANES, bytes_accessed=rows * model * 20, transcendentals=0
        ),
        name="finish_" + kind,
    )(*given)


def send_kernel(target_column, target_row, tokens_ref, adapter_ref, sent_ref, matrix_ref):
    rows = tokens_ref.shape[0]
    model = tokens_ref.shape[1]
    peer = adapter_ref.shape[0]
    column, row = target_column[:, 0:1], target_row[0:1, :]
    earlier = lax.broadcasted_iota(jnp.int32, (rows, rows), 0) < lax.broadcasted_iota(jnp.int32, (rows, rows), 1)
    same = jnp.where((column // rows == row // rows) & earlier, 1.0, 0.0)
    place = (row // rows) * peer + jnp.sum(same, axis=0, keepdims=True).astype(jnp.int32)
    matrix = (lax.broadcasted_iota(jnp.int32, (rows, rows), 0) == place).astype(BFLOAT)
    matrix_ref[...] = matrix
    sent_ref[:, :model] = dot(matrix, tokens_ref[...], (1, 0)).astype(BFLOAT)
    lane = lax.broadcasted_iota(jnp.int32, (rows, LANES), 1)
    slots = jnp.where(lane == 0, column % rows, 0).astype(FLOAT).astype(BFLOAT)
    notes = dot(matrix, slots, (1, 0))
    sent_ref[:, model:] = jnp.where(lane == 0, notes, adapter_ref[0:1, :]).astype(BFLOAT)


def send_tokens(target, tokens, adapters, peer):
    rows, model = tokens.shape
    notes = jnp.pad(adapters.astype(FLOAT), (1, LANES - 1 - adapters.shape[0]))
    return pl.pallas_call(
        send_kernel,
        in_specs=[pl.BlockSpec(memory_space=pltpu.VMEM)] * 4,
        out_specs=[pl.BlockSpec(memory_space=pltpu.VMEM)] * 2,
        out_shape=[
            jax.ShapeDtypeStruct((rows, model + LANES), BFLOAT),
            jax.ShapeDtypeStruct((rows, rows), BFLOAT),
        ],
        compiler_params=pltpu.CompilerParams(vmem_limit_bytes=DENSE_BYTES),
        name="send_tokens",
    )(
        jnp.broadcast_to(target[:, None], (rows, LANES)),
        jnp.broadcast_to(target[None, :], (8, rows)),
        tokens,
        jnp.broadcast_to(notes[None, :], (peer, LANES)),
    )


def arrive_kernel(arrived_ref, gain_ref, own_ref, matrix_ref, left_ref, right_ref):
    rows, model = own_ref.shape
    slots = arrived_ref[:, model:].astype(FLOAT).T[0:1, :]
    row = lax.broadcasted_iota(jnp.int32, (rows, rows), 0).astype(FLOAT)
    matrix = (row == slots).astype(BFLOAT)
    matrix_ref[...] = matrix
    own = dot(matrix, arrived_ref[:, :model], (1, 0))
    own_ref[...] = own
    normed = (own * root_mean(own) * gain_ref[0:1, :]).astype(BFLOAT)
    left_ref[...] = normed[:, : model // HALVES]
    right_ref[...] = normed[:, model // HALVES :]


def arrive_tokens(arrived, gain):
    rows, model = arrived.shape[0], arrived.shape[1] - LANES
    return pl.pallas_call(
        arrive_kernel,
        in_specs=[pl.BlockSpec(memory_space=pltpu.VMEM)] * 2,
        out_specs=[pl.BlockSpec(memory_space=pltpu.VMEM)] * 4,
        out_shape=[
            jax.ShapeDtypeStruct((rows, model), FLOAT),
            jax.ShapeDtypeStruct((rows, rows), BFLOAT),
            jax.ShapeDtypeStruct((rows, model // HALVES), BFLOAT),
            jax.ShapeDtypeStruct((rows, model // HALVES), BFLOAT),
        ],
        compiler_params=pltpu.CompilerParams(vmem_limit_bytes=DENSE_BYTES),
        name="arrive_tokens",
    )(arrived, gain)


GATE_WIDTH = DSSM // QUERY_HEADS
PAIR_WIDTH = 2 * KEY_VALUE_HEADS * HEAD_SIZE // QUERY_HEADS
STATE_WIDTH = 2 * NSTATE // QUERY_HEADS
STEP_WIDTH = NH // QUERY_HEADS
ALL_AXES = ("row", "col")


def pad_columns(values, width):
    return jnp.pad(values, ((0, 0), (0, width - values.shape[1])))


def after(values, *earlier):
    return lax.optimization_barrier((values, *earlier))[0]


def after_all(values, *earlier):
    return lax.optimization_barrier((*values, *earlier))[: len(values)]


def unit_parts(values, units):
    cuts = [0]
    for width in (GATE_WIDTH, GATE_WIDTH, HEAD_SIZE, PAIR_WIDTH, STATE_WIDTH, STEP_WIDTH):
        cuts.append(cuts[-1] + width)
    return [
        jnp.concatenate(
            [values[:, unit * UNIT_IN + low : unit * UNIT_IN + high] for unit in range(units)], axis=1
        )
        for low, high in zip(cuts[:-1], cuts[1:])
    ]


def restore_units(parts, units):
    ordered = []
    for unit in range(units):
        for part in parts:
            width = part.shape[1] // units
            ordered.append(part[:, unit * width : (unit + 1) * width])
    return jnp.concatenate(ordered, axis=1)


def split_halves(values, units, first, axis):
    block = values.shape[axis] // units
    take = lambda low, high: lax.slice_in_dim(values, low, high, axis=axis)
    parts = [take(unit * block, unit * block + first) for unit in range(units)]
    parts += [take(unit * block + first, (unit + 1) * block) for unit in range(units)]
    return jnp.concatenate(parts, axis=axis)


def join_halves(values, units, first, axis):
    block = values.shape[axis] // units
    rest = block - first
    take = lambda low, high: lax.slice_in_dim(values, low, high, axis=axis)
    parts = []
    for unit in range(units):
        parts.append(take(unit * first, (unit + 1) * first))
        parts.append(take(units * first + unit * rest, units * first + (unit + 1) * rest))
    return jnp.concatenate(parts, axis=axis)


def quick(rows):
    return lax.axis_size("col") == 4 and lax.axis_size("row") == 8 and rows == 256


def flip(values, mask):
    return lax.ppermute(values, "col", [(i, i ^ mask) for i in range(4)])


def gather_blocks(halves):
    left, right = halves
    far_left, near_right = flip(left, 2), flip(right, 1)
    near_left, far_right = flip(left, 1), flip(right, 2)
    corner_left, corner_right = flip(far_left, 1), flip(near_right, 2)
    return [
        (0, (left, right)),
        (1, (near_left, near_right)),
        (2, (far_left, far_right)),
        (3, (corner_left, corner_right)),
    ]


def rows_of(values, block, rows):
    return lax.dynamic_slice_in_dim(values, block * rows, rows, 0)


def spread_gathered(blocks, gathered, selector):
    held = None
    for mask, values in blocks:
        held = spread_block(mask, values, gathered, selector, held)
    return held


def spread_project(halves, gathered, selector):
    rows = halves[0].shape[0]
    if quick(rows):
        return spread_gathered(gather_blocks(halves), gathered, selector)
    wide, narrow_factor = gathered
    width = narrow_factor.shape[1]
    both = product(lax.all_gather(jnp.concatenate(halves, axis=1), "col", axis=0, tiled=True), wide)
    narrow = (selector * both[:, width:]).astype(BFLOAT)
    return (both[:, :width] + product(narrow, narrow_factor)).astype(BFLOAT), narrow


PIECE_TYPES = [(BFLOAT, BFLOAT), (BFLOAT, FLOAT), (FLOAT, BFLOAT), (FLOAT, FLOAT)]


def collect_pieces(values, gathered, at_once):
    if at_once:
        return collect_blocks([3, 1, 2, 0], values, gathered, PIECE_TYPES)
    (corner,) = collect_blocks([3], values, gathered, PIECE_TYPES[:1])
    values = after(values, corner[0])
    return [corner, *collect_blocks([1, 2, 0], values, gathered, PIECE_TYPES[1:])]


def collect_send(pieces, ordered=True):
    corner, near, far, own = pieces
    arriving = flip(corner[0], 1), flip(corner[1], 2)
    sent_near, sent_far = after_all((near[0], far[1]), *arriving) if ordered else (near[0], far[1])
    return own, flip(sent_near, 1), flip(sent_far, 2), far[0], near[1], arriving


def collect_middle(started):
    own, near_first, far_second, far_first, near_second, arriving = started
    onward = [
        (kept + part.astype(FLOAT)).astype(BFLOAT) for kept, part in zip((far_first, near_second), arriving)
    ]
    return (own, near_first, far_second), onward


def collect_onward(onward):
    return flip(onward[0], 2), flip(onward[1], 1)


def collect_end(kept, last, kind, gathered, own_selector, *operands):
    own, near_first, far_second = kept
    parts = [own[0], near_first, last[0], own[1], far_second, last[1]]
    return finish(kind, parts, gathered, own_selector, *operands)


def collect_project(values, gathered, kind, own_selector, *operands):
    rows, model = own_selector.shape[0], operands[0].shape[1]
    if quick(rows):
        kept, onward = collect_middle(collect_send(collect_pieces(values, gathered, False)))
        return collect_end(kept, collect_onward(onward), kind, gathered, own_selector, *operands)
    wide, narrow_factor = gathered
    width = narrow_factor.shape[1]
    partial = jnp.concatenate(
        [contract_last(values, wide[:, :width]), contract_last(values, narrow_factor)], axis=1
    ).astype(BFLOAT)
    summed = lax.psum_scatter(partial, "col", scatter_dimension=0, tiled=True).astype(FLOAT)
    inner = (own_selector * summed[:, model:]).astype(BFLOAT)
    summed = summed[:, :model] + contract_last(inner, wide[:, width:])
    if kind == "output":
        return (operands[0] + summed).astype(BFLOAT), inner
    if kind == "forward":
        residual, gain = operands
        hidden = residual + summed
        return hidden, inner, *cut_halves(rms_norm(hidden, gain[0]).astype(BFLOAT))
    values, upstream, gain = operands
    _, back = jax.vjp(lambda given: rms_norm(given, gain[0]), values)
    hidden = upstream.astype(FLOAT) + back(summed)[0]
    if kind == "input":
        return hidden.astype(BFLOAT), inner
    return hidden, inner, *cut_halves(hidden.astype(BFLOAT))


def cut_halves(values):
    half = values.shape[1] // HALVES
    return values[:, :half], values[:, half:]


def local(
    tokens_in,
    cotangent,
    target,
    sequence_lengths,
    sequence_adapter,
    norm_gains,
    weight_in,
    conv_values,
    conv_states,
    scan_params,
    weight_mix,
    weight_feed,
    weight_down,
    in_lower,
    in_raise,
    mix_lower,
    mix_raise,
    feed_lower,
    feed_raise,
    down_lower,
    down_raise,
):
    cols = lax.axis_size("col")
    rows_axis = lax.axis_size("row")
    col = lax.axis_index("col")
    devices = cols * rows_axis
    rows = tokens_in.shape[0]
    model = tokens_in.shape[1]
    total = rows * cols
    units = QUERY_HEADS // cols
    channels = units * GATE_WIDTH
    peer = rows // devices
    lengths, adapters = sequence_lengths[0], sequence_adapter[0]
    sequences = lengths.shape[0]
    fast = quick(rows)
    key_head = col * units // (QUERY_HEADS // KEY_VALUE_HEADS)
    exchange = lambda values: lax.all_to_all(values, ALL_AXES, split_axis=0, concat_axis=0, tiled=True)

    sent, send_matrix = send_tokens(target, tokens_in, adapters, peer)
    shards = []

    def gather_weight(weight, lower, raised):
        top = jnp.concatenate([weight, lower], axis=1)
        if fast:
            bottom = pad_columns(raised, top.shape[1])
            shards.append(jnp.concatenate([top, bottom], axis=0))
            return (lax.all_gather(shards[-1], "row", axis=0),)
        wide = lax.all_gather(top, "row", axis=0, tiled=True)
        return wide, lax.all_gather(raised, "row", axis=0, tiled=True)

    depth = weight_in.shape[0]
    height = depth + in_raise.shape[0]
    given = after(jnp.concatenate([weight_in, in_raise], axis=0), send_matrix)
    gates, convs, queries, pairs, states, steps = unit_parts(given, units)
    pair_width, state_width = pairs.shape[1], states.shape[1]
    taps = jnp.concatenate([jnp.zeros((KCONV + 1, pair_width), BFLOAT), conv_states], axis=1)
    taps = jnp.pad(taps, ((0, 16 - KCONV - 1), (0, 0)))
    shared = jnp.concatenate([jnp.concatenate([pairs, states], axis=1), taps], axis=0)
    own_columns = jnp.concatenate([gates, convs, queries, pad_columns(steps, LANES)], axis=1)
    if fast:
        shared_shard = shared
        shared = lax.all_gather(shared_shard, "row", axis=0)
        weights_own = gather_weight(own_columns[:depth], in_lower, own_columns[depth:])
    arrived = exchange(sent)
    gains = jnp.broadcast_to(norm_gains.astype(FLOAT)[:, None, :], (2, 8, model))
    if fast:
        near, far = flip(shared, 1), flip(shared, 2)
        arrived = after(arrived, near, far, shards[0])
    own_input, place_matrix, *normed_one = arrive_tokens(arrived.reshape(rows, model + LANES), gains[0])
    blocks_one = gather_blocks(normed_one) if fast else normed_one
    if fast:
        held = jnp.zeros((cols,) + shared.shape, BFLOAT)
        for block, values in ((col, shared), (col ^ 1, near), (col ^ 2, far)):
            held = lax.dynamic_update_index_in_dim(held, values, block, 0)
        split = shared.shape[0] // 2
        corner = jnp.concatenate([flip(near[:split], 2), flip(far[split:], 1)], axis=0)
        held = lax.dynamic_update_index_in_dim(held, corner, col ^ 3, 0)
    else:
        held = lax.all_gather(shared, "col", axis=0)
    all_pairs = jnp.concatenate([held[at, ..., :height, :pair_width] for at in range(cols)], axis=-1)
    pick = lambda start: lax.select_n(
        key_head,
        *[all_pairs[..., start + at * HEAD_SIZE : start + (at + 1) * HEAD_SIZE] for at in range(KEY_VALUE_HEADS)],
    )
    shared_columns = jnp.concatenate(
        [held[at, ..., :height, pair_width:] for at in range(cols)]
        + [pick(0), pick(KEY_VALUE_HEADS * HEAD_SIZE)],
        axis=-1,
    )
    tap_rows = held[:, 0] if fast else held
    all_taps = jnp.concatenate(
        [tap_rows[at, height : height + KCONV + 1, pair_width:] for at in range(cols)], axis=1
    )
    if fast:
        weights_in = (shared_columns, *weights_own)
    else:
        columns = jnp.concatenate([shared_columns, own_columns], axis=1)
        weights_in = gather_weight(columns[:depth], in_lower, columns[depth:])
    weights_mix = gather_weight(
        after(split_halves(weight_mix, units, GATE_WIDTH, 0).T, sent),
        mix_raise.T,
        split_halves(mix_lower, units, GATE_WIDTH, 0).T,
    )
    weights_feed = gather_weight(
        after(split_halves(weight_feed, units, UNIT_FF, 1), arrived),
        feed_lower,
        split_halves(feed_raise, units, UNIT_FF, 1),
    )

    source_adapters = arrived.reshape(rows, model + LANES)[::peer, model + 1 : model + 1 + sequences].astype(jnp.int32)
    segment, position, selector = sequence_tables(lengths, adapters, total)
    own_selector = rows_of(selector, col, rows)
    own_segment = rows_of(segment, col, rows)
    tables = mixer_tables(lengths, segment, position, conv_values, all_taps, scan_params)

    def compact_grad(narrow, values):
        parts = [
            lax.dynamic_slice_in_dim(narrow, adapters[at] * RANK, RANK, 1)
            * (own_segment == at).astype(BFLOAT)[:, None]
            for at in range(sequences)
        ]
        grad = contract_first(jnp.concatenate(parts, axis=1), values).astype(BFLOAT)
        kept = sequences * RANK
        grad = grad.reshape(kept, devices, model // devices).transpose(1, 0, 2)
        return grad.reshape(devices, peer, kept * model // devices // peer)

    def expand_grad(dealt):
        kept = sequences * RANK
        dealt = dealt.reshape(devices * kept, model // devices)
        adapter_row = (source_adapters[:, :, None] * RANK + jnp.arange(RANK, dtype=jnp.int32)).reshape(-1)
        chosen = (jnp.arange(NADAPT * RANK, dtype=jnp.int32)[:, None] == adapter_row[None, :]).astype(BFLOAT)
        return product(chosen, dealt)

    def send_back(values, grads, earlier=()):
        back = contract_first(place_matrix, values).astype(BFLOAT).reshape(devices, peer, model)
        payload = jnp.concatenate([back, *grads], axis=2)
        payload = after(payload, *earlier) if earlier else payload
        payloads.append(payload)
        return exchange(payload)

    payloads = []

    def take_back(dealt, count):
        returned = contract_first(send_matrix, dealt[:, :, :model].reshape(rows, model)).astype(BFLOAT)
        width = (dealt.shape[2] - model) // max(count, 1)
        return returned, [
            expand_grad(dealt[:, :, model + at * width : model + (at + 1) * width]) for at in range(count)
        ]

    projected, inner_in = (spread_gathered if fast else spread_project)(blocks_one, weights_in, selector)

    sent_grad = product(send_matrix, cotangent).astype(BFLOAT).reshape(devices, peer, model)
    arrived_grad = exchange(after(sent_grad, normed_one[0])).reshape(rows, model)
    branch_two = product(place_matrix, arrived_grad).astype(BFLOAT)
    weights_down = gather_weight(after(weight_down.T, projected), down_raise.T, down_lower.T)

    mixed_out = attention_forward(projected, tables)
    mixed_out, scanned, carried = scan_forward(projected, tables, mixed_out)
    hidden, inner_out, *normed_two = collect_project(mixed_out, weights_mix, "forward", own_selector, own_input, gains[1])
    gate_up, inner_feed = spread_project(normed_two, weights_feed, selector)
    act_grad, narrow_two = spread_project(cut_halves(after(branch_two, projected)), weights_down, selector)
    half_feed = units * UNIT_FF
    gate_part, up_part = gate_up[:, :half_feed].astype(FLOAT), gate_up[:, half_feed:].astype(FLOAT)
    gate = jax.nn.sigmoid(gate_part)
    silu = gate_part * gate
    activated = (silu * up_part).astype(BFLOAT)
    wide_grad = act_grad.astype(FLOAT)
    feed_grad = jnp.concatenate(
        [wide_grad * up_part * (gate * (1.0 + gate_part * (1.0 - gate))), wide_grad * silu], axis=1
    ).astype(BFLOAT)
    if fast:
        pieces = collect_pieces(after(activated, feed_grad), weights_down, True)
        kept, onward = collect_middle(collect_send(collect_pieces(feed_grad, weights_feed, False)))
        hidden_grad, narrow_three, *branch_one = collect_end(
            kept,
            collect_onward(onward),
            "backward",
            weights_feed,
            own_selector,
            after(hidden, pieces[3][0]),
            branch_two,
            gains[1],
        )
        blocks_branch = gather_blocks(branch_one)
    else:
        hidden_grad, narrow_three, *branch_one = collect_project(
            feed_grad, weights_feed, "backward", own_selector, hidden, branch_two, gains[1]
        )
    early_grads = [
        compact_grad(narrow_three, jnp.concatenate(normed_two, axis=1)),
        compact_grad(inner_out, jnp.concatenate(branch_one, axis=1)),
    ]
    if fast:
        blocks_branch[3] = (3, after_all(blocks_branch[3][1], *early_grads))
        mixed_grad, narrow_one = spread_gathered(blocks_branch, weights_mix, selector)
    else:
        mixed_grad, narrow_one = spread_project(branch_one, weights_mix, selector)

    if fast:
        near_parts = after_all((*pieces[0], pieces[1][0], pieces[2][1]), mixed_grad)
        started = collect_send(
            [near_parts[:2], (near_parts[2], pieces[1][1]), (pieces[2][0], near_parts[3]), pieces[3]], False
        )
        projected_grad = scan_backward(projected, tables, scanned, carried, after(mixed_grad, near_parts[0]))
        kept, onward = collect_middle((*started[:5], [after(part, projected_grad) for part in started[5]]))
        projected_grad = attention_backward(
            projected, tables, mixed_grad, after(projected_grad, *onward, *kept[1:])
        )
        last = collect_onward(onward)
        started_in = collect_send(collect_pieces(projected_grad, weights_in, True))
        kept_in, onward_in = collect_middle(started_in)
        block_out, inner_down = collect_end(
            kept, last, "output", weights_down, own_selector, after(hidden, started_in[0][0])
        )
    else:
        block_out, inner_down = collect_project(activated, weights_down, "output", own_selector, hidden)
        projected_grad = scan_backward(projected, tables, scanned, carried, mixed_grad)
        projected_grad = attention_backward(projected, tables, mixed_grad, projected_grad)
    dealt_out = send_back(
        block_out,
        [
            compact_grad(inner_down, branch_two),
            *early_grads,
        ],
    )

    def sum_rows(values):
        return lax.psum_scatter(values.astype(BFLOAT), "row", scatter_dimension=0, tiled=True).astype(FLOAT)

    early_parts = [
        contract_first(narrow_one, mixed_out),
        contract_first(inner_feed, feed_grad),
        contract_first(narrow_two, activated),
    ]
    early = sum_rows(jnp.concatenate(early_parts, axis=1))

    raise_grad = contract_first(inner_in, after(projected_grad, *onward_in) if fast else projected_grad)
    late = sum_rows(raise_grad)

    if fast:
        input_grad, narrow_four = collect_end(
            kept_in,
            collect_onward(onward_in),
            "input",
            weights_in,
            own_selector,
            own_input,
            after(hidden_grad, payloads[0]),
            gains[0],
        )
    else:
        input_grad, narrow_four = collect_project(
            projected_grad, weights_in, "input", own_selector, own_input, hidden_grad, gains[0]
        )
    dealt_grad = send_back(
        input_grad, [compact_grad(narrow_four, jnp.concatenate(normed_one, axis=1))], [dealt_out]
    )
    dealt_out, early, late = after_all((dealt_out, early, late), payloads[-1])
    early_cuts = [0, early_parts[0].shape[1]]
    early_cuts.append(early_cuts[1] + early_parts[1].shape[1])
    grad_mix_lower = join_halves(early[:, : early_cuts[1]], units, GATE_WIDTH, 1).T
    grad_feed_raise = join_halves(early[:, early_cuts[1] : early_cuts[2]], units, UNIT_FF, 1)
    grad_down_lower = early[:, early_cuts[2] :].T

    key_columns = late[:, STATES : STATES + HEAD_SIZE]
    value_columns = late[:, STATES + HEAD_SIZE : STATES + PAIR]
    mine = [(key_head == at).astype(FLOAT) for at in range(KEY_VALUE_HEADS)]
    pair_grad = jnp.concatenate([part * here for part in (key_columns, value_columns) for here in mine], axis=1)
    stacked = jnp.stack(
        [
            jnp.concatenate(
                [
                    pair_grad[:, at * pair_width : (at + 1) * pair_width],
                    late[:, at * state_width : (at + 1) * state_width],
                ],
                axis=1,
            )
            for at in range(cols)
        ]
    )
    if fast:
        piece = lambda mask: lax.dynamic_index_in_dim(stacked, col ^ mask, 0, False)
        shared_sum = piece(0) + flip(piece(1), 1) + flip(piece(2), 2) + flip(piece(3), 3)
    else:
        shared_sum = lax.psum_scatter(
            stacked.reshape(stacked.shape[0] * stacked.shape[1], -1), "col", scatter_dimension=0, tiled=True
        )
    late = jnp.concatenate([shared_sum, late[:, STATES + PAIR :]], axis=1)
    shared_width = pair_width + state_width
    cuts = [shared_width]
    for width in (channels, channels, units * HEAD_SIZE, units * STEP_WIDTH):
        cuts.append(cuts[-1] + width)
    gate_columns, conv_columns, query_columns, step_columns = [
        late[:, low:high] for low, high in zip(cuts[:-1], cuts[1:])
    ]
    grad_in_raise = restore_units(
        [
            gate_columns,
            conv_columns,
            query_columns,
            late[:, :pair_width],
            late[:, pair_width:shared_width],
            step_columns,
        ],
        units,
    )

    returned_out, (grad_down_raise, grad_feed_lower, grad_mix_raise) = take_back(dealt_out, 3)
    returned_grad, (grad_in_lower,) = take_back(dealt_grad, 1)
    return (
        returned_out,
        returned_grad,
        grad_in_lower.T,
        grad_in_raise,
        grad_mix_lower,
        grad_mix_raise,
        grad_feed_lower.T,
        grad_feed_raise,
        grad_down_lower,
        grad_down_raise,
    )


def solution(mesh):
    in_specs = (
        P(("row", "col"), None),
        P(("row", "col"), None),
        P(("row", "col")),
        P("row", None),
        P("row", None),
        P(),
        P("row", "col"),
        P(None, "col"),
        P(None, "col"),
        P(None, "col"),
        P("col", "row"),
        P("row", "col"),
        P("col", "row"),
        P("row", None),
        P("row", "col"),
        P("col", "row"),
        P(None, "row"),
        P("row", None),
        P("row", "col"),
        P("col", "row"),
        P(None, "row"),
    )
    out_specs = (
        P(("row", "col"), None),
        P(("row", "col"), None),
        P(("row", "col"), None),
        P("row", "col"),
        P("col", "row"),
        P(None, ("row", "col")),
        P(("row", "col"), None),
        P("row", "col"),
        P("col", "row"),
        P(None, ("row", "col")),
    )
    return jax.shard_map(local, mesh=mesh, in_specs=in_specs, out_specs=out_specs, check_vma=False)
```

```python
import functools
import math

import jax
import jax.numpy as jnp
from jax import lax
from jax.experimental import pallas as pl
from jax.experimental.pallas import tpu as pltpu
from jax.sharding import PartitionSpec as P

NH = 48
HP = 64
NSTATE = 256
KCONV = 4
QUERY_HEADS = 8
KEY_VALUE_HEADS = 2
HEAD_SIZE = 128
RANK = 16
NADAPT = 8
SSD_BLOCK = 256
DSSM = 3072
UNIT_IN = 1030
UNIT_FF = 512


EPSILON = 1e-05
ROPE_BASE = 10000.0
NEGATIVE = -1e30
FLOAT = jnp.float32
BFLOAT = jnp.bfloat16


def product(left, right):
    return jnp.dot(left, right, preferred_element_type=FLOAT)


def contract_last(left, right):
    return lax.dot_general(left, right, (((1,), (1,)), ((), ())), preferred_element_type=FLOAT)


def contract_first(left, right):
    return lax.dot_general(left, right, (((0,), (0,)), ((), ())), preferred_element_type=FLOAT)


def rms_norm(values, gain):
    return values * lax.rsqrt(jnp.mean(values * values, axis=-1, keepdims=True) + EPSILON) * gain


def sequence_tables(lengths, adapters, sequence_length):
    sequence_count = lengths.shape[0]
    boundary = jnp.cumsum(lengths)
    token_index = jnp.arange(sequence_length, dtype=jnp.int32)
    passed = (token_index[:, None] >= boundary[None, :]).astype(jnp.int32)
    segment = jnp.sum(passed, axis=1)
    segment_start = jnp.sum(passed * lengths[None, :], axis=1)
    position = token_index - segment_start
    member = (segment[:, None] == jnp.arange(sequence_count, dtype=jnp.int32)[None, :]).astype(
        jnp.int32
    )
    chosen = jnp.sum(member * adapters[None, :], axis=1)
    column = jnp.arange(NADAPT * RANK, dtype=jnp.int32) // RANK
    selector = (chosen[:, None] == column[None, :]).astype(FLOAT)
    return (segment, position, selector)


ESTIMATE = 16
SCAN_BYTES = 32 * 1024 * 1024
DENSE_BYTES = 16 * 1024 * 1024
FINISH_BYTES = 32 * 1024 * 1024
LANES = 128


def whole(shape):
    return pl.BlockSpec(shape, lambda *_: (0,) * len(shape))


def estimate(flops, bytes_accessed, transcendentals):
    return pl.CostEstimate(
        flops=flops // ESTIMATE,
        bytes_accessed=bytes_accessed // ESTIMATE,
        transcendentals=transcendentals // ESTIMATE,
    )


def dot(left, right, contract):
    return lax.dot_general(left, right, ((contract[:1], contract[1:]), ((), ())), preferred_element_type=FLOAT)


def parts_of(values, count):
    parts = []
    for _ in range(count):
        part = values.astype(BFLOAT)
        parts.append(part)
        values = values - part.astype(FLOAT)
    return parts


def running_sum(values, triangle, contract):
    width = values.shape[1]
    split = dot(triangle, jnp.concatenate(parts_of(values, 3), axis=1), contract)
    return split[:, :width] + split[:, width : 2 * width] + split[:, 2 * width :]


def head_spread(values, expand):
    return dot(jnp.concatenate(parts_of(values, 2), axis=1), expand, (1, 0))


def head_sum(values, expand):
    high, low = parts_of(values, 2)
    single = expand[:LANES]
    return dot(high, single, (1, 1)) + dot(low, single, (1, 1))


def silu_parts(values):
    gate = 1.0 / (1.0 + jnp.exp(-values))
    return values * gate, gate


def expand_table(channels):
    row = lax.broadcasted_iota(jnp.int32, (2 * LANES, channels), 0) % LANES
    channel = lax.broadcasted_iota(jnp.int32, (2 * LANES, channels), 1) // HP
    return (row == channel).astype(BFLOAT)


def conv_sum(current_ref, before_ref, taps_ref, meta):
    rows = SSD_BLOCK
    current = current_ref[...].astype(FLOAT)
    window = jnp.concatenate([before_ref[...].astype(FLOAT)[8:16], current], axis=0)
    summed = taps_ref[KCONV : KCONV + 1, :] + current * taps_ref[0:1, :]
    for lag in range(1, KCONV):
        shifted = window[8 - lag : 8 - lag + rows]
        summed = summed + jnp.where(meta[:, 1:2] >= lag, shifted, 0.0) * taps_ref[lag : lag + 1, :]
    return summed


def conv_back(summed_grad, later, taps_ref, meta):
    rows = SSD_BLOCK
    window = jnp.concatenate([summed_grad, later[...]], axis=0)
    grad = summed_grad * taps_ref[0:1, :]
    for lag in range(1, KCONV):
        grad = grad + jnp.where(meta[:, 2:3] >= lag, window[lag : lag + rows], 0.0) * taps_ref[lag : lag + 1, :]
    later[...] = summed_grad[:8]
    return grad


def silu_slope(values, gate):
    return gate * (1.0 + values * (1.0 - gate))


def scan_block(
    conv_ref, before_ref, state_ref, state_before_ref, step_ref, meta_ref, segment_ref, taps_ref, state_taps_ref, head_ref,
    turned_over,
):
    rows = SSD_BLOCK
    channels = conv_ref.shape[1]
    meta = meta_ref[...]
    summed = conv_sum(conv_ref, before_ref, taps_ref, meta)
    activated, conv_gate = silu_parts(summed)
    wide_inputs = activated.astype(BFLOAT).astype(FLOAT)
    state_summed = conv_sum(state_ref, state_before_ref, state_taps_ref, meta)
    state_values, state_gate = silu_parts(state_summed)
    write = state_values[:, :NSTATE].astype(BFLOAT)
    read = state_values[:, NSTATE:].astype(BFLOAT)
    raw = step_ref[...].astype(FLOAT) + head_ref[0:1, :]
    steps = jnp.maximum(raw, 0.0) + jnp.log1p(jnp.exp(-jnp.abs(raw)))
    row = lax.broadcasted_iota(jnp.int32, (rows, rows), 0)
    column = lax.broadcasted_iota(jnp.int32, (rows, rows), 1)
    triangle = (row >= column).astype(BFLOAT)
    total = running_sum(steps * head_ref[1:2, :], triangle, (1, 0))
    entered = jnp.exp(total) * meta[:, 3:4]
    leaving = jnp.exp(total[rows - 1 : rows] - total) * meta[:, 4:5]
    expand = expand_table(channels)
    spread = head_spread(jnp.concatenate([steps, entered, leaving * steps], axis=0), expand)
    ordered = row <= column if turned_over else row >= column
    blocked = jnp.where(ordered & (meta[:, 0:1] == segment_ref[0:1, :]), 0.0, NEGATIVE)
    return dict(
        summed=summed,
        conv_gate=conv_gate,
        state_summed=state_summed,
        state_gate=state_gate,
        write=write,
        read=read,
        wide_inputs=wide_inputs,
        raw=raw,
        steps=steps,
        triangle=triangle,
        total=total,
        total_rows=total.T,
        leaving=leaving,
        expand=expand,
        steps_wide=spread[:rows],
        entered_wide=spread[rows : 2 * rows],
        tail_wide=spread[2 * rows :],
        stepped=(wide_inputs * spread[:rows]).astype(BFLOAT),
        tailed=(wide_inputs * spread[2 * rows :]).astype(BFLOAT),
        blocked=blocked,
        crossing=dot(write, read, (1, 1)) if turned_over else dot(read, write, (1, 1)),
    )


def decay_of(block, head):
    difference = block["total"][:, head : head + 1] - block["total_rows"][head : head + 1, :]
    return jnp.exp(difference + block["blocked"])


def turned_decay_of(block, head):
    difference = block["total_rows"][head : head + 1, :] - block["total"][:, head : head + 1]
    return jnp.exp(difference + block["blocked"])


def scan_forward_kernel(
    gate_ref, conv_ref, before_ref, state_ref, state_before_ref, step_ref, meta_ref, segment_ref, taps_ref,
    state_taps_ref, head_ref, skip_ref, mixed_ref, out_ref, scanned_ref, states_ref, state,
):
    del mixed_ref

    @pl.when(pl.program_id(0) == 0)
    def _():
        state[...] = jnp.zeros_like(state)

    block = scan_block(
        conv_ref, before_ref, state_ref, state_before_ref, step_ref, meta_ref, segment_ref, taps_ref, state_taps_ref,
        head_ref, False,
    )
    heads = conv_ref.shape[1] // HP
    carried = state[...].astype(BFLOAT)
    states_ref[0] = carried
    across = dot(block["read"], carried, (1, 0)) * block["entered_wide"]
    within = []
    for head in range(heads):
        weights = (block["crossing"] * decay_of(block, head)).astype(BFLOAT)
        within.append(dot(weights, block["stepped"][:, head * HP : (head + 1) * HP], (1, 0)))
    scanned = across + jnp.concatenate(within, axis=1)
    scanned_ref[...] = scanned
    gated, _ = silu_parts(gate_ref[...].astype(FLOAT))
    out_ref[...] = ((scanned + skip_ref[0:1, :] * block["wide_inputs"]) * gated).astype(BFLOAT)
    state[...] = state[...] * block["entered_wide"][SSD_BLOCK - 1 : SSD_BLOCK, :] + dot(
        block["write"], block["tailed"], (0, 0)
    )


def scan_backward_kernel(
    gate_ref, conv_ref, before_ref, state_ref, state_before_ref, step_ref, meta_ref, segment_ref, taps_ref,
    state_taps_ref, head_ref, skip_ref, scanned_ref, states_ref, grad_ref, query_grad_ref, shared_grad_ref, *rest,
):
    out_ref, *running = rest[-4:]
    state_grad, later, state_later = running

    @pl.when(pl.program_id(0) == 0)
    def _():
        for at, ref in enumerate(running):
            ref[...] = rest[1 + at][...] if len(rest) > 4 else jnp.zeros_like(ref)

    block = scan_block(
        conv_ref, before_ref, state_ref, state_before_ref, step_ref, meta_ref, segment_ref, taps_ref, state_taps_ref,
        head_ref, True,
    )
    rows = SSD_BLOCK
    channels = conv_ref.shape[1]
    heads = channels // HP
    meta = meta_ref[...]
    read, write = block["read"], block["write"]
    inputs = block["wide_inputs"]
    scanned = scanned_ref[...]
    skip = skip_ref[0:1, :]
    gate_values = gate_ref[...].astype(FLOAT)
    gated, gate = silu_parts(gate_values)
    grad = grad_ref[...].astype(FLOAT)
    gate_grad = grad * (scanned + skip * inputs) * silu_slope(gate_values, gate)
    out_grad = grad * gated
    inputs_grad = skip * out_grad
    rounded = out_grad.astype(BFLOAT)
    wide_rounded = rounded.astype(FLOAT)
    carried = states_ref[0]
    after = state_grad[...]
    after_rounded = after.astype(BFLOAT)

    from_state = dot(write, after_rounded, (1, 0))
    entering = (wide_rounded * block["entered_wide"]).astype(BFLOAT)
    write_grad = dot(block["tailed"], after_rounded, (1, 1))
    read_grad = dot(entering, carried, (1, 1))
    last_entered = block["entered_wide"][rows - 1 : rows, :]
    through = jnp.sum(after * carried.astype(FLOAT), axis=0, keepdims=True) * last_entered
    state_grad[...] = after * last_entered + dot(read, entering, (0, 0))

    crossing_grad = jnp.zeros((rows, rows), FLOAT)
    pulled = []
    for head in range(heads):
        span = slice(head * HP, (head + 1) * HP)
        decay = turned_decay_of(block, head)
        weights = (block["crossing"] * decay).astype(BFLOAT)
        pulled.append(dot(weights, rounded[:, span], (1, 0)))
        crossing_grad = crossing_grad + dot(block["stepped"][:, span], rounded[:, span], (1, 1)) * decay
    pulled = jnp.concatenate(pulled, axis=1)
    crossing_rounded = crossing_grad.astype(BFLOAT)
    read_grad = read_grad + dot(crossing_rounded, write, (0, 0))
    write_grad = write_grad + dot(crossing_rounded, read, (1, 0))

    inputs_grad = inputs_grad + block["steps_wide"] * pulled + block["tail_wide"] * from_state
    sums = head_sum(
        jnp.concatenate(
            [
                wide_rounded * scanned - block["stepped"].astype(FLOAT) * pulled,
                inputs * pulled,
                inputs * from_state,
                jnp.broadcast_to(through, (8, channels)),
            ],
            axis=0,
        ),
        block["expand"],
    )
    leaving_grad = sums[2 * rows : 3 * rows] * block["leaving"]
    leaving_total = leaving_grad * block["steps"]
    last = sums[3 * rows : 3 * rows + 1] + jnp.sum(leaving_total, axis=0, keepdims=True)
    total_grad = sums[:rows] - leaving_total
    total_grad = total_grad + jnp.where(
        lax.broadcasted_iota(jnp.int32, total_grad.shape, 0) == rows - 1, last, 0.0
    )
    decay_grad = running_sum(total_grad, block["triangle"], (0, 0))
    steps_grad = sums[rows : 2 * rows] + leaving_grad + decay_grad * head_ref[1:2, :]
    raw_grad = steps_grad / (1.0 + jnp.exp(-block["raw"]))
    raw_grad = jnp.where(lax.broadcasted_iota(jnp.int32, raw_grad.shape, 1) < heads, raw_grad, 0.0)

    state_slope = silu_slope(block["state_summed"], block["state_gate"])
    state_pre = conv_back(
        jnp.concatenate([write_grad, read_grad], axis=1) * state_slope, state_later, state_taps_ref, meta
    )
    conv_pre = conv_back(inputs_grad * silu_slope(block["summed"], block["conv_gate"]), later, taps_ref, meta)
    out_ref[:, : 2 * NSTATE] = state_pre.astype(BFLOAT)
    start = 2 * NSTATE + 2 * HEAD_SIZE
    end = out_ref.shape[1] - LANES
    out_ref[:, 2 * NSTATE : start] = shared_grad_ref[...]
    out_ref[:, start + 2 * channels : end] = query_grad_ref[...]
    out_ref[:, start : start + channels] = gate_grad.astype(BFLOAT)
    out_ref[:, start + channels : start + 2 * channels] = conv_pre.astype(BFLOAT)
    out_ref[:, end:] = raw_grad.astype(BFLOAT)


STATES = 2 * NSTATE
PAIR = 2 * HEAD_SIZE


def scan_specs(channels, order):
    half = SSD_BLOCK // 16
    before = lambda i: jnp.maximum(order(i) * half - 1, 0)
    gate_at = (STATES + PAIR) // channels
    step_at = (STATES + PAIR + 2 * channels + channels * QUERY_HEADS // DSSM * HEAD_SIZE) // LANES
    return [
        pl.BlockSpec((SSD_BLOCK, channels), lambda i: (order(i), gate_at)),
        pl.BlockSpec((SSD_BLOCK, channels), lambda i: (order(i), gate_at + 1)),
        pl.BlockSpec((16, channels), lambda i: (before(i), gate_at + 1)),
        pl.BlockSpec((SSD_BLOCK, STATES), lambda i: (order(i), 0)),
        pl.BlockSpec((16, STATES), lambda i: (before(i), 0)),
        pl.BlockSpec((SSD_BLOCK, LANES), lambda i: (order(i), step_at)),
        pl.BlockSpec((SSD_BLOCK, LANES), lambda i: (order(i), 0)),
        pl.BlockSpec((8, SSD_BLOCK), lambda i: (0, order(i))),
        whole((8, channels)),
        whole((8, STATES)),
        whole((8, LANES)),
        whole((8, channels)),
    ]


def scan_operands(projected, tables):
    return [projected] * 6 + [
        tables[name] for name in ("meta", "segment_row", "taps", "state_taps", "head", "skip")
    ]


def scan_cost(tokens, channels, factor):
    heads = channels // HP
    return estimate(
        flops=factor * 2 * tokens * SSD_BLOCK * (3 * channels + NSTATE),
        bytes_accessed=factor * tokens * channels * 12,
        transcendentals=tokens * SSD_BLOCK * heads,
    )


def scan_forward(projected, tables, mixed):
    tokens = projected.shape[0]
    channels = tables["taps"].shape[1]
    blocks = tokens // SSD_BLOCK
    return pl.pallas_call(
        scan_forward_kernel,
        grid=(blocks,),
        in_specs=scan_specs(channels, lambda i: i) + [pl.BlockSpec(memory_space=pl.ANY)],
        out_specs=[
            pl.BlockSpec((SSD_BLOCK, channels), lambda i: (i, 0)),
            pl.BlockSpec((SSD_BLOCK, channels), lambda i: (i, 0)),
            pl.BlockSpec((1, NSTATE, channels), lambda i: (i, 0, 0)),
        ],
        out_shape=[
            jax.ShapeDtypeStruct(mixed.shape, BFLOAT),
            jax.ShapeDtypeStruct((tokens, channels), FLOAT),
            jax.ShapeDtypeStruct((blocks, NSTATE, channels), BFLOAT),
        ],
        scratch_shapes=[pltpu.VMEM((NSTATE, channels), FLOAT)],
        input_output_aliases={12: 0},
        compiler_params=pltpu.CompilerParams(vmem_limit_bytes=SCAN_BYTES),
        cost_estimate=scan_cost(tokens, channels, 1),
        name="scan_forward",
    )(*scan_operands(projected, tables), mixed)


def scan_backward(projected, tables, scanned, carried, mixed_grad, attended_grads, part, parts, before):
    tokens, width = projected.shape
    channels = tables["taps"].shape[1]
    blocks = tokens // SSD_BLOCK
    last = blocks - 1 - part * (blocks // parts)
    back = lambda i: (last - i, 0)
    running = [(NSTATE, channels), (8, channels), (8, STATES)]
    query_grad, shared_grad = attended_grads
    operands = [*scan_operands(projected, tables), scanned, carried, mixed_grad, query_grad, shared_grad]
    in_specs = scan_specs(channels, lambda i: last - i) + [
        pl.BlockSpec((SSD_BLOCK, channels), back),
        pl.BlockSpec((1, NSTATE, channels), lambda i: (last - i, 0, 0)),
        pl.BlockSpec((SSD_BLOCK, channels), back),
        pl.BlockSpec((SSD_BLOCK, query_grad.shape[1]), back),
        pl.BlockSpec((SSD_BLOCK, PAIR), back),
    ]
    aliases = {}
    if before is not None:
        aliases = {len(operands): 0}
        operands += list(before)
        in_specs += [pl.BlockSpec(memory_space=pl.ANY), *[whole(shape) for shape in running]]
    return pl.pallas_call(
        scan_backward_kernel,
        grid=(blocks // parts,),
        in_specs=in_specs,
        out_specs=[pl.BlockSpec((SSD_BLOCK, width), back), *[whole(shape) for shape in running]],
        out_shape=[
            jax.ShapeDtypeStruct((tokens, width), BFLOAT),
            *[jax.ShapeDtypeStruct(shape, FLOAT) for shape in running],
        ],
        input_output_aliases=aliases,
        compiler_params=pltpu.CompilerParams(vmem_limit_bytes=SCAN_BYTES),
        cost_estimate=scan_cost(tokens, channels, 2),
        name="scan_backward",
    )(*operands)


def turned(values, cosine, sine):
    return (values * cosine + pltpu.roll(values, HEAD_SIZE // 2, 1) * sine).astype(BFLOAT)


def turned_back(values, cosine, sine):
    return values * cosine + pltpu.roll(values * sine, HEAD_SIZE // 2, 1)


ATT_ROWS = 256


def attention_mask(meta_ref, segment_ref, start, extent):
    row = start + lax.broadcasted_iota(jnp.int32, (ATT_ROWS, extent), 0)
    column = lax.broadcasted_iota(jnp.int32, (ATT_ROWS, extent), 1)
    return (row >= column) & (meta_ref[start : start + ATT_ROWS, 0:1] == segment_ref[0:1, :extent])


def probabilities(query, keys, allowed):
    score = dot(query, keys, (1, 1)) * (1.0 / math.sqrt(HEAD_SIZE))
    score = jnp.where(allowed, score, NEGATIVE)
    exponent = jnp.exp(score - jnp.max(score, axis=1, keepdims=True))
    return exponent / jnp.sum(exponent, axis=1, keepdims=True)


def attention_forward_kernel(query_ref, key_ref, value_ref, cosine_ref, sine_ref, meta_ref, segment_ref, out_ref, keys):
    tokens = key_ref.shape[0]
    keys[...] = turned(key_ref[...].astype(FLOAT), cosine_ref[...], sine_ref[...])
    for start in range(0, tokens, ATT_ROWS):
        extent = start + ATT_ROWS
        here = slice(start, extent)
        allowed = attention_mask(meta_ref, segment_ref, start, extent)
        for unit in range(query_ref.shape[1] // HEAD_SIZE):
            span = slice(unit * HEAD_SIZE, (unit + 1) * HEAD_SIZE)
            query = turned(query_ref[here, span].astype(FLOAT), cosine_ref[here], sine_ref[here])
            weights = probabilities(query, keys[:extent], allowed).astype(BFLOAT)
            out_ref[here, span] = dot(weights, value_ref[:extent], (1, 0)).astype(BFLOAT)


def attention_backward_kernel(
    query_ref, key_ref, value_ref, cosine_ref, sine_ref, meta_ref, segment_ref, grad_ref,
    query_grad_ref, shared_grad_ref, keys, key_sum, value_sum,
):
    tokens = key_ref.shape[0]
    scale = 1.0 / math.sqrt(HEAD_SIZE)
    keys[...] = turned(key_ref[...].astype(FLOAT), cosine_ref[...], sine_ref[...])
    key_sum[...] = jnp.zeros_like(key_sum)
    value_sum[...] = jnp.zeros_like(value_sum)
    for start in range(0, tokens, ATT_ROWS):
        extent = start + ATT_ROWS
        here = slice(start, extent)
        allowed = attention_mask(meta_ref, segment_ref, start, extent)
        for unit in range(query_ref.shape[1] // HEAD_SIZE):
            span = slice(unit * HEAD_SIZE, (unit + 1) * HEAD_SIZE)
            query = turned(query_ref[here, span].astype(FLOAT), cosine_ref[here], sine_ref[here])
            weights = probabilities(query, keys[:extent], allowed)
            grad = grad_ref[here, span]
            weights_grad = dot(grad, value_ref[:extent], (1, 1))
            value_sum[:extent] += dot(weights.astype(BFLOAT), grad, (0, 0))
            mean_grad = jnp.sum(weights * weights_grad, axis=1, keepdims=True)
            score_grad = (weights * (weights_grad - mean_grad) * scale).astype(BFLOAT)
            query_grad = dot(score_grad, keys[:extent], (1, 0))
            key_sum[:extent] += dot(score_grad, query, (0, 0))
            query_grad_ref[here, span] = turned_back(query_grad, cosine_ref[here], sine_ref[here]).astype(BFLOAT)
    shared_grad_ref[:, :HEAD_SIZE] = turned_back(key_sum[...], cosine_ref[...], sine_ref[...]).astype(BFLOAT)
    shared_grad_ref[:, HEAD_SIZE:] = value_sum[...].astype(BFLOAT)


def attention_cost(tokens, width, factor):
    return estimate(
        flops=factor * 2 * tokens * tokens * width,
        bytes_accessed=factor * tokens * width * 8,
        transcendentals=tokens * tokens * width // (2 * HEAD_SIZE),
    )


def attention_specs(tokens, channels):
    width = channels * QUERY_HEADS // DSSM * HEAD_SIZE
    narrow = whole((tokens, HEAD_SIZE))
    return [
        pl.BlockSpec((tokens, width), lambda *_: (0, (STATES + PAIR + 2 * channels) // width)),
        pl.BlockSpec((tokens, HEAD_SIZE), lambda *_: (0, STATES // HEAD_SIZE)),
        pl.BlockSpec((tokens, HEAD_SIZE), lambda *_: (0, STATES // HEAD_SIZE + 1)),
        narrow,
        narrow,
        whole((tokens, LANES)),
        whole((8, tokens)),
    ]


def attention_operands(projected, tables):
    return [projected] * 3 + [tables[name] for name in ("cosine", "sine", "meta", "segment_row")]


def attention_forward(projected, tables):
    tokens = projected.shape[0]
    channels = tables["taps"].shape[1]
    width = channels * QUERY_HEADS // DSSM * HEAD_SIZE
    return pl.pallas_call(
        attention_forward_kernel,
        grid=(1,),
        in_specs=attention_specs(tokens, channels),
        out_specs=pl.BlockSpec((tokens, width), lambda *_: (0, channels // width)),
        out_shape=jax.ShapeDtypeStruct((tokens, channels + width), BFLOAT),
        scratch_shapes=[pltpu.VMEM((tokens, HEAD_SIZE), BFLOAT)],
        compiler_params=pltpu.CompilerParams(vmem_limit_bytes=SCAN_BYTES),
        cost_estimate=attention_cost(tokens, width, 1),
        name="attention_forward",
    )(*attention_operands(projected, tables))


def attention_backward(projected, tables, mixed_grad):
    tokens = projected.shape[0]
    channels = tables["taps"].shape[1]
    width = channels * QUERY_HEADS // DSSM * HEAD_SIZE
    return pl.pallas_call(
        attention_backward_kernel,
        grid=(1,),
        in_specs=attention_specs(tokens, channels)
        + [pl.BlockSpec((tokens, width), lambda *_: (0, channels // width))],
        out_specs=[whole((tokens, width)), whole((tokens, PAIR))],
        out_shape=[jax.ShapeDtypeStruct((tokens, width), BFLOAT), jax.ShapeDtypeStruct((tokens, PAIR), BFLOAT)],
        scratch_shapes=[
            pltpu.VMEM((tokens, HEAD_SIZE), BFLOAT),
            pltpu.VMEM((tokens, HEAD_SIZE), FLOAT),
            pltpu.VMEM((tokens, HEAD_SIZE), FLOAT),
        ],
        compiler_params=pltpu.CompilerParams(vmem_limit_bytes=SCAN_BYTES),
        cost_estimate=attention_cost(tokens, width, 3),
        name="attention_backward",
    )(*attention_operands(projected, tables), mixed_grad)


def mixer_tables(lengths, segment, position, conv_values, conv_states, scan_params):
    tokens = segment.shape[0]
    block = jnp.arange(tokens, dtype=jnp.int32) // SSD_BLOCK
    previous = jnp.concatenate([jnp.full((1,), -1, jnp.int32), segment[:-1]])
    first_previous = jnp.repeat(previous[::SSD_BLOCK], SSD_BLOCK)
    last_segment = jnp.repeat(segment[SSD_BLOCK - 1 :: SSD_BLOCK], SSD_BLOCK)
    length = jnp.sum(
        jnp.where(segment[:, None] == jnp.arange(lengths.shape[0], dtype=jnp.int32)[None, :], lengths[None, :], 0),
        axis=1,
    )
    columns = [
        segment,
        position,
        length - 1 - position,
        segment == first_previous,
        segment == last_segment,
    ]
    meta = jnp.stack([column.astype(FLOAT) for column in columns], axis=1)
    half_width = HEAD_SIZE // 2
    frequency = ROPE_BASE ** (-2.0 * jnp.arange(half_width, dtype=FLOAT) / HEAD_SIZE)
    angle = position.astype(FLOAT)[:, None] * frequency[None, :]
    cosine, sine = jnp.cos(angle), jnp.sin(angle)
    heads = scan_params.shape[1]
    head = jnp.stack([scan_params[0], -jnp.exp(scan_params[1]), scan_params[2]])
    return dict(
        meta=jnp.pad(meta, ((0, 0), (0, LANES - meta.shape[1]))),
        segment_row=jnp.broadcast_to(segment.astype(FLOAT)[None, :], (8, tokens)),
        taps=jnp.pad(conv_values.astype(FLOAT), ((0, 3), (0, 0))),
        state_taps=jnp.pad(conv_states.astype(FLOAT), ((0, 3), (0, 0))),
        head=jnp.pad(head, ((0, 5), (0, LANES - heads))),
        skip=jnp.broadcast_to(jnp.repeat(scan_params[2], HP)[None, :], (8, heads * HP)),
        cosine=jnp.concatenate([cosine, cosine], axis=1),
        sine=jnp.concatenate([-sine, sine], axis=1),
    )


HALVES = 2
DENSE_TILE = 1024


def matrix_rows(values):
    return values.reshape(values.shape[0] * values.shape[1], values.shape[2])


def cut_tiles(width, tile):
    return [(low, min(low + tile, width)) for low in range(0, width, tile)]


def spread_kernel(mask, count, left_ref, right_ref, chosen_ref, *rest):
    weights, (out_ref, narrow_ref, out_tile, narrow, sems) = rest[:count], rest[-5:]
    rows = left_ref.shape[0]
    shards = weights[0].shape[0]
    depth = shards // HALVES
    start = pl.multiple_of((lax.axis_index("col") ^ mask) * rows, rows)
    here = pl.ds(start, rows)

    def through(ref, low, high):
        return dot(left_ref[...], matrix_rows(ref[:depth, :rows, low:high]), (1, 0)) + dot(
            right_ref[...], matrix_rows(ref[depth:, :rows, low:high]), (1, 0)
        )

    lower = weights[-1].shape[2] - LANES
    narrow[...] = (chosen_ref[here, :] * through(weights[-1], lower, lower + LANES)).astype(BFLOAT)
    copies = [pltpu.make_async_copy(narrow, narrow_ref.at[here, :], sems.at[0])]
    copies[0].start()
    column = 0
    for ref in weights:
        for low, high in cut_tiles(ref.shape[2] - (LANES if ref is weights[-1] else 0), DENSE_TILE):
            span = slice(column, column + high - low)
            column += high - low
            raised = matrix_rows(ref[:, rows : rows + NADAPT * RANK // shards, low:high])
            out_tile[:, span] = (through(ref, low, high) + dot(narrow[...], raised, (1, 0))).astype(BFLOAT)
            copies.append(
                pltpu.make_async_copy(out_tile.at[:, span], out_ref.at[here, span], sems.at[len(copies)])
            )
            copies[-1].start()
    for copy in copies:
        copy.wait()


def weights_width(gathered):
    return sum(part.shape[2] for part in gathered) - LANES


def spread_block(mask, halves, gathered, selector, held):
    rows, half = halves[0].shape
    width = weights_width(gathered)
    total = selector.shape[0]
    fast, free = pl.BlockSpec(memory_space=pltpu.VMEM), pl.BlockSpec(memory_space=pl.ANY)
    operands = [*halves, selector, *gathered]
    in_specs = [fast] * len(operands)
    aliases = {}
    if held is not None:
        aliases = {len(operands): 0, len(operands) + 1: 1}
        operands += list(held)
        in_specs += [free] * 2
    copies = 1 + sum(-(-part.shape[2] // DENSE_TILE) for part in gathered)
    return pl.pallas_call(
        functools.partial(spread_kernel, mask, len(gathered)),
        in_specs=in_specs,
        out_specs=[free] * 2,
        out_shape=[
            jax.ShapeDtypeStruct((total, width), BFLOAT),
            jax.ShapeDtypeStruct((total, LANES), BFLOAT),
        ],
        scratch_shapes=[
            pltpu.VMEM((rows, width), BFLOAT),
            pltpu.VMEM((rows, LANES), BFLOAT),
            pltpu.SemaphoreType.DMA((copies,)),
        ],
        input_output_aliases=aliases,
        compiler_params=pltpu.CompilerParams(vmem_limit_bytes=DENSE_BYTES),
        cost_estimate=estimate(
            flops=4 * rows * half * (width + LANES), bytes_accessed=2 * rows * (2 * half + width), transcendentals=0
        ),
        name="spread_block",
    )(*operands)


def collect_kernel(masks, count, values_ref, *refs):
    weights, outs = refs[:count], refs[count:]
    rows = values_ref.shape[0] // 4
    shards = weights[0].shape[0]
    half = shards // HALVES * rows
    width = values_ref.shape[1]
    starts, column = [], 0
    for ref in weights:
        high = min(column + ref.shape[2], width)
        starts.append((column, high))
        column = high
    for at, mask in enumerate(masks):
        here = pl.ds(pl.multiple_of((lax.axis_index("col") ^ mask) * rows, rows), rows)
        first, second = outs[2 * at], outs[2 * at + 1]

        def through(cut):
            total = None
            for (low, high), ref in zip(starts, weights):
                part = dot(values_ref[here, low:high], cut(ref, high - low), (1, 1))
                total = part if total is None else total + part
            return total

        for shard in range(shards):
            out_ref = first if shard < shards // HALVES else second
            column = shard * rows % half
            out_ref[:, column : column + rows] = through(lambda ref, wide: ref[shard, :rows, :wide]).astype(
                out_ref.dtype
            )
        first[:, half:] = through(
            lambda ref, wide: matrix_rows(ref[:, rows : rows + NADAPT * RANK // shards, :wide])
        ).astype(first.dtype)


def collect_blocks(masks, values, gathered, types):
    rows = values.shape[0] // 4
    half = gathered[0].shape[0] // HALVES * rows
    fast = pl.BlockSpec(memory_space=pltpu.VMEM)
    out_shape = []
    for pair in types:
        out_shape.append(jax.ShapeDtypeStruct((rows, half + LANES), pair[0]))
        out_shape.append(jax.ShapeDtypeStruct((rows, half), pair[1]))
    outs = pl.pallas_call(
        functools.partial(collect_kernel, masks, len(gathered)),
        in_specs=[fast] * (1 + len(gathered)),
        out_specs=[fast] * len(out_shape),
        out_shape=out_shape,
        compiler_params=pltpu.CompilerParams(vmem_limit_bytes=DENSE_BYTES),
        cost_estimate=estimate(
            flops=4 * len(masks) * rows * half * values.shape[1],
            bytes_accessed=2 * len(masks) * rows * (values.shape[1] + 4 * half),
            transcendentals=0,
        ),
        name="collect_blocks",
    )(values, *gathered)
    return [tuple(outs[2 * at : 2 * at + 2]) for at in range(len(masks))]


def root_mean(values):
    return lax.rsqrt(jnp.mean(values * values, axis=1, keepdims=True) + EPSILON)


def packed_grad(narrow, values, choose):
    half = LANES // 2
    chosen = dot(narrow, choose, (1, 0)).astype(BFLOAT)
    grad = dot(chosen, values, (0, 0))
    low = lax.broadcasted_iota(jnp.int32, (8, LANES), 1) < half
    devices = []
    for start in range(0, grad.shape[1], LANES):
        own = grad[:, start : start + LANES]
        turned_own = pltpu.roll(own, half, 1)
        for first, second in ((own, turned_own), (turned_own, own)):
            devices.append(
                jnp.concatenate(
                    [jnp.where(low, first[at : at + 8], second[at + 8 : at + 16]) for at in (0, 16)], axis=1
                )
            )
    return jnp.concatenate(devices, axis=0).astype(BFLOAT)


def finish_kernel(kind, first_own, first_near, first_far, second_own, second_near, second_far, lower_ref, chosen_ref,
                  *refs):
    half = second_own.shape[1]
    model = HALVES * half
    wide = lambda ref: ref[...].astype(FLOAT)
    first = wide(first_own) + wide(first_near) + wide(first_far)
    second = wide(second_own) + wide(second_near) + wide(second_far)
    inner = (chosen_ref[...] * first[:, half:]).astype(BFLOAT)
    summed = jnp.concatenate([first[:, :half], second], axis=1) + dot(
        inner, matrix_rows(lower_ref[...]), (1, 1)
    )
    if kind == "output":
        residual_ref, place_ref, choose_ref, branch_ref, early_ref, out_ref = refs
        result = (residual_ref[...] + summed).astype(BFLOAT)
        out_ref[:, :model] = dot(place_ref[...], result, (0, 0)).astype(BFLOAT)
        out_ref[:, model : model + 2 * LANES] = packed_grad(inner, branch_ref[...], choose_ref[...])
        out_ref[:, model + 2 * LANES :] = early_ref[...]
        return
    if kind == "forward":
        residual_ref, gain_ref, out_ref, inner_ref, left_ref, right_ref = refs
        hidden = residual_ref[...] + summed
        normed = (hidden * root_mean(hidden) * gain_ref[0:1, :]).astype(BFLOAT)
    else:
        values_ref, upstream_ref, gain_ref, choose_ref, normed_left, normed_right = refs[:6]
        values = values_ref[...]
        scale = root_mean(values)
        weighted = summed * gain_ref[0:1, :]
        mean = jnp.mean(weighted * values, axis=1, keepdims=True)
        hidden = upstream_ref[...].astype(FLOAT) + scale * weighted - values * (scale * scale * scale * mean)
        normed = hidden.astype(BFLOAT)
        packed = packed_grad(
            inner, jnp.concatenate([normed_left[...], normed_right[...]], axis=1), choose_ref[...]
        )
        if kind == "input":
            place_ref, out_ref = refs[6:]
            out_ref[:, :model] = dot(place_ref[...], normed, (0, 0)).astype(BFLOAT)
            out_ref[:, model:] = packed
            return
        given_ref, out_ref, inner_ref, left_ref, right_ref, packed_ref = refs[6:]
        packed_ref[:, : 2 * LANES] = packed
        packed_ref[:, 2 * LANES :] = packed_grad(given_ref[...], normed, choose_ref[...])
    out_ref[...] = hidden
    inner_ref[...] = inner
    left_ref[...] = normed[:, :half]
    right_ref[...] = normed[:, half:]


def finish(kind, parts, gathered, own_selector, *operands):
    rows = own_selector.shape[0]
    half = parts[3].shape[1]
    shards = gathered[-1].shape[0]
    model = HALVES * half
    lower = gathered[-1][:, : model // shards, -LANES:]
    shaped = jax.ShapeDtypeStruct
    if kind in ("output", "input"):
        out_shape = shaped((rows, model + 2 * LANES * (3 if kind == "output" else 1)), BFLOAT)
        out_specs = whole(out_shape.shape)
    else:
        out_shape = [shaped((rows, model), FLOAT), shaped((rows, LANES), BFLOAT)]
        out_shape += [shaped((rows, half), BFLOAT)] * 2
        out_shape += [shaped((rows, 4 * LANES), BFLOAT)] * (kind == "backward")
        out_specs = [whole(shape.shape) for shape in out_shape]
    given = [*parts, lower, own_selector, *operands]
    return pl.pallas_call(
        functools.partial(finish_kernel, kind),
        grid=(1,),
        in_specs=[whole(value.shape) for value in given],
        out_specs=out_specs,
        out_shape=out_shape,
        compiler_params=pltpu.CompilerParams(vmem_limit_bytes=FINISH_BYTES),
        cost_estimate=estimate(
            flops=2 * rows * model * LANES, bytes_accessed=rows * model * 20, transcendentals=0
        ),
        name="finish_" + kind,
    )(*given)


def onward_kernel(first_kept, first_part, second_kept, second_part, first_ref, second_ref):
    first_ref[...] = (first_kept[...] + first_part[...].astype(FLOAT)).astype(BFLOAT)
    second_ref[...] = (second_kept[...] + second_part[...].astype(FLOAT)).astype(BFLOAT)


def sum_onward(first_kept, first_part, second_kept, second_part):
    return pl.pallas_call(
        onward_kernel,
        in_specs=[pl.BlockSpec(memory_space=pltpu.VMEM)] * 4,
        out_specs=[pl.BlockSpec(memory_space=pltpu.VMEM)] * 2,
        out_shape=[jax.ShapeDtypeStruct(part.shape, BFLOAT) for part in (first_part, second_part)],
        compiler_params=pltpu.CompilerParams(vmem_limit_bytes=DENSE_BYTES),
        name="sum_onward",
    )(first_kept, first_part, second_kept, second_part)


def send_kernel(target_column, target_row, tokens_ref, adapter_ref, sent_ref, matrix_ref):
    rows = tokens_ref.shape[0]
    model = tokens_ref.shape[1]
    peer = adapter_ref.shape[0]
    column, row = target_column[:, 0:1], target_row[0:1, :]
    earlier = lax.broadcasted_iota(jnp.int32, (rows, rows), 0) < lax.broadcasted_iota(jnp.int32, (rows, rows), 1)
    same = jnp.where((column // rows == row // rows) & earlier, 1.0, 0.0)
    place = (row // rows) * peer + jnp.sum(same, axis=0, keepdims=True).astype(jnp.int32)
    matrix = (lax.broadcasted_iota(jnp.int32, (rows, rows), 0) == place).astype(BFLOAT)
    matrix_ref[...] = matrix
    sent_ref[:, :model] = dot(matrix, tokens_ref[...], (1, 0)).astype(BFLOAT)
    lane = lax.broadcasted_iota(jnp.int32, (rows, LANES), 1)
    slots = jnp.where(lane == 0, column % rows, 0).astype(FLOAT).astype(BFLOAT)
    notes = dot(matrix, slots, (1, 0))
    sent_ref[:, model:] = jnp.where(lane == 0, notes, adapter_ref[0:1, :]).astype(BFLOAT)


def send_tokens(target, tokens, adapters, peer):
    rows, model = tokens.shape
    notes = jnp.pad(adapters.astype(FLOAT), (1, LANES - 1 - adapters.shape[0]))
    return pl.pallas_call(
        send_kernel,
        in_specs=[pl.BlockSpec(memory_space=pltpu.VMEM)] * 4,
        out_specs=[pl.BlockSpec(memory_space=pltpu.VMEM)] * 2,
        out_shape=[
            jax.ShapeDtypeStruct((rows, model + LANES), BFLOAT),
            jax.ShapeDtypeStruct((rows, rows), BFLOAT),
        ],
        compiler_params=pltpu.CompilerParams(vmem_limit_bytes=DENSE_BYTES),
        name="send_tokens",
    )(
        jnp.broadcast_to(target[:, None], (rows, LANES)),
        jnp.broadcast_to(target[None, :], (8, rows)),
        tokens,
        jnp.broadcast_to(notes[None, :], (peer, LANES)),
    )


def arrive_kernel(arrived_ref, gain_ref, own_ref, matrix_ref, left_ref, right_ref):
    rows, model = own_ref.shape
    slots = arrived_ref[:, model:].astype(FLOAT).T[0:1, :]
    row = lax.broadcasted_iota(jnp.int32, (rows, rows), 0).astype(FLOAT)
    matrix = (row == slots).astype(BFLOAT)
    matrix_ref[...] = matrix
    own = dot(matrix, arrived_ref[:, :model], (1, 0))
    own_ref[...] = own
    normed = (own * root_mean(own) * gain_ref[0:1, :]).astype(BFLOAT)
    left_ref[...] = normed[:, : model // HALVES]
    right_ref[...] = normed[:, model // HALVES :]


def arrive_tokens(arrived, gain):
    rows, model = arrived.shape[0], arrived.shape[1] - LANES
    return pl.pallas_call(
        arrive_kernel,
        in_specs=[pl.BlockSpec(memory_space=pltpu.VMEM)] * 2,
        out_specs=[pl.BlockSpec(memory_space=pltpu.VMEM)] * 4,
        out_shape=[
            jax.ShapeDtypeStruct((rows, model), FLOAT),
            jax.ShapeDtypeStruct((rows, rows), BFLOAT),
            jax.ShapeDtypeStruct((rows, model // HALVES), BFLOAT),
            jax.ShapeDtypeStruct((rows, model // HALVES), BFLOAT),
        ],
        compiler_params=pltpu.CompilerParams(vmem_limit_bytes=DENSE_BYTES),
        name="arrive_tokens",
    )(arrived, gain)


GATE_WIDTH = DSSM // QUERY_HEADS
PAIR_WIDTH = 2 * KEY_VALUE_HEADS * HEAD_SIZE // QUERY_HEADS
STATE_WIDTH = 2 * NSTATE // QUERY_HEADS
STEP_WIDTH = NH // QUERY_HEADS
ALL_AXES = ("row", "col")


def pad_columns(values, width):
    return jnp.pad(values, ((0, 0), (0, width - values.shape[1])))


def after(values, *earlier):
    return lax.optimization_barrier((values, *earlier))[0]


def after_all(values, *earlier):
    return lax.optimization_barrier((*values, *earlier))[: len(values)]


def unit_parts(values, units):
    cuts = [0]
    for width in (GATE_WIDTH, GATE_WIDTH, HEAD_SIZE, PAIR_WIDTH, STATE_WIDTH, STEP_WIDTH):
        cuts.append(cuts[-1] + width)
    return [
        jnp.concatenate(
            [values[:, unit * UNIT_IN + low : unit * UNIT_IN + high] for unit in range(units)], axis=1
        )
        for low, high in zip(cuts[:-1], cuts[1:])
    ]


def restore_units(parts, units):
    ordered = []
    for unit in range(units):
        for part in parts:
            width = part.shape[1] // units
            ordered.append(part[:, unit * width : (unit + 1) * width])
    return jnp.concatenate(ordered, axis=1)


def split_halves(values, units, first, axis):
    block = values.shape[axis] // units
    take = lambda low, high: lax.slice_in_dim(values, low, high, axis=axis)
    parts = [take(unit * block, unit * block + first) for unit in range(units)]
    parts += [take(unit * block + first, (unit + 1) * block) for unit in range(units)]
    return jnp.concatenate(parts, axis=axis)


def join_halves(values, units, first, axis):
    block = values.shape[axis] // units
    rest = block - first
    take = lambda low, high: lax.slice_in_dim(values, low, high, axis=axis)
    parts = []
    for unit in range(units):
        parts.append(take(unit * first, (unit + 1) * first))
        parts.append(take(units * first + unit * rest, units * first + (unit + 1) * rest))
    return jnp.concatenate(parts, axis=axis)


def quick(rows):
    return lax.axis_size("col") == 4 and lax.axis_size("row") == 8 and rows == 256


def spread_early(halves, gathered, selector):
    left, right = halves
    far_left, near_right = flip(left, 2), flip(right, 1)
    near_left, far_right = flip(left, 1), flip(right, 2)
    held = spread_block(0, halves, gathered, selector, None)
    onward_left, onward_right = after_all((far_left, near_right), held[1])
    corner = flip(onward_left, 1), flip(onward_right, 2)
    held = spread_block(1, (near_left, near_right), gathered, selector, held)
    held = spread_block(2, (far_left, far_right), gathered, selector, held)
    return spread_block(3, corner, gathered, selector, held)


def flip(values, mask):
    return lax.ppermute(values, "col", [(i, i ^ mask) for i in range(4)])


def gather_blocks(halves):
    left, right = halves
    far_left, near_right = flip(left, 2), flip(right, 1)
    near_left, far_right = flip(left, 1), flip(right, 2)
    corner_left, corner_right = flip(far_left, 1), flip(near_right, 2)
    return [
        (0, (left, right)),
        (1, (near_left, near_right)),
        (2, (far_left, far_right)),
        (3, (corner_left, corner_right)),
    ]


def rows_of(values, block, rows):
    return lax.dynamic_slice_in_dim(values, block * rows, rows, 0)


def spread_gathered(blocks, gathered, selector):
    held = None
    for mask, values in blocks:
        held = spread_block(mask, values, gathered, selector, held)
    return held


def spread_project(halves, gathered, selector):
    rows = halves[0].shape[0]
    if quick(rows):
        return spread_gathered(gather_blocks(halves), gathered, selector)
    wide, narrow_factor = gathered
    width = narrow_factor.shape[1]
    both = product(lax.all_gather(jnp.concatenate(halves, axis=1), "col", axis=0, tiled=True), wide)
    narrow = (selector * both[:, width:]).astype(BFLOAT)
    return (both[:, :width] + product(narrow, narrow_factor)).astype(BFLOAT), narrow


PIECE_TYPES = [(BFLOAT, BFLOAT), (BFLOAT, FLOAT), (FLOAT, BFLOAT), (FLOAT, FLOAT)]


def collect_pieces(values, gathered, at_once):
    if at_once:
        return collect_blocks([3, 1, 2, 0], values, gathered, PIECE_TYPES)
    (corner,) = collect_blocks([3], values, gathered, PIECE_TYPES[:1])
    values = after(values, corner[0])
    return [corner, *collect_blocks([1, 2, 0], values, gathered, PIECE_TYPES[1:])]


def collect_send(pieces, ordered=True):
    corner, near, far, own = pieces
    arriving = flip(corner[0], 1), flip(corner[1], 2)
    sent_near, sent_far = after_all((near[0], far[1]), *arriving) if ordered else (near[0], far[1])
    return own, flip(sent_near, 1), flip(sent_far, 2), far[0], near[1], arriving


def collect_middle(started):
    own, near_first, far_second, far_first, near_second, arriving = started
    return (own, near_first, far_second), sum_onward(far_first, arriving[0], near_second, arriving[1])


def collect_onward(onward):
    return flip(onward[0], 2), flip(onward[1], 1)


def collect_end(kept, last, kind, gathered, own_selector, *operands):
    own, near_first, far_second = kept
    parts = [own[0], near_first, last[0], own[1], far_second, last[1]]
    return finish(kind, parts, gathered, own_selector, *operands)


def collect_project(values, gathered, kind, own_selector, *operands):
    rows, model = own_selector.shape[0], operands[0].shape[1]
    if quick(rows):
        kept, onward = collect_middle(collect_send(collect_pieces(values, gathered, False)))
        return collect_end(kept, collect_onward(onward), kind, gathered, own_selector, *operands)
    wide, narrow_factor = gathered
    width = narrow_factor.shape[1]
    partial = jnp.concatenate(
        [contract_last(values, wide[:, :width]), contract_last(values, narrow_factor)], axis=1
    ).astype(BFLOAT)
    summed = lax.psum_scatter(partial, "col", scatter_dimension=0, tiled=True).astype(FLOAT)
    inner = (own_selector * summed[:, model:]).astype(BFLOAT)
    summed = summed[:, :model] + contract_last(inner, wide[:, width:])
    if kind == "output":
        return (operands[0] + summed).astype(BFLOAT), inner
    if kind == "forward":
        residual, gain = operands
        hidden = residual + summed
        return hidden, inner, *cut_halves(rms_norm(hidden, gain[0]).astype(BFLOAT))
    values, upstream, gain = operands
    _, back = jax.vjp(lambda given: rms_norm(given, gain[0]), values)
    hidden = upstream.astype(FLOAT) + back(summed)[0]
    if kind == "input":
        return hidden.astype(BFLOAT), inner
    return hidden, inner, *cut_halves(hidden.astype(BFLOAT))


def cut_halves(values):
    half = values.shape[1] // HALVES
    return values[:, :half], values[:, half:]


def local(
    tokens_in,
    cotangent,
    target,
    sequence_lengths,
    sequence_adapter,
    norm_gains,
    weight_in,
    conv_values,
    conv_states,
    scan_params,
    weight_mix,
    weight_feed,
    weight_down,
    in_lower,
    in_raise,
    mix_lower,
    mix_raise,
    feed_lower,
    feed_raise,
    down_lower,
    down_raise,
):
    cols = lax.axis_size("col")
    rows_axis = lax.axis_size("row")
    col = lax.axis_index("col")
    devices = cols * rows_axis
    rows = tokens_in.shape[0]
    model = tokens_in.shape[1]
    total = rows * cols
    units = QUERY_HEADS // cols
    channels = units * GATE_WIDTH
    peer = rows // devices
    lengths, adapters = sequence_lengths[0], sequence_adapter[0]
    sequences = lengths.shape[0]
    fast = quick(rows)
    key_head = col * units // (QUERY_HEADS // KEY_VALUE_HEADS)
    exchange = lambda values: lax.all_to_all(values, ALL_AXES, split_axis=0, concat_axis=0, tiled=True)

    sent, send_matrix = send_tokens(target, tokens_in, adapters, peer)
    shards = []

    def gather_weight(weight, lower, raised):
        top = jnp.concatenate([weight, lower], axis=1)
        if fast:
            bottom = pad_columns(raised, top.shape[1])
            shards.append(jnp.concatenate([top, bottom], axis=0))
            return (lax.all_gather(shards[-1], "row", axis=0),)
        wide = lax.all_gather(top, "row", axis=0, tiled=True)
        return wide, lax.all_gather(raised, "row", axis=0, tiled=True)

    depth = weight_in.shape[0]
    height = depth + in_raise.shape[0]
    given = after(jnp.concatenate([weight_in, in_raise], axis=0), send_matrix)
    gates, convs, queries, pairs, states, steps = unit_parts(given, units)
    pair_width, state_width = pairs.shape[1], states.shape[1]
    taps = jnp.concatenate([jnp.zeros((KCONV + 1, pair_width), BFLOAT), conv_states], axis=1)
    taps = jnp.pad(taps, ((0, 16 - KCONV - 1), (0, 0)))
    shared = jnp.concatenate([jnp.concatenate([pairs, states], axis=1), taps], axis=0)
    own_columns = jnp.concatenate([gates, convs, queries, pad_columns(steps, LANES)], axis=1)
    if fast:
        shared_shard = shared
        shared = lax.all_gather(shared_shard, "row", axis=0)
        weights_own = gather_weight(own_columns[:depth], in_lower, own_columns[depth:])
    arrived = exchange(sent)
    gains = jnp.broadcast_to(norm_gains.astype(FLOAT)[:, None, :], (2, 8, model))
    if fast:
        near, far = flip(shared, 1), flip(shared, 2)
        arrived = after(arrived, near, far, shards[0])
    own_input, place_matrix, *normed_one = arrive_tokens(arrived.reshape(rows, model + LANES), gains[0])
    blocks_one = gather_blocks(normed_one) if fast else normed_one
    if fast:
        held = jnp.zeros((cols,) + shared.shape, BFLOAT)
        for block, values in ((col, shared), (col ^ 1, near), (col ^ 2, far)):
            held = lax.dynamic_update_index_in_dim(held, values, block, 0)
        split = shared.shape[0] // 2
        corner = jnp.concatenate([flip(near[:split], 2), flip(far[split:], 1)], axis=0)
        held = lax.dynamic_update_index_in_dim(held, corner, col ^ 3, 0)
    else:
        held = lax.all_gather(shared, "col", axis=0)
    all_pairs = jnp.concatenate([held[at, ..., :height, :pair_width] for at in range(cols)], axis=-1)
    pick = lambda start: lax.select_n(
        key_head,
        *[all_pairs[..., start + at * HEAD_SIZE : start + (at + 1) * HEAD_SIZE] for at in range(KEY_VALUE_HEADS)],
    )
    shared_columns = jnp.concatenate(
        [held[at, ..., :height, pair_width:] for at in range(cols)]
        + [pick(0), pick(KEY_VALUE_HEADS * HEAD_SIZE)],
        axis=-1,
    )
    tap_rows = held[:, 0] if fast else held
    all_taps = jnp.concatenate(
        [tap_rows[at, height : height + KCONV + 1, pair_width:] for at in range(cols)], axis=1
    )
    if fast:
        weights_in = (shared_columns, *weights_own)
    else:
        columns = jnp.concatenate([shared_columns, own_columns], axis=1)
        weights_in = gather_weight(columns[:depth], in_lower, columns[depth:])
    weights_mix = gather_weight(
        after(split_halves(weight_mix, units, GATE_WIDTH, 0).T, sent),
        mix_raise.T,
        split_halves(mix_lower, units, GATE_WIDTH, 0).T,
    )
    weights_feed = gather_weight(
        after(split_halves(weight_feed, units, UNIT_FF, 1), arrived),
        feed_lower,
        split_halves(feed_raise, units, UNIT_FF, 1),
    )

    source_adapters = arrived.reshape(rows, model + LANES)[::peer, model + 1 : model + 1 + sequences].astype(jnp.int32)
    segment, position, selector = sequence_tables(lengths, adapters, total)
    own_selector = rows_of(selector, col, rows)
    own_segment = rows_of(segment, col, rows)
    tables = mixer_tables(lengths, segment, position, conv_values, all_taps, scan_params)

    def compact_grad(narrow, values):
        parts = [
            lax.dynamic_slice_in_dim(narrow, adapters[at] * RANK, RANK, 1)
            * (own_segment == at).astype(BFLOAT)[:, None]
            for at in range(sequences)
        ]
        grad = contract_first(jnp.concatenate(parts, axis=1), values).astype(BFLOAT)
        kept = sequences * RANK
        grad = grad.reshape(kept, devices, model // devices).transpose(1, 0, 2)
        return grad.reshape(devices, peer, kept * model // devices // peer)

    def expand_grad(dealt):
        kept = sequences * RANK
        dealt = dealt.reshape(devices * kept, model // devices)
        adapter_row = (source_adapters[:, :, None] * RANK + jnp.arange(RANK, dtype=jnp.int32)).reshape(-1)
        chosen = (jnp.arange(NADAPT * RANK, dtype=jnp.int32)[:, None] == adapter_row[None, :]).astype(BFLOAT)
        return product(chosen, dealt)

    def send_back(values, grads):
        back = contract_first(place_matrix, values).astype(BFLOAT).reshape(devices, peer, model)
        return exchange(jnp.concatenate([back, *grads], axis=2))

    def expand_packed(dealt, count):
        slots = dealt.shape[0] * peer
        block = jnp.arange(2 * LANES // (model // devices), dtype=jnp.int32)[:, None, None]
        row = jnp.arange(peer, dtype=jnp.int32)[None, None, :]
        place = block * peer + row
        adapter = jnp.where(place < RANK, source_adapters[None, :, 0:1], source_adapters[None, :, 1:2])
        adapter_row = (adapter * RANK + place % RANK).reshape(block.shape[0], 1, slots)
        chosen = (jnp.arange(NADAPT * RANK, dtype=jnp.int32)[None, :, None] == adapter_row).astype(BFLOAT)
        sums = product(chosen.reshape(-1, slots), dealt.reshape(slots, dealt.shape[2]))
        sums = sums.reshape(block.shape[0], NADAPT * RANK, dealt.shape[2])
        width = model // devices
        return [
            sum(
                sums[at, :, grad * 2 * LANES + at * width : grad * 2 * LANES + (at + 1) * width]
                for at in range(block.shape[0])
            )
            for grad in range(count)
        ]

    def take_back(dealt, count):
        returned = contract_first(send_matrix, dealt[:, :, :model].reshape(rows, model)).astype(BFLOAT)
        if fast:
            return returned, expand_packed(dealt[:, :, model:], count)
        width = (dealt.shape[2] - model) // count
        return returned, [
            expand_grad(dealt[:, :, model + at * width : model + (at + 1) * width]) for at in range(count)
        ]

    projected, inner_in = (spread_gathered if fast else spread_project)(blocks_one, weights_in, selector)

    sent_grad = product(send_matrix, cotangent).astype(BFLOAT).reshape(devices, peer, model)
    arrived_grad = exchange(after(sent_grad, normed_one[0])).reshape(rows, model)
    branch_two = product(place_matrix, arrived_grad).astype(BFLOAT)
    weights_down = gather_weight(after(weight_down.T, projected), down_raise.T, down_lower.T)

    mixed_out = attention_forward(projected, tables)
    mixed_out, scanned, carried = scan_forward(projected, tables, mixed_out)
    hidden, inner_out, *normed_two = collect_project(mixed_out, weights_mix, "forward", own_selector, own_input, gains[1])
    gate_up, inner_feed = spread_project(normed_two, weights_feed, selector)
    act_grad, narrow_two = spread_project(cut_halves(after(branch_two, projected)), weights_down, selector)
    half_feed = units * UNIT_FF
    gate_part, up_part = gate_up[:, :half_feed].astype(FLOAT), gate_up[:, half_feed:].astype(FLOAT)
    gate = jax.nn.sigmoid(gate_part)
    silu = gate_part * gate
    activated = (silu * up_part).astype(BFLOAT)
    wide_grad = act_grad.astype(FLOAT)
    feed_grad = jnp.concatenate(
        [wide_grad * up_part * (gate * (1.0 + gate_part * (1.0 - gate))), wide_grad * silu], axis=1
    ).astype(BFLOAT)
    choose = (
        jnp.arange(NADAPT * RANK, dtype=jnp.int32)[:, None]
        == (adapters[:, None] * RANK + jnp.arange(RANK, dtype=jnp.int32)[None, :]).reshape(1, -1)
    ).astype(BFLOAT)
    if fast:
        pieces = collect_pieces(after(activated, feed_grad), weights_down, True)
        kept, onward = collect_middle(collect_send(collect_pieces(feed_grad, weights_feed, False)))
        hidden_grad, narrow_three, left, right, early_grads = collect_end(
            kept,
            collect_onward(onward),
            "backward",
            weights_feed,
            own_selector,
            after(hidden, pieces[3][0]),
            branch_two,
            gains[1],
            choose,
            *normed_two,
            inner_out,
        )
        mixed_grad, narrow_one = spread_early((left, right), weights_mix, selector)
    else:
        hidden_grad, narrow_three, *branch_one = collect_project(
            feed_grad, weights_feed, "backward", own_selector, hidden, branch_two, gains[1]
        )
        mixed_grad, narrow_one = spread_project(branch_one, weights_mix, selector)

    if fast:
        near_parts = after_all((*pieces[0], pieces[1][0], pieces[2][1]), mixed_grad)
        started = collect_send(
            [near_parts[:2], (near_parts[2], pieces[1][1]), (pieces[2][0], near_parts[3]), pieces[3]], False
        )
        attended_grads = attention_backward(projected, tables, after(mixed_grad, near_parts[0]))
        kept, onward = collect_middle((*started[:5], after_all(started[5], attended_grads[1])))
        scan_inputs = (projected, tables, scanned, carried, after(mixed_grad, *onward), attended_grads)
        scan_part = list(scan_backward(*scan_inputs, 0, 2, None))
        payload = collect_end(
            kept,
            collect_onward(onward),
            "output",
            weights_down,
            own_selector,
            after(hidden, scan_part[2]),
            place_matrix,
            choose,
            branch_two,
            early_grads,
        )
        dealt_out = exchange(payload.reshape(devices, peer, -1))
        scan_part[2] = after(scan_part[2], payload)
        projected_grad = scan_backward(*scan_inputs, 1, 2, scan_part)[0]
        started_in = collect_send(collect_pieces(projected_grad, weights_in, True))
        kept_in, onward_in = collect_middle(started_in)
    else:
        block_out, inner_down = collect_project(activated, weights_down, "output", own_selector, hidden)
        attended_grads = attention_backward(projected, tables, mixed_grad)
        projected_grad = scan_backward(
            projected, tables, scanned, carried, mixed_grad, attended_grads, 0, 1, None
        )[0]
        dealt_out = send_back(
            block_out,
            [
                compact_grad(inner_down, branch_two),
                compact_grad(narrow_three, jnp.concatenate(normed_two, axis=1)),
                compact_grad(inner_out, jnp.concatenate(branch_one, axis=1)),
            ],
        )

    def sum_rows(values):
        return lax.psum_scatter(values.astype(BFLOAT), "row", scatter_dimension=0, tiled=True).astype(FLOAT)

    early_parts = [
        contract_first(narrow_one, mixed_out),
        contract_first(inner_feed, feed_grad),
        contract_first(narrow_two, activated),
    ]
    early = sum_rows(jnp.concatenate(early_parts, axis=1))

    raise_grad = contract_first(inner_in, after(projected_grad, *onward_in) if fast else projected_grad)
    late = sum_rows(raise_grad)

    if fast:
        payload = collect_end(
            kept_in,
            collect_onward(onward_in),
            "input",
            weights_in,
            own_selector,
            own_input,
            after(hidden_grad, dealt_out),
            gains[0],
            choose,
            *normed_one,
            place_matrix,
        )
        dealt_grad = exchange(payload.reshape(devices, peer, -1))
    else:
        input_grad, narrow_four = collect_project(
            projected_grad, weights_in, "input", own_selector, own_input, hidden_grad, gains[0]
        )
        dealt_grad = send_back(input_grad, [compact_grad(narrow_four, jnp.concatenate(normed_one, axis=1))])
        payload = input_grad
    dealt_out, early, late = after_all((dealt_out, early, late), payload)
    early_cuts = [0, early_parts[0].shape[1]]
    early_cuts.append(early_cuts[1] + early_parts[1].shape[1])
    grad_mix_lower = join_halves(early[:, : early_cuts[1]], units, GATE_WIDTH, 1).T
    grad_feed_raise = join_halves(early[:, early_cuts[1] : early_cuts[2]], units, UNIT_FF, 1)
    grad_down_lower = early[:, early_cuts[2] :].T

    key_columns = late[:, STATES : STATES + HEAD_SIZE]
    value_columns = late[:, STATES + HEAD_SIZE : STATES + PAIR]
    mine = [(key_head == at).astype(FLOAT) for at in range(KEY_VALUE_HEADS)]
    pair_grad = jnp.concatenate([part * here for part in (key_columns, value_columns) for here in mine], axis=1)
    stacked = jnp.stack(
        [
            jnp.concatenate(
                [
                    pair_grad[:, at * pair_width : (at + 1) * pair_width],
                    late[:, at * state_width : (at + 1) * state_width],
                ],
                axis=1,
            )
            for at in range(cols)
        ]
    )
    if fast:
        piece = lambda mask: lax.dynamic_index_in_dim(stacked, col ^ mask, 0, False)
        shared_sum = piece(0) + flip(piece(1), 1) + flip(piece(2), 2) + flip(piece(3), 3)
    else:
        shared_sum = lax.psum_scatter(
            stacked.reshape(stacked.shape[0] * stacked.shape[1], -1), "col", scatter_dimension=0, tiled=True
        )
    late = jnp.concatenate([shared_sum, late[:, STATES + PAIR :]], axis=1)
    shared_width = pair_width + state_width
    cuts = [shared_width]
    for width in (channels, channels, units * HEAD_SIZE, units * STEP_WIDTH):
        cuts.append(cuts[-1] + width)
    gate_columns, conv_columns, query_columns, step_columns = [
        late[:, low:high] for low, high in zip(cuts[:-1], cuts[1:])
    ]
    grad_in_raise = restore_units(
        [
            gate_columns,
            conv_columns,
            query_columns,
            late[:, :pair_width],
            late[:, pair_width:shared_width],
            step_columns,
        ],
        units,
    )

    returned_out, (grad_down_raise, grad_feed_lower, grad_mix_raise) = take_back(dealt_out, 3)
    returned_grad, (grad_in_lower,) = take_back(dealt_grad, 1)
    return (
        returned_out,
        returned_grad,
        grad_in_lower.T,
        grad_in_raise,
        grad_mix_lower,
        grad_mix_raise,
        grad_feed_lower.T,
        grad_feed_raise,
        grad_down_lower,
        grad_down_raise,
    )


def solution(mesh):
    in_specs = (
        P(("row", "col"), None),
        P(("row", "col"), None),
        P(("row", "col")),
        P("row", None),
        P("row", None),
        P(),
        P("row", "col"),
        P(None, "col"),
        P(None, "col"),
        P(None, "col"),
        P("col", "row"),
        P("row", "col"),
        P("col", "row"),
        P("row", None),
        P("row", "col"),
        P("col", "row"),
        P(None, "row"),
        P("row", None),
        P("row", "col"),
        P("col", "row"),
        P(None, "row"),
    )
    out_specs = (
        P(("row", "col"), None),
        P(("row", "col"), None),
        P(("row", "col"), None),
        P("row", "col"),
        P("col", "row"),
        P(None, ("row", "col")),
        P(("row", "col"), None),
        P("row", "col"),
        P("col", "row"),
        P(None, ("row", "col")),
    )
    return jax.shard_map(local, mesh=mesh, in_specs=in_specs, out_specs=out_specs, check_vma=False)
```

```python
import functools
import math

import jax
import jax.numpy as jnp
from jax import lax
from jax.experimental import pallas as pl
from jax.experimental.pallas import tpu as pltpu
from jax.sharding import PartitionSpec as P

NH = 48
HP = 64
NSTATE = 256
KCONV = 4
QUERY_HEADS = 8
KEY_VALUE_HEADS = 2
HEAD_SIZE = 128
RANK = 16
NADAPT = 8
SSD_BLOCK = 256
DSSM = 3072
UNIT_IN = 1030
UNIT_FF = 512


EPSILON = 1e-05
ROPE_BASE = 10000.0
NEGATIVE = -1e30
FLOAT = jnp.float32
BFLOAT = jnp.bfloat16


def product(left, right):
    return jnp.dot(left, right, preferred_element_type=FLOAT)


def contract_last(left, right):
    return lax.dot_general(left, right, (((1,), (1,)), ((), ())), preferred_element_type=FLOAT)


def contract_first(left, right):
    return lax.dot_general(left, right, (((0,), (0,)), ((), ())), preferred_element_type=FLOAT)


def rms_norm(values, gain):
    return values * lax.rsqrt(jnp.mean(values * values, axis=-1, keepdims=True) + EPSILON) * gain


def sequence_tables(lengths, adapters, sequence_length):
    sequence_count = lengths.shape[0]
    boundary = jnp.cumsum(lengths)
    token_index = jnp.arange(sequence_length, dtype=jnp.int32)
    passed = (token_index[:, None] >= boundary[None, :]).astype(jnp.int32)
    segment = jnp.sum(passed, axis=1)
    segment_start = jnp.sum(passed * lengths[None, :], axis=1)
    position = token_index - segment_start
    member = (segment[:, None] == jnp.arange(sequence_count, dtype=jnp.int32)[None, :]).astype(
        jnp.int32
    )
    chosen = jnp.sum(member * adapters[None, :], axis=1)
    column = jnp.arange(NADAPT * RANK, dtype=jnp.int32) // RANK
    selector = (chosen[:, None] == column[None, :]).astype(FLOAT)
    return (segment, position, selector)


ESTIMATE = 16
SCAN_BYTES = 32 * 1024 * 1024
ALONE_BYTES = 56 * 1024 * 1024
DENSE_BYTES = 16 * 1024 * 1024
FINISH_BYTES = 32 * 1024 * 1024
LANES = 128


def whole(shape):
    return pl.BlockSpec(shape, lambda *_: (0,) * len(shape))


def estimate(flops, bytes_accessed, transcendentals):
    return pl.CostEstimate(
        flops=flops // ESTIMATE,
        bytes_accessed=bytes_accessed // ESTIMATE,
        transcendentals=transcendentals // ESTIMATE,
    )


def dot(left, right, contract):
    return lax.dot_general(left, right, ((contract[:1], contract[1:]), ((), ())), preferred_element_type=FLOAT)


def parts_of(values, count):
    parts = []
    for _ in range(count):
        part = values.astype(BFLOAT)
        parts.append(part)
        values = values - part.astype(FLOAT)
    return parts


def running_sum(values, triangle, contract):
    width = values.shape[1]
    split = dot(triangle, jnp.concatenate(parts_of(values, 3), axis=1), contract)
    return split[:, :width] + split[:, width : 2 * width] + split[:, 2 * width :]


def head_spread(values, expand):
    return dot(jnp.concatenate(parts_of(values, 2), axis=1), expand, (1, 0))


def head_sum(values, expand):
    high, low = parts_of(values, 2)
    single = expand[:LANES]
    return dot(high, single, (1, 1)) + dot(low, single, (1, 1))


def silu_parts(values):
    gate = 1.0 / (1.0 + jnp.exp(-values))
    return values * gate, gate


def expand_table(channels):
    row = lax.broadcasted_iota(jnp.int32, (2 * LANES, channels), 0) % LANES
    channel = lax.broadcasted_iota(jnp.int32, (2 * LANES, channels), 1) // HP
    return (row == channel).astype(BFLOAT)


def conv_sum(current_ref, before_ref, taps_ref, meta):
    rows = SSD_BLOCK
    current = current_ref[...].astype(FLOAT)
    window = jnp.concatenate([before_ref[...].astype(FLOAT)[8:16], current], axis=0)
    summed = taps_ref[KCONV : KCONV + 1, :] + current * taps_ref[0:1, :]
    for lag in range(1, KCONV):
        shifted = window[8 - lag : 8 - lag + rows]
        summed = summed + jnp.where(meta[:, 1:2] >= lag, shifted, 0.0) * taps_ref[lag : lag + 1, :]
    return summed


def conv_back(summed_grad, later, taps_ref, meta):
    rows = SSD_BLOCK
    window = jnp.concatenate([summed_grad, later[...]], axis=0)
    grad = summed_grad * taps_ref[0:1, :]
    for lag in range(1, KCONV):
        grad = grad + jnp.where(meta[:, 2:3] >= lag, window[lag : lag + rows], 0.0) * taps_ref[lag : lag + 1, :]
    later[...] = summed_grad[:8]
    return grad


def silu_slope(values, gate):
    return gate * (1.0 + values * (1.0 - gate))


def scan_block(
    conv_ref, before_ref, state_ref, state_before_ref, step_ref, meta_ref, segment_ref, taps_ref, state_taps_ref, head_ref,
    turned_over,
):
    rows = SSD_BLOCK
    channels = conv_ref.shape[1]
    meta = meta_ref[...]
    summed = conv_sum(conv_ref, before_ref, taps_ref, meta)
    activated, conv_gate = silu_parts(summed)
    wide_inputs = activated.astype(BFLOAT).astype(FLOAT)
    state_summed = conv_sum(state_ref, state_before_ref, state_taps_ref, meta)
    state_values, state_gate = silu_parts(state_summed)
    write = state_values[:, :NSTATE].astype(BFLOAT)
    read = state_values[:, NSTATE:].astype(BFLOAT)
    raw = step_ref[...].astype(FLOAT) + head_ref[0:1, :]
    steps = jnp.maximum(raw, 0.0) + jnp.log1p(jnp.exp(-jnp.abs(raw)))
    row = lax.broadcasted_iota(jnp.int32, (rows, rows), 0)
    column = lax.broadcasted_iota(jnp.int32, (rows, rows), 1)
    triangle = (row >= column).astype(BFLOAT)
    total = running_sum(steps * head_ref[1:2, :], triangle, (1, 0))
    entered = jnp.exp(total) * meta[:, 3:4]
    leaving = jnp.exp(total[rows - 1 : rows] - total) * meta[:, 4:5]
    expand = expand_table(channels)
    spread = head_spread(jnp.concatenate([steps, entered, leaving * steps], axis=0), expand)
    ordered = row <= column if turned_over else row >= column
    blocked = jnp.where(ordered & (meta[:, 0:1] == segment_ref[0:1, :]), 0.0, NEGATIVE)
    return dict(
        summed=summed,
        conv_gate=conv_gate,
        state_summed=state_summed,
        state_gate=state_gate,
        write=write,
        read=read,
        wide_inputs=wide_inputs,
        raw=raw,
        steps=steps,
        triangle=triangle,
        total=total,
        total_rows=total.T,
        leaving=leaving,
        expand=expand,
        steps_wide=spread[:rows],
        entered_wide=spread[rows : 2 * rows],
        tail_wide=spread[2 * rows :],
        stepped=(wide_inputs * spread[:rows]).astype(BFLOAT),
        tailed=(wide_inputs * spread[2 * rows :]).astype(BFLOAT),
        blocked=blocked,
        crossing=dot(write, read, (1, 1)) if turned_over else dot(read, write, (1, 1)),
    )


def decay_of(block, head):
    difference = block["total"][:, head : head + 1] - block["total_rows"][head : head + 1, :]
    return jnp.exp(difference + block["blocked"])


def turned_decay_of(block, head):
    difference = block["total_rows"][head : head + 1, :] - block["total"][:, head : head + 1]
    return jnp.exp(difference + block["blocked"])


def scan_forward_kernel(
    gate_ref, conv_ref, before_ref, state_ref, state_before_ref, step_ref, meta_ref, segment_ref, taps_ref,
    state_taps_ref, head_ref, skip_ref, mixed_ref, out_ref, scanned_ref, states_ref, state,
):
    del mixed_ref

    @pl.when(pl.program_id(0) == 0)
    def _():
        state[...] = jnp.zeros_like(state)

    block = scan_block(
        conv_ref, before_ref, state_ref, state_before_ref, step_ref, meta_ref, segment_ref, taps_ref, state_taps_ref,
        head_ref, False,
    )
    heads = conv_ref.shape[1] // HP
    carried = state[...].astype(BFLOAT)
    states_ref[0] = carried
    across = dot(block["read"], carried, (1, 0)) * block["entered_wide"]
    within = []
    for head in range(heads):
        weights = (block["crossing"] * decay_of(block, head)).astype(BFLOAT)
        within.append(dot(weights, block["stepped"][:, head * HP : (head + 1) * HP], (1, 0)))
    scanned = across + jnp.concatenate(within, axis=1)
    scanned_ref[...] = scanned
    gated, _ = silu_parts(gate_ref[...].astype(FLOAT))
    out_ref[...] = ((scanned + skip_ref[0:1, :] * block["wide_inputs"]) * gated).astype(BFLOAT)
    state[...] = state[...] * block["entered_wide"][SSD_BLOCK - 1 : SSD_BLOCK, :] + dot(
        block["write"], block["tailed"], (0, 0)
    )


def scan_backward_kernel(
    gate_ref, conv_ref, before_ref, state_ref, state_before_ref, step_ref, meta_ref, segment_ref, taps_ref,
    state_taps_ref, head_ref, skip_ref, scanned_ref, states_ref, grad_ref, query_grad_ref, shared_grad_ref, *rest,
):
    out_ref, *running = rest[-4:]
    state_grad, later, state_later = running

    @pl.when(pl.program_id(0) == 0)
    def _():
        for at, ref in enumerate(running):
            ref[...] = rest[1 + at][...] if len(rest) > 4 else jnp.zeros_like(ref)

    block = scan_block(
        conv_ref, before_ref, state_ref, state_before_ref, step_ref, meta_ref, segment_ref, taps_ref, state_taps_ref,
        head_ref, True,
    )
    rows = SSD_BLOCK
    channels = conv_ref.shape[1]
    heads = channels // HP
    meta = meta_ref[...]
    read, write = block["read"], block["write"]
    inputs = block["wide_inputs"]
    scanned = scanned_ref[...]
    skip = skip_ref[0:1, :]
    gate_values = gate_ref[...].astype(FLOAT)
    gated, gate = silu_parts(gate_values)
    grad = grad_ref[...].astype(FLOAT)
    gate_grad = grad * (scanned + skip * inputs) * silu_slope(gate_values, gate)
    out_grad = grad * gated
    inputs_grad = skip * out_grad
    rounded = out_grad.astype(BFLOAT)
    wide_rounded = rounded.astype(FLOAT)
    carried = states_ref[0]
    after = state_grad[...]
    after_rounded = after.astype(BFLOAT)

    from_state = dot(write, after_rounded, (1, 0))
    entering = (wide_rounded * block["entered_wide"]).astype(BFLOAT)
    write_grad = dot(block["tailed"], after_rounded, (1, 1))
    read_grad = dot(entering, carried, (1, 1))
    last_entered = block["entered_wide"][rows - 1 : rows, :]
    through = jnp.sum(after * carried.astype(FLOAT), axis=0, keepdims=True) * last_entered
    state_grad[...] = after * last_entered + dot(read, entering, (0, 0))

    crossing_grad = jnp.zeros((rows, rows), FLOAT)
    pulled = []
    for head in range(heads):
        span = slice(head * HP, (head + 1) * HP)
        decay = turned_decay_of(block, head)
        weights = (block["crossing"] * decay).astype(BFLOAT)
        pulled.append(dot(weights, rounded[:, span], (1, 0)))
        crossing_grad = crossing_grad + dot(block["stepped"][:, span], rounded[:, span], (1, 1)) * decay
    pulled = jnp.concatenate(pulled, axis=1)
    crossing_rounded = crossing_grad.astype(BFLOAT)
    read_grad = read_grad + dot(crossing_rounded, write, (0, 0))
    write_grad = write_grad + dot(crossing_rounded, read, (1, 0))

    inputs_grad = inputs_grad + block["steps_wide"] * pulled + block["tail_wide"] * from_state
    sums = head_sum(
        jnp.concatenate(
            [
                wide_rounded * scanned - block["stepped"].astype(FLOAT) * pulled,
                inputs * pulled,
                inputs * from_state,
                jnp.broadcast_to(through, (8, channels)),
            ],
            axis=0,
        ),
        block["expand"],
    )
    leaving_grad = sums[2 * rows : 3 * rows] * block["leaving"]
    leaving_total = leaving_grad * block["steps"]
    last = sums[3 * rows : 3 * rows + 1] + jnp.sum(leaving_total, axis=0, keepdims=True)
    total_grad = sums[:rows] - leaving_total
    total_grad = total_grad + jnp.where(
        lax.broadcasted_iota(jnp.int32, total_grad.shape, 0) == rows - 1, last, 0.0
    )
    decay_grad = running_sum(total_grad, block["triangle"], (0, 0))
    steps_grad = sums[rows : 2 * rows] + leaving_grad + decay_grad * head_ref[1:2, :]
    raw_grad = steps_grad / (1.0 + jnp.exp(-block["raw"]))
    raw_grad = jnp.where(lax.broadcasted_iota(jnp.int32, raw_grad.shape, 1) < heads, raw_grad, 0.0)

    state_slope = silu_slope(block["state_summed"], block["state_gate"])
    state_pre = conv_back(
        jnp.concatenate([write_grad, read_grad], axis=1) * state_slope, state_later, state_taps_ref, meta
    )
    conv_pre = conv_back(inputs_grad * silu_slope(block["summed"], block["conv_gate"]), later, taps_ref, meta)
    out_ref[:, : 2 * NSTATE] = state_pre.astype(BFLOAT)
    start = 2 * NSTATE + 2 * HEAD_SIZE
    end = out_ref.shape[1] - LANES
    out_ref[:, 2 * NSTATE : start] = shared_grad_ref[...]
    out_ref[:, start + 2 * channels : end] = query_grad_ref[...]
    out_ref[:, start : start + channels] = gate_grad.astype(BFLOAT)
    out_ref[:, start + channels : start + 2 * channels] = conv_pre.astype(BFLOAT)
    out_ref[:, end:] = raw_grad.astype(BFLOAT)


STATES = 2 * NSTATE
PAIR = 2 * HEAD_SIZE


def scan_specs(channels, order):
    half = SSD_BLOCK // 16
    before = lambda i: jnp.maximum(order(i) * half - 1, 0)
    gate_at = (STATES + PAIR) // channels
    step_at = (STATES + PAIR + 2 * channels + channels * QUERY_HEADS // DSSM * HEAD_SIZE) // LANES
    return [
        pl.BlockSpec((SSD_BLOCK, channels), lambda i: (order(i), gate_at)),
        pl.BlockSpec((SSD_BLOCK, channels), lambda i: (order(i), gate_at + 1)),
        pl.BlockSpec((16, channels), lambda i: (before(i), gate_at + 1)),
        pl.BlockSpec((SSD_BLOCK, STATES), lambda i: (order(i), 0)),
        pl.BlockSpec((16, STATES), lambda i: (before(i), 0)),
        pl.BlockSpec((SSD_BLOCK, LANES), lambda i: (order(i), step_at)),
        pl.BlockSpec((SSD_BLOCK, LANES), lambda i: (order(i), 0)),
        pl.BlockSpec((8, SSD_BLOCK), lambda i: (0, order(i))),
        whole((8, channels)),
        whole((8, STATES)),
        whole((8, LANES)),
        whole((8, channels)),
    ]


def scan_operands(projected, tables):
    return [projected] * 6 + [
        tables[name] for name in ("meta", "segment_row", "taps", "state_taps", "head", "skip")
    ]


def scan_cost(tokens, channels, factor):
    heads = channels // HP
    return estimate(
        flops=factor * 2 * tokens * SSD_BLOCK * (3 * channels + NSTATE),
        bytes_accessed=factor * tokens * channels * 12,
        transcendentals=tokens * SSD_BLOCK * heads,
    )


def scan_forward(projected, tables, mixed):
    tokens = projected.shape[0]
    channels = tables["taps"].shape[1]
    blocks = tokens // SSD_BLOCK
    return pl.pallas_call(
        scan_forward_kernel,
        grid=(blocks,),
        in_specs=scan_specs(channels, lambda i: i) + [pl.BlockSpec(memory_space=pl.ANY)],
        out_specs=[
            pl.BlockSpec((SSD_BLOCK, channels), lambda i: (i, 0)),
            pl.BlockSpec((SSD_BLOCK, channels), lambda i: (i, 0)),
            pl.BlockSpec((1, NSTATE, channels), lambda i: (i, 0, 0)),
        ],
        out_shape=[
            jax.ShapeDtypeStruct(mixed.shape, BFLOAT),
            jax.ShapeDtypeStruct((tokens, channels), FLOAT),
            jax.ShapeDtypeStruct((blocks, NSTATE, channels), BFLOAT),
        ],
        scratch_shapes=[pltpu.VMEM((NSTATE, channels), FLOAT)],
        input_output_aliases={12: 0},
        compiler_params=pltpu.CompilerParams(vmem_limit_bytes=SCAN_BYTES),
        cost_estimate=scan_cost(tokens, channels, 1),
        name="scan_forward",
    )(*scan_operands(projected, tables), mixed)


def scan_backward(projected, tables, scanned, carried, mixed_grad, attended_grads, part, parts, before):
    tokens, width = projected.shape
    channels = tables["taps"].shape[1]
    blocks = tokens // SSD_BLOCK
    last = blocks - 1 - part * (blocks // parts)
    back = lambda i: (last - i, 0)
    running = [(NSTATE, channels), (8, channels), (8, STATES)]
    query_grad, shared_grad = attended_grads
    operands = [*scan_operands(projected, tables), scanned, carried, mixed_grad, query_grad, shared_grad]
    in_specs = scan_specs(channels, lambda i: last - i) + [
        pl.BlockSpec((SSD_BLOCK, channels), back),
        pl.BlockSpec((1, NSTATE, channels), lambda i: (last - i, 0, 0)),
        pl.BlockSpec((SSD_BLOCK, channels), back),
        pl.BlockSpec((SSD_BLOCK, query_grad.shape[1]), back),
        pl.BlockSpec((SSD_BLOCK, PAIR), back),
    ]
    aliases = {}
    if before is not None:
        aliases = {len(operands): 0}
        operands += list(before)
        in_specs += [pl.BlockSpec(memory_space=pl.ANY), *[whole(shape) for shape in running]]
    return pl.pallas_call(
        scan_backward_kernel,
        grid=(blocks // parts,),
        in_specs=in_specs,
        out_specs=[pl.BlockSpec((SSD_BLOCK, width), back), *[whole(shape) for shape in running]],
        out_shape=[
            jax.ShapeDtypeStruct((tokens, width), BFLOAT),
            *[jax.ShapeDtypeStruct(shape, FLOAT) for shape in running],
        ],
        input_output_aliases=aliases,
        compiler_params=pltpu.CompilerParams(vmem_limit_bytes=ALONE_BYTES),
        cost_estimate=scan_cost(tokens, channels, 2),
        name="scan_backward",
    )(*operands)


def turned(values, cosine, sine):
    return (values * cosine + pltpu.roll(values, HEAD_SIZE // 2, 1) * sine).astype(BFLOAT)


def turned_back(values, cosine, sine):
    return values * cosine + pltpu.roll(values * sine, HEAD_SIZE // 2, 1)


ATT_ROWS = 256


def attention_mask(meta_ref, segment_ref, start, extent):
    row = start + lax.broadcasted_iota(jnp.int32, (ATT_ROWS, extent), 0)
    column = lax.broadcasted_iota(jnp.int32, (ATT_ROWS, extent), 1)
    return (row >= column) & (meta_ref[start : start + ATT_ROWS, 0:1] == segment_ref[0:1, :extent])


def probabilities(query, keys, allowed):
    score = dot(query, keys, (1, 1)) * (1.0 / math.sqrt(HEAD_SIZE))
    score = jnp.where(allowed, score, NEGATIVE)
    exponent = jnp.exp(score - jnp.max(score, axis=1, keepdims=True))
    return exponent / jnp.sum(exponent, axis=1, keepdims=True)


def attention_forward_kernel(query_ref, key_ref, value_ref, cosine_ref, sine_ref, meta_ref, segment_ref, out_ref, keys):
    tokens = key_ref.shape[0]
    keys[...] = turned(key_ref[...].astype(FLOAT), cosine_ref[...], sine_ref[...])
    for start in range(0, tokens, ATT_ROWS):
        extent = start + ATT_ROWS
        here = slice(start, extent)
        allowed = attention_mask(meta_ref, segment_ref, start, extent)
        for unit in range(query_ref.shape[1] // HEAD_SIZE):
            span = slice(unit * HEAD_SIZE, (unit + 1) * HEAD_SIZE)
            query = turned(query_ref[here, span].astype(FLOAT), cosine_ref[here], sine_ref[here])
            weights = probabilities(query, keys[:extent], allowed).astype(BFLOAT)
            out_ref[here, span] = dot(weights, value_ref[:extent], (1, 0)).astype(BFLOAT)


def attention_backward_kernel(
    query_ref, key_ref, value_ref, cosine_ref, sine_ref, meta_ref, segment_ref, grad_ref,
    query_grad_ref, shared_grad_ref, keys, key_sum, value_sum,
):
    tokens = key_ref.shape[0]
    scale = 1.0 / math.sqrt(HEAD_SIZE)
    keys[...] = turned(key_ref[...].astype(FLOAT), cosine_ref[...], sine_ref[...])
    key_sum[...] = jnp.zeros_like(key_sum)
    value_sum[...] = jnp.zeros_like(value_sum)
    for start in range(0, tokens, ATT_ROWS):
        extent = start + ATT_ROWS
        here = slice(start, extent)
        allowed = attention_mask(meta_ref, segment_ref, start, extent)
        for unit in range(query_ref.shape[1] // HEAD_SIZE):
            span = slice(unit * HEAD_SIZE, (unit + 1) * HEAD_SIZE)
            query = turned(query_ref[here, span].astype(FLOAT), cosine_ref[here], sine_ref[here])
            weights = probabilities(query, keys[:extent], allowed)
            grad = grad_ref[here, span]
            weights_grad = dot(grad, value_ref[:extent], (1, 1))
            value_sum[:extent] += dot(weights.astype(BFLOAT), grad, (0, 0))
            mean_grad = jnp.sum(weights * weights_grad, axis=1, keepdims=True)
            score_grad = (weights * (weights_grad - mean_grad) * scale).astype(BFLOAT)
            query_grad = dot(score_grad, keys[:extent], (1, 0))
            key_sum[:extent] += dot(score_grad, query, (0, 0))
            query_grad_ref[here, span] = turned_back(query_grad, cosine_ref[here], sine_ref[here]).astype(BFLOAT)
    shared_grad_ref[:, :HEAD_SIZE] = turned_back(key_sum[...], cosine_ref[...], sine_ref[...]).astype(BFLOAT)
    shared_grad_ref[:, HEAD_SIZE:] = value_sum[...].astype(BFLOAT)


def attention_cost(tokens, width, factor):
    return estimate(
        flops=factor * 2 * tokens * tokens * width,
        bytes_accessed=factor * tokens * width * 8,
        transcendentals=tokens * tokens * width // (2 * HEAD_SIZE),
    )


def attention_specs(tokens, channels):
    width = channels * QUERY_HEADS // DSSM * HEAD_SIZE
    narrow = whole((tokens, HEAD_SIZE))
    return [
        pl.BlockSpec((tokens, width), lambda *_: (0, (STATES + PAIR + 2 * channels) // width)),
        pl.BlockSpec((tokens, HEAD_SIZE), lambda *_: (0, STATES // HEAD_SIZE)),
        pl.BlockSpec((tokens, HEAD_SIZE), lambda *_: (0, STATES // HEAD_SIZE + 1)),
        narrow,
        narrow,
        whole((tokens, LANES)),
        whole((8, tokens)),
    ]


def attention_operands(projected, tables):
    return [projected] * 3 + [tables[name] for name in ("cosine", "sine", "meta", "segment_row")]


def attention_forward(projected, tables):
    tokens = projected.shape[0]
    channels = tables["taps"].shape[1]
    width = channels * QUERY_HEADS // DSSM * HEAD_SIZE
    return pl.pallas_call(
        attention_forward_kernel,
        grid=(1,),
        in_specs=attention_specs(tokens, channels),
        out_specs=pl.BlockSpec((tokens, width), lambda *_: (0, channels // width)),
        out_shape=jax.ShapeDtypeStruct((tokens, channels + width), BFLOAT),
        scratch_shapes=[pltpu.VMEM((tokens, HEAD_SIZE), BFLOAT)],
        compiler_params=pltpu.CompilerParams(vmem_limit_bytes=SCAN_BYTES),
        cost_estimate=attention_cost(tokens, width, 1),
        name="attention_forward",
    )(*attention_operands(projected, tables))


def attention_backward(projected, tables, mixed_grad):
    tokens = projected.shape[0]
    channels = tables["taps"].shape[1]
    width = channels * QUERY_HEADS // DSSM * HEAD_SIZE
    return pl.pallas_call(
        attention_backward_kernel,
        grid=(1,),
        in_specs=attention_specs(tokens, channels)
        + [pl.BlockSpec((tokens, width), lambda *_: (0, channels // width))],
        out_specs=[whole((tokens, width)), whole((tokens, PAIR))],
        out_shape=[jax.ShapeDtypeStruct((tokens, width), BFLOAT), jax.ShapeDtypeStruct((tokens, PAIR), BFLOAT)],
        scratch_shapes=[
            pltpu.VMEM((tokens, HEAD_SIZE), BFLOAT),
            pltpu.VMEM((tokens, HEAD_SIZE), FLOAT),
            pltpu.VMEM((tokens, HEAD_SIZE), FLOAT),
        ],
        compiler_params=pltpu.CompilerParams(vmem_limit_bytes=SCAN_BYTES),
        cost_estimate=attention_cost(tokens, width, 3),
        name="attention_backward",
    )(*attention_operands(projected, tables), mixed_grad)


def mixer_tables(lengths, segment, position, conv_values, conv_states, scan_params):
    tokens = segment.shape[0]
    block = jnp.arange(tokens, dtype=jnp.int32) // SSD_BLOCK
    previous = jnp.concatenate([jnp.full((1,), -1, jnp.int32), segment[:-1]])
    first_previous = jnp.repeat(previous[::SSD_BLOCK], SSD_BLOCK)
    last_segment = jnp.repeat(segment[SSD_BLOCK - 1 :: SSD_BLOCK], SSD_BLOCK)
    length = jnp.sum(
        jnp.where(segment[:, None] == jnp.arange(lengths.shape[0], dtype=jnp.int32)[None, :], lengths[None, :], 0),
        axis=1,
    )
    columns = [
        segment,
        position,
        length - 1 - position,
        segment == first_previous,
        segment == last_segment,
    ]
    meta = jnp.stack([column.astype(FLOAT) for column in columns], axis=1)
    half_width = HEAD_SIZE // 2
    frequency = ROPE_BASE ** (-2.0 * jnp.arange(half_width, dtype=FLOAT) / HEAD_SIZE)
    angle = position.astype(FLOAT)[:, None] * frequency[None, :]
    cosine, sine = jnp.cos(angle), jnp.sin(angle)
    heads = scan_params.shape[1]
    head = jnp.stack([scan_params[0], -jnp.exp(scan_params[1]), scan_params[2]])
    return dict(
        meta=jnp.pad(meta, ((0, 0), (0, LANES - meta.shape[1]))),
        segment_row=jnp.broadcast_to(segment.astype(FLOAT)[None, :], (8, tokens)),
        taps=jnp.pad(conv_values.astype(FLOAT), ((0, 3), (0, 0))),
        state_taps=jnp.pad(conv_states.astype(FLOAT), ((0, 3), (0, 0))),
        head=jnp.pad(head, ((0, 5), (0, LANES - heads))),
        skip=jnp.broadcast_to(jnp.repeat(scan_params[2], HP)[None, :], (8, heads * HP)),
        cosine=jnp.concatenate([cosine, cosine], axis=1),
        sine=jnp.concatenate([-sine, sine], axis=1),
    )


HALVES = 2
DENSE_TILE = 1024


def matrix_rows(values):
    return values.reshape(values.shape[0] * values.shape[1], values.shape[2])


def cut_tiles(width, tile):
    return [(low, min(low + tile, width)) for low in range(0, width, tile)]


def spread_kernel(masks, count, chosen_ref, *rest):
    halves, weights = rest[: 2 * len(masks)], rest[2 * len(masks) : 2 * len(masks) + count]
    out_ref, narrow_ref, out_tile, narrow, sems = rest[-5:]
    rows = halves[0].shape[0]
    shards = weights[0].shape[0]
    depth = shards // HALVES
    lower = weights[-1].shape[2] - LANES
    copies = []
    for at, mask in enumerate(masks):
        left_ref, right_ref = halves[2 * at : 2 * at + 2]
        here = pl.ds(pl.multiple_of((lax.axis_index("col") ^ mask) * rows, rows), rows)

        def through(ref, low, high):
            return dot(left_ref[...], matrix_rows(ref[:depth, :rows, low:high]), (1, 0)) + dot(
                right_ref[...], matrix_rows(ref[depth:, :rows, low:high]), (1, 0)
            )

        def send(tile, target):
            copies.append(pltpu.make_async_copy(tile, target, sems.at[len(copies)]))
            copies[-1].start()

        narrow[at] = (chosen_ref[here, :] * through(weights[-1], lower, lower + LANES)).astype(BFLOAT)
        send(narrow.at[at], narrow_ref.at[here, :])
        column = 0
        for ref in weights:
            for low, high in cut_tiles(ref.shape[2] - (LANES if ref is weights[-1] else 0), DENSE_TILE):
                span = slice(column, column + high - low)
                column += high - low
                raised = matrix_rows(ref[:, rows : rows + NADAPT * RANK // shards, low:high])
                out_tile[at, :, span] = (through(ref, low, high) + dot(narrow[at], raised, (1, 0))).astype(BFLOAT)
                send(out_tile.at[at, :, span], out_ref.at[here, span])
    for copy in copies:
        copy.wait()


def weights_width(gathered):
    return sum(part.shape[2] for part in gathered) - LANES


def spread_blocks(blocks, gathered, selector, held):
    masks = [mask for mask, _ in blocks]
    rows, half = blocks[0][1][0].shape
    width = weights_width(gathered)
    total = selector.shape[0]
    fast, free = pl.BlockSpec(memory_space=pltpu.VMEM), pl.BlockSpec(memory_space=pl.ANY)
    operands = [selector, *[part for _, halves in blocks for part in halves], *gathered]
    in_specs = [fast] * len(operands)
    aliases = {}
    if held is not None:
        aliases = {len(operands): 0, len(operands) + 1: 1}
        operands += list(held)
        in_specs += [free] * 2
    copies = len(masks) * (1 + sum(-(-part.shape[2] // DENSE_TILE) for part in gathered))
    return pl.pallas_call(
        functools.partial(spread_kernel, masks, len(gathered)),
        in_specs=in_specs,
        out_specs=[free] * 2,
        out_shape=[
            jax.ShapeDtypeStruct((total, width), BFLOAT),
            jax.ShapeDtypeStruct((total, LANES), BFLOAT),
        ],
        scratch_shapes=[
            pltpu.VMEM((len(masks), rows, width), BFLOAT),
            pltpu.VMEM((len(masks), rows, LANES), BFLOAT),
            pltpu.SemaphoreType.DMA((copies,)),
        ],
        input_output_aliases=aliases,
        compiler_params=pltpu.CompilerParams(vmem_limit_bytes=DENSE_BYTES),
        cost_estimate=estimate(
            flops=4 * len(masks) * rows * half * (width + LANES),
            bytes_accessed=2 * len(masks) * rows * (2 * half + width),
            transcendentals=0,
        ),
        name="spread_blocks",
    )(*operands)


def collect_kernel(masks, count, values_ref, *refs):
    weights, outs = refs[:count], refs[count:]
    rows = values_ref.shape[0] // 4
    shards = weights[0].shape[0]
    half = shards // HALVES * rows
    width = values_ref.shape[1]
    starts, column = [], 0
    for ref in weights:
        high = min(column + ref.shape[2], width)
        starts.append((column, high))
        column = high
    for at, mask in enumerate(masks):
        here = pl.ds(pl.multiple_of((lax.axis_index("col") ^ mask) * rows, rows), rows)
        first, second = outs[2 * at], outs[2 * at + 1]

        def through(cut):
            total = None
            for (low, high), ref in zip(starts, weights):
                part = dot(values_ref[here, low:high], cut(ref, high - low), (1, 1))
                total = part if total is None else total + part
            return total

        for shard in range(shards):
            out_ref = first if shard < shards // HALVES else second
            column = shard * rows % half
            out_ref[:, column : column + rows] = through(lambda ref, wide: ref[shard, :rows, :wide]).astype(
                out_ref.dtype
            )
        first[:, half:] = through(
            lambda ref, wide: matrix_rows(ref[:, rows : rows + NADAPT * RANK // shards, :wide])
        ).astype(first.dtype)


def collect_blocks(masks, values, gathered, types):
    rows = values.shape[0] // 4
    half = gathered[0].shape[0] // HALVES * rows
    fast = pl.BlockSpec(memory_space=pltpu.VMEM)
    out_shape = []
    for pair in types:
        out_shape.append(jax.ShapeDtypeStruct((rows, half + LANES), pair[0]))
        out_shape.append(jax.ShapeDtypeStruct((rows, half), pair[1]))
    outs = pl.pallas_call(
        functools.partial(collect_kernel, masks, len(gathered)),
        in_specs=[fast] * (1 + len(gathered)),
        out_specs=[fast] * len(out_shape),
        out_shape=out_shape,
        compiler_params=pltpu.CompilerParams(vmem_limit_bytes=DENSE_BYTES),
        cost_estimate=estimate(
            flops=4 * len(masks) * rows * half * values.shape[1],
            bytes_accessed=2 * len(masks) * rows * (values.shape[1] + 4 * half),
            transcendentals=0,
        ),
        name="collect_blocks",
    )(values, *gathered)
    return [tuple(outs[2 * at : 2 * at + 2]) for at in range(len(masks))]


def root_mean(values):
    return lax.rsqrt(jnp.mean(values * values, axis=1, keepdims=True) + EPSILON)


def packed_grad(narrow, values, choose):
    half = LANES // 2
    chosen = dot(narrow, choose, (1, 0)).astype(BFLOAT)
    grad = dot(chosen, values, (0, 0))
    low = lax.broadcasted_iota(jnp.int32, (8, LANES), 1) < half
    devices = []
    for start in range(0, grad.shape[1], LANES):
        own = grad[:, start : start + LANES]
        turned_own = pltpu.roll(own, half, 1)
        for first, second in ((own, turned_own), (turned_own, own)):
            devices.append(
                jnp.concatenate(
                    [jnp.where(low, first[at : at + 8], second[at + 8 : at + 16]) for at in (0, 16)], axis=1
                )
            )
    return jnp.concatenate(devices, axis=0).astype(BFLOAT)


def finish_kernel(kind, first_own, first_near, first_far, second_own, second_near, second_far, lower_ref, chosen_ref,
                  *refs):
    half = second_own.shape[1]
    model = HALVES * half
    wide = lambda ref: ref[...].astype(FLOAT)
    first = wide(first_own) + wide(first_near) + wide(first_far)
    second = wide(second_own) + wide(second_near) + wide(second_far)
    inner = (chosen_ref[...] * first[:, half:]).astype(BFLOAT)
    summed = jnp.concatenate([first[:, :half], second], axis=1) + dot(
        inner, matrix_rows(lower_ref[...]), (1, 1)
    )
    if kind == "output":
        residual_ref, place_ref, choose_ref, branch_ref, early_ref, out_ref = refs
        result = (residual_ref[...] + summed).astype(BFLOAT)
        out_ref[:, :model] = dot(place_ref[...], result, (0, 0)).astype(BFLOAT)
        out_ref[:, model : model + 2 * LANES] = packed_grad(inner, branch_ref[...], choose_ref[...])
        out_ref[:, model + 2 * LANES :] = early_ref[...]
        return
    if kind == "forward":
        residual_ref, gain_ref, out_ref, inner_ref, left_ref, right_ref = refs
        hidden = residual_ref[...] + summed
        normed = (hidden * root_mean(hidden) * gain_ref[0:1, :]).astype(BFLOAT)
    else:
        values_ref, upstream_ref, gain_ref, choose_ref, normed_left, normed_right = refs[:6]
        values = values_ref[...]
        scale = root_mean(values)
        weighted = summed * gain_ref[0:1, :]
        mean = jnp.mean(weighted * values, axis=1, keepdims=True)
        hidden = upstream_ref[...].astype(FLOAT) + scale * weighted - values * (scale * scale * scale * mean)
        normed = hidden.astype(BFLOAT)
        packed = packed_grad(
            inner, jnp.concatenate([normed_left[...], normed_right[...]], axis=1), choose_ref[...]
        )
        if kind == "input":
            place_ref, out_ref = refs[6:]
            out_ref[:, :model] = dot(place_ref[...], normed, (0, 0)).astype(BFLOAT)
            out_ref[:, model:] = packed
            return
        given_ref, out_ref, inner_ref, left_ref, right_ref, packed_ref = refs[6:]
        packed_ref[:, : 2 * LANES] = packed
        packed_ref[:, 2 * LANES :] = packed_grad(given_ref[...], normed, choose_ref[...])
    out_ref[...] = hidden
    inner_ref[...] = inner
    left_ref[...] = normed[:, :half]
    right_ref[...] = normed[:, half:]


def finish(kind, parts, gathered, own_selector, *operands):
    rows = own_selector.shape[0]
    half = parts[3].shape[1]
    shards = gathered[-1].shape[0]
    model = HALVES * half
    lower = gathered[-1][:, : model // shards, -LANES:]
    shaped = jax.ShapeDtypeStruct
    if kind in ("output", "input"):
        out_shape = shaped((rows, model + 2 * LANES * (3 if kind == "output" else 1)), BFLOAT)
        out_specs = whole(out_shape.shape)
    else:
        out_shape = [shaped((rows, model), FLOAT), shaped((rows, LANES), BFLOAT)]
        out_shape += [shaped((rows, half), BFLOAT)] * 2
        out_shape += [shaped((rows, 4 * LANES), BFLOAT)] * (kind == "backward")
        out_specs = [whole(shape.shape) for shape in out_shape]
    given = [*parts, lower, own_selector, *operands]
    return pl.pallas_call(
        functools.partial(finish_kernel, kind),
        grid=(1,),
        in_specs=[whole(value.shape) for value in given],
        out_specs=out_specs,
        out_shape=out_shape,
        compiler_params=pltpu.CompilerParams(vmem_limit_bytes=FINISH_BYTES),
        cost_estimate=estimate(
            flops=2 * rows * model * LANES, bytes_accessed=rows * model * 20, transcendentals=0
        ),
        name="finish_" + kind,
    )(*given)


def onward_kernel(first_kept, first_part, second_kept, second_part, first_ref, second_ref):
    first_ref[...] = (first_kept[...] + first_part[...].astype(FLOAT)).astype(BFLOAT)
    second_ref[...] = (second_kept[...] + second_part[...].astype(FLOAT)).astype(BFLOAT)


def sum_onward(first_kept, first_part, second_kept, second_part):
    return pl.pallas_call(
        onward_kernel,
        in_specs=[pl.BlockSpec(memory_space=pltpu.VMEM)] * 4,
        out_specs=[pl.BlockSpec(memory_space=pltpu.VMEM)] * 2,
        out_shape=[jax.ShapeDtypeStruct(part.shape, BFLOAT) for part in (first_part, second_part)],
        compiler_params=pltpu.CompilerParams(vmem_limit_bytes=DENSE_BYTES),
        name="sum_onward",
    )(first_kept, first_part, second_kept, second_part)


def send_kernel(target_column, target_row, tokens_ref, adapter_ref, sent_ref, matrix_ref):
    rows = tokens_ref.shape[0]
    model = tokens_ref.shape[1]
    peer = adapter_ref.shape[0]
    column, row = target_column[:, 0:1], target_row[0:1, :]
    earlier = lax.broadcasted_iota(jnp.int32, (rows, rows), 0) < lax.broadcasted_iota(jnp.int32, (rows, rows), 1)
    same = jnp.where((column // rows == row // rows) & earlier, 1.0, 0.0)
    place = (row // rows) * peer + jnp.sum(same, axis=0, keepdims=True).astype(jnp.int32)
    matrix = (lax.broadcasted_iota(jnp.int32, (rows, rows), 0) == place).astype(BFLOAT)
    matrix_ref[...] = matrix
    sent_ref[:, :model] = dot(matrix, tokens_ref[...], (1, 0)).astype(BFLOAT)
    lane = lax.broadcasted_iota(jnp.int32, (rows, LANES), 1)
    slots = jnp.where(lane == 0, column % rows, 0).astype(FLOAT).astype(BFLOAT)
    notes = dot(matrix, slots, (1, 0))
    sent_ref[:, model:] = jnp.where(lane == 0, notes, adapter_ref[0:1, :]).astype(BFLOAT)


def send_tokens(target, tokens, adapters, peer):
    rows, model = tokens.shape
    notes = jnp.pad(adapters.astype(FLOAT), (1, LANES - 1 - adapters.shape[0]))
    return pl.pallas_call(
        send_kernel,
        in_specs=[pl.BlockSpec(memory_space=pltpu.VMEM)] * 4,
        out_specs=[pl.BlockSpec(memory_space=pltpu.VMEM)] * 2,
        out_shape=[
            jax.ShapeDtypeStruct((rows, model + LANES), BFLOAT),
            jax.ShapeDtypeStruct((rows, rows), BFLOAT),
        ],
        compiler_params=pltpu.CompilerParams(vmem_limit_bytes=DENSE_BYTES),
        name="send_tokens",
    )(
        jnp.broadcast_to(target[:, None], (rows, LANES)),
        jnp.broadcast_to(target[None, :], (8, rows)),
        tokens,
        jnp.broadcast_to(notes[None, :], (peer, LANES)),
    )


def arrive_kernel(arrived_ref, gain_ref, own_ref, matrix_ref, left_ref, right_ref):
    rows, model = own_ref.shape
    slots = arrived_ref[:, model:].astype(FLOAT).T[0:1, :]
    row = lax.broadcasted_iota(jnp.int32, (rows, rows), 0).astype(FLOAT)
    matrix = (row == slots).astype(BFLOAT)
    matrix_ref[...] = matrix
    own = dot(matrix, arrived_ref[:, :model], (1, 0))
    own_ref[...] = own
    normed = (own * root_mean(own) * gain_ref[0:1, :]).astype(BFLOAT)
    left_ref[...] = normed[:, : model // HALVES]
    right_ref[...] = normed[:, model // HALVES :]


def arrive_tokens(arrived, gain):
    rows, model = arrived.shape[0], arrived.shape[1] - LANES
    return pl.pallas_call(
        arrive_kernel,
        in_specs=[pl.BlockSpec(memory_space=pltpu.VMEM)] * 2,
        out_specs=[pl.BlockSpec(memory_space=pltpu.VMEM)] * 4,
        out_shape=[
            jax.ShapeDtypeStruct((rows, model), FLOAT),
            jax.ShapeDtypeStruct((rows, rows), BFLOAT),
            jax.ShapeDtypeStruct((rows, model // HALVES), BFLOAT),
            jax.ShapeDtypeStruct((rows, model // HALVES), BFLOAT),
        ],
        compiler_params=pltpu.CompilerParams(vmem_limit_bytes=DENSE_BYTES),
        name="arrive_tokens",
    )(arrived, gain)


GATE_WIDTH = DSSM // QUERY_HEADS
PAIR_WIDTH = 2 * KEY_VALUE_HEADS * HEAD_SIZE // QUERY_HEADS
STATE_WIDTH = 2 * NSTATE // QUERY_HEADS
STEP_WIDTH = NH // QUERY_HEADS
ALL_AXES = ("row", "col")


def pad_columns(values, width):
    return jnp.pad(values, ((0, 0), (0, width - values.shape[1])))


def after(values, *earlier):
    return lax.optimization_barrier((values, *earlier))[0]


def after_all(values, *earlier):
    return lax.optimization_barrier((*values, *earlier))[: len(values)]


def unit_parts(values, units):
    cuts = [0]
    for width in (GATE_WIDTH, GATE_WIDTH, HEAD_SIZE, PAIR_WIDTH, STATE_WIDTH, STEP_WIDTH):
        cuts.append(cuts[-1] + width)
    return [
        jnp.concatenate(
            [values[:, unit * UNIT_IN + low : unit * UNIT_IN + high] for unit in range(units)], axis=1
        )
        for low, high in zip(cuts[:-1], cuts[1:])
    ]


def restore_units(parts, units):
    ordered = []
    for unit in range(units):
        for part in parts:
            width = part.shape[1] // units
            ordered.append(part[:, unit * width : (unit + 1) * width])
    return jnp.concatenate(ordered, axis=1)


def split_halves(values, units, first, axis):
    block = values.shape[axis] // units
    take = lambda low, high: lax.slice_in_dim(values, low, high, axis=axis)
    parts = [take(unit * block, unit * block + first) for unit in range(units)]
    parts += [take(unit * block + first, (unit + 1) * block) for unit in range(units)]
    return jnp.concatenate(parts, axis=axis)


def join_halves(values, units, first, axis):
    block = values.shape[axis] // units
    rest = block - first
    take = lambda low, high: lax.slice_in_dim(values, low, high, axis=axis)
    parts = []
    for unit in range(units):
        parts.append(take(unit * first, (unit + 1) * first))
        parts.append(take(units * first + unit * rest, units * first + (unit + 1) * rest))
    return jnp.concatenate(parts, axis=axis)


def quick(rows):
    return lax.axis_size("col") == 4 and lax.axis_size("row") == 8 and rows == 256


def spread_early(halves, gathered, selector):
    left, right = halves
    far_left, near_right = flip(left, 2), flip(right, 1)
    near_left, far_right = flip(left, 1), flip(right, 2)
    held = spread_blocks([(0, halves)], gathered, selector, None)
    onward_left, onward_right = after_all((far_left, near_right), held[1])
    corner = flip(onward_left, 1), flip(onward_right, 2)
    held = spread_blocks([(1, (near_left, near_right))], gathered, selector, held)
    held = spread_blocks([(2, (far_left, far_right))], gathered, selector, held)
    return spread_blocks([(3, corner)], gathered, selector, held)


def flip(values, mask):
    return lax.ppermute(values, "col", [(i, i ^ mask) for i in range(4)])


def gather_blocks(halves):
    left, right = halves
    far_left, near_right = flip(left, 2), flip(right, 1)
    near_left, far_right = flip(left, 1), flip(right, 2)
    corner_left, corner_right = flip(far_left, 1), flip(near_right, 2)
    return [
        (0, (left, right)),
        (1, (near_left, near_right)),
        (2, (far_left, far_right)),
        (3, (corner_left, corner_right)),
    ]


def rows_of(values, block, rows):
    return lax.dynamic_slice_in_dim(values, block * rows, rows, 0)


def spread_gathered(blocks, gathered, selector):
    held = None
    for block in blocks:
        held = spread_blocks([block], gathered, selector, held)
    return held


def spread_project(halves, gathered, selector):
    rows = halves[0].shape[0]
    if quick(rows):
        return spread_gathered(gather_blocks(halves), gathered, selector)
    wide, narrow_factor = gathered
    width = narrow_factor.shape[1]
    both = product(lax.all_gather(jnp.concatenate(halves, axis=1), "col", axis=0, tiled=True), wide)
    narrow = (selector * both[:, width:]).astype(BFLOAT)
    return (both[:, :width] + product(narrow, narrow_factor)).astype(BFLOAT), narrow


PIECE_TYPES = [(BFLOAT, BFLOAT), (BFLOAT, FLOAT), (FLOAT, BFLOAT), (FLOAT, FLOAT)]


def collect_pieces(values, gathered, at_once):
    if at_once:
        return collect_blocks([3, 1, 2, 0], values, gathered, PIECE_TYPES)
    (corner,) = collect_blocks([3], values, gathered, PIECE_TYPES[:1])
    values = after(values, corner[0])
    return [corner, *collect_blocks([1, 2, 0], values, gathered, PIECE_TYPES[1:])]


def collect_send(pieces, ordered=True):
    corner, near, far, own = pieces
    arriving = flip(corner[0], 1), flip(corner[1], 2)
    sent_near, sent_far = after_all((near[0], far[1]), *arriving) if ordered else (near[0], far[1])
    return own, flip(sent_near, 1), flip(sent_far, 2), far[0], near[1], arriving


def collect_middle(started):
    own, near_first, far_second, far_first, near_second, arriving = started
    return (own, near_first, far_second), sum_onward(far_first, arriving[0], near_second, arriving[1])


def collect_onward(onward):
    return flip(onward[0], 2), flip(onward[1], 1)


def collect_end(kept, last, kind, gathered, own_selector, *operands):
    own, near_first, far_second = kept
    parts = [own[0], near_first, last[0], own[1], far_second, last[1]]
    return finish(kind, parts, gathered, own_selector, *operands)


def collect_project(values, gathered, kind, own_selector, *operands):
    rows, model = own_selector.shape[0], operands[0].shape[1]
    if quick(rows):
        kept, onward = collect_middle(collect_send(collect_pieces(values, gathered, False)))
        return collect_end(kept, collect_onward(onward), kind, gathered, own_selector, *operands)
    wide, narrow_factor = gathered
    width = narrow_factor.shape[1]
    partial = jnp.concatenate(
        [contract_last(values, wide[:, :width]), contract_last(values, narrow_factor)], axis=1
    ).astype(BFLOAT)
    summed = lax.psum_scatter(partial, "col", scatter_dimension=0, tiled=True).astype(FLOAT)
    inner = (own_selector * summed[:, model:]).astype(BFLOAT)
    summed = summed[:, :model] + contract_last(inner, wide[:, width:])
    if kind == "output":
        return (operands[0] + summed).astype(BFLOAT), inner
    if kind == "forward":
        residual, gain = operands
        hidden = residual + summed
        return hidden, inner, *cut_halves(rms_norm(hidden, gain[0]).astype(BFLOAT))
    values, upstream, gain = operands
    _, back = jax.vjp(lambda given: rms_norm(given, gain[0]), values)
    hidden = upstream.astype(FLOAT) + back(summed)[0]
    if kind == "input":
        return hidden.astype(BFLOAT), inner
    return hidden, inner, *cut_halves(hidden.astype(BFLOAT))


def cut_halves(values):
    half = values.shape[1] // HALVES
    return values[:, :half], values[:, half:]


def local(
    tokens_in,
    cotangent,
    target,
    sequence_lengths,
    sequence_adapter,
    norm_gains,
    weight_in,
    conv_values,
    conv_states,
    scan_params,
    weight_mix,
    weight_feed,
    weight_down,
    in_lower,
    in_raise,
    mix_lower,
    mix_raise,
    feed_lower,
    feed_raise,
    down_lower,
    down_raise,
):
    cols = lax.axis_size("col")
    rows_axis = lax.axis_size("row")
    col = lax.axis_index("col")
    devices = cols * rows_axis
    rows = tokens_in.shape[0]
    model = tokens_in.shape[1]
    total = rows * cols
    units = QUERY_HEADS // cols
    channels = units * GATE_WIDTH
    peer = rows // devices
    lengths, adapters = sequence_lengths[0], sequence_adapter[0]
    sequences = lengths.shape[0]
    fast = quick(rows)
    key_head = col * units // (QUERY_HEADS // KEY_VALUE_HEADS)
    exchange = lambda values: lax.all_to_all(values, ALL_AXES, split_axis=0, concat_axis=0, tiled=True)

    sent, send_matrix = send_tokens(target, tokens_in, adapters, peer)
    shards = []

    def gather_weight(weight, lower, raised):
        top = jnp.concatenate([weight, lower], axis=1)
        if fast:
            bottom = pad_columns(raised, top.shape[1])
            shards.append(jnp.concatenate([top, bottom], axis=0))
            return (lax.all_gather(shards[-1], "row", axis=0),)
        wide = lax.all_gather(top, "row", axis=0, tiled=True)
        return wide, lax.all_gather(raised, "row", axis=0, tiled=True)

    depth = weight_in.shape[0]
    height = depth + in_raise.shape[0]
    given = after(jnp.concatenate([weight_in, in_raise], axis=0), send_matrix)
    gates, convs, queries, pairs, states, steps = unit_parts(given, units)
    pair_width, state_width = pairs.shape[1], states.shape[1]
    taps = jnp.concatenate([jnp.zeros((KCONV + 1, pair_width), BFLOAT), conv_states], axis=1)
    taps = jnp.pad(taps, ((0, 16 - KCONV - 1), (0, 0)))
    shared = jnp.concatenate([jnp.concatenate([pairs, states], axis=1), taps], axis=0)
    own_columns = jnp.concatenate([gates, convs, queries, pad_columns(steps, LANES)], axis=1)
    if fast:
        shared_shard = shared
        shared = lax.all_gather(shared_shard, "row", axis=0)
        weights_own = gather_weight(own_columns[:depth], in_lower, own_columns[depth:])
    arrived = exchange(sent)
    gains = jnp.broadcast_to(norm_gains.astype(FLOAT)[:, None, :], (2, 8, model))
    if fast:
        near, far = flip(shared, 1), flip(shared, 2)
        arrived = after(arrived, near, far, shards[0])
    own_input, place_matrix, *normed_one = arrive_tokens(arrived.reshape(rows, model + LANES), gains[0])
    blocks_one = gather_blocks(normed_one) if fast else normed_one
    if fast:
        held = jnp.zeros((cols,) + shared.shape, BFLOAT)
        for block, values in ((col, shared), (col ^ 1, near), (col ^ 2, far)):
            held = lax.dynamic_update_index_in_dim(held, values, block, 0)
        split = shared.shape[0] // 2
        corner = jnp.concatenate([flip(near[:split], 2), flip(far[split:], 1)], axis=0)
        held = lax.dynamic_update_index_in_dim(held, corner, col ^ 3, 0)
    else:
        held = lax.all_gather(shared, "col", axis=0)
    all_pairs = jnp.concatenate([held[at, ..., :height, :pair_width] for at in range(cols)], axis=-1)
    pick = lambda start: lax.select_n(
        key_head,
        *[all_pairs[..., start + at * HEAD_SIZE : start + (at + 1) * HEAD_SIZE] for at in range(KEY_VALUE_HEADS)],
    )
    shared_columns = jnp.concatenate(
        [held[at, ..., :height, pair_width:] for at in range(cols)]
        + [pick(0), pick(KEY_VALUE_HEADS * HEAD_SIZE)],
        axis=-1,
    )
    tap_rows = held[:, 0] if fast else held
    all_taps = jnp.concatenate(
        [tap_rows[at, height : height + KCONV + 1, pair_width:] for at in range(cols)], axis=1
    )
    if fast:
        weights_in = (shared_columns, *weights_own)
    else:
        columns = jnp.concatenate([shared_columns, own_columns], axis=1)
        weights_in = gather_weight(columns[:depth], in_lower, columns[depth:])
    weights_mix = gather_weight(
        after(split_halves(weight_mix, units, GATE_WIDTH, 0).T, sent),
        mix_raise.T,
        split_halves(mix_lower, units, GATE_WIDTH, 0).T,
    )
    weights_feed = gather_weight(
        after(split_halves(weight_feed, units, UNIT_FF, 1), arrived),
        feed_lower,
        split_halves(feed_raise, units, UNIT_FF, 1),
    )

    source_adapters = arrived.reshape(rows, model + LANES)[::peer, model + 1 : model + 1 + sequences].astype(jnp.int32)
    segment, position, selector = sequence_tables(lengths, adapters, total)
    own_selector = rows_of(selector, col, rows)
    own_segment = rows_of(segment, col, rows)
    tables = mixer_tables(lengths, segment, position, conv_values, all_taps, scan_params)

    def compact_grad(narrow, values):
        parts = [
            lax.dynamic_slice_in_dim(narrow, adapters[at] * RANK, RANK, 1)
            * (own_segment == at).astype(BFLOAT)[:, None]
            for at in range(sequences)
        ]
        grad = contract_first(jnp.concatenate(parts, axis=1), values).astype(BFLOAT)
        kept = sequences * RANK
        grad = grad.reshape(kept, devices, model // devices).transpose(1, 0, 2)
        return grad.reshape(devices, peer, kept * model // devices // peer)

    def expand_grad(dealt):
        kept = sequences * RANK
        dealt = dealt.reshape(devices * kept, model // devices)
        adapter_row = (source_adapters[:, :, None] * RANK + jnp.arange(RANK, dtype=jnp.int32)).reshape(-1)
        chosen = (jnp.arange(NADAPT * RANK, dtype=jnp.int32)[:, None] == adapter_row[None, :]).astype(BFLOAT)
        return product(chosen, dealt)

    def send_back(values, grads):
        back = contract_first(place_matrix, values).astype(BFLOAT).reshape(devices, peer, model)
        return exchange(jnp.concatenate([back, *grads], axis=2))

    def expand_packed(dealt, count):
        slots = dealt.shape[0] * peer
        block = jnp.arange(2 * LANES // (model // devices), dtype=jnp.int32)[:, None, None]
        row = jnp.arange(peer, dtype=jnp.int32)[None, None, :]
        place = block * peer + row
        adapter = jnp.where(place < RANK, source_adapters[None, :, 0:1], source_adapters[None, :, 1:2])
        adapter_row = (adapter * RANK + place % RANK).reshape(block.shape[0], 1, slots)
        chosen = (jnp.arange(NADAPT * RANK, dtype=jnp.int32)[None, :, None] == adapter_row).astype(BFLOAT)
        sums = product(chosen.reshape(-1, slots), dealt.reshape(slots, dealt.shape[2]))
        sums = sums.reshape(block.shape[0], NADAPT * RANK, dealt.shape[2])
        width = model // devices
        return [
            sum(
                sums[at, :, grad * 2 * LANES + at * width : grad * 2 * LANES + (at + 1) * width]
                for at in range(block.shape[0])
            )
            for grad in range(count)
        ]

    def take_back(dealt, count):
        returned = contract_first(send_matrix, dealt[:, :, :model].reshape(rows, model)).astype(BFLOAT)
        if fast:
            return returned, expand_packed(dealt[:, :, model:], count)
        width = (dealt.shape[2] - model) // count
        return returned, [
            expand_grad(dealt[:, :, model + at * width : model + (at + 1) * width]) for at in range(count)
        ]

    if fast:
        projected, inner_in = spread_blocks(blocks_one, weights_in, selector, None)
    else:
        projected, inner_in = spread_project(blocks_one, weights_in, selector)

    sent_grad = product(send_matrix, cotangent).astype(BFLOAT).reshape(devices, peer, model)
    arrived_grad = exchange(after(sent_grad, normed_one[0])).reshape(rows, model)
    branch_two = product(place_matrix, arrived_grad).astype(BFLOAT)
    weights_down = gather_weight(after(weight_down.T, projected), down_raise.T, down_lower.T)

    mixed_out = attention_forward(projected, tables)
    mixed_out, scanned, carried = scan_forward(projected, tables, mixed_out)
    hidden, inner_out, *normed_two = collect_project(mixed_out, weights_mix, "forward", own_selector, own_input, gains[1])
    gate_up, inner_feed = spread_project(normed_two, weights_feed, selector)
    branch_halves = cut_halves(after(branch_two, projected))
    if fast:
        act_grad, narrow_two = spread_blocks(gather_blocks(branch_halves), weights_down, selector, None)
    else:
        act_grad, narrow_two = spread_project(branch_halves, weights_down, selector)
    half_feed = units * UNIT_FF
    gate_part, up_part = gate_up[:, :half_feed].astype(FLOAT), gate_up[:, half_feed:].astype(FLOAT)
    gate = jax.nn.sigmoid(gate_part)
    silu = gate_part * gate
    activated = (silu * up_part).astype(BFLOAT)
    wide_grad = act_grad.astype(FLOAT)
    feed_grad = jnp.concatenate(
        [wide_grad * up_part * (gate * (1.0 + gate_part * (1.0 - gate))), wide_grad * silu], axis=1
    ).astype(BFLOAT)
    choose = (
        jnp.arange(NADAPT * RANK, dtype=jnp.int32)[:, None]
        == (adapters[:, None] * RANK + jnp.arange(RANK, dtype=jnp.int32)[None, :]).reshape(1, -1)
    ).astype(BFLOAT)
    if fast:
        pieces = collect_pieces(after(activated, feed_grad), weights_down, True)
        kept, onward = collect_middle(collect_send(collect_pieces(feed_grad, weights_feed, False)))
        hidden_grad, narrow_three, left, right, early_grads = collect_end(
            kept,
            collect_onward(onward),
            "backward",
            weights_feed,
            own_selector,
            after(hidden, pieces[3][0]),
            branch_two,
            gains[1],
            choose,
            *normed_two,
            inner_out,
        )
        mixed_grad, narrow_one = spread_early((left, right), weights_mix, selector)
    else:
        hidden_grad, narrow_three, *branch_one = collect_project(
            feed_grad, weights_feed, "backward", own_selector, hidden, branch_two, gains[1]
        )
        mixed_grad, narrow_one = spread_project(branch_one, weights_mix, selector)

    if fast:
        near_parts = after_all((*pieces[0], pieces[1][0], pieces[2][1]), mixed_grad)
        started = collect_send(
            [near_parts[:2], (near_parts[2], pieces[1][1]), (pieces[2][0], near_parts[3]), pieces[3]], False
        )
        attended_grads = attention_backward(projected, tables, after(mixed_grad, near_parts[0]))
        kept, onward = collect_middle((*started[:5], after_all(started[5], attended_grads[1])))
        scan_inputs = (projected, tables, scanned, carried, after(mixed_grad, *onward), attended_grads)
        scan_part = list(scan_backward(*scan_inputs, 0, 2, None))
        payload = collect_end(
            kept,
            collect_onward(onward),
            "output",
            weights_down,
            own_selector,
            after(hidden, scan_part[2]),
            place_matrix,
            choose,
            branch_two,
            early_grads,
        )
        dealt_out = exchange(payload.reshape(devices, peer, -1))
        scan_part[2] = after(scan_part[2], payload)
        projected_grad = scan_backward(*scan_inputs, 1, 2, scan_part)[0]
        raise_grad = contract_first(inner_in, projected_grad).astype(BFLOAT)
        projected_grad = after(projected_grad, raise_grad)
        started_in = collect_send(collect_pieces(projected_grad, weights_in, True))
        kept_in, onward_in = collect_middle(started_in)
    else:
        block_out, inner_down = collect_project(activated, weights_down, "output", own_selector, hidden)
        attended_grads = attention_backward(projected, tables, mixed_grad)
        projected_grad = scan_backward(
            projected, tables, scanned, carried, mixed_grad, attended_grads, 0, 1, None
        )[0]
        dealt_out = send_back(
            block_out,
            [
                compact_grad(inner_down, branch_two),
                compact_grad(narrow_three, jnp.concatenate(normed_two, axis=1)),
                compact_grad(inner_out, jnp.concatenate(branch_one, axis=1)),
            ],
        )

    def sum_rows(values):
        return lax.psum_scatter(values.astype(BFLOAT), "row", scatter_dimension=0, tiled=True).astype(FLOAT)

    early_parts = [
        contract_first(narrow_one, mixed_out),
        contract_first(inner_feed, feed_grad),
        contract_first(narrow_two, activated),
    ]
    early = sum_rows(jnp.concatenate(early_parts, axis=1))

    late = sum_rows(raise_grad if fast else contract_first(inner_in, projected_grad))

    if fast:
        payload = collect_end(
            kept_in,
            collect_onward(onward_in),
            "input",
            weights_in,
            own_selector,
            own_input,
            after(hidden_grad, dealt_out),
            gains[0],
            choose,
            *normed_one,
            place_matrix,
        )
        dealt_grad = exchange(payload.reshape(devices, peer, -1))
    else:
        input_grad, narrow_four = collect_project(
            projected_grad, weights_in, "input", own_selector, own_input, hidden_grad, gains[0]
        )
        dealt_grad = send_back(input_grad, [compact_grad(narrow_four, jnp.concatenate(normed_one, axis=1))])
        payload = input_grad
    dealt_out, early, late = after_all((dealt_out, early, late), payload)
    early_cuts = [0, early_parts[0].shape[1]]
    early_cuts.append(early_cuts[1] + early_parts[1].shape[1])
    grad_mix_lower = join_halves(early[:, : early_cuts[1]], units, GATE_WIDTH, 1).T
    grad_feed_raise = join_halves(early[:, early_cuts[1] : early_cuts[2]], units, UNIT_FF, 1)
    grad_down_lower = early[:, early_cuts[2] :].T

    key_columns = late[:, STATES : STATES + HEAD_SIZE]
    value_columns = late[:, STATES + HEAD_SIZE : STATES + PAIR]
    mine = [(key_head == at).astype(FLOAT) for at in range(KEY_VALUE_HEADS)]
    pair_grad = jnp.concatenate([part * here for part in (key_columns, value_columns) for here in mine], axis=1)
    stacked = jnp.stack(
        [
            jnp.concatenate(
                [
                    pair_grad[:, at * pair_width : (at + 1) * pair_width],
                    late[:, at * state_width : (at + 1) * state_width],
                ],
                axis=1,
            )
            for at in range(cols)
        ]
    )
    if fast:
        piece = lambda mask: lax.dynamic_index_in_dim(stacked, col ^ mask, 0, False)
        shared_sum = piece(0) + flip(piece(1), 1) + flip(piece(2), 2) + flip(piece(3), 3)
    else:
        shared_sum = lax.psum_scatter(
            stacked.reshape(stacked.shape[0] * stacked.shape[1], -1), "col", scatter_dimension=0, tiled=True
        )
    late = jnp.concatenate([shared_sum, late[:, STATES + PAIR :]], axis=1)
    shared_width = pair_width + state_width
    cuts = [shared_width]
    for width in (channels, channels, units * HEAD_SIZE, units * STEP_WIDTH):
        cuts.append(cuts[-1] + width)
    gate_columns, conv_columns, query_columns, step_columns = [
        late[:, low:high] for low, high in zip(cuts[:-1], cuts[1:])
    ]
    grad_in_raise = restore_units(
        [
            gate_columns,
            conv_columns,
            query_columns,
            late[:, :pair_width],
            late[:, pair_width:shared_width],
            step_columns,
        ],
        units,
    )

    returned_out, (grad_down_raise, grad_feed_lower, grad_mix_raise) = take_back(dealt_out, 3)
    returned_grad, (grad_in_lower,) = take_back(dealt_grad, 1)
    return (
        returned_out,
        returned_grad,
        grad_in_lower.T,
        grad_in_raise,
        grad_mix_lower,
        grad_mix_raise,
        grad_feed_lower.T,
        grad_feed_raise,
        grad_down_lower,
        grad_down_raise,
    )


def solution(mesh):
    in_specs = (
        P(("row", "col"), None),
        P(("row", "col"), None),
        P(("row", "col")),
        P("row", None),
        P("row", None),
        P(),
        P("row", "col"),
        P(None, "col"),
        P(None, "col"),
        P(None, "col"),
        P("col", "row"),
        P("row", "col"),
        P("col", "row"),
        P("row", None),
        P("row", "col"),
        P("col", "row"),
        P(None, "row"),
        P("row", None),
        P("row", "col"),
        P("col", "row"),
        P(None, "row"),
    )
    out_specs = (
        P(("row", "col"), None),
        P(("row", "col"), None),
        P(("row", "col"), None),
        P("row", "col"),
        P("col", "row"),
        P(None, ("row", "col")),
        P(("row", "col"), None),
        P("row", "col"),
        P("col", "row"),
        P(None, ("row", "col")),
    )
    return jax.shard_map(local, mesh=mesh, in_specs=in_specs, out_specs=out_specs, check_vma=False)
```

```python
import functools
import math

import jax
import jax.numpy as jnp
from jax import lax
from jax.experimental import pallas as pl
from jax.experimental.pallas import tpu as pltpu
from jax.sharding import PartitionSpec as P

NH = 48
HP = 64
NSTATE = 256
KCONV = 4
QUERY_HEADS = 8
KEY_VALUE_HEADS = 2
HEAD_SIZE = 128
RANK = 16
NADAPT = 8
SSD_BLOCK = 256
DSSM = 3072
UNIT_IN = 1030
UNIT_FF = 512


EPSILON = 1e-05
ROPE_BASE = 10000.0
NEGATIVE = -1e30
FLOAT = jnp.float32
BFLOAT = jnp.bfloat16


def product(left, right):
    return jnp.dot(left, right, preferred_element_type=FLOAT)


def contract_last(left, right):
    return lax.dot_general(left, right, (((1,), (1,)), ((), ())), preferred_element_type=FLOAT)


def contract_first(left, right):
    return lax.dot_general(left, right, (((0,), (0,)), ((), ())), preferred_element_type=FLOAT)


def rms_norm(values, gain):
    return values * lax.rsqrt(jnp.mean(values * values, axis=-1, keepdims=True) + EPSILON) * gain


def sequence_tables(lengths, adapters, sequence_length):
    sequence_count = lengths.shape[0]
    boundary = jnp.cumsum(lengths)
    token_index = jnp.arange(sequence_length, dtype=jnp.int32)
    passed = (token_index[:, None] >= boundary[None, :]).astype(jnp.int32)
    segment = jnp.sum(passed, axis=1)
    segment_start = jnp.sum(passed * lengths[None, :], axis=1)
    position = token_index - segment_start
    member = (segment[:, None] == jnp.arange(sequence_count, dtype=jnp.int32)[None, :]).astype(
        jnp.int32
    )
    chosen = jnp.sum(member * adapters[None, :], axis=1)
    column = jnp.arange(NADAPT * RANK, dtype=jnp.int32) // RANK
    selector = (chosen[:, None] == column[None, :]).astype(FLOAT)
    return (segment, position, selector)


ESTIMATE = 16
SCAN_BYTES = 32 * 1024 * 1024
DENSE_BYTES = 16 * 1024 * 1024
FINISH_BYTES = 32 * 1024 * 1024
LANES = 128


def whole(shape):
    return pl.BlockSpec(shape, lambda *_: (0,) * len(shape))


def estimate(flops, bytes_accessed, transcendentals):
    return pl.CostEstimate(
        flops=flops // ESTIMATE,
        bytes_accessed=bytes_accessed // ESTIMATE,
        transcendentals=transcendentals // ESTIMATE,
    )


def dot(left, right, contract):
    return lax.dot_general(left, right, ((contract[:1], contract[1:]), ((), ())), preferred_element_type=FLOAT)


def parts_of(values, count):
    parts = []
    for _ in range(count):
        part = values.astype(BFLOAT)
        parts.append(part)
        values = values - part.astype(FLOAT)
    return parts


def running_sum(values, triangle, contract):
    width = values.shape[1]
    split = dot(triangle, jnp.concatenate(parts_of(values, 3), axis=1), contract)
    return split[:, :width] + split[:, width : 2 * width] + split[:, 2 * width :]


def head_spread(values, expand):
    return dot(jnp.concatenate(parts_of(values, 2), axis=1), expand, (1, 0))


def head_sum(values, expand):
    high, low = parts_of(values, 2)
    single = expand[:LANES]
    return dot(high, single, (1, 1)) + dot(low, single, (1, 1))


def silu_parts(values):
    gate = 1.0 / (1.0 + jnp.exp(-values))
    return values * gate, gate


def expand_table(channels):
    row = lax.broadcasted_iota(jnp.int32, (2 * LANES, channels), 0) % LANES
    channel = lax.broadcasted_iota(jnp.int32, (2 * LANES, channels), 1) // HP
    return (row == channel).astype(BFLOAT)


def conv_sum(current_ref, before_ref, taps_ref, meta):
    rows = SSD_BLOCK
    current = current_ref[...].astype(FLOAT)
    window = jnp.concatenate([before_ref[...].astype(FLOAT)[8:16], current], axis=0)
    summed = taps_ref[KCONV : KCONV + 1, :] + current * taps_ref[0:1, :]
    for lag in range(1, KCONV):
        shifted = window[8 - lag : 8 - lag + rows]
        summed = summed + jnp.where(meta[:, 1:2] >= lag, shifted, 0.0) * taps_ref[lag : lag + 1, :]
    return summed


def conv_back(summed_grad, later, taps_ref, meta):
    rows = SSD_BLOCK
    window = jnp.concatenate([summed_grad, later[...]], axis=0)
    grad = summed_grad * taps_ref[0:1, :]
    for lag in range(1, KCONV):
        grad = grad + jnp.where(meta[:, 2:3] >= lag, window[lag : lag + rows], 0.0) * taps_ref[lag : lag + 1, :]
    later[...] = summed_grad[:8]
    return grad


def silu_slope(values, gate):
    return gate * (1.0 + values * (1.0 - gate))


def scan_block(
    conv_ref, before_ref, state_ref, state_before_ref, step_ref, meta_ref, segment_ref, taps_ref, state_taps_ref, head_ref,
    turned_over,
):
    rows = SSD_BLOCK
    channels = conv_ref.shape[1]
    meta = meta_ref[...]
    summed = conv_sum(conv_ref, before_ref, taps_ref, meta)
    activated, conv_gate = silu_parts(summed)
    wide_inputs = activated.astype(BFLOAT).astype(FLOAT)
    state_summed = conv_sum(state_ref, state_before_ref, state_taps_ref, meta)
    state_values, state_gate = silu_parts(state_summed)
    write = state_values[:, :NSTATE].astype(BFLOAT)
    read = state_values[:, NSTATE:].astype(BFLOAT)
    raw = step_ref[...].astype(FLOAT) + head_ref[0:1, :]
    steps = jnp.maximum(raw, 0.0) + jnp.log1p(jnp.exp(-jnp.abs(raw)))
    row = lax.broadcasted_iota(jnp.int32, (rows, rows), 0)
    column = lax.broadcasted_iota(jnp.int32, (rows, rows), 1)
    triangle = (row >= column).astype(BFLOAT)
    total = running_sum(steps * head_ref[1:2, :], triangle, (1, 0))
    entered = jnp.exp(total) * meta[:, 3:4]
    leaving = jnp.exp(total[rows - 1 : rows] - total) * meta[:, 4:5]
    expand = expand_table(channels)
    spread = head_spread(jnp.concatenate([steps, entered, leaving * steps], axis=0), expand)
    ordered = row <= column if turned_over else row >= column
    blocked = jnp.where(ordered & (meta[:, 0:1] == segment_ref[0:1, :]), 0.0, NEGATIVE)
    return dict(
        summed=summed,
        conv_gate=conv_gate,
        state_summed=state_summed,
        state_gate=state_gate,
        write=write,
        read=read,
        wide_inputs=wide_inputs,
        raw=raw,
        steps=steps,
        triangle=triangle,
        total=total,
        total_rows=total.T,
        leaving=leaving,
        expand=expand,
        steps_wide=spread[:rows],
        entered_wide=spread[rows : 2 * rows],
        tail_wide=spread[2 * rows :],
        stepped=(wide_inputs * spread[:rows]).astype(BFLOAT),
        tailed=(wide_inputs * spread[2 * rows :]).astype(BFLOAT),
        blocked=blocked,
        crossing=dot(write, read, (1, 1)) if turned_over else dot(read, write, (1, 1)),
    )


def decay_of(block, head):
    difference = block["total"][:, head : head + 1] - block["total_rows"][head : head + 1, :]
    return jnp.exp(difference + block["blocked"])


def turned_decay_of(block, head):
    difference = block["total_rows"][head : head + 1, :] - block["total"][:, head : head + 1]
    return jnp.exp(difference + block["blocked"])


def scan_forward_kernel(
    gate_ref, conv_ref, before_ref, state_ref, state_before_ref, step_ref, meta_ref, segment_ref, taps_ref,
    state_taps_ref, head_ref, skip_ref, mixed_ref, out_ref, scanned_ref, states_ref, state,
):
    del mixed_ref

    @pl.when(pl.program_id(0) == 0)
    def _():
        state[...] = jnp.zeros_like(state)

    block = scan_block(
        conv_ref, before_ref, state_ref, state_before_ref, step_ref, meta_ref, segment_ref, taps_ref, state_taps_ref,
        head_ref, False,
    )
    heads = conv_ref.shape[1] // HP
    carried = state[...].astype(BFLOAT)
    states_ref[0] = carried
    across = dot(block["read"], carried, (1, 0)) * block["entered_wide"]
    within = []
    for head in range(heads):
        weights = (block["crossing"] * decay_of(block, head)).astype(BFLOAT)
        within.append(dot(weights, block["stepped"][:, head * HP : (head + 1) * HP], (1, 0)))
    scanned = across + jnp.concatenate(within, axis=1)
    scanned_ref[...] = scanned
    gated, _ = silu_parts(gate_ref[...].astype(FLOAT))
    out_ref[...] = ((scanned + skip_ref[0:1, :] * block["wide_inputs"]) * gated).astype(BFLOAT)
    state[...] = state[...] * block["entered_wide"][SSD_BLOCK - 1 : SSD_BLOCK, :] + dot(
        block["write"], block["tailed"], (0, 0)
    )


def scan_backward_kernel(
    gate_ref, conv_ref, before_ref, state_ref, state_before_ref, step_ref, meta_ref, segment_ref, taps_ref,
    state_taps_ref, head_ref, skip_ref, scanned_ref, states_ref, grad_ref, query_grad_ref, shared_grad_ref, *rest,
):
    out_ref, *running = rest[-4:]
    state_grad, later, state_later = running

    @pl.when(pl.program_id(0) == 0)
    def _():
        for at, ref in enumerate(running):
            ref[...] = rest[1 + at][...] if len(rest) > 4 else jnp.zeros_like(ref)

    block = scan_block(
        conv_ref, before_ref, state_ref, state_before_ref, step_ref, meta_ref, segment_ref, taps_ref, state_taps_ref,
        head_ref, True,
    )
    rows = SSD_BLOCK
    channels = conv_ref.shape[1]
    heads = channels // HP
    meta = meta_ref[...]
    read, write = block["read"], block["write"]
    inputs = block["wide_inputs"]
    scanned = scanned_ref[...]
    skip = skip_ref[0:1, :]
    gate_values = gate_ref[...].astype(FLOAT)
    gated, gate = silu_parts(gate_values)
    grad = grad_ref[...].astype(FLOAT)
    gate_grad = grad * (scanned + skip * inputs) * silu_slope(gate_values, gate)
    out_grad = grad * gated
    inputs_grad = skip * out_grad
    rounded = out_grad.astype(BFLOAT)
    wide_rounded = rounded.astype(FLOAT)
    carried = states_ref[0]
    after = state_grad[...]
    after_rounded = after.astype(BFLOAT)

    from_state = dot(write, after_rounded, (1, 0))
    entering = (wide_rounded * block["entered_wide"]).astype(BFLOAT)
    write_grad = dot(block["tailed"], after_rounded, (1, 1))
    read_grad = dot(entering, carried, (1, 1))
    last_entered = block["entered_wide"][rows - 1 : rows, :]
    through = jnp.sum(after * carried.astype(FLOAT), axis=0, keepdims=True) * last_entered
    state_grad[...] = after * last_entered + dot(read, entering, (0, 0))

    crossing_grad = jnp.zeros((rows, rows), FLOAT)
    pulled = []
    for head in range(heads):
        span = slice(head * HP, (head + 1) * HP)
        decay = turned_decay_of(block, head)
        weights = (block["crossing"] * decay).astype(BFLOAT)
        pulled.append(dot(weights, rounded[:, span], (1, 0)))
        crossing_grad = crossing_grad + dot(block["stepped"][:, span], rounded[:, span], (1, 1)) * decay
    pulled = jnp.concatenate(pulled, axis=1)
    crossing_rounded = crossing_grad.astype(BFLOAT)
    read_grad = read_grad + dot(crossing_rounded, write, (0, 0))
    write_grad = write_grad + dot(crossing_rounded, read, (1, 0))

    inputs_grad = inputs_grad + block["steps_wide"] * pulled + block["tail_wide"] * from_state
    sums = head_sum(
        jnp.concatenate(
            [
                wide_rounded * scanned - block["stepped"].astype(FLOAT) * pulled,
                inputs * pulled,
                inputs * from_state,
                jnp.broadcast_to(through, (8, channels)),
            ],
            axis=0,
        ),
        block["expand"],
    )
    leaving_grad = sums[2 * rows : 3 * rows] * block["leaving"]
    leaving_total = leaving_grad * block["steps"]
    last = sums[3 * rows : 3 * rows + 1] + jnp.sum(leaving_total, axis=0, keepdims=True)
    total_grad = sums[:rows] - leaving_total
    total_grad = total_grad + jnp.where(
        lax.broadcasted_iota(jnp.int32, total_grad.shape, 0) == rows - 1, last, 0.0
    )
    decay_grad = running_sum(total_grad, block["triangle"], (0, 0))
    steps_grad = sums[rows : 2 * rows] + leaving_grad + decay_grad * head_ref[1:2, :]
    raw_grad = steps_grad / (1.0 + jnp.exp(-block["raw"]))
    raw_grad = jnp.where(lax.broadcasted_iota(jnp.int32, raw_grad.shape, 1) < heads, raw_grad, 0.0)

    state_slope = silu_slope(block["state_summed"], block["state_gate"])
    state_pre = conv_back(
        jnp.concatenate([write_grad, read_grad], axis=1) * state_slope, state_later, state_taps_ref, meta
    )
    conv_pre = conv_back(inputs_grad * silu_slope(block["summed"], block["conv_gate"]), later, taps_ref, meta)
    out_ref[:, : 2 * NSTATE] = state_pre.astype(BFLOAT)
    start = 2 * NSTATE + 2 * HEAD_SIZE
    end = out_ref.shape[1] - LANES
    out_ref[:, 2 * NSTATE : start] = shared_grad_ref[...]
    out_ref[:, start + 2 * channels : end] = query_grad_ref[...]
    out_ref[:, start : start + channels] = gate_grad.astype(BFLOAT)
    out_ref[:, start + channels : start + 2 * channels] = conv_pre.astype(BFLOAT)
    out_ref[:, end:] = raw_grad.astype(BFLOAT)


STATES = 2 * NSTATE
PAIR = 2 * HEAD_SIZE


def scan_specs(channels, order):
    half = SSD_BLOCK // 16
    before = lambda i: jnp.maximum(order(i) * half - 1, 0)
    gate_at = (STATES + PAIR) // channels
    step_at = (STATES + PAIR + 2 * channels + channels * QUERY_HEADS // DSSM * HEAD_SIZE) // LANES
    return [
        pl.BlockSpec((SSD_BLOCK, channels), lambda i: (order(i), gate_at)),
        pl.BlockSpec((SSD_BLOCK, channels), lambda i: (order(i), gate_at + 1)),
        pl.BlockSpec((16, channels), lambda i: (before(i), gate_at + 1)),
        pl.BlockSpec((SSD_BLOCK, STATES), lambda i: (order(i), 0)),
        pl.BlockSpec((16, STATES), lambda i: (before(i), 0)),
        pl.BlockSpec((SSD_BLOCK, LANES), lambda i: (order(i), step_at)),
        pl.BlockSpec((SSD_BLOCK, LANES), lambda i: (order(i), 0)),
        pl.BlockSpec((8, SSD_BLOCK), lambda i: (0, order(i))),
        whole((8, channels)),
        whole((8, STATES)),
        whole((8, LANES)),
        whole((8, channels)),
    ]


def scan_operands(projected, tables):
    return [projected] * 6 + [
        tables[name] for name in ("meta", "segment_row", "taps", "state_taps", "head", "skip")
    ]


def scan_cost(tokens, channels, factor):
    heads = channels // HP
    return estimate(
        flops=factor * 2 * tokens * SSD_BLOCK * (3 * channels + NSTATE),
        bytes_accessed=factor * tokens * channels * 12,
        transcendentals=tokens * SSD_BLOCK * heads,
    )


def scan_forward(projected, tables, mixed):
    tokens = projected.shape[0]
    channels = tables["taps"].shape[1]
    blocks = tokens // SSD_BLOCK
    return pl.pallas_call(
        scan_forward_kernel,
        grid=(blocks,),
        in_specs=scan_specs(channels, lambda i: i) + [pl.BlockSpec(memory_space=pl.ANY)],
        out_specs=[
            pl.BlockSpec((SSD_BLOCK, channels), lambda i: (i, 0)),
            pl.BlockSpec((SSD_BLOCK, channels), lambda i: (i, 0)),
            pl.BlockSpec((1, NSTATE, channels), lambda i: (i, 0, 0)),
        ],
        out_shape=[
            jax.ShapeDtypeStruct(mixed.shape, BFLOAT),
            jax.ShapeDtypeStruct((tokens, channels), FLOAT),
            jax.ShapeDtypeStruct((blocks, NSTATE, channels), BFLOAT),
        ],
        scratch_shapes=[pltpu.VMEM((NSTATE, channels), FLOAT)],
        input_output_aliases={12: 0},
        compiler_params=pltpu.CompilerParams(vmem_limit_bytes=SCAN_BYTES),
        cost_estimate=scan_cost(tokens, channels, 1),
        name="scan_forward",
    )(*scan_operands(projected, tables), mixed)


def scan_backward(projected, tables, scanned, carried, mixed_grad, attended_grads, part, parts, before):
    tokens, width = projected.shape
    channels = tables["taps"].shape[1]
    blocks = tokens // SSD_BLOCK
    last = blocks - 1 - part * (blocks // parts)
    back = lambda i: (last - i, 0)
    running = [(NSTATE, channels), (8, channels), (8, STATES)]
    query_grad, shared_grad = attended_grads
    operands = [*scan_operands(projected, tables), scanned, carried, mixed_grad, query_grad, shared_grad]
    in_specs = scan_specs(channels, lambda i: last - i) + [
        pl.BlockSpec((SSD_BLOCK, channels), back),
        pl.BlockSpec((1, NSTATE, channels), lambda i: (last - i, 0, 0)),
        pl.BlockSpec((SSD_BLOCK, channels), back),
        pl.BlockSpec((SSD_BLOCK, query_grad.shape[1]), back),
        pl.BlockSpec((SSD_BLOCK, PAIR), back),
    ]
    aliases = {}
    if before is not None:
        aliases = {len(operands): 0}
        operands += list(before)
        in_specs += [pl.BlockSpec(memory_space=pl.ANY), *[whole(shape) for shape in running]]
    return pl.pallas_call(
        scan_backward_kernel,
        grid=(blocks // parts,),
        in_specs=in_specs,
        out_specs=[pl.BlockSpec((SSD_BLOCK, width), back), *[whole(shape) for shape in running]],
        out_shape=[
            jax.ShapeDtypeStruct((tokens, width), BFLOAT),
            *[jax.ShapeDtypeStruct(shape, FLOAT) for shape in running],
        ],
        input_output_aliases=aliases,
        compiler_params=pltpu.CompilerParams(vmem_limit_bytes=SCAN_BYTES),
        cost_estimate=scan_cost(tokens, channels, 2),
        name="scan_backward",
    )(*operands)


def turned(values, cosine, sine):
    return (values * cosine + pltpu.roll(values, HEAD_SIZE // 2, 1) * sine).astype(BFLOAT)


def turned_back(values, cosine, sine):
    return values * cosine + pltpu.roll(values * sine, HEAD_SIZE // 2, 1)


ATT_ROWS = 256


def attention_mask(meta_ref, segment_ref, start, extent):
    row = start + lax.broadcasted_iota(jnp.int32, (ATT_ROWS, extent), 0)
    column = lax.broadcasted_iota(jnp.int32, (ATT_ROWS, extent), 1)
    return (row >= column) & (meta_ref[start : start + ATT_ROWS, 0:1] == segment_ref[0:1, :extent])


def probabilities(query, keys, allowed):
    score = dot(query, keys, (1, 1)) * (1.0 / math.sqrt(HEAD_SIZE))
    score = jnp.where(allowed, score, NEGATIVE)
    exponent = jnp.exp(score - jnp.max(score, axis=1, keepdims=True))
    return exponent / jnp.sum(exponent, axis=1, keepdims=True)


def attention_forward_kernel(query_ref, key_ref, value_ref, cosine_ref, sine_ref, meta_ref, segment_ref, out_ref, keys):
    tokens = key_ref.shape[0]
    keys[...] = turned(key_ref[...].astype(FLOAT), cosine_ref[...], sine_ref[...])
    for start in range(0, tokens, ATT_ROWS):
        extent = start + ATT_ROWS
        here = slice(start, extent)
        allowed = attention_mask(meta_ref, segment_ref, start, extent)
        for unit in range(query_ref.shape[1] // HEAD_SIZE):
            span = slice(unit * HEAD_SIZE, (unit + 1) * HEAD_SIZE)
            query = turned(query_ref[here, span].astype(FLOAT), cosine_ref[here], sine_ref[here])
            weights = probabilities(query, keys[:extent], allowed).astype(BFLOAT)
            out_ref[here, span] = dot(weights, value_ref[:extent], (1, 0)).astype(BFLOAT)


def attention_backward_kernel(
    query_ref, key_ref, value_ref, cosine_ref, sine_ref, meta_ref, segment_ref, grad_ref,
    query_grad_ref, shared_grad_ref, keys, key_sum, value_sum,
):
    tokens = key_ref.shape[0]
    scale = 1.0 / math.sqrt(HEAD_SIZE)
    keys[...] = turned(key_ref[...].astype(FLOAT), cosine_ref[...], sine_ref[...])
    key_sum[...] = jnp.zeros_like(key_sum)
    value_sum[...] = jnp.zeros_like(value_sum)
    for start in range(0, tokens, ATT_ROWS):
        extent = start + ATT_ROWS
        here = slice(start, extent)
        allowed = attention_mask(meta_ref, segment_ref, start, extent)
        for unit in range(query_ref.shape[1] // HEAD_SIZE):
            span = slice(unit * HEAD_SIZE, (unit + 1) * HEAD_SIZE)
            query = turned(query_ref[here, span].astype(FLOAT), cosine_ref[here], sine_ref[here])
            weights = probabilities(query, keys[:extent], allowed)
            grad = grad_ref[here, span]
            weights_grad = dot(grad, value_ref[:extent], (1, 1))
            value_sum[:extent] += dot(weights.astype(BFLOAT), grad, (0, 0))
            mean_grad = jnp.sum(weights * weights_grad, axis=1, keepdims=True)
            score_grad = (weights * (weights_grad - mean_grad) * scale).astype(BFLOAT)
            query_grad = dot(score_grad, keys[:extent], (1, 0))
            key_sum[:extent] += dot(score_grad, query, (0, 0))
            query_grad_ref[here, span] = turned_back(query_grad, cosine_ref[here], sine_ref[here]).astype(BFLOAT)
    shared_grad_ref[:, :HEAD_SIZE] = turned_back(key_sum[...], cosine_ref[...], sine_ref[...]).astype(BFLOAT)
    shared_grad_ref[:, HEAD_SIZE:] = value_sum[...].astype(BFLOAT)


def attention_cost(tokens, width, factor):
    return estimate(
        flops=factor * 2 * tokens * tokens * width,
        bytes_accessed=factor * tokens * width * 8,
        transcendentals=tokens * tokens * width // (2 * HEAD_SIZE),
    )


def attention_specs(tokens, channels):
    width = channels * QUERY_HEADS // DSSM * HEAD_SIZE
    narrow = whole((tokens, HEAD_SIZE))
    return [
        pl.BlockSpec((tokens, width), lambda *_: (0, (STATES + PAIR + 2 * channels) // width)),
        pl.BlockSpec((tokens, HEAD_SIZE), lambda *_: (0, STATES // HEAD_SIZE)),
        pl.BlockSpec((tokens, HEAD_SIZE), lambda *_: (0, STATES // HEAD_SIZE + 1)),
        narrow,
        narrow,
        whole((tokens, LANES)),
        whole((8, tokens)),
    ]


def attention_operands(projected, tables):
    return [projected] * 3 + [tables[name] for name in ("cosine", "sine", "meta", "segment_row")]


def attention_forward(projected, tables):
    tokens = projected.shape[0]
    channels = tables["taps"].shape[1]
    width = channels * QUERY_HEADS // DSSM * HEAD_SIZE
    return pl.pallas_call(
        attention_forward_kernel,
        grid=(1,),
        in_specs=attention_specs(tokens, channels),
        out_specs=pl.BlockSpec((tokens, width), lambda *_: (0, channels // width)),
        out_shape=jax.ShapeDtypeStruct((tokens, channels + width), BFLOAT),
        scratch_shapes=[pltpu.VMEM((tokens, HEAD_SIZE), BFLOAT)],
        compiler_params=pltpu.CompilerParams(vmem_limit_bytes=SCAN_BYTES),
        cost_estimate=attention_cost(tokens, width, 1),
        name="attention_forward",
    )(*attention_operands(projected, tables))


def attention_backward(projected, tables, mixed_grad):
    tokens = projected.shape[0]
    channels = tables["taps"].shape[1]
    width = channels * QUERY_HEADS // DSSM * HEAD_SIZE
    return pl.pallas_call(
        attention_backward_kernel,
        grid=(1,),
        in_specs=attention_specs(tokens, channels)
        + [pl.BlockSpec((tokens, width), lambda *_: (0, channels // width))],
        out_specs=[whole((tokens, width)), whole((tokens, PAIR))],
        out_shape=[jax.ShapeDtypeStruct((tokens, width), BFLOAT), jax.ShapeDtypeStruct((tokens, PAIR), BFLOAT)],
        scratch_shapes=[
            pltpu.VMEM((tokens, HEAD_SIZE), BFLOAT),
            pltpu.VMEM((tokens, HEAD_SIZE), FLOAT),
            pltpu.VMEM((tokens, HEAD_SIZE), FLOAT),
        ],
        compiler_params=pltpu.CompilerParams(vmem_limit_bytes=SCAN_BYTES),
        cost_estimate=attention_cost(tokens, width, 3),
        name="attention_backward",
    )(*attention_operands(projected, tables), mixed_grad)


def mixer_tables(lengths, segment, position, conv_values, conv_states, scan_params):
    tokens = segment.shape[0]
    block = jnp.arange(tokens, dtype=jnp.int32) // SSD_BLOCK
    previous = jnp.concatenate([jnp.full((1,), -1, jnp.int32), segment[:-1]])
    first_previous = jnp.repeat(previous[::SSD_BLOCK], SSD_BLOCK)
    last_segment = jnp.repeat(segment[SSD_BLOCK - 1 :: SSD_BLOCK], SSD_BLOCK)
    length = jnp.sum(
        jnp.where(segment[:, None] == jnp.arange(lengths.shape[0], dtype=jnp.int32)[None, :], lengths[None, :], 0),
        axis=1,
    )
    columns = [
        segment,
        position,
        length - 1 - position,
        segment == first_previous,
        segment == last_segment,
    ]
    meta = jnp.stack([column.astype(FLOAT) for column in columns], axis=1)
    half_width = HEAD_SIZE // 2
    frequency = ROPE_BASE ** (-2.0 * jnp.arange(half_width, dtype=FLOAT) / HEAD_SIZE)
    angle = position.astype(FLOAT)[:, None] * frequency[None, :]
    cosine, sine = jnp.cos(angle), jnp.sin(angle)
    heads = scan_params.shape[1]
    head = jnp.stack([scan_params[0], -jnp.exp(scan_params[1]), scan_params[2]])
    return dict(
        meta=jnp.pad(meta, ((0, 0), (0, LANES - meta.shape[1]))),
        segment_row=jnp.broadcast_to(segment.astype(FLOAT)[None, :], (8, tokens)),
        taps=jnp.pad(conv_values.astype(FLOAT), ((0, 3), (0, 0))),
        state_taps=jnp.pad(conv_states.astype(FLOAT), ((0, 3), (0, 0))),
        head=jnp.pad(head, ((0, 5), (0, LANES - heads))),
        skip=jnp.broadcast_to(jnp.repeat(scan_params[2], HP)[None, :], (8, heads * HP)),
        cosine=jnp.concatenate([cosine, cosine], axis=1),
        sine=jnp.concatenate([-sine, sine], axis=1),
    )


HALVES = 2
DENSE_TILE = 1024


def matrix_rows(values):
    return values.reshape(values.shape[0] * values.shape[1], values.shape[2])


def cut_tiles(width, tile):
    return [(low, min(low + tile, width)) for low in range(0, width, tile)]


def spread_kernel(masks, count, times, chosen_ref, *rest):
    halves, weights = rest[: 2 * len(masks)], rest[2 * len(masks) : 2 * len(masks) + count]
    factors = rest[2 * len(masks) + count : 2 * len(masks) + count + times]
    out_ref, narrow_ref, out_tile, narrow, sems, factor_tile, factor_sems = rest[-7:]
    rows = halves[0].shape[0]
    shards = weights[0].shape[0]
    depth = shards // HALVES
    lower = weights[-1].shape[2] - LANES
    copies = []
    fetches = []
    for at, mask in enumerate(masks):
        here = pl.ds(pl.multiple_of((lax.axis_index("col") ^ mask) * rows, rows), rows)
        for place, factor in enumerate(factors):
            fetches.append(
                pltpu.make_async_copy(factor.at[here, :], factor_tile.at[at, place], factor_sems.at[at, place])
            )
            fetches[-1].start()
    for at, mask in enumerate(masks):
        left_ref, right_ref = halves[2 * at : 2 * at + 2]
        here = pl.ds(pl.multiple_of((lax.axis_index("col") ^ mask) * rows, rows), rows)

        def through(ref, low, high):
            return dot(left_ref[...], matrix_rows(ref[:depth, :rows, low:high]), (1, 0)) + dot(
                right_ref[...], matrix_rows(ref[depth:, :rows, low:high]), (1, 0)
            )

        def send(tile, target):
            copies.append(pltpu.make_async_copy(tile, target, sems.at[len(copies)]))
            copies[-1].start()

        narrow[at] = (chosen_ref[here, :] * through(weights[-1], lower, lower + LANES)).astype(BFLOAT)
        send(narrow.at[at], narrow_ref.at[here, :])
        column = 0
        for ref in weights:
            for low, high in cut_tiles(ref.shape[2] - (LANES if ref is weights[-1] else 0), DENSE_TILE):
                span = slice(column, column + high - low)
                column += high - low
                raised = matrix_rows(ref[:, rows : rows + NADAPT * RANK // shards, low:high])
                result = (through(ref, low, high) + dot(narrow[at], raised, (1, 0))).astype(BFLOAT)
                if not factors:
                    out_tile[at, :, span] = result
                    send(out_tile.at[at, :, span], out_ref.at[here, span])
                for place, factor in enumerate(factors):
                    if low == 0:
                        fetches[at * times + place].wait()
                    shift = place * factor.shape[1]
                    wide = slice(span.start + shift, span.stop + shift)
                    out_tile[at, :, wide] = (result.astype(FLOAT) * factor_tile[at, place, :, span]).astype(BFLOAT)
                    send(out_tile.at[at, :, wide], out_ref.at[here, wide])
    for copy in copies:
        copy.wait()


def weights_width(gathered):
    return sum(part.shape[2] for part in gathered) - LANES


def spread_blocks(blocks, gathered, selector, held, factors=()):
    masks = [mask for mask, _ in blocks]
    rows, half = blocks[0][1][0].shape
    width = weights_width(gathered)
    total = selector.shape[0]
    fast, free = pl.BlockSpec(memory_space=pltpu.VMEM), pl.BlockSpec(memory_space=pl.ANY)
    operands = [selector, *[part for _, halves in blocks for part in halves], *gathered]
    wide = width * max(len(factors), 1)
    in_specs = [fast] * len(operands) + [free] * len(factors)
    operands += list(factors)
    aliases = {}
    if held is not None:
        aliases = {len(operands): 0, len(operands) + 1: 1}
        operands += list(held)
        in_specs += [free] * 2
    tiles = sum(-(-part.shape[2] // DENSE_TILE) for part in gathered)
    copies = len(masks) * (1 + tiles * max(len(factors), 1))
    return pl.pallas_call(
        functools.partial(spread_kernel, masks, len(gathered), len(factors)),
        in_specs=in_specs,
        out_specs=[free] * 2,
        out_shape=[
            jax.ShapeDtypeStruct((total, wide), BFLOAT),
            jax.ShapeDtypeStruct((total, LANES), BFLOAT),
        ],
        scratch_shapes=[
            pltpu.VMEM((len(masks), rows, wide), BFLOAT),
            pltpu.VMEM((len(masks), rows, LANES), BFLOAT),
            pltpu.SemaphoreType.DMA((copies,)),
            pltpu.VMEM((len(masks), len(factors), rows, width) if factors else (1, 1, 8, LANES), FLOAT),
            pltpu.SemaphoreType.DMA((len(masks), max(len(factors), 1))),
        ],
        input_output_aliases=aliases,
        compiler_params=pltpu.CompilerParams(vmem_limit_bytes=FINISH_BYTES if factors else DENSE_BYTES),
        cost_estimate=estimate(
            flops=4 * len(masks) * rows * half * (width + LANES),
            bytes_accessed=2 * len(masks) * rows * (2 * half + width),
            transcendentals=0,
        ),
        name="spread_blocks",
    )(*operands)


def collect_kernel(masks, count, values_ref, *refs):
    weights, outs = refs[:count], refs[count:]
    rows = values_ref.shape[0] // 4
    shards = weights[0].shape[0]
    half = shards // HALVES * rows
    width = values_ref.shape[1]
    starts, column = [], 0
    for ref in weights:
        high = min(column + ref.shape[2], width)
        starts.append((column, high))
        column = high
    for at, mask in enumerate(masks):
        here = pl.ds(pl.multiple_of((lax.axis_index("col") ^ mask) * rows, rows), rows)
        first, second = outs[2 * at], outs[2 * at + 1]

        def through(cut):
            total = None
            for (low, high), ref in zip(starts, weights):
                part = dot(values_ref[here, low:high], cut(ref, high - low), (1, 1))
                total = part if total is None else total + part
            return total

        for shard in range(shards):
            out_ref = first if shard < shards // HALVES else second
            column = shard * rows % half
            out_ref[:, column : column + rows] = through(lambda ref, wide: ref[shard, :rows, :wide]).astype(
                out_ref.dtype
            )
        first[:, half:] = through(
            lambda ref, wide: matrix_rows(ref[:, rows : rows + NADAPT * RANK // shards, :wide])
        ).astype(first.dtype)


def collect_blocks(masks, values, gathered, types):
    rows = values.shape[0] // 4
    half = gathered[0].shape[0] // HALVES * rows
    fast = pl.BlockSpec(memory_space=pltpu.VMEM)
    out_shape = []
    for pair in types:
        out_shape.append(jax.ShapeDtypeStruct((rows, half + LANES), pair[0]))
        out_shape.append(jax.ShapeDtypeStruct((rows, half), pair[1]))
    outs = pl.pallas_call(
        functools.partial(collect_kernel, masks, len(gathered)),
        in_specs=[fast] * (1 + len(gathered)),
        out_specs=[fast] * len(out_shape),
        out_shape=out_shape,
        compiler_params=pltpu.CompilerParams(vmem_limit_bytes=DENSE_BYTES),
        cost_estimate=estimate(
            flops=4 * len(masks) * rows * half * values.shape[1],
            bytes_accessed=2 * len(masks) * rows * (values.shape[1] + 4 * half),
            transcendentals=0,
        ),
        name="collect_blocks",
    )(values, *gathered)
    return [tuple(outs[2 * at : 2 * at + 2]) for at in range(len(masks))]


def root_mean(values):
    return lax.rsqrt(jnp.mean(values * values, axis=1, keepdims=True) + EPSILON)


def packed_grad(narrow, values, choose):
    half = LANES // 2
    chosen = dot(narrow, choose, (1, 0)).astype(BFLOAT)
    grad = dot(chosen, values, (0, 0))
    low = lax.broadcasted_iota(jnp.int32, (8, LANES), 1) < half
    devices = []
    for start in range(0, grad.shape[1], LANES):
        own = grad[:, start : start + LANES]
        turned_own = pltpu.roll(own, half, 1)
        for first, second in ((own, turned_own), (turned_own, own)):
            devices.append(
                jnp.concatenate(
                    [jnp.where(low, first[at : at + 8], second[at + 8 : at + 16]) for at in (0, 16)], axis=1
                )
            )
    return jnp.concatenate(devices, axis=0).astype(BFLOAT)


def finish_kernel(kind, first_own, first_near, first_far, second_own, second_near, second_far, lower_ref, chosen_ref,
                  *refs):
    half = second_own.shape[1]
    model = HALVES * half
    wide = lambda ref: ref[...].astype(FLOAT)
    first = wide(first_own) + wide(first_near) + wide(first_far)
    second = wide(second_own) + wide(second_near) + wide(second_far)
    inner = (chosen_ref[...] * first[:, half:]).astype(BFLOAT)
    summed = jnp.concatenate([first[:, :half], second], axis=1) + dot(
        inner, matrix_rows(lower_ref[...]), (1, 1)
    )
    if kind == "output":
        residual_ref, place_ref, choose_ref, branch_ref, early_ref, out_ref = refs
        result = (residual_ref[...] + summed).astype(BFLOAT)
        out_ref[:, :model] = dot(place_ref[...], result, (0, 0)).astype(BFLOAT)
        out_ref[:, model : model + 2 * LANES] = packed_grad(inner, branch_ref[...], choose_ref[...])
        out_ref[:, model + 2 * LANES :] = early_ref[...]
        return
    if kind == "forward":
        residual_ref, gain_ref, out_ref, inner_ref, left_ref, right_ref = refs
        hidden = residual_ref[...] + summed
        normed = (hidden * root_mean(hidden) * gain_ref[0:1, :]).astype(BFLOAT)
    else:
        values_ref, upstream_ref, gain_ref, choose_ref, normed_left, normed_right = refs[:6]
        values = values_ref[...]
        scale = root_mean(values)
        weighted = summed * gain_ref[0:1, :]
        mean = jnp.mean(weighted * values, axis=1, keepdims=True)
        hidden = upstream_ref[...].astype(FLOAT) + scale * weighted - values * (scale * scale * scale * mean)
        normed = hidden.astype(BFLOAT)
        packed = packed_grad(
            inner, jnp.concatenate([normed_left[...], normed_right[...]], axis=1), choose_ref[...]
        )
        if kind == "input":
            place_ref, out_ref = refs[6:]
            out_ref[:, :model] = dot(place_ref[...], normed, (0, 0)).astype(BFLOAT)
            out_ref[:, model:] = packed
            return
        given_ref, out_ref, inner_ref, left_ref, right_ref, packed_ref = refs[6:]
        packed_ref[:, : 2 * LANES] = packed
        packed_ref[:, 2 * LANES :] = packed_grad(given_ref[...], normed, choose_ref[...])
    out_ref[...] = hidden
    inner_ref[...] = inner
    left_ref[...] = normed[:, :half]
    right_ref[...] = normed[:, half:]


def finish(kind, parts, gathered, own_selector, *operands):
    rows = own_selector.shape[0]
    half = parts[3].shape[1]
    shards = gathered[-1].shape[0]
    model = HALVES * half
    lower = gathered[-1][:, : model // shards, -LANES:]
    shaped = jax.ShapeDtypeStruct
    if kind in ("output", "input"):
        out_shape = shaped((rows, model + 2 * LANES * (3 if kind == "output" else 1)), BFLOAT)
        out_specs = whole(out_shape.shape)
    else:
        out_shape = [shaped((rows, model), FLOAT), shaped((rows, LANES), BFLOAT)]
        out_shape += [shaped((rows, half), BFLOAT)] * 2
        out_shape += [shaped((rows, 4 * LANES), BFLOAT)] * (kind == "backward")
        out_specs = [whole(shape.shape) for shape in out_shape]
    given = [*parts, lower, own_selector, *operands]
    return pl.pallas_call(
        functools.partial(finish_kernel, kind),
        grid=(1,),
        in_specs=[whole(value.shape) for value in given],
        out_specs=out_specs,
        out_shape=out_shape,
        compiler_params=pltpu.CompilerParams(vmem_limit_bytes=FINISH_BYTES),
        cost_estimate=estimate(
            flops=2 * rows * model * LANES, bytes_accessed=rows * model * 20, transcendentals=0
        ),
        name="finish_" + kind,
    )(*given)


def onward_kernel(first_kept, first_part, second_kept, second_part, first_ref, second_ref):
    first_ref[...] = (first_kept[...] + first_part[...].astype(FLOAT)).astype(BFLOAT)
    second_ref[...] = (second_kept[...] + second_part[...].astype(FLOAT)).astype(BFLOAT)


def sum_onward(first_kept, first_part, second_kept, second_part):
    return pl.pallas_call(
        onward_kernel,
        in_specs=[pl.BlockSpec(memory_space=pltpu.VMEM)] * 4,
        out_specs=[pl.BlockSpec(memory_space=pltpu.VMEM)] * 2,
        out_shape=[jax.ShapeDtypeStruct(part.shape, BFLOAT) for part in (first_part, second_part)],
        compiler_params=pltpu.CompilerParams(vmem_limit_bytes=DENSE_BYTES),
        name="sum_onward",
    )(first_kept, first_part, second_kept, second_part)


def send_kernel(target_column, target_row, tokens_ref, adapter_ref, sent_ref, matrix_ref):
    rows = tokens_ref.shape[0]
    model = tokens_ref.shape[1]
    peer = adapter_ref.shape[0]
    column, row = target_column[:, 0:1], target_row[0:1, :]
    earlier = lax.broadcasted_iota(jnp.int32, (rows, rows), 0) < lax.broadcasted_iota(jnp.int32, (rows, rows), 1)
    same = jnp.where((column // rows == row // rows) & earlier, 1.0, 0.0)
    place = (row // rows) * peer + jnp.sum(same, axis=0, keepdims=True).astype(jnp.int32)
    matrix = (lax.broadcasted_iota(jnp.int32, (rows, rows), 0) == place).astype(BFLOAT)
    matrix_ref[...] = matrix
    sent_ref[:, :model] = dot(matrix, tokens_ref[...], (1, 0)).astype(BFLOAT)
    lane = lax.broadcasted_iota(jnp.int32, (rows, LANES), 1)
    slots = jnp.where(lane == 0, column % rows, 0).astype(FLOAT).astype(BFLOAT)
    notes = dot(matrix, slots, (1, 0))
    sent_ref[:, model:] = jnp.where(lane == 0, notes, adapter_ref[0:1, :]).astype(BFLOAT)


def send_tokens(target, tokens, adapters, peer):
    rows, model = tokens.shape
    notes = jnp.pad(adapters.astype(FLOAT), (1, LANES - 1 - adapters.shape[0]))
    return pl.pallas_call(
        send_kernel,
        in_specs=[pl.BlockSpec(memory_space=pltpu.VMEM)] * 4,
        out_specs=[pl.BlockSpec(memory_space=pltpu.VMEM)] * 2,
        out_shape=[
            jax.ShapeDtypeStruct((rows, model + LANES), BFLOAT),
            jax.ShapeDtypeStruct((rows, rows), BFLOAT),
        ],
        compiler_params=pltpu.CompilerParams(vmem_limit_bytes=DENSE_BYTES),
        name="send_tokens",
    )(
        jnp.broadcast_to(target[:, None], (rows, LANES)),
        jnp.broadcast_to(target[None, :], (8, rows)),
        tokens,
        jnp.broadcast_to(notes[None, :], (peer, LANES)),
    )


def arrive_kernel(arrived_ref, gain_ref, own_ref, matrix_ref, left_ref, right_ref):
    rows, model = own_ref.shape
    slots = arrived_ref[:, model:].astype(FLOAT).T[0:1, :]
    row = lax.broadcasted_iota(jnp.int32, (rows, rows), 0).astype(FLOAT)
    matrix = (row == slots).astype(BFLOAT)
    matrix_ref[...] = matrix
    own = dot(matrix, arrived_ref[:, :model], (1, 0))
    own_ref[...] = own
    normed = (own * root_mean(own) * gain_ref[0:1, :]).astype(BFLOAT)
    left_ref[...] = normed[:, : model // HALVES]
    right_ref[...] = normed[:, model // HALVES :]


def arrive_tokens(arrived, gain):
    rows, model = arrived.shape[0], arrived.shape[1] - LANES
    return pl.pallas_call(
        arrive_kernel,
        in_specs=[pl.BlockSpec(memory_space=pltpu.VMEM)] * 2,
        out_specs=[pl.BlockSpec(memory_space=pltpu.VMEM)] * 4,
        out_shape=[
            jax.ShapeDtypeStruct((rows, model), FLOAT),
            jax.ShapeDtypeStruct((rows, rows), BFLOAT),
            jax.ShapeDtypeStruct((rows, model // HALVES), BFLOAT),
            jax.ShapeDtypeStruct((rows, model // HALVES), BFLOAT),
        ],
        compiler_params=pltpu.CompilerParams(vmem_limit_bytes=DENSE_BYTES),
        name="arrive_tokens",
    )(arrived, gain)


GATE_WIDTH = DSSM // QUERY_HEADS
PAIR_WIDTH = 2 * KEY_VALUE_HEADS * HEAD_SIZE // QUERY_HEADS
STATE_WIDTH = 2 * NSTATE // QUERY_HEADS
STEP_WIDTH = NH // QUERY_HEADS
ALL_AXES = ("row", "col")


def pad_columns(values, width):
    return jnp.pad(values, ((0, 0), (0, width - values.shape[1])))


def after(values, *earlier):
    return lax.optimization_barrier((values, *earlier))[0]


def after_all(values, *earlier):
    return lax.optimization_barrier((*values, *earlier))[: len(values)]


def unit_parts(values, units):
    cuts = [0]
    for width in (GATE_WIDTH, GATE_WIDTH, HEAD_SIZE, PAIR_WIDTH, STATE_WIDTH, STEP_WIDTH):
        cuts.append(cuts[-1] + width)
    return [
        jnp.concatenate(
            [values[:, unit * UNIT_IN + low : unit * UNIT_IN + high] for unit in range(units)], axis=1
        )
        for low, high in zip(cuts[:-1], cuts[1:])
    ]


def restore_units(parts, units):
    ordered = []
    for unit in range(units):
        for part in parts:
            width = part.shape[1] // units
            ordered.append(part[:, unit * width : (unit + 1) * width])
    return jnp.concatenate(ordered, axis=1)


def split_halves(values, units, first, axis):
    block = values.shape[axis] // units
    take = lambda low, high: lax.slice_in_dim(values, low, high, axis=axis)
    parts = [take(unit * block, unit * block + first) for unit in range(units)]
    parts += [take(unit * block + first, (unit + 1) * block) for unit in range(units)]
    return jnp.concatenate(parts, axis=axis)


def join_halves(values, units, first, axis):
    block = values.shape[axis] // units
    rest = block - first
    take = lambda low, high: lax.slice_in_dim(values, low, high, axis=axis)
    parts = []
    for unit in range(units):
        parts.append(take(unit * first, (unit + 1) * first))
        parts.append(take(units * first + unit * rest, units * first + (unit + 1) * rest))
    return jnp.concatenate(parts, axis=axis)


def quick(rows):
    return lax.axis_size("col") == 4 and lax.axis_size("row") == 8 and rows == 256


def spread_early(halves, gathered, selector):
    left, right = halves
    far_left, near_right = flip(left, 2), flip(right, 1)
    near_left, far_right = flip(left, 1), flip(right, 2)
    held = spread_blocks([(0, halves)], gathered, selector, None)
    onward_left, onward_right = after_all((far_left, near_right), held[1])
    corner = flip(onward_left, 1), flip(onward_right, 2)
    held = spread_blocks([(1, (near_left, near_right))], gathered, selector, held)
    held = spread_blocks([(2, (far_left, far_right))], gathered, selector, held)
    return spread_blocks([(3, corner)], gathered, selector, held)


def flip(values, mask):
    return lax.ppermute(values, "col", [(i, i ^ mask) for i in range(4)])


def gather_blocks(halves):
    left, right = halves
    far_left, near_right = flip(left, 2), flip(right, 1)
    near_left, far_right = flip(left, 1), flip(right, 2)
    corner_left, corner_right = flip(far_left, 1), flip(near_right, 2)
    return [
        (0, (left, right)),
        (1, (near_left, near_right)),
        (2, (far_left, far_right)),
        (3, (corner_left, corner_right)),
    ]


def rows_of(values, block, rows):
    return lax.dynamic_slice_in_dim(values, block * rows, rows, 0)


def spread_gathered(blocks, gathered, selector):
    held = None
    for block in blocks:
        held = spread_blocks([block], gathered, selector, held)
    return held


def spread_project(halves, gathered, selector):
    rows = halves[0].shape[0]
    if quick(rows):
        return spread_gathered(gather_blocks(halves), gathered, selector)
    wide, narrow_factor = gathered
    width = narrow_factor.shape[1]
    both = product(lax.all_gather(jnp.concatenate(halves, axis=1), "col", axis=0, tiled=True), wide)
    narrow = (selector * both[:, width:]).astype(BFLOAT)
    return (both[:, :width] + product(narrow, narrow_factor)).astype(BFLOAT), narrow


PIECE_TYPES = [(BFLOAT, BFLOAT), (BFLOAT, FLOAT), (FLOAT, BFLOAT), (FLOAT, FLOAT)]


def collect_pieces(values, gathered, at_once):
    if at_once:
        return collect_blocks([3, 1, 2, 0], values, gathered, PIECE_TYPES)
    (corner,) = collect_blocks([3], values, gathered, PIECE_TYPES[:1])
    values = after(values, corner[0])
    return [corner, *collect_blocks([1, 2, 0], values, gathered, PIECE_TYPES[1:])]


def collect_send(pieces, ordered=True):
    corner, near, far, own = pieces
    arriving = flip(corner[0], 1), flip(corner[1], 2)
    sent_near, sent_far = after_all((near[0], far[1]), *arriving) if ordered else (near[0], far[1])
    return own, flip(sent_near, 1), flip(sent_far, 2), far[0], near[1], arriving


def collect_middle(started):
    own, near_first, far_second, far_first, near_second, arriving = started
    return (own, near_first, far_second), sum_onward(far_first, arriving[0], near_second, arriving[1])


def collect_onward(onward):
    return flip(onward[0], 2), flip(onward[1], 1)


def collect_end(kept, last, kind, gathered, own_selector, *operands):
    own, near_first, far_second = kept
    parts = [own[0], near_first, last[0], own[1], far_second, last[1]]
    return finish(kind, parts, gathered, own_selector, *operands)


def collect_project(values, gathered, kind, own_selector, *operands):
    rows, model = own_selector.shape[0], operands[0].shape[1]
    if quick(rows):
        kept, onward = collect_middle(collect_send(collect_pieces(values, gathered, False)))
        return collect_end(kept, collect_onward(onward), kind, gathered, own_selector, *operands)
    wide, narrow_factor = gathered
    width = narrow_factor.shape[1]
    partial = jnp.concatenate(
        [contract_last(values, wide[:, :width]), contract_last(values, narrow_factor)], axis=1
    ).astype(BFLOAT)
    summed = lax.psum_scatter(partial, "col", scatter_dimension=0, tiled=True).astype(FLOAT)
    inner = (own_selector * summed[:, model:]).astype(BFLOAT)
    summed = summed[:, :model] + contract_last(inner, wide[:, width:])
    if kind == "output":
        return (operands[0] + summed).astype(BFLOAT), inner
    if kind == "forward":
        residual, gain = operands
        hidden = residual + summed
        return hidden, inner, *cut_halves(rms_norm(hidden, gain[0]).astype(BFLOAT))
    values, upstream, gain = operands
    _, back = jax.vjp(lambda given: rms_norm(given, gain[0]), values)
    hidden = upstream.astype(FLOAT) + back(summed)[0]
    if kind == "input":
        return hidden.astype(BFLOAT), inner
    return hidden, inner, *cut_halves(hidden.astype(BFLOAT))


def cut_halves(values):
    half = values.shape[1] // HALVES
    return values[:, :half], values[:, half:]


def local(
    tokens_in,
    cotangent,
    target,
    sequence_lengths,
    sequence_adapter,
    norm_gains,
    weight_in,
    conv_values,
    conv_states,
    scan_params,
    weight_mix,
    weight_feed,
    weight_down,
    in_lower,
    in_raise,
    mix_lower,
    mix_raise,
    feed_lower,
    feed_raise,
    down_lower,
    down_raise,
):
    cols = lax.axis_size("col")
    rows_axis = lax.axis_size("row")
    col = lax.axis_index("col")
    devices = cols * rows_axis
    rows = tokens_in.shape[0]
    model = tokens_in.shape[1]
    total = rows * cols
    units = QUERY_HEADS // cols
    channels = units * GATE_WIDTH
    peer = rows // devices
    lengths, adapters = sequence_lengths[0], sequence_adapter[0]
    sequences = lengths.shape[0]
    fast = quick(rows)
    key_head = col * units // (QUERY_HEADS // KEY_VALUE_HEADS)
    exchange = lambda values: lax.all_to_all(values, ALL_AXES, split_axis=0, concat_axis=0, tiled=True)

    sent, send_matrix = send_tokens(target, tokens_in, adapters, peer)
    shards = []

    def gather_weight(weight, lower, raised):
        top = jnp.concatenate([weight, lower], axis=1)
        if fast:
            bottom = pad_columns(raised, top.shape[1])
            shards.append(jnp.concatenate([top, bottom], axis=0))
            return (lax.all_gather(shards[-1], "row", axis=0),)
        wide = lax.all_gather(top, "row", axis=0, tiled=True)
        return wide, lax.all_gather(raised, "row", axis=0, tiled=True)

    depth = weight_in.shape[0]
    height = depth + in_raise.shape[0]
    given = after(jnp.concatenate([weight_in, in_raise], axis=0), send_matrix)
    gates, convs, queries, pairs, states, steps = unit_parts(given, units)
    pair_width, state_width = pairs.shape[1], states.shape[1]
    taps = jnp.concatenate([jnp.zeros((KCONV + 1, pair_width), BFLOAT), conv_states], axis=1)
    taps = jnp.pad(taps, ((0, 16 - KCONV - 1), (0, 0)))
    shared = jnp.concatenate([jnp.concatenate([pairs, states], axis=1), taps], axis=0)
    own_columns = jnp.concatenate([gates, convs, queries, pad_columns(steps, LANES)], axis=1)
    if fast:
        shared_shard = shared
        shared = lax.all_gather(shared_shard, "row", axis=0)
        weights_own = gather_weight(own_columns[:depth], in_lower, own_columns[depth:])
    arrived = exchange(sent)
    gains = jnp.broadcast_to(norm_gains.astype(FLOAT)[:, None, :], (2, 8, model))
    if fast:
        near, far = flip(shared, 1), flip(shared, 2)
        arrived = after(arrived, near, far, shards[0])
    own_input, place_matrix, *normed_one = arrive_tokens(arrived.reshape(rows, model + LANES), gains[0])
    blocks_one = gather_blocks(normed_one) if fast else normed_one
    if fast:
        held = jnp.zeros((cols,) + shared.shape, BFLOAT)
        for block, values in ((col, shared), (col ^ 1, near), (col ^ 2, far)):
            held = lax.dynamic_update_index_in_dim(held, values, block, 0)
        split = shared.shape[0] // 2
        corner = jnp.concatenate([flip(near[:split], 2), flip(far[split:], 1)], axis=0)
        held = lax.dynamic_update_index_in_dim(held, corner, col ^ 3, 0)
    else:
        held = lax.all_gather(shared, "col", axis=0)
    all_pairs = jnp.concatenate([held[at, ..., :height, :pair_width] for at in range(cols)], axis=-1)
    pick = lambda start: lax.select_n(
        key_head,
        *[all_pairs[..., start + at * HEAD_SIZE : start + (at + 1) * HEAD_SIZE] for at in range(KEY_VALUE_HEADS)],
    )
    shared_columns = jnp.concatenate(
        [held[at, ..., :height, pair_width:] for at in range(cols)]
        + [pick(0), pick(KEY_VALUE_HEADS * HEAD_SIZE)],
        axis=-1,
    )
    tap_rows = held[:, 0] if fast else held
    all_taps = jnp.concatenate(
        [tap_rows[at, height : height + KCONV + 1, pair_width:] for at in range(cols)], axis=1
    )
    if fast:
        weights_in = (shared_columns, *weights_own)
    else:
        columns = jnp.concatenate([shared_columns, own_columns], axis=1)
        weights_in = gather_weight(columns[:depth], in_lower, columns[depth:])
    weights_mix = gather_weight(
        after(split_halves(weight_mix, units, GATE_WIDTH, 0).T, sent),
        mix_raise.T,
        split_halves(mix_lower, units, GATE_WIDTH, 0).T,
    )
    weights_feed = gather_weight(
        after(split_halves(weight_feed, units, UNIT_FF, 1), arrived),
        feed_lower,
        split_halves(feed_raise, units, UNIT_FF, 1),
    )

    source_adapters = arrived.reshape(rows, model + LANES)[::peer, model + 1 : model + 1 + sequences].astype(jnp.int32)
    segment, position, selector = sequence_tables(lengths, adapters, total)
    own_selector = rows_of(selector, col, rows)
    own_segment = rows_of(segment, col, rows)
    tables = mixer_tables(lengths, segment, position, conv_values, all_taps, scan_params)

    def compact_grad(narrow, values):
        parts = [
            lax.dynamic_slice_in_dim(narrow, adapters[at] * RANK, RANK, 1)
            * (own_segment == at).astype(BFLOAT)[:, None]
            for at in range(sequences)
        ]
        grad = contract_first(jnp.concatenate(parts, axis=1), values).astype(BFLOAT)
        kept = sequences * RANK
        grad = grad.reshape(kept, devices, model // devices).transpose(1, 0, 2)
        return grad.reshape(devices, peer, kept * model // devices // peer)

    def expand_grad(dealt):
        kept = sequences * RANK
        dealt = dealt.reshape(devices * kept, model // devices)
        adapter_row = (source_adapters[:, :, None] * RANK + jnp.arange(RANK, dtype=jnp.int32)).reshape(-1)
        chosen = (jnp.arange(NADAPT * RANK, dtype=jnp.int32)[:, None] == adapter_row[None, :]).astype(BFLOAT)
        return product(chosen, dealt)

    def send_back(values, grads):
        back = contract_first(place_matrix, values).astype(BFLOAT).reshape(devices, peer, model)
        return exchange(jnp.concatenate([back, *grads], axis=2))

    def expand_packed(dealt, count):
        slots = dealt.shape[0] * peer
        block = jnp.arange(2 * LANES // (model // devices), dtype=jnp.int32)[:, None, None]
        row = jnp.arange(peer, dtype=jnp.int32)[None, None, :]
        place = block * peer + row
        adapter = jnp.where(place < RANK, source_adapters[None, :, 0:1], source_adapters[None, :, 1:2])
        adapter_row = (adapter * RANK + place % RANK).reshape(block.shape[0], 1, slots)
        chosen = (jnp.arange(NADAPT * RANK, dtype=jnp.int32)[None, :, None] == adapter_row).astype(BFLOAT)
        sums = product(chosen.reshape(-1, slots), dealt.reshape(slots, dealt.shape[2]))
        sums = sums.reshape(block.shape[0], NADAPT * RANK, dealt.shape[2])
        width = model // devices
        return [
            sum(
                sums[at, :, grad * 2 * LANES + at * width : grad * 2 * LANES + (at + 1) * width]
                for at in range(block.shape[0])
            )
            for grad in range(count)
        ]

    def take_back(dealt, count):
        returned = contract_first(send_matrix, dealt[:, :, :model].reshape(rows, model)).astype(BFLOAT)
        if fast:
            return returned, expand_packed(dealt[:, :, model:], count)
        width = (dealt.shape[2] - model) // count
        return returned, [
            expand_grad(dealt[:, :, model + at * width : model + (at + 1) * width]) for at in range(count)
        ]

    if fast:
        projected, inner_in = spread_gathered(blocks_one, weights_in, selector)
    else:
        projected, inner_in = spread_project(blocks_one, weights_in, selector)

    sent_grad = product(send_matrix, cotangent).astype(BFLOAT).reshape(devices, peer, model)
    arrived_grad = exchange(after(sent_grad, normed_one[0])).reshape(rows, model)
    branch_two = product(place_matrix, arrived_grad).astype(BFLOAT)
    weights_down = gather_weight(after(weight_down.T, projected), down_raise.T, down_lower.T)

    mixed_out = attention_forward(projected, tables)
    mixed_out, scanned, carried = scan_forward(projected, tables, mixed_out)
    hidden, inner_out, *normed_two = collect_project(mixed_out, weights_mix, "forward", own_selector, own_input, gains[1])
    gate_up, inner_feed = spread_project(normed_two, weights_feed, selector)
    half_feed = units * UNIT_FF
    gate_part, up_part = gate_up[:, :half_feed].astype(FLOAT), gate_up[:, half_feed:].astype(FLOAT)
    gate = jax.nn.sigmoid(gate_part)
    silu = gate_part * gate
    activated = (silu * up_part).astype(BFLOAT)
    slope = up_part * (gate * (1.0 + gate_part * (1.0 - gate)))
    branch_halves = cut_halves(after(branch_two, projected))
    if fast:
        feed_grad, narrow_two = spread_blocks(
            gather_blocks(branch_halves), weights_down, selector, None, [slope, silu]
        )
    else:
        act_grad, narrow_two = spread_project(branch_halves, weights_down, selector)
        wide_grad = act_grad.astype(FLOAT)
        feed_grad = jnp.concatenate([wide_grad * slope, wide_grad * silu], axis=1).astype(BFLOAT)
    choose = (
        jnp.arange(NADAPT * RANK, dtype=jnp.int32)[:, None]
        == (adapters[:, None] * RANK + jnp.arange(RANK, dtype=jnp.int32)[None, :]).reshape(1, -1)
    ).astype(BFLOAT)
    if fast:
        pieces = collect_pieces(after(activated, feed_grad), weights_down, True)
        kept, onward = collect_middle(collect_send(collect_pieces(feed_grad, weights_feed, False)))
        hidden_grad, narrow_three, left, right, early_grads = collect_end(
            kept,
            collect_onward(onward),
            "backward",
            weights_feed,
            own_selector,
            after(hidden, pieces[3][0]),
            branch_two,
            gains[1],
            choose,
            *normed_two,
            inner_out,
        )
        mixed_grad, narrow_one = spread_early((left, right), weights_mix, selector)
    else:
        hidden_grad, narrow_three, *branch_one = collect_project(
            feed_grad, weights_feed, "backward", own_selector, hidden, branch_two, gains[1]
        )
        mixed_grad, narrow_one = spread_project(branch_one, weights_mix, selector)

    if fast:
        near_parts = after_all((*pieces[0], pieces[1][0], pieces[2][1]), mixed_grad)
        started = collect_send(
            [near_parts[:2], (near_parts[2], pieces[1][1]), (pieces[2][0], near_parts[3]), pieces[3]], False
        )
        attended_grads = attention_backward(projected, tables, after(mixed_grad, near_parts[0]))
        kept, onward = collect_middle((*started[:5], after_all(started[5], attended_grads[1])))
        scan_inputs = (projected, tables, scanned, carried, after(mixed_grad, *onward), attended_grads)
        scan_part = list(scan_backward(*scan_inputs, 0, 2, None))
        payload = collect_end(
            kept,
            collect_onward(onward),
            "output",
            weights_down,
            own_selector,
            after(hidden, scan_part[2]),
            place_matrix,
            choose,
            branch_two,
            early_grads,
        )
        dealt_out = exchange(payload.reshape(devices, peer, -1))
        scan_part[2] = after(scan_part[2], payload)
        projected_grad = scan_backward(*scan_inputs, 1, 2, scan_part)[0]
        raise_grad = contract_first(inner_in, projected_grad).astype(BFLOAT)
        projected_grad = after(projected_grad, raise_grad)
        started_in = collect_send(collect_pieces(projected_grad, weights_in, True), False)
        kept_in, onward_in = collect_middle(started_in)
    else:
        block_out, inner_down = collect_project(activated, weights_down, "output", own_selector, hidden)
        attended_grads = attention_backward(projected, tables, mixed_grad)
        projected_grad = scan_backward(
            projected, tables, scanned, carried, mixed_grad, attended_grads, 0, 1, None
        )[0]
        dealt_out = send_back(
            block_out,
            [
                compact_grad(inner_down, branch_two),
                compact_grad(narrow_three, jnp.concatenate(normed_two, axis=1)),
                compact_grad(inner_out, jnp.concatenate(branch_one, axis=1)),
            ],
        )

    def sum_rows(values):
        return lax.psum_scatter(values.astype(BFLOAT), "row", scatter_dimension=0, tiled=True).astype(FLOAT)

    early_parts = [
        contract_first(narrow_one, mixed_out),
        contract_first(inner_feed, feed_grad),
        contract_first(narrow_two, activated),
    ]
    early = sum_rows(jnp.concatenate(early_parts, axis=1))

    late = sum_rows(raise_grad if fast else contract_first(inner_in, projected_grad))

    if fast:
        payload = collect_end(
            kept_in,
            collect_onward(onward_in),
            "input",
            weights_in,
            own_selector,
            own_input,
            after(hidden_grad, dealt_out),
            gains[0],
            choose,
            *normed_one,
            place_matrix,
        )
        dealt_grad = exchange(payload.reshape(devices, peer, -1))
    else:
        input_grad, narrow_four = collect_project(
            projected_grad, weights_in, "input", own_selector, own_input, hidden_grad, gains[0]
        )
        dealt_grad = send_back(input_grad, [compact_grad(narrow_four, jnp.concatenate(normed_one, axis=1))])
        payload = input_grad
    dealt_out, early, late = after_all((dealt_out, early, late), payload)
    early_cuts = [0, early_parts[0].shape[1]]
    early_cuts.append(early_cuts[1] + early_parts[1].shape[1])
    grad_mix_lower = join_halves(early[:, : early_cuts[1]], units, GATE_WIDTH, 1).T
    grad_feed_raise = join_halves(early[:, early_cuts[1] : early_cuts[2]], units, UNIT_FF, 1)
    grad_down_lower = early[:, early_cuts[2] :].T

    key_columns = late[:, STATES : STATES + HEAD_SIZE]
    value_columns = late[:, STATES + HEAD_SIZE : STATES + PAIR]
    mine = [(key_head == at).astype(FLOAT) for at in range(KEY_VALUE_HEADS)]
    pair_grad = jnp.concatenate([part * here for part in (key_columns, value_columns) for here in mine], axis=1)
    stacked = jnp.stack(
        [
            jnp.concatenate(
                [
                    pair_grad[:, at * pair_width : (at + 1) * pair_width],
                    late[:, at * state_width : (at + 1) * state_width],
                ],
                axis=1,
            )
            for at in range(cols)
        ]
    )
    if fast:
        piece = lambda mask: lax.dynamic_index_in_dim(stacked, col ^ mask, 0, False)
        shared_sum = piece(0) + flip(piece(1), 1) + flip(piece(2), 2) + flip(piece(3), 3)
    else:
        shared_sum = lax.psum_scatter(
            stacked.reshape(stacked.shape[0] * stacked.shape[1], -1), "col", scatter_dimension=0, tiled=True
        )
    late = jnp.concatenate([shared_sum, late[:, STATES + PAIR :]], axis=1)
    shared_width = pair_width + state_width
    cuts = [shared_width]
    for width in (channels, channels, units * HEAD_SIZE, units * STEP_WIDTH):
        cuts.append(cuts[-1] + width)
    gate_columns, conv_columns, query_columns, step_columns = [
        late[:, low:high] for low, high in zip(cuts[:-1], cuts[1:])
    ]
    grad_in_raise = restore_units(
        [
            gate_columns,
            conv_columns,
            query_columns,
            late[:, :pair_width],
            late[:, pair_width:shared_width],
            step_columns,
        ],
        units,
    )

    returned_out, (grad_down_raise, grad_feed_lower, grad_mix_raise) = take_back(dealt_out, 3)
    returned_grad, (grad_in_lower,) = take_back(dealt_grad, 1)
    return (
        returned_out,
        returned_grad,
        grad_in_lower.T,
        grad_in_raise,
        grad_mix_lower,
        grad_mix_raise,
        grad_feed_lower.T,
        grad_feed_raise,
        grad_down_lower,
        grad_down_raise,
    )


def solution(mesh):
    in_specs = (
        P(("row", "col"), None),
        P(("row", "col"), None),
        P(("row", "col")),
        P("row", None),
        P("row", None),
        P(),
        P("row", "col"),
        P(None, "col"),
        P(None, "col"),
        P(None, "col"),
        P("col", "row"),
        P("row", "col"),
        P("col", "row"),
        P("row", None),
        P("row", "col"),
        P("col", "row"),
        P(None, "row"),
        P("row", None),
        P("row", "col"),
        P("col", "row"),
        P(None, "row"),
    )
    out_specs = (
        P(("row", "col"), None),
        P(("row", "col"), None),
        P(("row", "col"), None),
        P("row", "col"),
        P("col", "row"),
        P(None, ("row", "col")),
        P(("row", "col"), None),
        P("row", "col"),
        P("col", "row"),
        P(None, ("row", "col")),
    )
    return jax.shard_map(local, mesh=mesh, in_specs=in_specs, out_specs=out_specs, check_vma=False)
```

```python
import functools
import math

import jax
import jax.numpy as jnp
from jax import lax
from jax.experimental import pallas as pl
from jax.experimental.pallas import tpu as pltpu
from jax.sharding import PartitionSpec as P

NH = 48
HP = 64
NSTATE = 256
KCONV = 4
QUERY_HEADS = 8
KEY_VALUE_HEADS = 2
HEAD_SIZE = 128
RANK = 16
NADAPT = 8
SSD_BLOCK = 256
DSSM = 3072
UNIT_IN = 1030
UNIT_FF = 512


EPSILON = 1e-05
ROPE_BASE = 10000.0
NEGATIVE = -1e30
FLOAT = jnp.float32
BFLOAT = jnp.bfloat16


def product(left, right):
    return jnp.dot(left, right, preferred_element_type=FLOAT)


def contract_last(left, right):
    return lax.dot_general(left, right, (((1,), (1,)), ((), ())), preferred_element_type=FLOAT)


def contract_first(left, right):
    return lax.dot_general(left, right, (((0,), (0,)), ((), ())), preferred_element_type=FLOAT)


def rms_norm(values, gain):
    return values * lax.rsqrt(jnp.mean(values * values, axis=-1, keepdims=True) + EPSILON) * gain


def sequence_tables(lengths, adapters, sequence_length):
    sequence_count = lengths.shape[0]
    boundary = jnp.cumsum(lengths)
    token_index = jnp.arange(sequence_length, dtype=jnp.int32)
    passed = (token_index[:, None] >= boundary[None, :]).astype(jnp.int32)
    segment = jnp.sum(passed, axis=1)
    segment_start = jnp.sum(passed * lengths[None, :], axis=1)
    position = token_index - segment_start
    member = (segment[:, None] == jnp.arange(sequence_count, dtype=jnp.int32)[None, :]).astype(
        jnp.int32
    )
    chosen = jnp.sum(member * adapters[None, :], axis=1)
    column = jnp.arange(NADAPT * RANK, dtype=jnp.int32) // RANK
    selector = (chosen[:, None] == column[None, :]).astype(FLOAT)
    return (segment, position, selector)


ESTIMATE = 16
SCAN_BYTES = 32 * 1024 * 1024
DENSE_BYTES = 16 * 1024 * 1024
FINISH_BYTES = 32 * 1024 * 1024
LANES = 128


def whole(shape):
    return pl.BlockSpec(shape, lambda *_: (0,) * len(shape))


def estimate(flops, bytes_accessed, transcendentals):
    return pl.CostEstimate(
        flops=flops // ESTIMATE,
        bytes_accessed=bytes_accessed // ESTIMATE,
        transcendentals=transcendentals // ESTIMATE,
    )


def dot(left, right, contract):
    return lax.dot_general(left, right, ((contract[:1], contract[1:]), ((), ())), preferred_element_type=FLOAT)


def parts_of(values, count):
    parts = []
    for _ in range(count):
        part = values.astype(BFLOAT)
        parts.append(part)
        values = values - part.astype(FLOAT)
    return parts


def running_sum(values, triangle, contract):
    width = values.shape[1]
    split = dot(triangle, jnp.concatenate(parts_of(values, 3), axis=1), contract)
    return split[:, :width] + split[:, width : 2 * width] + split[:, 2 * width :]


def head_spread(values, expand):
    return dot(jnp.concatenate(parts_of(values, 2), axis=1), expand, (1, 0))


def head_sum(values, expand):
    high, low = parts_of(values, 2)
    single = expand[:LANES]
    return dot(high, single, (1, 1)) + dot(low, single, (1, 1))


def silu_parts(values):
    gate = 1.0 / (1.0 + jnp.exp(-values))
    return values * gate, gate


def expand_table(channels):
    row = lax.broadcasted_iota(jnp.int32, (2 * LANES, channels), 0) % LANES
    channel = lax.broadcasted_iota(jnp.int32, (2 * LANES, channels), 1) // HP
    return (row == channel).astype(BFLOAT)


def conv_sum(current_ref, before_ref, taps_ref, meta):
    rows = SSD_BLOCK
    current = current_ref[...].astype(FLOAT)
    window = jnp.concatenate([before_ref[...].astype(FLOAT)[8:16], current], axis=0)
    summed = taps_ref[KCONV : KCONV + 1, :] + current * taps_ref[0:1, :]
    for lag in range(1, KCONV):
        shifted = window[8 - lag : 8 - lag + rows]
        summed = summed + jnp.where(meta[:, 1:2] >= lag, shifted, 0.0) * taps_ref[lag : lag + 1, :]
    return summed


def conv_back(summed_grad, later, taps_ref, meta):
    rows = SSD_BLOCK
    window = jnp.concatenate([summed_grad, later[...]], axis=0)
    grad = summed_grad * taps_ref[0:1, :]
    for lag in range(1, KCONV):
        grad = grad + jnp.where(meta[:, 2:3] >= lag, window[lag : lag + rows], 0.0) * taps_ref[lag : lag + 1, :]
    later[...] = summed_grad[:8]
    return grad


def silu_slope(values, gate):
    return gate * (1.0 + values * (1.0 - gate))


def scan_block(
    conv_ref, before_ref, state_ref, state_before_ref, step_ref, meta_ref, segment_ref, taps_ref, state_taps_ref, head_ref,
    turned_over,
):
    rows = SSD_BLOCK
    channels = conv_ref.shape[1]
    meta = meta_ref[...]
    summed = conv_sum(conv_ref, before_ref, taps_ref, meta)
    activated, conv_gate = silu_parts(summed)
    wide_inputs = activated.astype(BFLOAT).astype(FLOAT)
    state_summed = conv_sum(state_ref, state_before_ref, state_taps_ref, meta)
    state_values, state_gate = silu_parts(state_summed)
    write = state_values[:, :NSTATE].astype(BFLOAT)
    read = state_values[:, NSTATE:].astype(BFLOAT)
    raw = step_ref[...].astype(FLOAT) + head_ref[0:1, :]
    steps = jnp.maximum(raw, 0.0) + jnp.log1p(jnp.exp(-jnp.abs(raw)))
    row = lax.broadcasted_iota(jnp.int32, (rows, rows), 0)
    column = lax.broadcasted_iota(jnp.int32, (rows, rows), 1)
    triangle = (row >= column).astype(BFLOAT)
    total = running_sum(steps * head_ref[1:2, :], triangle, (1, 0))
    entered = jnp.exp(total) * meta[:, 3:4]
    leaving = jnp.exp(total[rows - 1 : rows] - total) * meta[:, 4:5]
    expand = expand_table(channels)
    spread = head_spread(jnp.concatenate([steps, entered, leaving * steps], axis=0), expand)
    ordered = row <= column if turned_over else row >= column
    blocked = jnp.where(ordered & (meta[:, 0:1] == segment_ref[0:1, :]), 0.0, NEGATIVE)
    return dict(
        summed=summed,
        conv_gate=conv_gate,
        state_summed=state_summed,
        state_gate=state_gate,
        write=write,
        read=read,
        wide_inputs=wide_inputs,
        raw=raw,
        steps=steps,
        triangle=triangle,
        total=total,
        total_rows=total.T,
        leaving=leaving,
        expand=expand,
        steps_wide=spread[:rows],
        entered_wide=spread[rows : 2 * rows],
        tail_wide=spread[2 * rows :],
        stepped=(wide_inputs * spread[:rows]).astype(BFLOAT),
        tailed=(wide_inputs * spread[2 * rows :]).astype(BFLOAT),
        blocked=blocked,
        crossing=dot(write, read, (1, 1)) if turned_over else dot(read, write, (1, 1)),
    )


def decay_of(block, head):
    difference = block["total"][:, head : head + 1] - block["total_rows"][head : head + 1, :]
    return jnp.exp(difference + block["blocked"])


def turned_decay_of(block, head):
    difference = block["total_rows"][head : head + 1, :] - block["total"][:, head : head + 1]
    return jnp.exp(difference + block["blocked"])


def scan_forward_kernel(
    gate_ref, conv_ref, before_ref, state_ref, state_before_ref, step_ref, meta_ref, segment_ref, taps_ref,
    state_taps_ref, head_ref, skip_ref, mixed_ref, out_ref, scanned_ref, states_ref, state,
):
    del mixed_ref

    @pl.when(pl.program_id(0) == 0)
    def _():
        state[...] = jnp.zeros_like(state)

    block = scan_block(
        conv_ref, before_ref, state_ref, state_before_ref, step_ref, meta_ref, segment_ref, taps_ref, state_taps_ref,
        head_ref, False,
    )
    heads = conv_ref.shape[1] // HP
    carried = state[...].astype(BFLOAT)
    states_ref[0] = carried
    across = dot(block["read"], carried, (1, 0)) * block["entered_wide"]
    within = []
    for head in range(heads):
        weights = (block["crossing"] * decay_of(block, head)).astype(BFLOAT)
        within.append(dot(weights, block["stepped"][:, head * HP : (head + 1) * HP], (1, 0)))
    scanned = across + jnp.concatenate(within, axis=1)
    scanned_ref[...] = scanned
    gated, _ = silu_parts(gate_ref[...].astype(FLOAT))
    out_ref[...] = ((scanned + skip_ref[0:1, :] * block["wide_inputs"]) * gated).astype(BFLOAT)
    state[...] = state[...] * block["entered_wide"][SSD_BLOCK - 1 : SSD_BLOCK, :] + dot(
        block["write"], block["tailed"], (0, 0)
    )


def scan_backward_kernel(
    gate_ref, conv_ref, before_ref, state_ref, state_before_ref, step_ref, meta_ref, segment_ref, taps_ref,
    state_taps_ref, head_ref, skip_ref, scanned_ref, states_ref, grad_ref, query_grad_ref, shared_grad_ref, *rest,
):
    out_ref, *running = rest[-4:]
    state_grad, later, state_later = running

    @pl.when(pl.program_id(0) == 0)
    def _():
        for at, ref in enumerate(running):
            ref[...] = rest[1 + at][...] if len(rest) > 4 else jnp.zeros_like(ref)

    block = scan_block(
        conv_ref, before_ref, state_ref, state_before_ref, step_ref, meta_ref, segment_ref, taps_ref, state_taps_ref,
        head_ref, True,
    )
    rows = SSD_BLOCK
    channels = conv_ref.shape[1]
    heads = channels // HP
    meta = meta_ref[...]
    read, write = block["read"], block["write"]
    inputs = block["wide_inputs"]
    scanned = scanned_ref[...]
    skip = skip_ref[0:1, :]
    gate_values = gate_ref[...].astype(FLOAT)
    gated, gate = silu_parts(gate_values)
    grad = grad_ref[...].astype(FLOAT)
    gate_grad = grad * (scanned + skip * inputs) * silu_slope(gate_values, gate)
    out_grad = grad * gated
    inputs_grad = skip * out_grad
    rounded = out_grad.astype(BFLOAT)
    wide_rounded = rounded.astype(FLOAT)
    carried = states_ref[0]
    after = state_grad[...]
    after_rounded = after.astype(BFLOAT)

    from_state = dot(write, after_rounded, (1, 0))
    entering = (wide_rounded * block["entered_wide"]).astype(BFLOAT)
    write_grad = dot(block["tailed"], after_rounded, (1, 1))
    read_grad = dot(entering, carried, (1, 1))
    last_entered = block["entered_wide"][rows - 1 : rows, :]
    through = jnp.sum(after * carried.astype(FLOAT), axis=0, keepdims=True) * last_entered
    state_grad[...] = after * last_entered + dot(read, entering, (0, 0))

    crossing_grad = jnp.zeros((rows, rows), FLOAT)
    pulled = []
    for head in range(heads):
        span = slice(head * HP, (head + 1) * HP)
        decay = turned_decay_of(block, head)
        weights = (block["crossing"] * decay).astype(BFLOAT)
        pulled.append(dot(weights, rounded[:, span], (1, 0)))
        crossing_grad = crossing_grad + dot(block["stepped"][:, span], rounded[:, span], (1, 1)) * decay
    pulled = jnp.concatenate(pulled, axis=1)
    crossing_rounded = crossing_grad.astype(BFLOAT)
    read_grad = read_grad + dot(crossing_rounded, write, (0, 0))
    write_grad = write_grad + dot(crossing_rounded, read, (1, 0))

    inputs_grad = inputs_grad + block["steps_wide"] * pulled + block["tail_wide"] * from_state
    sums = head_sum(
        jnp.concatenate(
            [
                wide_rounded * scanned - block["stepped"].astype(FLOAT) * pulled,
                inputs * pulled,
                inputs * from_state,
                jnp.broadcast_to(through, (8, channels)),
            ],
            axis=0,
        ),
        block["expand"],
    )
    leaving_grad = sums[2 * rows : 3 * rows] * block["leaving"]
    leaving_total = leaving_grad * block["steps"]
    last = sums[3 * rows : 3 * rows + 1] + jnp.sum(leaving_total, axis=0, keepdims=True)
    total_grad = sums[:rows] - leaving_total
    total_grad = total_grad + jnp.where(
        lax.broadcasted_iota(jnp.int32, total_grad.shape, 0) == rows - 1, last, 0.0
    )
    decay_grad = running_sum(total_grad, block["triangle"], (0, 0))
    steps_grad = sums[rows : 2 * rows] + leaving_grad + decay_grad * head_ref[1:2, :]
    raw_grad = steps_grad / (1.0 + jnp.exp(-block["raw"]))
    raw_grad = jnp.where(lax.broadcasted_iota(jnp.int32, raw_grad.shape, 1) < heads, raw_grad, 0.0)

    state_slope = silu_slope(block["state_summed"], block["state_gate"])
    state_pre = conv_back(
        jnp.concatenate([write_grad, read_grad], axis=1) * state_slope, state_later, state_taps_ref, meta
    )
    conv_pre = conv_back(inputs_grad * silu_slope(block["summed"], block["conv_gate"]), later, taps_ref, meta)
    out_ref[:, : 2 * NSTATE] = state_pre.astype(BFLOAT)
    start = 2 * NSTATE + 2 * HEAD_SIZE
    end = out_ref.shape[1] - LANES
    out_ref[:, 2 * NSTATE : start] = shared_grad_ref[...]
    out_ref[:, start + 2 * channels : end] = query_grad_ref[...]
    out_ref[:, start : start + channels] = gate_grad.astype(BFLOAT)
    out_ref[:, start + channels : start + 2 * channels] = conv_pre.astype(BFLOAT)
    out_ref[:, end:] = raw_grad.astype(BFLOAT)


STATES = 2 * NSTATE
PAIR = 2 * HEAD_SIZE


def scan_specs(channels, order):
    half = SSD_BLOCK // 16
    before = lambda i: jnp.maximum(order(i) * half - 1, 0)
    gate_at = (STATES + PAIR) // channels
    step_at = (STATES + PAIR + 2 * channels + channels * QUERY_HEADS // DSSM * HEAD_SIZE) // LANES
    return [
        pl.BlockSpec((SSD_BLOCK, channels), lambda i: (order(i), gate_at)),
        pl.BlockSpec((SSD_BLOCK, channels), lambda i: (order(i), gate_at + 1)),
        pl.BlockSpec((16, channels), lambda i: (before(i), gate_at + 1)),
        pl.BlockSpec((SSD_BLOCK, STATES), lambda i: (order(i), 0)),
        pl.BlockSpec((16, STATES), lambda i: (before(i), 0)),
        pl.BlockSpec((SSD_BLOCK, LANES), lambda i: (order(i), step_at)),
        pl.BlockSpec((SSD_BLOCK, LANES), lambda i: (order(i), 0)),
        pl.BlockSpec((8, SSD_BLOCK), lambda i: (0, order(i))),
        whole((8, channels)),
        whole((8, STATES)),
        whole((8, LANES)),
        whole((8, channels)),
    ]


def scan_operands(projected, tables):
    return [projected] * 6 + [
        tables[name] for name in ("meta", "segment_row", "taps", "state_taps", "head", "skip")
    ]


def scan_cost(tokens, channels, factor):
    heads = channels // HP
    return estimate(
        flops=factor * 2 * tokens * SSD_BLOCK * (3 * channels + NSTATE),
        bytes_accessed=factor * tokens * channels * 12,
        transcendentals=tokens * SSD_BLOCK * heads,
    )


def scan_forward(projected, tables, mixed):
    tokens = projected.shape[0]
    channels = tables["taps"].shape[1]
    blocks = tokens // SSD_BLOCK
    return pl.pallas_call(
        scan_forward_kernel,
        grid=(blocks,),
        in_specs=scan_specs(channels, lambda i: i) + [pl.BlockSpec(memory_space=pl.ANY)],
        out_specs=[
            pl.BlockSpec((SSD_BLOCK, channels), lambda i: (i, 0)),
            pl.BlockSpec((SSD_BLOCK, channels), lambda i: (i, 0)),
            pl.BlockSpec((1, NSTATE, channels), lambda i: (i, 0, 0)),
        ],
        out_shape=[
            jax.ShapeDtypeStruct(mixed.shape, BFLOAT),
            jax.ShapeDtypeStruct((tokens, channels), FLOAT),
            jax.ShapeDtypeStruct((blocks, NSTATE, channels), BFLOAT),
        ],
        scratch_shapes=[pltpu.VMEM((NSTATE, channels), FLOAT)],
        input_output_aliases={12: 0},
        compiler_params=pltpu.CompilerParams(vmem_limit_bytes=SCAN_BYTES),
        cost_estimate=scan_cost(tokens, channels, 1),
        name="scan_forward",
    )(*scan_operands(projected, tables), mixed)


def scan_backward(projected, tables, scanned, carried, mixed_grad, attended_grads, part, parts, before):
    tokens, width = projected.shape
    channels = tables["taps"].shape[1]
    blocks = tokens // SSD_BLOCK
    last = blocks - 1 - part * (blocks // parts)
    back = lambda i: (last - i, 0)
    running = [(NSTATE, channels), (8, channels), (8, STATES)]
    query_grad, shared_grad = attended_grads
    operands = [*scan_operands(projected, tables), scanned, carried, mixed_grad, query_grad, shared_grad]
    in_specs = scan_specs(channels, lambda i: last - i) + [
        pl.BlockSpec((SSD_BLOCK, channels), back),
        pl.BlockSpec((1, NSTATE, channels), lambda i: (last - i, 0, 0)),
        pl.BlockSpec((SSD_BLOCK, channels), back),
        pl.BlockSpec((SSD_BLOCK, query_grad.shape[1]), back),
        pl.BlockSpec((SSD_BLOCK, PAIR), back),
    ]
    aliases = {}
    if before is not None:
        aliases = {len(operands): 0}
        operands += list(before)
        in_specs += [pl.BlockSpec(memory_space=pl.ANY), *[whole(shape) for shape in running]]
    return pl.pallas_call(
        scan_backward_kernel,
        grid=(blocks // parts,),
        in_specs=in_specs,
        out_specs=[pl.BlockSpec((SSD_BLOCK, width), back), *[whole(shape) for shape in running]],
        out_shape=[
            jax.ShapeDtypeStruct((tokens, width), BFLOAT),
            *[jax.ShapeDtypeStruct(shape, FLOAT) for shape in running],
        ],
        input_output_aliases=aliases,
        compiler_params=pltpu.CompilerParams(vmem_limit_bytes=SCAN_BYTES),
        cost_estimate=scan_cost(tokens, channels, 2),
        name="scan_backward",
    )(*operands)


def turned(values, cosine, sine):
    return (values * cosine + pltpu.roll(values, HEAD_SIZE // 2, 1) * sine).astype(BFLOAT)


def turned_back(values, cosine, sine):
    return values * cosine + pltpu.roll(values * sine, HEAD_SIZE // 2, 1)


ATT_ROWS = 256


def attention_mask(meta_ref, segment_ref, start, extent):
    row = start + lax.broadcasted_iota(jnp.int32, (ATT_ROWS, extent), 0)
    column = lax.broadcasted_iota(jnp.int32, (ATT_ROWS, extent), 1)
    return (row >= column) & (meta_ref[start : start + ATT_ROWS, 0:1] == segment_ref[0:1, :extent])


def probabilities(query, keys, allowed):
    score = dot(query, keys, (1, 1)) * (1.0 / math.sqrt(HEAD_SIZE))
    score = jnp.where(allowed, score, NEGATIVE)
    exponent = jnp.exp(score - jnp.max(score, axis=1, keepdims=True))
    return exponent / jnp.sum(exponent, axis=1, keepdims=True)


def attention_forward_kernel(query_ref, key_ref, value_ref, cosine_ref, sine_ref, meta_ref, segment_ref, out_ref, keys):
    tokens = key_ref.shape[0]
    keys[...] = turned(key_ref[...].astype(FLOAT), cosine_ref[...], sine_ref[...])
    for start in range(0, tokens, ATT_ROWS):
        extent = start + ATT_ROWS
        here = slice(start, extent)
        allowed = attention_mask(meta_ref, segment_ref, start, extent)
        for unit in range(query_ref.shape[1] // HEAD_SIZE):
            span = slice(unit * HEAD_SIZE, (unit + 1) * HEAD_SIZE)
            query = turned(query_ref[here, span].astype(FLOAT), cosine_ref[here], sine_ref[here])
            weights = probabilities(query, keys[:extent], allowed).astype(BFLOAT)
            out_ref[here, span] = dot(weights, value_ref[:extent], (1, 0)).astype(BFLOAT)


def attention_backward_kernel(
    query_ref, key_ref, value_ref, cosine_ref, sine_ref, meta_ref, segment_ref, grad_ref,
    query_grad_ref, shared_grad_ref, keys, key_sum, value_sum,
):
    tokens = key_ref.shape[0]
    scale = 1.0 / math.sqrt(HEAD_SIZE)
    keys[...] = turned(key_ref[...].astype(FLOAT), cosine_ref[...], sine_ref[...])
    key_sum[...] = jnp.zeros_like(key_sum)
    value_sum[...] = jnp.zeros_like(value_sum)
    for start in range(0, tokens, ATT_ROWS):
        extent = start + ATT_ROWS
        here = slice(start, extent)
        allowed = attention_mask(meta_ref, segment_ref, start, extent)
        for unit in range(query_ref.shape[1] // HEAD_SIZE):
            span = slice(unit * HEAD_SIZE, (unit + 1) * HEAD_SIZE)
            query = turned(query_ref[here, span].astype(FLOAT), cosine_ref[here], sine_ref[here])
            weights = probabilities(query, keys[:extent], allowed)
            grad = grad_ref[here, span]
            weights_grad = dot(grad, value_ref[:extent], (1, 1))
            value_sum[:extent] += dot(weights.astype(BFLOAT), grad, (0, 0))
            mean_grad = jnp.sum(weights * weights_grad, axis=1, keepdims=True)
            score_grad = (weights * (weights_grad - mean_grad) * scale).astype(BFLOAT)
            query_grad = dot(score_grad, keys[:extent], (1, 0))
            key_sum[:extent] += dot(score_grad, query, (0, 0))
            query_grad_ref[here, span] = turned_back(query_grad, cosine_ref[here], sine_ref[here]).astype(BFLOAT)
    shared_grad_ref[:, :HEAD_SIZE] = turned_back(key_sum[...], cosine_ref[...], sine_ref[...]).astype(BFLOAT)
    shared_grad_ref[:, HEAD_SIZE:] = value_sum[...].astype(BFLOAT)


def attention_cost(tokens, width, factor):
    return estimate(
        flops=factor * 2 * tokens * tokens * width,
        bytes_accessed=factor * tokens * width * 8,
        transcendentals=tokens * tokens * width // (2 * HEAD_SIZE),
    )


def attention_specs(tokens, channels):
    width = channels * QUERY_HEADS // DSSM * HEAD_SIZE
    narrow = whole((tokens, HEAD_SIZE))
    return [
        pl.BlockSpec((tokens, width), lambda *_: (0, (STATES + PAIR + 2 * channels) // width)),
        pl.BlockSpec((tokens, HEAD_SIZE), lambda *_: (0, STATES // HEAD_SIZE)),
        pl.BlockSpec((tokens, HEAD_SIZE), lambda *_: (0, STATES // HEAD_SIZE + 1)),
        narrow,
        narrow,
        whole((tokens, LANES)),
        whole((8, tokens)),
    ]


def attention_operands(projected, tables):
    return [projected] * 3 + [tables[name] for name in ("cosine", "sine", "meta", "segment_row")]


def attention_forward(projected, tables):
    tokens = projected.shape[0]
    channels = tables["taps"].shape[1]
    width = channels * QUERY_HEADS // DSSM * HEAD_SIZE
    return pl.pallas_call(
        attention_forward_kernel,
        grid=(1,),
        in_specs=attention_specs(tokens, channels),
        out_specs=pl.BlockSpec((tokens, width), lambda *_: (0, channels // width)),
        out_shape=jax.ShapeDtypeStruct((tokens, channels + width), BFLOAT),
        scratch_shapes=[pltpu.VMEM((tokens, HEAD_SIZE), BFLOAT)],
        compiler_params=pltpu.CompilerParams(vmem_limit_bytes=SCAN_BYTES),
        cost_estimate=attention_cost(tokens, width, 1),
        name="attention_forward",
    )(*attention_operands(projected, tables))


def attention_backward(projected, tables, mixed_grad):
    tokens = projected.shape[0]
    channels = tables["taps"].shape[1]
    width = channels * QUERY_HEADS // DSSM * HEAD_SIZE
    return pl.pallas_call(
        attention_backward_kernel,
        grid=(1,),
        in_specs=attention_specs(tokens, channels)
        + [pl.BlockSpec((tokens, width), lambda *_: (0, channels // width))],
        out_specs=[whole((tokens, width)), whole((tokens, PAIR))],
        out_shape=[jax.ShapeDtypeStruct((tokens, width), BFLOAT), jax.ShapeDtypeStruct((tokens, PAIR), BFLOAT)],
        scratch_shapes=[
            pltpu.VMEM((tokens, HEAD_SIZE), BFLOAT),
            pltpu.VMEM((tokens, HEAD_SIZE), FLOAT),
            pltpu.VMEM((tokens, HEAD_SIZE), FLOAT),
        ],
        compiler_params=pltpu.CompilerParams(vmem_limit_bytes=SCAN_BYTES),
        cost_estimate=attention_cost(tokens, width, 3),
        name="attention_backward",
    )(*attention_operands(projected, tables), mixed_grad)


def mixer_tables(lengths, segment, position, conv_values, conv_states, scan_params):
    tokens = segment.shape[0]
    block = jnp.arange(tokens, dtype=jnp.int32) // SSD_BLOCK
    previous = jnp.concatenate([jnp.full((1,), -1, jnp.int32), segment[:-1]])
    first_previous = jnp.repeat(previous[::SSD_BLOCK], SSD_BLOCK)
    last_segment = jnp.repeat(segment[SSD_BLOCK - 1 :: SSD_BLOCK], SSD_BLOCK)
    length = jnp.sum(
        jnp.where(segment[:, None] == jnp.arange(lengths.shape[0], dtype=jnp.int32)[None, :], lengths[None, :], 0),
        axis=1,
    )
    columns = [
        segment,
        position,
        length - 1 - position,
        segment == first_previous,
        segment == last_segment,
    ]
    meta = jnp.stack([column.astype(FLOAT) for column in columns], axis=1)
    half_width = HEAD_SIZE // 2
    frequency = ROPE_BASE ** (-2.0 * jnp.arange(half_width, dtype=FLOAT) / HEAD_SIZE)
    angle = position.astype(FLOAT)[:, None] * frequency[None, :]
    cosine, sine = jnp.cos(angle), jnp.sin(angle)
    heads = scan_params.shape[1]
    head = jnp.stack([scan_params[0], -jnp.exp(scan_params[1]), scan_params[2]])
    return dict(
        meta=jnp.pad(meta, ((0, 0), (0, LANES - meta.shape[1]))),
        segment_row=jnp.broadcast_to(segment.astype(FLOAT)[None, :], (8, tokens)),
        taps=jnp.pad(conv_values.astype(FLOAT), ((0, 3), (0, 0))),
        state_taps=jnp.pad(conv_states.astype(FLOAT), ((0, 3), (0, 0))),
        head=jnp.pad(head, ((0, 5), (0, LANES - heads))),
        skip=jnp.broadcast_to(jnp.repeat(scan_params[2], HP)[None, :], (8, heads * HP)),
        cosine=jnp.concatenate([cosine, cosine], axis=1),
        sine=jnp.concatenate([-sine, sine], axis=1),
    )


HALVES = 2
DENSE_TILE = 1024


def matrix_rows(values):
    return values.reshape(values.shape[0] * values.shape[1], values.shape[2])


def cut_tiles(width, tile):
    return [(low, min(low + tile, width)) for low in range(0, width, tile)]


def spread_kernel(masks, count, chosen_ref, *rest):
    halves, weights = rest[: 2 * len(masks)], rest[2 * len(masks) : 2 * len(masks) + count]
    out_ref, narrow_ref, out_tile, narrow, sems = rest[-5:]
    rows = halves[0].shape[0]
    shards = weights[0].shape[0]
    depth = shards // HALVES
    lower = weights[-1].shape[2] - LANES
    copies = []
    for at, mask in enumerate(masks):
        left_ref, right_ref = halves[2 * at : 2 * at + 2]
        here = pl.ds(pl.multiple_of((lax.axis_index("col") ^ mask) * rows, rows), rows)

        def through(ref, low, high):
            return dot(left_ref[...], matrix_rows(ref[:depth, :rows, low:high]), (1, 0)) + dot(
                right_ref[...], matrix_rows(ref[depth:, :rows, low:high]), (1, 0)
            )

        def send(tile, target):
            copies.append(pltpu.make_async_copy(tile, target, sems.at[len(copies)]))
            copies[-1].start()

        narrow[at] = (chosen_ref[here, :] * through(weights[-1], lower, lower + LANES)).astype(BFLOAT)
        send(narrow.at[at], narrow_ref.at[here, :])
        column = 0
        for ref in weights:
            for low, high in cut_tiles(ref.shape[2] - (LANES if ref is weights[-1] else 0), DENSE_TILE):
                span = slice(column, column + high - low)
                column += high - low
                raised = matrix_rows(ref[:, rows : rows + NADAPT * RANK // shards, low:high])
                out_tile[at, :, span] = (through(ref, low, high) + dot(narrow[at], raised, (1, 0))).astype(BFLOAT)
                send(out_tile.at[at, :, span], out_ref.at[here, span])
    for copy in copies:
        copy.wait()


def weights_width(gathered):
    return sum(part.shape[2] for part in gathered) - LANES


def spread_blocks(blocks, gathered, selector, held):
    masks = [mask for mask, _ in blocks]
    rows, half = blocks[0][1][0].shape
    width = weights_width(gathered)
    total = selector.shape[0]
    fast, free = pl.BlockSpec(memory_space=pltpu.VMEM), pl.BlockSpec(memory_space=pl.ANY)
    operands = [selector, *[part for _, halves in blocks for part in halves], *gathered]
    in_specs = [fast] * len(operands)
    aliases = {}
    if held is not None:
        aliases = {len(operands): 0, len(operands) + 1: 1}
        operands += list(held)
        in_specs += [free] * 2
    copies = len(masks) * (1 + sum(-(-part.shape[2] // DENSE_TILE) for part in gathered))
    return pl.pallas_call(
        functools.partial(spread_kernel, masks, len(gathered)),
        in_specs=in_specs,
        out_specs=[free] * 2,
        out_shape=[
            jax.ShapeDtypeStruct((total, width), BFLOAT),
            jax.ShapeDtypeStruct((total, LANES), BFLOAT),
        ],
        scratch_shapes=[
            pltpu.VMEM((len(masks), rows, width), BFLOAT),
            pltpu.VMEM((len(masks), rows, LANES), BFLOAT),
            pltpu.SemaphoreType.DMA((copies,)),
        ],
        input_output_aliases=aliases,
        compiler_params=pltpu.CompilerParams(vmem_limit_bytes=DENSE_BYTES),
        cost_estimate=estimate(
            flops=4 * len(masks) * rows * half * (width + LANES),
            bytes_accessed=2 * len(masks) * rows * (2 * half + width),
            transcendentals=0,
        ),
        name="spread_blocks",
    )(*operands)


def collect_kernel(masks, count, values_ref, *refs):
    weights, outs = refs[:count], refs[count:]
    if len(outs) > 2 * len(masks):
        inner_ref, *outs, raise_ref = outs
        raise_ref[...] = dot(inner_ref[...], values_ref[...], (0, 0)).astype(BFLOAT)
    rows = values_ref.shape[0] // 4
    shards = weights[0].shape[0]
    half = shards // HALVES * rows
    width = values_ref.shape[1]
    starts, column = [], 0
    for ref in weights:
        high = min(column + ref.shape[2], width)
        starts.append((column, high))
        column = high
    for at, mask in enumerate(masks):
        here = pl.ds(pl.multiple_of((lax.axis_index("col") ^ mask) * rows, rows), rows)
        first, second = outs[2 * at], outs[2 * at + 1]

        def through(cut):
            total = None
            for (low, high), ref in zip(starts, weights):
                part = dot(values_ref[here, low:high], cut(ref, high - low), (1, 1))
                total = part if total is None else total + part
            return total

        for shard in range(shards):
            out_ref = first if shard < shards // HALVES else second
            column = shard * rows % half
            out_ref[:, column : column + rows] = through(lambda ref, wide: ref[shard, :rows, :wide]).astype(
                out_ref.dtype
            )
        first[:, half:] = through(
            lambda ref, wide: matrix_rows(ref[:, rows : rows + NADAPT * RANK // shards, :wide])
        ).astype(first.dtype)


def collect_blocks(masks, values, gathered, types, inner=()):
    rows = values.shape[0] // 4
    half = gathered[0].shape[0] // HALVES * rows
    fast = pl.BlockSpec(memory_space=pltpu.VMEM)
    out_shape = []
    for pair in types:
        out_shape.append(jax.ShapeDtypeStruct((rows, half + LANES), pair[0]))
        out_shape.append(jax.ShapeDtypeStruct((rows, half), pair[1]))
    out_shape += [jax.ShapeDtypeStruct((LANES, values.shape[1]), BFLOAT) for _ in inner]
    outs = pl.pallas_call(
        functools.partial(collect_kernel, masks, len(gathered)),
        in_specs=[fast] * (1 + len(gathered) + len(inner)),
        out_specs=[fast] * len(out_shape),
        out_shape=out_shape,
        compiler_params=pltpu.CompilerParams(vmem_limit_bytes=DENSE_BYTES),
        cost_estimate=estimate(
            flops=4 * len(masks) * rows * half * values.shape[1],
            bytes_accessed=2 * len(masks) * rows * (values.shape[1] + 4 * half),
            transcendentals=0,
        ),
        name="collect_blocks",
    )(values, *gathered, *inner)
    return [tuple(outs[2 * at : 2 * at + 2]) for at in range(len(masks))] + list(outs[2 * len(masks) :])


def root_mean(values):
    return lax.rsqrt(jnp.mean(values * values, axis=1, keepdims=True) + EPSILON)


def packed_grad(narrow, values, choose):
    half = LANES // 2
    chosen = dot(narrow, choose, (1, 0)).astype(BFLOAT)
    grad = dot(chosen, values, (0, 0))
    low = lax.broadcasted_iota(jnp.int32, (8, LANES), 1) < half
    devices = []
    for start in range(0, grad.shape[1], LANES):
        own = grad[:, start : start + LANES]
        turned_own = pltpu.roll(own, half, 1)
        for first, second in ((own, turned_own), (turned_own, own)):
            devices.append(
                jnp.concatenate(
                    [jnp.where(low, first[at : at + 8], second[at + 8 : at + 16]) for at in (0, 16)], axis=1
                )
            )
    return jnp.concatenate(devices, axis=0).astype(BFLOAT)


def finish_kernel(kind, first_own, first_near, first_far, second_own, second_near, second_far, lower_ref, chosen_ref,
                  *refs):
    half = second_own.shape[1]
    model = HALVES * half
    wide = lambda ref: ref[...].astype(FLOAT)
    first = wide(first_own) + wide(first_near) + wide(first_far)
    second = wide(second_own) + wide(second_near) + wide(second_far)
    inner = (chosen_ref[...] * first[:, half:]).astype(BFLOAT)
    summed = jnp.concatenate([first[:, :half], second], axis=1) + dot(
        inner, matrix_rows(lower_ref[...]), (1, 1)
    )
    if kind == "output":
        residual_ref, place_ref, choose_ref, branch_ref, early_ref, out_ref = refs
        result = (residual_ref[...] + summed).astype(BFLOAT)
        out_ref[:, :model] = dot(place_ref[...], result, (0, 0)).astype(BFLOAT)
        out_ref[:, model : model + 2 * LANES] = packed_grad(inner, branch_ref[...], choose_ref[...])
        out_ref[:, model + 2 * LANES :] = early_ref[...]
        return
    if kind == "forward":
        residual_ref, gain_ref, out_ref, inner_ref, left_ref, right_ref = refs
        hidden = residual_ref[...] + summed
        normed = (hidden * root_mean(hidden) * gain_ref[0:1, :]).astype(BFLOAT)
    else:
        values_ref, upstream_ref, gain_ref, choose_ref, normed_left, normed_right = refs[:6]
        values = values_ref[...]
        scale = root_mean(values)
        weighted = summed * gain_ref[0:1, :]
        mean = jnp.mean(weighted * values, axis=1, keepdims=True)
        hidden = upstream_ref[...].astype(FLOAT) + scale * weighted - values * (scale * scale * scale * mean)
        normed = hidden.astype(BFLOAT)
        packed = packed_grad(
            inner, jnp.concatenate([normed_left[...], normed_right[...]], axis=1), choose_ref[...]
        )
        if kind == "input":
            place_ref, out_ref = refs[6:]
            out_ref[:, :model] = dot(place_ref[...], normed, (0, 0)).astype(BFLOAT)
            out_ref[:, model:] = packed
            return
        given_ref, out_ref, inner_ref, left_ref, right_ref, packed_ref = refs[6:]
        packed_ref[:, : 2 * LANES] = packed
        packed_ref[:, 2 * LANES :] = packed_grad(given_ref[...], normed, choose_ref[...])
    out_ref[...] = hidden
    inner_ref[...] = inner
    left_ref[...] = normed[:, :half]
    right_ref[...] = normed[:, half:]


def finish(kind, parts, gathered, own_selector, *operands):
    rows = own_selector.shape[0]
    half = parts[3].shape[1]
    shards = gathered[-1].shape[0]
    model = HALVES * half
    lower = gathered[-1][:, : model // shards, -LANES:]
    shaped = jax.ShapeDtypeStruct
    if kind in ("output", "input"):
        out_shape = shaped((rows, model + 2 * LANES * (3 if kind == "output" else 1)), BFLOAT)
        out_specs = whole(out_shape.shape)
    else:
        out_shape = [shaped((rows, model), FLOAT), shaped((rows, LANES), BFLOAT)]
        out_shape += [shaped((rows, half), BFLOAT)] * 2
        out_shape += [shaped((rows, 4 * LANES), BFLOAT)] * (kind == "backward")
        out_specs = [whole(shape.shape) for shape in out_shape]
    given = [*parts, lower, own_selector, *operands]
    return pl.pallas_call(
        functools.partial(finish_kernel, kind),
        grid=(1,),
        in_specs=[whole(value.shape) for value in given],
        out_specs=out_specs,
        out_shape=out_shape,
        compiler_params=pltpu.CompilerParams(vmem_limit_bytes=FINISH_BYTES),
        cost_estimate=estimate(
            flops=2 * rows * model * LANES, bytes_accessed=rows * model * 20, transcendentals=0
        ),
        name="finish_" + kind,
    )(*given)


def onward_kernel(first_kept, first_part, second_kept, second_part, first_ref, second_ref):
    first_ref[...] = (first_kept[...] + first_part[...].astype(FLOAT)).astype(BFLOAT)
    second_ref[...] = (second_kept[...] + second_part[...].astype(FLOAT)).astype(BFLOAT)


def sum_onward(first_kept, first_part, second_kept, second_part):
    return pl.pallas_call(
        onward_kernel,
        in_specs=[pl.BlockSpec(memory_space=pltpu.VMEM)] * 4,
        out_specs=[pl.BlockSpec(memory_space=pltpu.VMEM)] * 2,
        out_shape=[jax.ShapeDtypeStruct(part.shape, BFLOAT) for part in (first_part, second_part)],
        compiler_params=pltpu.CompilerParams(vmem_limit_bytes=DENSE_BYTES),
        name="sum_onward",
    )(first_kept, first_part, second_kept, second_part)


def send_kernel(target_column, target_row, tokens_ref, adapter_ref, sent_ref, matrix_ref):
    rows = tokens_ref.shape[0]
    model = tokens_ref.shape[1]
    peer = adapter_ref.shape[0]
    column, row = target_column[:, 0:1], target_row[0:1, :]
    earlier = lax.broadcasted_iota(jnp.int32, (rows, rows), 0) < lax.broadcasted_iota(jnp.int32, (rows, rows), 1)
    same = jnp.where((column // rows == row // rows) & earlier, 1.0, 0.0)
    place = (row // rows) * peer + jnp.sum(same, axis=0, keepdims=True).astype(jnp.int32)
    matrix = (lax.broadcasted_iota(jnp.int32, (rows, rows), 0) == place).astype(BFLOAT)
    matrix_ref[...] = matrix
    sent_ref[:, :model] = dot(matrix, tokens_ref[...], (1, 0)).astype(BFLOAT)
    lane = lax.broadcasted_iota(jnp.int32, (rows, LANES), 1)
    slots = jnp.where(lane == 0, column % rows, 0).astype(FLOAT).astype(BFLOAT)
    notes = dot(matrix, slots, (1, 0))
    sent_ref[:, model:] = jnp.where(lane == 0, notes, adapter_ref[0:1, :]).astype(BFLOAT)


def send_tokens(target, tokens, adapters, peer):
    rows, model = tokens.shape
    notes = jnp.pad(adapters.astype(FLOAT), (1, LANES - 1 - adapters.shape[0]))
    return pl.pallas_call(
        send_kernel,
        in_specs=[pl.BlockSpec(memory_space=pltpu.VMEM)] * 4,
        out_specs=[pl.BlockSpec(memory_space=pltpu.VMEM)] * 2,
        out_shape=[
            jax.ShapeDtypeStruct((rows, model + LANES), BFLOAT),
            jax.ShapeDtypeStruct((rows, rows), BFLOAT),
        ],
        compiler_params=pltpu.CompilerParams(vmem_limit_bytes=DENSE_BYTES),
        name="send_tokens",
    )(
        jnp.broadcast_to(target[:, None], (rows, LANES)),
        jnp.broadcast_to(target[None, :], (8, rows)),
        tokens,
        jnp.broadcast_to(notes[None, :], (peer, LANES)),
    )


def arrive_kernel(arrived_ref, gain_ref, own_ref, matrix_ref, left_ref, right_ref):
    rows, model = own_ref.shape
    slots = arrived_ref[:, model:].astype(FLOAT).T[0:1, :]
    row = lax.broadcasted_iota(jnp.int32, (rows, rows), 0).astype(FLOAT)
    matrix = (row == slots).astype(BFLOAT)
    matrix_ref[...] = matrix
    own = dot(matrix, arrived_ref[:, :model], (1, 0))
    own_ref[...] = own
    normed = (own * root_mean(own) * gain_ref[0:1, :]).astype(BFLOAT)
    left_ref[...] = normed[:, : model // HALVES]
    right_ref[...] = normed[:, model // HALVES :]


def arrive_tokens(arrived, gain):
    rows, model = arrived.shape[0], arrived.shape[1] - LANES
    return pl.pallas_call(
        arrive_kernel,
        in_specs=[pl.BlockSpec(memory_space=pltpu.VMEM)] * 2,
        out_specs=[pl.BlockSpec(memory_space=pltpu.VMEM)] * 4,
        out_shape=[
            jax.ShapeDtypeStruct((rows, model), FLOAT),
            jax.ShapeDtypeStruct((rows, rows), BFLOAT),
            jax.ShapeDtypeStruct((rows, model // HALVES), BFLOAT),
            jax.ShapeDtypeStruct((rows, model // HALVES), BFLOAT),
        ],
        compiler_params=pltpu.CompilerParams(vmem_limit_bytes=DENSE_BYTES),
        name="arrive_tokens",
    )(arrived, gain)


GATE_WIDTH = DSSM // QUERY_HEADS
PAIR_WIDTH = 2 * KEY_VALUE_HEADS * HEAD_SIZE // QUERY_HEADS
STATE_WIDTH = 2 * NSTATE // QUERY_HEADS
STEP_WIDTH = NH // QUERY_HEADS
ALL_AXES = ("row", "col")


def pad_columns(values, width):
    return jnp.pad(values, ((0, 0), (0, width - values.shape[1])))


def after(values, *earlier):
    return lax.optimization_barrier((values, *earlier))[0]


def after_all(values, *earlier):
    return lax.optimization_barrier((*values, *earlier))[: len(values)]


def unit_parts(values, units):
    cuts = [0]
    for width in (GATE_WIDTH, GATE_WIDTH, HEAD_SIZE, PAIR_WIDTH, STATE_WIDTH, STEP_WIDTH):
        cuts.append(cuts[-1] + width)
    return [
        jnp.concatenate(
            [values[:, unit * UNIT_IN + low : unit * UNIT_IN + high] for unit in range(units)], axis=1
        )
        for low, high in zip(cuts[:-1], cuts[1:])
    ]


def restore_units(parts, units):
    ordered = []
    for unit in range(units):
        for part in parts:
            width = part.shape[1] // units
            ordered.append(part[:, unit * width : (unit + 1) * width])
    return jnp.concatenate(ordered, axis=1)


def split_halves(values, units, first, axis):
    block = values.shape[axis] // units
    take = lambda low, high: lax.slice_in_dim(values, low, high, axis=axis)
    parts = [take(unit * block, unit * block + first) for unit in range(units)]
    parts += [take(unit * block + first, (unit + 1) * block) for unit in range(units)]
    return jnp.concatenate(parts, axis=axis)


def join_halves(values, units, first, axis):
    block = values.shape[axis] // units
    rest = block - first
    take = lambda low, high: lax.slice_in_dim(values, low, high, axis=axis)
    parts = []
    for unit in range(units):
        parts.append(take(unit * first, (unit + 1) * first))
        parts.append(take(units * first + unit * rest, units * first + (unit + 1) * rest))
    return jnp.concatenate(parts, axis=axis)


def quick(rows):
    return lax.axis_size("col") == 4 and lax.axis_size("row") == 8 and rows == 256


def spread_early(halves, gathered, selector):
    left, right = halves
    far_left, near_right = flip(left, 2), flip(right, 1)
    near_left, far_right = flip(left, 1), flip(right, 2)
    held = spread_blocks([(0, halves)], gathered, selector, None)
    onward_left, onward_right = after_all((far_left, near_right), held[1])
    corner = flip(onward_left, 1), flip(onward_right, 2)
    held = spread_blocks([(1, (near_left, near_right))], gathered, selector, held)
    held = spread_blocks([(2, (far_left, far_right))], gathered, selector, held)
    return spread_blocks([(3, corner)], gathered, selector, held)


def flip(values, mask):
    return lax.ppermute(values, "col", [(i, i ^ mask) for i in range(4)])


def gather_blocks(halves):
    left, right = halves
    far_left, near_right = flip(left, 2), flip(right, 1)
    near_left, far_right = flip(left, 1), flip(right, 2)
    corner_left, corner_right = flip(far_left, 1), flip(near_right, 2)
    return [
        (0, (left, right)),
        (1, (near_left, near_right)),
        (2, (far_left, far_right)),
        (3, (corner_left, corner_right)),
    ]


def rows_of(values, block, rows):
    return lax.dynamic_slice_in_dim(values, block * rows, rows, 0)


def spread_gathered(blocks, gathered, selector):
    held = None
    for block in blocks:
        held = spread_blocks([block], gathered, selector, held)
    return held


def spread_project(halves, gathered, selector):
    rows = halves[0].shape[0]
    if quick(rows):
        return spread_gathered(gather_blocks(halves), gathered, selector)
    wide, narrow_factor = gathered
    width = narrow_factor.shape[1]
    both = product(lax.all_gather(jnp.concatenate(halves, axis=1), "col", axis=0, tiled=True), wide)
    narrow = (selector * both[:, width:]).astype(BFLOAT)
    return (both[:, :width] + product(narrow, narrow_factor)).astype(BFLOAT), narrow


PIECE_TYPES = [(BFLOAT, BFLOAT), (BFLOAT, FLOAT), (FLOAT, BFLOAT), (FLOAT, FLOAT)]


def collect_pieces(values, gathered, at_once):
    if at_once:
        return collect_blocks([3, 1, 2, 0], values, gathered, PIECE_TYPES)
    (corner,) = collect_blocks([3], values, gathered, PIECE_TYPES[:1])
    values = after(values, corner[0])
    return [corner, *collect_blocks([1, 2, 0], values, gathered, PIECE_TYPES[1:])]


def collect_send(pieces, ordered=True):
    corner, near, far, own = pieces
    arriving = flip(corner[0], 1), flip(corner[1], 2)
    sent_near, sent_far = after_all((near[0], far[1]), *arriving) if ordered else (near[0], far[1])
    return own, flip(sent_near, 1), flip(sent_far, 2), far[0], near[1], arriving


def collect_middle(started):
    own, near_first, far_second, far_first, near_second, arriving = started
    return (own, near_first, far_second), sum_onward(far_first, arriving[0], near_second, arriving[1])


def collect_onward(onward):
    return flip(onward[0], 2), flip(onward[1], 1)


def collect_end(kept, last, kind, gathered, own_selector, *operands):
    own, near_first, far_second = kept
    parts = [own[0], near_first, last[0], own[1], far_second, last[1]]
    return finish(kind, parts, gathered, own_selector, *operands)


def collect_project(values, gathered, kind, own_selector, *operands):
    rows, model = own_selector.shape[0], operands[0].shape[1]
    if quick(rows):
        kept, onward = collect_middle(collect_send(collect_pieces(values, gathered, False)))
        return collect_end(kept, collect_onward(onward), kind, gathered, own_selector, *operands)
    wide, narrow_factor = gathered
    width = narrow_factor.shape[1]
    partial = jnp.concatenate(
        [contract_last(values, wide[:, :width]), contract_last(values, narrow_factor)], axis=1
    ).astype(BFLOAT)
    summed = lax.psum_scatter(partial, "col", scatter_dimension=0, tiled=True).astype(FLOAT)
    inner = (own_selector * summed[:, model:]).astype(BFLOAT)
    summed = summed[:, :model] + contract_last(inner, wide[:, width:])
    if kind == "output":
        return (operands[0] + summed).astype(BFLOAT), inner
    if kind == "forward":
        residual, gain = operands
        hidden = residual + summed
        return hidden, inner, *cut_halves(rms_norm(hidden, gain[0]).astype(BFLOAT))
    values, upstream, gain = operands
    _, back = jax.vjp(lambda given: rms_norm(given, gain[0]), values)
    hidden = upstream.astype(FLOAT) + back(summed)[0]
    if kind == "input":
        return hidden.astype(BFLOAT), inner
    return hidden, inner, *cut_halves(hidden.astype(BFLOAT))


def cut_halves(values):
    half = values.shape[1] // HALVES
    return values[:, :half], values[:, half:]


def local(
    tokens_in,
    cotangent,
    target,
    sequence_lengths,
    sequence_adapter,
    norm_gains,
    weight_in,
    conv_values,
    conv_states,
    scan_params,
    weight_mix,
    weight_feed,
    weight_down,
    in_lower,
    in_raise,
    mix_lower,
    mix_raise,
    feed_lower,
    feed_raise,
    down_lower,
    down_raise,
):
    cols = lax.axis_size("col")
    rows_axis = lax.axis_size("row")
    col = lax.axis_index("col")
    devices = cols * rows_axis
    rows = tokens_in.shape[0]
    model = tokens_in.shape[1]
    total = rows * cols
    units = QUERY_HEADS // cols
    channels = units * GATE_WIDTH
    peer = rows // devices
    lengths, adapters = sequence_lengths[0], sequence_adapter[0]
    sequences = lengths.shape[0]
    fast = quick(rows)
    key_head = col * units // (QUERY_HEADS // KEY_VALUE_HEADS)
    exchange = lambda values: lax.all_to_all(values, ALL_AXES, split_axis=0, concat_axis=0, tiled=True)

    sent, send_matrix = send_tokens(target, tokens_in, adapters, peer)
    shards = []

    def gather_weight(weight, lower, raised):
        top = jnp.concatenate([weight, lower], axis=1)
        if fast:
            bottom = pad_columns(raised, top.shape[1])
            shards.append(jnp.concatenate([top, bottom], axis=0))
            return (lax.all_gather(shards[-1], "row", axis=0),)
        wide = lax.all_gather(top, "row", axis=0, tiled=True)
        return wide, lax.all_gather(raised, "row", axis=0, tiled=True)

    depth = weight_in.shape[0]
    height = depth + in_raise.shape[0]
    given = after(jnp.concatenate([weight_in, in_raise], axis=0), send_matrix)
    gates, convs, queries, pairs, states, steps = unit_parts(given, units)
    pair_width, state_width = pairs.shape[1], states.shape[1]
    taps = jnp.concatenate([jnp.zeros((KCONV + 1, pair_width), BFLOAT), conv_states], axis=1)
    taps = jnp.pad(taps, ((0, 16 - KCONV - 1), (0, 0)))
    shared = jnp.concatenate([jnp.concatenate([pairs, states], axis=1), taps], axis=0)
    own_columns = jnp.concatenate([gates, convs, queries, pad_columns(steps, LANES)], axis=1)
    if fast:
        shared_shard = shared
        shared = lax.all_gather(shared_shard, "row", axis=0)
        weights_own = gather_weight(own_columns[:depth], in_lower, own_columns[depth:])
    arrived = exchange(sent)
    gains = jnp.broadcast_to(norm_gains.astype(FLOAT)[:, None, :], (2, 8, model))
    if fast:
        near, far = flip(shared, 1), flip(shared, 2)
        arrived = after(arrived, near, far, shards[0])
    own_input, place_matrix, *normed_one = arrive_tokens(arrived.reshape(rows, model + LANES), gains[0])
    blocks_one = gather_blocks(normed_one) if fast else normed_one
    if fast:
        held = jnp.zeros((cols,) + shared.shape, BFLOAT)
        for block, values in ((col, shared), (col ^ 1, near), (col ^ 2, far)):
            held = lax.dynamic_update_index_in_dim(held, values, block, 0)
        split = shared.shape[0] // 2
        corner = jnp.concatenate([flip(near[:split], 2), flip(far[split:], 1)], axis=0)
        held = lax.dynamic_update_index_in_dim(held, corner, col ^ 3, 0)
    else:
        held = lax.all_gather(shared, "col", axis=0)
    all_pairs = jnp.concatenate([held[at, ..., :height, :pair_width] for at in range(cols)], axis=-1)
    pick = lambda start: lax.select_n(
        key_head,
        *[all_pairs[..., start + at * HEAD_SIZE : start + (at + 1) * HEAD_SIZE] for at in range(KEY_VALUE_HEADS)],
    )
    shared_columns = jnp.concatenate(
        [held[at, ..., :height, pair_width:] for at in range(cols)]
        + [pick(0), pick(KEY_VALUE_HEADS * HEAD_SIZE)],
        axis=-1,
    )
    tap_rows = held[:, 0] if fast else held
    all_taps = jnp.concatenate(
        [tap_rows[at, height : height + KCONV + 1, pair_width:] for at in range(cols)], axis=1
    )
    if fast:
        weights_in = (shared_columns, *weights_own)
    else:
        columns = jnp.concatenate([shared_columns, own_columns], axis=1)
        weights_in = gather_weight(columns[:depth], in_lower, columns[depth:])
    weights_mix = gather_weight(
        after(split_halves(weight_mix, units, GATE_WIDTH, 0).T, sent),
        mix_raise.T,
        split_halves(mix_lower, units, GATE_WIDTH, 0).T,
    )
    weights_feed = gather_weight(
        after(split_halves(weight_feed, units, UNIT_FF, 1), arrived),
        feed_lower,
        split_halves(feed_raise, units, UNIT_FF, 1),
    )

    source_adapters = arrived.reshape(rows, model + LANES)[::peer, model + 1 : model + 1 + sequences].astype(jnp.int32)
    segment, position, selector = sequence_tables(lengths, adapters, total)
    own_selector = rows_of(selector, col, rows)
    own_segment = rows_of(segment, col, rows)
    tables = mixer_tables(lengths, segment, position, conv_values, all_taps, scan_params)

    def compact_grad(narrow, values):
        parts = [
            lax.dynamic_slice_in_dim(narrow, adapters[at] * RANK, RANK, 1)
            * (own_segment == at).astype(BFLOAT)[:, None]
            for at in range(sequences)
        ]
        grad = contract_first(jnp.concatenate(parts, axis=1), values).astype(BFLOAT)
        kept = sequences * RANK
        grad = grad.reshape(kept, devices, model // devices).transpose(1, 0, 2)
        return grad.reshape(devices, peer, kept * model // devices // peer)

    def expand_grad(dealt):
        kept = sequences * RANK
        dealt = dealt.reshape(devices * kept, model // devices)
        adapter_row = (source_adapters[:, :, None] * RANK + jnp.arange(RANK, dtype=jnp.int32)).reshape(-1)
        chosen = (jnp.arange(NADAPT * RANK, dtype=jnp.int32)[:, None] == adapter_row[None, :]).astype(BFLOAT)
        return product(chosen, dealt)

    def send_back(values, grads):
        back = contract_first(place_matrix, values).astype(BFLOAT).reshape(devices, peer, model)
        return exchange(jnp.concatenate([back, *grads], axis=2))

    def expand_packed(dealt, count):
        slots = dealt.shape[0] * peer
        block = jnp.arange(2 * LANES // (model // devices), dtype=jnp.int32)[:, None, None]
        row = jnp.arange(peer, dtype=jnp.int32)[None, None, :]
        place = block * peer + row
        adapter = jnp.where(place < RANK, source_adapters[None, :, 0:1], source_adapters[None, :, 1:2])
        adapter_row = (adapter * RANK + place % RANK).reshape(block.shape[0], 1, slots)
        chosen = (jnp.arange(NADAPT * RANK, dtype=jnp.int32)[None, :, None] == adapter_row).astype(BFLOAT)
        sums = product(chosen.reshape(-1, slots), dealt.reshape(slots, dealt.shape[2]))
        sums = sums.reshape(block.shape[0], NADAPT * RANK, dealt.shape[2])
        width = model // devices
        return [
            sum(
                sums[at, :, grad * 2 * LANES + at * width : grad * 2 * LANES + (at + 1) * width]
                for at in range(block.shape[0])
            )
            for grad in range(count)
        ]

    def take_back(dealt, count):
        returned = contract_first(send_matrix, dealt[:, :, :model].reshape(rows, model)).astype(BFLOAT)
        if fast:
            return returned, expand_packed(dealt[:, :, model:], count)
        width = (dealt.shape[2] - model) // count
        return returned, [
            expand_grad(dealt[:, :, model + at * width : model + (at + 1) * width]) for at in range(count)
        ]

    projected, inner_in = (spread_gathered if fast else spread_project)(blocks_one, weights_in, selector)

    sent_grad = product(send_matrix, cotangent).astype(BFLOAT).reshape(devices, peer, model)
    arrived_grad = exchange(after(sent_grad, normed_one[0])).reshape(rows, model)
    branch_two = product(place_matrix, arrived_grad).astype(BFLOAT)
    weights_down = gather_weight(after(weight_down.T, projected), down_raise.T, down_lower.T)

    mixed_out = attention_forward(projected, tables)
    mixed_out, scanned, carried = scan_forward(projected, tables, mixed_out)
    hidden, inner_out, *normed_two = collect_project(mixed_out, weights_mix, "forward", own_selector, own_input, gains[1])
    gate_up, inner_feed = spread_project(normed_two, weights_feed, selector)
    branch_halves = cut_halves(after(branch_two, projected))
    if fast:
        act_grad, narrow_two = spread_blocks(gather_blocks(branch_halves), weights_down, selector, None)
    else:
        act_grad, narrow_two = spread_project(branch_halves, weights_down, selector)
    half_feed = units * UNIT_FF
    gate_part, up_part = gate_up[:, :half_feed].astype(FLOAT), gate_up[:, half_feed:].astype(FLOAT)
    gate = jax.nn.sigmoid(gate_part)
    silu = gate_part * gate
    activated = (silu * up_part).astype(BFLOAT)
    wide_grad = act_grad.astype(FLOAT)
    feed_grad = jnp.concatenate(
        [wide_grad * up_part * (gate * (1.0 + gate_part * (1.0 - gate))), wide_grad * silu], axis=1
    ).astype(BFLOAT)
    choose = (
        jnp.arange(NADAPT * RANK, dtype=jnp.int32)[:, None]
        == (adapters[:, None] * RANK + jnp.arange(RANK, dtype=jnp.int32)[None, :]).reshape(1, -1)
    ).astype(BFLOAT)
    if fast:
        pieces = collect_pieces(after(activated, feed_grad), weights_down, True)
        kept, onward = collect_middle(collect_send(collect_pieces(feed_grad, weights_feed, False)))
        hidden_grad, narrow_three, left, right, early_grads = collect_end(
            kept,
            collect_onward(onward),
            "backward",
            weights_feed,
            own_selector,
            after(hidden, pieces[3][0]),
            branch_two,
            gains[1],
            choose,
            *normed_two,
            inner_out,
        )
        mixed_grad, narrow_one = spread_early((left, right), weights_mix, selector)
    else:
        hidden_grad, narrow_three, *branch_one = collect_project(
            feed_grad, weights_feed, "backward", own_selector, hidden, branch_two, gains[1]
        )
        mixed_grad, narrow_one = spread_project(branch_one, weights_mix, selector)

    if fast:
        near_parts = after_all((*pieces[0], pieces[1][0], pieces[2][1]), mixed_grad)
        started = collect_send(
            [near_parts[:2], (near_parts[2], pieces[1][1]), (pieces[2][0], near_parts[3]), pieces[3]], False
        )
        attended_grads = attention_backward(projected, tables, after(mixed_grad, near_parts[0]))
        kept, onward = collect_middle((*started[:5], after_all(started[5], attended_grads[1])))
        scan_inputs = (projected, tables, scanned, carried, after(mixed_grad, *onward), attended_grads)
        scan_part = list(scan_backward(*scan_inputs, 0, 2, None))
        payload = collect_end(
            kept,
            collect_onward(onward),
            "output",
            weights_down,
            own_selector,
            after(hidden, scan_part[2]),
            place_matrix,
            choose,
            branch_two,
            early_grads,
        )
        dealt_out = exchange(payload.reshape(devices, peer, -1))
        scan_part[2] = after(scan_part[2], payload)
        projected_grad = scan_backward(*scan_inputs, 1, 2, scan_part)[0]
        *pieces_in, raise_grad = collect_blocks([3, 1, 2, 0], projected_grad, weights_in, PIECE_TYPES, [inner_in])
        started_in = collect_send(pieces_in)
        kept_in, onward_in = collect_middle(started_in)
    else:
        block_out, inner_down = collect_project(activated, weights_down, "output", own_selector, hidden)
        attended_grads = attention_backward(projected, tables, mixed_grad)
        projected_grad = scan_backward(
            projected, tables, scanned, carried, mixed_grad, attended_grads, 0, 1, None
        )[0]
        dealt_out = send_back(
            block_out,
            [
                compact_grad(inner_down, branch_two),
                compact_grad(narrow_three, jnp.concatenate(normed_two, axis=1)),
                compact_grad(inner_out, jnp.concatenate(branch_one, axis=1)),
            ],
        )

    def sum_rows(values):
        return lax.psum_scatter(values.astype(BFLOAT), "row", scatter_dimension=0, tiled=True).astype(FLOAT)

    early_parts = [
        contract_first(narrow_one, mixed_out),
        contract_first(inner_feed, feed_grad),
        contract_first(narrow_two, activated),
    ]
    early = sum_rows(jnp.concatenate(early_parts, axis=1))

    late = sum_rows(raise_grad if fast else contract_first(inner_in, projected_grad))

    if fast:
        payload = collect_end(
            kept_in,
            collect_onward(onward_in),
            "input",
            weights_in,
            own_selector,
            own_input,
            after(hidden_grad, dealt_out),
            gains[0],
            choose,
            *normed_one,
            place_matrix,
        )
        dealt_grad = exchange(payload.reshape(devices, peer, -1))
    else:
        input_grad, narrow_four = collect_project(
            projected_grad, weights_in, "input", own_selector, own_input, hidden_grad, gains[0]
        )
        dealt_grad = send_back(input_grad, [compact_grad(narrow_four, jnp.concatenate(normed_one, axis=1))])
        payload = input_grad
    dealt_out, early, late = after_all((dealt_out, early, late), payload)
    early_cuts = [0, early_parts[0].shape[1]]
    early_cuts.append(early_cuts[1] + early_parts[1].shape[1])
    grad_mix_lower = join_halves(early[:, : early_cuts[1]], units, GATE_WIDTH, 1).T
    grad_feed_raise = join_halves(early[:, early_cuts[1] : early_cuts[2]], units, UNIT_FF, 1)
    grad_down_lower = early[:, early_cuts[2] :].T

    key_columns = late[:, STATES : STATES + HEAD_SIZE]
    value_columns = late[:, STATES + HEAD_SIZE : STATES + PAIR]
    mine = [(key_head == at).astype(FLOAT) for at in range(KEY_VALUE_HEADS)]
    pair_grad = jnp.concatenate([part * here for part in (key_columns, value_columns) for here in mine], axis=1)
    stacked = jnp.stack(
        [
            jnp.concatenate(
                [
                    pair_grad[:, at * pair_width : (at + 1) * pair_width],
                    late[:, at * state_width : (at + 1) * state_width],
                ],
                axis=1,
            )
            for at in range(cols)
        ]
    )
    if fast:
        piece = lambda mask: lax.dynamic_index_in_dim(stacked, col ^ mask, 0, False)
        shared_sum = piece(0) + flip(piece(1), 1) + flip(piece(2), 2) + flip(piece(3), 3)
    else:
        shared_sum = lax.psum_scatter(
            stacked.reshape(stacked.shape[0] * stacked.shape[1], -1), "col", scatter_dimension=0, tiled=True
        )
    late = jnp.concatenate([shared_sum, late[:, STATES + PAIR :]], axis=1)
    shared_width = pair_width + state_width
    cuts = [shared_width]
    for width in (channels, channels, units * HEAD_SIZE, units * STEP_WIDTH):
        cuts.append(cuts[-1] + width)
    gate_columns, conv_columns, query_columns, step_columns = [
        late[:, low:high] for low, high in zip(cuts[:-1], cuts[1:])
    ]
    grad_in_raise = restore_units(
        [
            gate_columns,
            conv_columns,
            query_columns,
            late[:, :pair_width],
            late[:, pair_width:shared_width],
            step_columns,
        ],
        units,
    )

    returned_out, (grad_down_raise, grad_feed_lower, grad_mix_raise) = take_back(dealt_out, 3)
    returned_grad, (grad_in_lower,) = take_back(dealt_grad, 1)
    return (
        returned_out,
        returned_grad,
        grad_in_lower.T,
        grad_in_raise,
        grad_mix_lower,
        grad_mix_raise,
        grad_feed_lower.T,
        grad_feed_raise,
        grad_down_lower,
        grad_down_raise,
    )


def solution(mesh):
    in_specs = (
        P(("row", "col"), None),
        P(("row", "col"), None),
        P(("row", "col")),
        P("row", None),
        P("row", None),
        P(),
        P("row", "col"),
        P(None, "col"),
        P(None, "col"),
        P(None, "col"),
        P("col", "row"),
        P("row", "col"),
        P("col", "row"),
        P("row", None),
        P("row", "col"),
        P("col", "row"),
        P(None, "row"),
        P("row", None),
        P("row", "col"),
        P("col", "row"),
        P(None, "row"),
    )
    out_specs = (
        P(("row", "col"), None),
        P(("row", "col"), None),
        P(("row", "col"), None),
        P("row", "col"),
        P("col", "row"),
        P(None, ("row", "col")),
        P(("row", "col"), None),
        P("row", "col"),
        P("col", "row"),
        P(None, ("row", "col")),
    )
    return jax.shard_map(local, mesh=mesh, in_specs=in_specs, out_specs=out_specs, check_vma=False)
```

```python
import functools
import math

import jax
import jax.numpy as jnp
from jax import lax
from jax.experimental import pallas as pl
from jax.experimental.pallas import tpu as pltpu
from jax.sharding import PartitionSpec as P

NH = 48
HP = 64
NSTATE = 256
KCONV = 4
QUERY_HEADS = 8
KEY_VALUE_HEADS = 2
HEAD_SIZE = 128
RANK = 16
NADAPT = 8
SSD_BLOCK = 256
DSSM = 3072
UNIT_IN = 1030
UNIT_FF = 512


EPSILON = 1e-05
ROPE_BASE = 10000.0
NEGATIVE = -1e30
FLOAT = jnp.float32
BFLOAT = jnp.bfloat16


def product(left, right):
    return jnp.dot(left, right, preferred_element_type=FLOAT)


def contract_last(left, right):
    return lax.dot_general(left, right, (((1,), (1,)), ((), ())), preferred_element_type=FLOAT)


def contract_first(left, right):
    return lax.dot_general(left, right, (((0,), (0,)), ((), ())), preferred_element_type=FLOAT)


def rms_norm(values, gain):
    return values * lax.rsqrt(jnp.mean(values * values, axis=-1, keepdims=True) + EPSILON) * gain


def sequence_tables(lengths, adapters, sequence_length):
    sequence_count = lengths.shape[0]
    boundary = jnp.cumsum(lengths)
    token_index = jnp.arange(sequence_length, dtype=jnp.int32)
    passed = (token_index[:, None] >= boundary[None, :]).astype(jnp.int32)
    segment = jnp.sum(passed, axis=1)
    segment_start = jnp.sum(passed * lengths[None, :], axis=1)
    position = token_index - segment_start
    member = (segment[:, None] == jnp.arange(sequence_count, dtype=jnp.int32)[None, :]).astype(
        jnp.int32
    )
    chosen = jnp.sum(member * adapters[None, :], axis=1)
    column = jnp.arange(NADAPT * RANK, dtype=jnp.int32) // RANK
    selector = (chosen[:, None] == column[None, :]).astype(FLOAT)
    return (segment, position, selector)


ESTIMATE = 16
SCAN_BYTES = 32 * 1024 * 1024
DENSE_BYTES = 16 * 1024 * 1024
FINISH_BYTES = 32 * 1024 * 1024
LANES = 128


def whole(shape):
    return pl.BlockSpec(shape, lambda *_: (0,) * len(shape))


def estimate(flops, bytes_accessed, transcendentals):
    return pl.CostEstimate(
        flops=flops // ESTIMATE,
        bytes_accessed=bytes_accessed // ESTIMATE,
        transcendentals=transcendentals // ESTIMATE,
    )


def dot(left, right, contract):
    return lax.dot_general(left, right, ((contract[:1], contract[1:]), ((), ())), preferred_element_type=FLOAT)


def parts_of(values, count):
    parts = []
    for _ in range(count):
        part = values.astype(BFLOAT)
        parts.append(part)
        values = values - part.astype(FLOAT)
    return parts


def running_sum(values, triangle, contract):
    width = values.shape[1]
    split = dot(triangle, jnp.concatenate(parts_of(values, 3), axis=1), contract)
    return split[:, :width] + split[:, width : 2 * width] + split[:, 2 * width :]


def head_spread(values, expand):
    return dot(jnp.concatenate(parts_of(values, 2), axis=1), expand, (1, 0))


def head_sum(values, expand):
    high, low = parts_of(values, 2)
    single = expand[:LANES]
    return dot(high, single, (1, 1)) + dot(low, single, (1, 1))


def silu_parts(values):
    gate = 1.0 / (1.0 + jnp.exp(-values))
    return values * gate, gate


def expand_table(channels):
    row = lax.broadcasted_iota(jnp.int32, (2 * LANES, channels), 0) % LANES
    channel = lax.broadcasted_iota(jnp.int32, (2 * LANES, channels), 1) // HP
    return (row == channel).astype(BFLOAT)


def conv_sum(current_ref, before_ref, taps_ref, meta):
    rows = SSD_BLOCK
    current = current_ref[...].astype(FLOAT)
    window = jnp.concatenate([before_ref[...].astype(FLOAT)[8:16], current], axis=0)
    summed = taps_ref[KCONV : KCONV + 1, :] + current * taps_ref[0:1, :]
    for lag in range(1, KCONV):
        shifted = window[8 - lag : 8 - lag + rows]
        summed = summed + jnp.where(meta[:, 1:2] >= lag, shifted, 0.0) * taps_ref[lag : lag + 1, :]
    return summed


def conv_back(summed_grad, later, taps_ref, meta):
    rows = SSD_BLOCK
    window = jnp.concatenate([summed_grad, later[...]], axis=0)
    grad = summed_grad * taps_ref[0:1, :]
    for lag in range(1, KCONV):
        grad = grad + jnp.where(meta[:, 2:3] >= lag, window[lag : lag + rows], 0.0) * taps_ref[lag : lag + 1, :]
    later[...] = summed_grad[:8]
    return grad


def silu_slope(values, gate):
    return gate * (1.0 + values * (1.0 - gate))


def scan_block(
    conv_ref, before_ref, state_ref, state_before_ref, step_ref, meta_ref, segment_ref, taps_ref, state_taps_ref, head_ref,
    turned_over,
):
    rows = SSD_BLOCK
    channels = conv_ref.shape[1]
    meta = meta_ref[...]
    summed = conv_sum(conv_ref, before_ref, taps_ref, meta)
    activated, conv_gate = silu_parts(summed)
    wide_inputs = activated.astype(BFLOAT).astype(FLOAT)
    state_summed = conv_sum(state_ref, state_before_ref, state_taps_ref, meta)
    state_values, state_gate = silu_parts(state_summed)
    write = state_values[:, :NSTATE].astype(BFLOAT)
    read = state_values[:, NSTATE:].astype(BFLOAT)
    raw = step_ref[...].astype(FLOAT) + head_ref[0:1, :]
    steps = jnp.maximum(raw, 0.0) + jnp.log1p(jnp.exp(-jnp.abs(raw)))
    row = lax.broadcasted_iota(jnp.int32, (rows, rows), 0)
    column = lax.broadcasted_iota(jnp.int32, (rows, rows), 1)
    triangle = (row >= column).astype(BFLOAT)
    total = running_sum(steps * head_ref[1:2, :], triangle, (1, 0))
    entered = jnp.exp(total) * meta[:, 3:4]
    leaving = jnp.exp(total[rows - 1 : rows] - total) * meta[:, 4:5]
    expand = expand_table(channels)
    spread = head_spread(jnp.concatenate([steps, entered, leaving * steps], axis=0), expand)
    ordered = row <= column if turned_over else row >= column
    blocked = jnp.where(ordered & (meta[:, 0:1] == segment_ref[0:1, :]), 0.0, NEGATIVE)
    return dict(
        summed=summed,
        conv_gate=conv_gate,
        state_summed=state_summed,
        state_gate=state_gate,
        write=write,
        read=read,
        wide_inputs=wide_inputs,
        raw=raw,
        steps=steps,
        triangle=triangle,
        total=total,
        total_rows=total.T,
        leaving=leaving,
        expand=expand,
        steps_wide=spread[:rows],
        entered_wide=spread[rows : 2 * rows],
        tail_wide=spread[2 * rows :],
        stepped=(wide_inputs * spread[:rows]).astype(BFLOAT),
        tailed=(wide_inputs * spread[2 * rows :]).astype(BFLOAT),
        blocked=blocked,
        crossing=dot(write, read, (1, 1)) if turned_over else dot(read, write, (1, 1)),
    )


def decay_of(block, head):
    difference = block["total"][:, head : head + 1] - block["total_rows"][head : head + 1, :]
    return jnp.exp(difference + block["blocked"])


def turned_decay_of(block, head):
    difference = block["total_rows"][head : head + 1, :] - block["total"][:, head : head + 1]
    return jnp.exp(difference + block["blocked"])


def scan_forward_kernel(
    gate_ref, conv_ref, before_ref, state_ref, state_before_ref, step_ref, meta_ref, segment_ref, taps_ref,
    state_taps_ref, head_ref, skip_ref, mixed_ref, out_ref, scanned_ref, states_ref, state,
):
    del mixed_ref

    @pl.when(pl.program_id(0) == 0)
    def _():
        state[...] = jnp.zeros_like(state)

    block = scan_block(
        conv_ref, before_ref, state_ref, state_before_ref, step_ref, meta_ref, segment_ref, taps_ref, state_taps_ref,
        head_ref, False,
    )
    heads = conv_ref.shape[1] // HP
    carried = state[...].astype(BFLOAT)
    states_ref[0] = carried
    across = dot(block["read"], carried, (1, 0)) * block["entered_wide"]
    within = []
    for head in range(heads):
        weights = (block["crossing"] * decay_of(block, head)).astype(BFLOAT)
        within.append(dot(weights, block["stepped"][:, head * HP : (head + 1) * HP], (1, 0)))
    scanned = across + jnp.concatenate(within, axis=1)
    scanned_ref[...] = scanned
    gated, _ = silu_parts(gate_ref[...].astype(FLOAT))
    out_ref[...] = ((scanned + skip_ref[0:1, :] * block["wide_inputs"]) * gated).astype(BFLOAT)
    state[...] = state[...] * block["entered_wide"][SSD_BLOCK - 1 : SSD_BLOCK, :] + dot(
        block["write"], block["tailed"], (0, 0)
    )


def scan_backward_kernel(
    gate_ref, conv_ref, before_ref, state_ref, state_before_ref, step_ref, meta_ref, segment_ref, taps_ref,
    state_taps_ref, head_ref, skip_ref, scanned_ref, states_ref, grad_ref, query_grad_ref, shared_grad_ref, *rest,
):
    out_ref, *running = rest[-4:]
    state_grad, later, state_later = running

    @pl.when(pl.program_id(0) == 0)
    def _():
        for at, ref in enumerate(running):
            ref[...] = rest[1 + at][...] if len(rest) > 4 else jnp.zeros_like(ref)

    block = scan_block(
        conv_ref, before_ref, state_ref, state_before_ref, step_ref, meta_ref, segment_ref, taps_ref, state_taps_ref,
        head_ref, True,
    )
    rows = SSD_BLOCK
    channels = conv_ref.shape[1]
    heads = channels // HP
    meta = meta_ref[...]
    read, write = block["read"], block["write"]
    inputs = block["wide_inputs"]
    scanned = scanned_ref[...]
    skip = skip_ref[0:1, :]
    gate_values = gate_ref[...].astype(FLOAT)
    gated, gate = silu_parts(gate_values)
    grad = grad_ref[...].astype(FLOAT)
    gate_grad = grad * (scanned + skip * inputs) * silu_slope(gate_values, gate)
    out_grad = grad * gated
    inputs_grad = skip * out_grad
    rounded = out_grad.astype(BFLOAT)
    wide_rounded = rounded.astype(FLOAT)
    carried = states_ref[0]
    after = state_grad[...]
    after_rounded = after.astype(BFLOAT)

    from_state = dot(write, after_rounded, (1, 0))
    entering = (wide_rounded * block["entered_wide"]).astype(BFLOAT)
    write_grad = dot(block["tailed"], after_rounded, (1, 1))
    read_grad = dot(entering, carried, (1, 1))
    last_entered = block["entered_wide"][rows - 1 : rows, :]
    through = jnp.sum(after * carried.astype(FLOAT), axis=0, keepdims=True) * last_entered
    state_grad[...] = after * last_entered + dot(read, entering, (0, 0))

    crossing_grad = jnp.zeros((rows, rows), FLOAT)
    pulled = []
    for head in range(heads):
        span = slice(head * HP, (head + 1) * HP)
        decay = turned_decay_of(block, head)
        weights = (block["crossing"] * decay).astype(BFLOAT)
        pulled.append(dot(weights, rounded[:, span], (1, 0)))
        crossing_grad = crossing_grad + dot(block["stepped"][:, span], rounded[:, span], (1, 1)) * decay
    pulled = jnp.concatenate(pulled, axis=1)
    crossing_rounded = crossing_grad.astype(BFLOAT)
    read_grad = read_grad + dot(crossing_rounded, write, (0, 0))
    write_grad = write_grad + dot(crossing_rounded, read, (1, 0))

    inputs_grad = inputs_grad + block["steps_wide"] * pulled + block["tail_wide"] * from_state
    sums = head_sum(
        jnp.concatenate(
            [
                wide_rounded * scanned - block["stepped"].astype(FLOAT) * pulled,
                inputs * pulled,
                inputs * from_state,
                jnp.broadcast_to(through, (8, channels)),
            ],
            axis=0,
        ),
        block["expand"],
    )
    leaving_grad = sums[2 * rows : 3 * rows] * block["leaving"]
    leaving_total = leaving_grad * block["steps"]
    last = sums[3 * rows : 3 * rows + 1] + jnp.sum(leaving_total, axis=0, keepdims=True)
    total_grad = sums[:rows] - leaving_total
    total_grad = total_grad + jnp.where(
        lax.broadcasted_iota(jnp.int32, total_grad.shape, 0) == rows - 1, last, 0.0
    )
    decay_grad = running_sum(total_grad, block["triangle"], (0, 0))
    steps_grad = sums[rows : 2 * rows] + leaving_grad + decay_grad * head_ref[1:2, :]
    raw_grad = steps_grad / (1.0 + jnp.exp(-block["raw"]))
    raw_grad = jnp.where(lax.broadcasted_iota(jnp.int32, raw_grad.shape, 1) < heads, raw_grad, 0.0)

    state_slope = silu_slope(block["state_summed"], block["state_gate"])
    state_pre = conv_back(
        jnp.concatenate([write_grad, read_grad], axis=1) * state_slope, state_later, state_taps_ref, meta
    )
    conv_pre = conv_back(inputs_grad * silu_slope(block["summed"], block["conv_gate"]), later, taps_ref, meta)
    out_ref[:, : 2 * NSTATE] = state_pre.astype(BFLOAT)
    start = 2 * NSTATE + 2 * HEAD_SIZE
    end = out_ref.shape[1] - LANES
    out_ref[:, 2 * NSTATE : start] = shared_grad_ref[...]
    out_ref[:, start + 2 * channels : end] = query_grad_ref[...]
    out_ref[:, start : start + channels] = gate_grad.astype(BFLOAT)
    out_ref[:, start + channels : start + 2 * channels] = conv_pre.astype(BFLOAT)
    out_ref[:, end:] = raw_grad.astype(BFLOAT)


STATES = 2 * NSTATE
PAIR = 2 * HEAD_SIZE


def scan_specs(channels, order):
    half = SSD_BLOCK // 16
    before = lambda i: jnp.maximum(order(i) * half - 1, 0)
    gate_at = (STATES + PAIR) // channels
    step_at = (STATES + PAIR + 2 * channels + channels * QUERY_HEADS // DSSM * HEAD_SIZE) // LANES
    return [
        pl.BlockSpec((SSD_BLOCK, channels), lambda i: (order(i), gate_at)),
        pl.BlockSpec((SSD_BLOCK, channels), lambda i: (order(i), gate_at + 1)),
        pl.BlockSpec((16, channels), lambda i: (before(i), gate_at + 1)),
        pl.BlockSpec((SSD_BLOCK, STATES), lambda i: (order(i), 0)),
        pl.BlockSpec((16, STATES), lambda i: (before(i), 0)),
        pl.BlockSpec((SSD_BLOCK, LANES), lambda i: (order(i), step_at)),
        pl.BlockSpec((SSD_BLOCK, LANES), lambda i: (order(i), 0)),
        pl.BlockSpec((8, SSD_BLOCK), lambda i: (0, order(i))),
        whole((8, channels)),
        whole((8, STATES)),
        whole((8, LANES)),
        whole((8, channels)),
    ]


def scan_operands(projected, tables):
    return [projected] * 6 + [
        tables[name] for name in ("meta", "segment_row", "taps", "state_taps", "head", "skip")
    ]


def scan_cost(tokens, channels, factor):
    heads = channels // HP
    return estimate(
        flops=factor * 2 * tokens * SSD_BLOCK * (3 * channels + NSTATE),
        bytes_accessed=factor * tokens * channels * 12,
        transcendentals=tokens * SSD_BLOCK * heads,
    )


def scan_forward(projected, tables, mixed):
    tokens = projected.shape[0]
    channels = tables["taps"].shape[1]
    blocks = tokens // SSD_BLOCK
    return pl.pallas_call(
        scan_forward_kernel,
        grid=(blocks,),
        in_specs=scan_specs(channels, lambda i: i) + [pl.BlockSpec(memory_space=pl.ANY)],
        out_specs=[
            pl.BlockSpec((SSD_BLOCK, channels), lambda i: (i, 0)),
            pl.BlockSpec((SSD_BLOCK, channels), lambda i: (i, 0)),
            pl.BlockSpec((1, NSTATE, channels), lambda i: (i, 0, 0)),
        ],
        out_shape=[
            jax.ShapeDtypeStruct(mixed.shape, BFLOAT),
            jax.ShapeDtypeStruct((tokens, channels), FLOAT),
            jax.ShapeDtypeStruct((blocks, NSTATE, channels), BFLOAT),
        ],
        scratch_shapes=[pltpu.VMEM((NSTATE, channels), FLOAT)],
        input_output_aliases={12: 0},
        compiler_params=pltpu.CompilerParams(vmem_limit_bytes=SCAN_BYTES),
        cost_estimate=scan_cost(tokens, channels, 1),
        name="scan_forward",
    )(*scan_operands(projected, tables), mixed)


def scan_backward(projected, tables, scanned, carried, mixed_grad, attended_grads, part, parts, before):
    tokens, width = projected.shape
    channels = tables["taps"].shape[1]
    blocks = tokens // SSD_BLOCK
    last = blocks - 1 - part * (blocks // parts)
    back = lambda i: (last - i, 0)
    running = [(NSTATE, channels), (8, channels), (8, STATES)]
    query_grad, shared_grad = attended_grads
    operands = [*scan_operands(projected, tables), scanned, carried, mixed_grad, query_grad, shared_grad]
    in_specs = scan_specs(channels, lambda i: last - i) + [
        pl.BlockSpec((SSD_BLOCK, channels), back),
        pl.BlockSpec((1, NSTATE, channels), lambda i: (last - i, 0, 0)),
        pl.BlockSpec((SSD_BLOCK, channels), back),
        pl.BlockSpec((SSD_BLOCK, query_grad.shape[1]), back),
        pl.BlockSpec((SSD_BLOCK, PAIR), back),
    ]
    aliases = {}
    if before is not None:
        aliases = {len(operands): 0}
        operands += list(before)
        in_specs += [pl.BlockSpec(memory_space=pl.ANY), *[whole(shape) for shape in running]]
    return pl.pallas_call(
        scan_backward_kernel,
        grid=(blocks // parts,),
        in_specs=in_specs,
        out_specs=[pl.BlockSpec((SSD_BLOCK, width), back), *[whole(shape) for shape in running]],
        out_shape=[
            jax.ShapeDtypeStruct((tokens, width), BFLOAT),
            *[jax.ShapeDtypeStruct(shape, FLOAT) for shape in running],
        ],
        input_output_aliases=aliases,
        compiler_params=pltpu.CompilerParams(vmem_limit_bytes=SCAN_BYTES),
        cost_estimate=scan_cost(tokens, channels, 2),
        name="scan_backward",
    )(*operands)


def turned(values, cosine, sine):
    return (values * cosine + pltpu.roll(values, HEAD_SIZE // 2, 1) * sine).astype(BFLOAT)


def turned_back(values, cosine, sine):
    return values * cosine + pltpu.roll(values * sine, HEAD_SIZE // 2, 1)


ATT_ROWS = 256


def attention_mask(meta_ref, segment_ref, start, extent):
    row = start + lax.broadcasted_iota(jnp.int32, (ATT_ROWS, extent), 0)
    column = lax.broadcasted_iota(jnp.int32, (ATT_ROWS, extent), 1)
    return (row >= column) & (meta_ref[start : start + ATT_ROWS, 0:1] == segment_ref[0:1, :extent])


def probabilities(query, keys, allowed):
    score = dot(query, keys, (1, 1)) * (1.0 / math.sqrt(HEAD_SIZE))
    score = jnp.where(allowed, score, NEGATIVE)
    exponent = jnp.exp(score - jnp.max(score, axis=1, keepdims=True))
    return exponent / jnp.sum(exponent, axis=1, keepdims=True)


def attention_forward_kernel(query_ref, key_ref, value_ref, cosine_ref, sine_ref, meta_ref, segment_ref, out_ref, keys):
    tokens = key_ref.shape[0]
    keys[...] = turned(key_ref[...].astype(FLOAT), cosine_ref[...], sine_ref[...])
    for start in range(0, tokens, ATT_ROWS):
        extent = start + ATT_ROWS
        here = slice(start, extent)
        allowed = attention_mask(meta_ref, segment_ref, start, extent)
        for unit in range(query_ref.shape[1] // HEAD_SIZE):
            span = slice(unit * HEAD_SIZE, (unit + 1) * HEAD_SIZE)
            query = turned(query_ref[here, span].astype(FLOAT), cosine_ref[here], sine_ref[here])
            weights = probabilities(query, keys[:extent], allowed).astype(BFLOAT)
            out_ref[here, span] = dot(weights, value_ref[:extent], (1, 0)).astype(BFLOAT)


def attention_backward_kernel(
    query_ref, key_ref, value_ref, cosine_ref, sine_ref, meta_ref, segment_ref, grad_ref,
    query_grad_ref, shared_grad_ref, keys, key_sum, value_sum,
):
    tokens = key_ref.shape[0]
    scale = 1.0 / math.sqrt(HEAD_SIZE)
    keys[...] = turned(key_ref[...].astype(FLOAT), cosine_ref[...], sine_ref[...])
    key_sum[...] = jnp.zeros_like(key_sum)
    value_sum[...] = jnp.zeros_like(value_sum)
    for start in range(0, tokens, ATT_ROWS):
        extent = start + ATT_ROWS
        here = slice(start, extent)
        allowed = attention_mask(meta_ref, segment_ref, start, extent)
        for unit in range(query_ref.shape[1] // HEAD_SIZE):
            span = slice(unit * HEAD_SIZE, (unit + 1) * HEAD_SIZE)
            query = turned(query_ref[here, span].astype(FLOAT), cosine_ref[here], sine_ref[here])
            weights = probabilities(query, keys[:extent], allowed)
            grad = grad_ref[here, span]
            weights_grad = dot(grad, value_ref[:extent], (1, 1))
            value_sum[:extent] += dot(weights.astype(BFLOAT), grad, (0, 0))
            mean_grad = jnp.sum(weights * weights_grad, axis=1, keepdims=True)
            score_grad = (weights * (weights_grad - mean_grad) * scale).astype(BFLOAT)
            query_grad = dot(score_grad, keys[:extent], (1, 0))
            key_sum[:extent] += dot(score_grad, query, (0, 0))
            query_grad_ref[here, span] = turned_back(query_grad, cosine_ref[here], sine_ref[here]).astype(BFLOAT)
    shared_grad_ref[:, :HEAD_SIZE] = turned_back(key_sum[...], cosine_ref[...], sine_ref[...]).astype(BFLOAT)
    shared_grad_ref[:, HEAD_SIZE:] = value_sum[...].astype(BFLOAT)


def attention_cost(tokens, width, factor):
    return estimate(
        flops=factor * 2 * tokens * tokens * width,
        bytes_accessed=factor * tokens * width * 8,
        transcendentals=tokens * tokens * width // (2 * HEAD_SIZE),
    )


def attention_specs(tokens, channels):
    width = channels * QUERY_HEADS // DSSM * HEAD_SIZE
    narrow = whole((tokens, HEAD_SIZE))
    return [
        pl.BlockSpec((tokens, width), lambda *_: (0, (STATES + PAIR + 2 * channels) // width)),
        pl.BlockSpec((tokens, HEAD_SIZE), lambda *_: (0, STATES // HEAD_SIZE)),
        pl.BlockSpec((tokens, HEAD_SIZE), lambda *_: (0, STATES // HEAD_SIZE + 1)),
        narrow,
        narrow,
        whole((tokens, LANES)),
        whole((8, tokens)),
    ]


def attention_operands(projected, tables):
    return [projected] * 3 + [tables[name] for name in ("cosine", "sine", "meta", "segment_row")]


def attention_forward(projected, tables):
    tokens = projected.shape[0]
    channels = tables["taps"].shape[1]
    width = channels * QUERY_HEADS // DSSM * HEAD_SIZE
    return pl.pallas_call(
        attention_forward_kernel,
        grid=(1,),
        in_specs=attention_specs(tokens, channels),
        out_specs=pl.BlockSpec((tokens, width), lambda *_: (0, channels // width)),
        out_shape=jax.ShapeDtypeStruct((tokens, channels + width), BFLOAT),
        scratch_shapes=[pltpu.VMEM((tokens, HEAD_SIZE), BFLOAT)],
        compiler_params=pltpu.CompilerParams(vmem_limit_bytes=SCAN_BYTES),
        cost_estimate=attention_cost(tokens, width, 1),
        name="attention_forward",
    )(*attention_operands(projected, tables))


def attention_backward(projected, tables, mixed_grad):
    tokens = projected.shape[0]
    channels = tables["taps"].shape[1]
    width = channels * QUERY_HEADS // DSSM * HEAD_SIZE
    return pl.pallas_call(
        attention_backward_kernel,
        grid=(1,),
        in_specs=attention_specs(tokens, channels)
        + [pl.BlockSpec((tokens, width), lambda *_: (0, channels // width))],
        out_specs=[whole((tokens, width)), whole((tokens, PAIR))],
        out_shape=[jax.ShapeDtypeStruct((tokens, width), BFLOAT), jax.ShapeDtypeStruct((tokens, PAIR), BFLOAT)],
        scratch_shapes=[
            pltpu.VMEM((tokens, HEAD_SIZE), BFLOAT),
            pltpu.VMEM((tokens, HEAD_SIZE), FLOAT),
            pltpu.VMEM((tokens, HEAD_SIZE), FLOAT),
        ],
        compiler_params=pltpu.CompilerParams(vmem_limit_bytes=SCAN_BYTES),
        cost_estimate=attention_cost(tokens, width, 3),
        name="attention_backward",
    )(*attention_operands(projected, tables), mixed_grad)


def mixer_tables(lengths, segment, position, conv_values, conv_states, scan_params):
    tokens = segment.shape[0]
    block = jnp.arange(tokens, dtype=jnp.int32) // SSD_BLOCK
    previous = jnp.concatenate([jnp.full((1,), -1, jnp.int32), segment[:-1]])
    first_previous = jnp.repeat(previous[::SSD_BLOCK], SSD_BLOCK)
    last_segment = jnp.repeat(segment[SSD_BLOCK - 1 :: SSD_BLOCK], SSD_BLOCK)
    length = jnp.sum(
        jnp.where(segment[:, None] == jnp.arange(lengths.shape[0], dtype=jnp.int32)[None, :], lengths[None, :], 0),
        axis=1,
    )
    columns = [
        segment,
        position,
        length - 1 - position,
        segment == first_previous,
        segment == last_segment,
    ]
    meta = jnp.stack([column.astype(FLOAT) for column in columns], axis=1)
    half_width = HEAD_SIZE // 2
    frequency = ROPE_BASE ** (-2.0 * jnp.arange(half_width, dtype=FLOAT) / HEAD_SIZE)
    angle = position.astype(FLOAT)[:, None] * frequency[None, :]
    cosine, sine = jnp.cos(angle), jnp.sin(angle)
    heads = scan_params.shape[1]
    head = jnp.stack([scan_params[0], -jnp.exp(scan_params[1]), scan_params[2]])
    return dict(
        meta=jnp.pad(meta, ((0, 0), (0, LANES - meta.shape[1]))),
        segment_row=jnp.broadcast_to(segment.astype(FLOAT)[None, :], (8, tokens)),
        taps=jnp.pad(conv_values.astype(FLOAT), ((0, 3), (0, 0))),
        state_taps=jnp.pad(conv_states.astype(FLOAT), ((0, 3), (0, 0))),
        head=jnp.pad(head, ((0, 5), (0, LANES - heads))),
        skip=jnp.broadcast_to(jnp.repeat(scan_params[2], HP)[None, :], (8, heads * HP)),
        cosine=jnp.concatenate([cosine, cosine], axis=1),
        sine=jnp.concatenate([-sine, sine], axis=1),
    )


HALVES = 2
DENSE_TILE = 1024


def matrix_rows(values):
    return values.reshape(values.shape[0] * values.shape[1], values.shape[2])


def cut_tiles(width, tile):
    return [(low, min(low + tile, width)) for low in range(0, width, tile)]


def spread_kernel(masks, count, chosen_ref, *rest):
    halves, weights = rest[: 2 * len(masks)], rest[2 * len(masks) : 2 * len(masks) + count]
    out_ref, narrow_ref, out_tile, narrow, sems = rest[-5:]
    rows = halves[0].shape[0]
    shards = weights[0].shape[0]
    depth = shards // HALVES
    lower = weights[-1].shape[2] - LANES
    copies = []
    for at, mask in enumerate(masks):
        left_ref, right_ref = halves[2 * at : 2 * at + 2]
        here = pl.ds(pl.multiple_of((lax.axis_index("col") ^ mask) * rows, rows), rows)

        def through(ref, low, high):
            return dot(left_ref[...], matrix_rows(ref[:depth, :rows, low:high]), (1, 0)) + dot(
                right_ref[...], matrix_rows(ref[depth:, :rows, low:high]), (1, 0)
            )

        def send(tile, target):
            copies.append(pltpu.make_async_copy(tile, target, sems.at[len(copies)]))
            copies[-1].start()

        narrow[at] = (chosen_ref[here, :] * through(weights[-1], lower, lower + LANES)).astype(BFLOAT)
        send(narrow.at[at], narrow_ref.at[here, :])
        column = 0
        for ref in weights:
            for low, high in cut_tiles(ref.shape[2] - (LANES if ref is weights[-1] else 0), DENSE_TILE):
                span = slice(column, column + high - low)
                column += high - low
                raised = matrix_rows(ref[:, rows : rows + NADAPT * RANK // shards, low:high])
                out_tile[at, :, span] = (through(ref, low, high) + dot(narrow[at], raised, (1, 0))).astype(BFLOAT)
                send(out_tile.at[at, :, span], out_ref.at[here, span])
    for copy in copies:
        copy.wait()


def weights_width(gathered):
    return sum(part.shape[2] for part in gathered) - LANES


def spread_blocks(blocks, gathered, selector, held):
    masks = [mask for mask, _ in blocks]
    rows, half = blocks[0][1][0].shape
    width = weights_width(gathered)
    total = selector.shape[0]
    fast, free = pl.BlockSpec(memory_space=pltpu.VMEM), pl.BlockSpec(memory_space=pl.ANY)
    operands = [selector, *[part for _, halves in blocks for part in halves], *gathered]
    in_specs = [fast] * len(operands)
    aliases = {}
    if held is not None:
        aliases = {len(operands): 0, len(operands) + 1: 1}
        operands += list(held)
        in_specs += [free] * 2
    copies = len(masks) * (1 + sum(-(-part.shape[2] // DENSE_TILE) for part in gathered))
    return pl.pallas_call(
        functools.partial(spread_kernel, masks, len(gathered)),
        in_specs=in_specs,
        out_specs=[free] * 2,
        out_shape=[
            jax.ShapeDtypeStruct((total, width), BFLOAT),
            jax.ShapeDtypeStruct((total, LANES), BFLOAT),
        ],
        scratch_shapes=[
            pltpu.VMEM((len(masks), rows, width), BFLOAT),
            pltpu.VMEM((len(masks), rows, LANES), BFLOAT),
            pltpu.SemaphoreType.DMA((copies,)),
        ],
        input_output_aliases=aliases,
        compiler_params=pltpu.CompilerParams(vmem_limit_bytes=DENSE_BYTES),
        cost_estimate=estimate(
            flops=4 * len(masks) * rows * half * (width + LANES),
            bytes_accessed=2 * len(masks) * rows * (2 * half + width),
            transcendentals=0,
        ),
        name="spread_blocks",
    )(*operands)


def collect_kernel(masks, count, values_ref, *refs):
    weights, outs = refs[:count], refs[count:]
    if len(outs) > 2 * len(masks):
        inner_ref, *outs, raise_ref = outs
        raise_ref[...] = dot(inner_ref[...], values_ref[...], (0, 0)).astype(BFLOAT)
    rows = values_ref.shape[0] // 4
    shards = weights[0].shape[0]
    half = shards // HALVES * rows
    width = values_ref.shape[1]
    starts, column = [], 0
    for ref in weights:
        high = min(column + ref.shape[2], width)
        starts.append((column, high))
        column = high
    for at, mask in enumerate(masks):
        here = pl.ds(pl.multiple_of((lax.axis_index("col") ^ mask) * rows, rows), rows)
        first, second = outs[2 * at], outs[2 * at + 1]

        def through(cut):
            total = None
            for (low, high), ref in zip(starts, weights):
                part = dot(values_ref[here, low:high], cut(ref, high - low), (1, 1))
                total = part if total is None else total + part
            return total

        for shard in range(shards):
            out_ref = first if shard < shards // HALVES else second
            column = shard * rows % half
            out_ref[:, column : column + rows] = through(lambda ref, wide: ref[shard, :rows, :wide]).astype(
                out_ref.dtype
            )
        first[:, half:] = through(
            lambda ref, wide: matrix_rows(ref[:, rows : rows + NADAPT * RANK // shards, :wide])
        ).astype(first.dtype)


def collect_blocks(masks, values, gathered, types, inner=()):
    rows = values.shape[0] // 4
    half = gathered[0].shape[0] // HALVES * rows
    fast = pl.BlockSpec(memory_space=pltpu.VMEM)
    out_shape = []
    for pair in types:
        out_shape.append(jax.ShapeDtypeStruct((rows, half + LANES), pair[0]))
        out_shape.append(jax.ShapeDtypeStruct((rows, half), pair[1]))
    out_shape += [jax.ShapeDtypeStruct((LANES, values.shape[1]), BFLOAT) for _ in inner]
    outs = pl.pallas_call(
        functools.partial(collect_kernel, masks, len(gathered)),
        in_specs=[fast] * (1 + len(gathered) + len(inner)),
        out_specs=[fast] * len(out_shape),
        out_shape=out_shape,
        compiler_params=pltpu.CompilerParams(vmem_limit_bytes=DENSE_BYTES),
        cost_estimate=estimate(
            flops=4 * len(masks) * rows * half * values.shape[1],
            bytes_accessed=2 * len(masks) * rows * (values.shape[1] + 4 * half),
            transcendentals=0,
        ),
        name="collect_blocks",
    )(values, *gathered, *inner)
    return [tuple(outs[2 * at : 2 * at + 2]) for at in range(len(masks))] + list(outs[2 * len(masks) :])


def root_mean(values):
    return lax.rsqrt(jnp.mean(values * values, axis=1, keepdims=True) + EPSILON)


def packed_grad(narrow, values, choose):
    half = LANES // 2
    chosen = dot(narrow, choose, (1, 0)).astype(BFLOAT)
    grad = dot(chosen, values, (0, 0))
    low = lax.broadcasted_iota(jnp.int32, (8, LANES), 1) < half
    devices = []
    for start in range(0, grad.shape[1], LANES):
        own = grad[:, start : start + LANES]
        turned_own = pltpu.roll(own, half, 1)
        for first, second in ((own, turned_own), (turned_own, own)):
            devices.append(
                jnp.concatenate(
                    [jnp.where(low, first[at : at + 8], second[at + 8 : at + 16]) for at in (0, 16)], axis=1
                )
            )
    return jnp.concatenate(devices, axis=0).astype(BFLOAT)


def finish_kernel(kind, first_own, first_near, first_far, second_own, second_near, second_far, lower_ref, chosen_ref,
                  *refs):
    half = second_own.shape[1]
    model = HALVES * half
    wide = lambda ref: ref[...].astype(FLOAT)
    first = wide(first_own) + wide(first_near) + wide(first_far)
    second = wide(second_own) + wide(second_near) + wide(second_far)
    inner = (chosen_ref[...] * first[:, half:]).astype(BFLOAT)
    summed = jnp.concatenate([first[:, :half], second], axis=1) + dot(
        inner, matrix_rows(lower_ref[...]), (1, 1)
    )
    if kind == "output":
        residual_ref, place_ref, choose_ref, branch_ref, early_ref, out_ref = refs
        result = (residual_ref[...] + summed).astype(BFLOAT)
        out_ref[:, :model] = dot(place_ref[...], result, (0, 0)).astype(BFLOAT)
        out_ref[:, model : model + 2 * LANES] = packed_grad(inner, branch_ref[...], choose_ref[...])
        out_ref[:, model + 2 * LANES :] = early_ref[...]
        return
    if kind == "forward":
        residual_ref, gain_ref, out_ref, inner_ref, left_ref, right_ref = refs
        hidden = residual_ref[...] + summed
        normed = (hidden * root_mean(hidden) * gain_ref[0:1, :]).astype(BFLOAT)
    else:
        values_ref, upstream_ref, gain_ref, choose_ref, normed_left, normed_right = refs[:6]
        values = values_ref[...]
        scale = root_mean(values)
        weighted = summed * gain_ref[0:1, :]
        mean = jnp.mean(weighted * values, axis=1, keepdims=True)
        hidden = upstream_ref[...].astype(FLOAT) + scale * weighted - values * (scale * scale * scale * mean)
        normed = hidden.astype(BFLOAT)
        packed = packed_grad(
            inner, jnp.concatenate([normed_left[...], normed_right[...]], axis=1), choose_ref[...]
        )
        if kind == "input":
            place_ref, out_ref = refs[6:]
            out_ref[:, :model] = dot(place_ref[...], normed, (0, 0)).astype(BFLOAT)
            out_ref[:, model:] = packed
            return
        given_ref, out_ref, inner_ref, left_ref, right_ref, packed_ref = refs[6:]
        packed_ref[:, : 2 * LANES] = packed
        packed_ref[:, 2 * LANES :] = packed_grad(given_ref[...], normed, choose_ref[...])
    out_ref[...] = hidden
    inner_ref[...] = inner
    left_ref[...] = normed[:, :half]
    right_ref[...] = normed[:, half:]


def finish(kind, parts, gathered, own_selector, *operands):
    rows = own_selector.shape[0]
    half = parts[3].shape[1]
    shards = gathered[-1].shape[0]
    model = HALVES * half
    lower = gathered[-1][:, : model // shards, -LANES:]
    shaped = jax.ShapeDtypeStruct
    if kind in ("output", "input"):
        out_shape = shaped((rows, model + 2 * LANES * (3 if kind == "output" else 1)), BFLOAT)
        out_specs = whole(out_shape.shape)
    else:
        out_shape = [shaped((rows, model), FLOAT), shaped((rows, LANES), BFLOAT)]
        out_shape += [shaped((rows, half), BFLOAT)] * 2
        out_shape += [shaped((rows, 4 * LANES), BFLOAT)] * (kind == "backward")
        out_specs = [whole(shape.shape) for shape in out_shape]
    given = [*parts, lower, own_selector, *operands]
    return pl.pallas_call(
        functools.partial(finish_kernel, kind),
        grid=(1,),
        in_specs=[whole(value.shape) for value in given],
        out_specs=out_specs,
        out_shape=out_shape,
        compiler_params=pltpu.CompilerParams(vmem_limit_bytes=FINISH_BYTES),
        cost_estimate=estimate(
            flops=2 * rows * model * LANES, bytes_accessed=rows * model * 20, transcendentals=0
        ),
        name="finish_" + kind,
    )(*given)


def onward_kernel(first_kept, first_part, second_kept, second_part, first_ref, second_ref):
    first_ref[...] = (first_kept[...] + first_part[...].astype(FLOAT)).astype(BFLOAT)
    second_ref[...] = (second_kept[...] + second_part[...].astype(FLOAT)).astype(BFLOAT)


def sum_onward(first_kept, first_part, second_kept, second_part):
    return pl.pallas_call(
        onward_kernel,
        in_specs=[pl.BlockSpec(memory_space=pltpu.VMEM)] * 4,
        out_specs=[pl.BlockSpec(memory_space=pltpu.VMEM)] * 2,
        out_shape=[jax.ShapeDtypeStruct(part.shape, BFLOAT) for part in (first_part, second_part)],
        compiler_params=pltpu.CompilerParams(vmem_limit_bytes=DENSE_BYTES),
        name="sum_onward",
    )(first_kept, first_part, second_kept, second_part)


def send_kernel(target_column, target_row, tokens_ref, adapter_ref, sent_ref, matrix_ref):
    rows = tokens_ref.shape[0]
    model = tokens_ref.shape[1]
    peer = adapter_ref.shape[0]
    column, row = target_column[:, 0:1], target_row[0:1, :]
    earlier = lax.broadcasted_iota(jnp.int32, (rows, rows), 0) < lax.broadcasted_iota(jnp.int32, (rows, rows), 1)
    same = jnp.where((column // rows == row // rows) & earlier, 1.0, 0.0)
    place = (row // rows) * peer + jnp.sum(same, axis=0, keepdims=True).astype(jnp.int32)
    matrix = (lax.broadcasted_iota(jnp.int32, (rows, rows), 0) == place).astype(BFLOAT)
    matrix_ref[...] = matrix
    sent_ref[:, :model] = dot(matrix, tokens_ref[...], (1, 0)).astype(BFLOAT)
    lane = lax.broadcasted_iota(jnp.int32, (rows, LANES), 1)
    slots = jnp.where(lane == 0, column % rows, 0).astype(FLOAT).astype(BFLOAT)
    notes = dot(matrix, slots, (1, 0))
    sent_ref[:, model:] = jnp.where(lane == 0, notes, adapter_ref[0:1, :]).astype(BFLOAT)


def send_tokens(target, tokens, adapters, peer):
    rows, model = tokens.shape
    notes = jnp.pad(adapters.astype(FLOAT), (1, LANES - 1 - adapters.shape[0]))
    return pl.pallas_call(
        send_kernel,
        in_specs=[pl.BlockSpec(memory_space=pltpu.VMEM)] * 4,
        out_specs=[pl.BlockSpec(memory_space=pltpu.VMEM)] * 2,
        out_shape=[
            jax.ShapeDtypeStruct((rows, model + LANES), BFLOAT),
            jax.ShapeDtypeStruct((rows, rows), BFLOAT),
        ],
        compiler_params=pltpu.CompilerParams(vmem_limit_bytes=DENSE_BYTES),
        name="send_tokens",
    )(
        jnp.broadcast_to(target[:, None], (rows, LANES)),
        jnp.broadcast_to(target[None, :], (8, rows)),
        tokens,
        jnp.broadcast_to(notes[None, :], (peer, LANES)),
    )


def shards_kernel(given_ref, lower_ref, taps_ref, own_ref, shared_ref):
    half = LANES // 2
    given = given_ref[...].astype(FLOAT)
    tall, width = given.shape
    second = pltpu.roll(given, width - UNIT_IN, 1)
    gate = DSSM // QUERY_HEADS
    pair_at = 2 * gate + HEAD_SIZE
    start = 0
    for low, high in ((0, gate), (gate, 2 * gate), (2 * gate, pair_at)):
        for unit in (given, second):
            own_ref[:, start : start + high - low] = unit[:, low:high].astype(BFLOAT)
            start += high - low
    lane = lax.broadcasted_iota(jnp.int32, (tall, LANES), 1)
    heads = NH // QUERY_HEADS
    steps_at = pair_at + LANES
    other = pltpu.roll(second[:, steps_at : steps_at + LANES], heads, 1)
    steps = jnp.where(lane < heads, given[:, steps_at : steps_at + LANES], jnp.where(lane < 2 * heads, other, 0.0))
    own_ref[:, start : start + LANES] = steps.astype(BFLOAT)
    rows = lower_ref.shape[0]
    own_ref[:rows, start + LANES :] = lower_ref[...]
    own_ref[rows:, start + LANES :] = jnp.zeros((tall - rows, LANES), BFLOAT)
    first_tile, second_tile = given[:, pair_at:steps_at], second[:, pair_at:steps_at]
    shared_ref[:tall, :LANES] = jnp.where(lane < half, first_tile, pltpu.roll(second_tile, half, 1)).astype(BFLOAT)
    shared_ref[:tall, LANES:] = jnp.where(lane < half, pltpu.roll(first_tile, half, 1), second_tile).astype(BFLOAT)
    shared_ref[tall:, :LANES] = jnp.zeros(taps_ref.shape, BFLOAT)
    shared_ref[tall:, LANES:] = taps_ref[...]


def make_shards(given, lower, taps):
    tall = given.shape[0]
    own = 2 * (2 * DSSM // QUERY_HEADS + HEAD_SIZE) + 2 * LANES
    return pl.pallas_call(
        shards_kernel,
        in_specs=[pl.BlockSpec(memory_space=pltpu.VMEM)] * 3,
        out_specs=[pl.BlockSpec(memory_space=pltpu.VMEM)] * 2,
        out_shape=[
            jax.ShapeDtypeStruct((tall, own), BFLOAT),
            jax.ShapeDtypeStruct((tall + taps.shape[0], 2 * LANES), BFLOAT),
        ],
        compiler_params=pltpu.CompilerParams(vmem_limit_bytes=DENSE_BYTES),
        name="make_shards",
    )(given, lower, taps)


def arrive_kernel(arrived_ref, gain_ref, own_ref, matrix_ref, left_ref, right_ref):
    rows, model = own_ref.shape
    slots = arrived_ref[:, model:].astype(FLOAT).T[0:1, :]
    row = lax.broadcasted_iota(jnp.int32, (rows, rows), 0).astype(FLOAT)
    matrix = (row == slots).astype(BFLOAT)
    matrix_ref[...] = matrix
    own = dot(matrix, arrived_ref[:, :model], (1, 0))
    own_ref[...] = own
    normed = (own * root_mean(own) * gain_ref[0:1, :]).astype(BFLOAT)
    left_ref[...] = normed[:, : model // HALVES]
    right_ref[...] = normed[:, model // HALVES :]


def arrive_tokens(arrived, gain):
    rows, model = arrived.shape[0], arrived.shape[1] - LANES
    return pl.pallas_call(
        arrive_kernel,
        in_specs=[pl.BlockSpec(memory_space=pltpu.VMEM)] * 2,
        out_specs=[pl.BlockSpec(memory_space=pltpu.VMEM)] * 4,
        out_shape=[
            jax.ShapeDtypeStruct((rows, model), FLOAT),
            jax.ShapeDtypeStruct((rows, rows), BFLOAT),
            jax.ShapeDtypeStruct((rows, model // HALVES), BFLOAT),
            jax.ShapeDtypeStruct((rows, model // HALVES), BFLOAT),
        ],
        compiler_params=pltpu.CompilerParams(vmem_limit_bytes=DENSE_BYTES),
        name="arrive_tokens",
    )(arrived, gain)


GATE_WIDTH = DSSM // QUERY_HEADS
PAIR_WIDTH = 2 * KEY_VALUE_HEADS * HEAD_SIZE // QUERY_HEADS
STATE_WIDTH = 2 * NSTATE // QUERY_HEADS
STEP_WIDTH = NH // QUERY_HEADS
ALL_AXES = ("row", "col")


def pad_columns(values, width):
    return jnp.pad(values, ((0, 0), (0, width - values.shape[1])))


def after(values, *earlier):
    return lax.optimization_barrier((values, *earlier))[0]


def after_all(values, *earlier):
    return lax.optimization_barrier((*values, *earlier))[: len(values)]


def unit_parts(values, units):
    cuts = [0]
    for width in (GATE_WIDTH, GATE_WIDTH, HEAD_SIZE, PAIR_WIDTH, STATE_WIDTH, STEP_WIDTH):
        cuts.append(cuts[-1] + width)
    return [
        jnp.concatenate(
            [values[:, unit * UNIT_IN + low : unit * UNIT_IN + high] for unit in range(units)], axis=1
        )
        for low, high in zip(cuts[:-1], cuts[1:])
    ]


def restore_units(parts, units):
    ordered = []
    for unit in range(units):
        for part in parts:
            width = part.shape[1] // units
            ordered.append(part[:, unit * width : (unit + 1) * width])
    return jnp.concatenate(ordered, axis=1)


def split_halves(values, units, first, axis):
    block = values.shape[axis] // units
    take = lambda low, high: lax.slice_in_dim(values, low, high, axis=axis)
    parts = [take(unit * block, unit * block + first) for unit in range(units)]
    parts += [take(unit * block + first, (unit + 1) * block) for unit in range(units)]
    return jnp.concatenate(parts, axis=axis)


def join_halves(values, units, first, axis):
    block = values.shape[axis] // units
    rest = block - first
    take = lambda low, high: lax.slice_in_dim(values, low, high, axis=axis)
    parts = []
    for unit in range(units):
        parts.append(take(unit * first, (unit + 1) * first))
        parts.append(take(units * first + unit * rest, units * first + (unit + 1) * rest))
    return jnp.concatenate(parts, axis=axis)


def quick(rows):
    return lax.axis_size("col") == 4 and lax.axis_size("row") == 8 and rows == 256


def spread_early(halves, gathered, selector):
    left, right = halves
    far_left, near_right = flip(left, 2), flip(right, 1)
    near_left, far_right = flip(left, 1), flip(right, 2)
    held = spread_blocks([(0, halves)], gathered, selector, None)
    onward_left, onward_right = after_all((far_left, near_right), held[1])
    corner = flip(onward_left, 1), flip(onward_right, 2)
    held = spread_blocks([(1, (near_left, near_right))], gathered, selector, held)
    held = spread_blocks([(2, (far_left, far_right))], gathered, selector, held)
    return spread_blocks([(3, corner)], gathered, selector, held)


def flip(values, mask):
    return lax.ppermute(values, "col", [(i, i ^ mask) for i in range(4)])


def gather_blocks(halves):
    left, right = halves
    far_left, near_right = flip(left, 2), flip(right, 1)
    near_left, far_right = flip(left, 1), flip(right, 2)
    corner_left, corner_right = flip(far_left, 1), flip(near_right, 2)
    return [
        (0, (left, right)),
        (1, (near_left, near_right)),
        (2, (far_left, far_right)),
        (3, (corner_left, corner_right)),
    ]


def rows_of(values, block, rows):
    return lax.dynamic_slice_in_dim(values, block * rows, rows, 0)


def spread_gathered(blocks, gathered, selector):
    held = None
    for block in blocks:
        held = spread_blocks([block], gathered, selector, held)
    return held


def spread_project(halves, gathered, selector):
    rows = halves[0].shape[0]
    if quick(rows):
        return spread_gathered(gather_blocks(halves), gathered, selector)
    wide, narrow_factor = gathered
    width = narrow_factor.shape[1]
    both = product(lax.all_gather(jnp.concatenate(halves, axis=1), "col", axis=0, tiled=True), wide)
    narrow = (selector * both[:, width:]).astype(BFLOAT)
    return (both[:, :width] + product(narrow, narrow_factor)).astype(BFLOAT), narrow


PIECE_TYPES = [(BFLOAT, BFLOAT), (BFLOAT, FLOAT), (FLOAT, BFLOAT), (FLOAT, FLOAT)]


def collect_pieces(values, gathered, at_once):
    if at_once:
        return collect_blocks([3, 1, 2, 0], values, gathered, PIECE_TYPES)
    (corner,) = collect_blocks([3], values, gathered, PIECE_TYPES[:1])
    values = after(values, corner[0])
    return [corner, *collect_blocks([1, 2, 0], values, gathered, PIECE_TYPES[1:])]


def collect_send(pieces, ordered=True):
    corner, near, far, own = pieces
    arriving = flip(corner[0], 1), flip(corner[1], 2)
    sent_near, sent_far = after_all((near[0], far[1]), *arriving) if ordered else (near[0], far[1])
    return own, flip(sent_near, 1), flip(sent_far, 2), far[0], near[1], arriving


def collect_middle(started):
    own, near_first, far_second, far_first, near_second, arriving = started
    return (own, near_first, far_second), sum_onward(far_first, arriving[0], near_second, arriving[1])


def collect_onward(onward):
    return flip(onward[0], 2), flip(onward[1], 1)


def collect_end(kept, last, kind, gathered, own_selector, *operands):
    own, near_first, far_second = kept
    parts = [own[0], near_first, last[0], own[1], far_second, last[1]]
    return finish(kind, parts, gathered, own_selector, *operands)


def collect_project(values, gathered, kind, own_selector, *operands):
    rows, model = own_selector.shape[0], operands[0].shape[1]
    if quick(rows):
        kept, onward = collect_middle(collect_send(collect_pieces(values, gathered, False)))
        return collect_end(kept, collect_onward(onward), kind, gathered, own_selector, *operands)
    wide, narrow_factor = gathered
    width = narrow_factor.shape[1]
    partial = jnp.concatenate(
        [contract_last(values, wide[:, :width]), contract_last(values, narrow_factor)], axis=1
    ).astype(BFLOAT)
    summed = lax.psum_scatter(partial, "col", scatter_dimension=0, tiled=True).astype(FLOAT)
    inner = (own_selector * summed[:, model:]).astype(BFLOAT)
    summed = summed[:, :model] + contract_last(inner, wide[:, width:])
    if kind == "output":
        return (operands[0] + summed).astype(BFLOAT), inner
    if kind == "forward":
        residual, gain = operands
        hidden = residual + summed
        return hidden, inner, *cut_halves(rms_norm(hidden, gain[0]).astype(BFLOAT))
    values, upstream, gain = operands
    _, back = jax.vjp(lambda given: rms_norm(given, gain[0]), values)
    hidden = upstream.astype(FLOAT) + back(summed)[0]
    if kind == "input":
        return hidden.astype(BFLOAT), inner
    return hidden, inner, *cut_halves(hidden.astype(BFLOAT))


def cut_halves(values):
    half = values.shape[1] // HALVES
    return values[:, :half], values[:, half:]


def local(
    tokens_in,
    cotangent,
    target,
    sequence_lengths,
    sequence_adapter,
    norm_gains,
    weight_in,
    conv_values,
    conv_states,
    scan_params,
    weight_mix,
    weight_feed,
    weight_down,
    in_lower,
    in_raise,
    mix_lower,
    mix_raise,
    feed_lower,
    feed_raise,
    down_lower,
    down_raise,
):
    cols = lax.axis_size("col")
    rows_axis = lax.axis_size("row")
    col = lax.axis_index("col")
    devices = cols * rows_axis
    rows = tokens_in.shape[0]
    model = tokens_in.shape[1]
    total = rows * cols
    units = QUERY_HEADS // cols
    channels = units * GATE_WIDTH
    peer = rows // devices
    lengths, adapters = sequence_lengths[0], sequence_adapter[0]
    sequences = lengths.shape[0]
    fast = quick(rows)
    key_head = col * units // (QUERY_HEADS // KEY_VALUE_HEADS)
    exchange = lambda values: lax.all_to_all(values, ALL_AXES, split_axis=0, concat_axis=0, tiled=True)

    sent, send_matrix = send_tokens(target, tokens_in, adapters, peer)
    shards = []

    def gather_weight(weight, lower, raised):
        top = jnp.concatenate([weight, lower], axis=1)
        if fast:
            bottom = pad_columns(raised, top.shape[1])
            shards.append(jnp.concatenate([top, bottom], axis=0))
            return (lax.all_gather(shards[-1], "row", axis=0),)
        wide = lax.all_gather(top, "row", axis=0, tiled=True)
        return wide, lax.all_gather(raised, "row", axis=0, tiled=True)

    depth = weight_in.shape[0]
    height = depth + in_raise.shape[0]
    given = after(jnp.concatenate([weight_in, in_raise], axis=0), send_matrix)
    pair_width, state_width = units * PAIR_WIDTH, units * STATE_WIDTH
    taps = jnp.pad(conv_states, ((0, 16 - KCONV - 1), (0, 0)))
    if fast:
        full = -(-given.shape[1] // LANES) * LANES
        own_shard, shared_shard = make_shards(pad_columns(given, full), in_lower, taps)
        shared = lax.all_gather(shared_shard, "row", axis=0)
        shards.append(own_shard)
        weights_own = (lax.all_gather(own_shard, "row", axis=0),)
    else:
        gates, convs, queries, pairs, states, steps = unit_parts(given, units)
        taps = jnp.concatenate([jnp.zeros((taps.shape[0], pair_width), BFLOAT), taps], axis=1)
        shared = jnp.concatenate([jnp.concatenate([pairs, states], axis=1), taps], axis=0)
        own_columns = jnp.concatenate([gates, convs, queries, pad_columns(steps, LANES)], axis=1)
    arrived = exchange(sent)
    gains = jnp.broadcast_to(norm_gains.astype(FLOAT)[:, None, :], (2, 8, model))
    if fast:
        near, far = flip(shared, 1), flip(shared, 2)
        arrived = after(arrived, near, far, shards[0])
    own_input, place_matrix, *normed_one = arrive_tokens(arrived.reshape(rows, model + LANES), gains[0])
    blocks_one = gather_blocks(normed_one) if fast else normed_one
    if fast:
        held = jnp.zeros((cols,) + shared.shape, BFLOAT)
        for block, values in ((col, shared), (col ^ 1, near), (col ^ 2, far)):
            held = lax.dynamic_update_index_in_dim(held, values, block, 0)
        split = shared.shape[0] // 2
        corner = jnp.concatenate([flip(near[:split], 2), flip(far[split:], 1)], axis=0)
        held = lax.dynamic_update_index_in_dim(held, corner, col ^ 3, 0)
    else:
        held = lax.all_gather(shared, "col", axis=0)
    all_pairs = jnp.concatenate([held[at, ..., :height, :pair_width] for at in range(cols)], axis=-1)
    pick = lambda start: lax.select_n(
        key_head,
        *[all_pairs[..., start + at * HEAD_SIZE : start + (at + 1) * HEAD_SIZE] for at in range(KEY_VALUE_HEADS)],
    )
    shared_columns = jnp.concatenate(
        [held[at, ..., :height, pair_width:] for at in range(cols)]
        + [pick(0), pick(KEY_VALUE_HEADS * HEAD_SIZE)],
        axis=-1,
    )
    tap_rows = held[:, 0] if fast else held
    all_taps = jnp.concatenate(
        [tap_rows[at, height : height + KCONV + 1, pair_width:] for at in range(cols)], axis=1
    )
    if fast:
        weights_in = (shared_columns, *weights_own)
    else:
        columns = jnp.concatenate([shared_columns, own_columns], axis=1)
        weights_in = gather_weight(columns[:depth], in_lower, columns[depth:])
    weights_mix = gather_weight(
        after(split_halves(weight_mix, units, GATE_WIDTH, 0).T, sent),
        mix_raise.T,
        split_halves(mix_lower, units, GATE_WIDTH, 0).T,
    )
    weights_feed = gather_weight(
        after(split_halves(weight_feed, units, UNIT_FF, 1), arrived),
        feed_lower,
        split_halves(feed_raise, units, UNIT_FF, 1),
    )

    source_adapters = arrived.reshape(rows, model + LANES)[::peer, model + 1 : model + 1 + sequences].astype(jnp.int32)
    segment, position, selector = sequence_tables(lengths, adapters, total)
    own_selector = rows_of(selector, col, rows)
    own_segment = rows_of(segment, col, rows)
    tables = mixer_tables(lengths, segment, position, conv_values, all_taps, scan_params)

    def compact_grad(narrow, values):
        parts = [
            lax.dynamic_slice_in_dim(narrow, adapters[at] * RANK, RANK, 1)
            * (own_segment == at).astype(BFLOAT)[:, None]
            for at in range(sequences)
        ]
        grad = contract_first(jnp.concatenate(parts, axis=1), values).astype(BFLOAT)
        kept = sequences * RANK
        grad = grad.reshape(kept, devices, model // devices).transpose(1, 0, 2)
        return grad.reshape(devices, peer, kept * model // devices // peer)

    def expand_grad(dealt):
        kept = sequences * RANK
        dealt = dealt.reshape(devices * kept, model // devices)
        adapter_row = (source_adapters[:, :, None] * RANK + jnp.arange(RANK, dtype=jnp.int32)).reshape(-1)
        chosen = (jnp.arange(NADAPT * RANK, dtype=jnp.int32)[:, None] == adapter_row[None, :]).astype(BFLOAT)
        return product(chosen, dealt)

    def send_back(values, grads):
        back = contract_first(place_matrix, values).astype(BFLOAT).reshape(devices, peer, model)
        return exchange(jnp.concatenate([back, *grads], axis=2))

    def expand_packed(dealt, count):
        slots = dealt.shape[0] * peer
        block = jnp.arange(2 * LANES // (model // devices), dtype=jnp.int32)[:, None, None]
        row = jnp.arange(peer, dtype=jnp.int32)[None, None, :]
        place = block * peer + row
        adapter = jnp.where(place < RANK, source_adapters[None, :, 0:1], source_adapters[None, :, 1:2])
        adapter_row = (adapter * RANK + place % RANK).reshape(block.shape[0], 1, slots)
        chosen = (jnp.arange(NADAPT * RANK, dtype=jnp.int32)[None, :, None] == adapter_row).astype(BFLOAT)
        sums = product(chosen.reshape(-1, slots), dealt.reshape(slots, dealt.shape[2]))
        sums = sums.reshape(block.shape[0], NADAPT * RANK, dealt.shape[2])
        width = model // devices
        return [
            sum(
                sums[at, :, grad * 2 * LANES + at * width : grad * 2 * LANES + (at + 1) * width]
                for at in range(block.shape[0])
            )
            for grad in range(count)
        ]

    def take_back(dealt, count):
        returned = contract_first(send_matrix, dealt[:, :, :model].reshape(rows, model)).astype(BFLOAT)
        if fast:
            return returned, expand_packed(dealt[:, :, model:], count)
        width = (dealt.shape[2] - model) // count
        return returned, [
            expand_grad(dealt[:, :, model + at * width : model + (at + 1) * width]) for at in range(count)
        ]

    projected, inner_in = (spread_gathered if fast else spread_project)(blocks_one, weights_in, selector)

    sent_grad = product(send_matrix, cotangent).astype(BFLOAT).reshape(devices, peer, model)
    arrived_grad = exchange(after(sent_grad, normed_one[0])).reshape(rows, model)
    branch_two = product(place_matrix, arrived_grad).astype(BFLOAT)
    weights_down = gather_weight(after(weight_down.T, projected), down_raise.T, down_lower.T)

    mixed_out = attention_forward(projected, tables)
    mixed_out, scanned, carried = scan_forward(projected, tables, mixed_out)
    hidden, inner_out, *normed_two = collect_project(mixed_out, weights_mix, "forward", own_selector, own_input, gains[1])
    gate_up, inner_feed = spread_project(normed_two, weights_feed, selector)
    branch_halves = cut_halves(after(branch_two, projected))
    if fast:
        act_grad, narrow_two = spread_blocks(gather_blocks(branch_halves), weights_down, selector, None)
    else:
        act_grad, narrow_two = spread_project(branch_halves, weights_down, selector)
    half_feed = units * UNIT_FF
    gate_part, up_part = gate_up[:, :half_feed].astype(FLOAT), gate_up[:, half_feed:].astype(FLOAT)
    gate = jax.nn.sigmoid(gate_part)
    silu = gate_part * gate
    activated = (silu * up_part).astype(BFLOAT)
    wide_grad = act_grad.astype(FLOAT)
    feed_grad = jnp.concatenate(
        [wide_grad * up_part * (gate * (1.0 + gate_part * (1.0 - gate))), wide_grad * silu], axis=1
    ).astype(BFLOAT)
    choose = (
        jnp.arange(NADAPT * RANK, dtype=jnp.int32)[:, None]
        == (adapters[:, None] * RANK + jnp.arange(RANK, dtype=jnp.int32)[None, :]).reshape(1, -1)
    ).astype(BFLOAT)
    if fast:
        pieces = collect_pieces(after(activated, feed_grad), weights_down, True)
        kept, onward = collect_middle(collect_send(collect_pieces(feed_grad, weights_feed, False)))
        hidden_grad, narrow_three, left, right, early_grads = collect_end(
            kept,
            collect_onward(onward),
            "backward",
            weights_feed,
            own_selector,
            after(hidden, pieces[3][0]),
            branch_two,
            gains[1],
            choose,
            *normed_two,
            inner_out,
        )
        mixed_grad, narrow_one = spread_early((left, right), weights_mix, selector)
    else:
        hidden_grad, narrow_three, *branch_one = collect_project(
            feed_grad, weights_feed, "backward", own_selector, hidden, branch_two, gains[1]
        )
        mixed_grad, narrow_one = spread_project(branch_one, weights_mix, selector)

    if fast:
        near_parts = after_all((*pieces[0], pieces[1][0], pieces[2][1]), mixed_grad)
        started = collect_send(
            [near_parts[:2], (near_parts[2], pieces[1][1]), (pieces[2][0], near_parts[3]), pieces[3]], False
        )
        attended_grads = attention_backward(projected, tables, after(mixed_grad, near_parts[0]))
        kept, onward = collect_middle((*started[:5], after_all(started[5], attended_grads[1])))
        scan_inputs = (projected, tables, scanned, carried, after(mixed_grad, *onward), attended_grads)
        scan_part = list(scan_backward(*scan_inputs, 0, 2, None))
        payload = collect_end(
            kept,
            collect_onward(onward),
            "output",
            weights_down,
            own_selector,
            after(hidden, scan_part[2]),
            place_matrix,
            choose,
            branch_two,
            early_grads,
        )
        dealt_out = exchange(payload.reshape(devices, peer, -1))
        scan_part[2] = after(scan_part[2], payload)
        projected_grad = scan_backward(*scan_inputs, 1, 2, scan_part)[0]
        *pieces_in, raise_grad = collect_blocks([3, 1, 2, 0], projected_grad, weights_in, PIECE_TYPES, [inner_in])
        started_in = collect_send(pieces_in)
        kept_in, onward_in = collect_middle(started_in)
    else:
        block_out, inner_down = collect_project(activated, weights_down, "output", own_selector, hidden)
        attended_grads = attention_backward(projected, tables, mixed_grad)
        projected_grad = scan_backward(
            projected, tables, scanned, carried, mixed_grad, attended_grads, 0, 1, None
        )[0]
        dealt_out = send_back(
            block_out,
            [
                compact_grad(inner_down, branch_two),
                compact_grad(narrow_three, jnp.concatenate(normed_two, axis=1)),
                compact_grad(inner_out, jnp.concatenate(branch_one, axis=1)),
            ],
        )

    def sum_rows(values):
        return lax.psum_scatter(values.astype(BFLOAT), "row", scatter_dimension=0, tiled=True).astype(FLOAT)

    early_parts = [
        contract_first(narrow_one, mixed_out),
        contract_first(inner_feed, feed_grad),
        contract_first(narrow_two, activated),
    ]
    early = sum_rows(jnp.concatenate(early_parts, axis=1))

    late = sum_rows(raise_grad if fast else contract_first(inner_in, projected_grad))

    if fast:
        payload = collect_end(
            kept_in,
            collect_onward(onward_in),
            "input",
            weights_in,
            own_selector,
            own_input,
            after(hidden_grad, dealt_out),
            gains[0],
            choose,
            *normed_one,
            place_matrix,
        )
        dealt_grad = exchange(payload.reshape(devices, peer, -1))
    else:
        input_grad, narrow_four = collect_project(
            projected_grad, weights_in, "input", own_selector, own_input, hidden_grad, gains[0]
        )
        dealt_grad = send_back(input_grad, [compact_grad(narrow_four, jnp.concatenate(normed_one, axis=1))])
        payload = input_grad
    dealt_out, early, late = after_all((dealt_out, early, late), payload)
    early_cuts = [0, early_parts[0].shape[1]]
    early_cuts.append(early_cuts[1] + early_parts[1].shape[1])
    grad_mix_lower = join_halves(early[:, : early_cuts[1]], units, GATE_WIDTH, 1).T
    grad_feed_raise = join_halves(early[:, early_cuts[1] : early_cuts[2]], units, UNIT_FF, 1)
    grad_down_lower = early[:, early_cuts[2] :].T

    key_columns = late[:, STATES : STATES + HEAD_SIZE]
    value_columns = late[:, STATES + HEAD_SIZE : STATES + PAIR]
    mine = [(key_head == at).astype(FLOAT) for at in range(KEY_VALUE_HEADS)]
    pair_grad = jnp.concatenate([part * here for part in (key_columns, value_columns) for here in mine], axis=1)
    stacked = jnp.stack(
        [
            jnp.concatenate(
                [
                    pair_grad[:, at * pair_width : (at + 1) * pair_width],
                    late[:, at * state_width : (at + 1) * state_width],
                ],
                axis=1,
            )
            for at in range(cols)
        ]
    )
    if fast:
        piece = lambda mask: lax.dynamic_index_in_dim(stacked, col ^ mask, 0, False)
        shared_sum = piece(0) + flip(piece(1), 1) + flip(piece(2), 2) + flip(piece(3), 3)
    else:
        shared_sum = lax.psum_scatter(
            stacked.reshape(stacked.shape[0] * stacked.shape[1], -1), "col", scatter_dimension=0, tiled=True
        )
    late = jnp.concatenate([shared_sum, late[:, STATES + PAIR :]], axis=1)
    shared_width = pair_width + state_width
    cuts = [shared_width]
    for width in (channels, channels, units * HEAD_SIZE, units * STEP_WIDTH):
        cuts.append(cuts[-1] + width)
    gate_columns, conv_columns, query_columns, step_columns = [
        late[:, low:high] for low, high in zip(cuts[:-1], cuts[1:])
    ]
    grad_in_raise = restore_units(
        [
            gate_columns,
            conv_columns,
            query_columns,
            late[:, :pair_width],
            late[:, pair_width:shared_width],
            step_columns,
        ],
        units,
    )

    returned_out, (grad_down_raise, grad_feed_lower, grad_mix_raise) = take_back(dealt_out, 3)
    returned_grad, (grad_in_lower,) = take_back(dealt_grad, 1)
    return (
        returned_out,
        returned_grad,
        grad_in_lower.T,
        grad_in_raise,
        grad_mix_lower,
        grad_mix_raise,
        grad_feed_lower.T,
        grad_feed_raise,
        grad_down_lower,
        grad_down_raise,
    )


def solution(mesh):
    in_specs = (
        P(("row", "col"), None),
        P(("row", "col"), None),
        P(("row", "col")),
        P("row", None),
        P("row", None),
        P(),
        P("row", "col"),
        P(None, "col"),
        P(None, "col"),
        P(None, "col"),
        P("col", "row"),
        P("row", "col"),
        P("col", "row"),
        P("row", None),
        P("row", "col"),
        P("col", "row"),
        P(None, "row"),
        P("row", None),
        P("row", "col"),
        P("col", "row"),
        P(None, "row"),
    )
    out_specs = (
        P(("row", "col"), None),
        P(("row", "col"), None),
        P(("row", "col"), None),
        P("row", "col"),
        P("col", "row"),
        P(None, ("row", "col")),
        P(("row", "col"), None),
        P("row", "col"),
        P("col", "row"),
        P(None, ("row", "col")),
    )
    return jax.shard_map(local, mesh=mesh, in_specs=in_specs, out_specs=out_specs, check_vma=False)
```

```python
import functools
import math

import jax
import jax.numpy as jnp
from jax import lax
from jax.experimental import pallas as pl
from jax.experimental.pallas import tpu as pltpu
from jax.sharding import PartitionSpec as P

NH = 48
HP = 64
NSTATE = 256
KCONV = 4
QUERY_HEADS = 8
KEY_VALUE_HEADS = 2
HEAD_SIZE = 128
RANK = 16
NADAPT = 8
SSD_BLOCK = 256
DSSM = 3072
UNIT_IN = 1030
UNIT_FF = 512


EPSILON = 1e-05
ROPE_BASE = 10000.0
NEGATIVE = -1e30
FLOAT = jnp.float32
BFLOAT = jnp.bfloat16


def product(left, right):
    return jnp.dot(left, right, preferred_element_type=FLOAT)


def contract_last(left, right):
    return lax.dot_general(left, right, (((1,), (1,)), ((), ())), preferred_element_type=FLOAT)


def contract_first(left, right):
    return lax.dot_general(left, right, (((0,), (0,)), ((), ())), preferred_element_type=FLOAT)


def rms_norm(values, gain):
    return values * lax.rsqrt(jnp.mean(values * values, axis=-1, keepdims=True) + EPSILON) * gain


def sequence_tables(lengths, adapters, sequence_length):
    sequence_count = lengths.shape[0]
    boundary = jnp.cumsum(lengths)
    token_index = jnp.arange(sequence_length, dtype=jnp.int32)
    passed = (token_index[:, None] >= boundary[None, :]).astype(jnp.int32)
    segment = jnp.sum(passed, axis=1)
    segment_start = jnp.sum(passed * lengths[None, :], axis=1)
    position = token_index - segment_start
    member = (segment[:, None] == jnp.arange(sequence_count, dtype=jnp.int32)[None, :]).astype(
        jnp.int32
    )
    chosen = jnp.sum(member * adapters[None, :], axis=1)
    column = jnp.arange(NADAPT * RANK, dtype=jnp.int32) // RANK
    selector = (chosen[:, None] == column[None, :]).astype(FLOAT)
    return (segment, position, selector)


ESTIMATE = 16
SCAN_BYTES = 32 * 1024 * 1024
DENSE_BYTES = 16 * 1024 * 1024
FINISH_BYTES = 32 * 1024 * 1024
LANES = 128


def whole(shape):
    return pl.BlockSpec(shape, lambda *_: (0,) * len(shape))


def estimate(flops, bytes_accessed, transcendentals):
    return pl.CostEstimate(
        flops=flops // ESTIMATE,
        bytes_accessed=bytes_accessed // ESTIMATE,
        transcendentals=transcendentals // ESTIMATE,
    )


def dot(left, right, contract):
    return lax.dot_general(left, right, ((contract[:1], contract[1:]), ((), ())), preferred_element_type=FLOAT)


def parts_of(values, count):
    parts = []
    for _ in range(count):
        part = values.astype(BFLOAT)
        parts.append(part)
        values = values - part.astype(FLOAT)
    return parts


def running_sum(values, triangle, contract):
    width = values.shape[1]
    split = dot(triangle, jnp.concatenate(parts_of(values, 3), axis=1), contract)
    return split[:, :width] + split[:, width : 2 * width] + split[:, 2 * width :]


def head_spread(values, expand):
    return dot(jnp.concatenate(parts_of(values, 2), axis=1), expand, (1, 0))


def head_sum(values, expand):
    high, low = parts_of(values, 2)
    single = expand[:LANES]
    return dot(high, single, (1, 1)) + dot(low, single, (1, 1))


def silu_parts(values):
    gate = 1.0 / (1.0 + jnp.exp(-values))
    return values * gate, gate


def expand_table(channels):
    row = lax.broadcasted_iota(jnp.int32, (2 * LANES, channels), 0) % LANES
    channel = lax.broadcasted_iota(jnp.int32, (2 * LANES, channels), 1) // HP
    return (row == channel).astype(BFLOAT)


def conv_sum(current_ref, before_ref, taps_ref, meta):
    rows = SSD_BLOCK
    current = current_ref[...].astype(FLOAT)
    window = jnp.concatenate([before_ref[...].astype(FLOAT)[8:16], current], axis=0)
    summed = taps_ref[KCONV : KCONV + 1, :] + current * taps_ref[0:1, :]
    for lag in range(1, KCONV):
        shifted = window[8 - lag : 8 - lag + rows]
        summed = summed + jnp.where(meta[:, 1:2] >= lag, shifted, 0.0) * taps_ref[lag : lag + 1, :]
    return summed


def conv_back(summed_grad, later, taps_ref, meta):
    rows = SSD_BLOCK
    window = jnp.concatenate([summed_grad, later[...]], axis=0)
    grad = summed_grad * taps_ref[0:1, :]
    for lag in range(1, KCONV):
        grad = grad + jnp.where(meta[:, 2:3] >= lag, window[lag : lag + rows], 0.0) * taps_ref[lag : lag + 1, :]
    later[...] = summed_grad[:8]
    return grad


def silu_slope(values, gate):
    return gate * (1.0 + values * (1.0 - gate))


def scan_block(
    conv_ref, before_ref, state_ref, state_before_ref, step_ref, meta_ref, segment_ref, taps_ref, state_taps_ref, head_ref,
    turned_over,
):
    rows = SSD_BLOCK
    channels = conv_ref.shape[1]
    meta = meta_ref[...]
    summed = conv_sum(conv_ref, before_ref, taps_ref, meta)
    activated, conv_gate = silu_parts(summed)
    wide_inputs = activated.astype(BFLOAT).astype(FLOAT)
    state_summed = conv_sum(state_ref, state_before_ref, state_taps_ref, meta)
    state_values, state_gate = silu_parts(state_summed)
    write = state_values[:, :NSTATE].astype(BFLOAT)
    read = state_values[:, NSTATE:].astype(BFLOAT)
    raw = step_ref[...].astype(FLOAT) + head_ref[0:1, :]
    steps = jnp.maximum(raw, 0.0) + jnp.log1p(jnp.exp(-jnp.abs(raw)))
    row = lax.broadcasted_iota(jnp.int32, (rows, rows), 0)
    column = lax.broadcasted_iota(jnp.int32, (rows, rows), 1)
    triangle = (row >= column).astype(BFLOAT)
    total = running_sum(steps * head_ref[1:2, :], triangle, (1, 0))
    entered = jnp.exp(total) * meta[:, 3:4]
    leaving = jnp.exp(total[rows - 1 : rows] - total) * meta[:, 4:5]
    expand = expand_table(channels)
    spread = head_spread(jnp.concatenate([steps, entered, leaving * steps], axis=0), expand)
    ordered = row <= column if turned_over else row >= column
    blocked = jnp.where(ordered & (meta[:, 0:1] == segment_ref[0:1, :]), 0.0, NEGATIVE)
    return dict(
        summed=summed,
        conv_gate=conv_gate,
        state_summed=state_summed,
        state_gate=state_gate,
        write=write,
        read=read,
        wide_inputs=wide_inputs,
        raw=raw,
        steps=steps,
        triangle=triangle,
        total=total,
        total_rows=total.T,
        leaving=leaving,
        expand=expand,
        steps_wide=spread[:rows],
        entered_wide=spread[rows : 2 * rows],
        tail_wide=spread[2 * rows :],
        stepped=(wide_inputs * spread[:rows]).astype(BFLOAT),
        tailed=(wide_inputs * spread[2 * rows :]).astype(BFLOAT),
        blocked=blocked,
        crossing=dot(write, read, (1, 1)) if turned_over else dot(read, write, (1, 1)),
    )


def decay_of(block, head):
    difference = block["total"][:, head : head + 1] - block["total_rows"][head : head + 1, :]
    return jnp.exp(difference + block["blocked"])


def turned_decay_of(block, head):
    difference = block["total_rows"][head : head + 1, :] - block["total"][:, head : head + 1]
    return jnp.exp(difference + block["blocked"])


def scan_forward_kernel(
    gate_ref, conv_ref, before_ref, state_ref, state_before_ref, step_ref, meta_ref, segment_ref, taps_ref,
    state_taps_ref, head_ref, skip_ref, mixed_ref, out_ref, scanned_ref, states_ref, state,
):
    del mixed_ref

    @pl.when(pl.program_id(0) == 0)
    def _():
        state[...] = jnp.zeros_like(state)

    block = scan_block(
        conv_ref, before_ref, state_ref, state_before_ref, step_ref, meta_ref, segment_ref, taps_ref, state_taps_ref,
        head_ref, False,
    )
    heads = conv_ref.shape[1] // HP
    carried = state[...].astype(BFLOAT)
    states_ref[0] = carried
    across = dot(block["read"], carried, (1, 0)) * block["entered_wide"]
    within = []
    for head in range(heads):
        weights = (block["crossing"] * decay_of(block, head)).astype(BFLOAT)
        within.append(dot(weights, block["stepped"][:, head * HP : (head + 1) * HP], (1, 0)))
    scanned = across + jnp.concatenate(within, axis=1)
    scanned_ref[...] = scanned
    gated, _ = silu_parts(gate_ref[...].astype(FLOAT))
    out_ref[...] = ((scanned + skip_ref[0:1, :] * block["wide_inputs"]) * gated).astype(BFLOAT)
    state[...] = state[...] * block["entered_wide"][SSD_BLOCK - 1 : SSD_BLOCK, :] + dot(
        block["write"], block["tailed"], (0, 0)
    )


def scan_backward_kernel(
    gate_ref, conv_ref, before_ref, state_ref, state_before_ref, step_ref, meta_ref, segment_ref, taps_ref,
    state_taps_ref, head_ref, skip_ref, scanned_ref, states_ref, grad_ref, query_grad_ref, shared_grad_ref, *rest,
):
    out_ref, *running = rest[-4:]
    state_grad, later, state_later = running

    @pl.when(pl.program_id(0) == 0)
    def _():
        for at, ref in enumerate(running):
            ref[...] = rest[1 + at][...] if len(rest) > 4 else jnp.zeros_like(ref)

    block = scan_block(
        conv_ref, before_ref, state_ref, state_before_ref, step_ref, meta_ref, segment_ref, taps_ref, state_taps_ref,
        head_ref, True,
    )
    rows = SSD_BLOCK
    channels = conv_ref.shape[1]
    heads = channels // HP
    meta = meta_ref[...]
    read, write = block["read"], block["write"]
    inputs = block["wide_inputs"]
    scanned = scanned_ref[...]
    skip = skip_ref[0:1, :]
    gate_values = gate_ref[...].astype(FLOAT)
    gated, gate = silu_parts(gate_values)
    grad = grad_ref[...].astype(FLOAT)
    gate_grad = grad * (scanned + skip * inputs) * silu_slope(gate_values, gate)
    out_grad = grad * gated
    inputs_grad = skip * out_grad
    rounded = out_grad.astype(BFLOAT)
    wide_rounded = rounded.astype(FLOAT)
    carried = states_ref[0]
    after = state_grad[...]
    after_rounded = after.astype(BFLOAT)

    from_state = dot(write, after_rounded, (1, 0))
    entering = (wide_rounded * block["entered_wide"]).astype(BFLOAT)
    write_grad = dot(block["tailed"], after_rounded, (1, 1))
    read_grad = dot(entering, carried, (1, 1))
    last_entered = block["entered_wide"][rows - 1 : rows, :]
    through = jnp.sum(after * carried.astype(FLOAT), axis=0, keepdims=True) * last_entered
    state_grad[...] = after * last_entered + dot(read, entering, (0, 0))

    crossing_grad = jnp.zeros((rows, rows), FLOAT)
    pulled = []
    for head in range(heads):
        span = slice(head * HP, (head + 1) * HP)
        decay = turned_decay_of(block, head)
        weights = (block["crossing"] * decay).astype(BFLOAT)
        pulled.append(dot(weights, rounded[:, span], (1, 0)))
        crossing_grad = crossing_grad + dot(block["stepped"][:, span], rounded[:, span], (1, 1)) * decay
    pulled = jnp.concatenate(pulled, axis=1)
    crossing_rounded = crossing_grad.astype(BFLOAT)
    read_grad = read_grad + dot(crossing_rounded, write, (0, 0))
    write_grad = write_grad + dot(crossing_rounded, read, (1, 0))

    inputs_grad = inputs_grad + block["steps_wide"] * pulled + block["tail_wide"] * from_state
    sums = head_sum(
        jnp.concatenate(
            [
                wide_rounded * scanned - block["stepped"].astype(FLOAT) * pulled,
                inputs * pulled,
                inputs * from_state,
                jnp.broadcast_to(through, (8, channels)),
            ],
            axis=0,
        ),
        block["expand"],
    )
    leaving_grad = sums[2 * rows : 3 * rows] * block["leaving"]
    leaving_total = leaving_grad * block["steps"]
    last = sums[3 * rows : 3 * rows + 1] + jnp.sum(leaving_total, axis=0, keepdims=True)
    total_grad = sums[:rows] - leaving_total
    total_grad = total_grad + jnp.where(
        lax.broadcasted_iota(jnp.int32, total_grad.shape, 0) == rows - 1, last, 0.0
    )
    decay_grad = running_sum(total_grad, block["triangle"], (0, 0))
    steps_grad = sums[rows : 2 * rows] + leaving_grad + decay_grad * head_ref[1:2, :]
    raw_grad = steps_grad / (1.0 + jnp.exp(-block["raw"]))
    raw_grad = jnp.where(lax.broadcasted_iota(jnp.int32, raw_grad.shape, 1) < heads, raw_grad, 0.0)

    state_slope = silu_slope(block["state_summed"], block["state_gate"])
    state_pre = conv_back(
        jnp.concatenate([write_grad, read_grad], axis=1) * state_slope, state_later, state_taps_ref, meta
    )
    conv_pre = conv_back(inputs_grad * silu_slope(block["summed"], block["conv_gate"]), later, taps_ref, meta)
    out_ref[:, : 2 * NSTATE] = state_pre.astype(BFLOAT)
    start = 2 * NSTATE + 2 * HEAD_SIZE
    end = out_ref.shape[1] - LANES
    out_ref[:, 2 * NSTATE : start] = shared_grad_ref[...]
    out_ref[:, start + 2 * channels : end] = query_grad_ref[...]
    out_ref[:, start : start + channels] = gate_grad.astype(BFLOAT)
    out_ref[:, start + channels : start + 2 * channels] = conv_pre.astype(BFLOAT)
    out_ref[:, end:] = raw_grad.astype(BFLOAT)


STATES = 2 * NSTATE
PAIR = 2 * HEAD_SIZE


def scan_specs(channels, order):
    half = SSD_BLOCK // 16
    before = lambda i: jnp.maximum(order(i) * half - 1, 0)
    gate_at = (STATES + PAIR) // channels
    step_at = (STATES + PAIR + 2 * channels + channels * QUERY_HEADS // DSSM * HEAD_SIZE) // LANES
    return [
        pl.BlockSpec((SSD_BLOCK, channels), lambda i: (order(i), gate_at)),
        pl.BlockSpec((SSD_BLOCK, channels), lambda i: (order(i), gate_at + 1)),
        pl.BlockSpec((16, channels), lambda i: (before(i), gate_at + 1)),
        pl.BlockSpec((SSD_BLOCK, STATES), lambda i: (order(i), 0)),
        pl.BlockSpec((16, STATES), lambda i: (before(i), 0)),
        pl.BlockSpec((SSD_BLOCK, LANES), lambda i: (order(i), step_at)),
        pl.BlockSpec((SSD_BLOCK, LANES), lambda i: (order(i), 0)),
        pl.BlockSpec((8, SSD_BLOCK), lambda i: (0, order(i))),
        whole((8, channels)),
        whole((8, STATES)),
        whole((8, LANES)),
        whole((8, channels)),
    ]


def scan_operands(projected, tables):
    return [projected] * 6 + [
        tables[name] for name in ("meta", "segment_row", "taps", "state_taps", "head", "skip")
    ]


def scan_cost(tokens, channels, factor):
    heads = channels // HP
    return estimate(
        flops=factor * 2 * tokens * SSD_BLOCK * (3 * channels + NSTATE),
        bytes_accessed=factor * tokens * channels * 12,
        transcendentals=tokens * SSD_BLOCK * heads,
    )


def scan_forward(projected, tables, mixed):
    tokens = projected.shape[0]
    channels = tables["taps"].shape[1]
    blocks = tokens // SSD_BLOCK
    return pl.pallas_call(
        scan_forward_kernel,
        grid=(blocks,),
        in_specs=scan_specs(channels, lambda i: i) + [pl.BlockSpec(memory_space=pl.ANY)],
        out_specs=[
            pl.BlockSpec((SSD_BLOCK, channels), lambda i: (i, 0)),
            pl.BlockSpec((SSD_BLOCK, channels), lambda i: (i, 0)),
            pl.BlockSpec((1, NSTATE, channels), lambda i: (i, 0, 0)),
        ],
        out_shape=[
            jax.ShapeDtypeStruct(mixed.shape, BFLOAT),
            jax.ShapeDtypeStruct((tokens, channels), FLOAT),
            jax.ShapeDtypeStruct((blocks, NSTATE, channels), BFLOAT),
        ],
        scratch_shapes=[pltpu.VMEM((NSTATE, channels), FLOAT)],
        input_output_aliases={12: 0},
        compiler_params=pltpu.CompilerParams(vmem_limit_bytes=SCAN_BYTES),
        cost_estimate=scan_cost(tokens, channels, 1),
        name="scan_forward",
    )(*scan_operands(projected, tables), mixed)


def scan_backward(projected, tables, scanned, carried, mixed_grad, attended_grads, part, parts, before):
    tokens, width = projected.shape
    channels = tables["taps"].shape[1]
    blocks = tokens // SSD_BLOCK
    last = blocks - 1 - part * (blocks // parts)
    back = lambda i: (last - i, 0)
    running = [(NSTATE, channels), (8, channels), (8, STATES)]
    query_grad, shared_grad = attended_grads
    operands = [*scan_operands(projected, tables), scanned, carried, mixed_grad, query_grad, shared_grad]
    in_specs = scan_specs(channels, lambda i: last - i) + [
        pl.BlockSpec((SSD_BLOCK, channels), back),
        pl.BlockSpec((1, NSTATE, channels), lambda i: (last - i, 0, 0)),
        pl.BlockSpec((SSD_BLOCK, channels), back),
        pl.BlockSpec((SSD_BLOCK, query_grad.shape[1]), back),
        pl.BlockSpec((SSD_BLOCK, PAIR), back),
    ]
    aliases = {}
    if before is not None:
        aliases = {len(operands): 0}
        operands += list(before)
        in_specs += [pl.BlockSpec(memory_space=pl.ANY), *[whole(shape) for shape in running]]
    return pl.pallas_call(
        scan_backward_kernel,
        grid=(blocks // parts,),
        in_specs=in_specs,
        out_specs=[pl.BlockSpec((SSD_BLOCK, width), back), *[whole(shape) for shape in running]],
        out_shape=[
            jax.ShapeDtypeStruct((tokens, width), BFLOAT),
            *[jax.ShapeDtypeStruct(shape, FLOAT) for shape in running],
        ],
        input_output_aliases=aliases,
        compiler_params=pltpu.CompilerParams(vmem_limit_bytes=SCAN_BYTES),
        cost_estimate=scan_cost(tokens, channels, 2),
        name="scan_backward",
    )(*operands)


def turned(values, cosine, sine):
    return (values * cosine + pltpu.roll(values, HEAD_SIZE // 2, 1) * sine).astype(BFLOAT)


def turned_back(values, cosine, sine):
    return values * cosine + pltpu.roll(values * sine, HEAD_SIZE // 2, 1)


ATT_ROWS = 256


def attention_mask(meta_ref, segment_ref, start, extent):
    row = start + lax.broadcasted_iota(jnp.int32, (ATT_ROWS, extent), 0)
    column = lax.broadcasted_iota(jnp.int32, (ATT_ROWS, extent), 1)
    return (row >= column) & (meta_ref[start : start + ATT_ROWS, 0:1] == segment_ref[0:1, :extent])


def probabilities(query, keys, allowed):
    score = dot(query, keys, (1, 1)) * (1.0 / math.sqrt(HEAD_SIZE))
    score = jnp.where(allowed, score, NEGATIVE)
    exponent = jnp.exp(score - jnp.max(score, axis=1, keepdims=True))
    return exponent / jnp.sum(exponent, axis=1, keepdims=True)


def attention_forward_kernel(query_ref, key_ref, value_ref, cosine_ref, sine_ref, meta_ref, segment_ref, out_ref, keys):
    tokens = key_ref.shape[0]
    keys[...] = turned(key_ref[...].astype(FLOAT), cosine_ref[...], sine_ref[...])
    for start in range(0, tokens, ATT_ROWS):
        extent = start + ATT_ROWS
        here = slice(start, extent)
        allowed = attention_mask(meta_ref, segment_ref, start, extent)
        for unit in range(query_ref.shape[1] // HEAD_SIZE):
            span = slice(unit * HEAD_SIZE, (unit + 1) * HEAD_SIZE)
            query = turned(query_ref[here, span].astype(FLOAT), cosine_ref[here], sine_ref[here])
            weights = probabilities(query, keys[:extent], allowed).astype(BFLOAT)
            out_ref[here, span] = dot(weights, value_ref[:extent], (1, 0)).astype(BFLOAT)


def attention_backward_kernel(
    query_ref, key_ref, value_ref, cosine_ref, sine_ref, meta_ref, segment_ref, grad_ref,
    query_grad_ref, shared_grad_ref, keys, key_sum, value_sum,
):
    tokens = key_ref.shape[0]
    scale = 1.0 / math.sqrt(HEAD_SIZE)
    keys[...] = turned(key_ref[...].astype(FLOAT), cosine_ref[...], sine_ref[...])
    key_sum[...] = jnp.zeros_like(key_sum)
    value_sum[...] = jnp.zeros_like(value_sum)
    for start in range(0, tokens, ATT_ROWS):
        extent = start + ATT_ROWS
        here = slice(start, extent)
        allowed = attention_mask(meta_ref, segment_ref, start, extent)
        for unit in range(query_ref.shape[1] // HEAD_SIZE):
            span = slice(unit * HEAD_SIZE, (unit + 1) * HEAD_SIZE)
            query = turned(query_ref[here, span].astype(FLOAT), cosine_ref[here], sine_ref[here])
            weights = probabilities(query, keys[:extent], allowed)
            grad = grad_ref[here, span]
            weights_grad = dot(grad, value_ref[:extent], (1, 1))
            value_sum[:extent] += dot(weights.astype(BFLOAT), grad, (0, 0))
            mean_grad = jnp.sum(weights * weights_grad, axis=1, keepdims=True)
            score_grad = (weights * (weights_grad - mean_grad) * scale).astype(BFLOAT)
            query_grad = dot(score_grad, keys[:extent], (1, 0))
            key_sum[:extent] += dot(score_grad, query, (0, 0))
            query_grad_ref[here, span] = turned_back(query_grad, cosine_ref[here], sine_ref[here]).astype(BFLOAT)
    shared_grad_ref[:, :HEAD_SIZE] = turned_back(key_sum[...], cosine_ref[...], sine_ref[...]).astype(BFLOAT)
    shared_grad_ref[:, HEAD_SIZE:] = value_sum[...].astype(BFLOAT)


def attention_cost(tokens, width, factor):
    return estimate(
        flops=factor * 2 * tokens * tokens * width,
        bytes_accessed=factor * tokens * width * 8,
        transcendentals=tokens * tokens * width // (2 * HEAD_SIZE),
    )


def attention_specs(tokens, channels):
    width = channels * QUERY_HEADS // DSSM * HEAD_SIZE
    narrow = whole((tokens, HEAD_SIZE))
    return [
        pl.BlockSpec((tokens, width), lambda *_: (0, (STATES + PAIR + 2 * channels) // width)),
        pl.BlockSpec((tokens, HEAD_SIZE), lambda *_: (0, STATES // HEAD_SIZE)),
        pl.BlockSpec((tokens, HEAD_SIZE), lambda *_: (0, STATES // HEAD_SIZE + 1)),
        narrow,
        narrow,
        whole((tokens, LANES)),
        whole((8, tokens)),
    ]


def attention_operands(projected, tables):
    return [projected] * 3 + [tables[name] for name in ("cosine", "sine", "meta", "segment_row")]


def attention_forward(projected, tables):
    tokens = projected.shape[0]
    channels = tables["taps"].shape[1]
    width = channels * QUERY_HEADS // DSSM * HEAD_SIZE
    return pl.pallas_call(
        attention_forward_kernel,
        grid=(1,),
        in_specs=attention_specs(tokens, channels),
        out_specs=pl.BlockSpec((tokens, width), lambda *_: (0, channels // width)),
        out_shape=jax.ShapeDtypeStruct((tokens, channels + width), BFLOAT),
        scratch_shapes=[pltpu.VMEM((tokens, HEAD_SIZE), BFLOAT)],
        compiler_params=pltpu.CompilerParams(vmem_limit_bytes=SCAN_BYTES),
        cost_estimate=attention_cost(tokens, width, 1),
        name="attention_forward",
    )(*attention_operands(projected, tables))


def attention_backward(projected, tables, mixed_grad):
    tokens = projected.shape[0]
    channels = tables["taps"].shape[1]
    width = channels * QUERY_HEADS // DSSM * HEAD_SIZE
    return pl.pallas_call(
        attention_backward_kernel,
        grid=(1,),
        in_specs=attention_specs(tokens, channels)
        + [pl.BlockSpec((tokens, width), lambda *_: (0, channels // width))],
        out_specs=[whole((tokens, width)), whole((tokens, PAIR))],
        out_shape=[jax.ShapeDtypeStruct((tokens, width), BFLOAT), jax.ShapeDtypeStruct((tokens, PAIR), BFLOAT)],
        scratch_shapes=[
            pltpu.VMEM((tokens, HEAD_SIZE), BFLOAT),
            pltpu.VMEM((tokens, HEAD_SIZE), FLOAT),
            pltpu.VMEM((tokens, HEAD_SIZE), FLOAT),
        ],
        compiler_params=pltpu.CompilerParams(vmem_limit_bytes=SCAN_BYTES),
        cost_estimate=attention_cost(tokens, width, 3),
        name="attention_backward",
    )(*attention_operands(projected, tables), mixed_grad)


def mixer_tables(lengths, segment, position, conv_values, conv_states, scan_params):
    tokens = segment.shape[0]
    block = jnp.arange(tokens, dtype=jnp.int32) // SSD_BLOCK
    previous = jnp.concatenate([jnp.full((1,), -1, jnp.int32), segment[:-1]])
    first_previous = jnp.repeat(previous[::SSD_BLOCK], SSD_BLOCK)
    last_segment = jnp.repeat(segment[SSD_BLOCK - 1 :: SSD_BLOCK], SSD_BLOCK)
    length = jnp.sum(
        jnp.where(segment[:, None] == jnp.arange(lengths.shape[0], dtype=jnp.int32)[None, :], lengths[None, :], 0),
        axis=1,
    )
    columns = [
        segment,
        position,
        length - 1 - position,
        segment == first_previous,
        segment == last_segment,
    ]
    meta = jnp.stack([column.astype(FLOAT) for column in columns], axis=1)
    half_width = HEAD_SIZE // 2
    frequency = ROPE_BASE ** (-2.0 * jnp.arange(half_width, dtype=FLOAT) / HEAD_SIZE)
    angle = position.astype(FLOAT)[:, None] * frequency[None, :]
    cosine, sine = jnp.cos(angle), jnp.sin(angle)
    heads = scan_params.shape[1]
    head = jnp.stack([scan_params[0], -jnp.exp(scan_params[1]), scan_params[2]])
    return dict(
        meta=jnp.pad(meta, ((0, 0), (0, LANES - meta.shape[1]))),
        segment_row=jnp.broadcast_to(segment.astype(FLOAT)[None, :], (8, tokens)),
        taps=jnp.pad(conv_values.astype(FLOAT), ((0, 3), (0, 0))),
        state_taps=jnp.pad(conv_states.astype(FLOAT), ((0, 3), (0, 0))),
        head=jnp.pad(head, ((0, 5), (0, LANES - heads))),
        skip=jnp.broadcast_to(jnp.repeat(scan_params[2], HP)[None, :], (8, heads * HP)),
        cosine=jnp.concatenate([cosine, cosine], axis=1),
        sine=jnp.concatenate([-sine, sine], axis=1),
    )


HALVES = 2
DENSE_TILE = 1024


def matrix_rows(values):
    return values.reshape(values.shape[0] * values.shape[1], values.shape[2])


def cut_tiles(width, tile):
    return [(low, min(low + tile, width)) for low in range(0, width, tile)]


def spread_kernel(masks, count, chosen_ref, *rest):
    halves, weights = rest[: 2 * len(masks)], rest[2 * len(masks) : 2 * len(masks) + count]
    out_ref, narrow_ref, out_tile, narrow, sems = rest[-5:]
    rows = halves[0].shape[0]
    shards = weights[0].shape[0]
    depth = shards // HALVES
    lower = weights[-1].shape[2] - LANES
    copies = []
    for at, mask in enumerate(masks):
        left_ref, right_ref = halves[2 * at : 2 * at + 2]
        here = pl.ds(pl.multiple_of((lax.axis_index("col") ^ mask) * rows, rows), rows)

        def through(ref, low, high):
            return dot(left_ref[...], matrix_rows(ref[:depth, :rows, low:high]), (1, 0)) + dot(
                right_ref[...], matrix_rows(ref[depth:, :rows, low:high]), (1, 0)
            )

        def send(tile, target):
            copies.append(pltpu.make_async_copy(tile, target, sems.at[len(copies)]))
            copies[-1].start()

        narrow[at] = (chosen_ref[here, :] * through(weights[-1], lower, lower + LANES)).astype(BFLOAT)
        send(narrow.at[at], narrow_ref.at[here, :])
        column = 0
        for ref in weights:
            for low, high in cut_tiles(ref.shape[2] - (LANES if ref is weights[-1] else 0), DENSE_TILE):
                span = slice(column, column + high - low)
                column += high - low
                raised = matrix_rows(ref[:, rows : rows + NADAPT * RANK // shards, low:high])
                out_tile[at, :, span] = (through(ref, low, high) + dot(narrow[at], raised, (1, 0))).astype(BFLOAT)
                send(out_tile.at[at, :, span], out_ref.at[here, span])
    for copy in copies:
        copy.wait()


def weights_width(gathered):
    return sum(part.shape[2] for part in gathered) - LANES


def spread_blocks(blocks, gathered, selector, held):
    masks = [mask for mask, _ in blocks]
    rows, half = blocks[0][1][0].shape
    width = weights_width(gathered)
    total = selector.shape[0]
    fast, free = pl.BlockSpec(memory_space=pltpu.VMEM), pl.BlockSpec(memory_space=pl.ANY)
    operands = [selector, *[part for _, halves in blocks for part in halves], *gathered]
    in_specs = [fast] * len(operands)
    aliases = {}
    if held is not None:
        aliases = {len(operands): 0, len(operands) + 1: 1}
        operands += list(held)
        in_specs += [free] * 2
    copies = len(masks) * (1 + sum(-(-part.shape[2] // DENSE_TILE) for part in gathered))
    return pl.pallas_call(
        functools.partial(spread_kernel, masks, len(gathered)),
        in_specs=in_specs,
        out_specs=[free] * 2,
        out_shape=[
            jax.ShapeDtypeStruct((total, width), BFLOAT),
            jax.ShapeDtypeStruct((total, LANES), BFLOAT),
        ],
        scratch_shapes=[
            pltpu.VMEM((len(masks), rows, width), BFLOAT),
            pltpu.VMEM((len(masks), rows, LANES), BFLOAT),
            pltpu.SemaphoreType.DMA((copies,)),
        ],
        input_output_aliases=aliases,
        compiler_params=pltpu.CompilerParams(vmem_limit_bytes=DENSE_BYTES),
        cost_estimate=estimate(
            flops=4 * len(masks) * rows * half * (width + LANES),
            bytes_accessed=2 * len(masks) * rows * (2 * half + width),
            transcendentals=0,
        ),
        name="spread_blocks",
    )(*operands)


def collect_kernel(masks, count, values_ref, *refs):
    weights, outs = refs[:count], refs[count:]
    if len(outs) > 2 * len(masks):
        inner_ref, *outs, raise_ref = outs
        raise_ref[...] = dot(inner_ref[...], values_ref[...], (0, 0)).astype(BFLOAT)
    rows = values_ref.shape[0] // 4
    shards = weights[0].shape[0]
    half = shards // HALVES * rows
    width = values_ref.shape[1]
    starts, column = [], 0
    for ref in weights:
        high = min(column + ref.shape[2], width)
        starts.append((column, high))
        column = high
    for at, mask in enumerate(masks):
        here = pl.ds(pl.multiple_of((lax.axis_index("col") ^ mask) * rows, rows), rows)
        first, second = outs[2 * at], outs[2 * at + 1]

        def through(cut):
            total = None
            for (low, high), ref in zip(starts, weights):
                part = dot(values_ref[here, low:high], cut(ref, high - low), (1, 1))
                total = part if total is None else total + part
            return total

        for shard in range(shards):
            out_ref = first if shard < shards // HALVES else second
            column = shard * rows % half
            out_ref[:, column : column + rows] = through(lambda ref, wide: ref[shard, :rows, :wide]).astype(
                out_ref.dtype
            )
        first[:, half:] = through(
            lambda ref, wide: matrix_rows(ref[:, rows : rows + NADAPT * RANK // shards, :wide])
        ).astype(first.dtype)


def collect_blocks(masks, values, gathered, types, inner=()):
    rows = values.shape[0] // 4
    half = gathered[0].shape[0] // HALVES * rows
    fast = pl.BlockSpec(memory_space=pltpu.VMEM)
    out_shape = []
    for pair in types:
        out_shape.append(jax.ShapeDtypeStruct((rows, half + LANES), pair[0]))
        out_shape.append(jax.ShapeDtypeStruct((rows, half), pair[1]))
    out_shape += [jax.ShapeDtypeStruct((LANES, values.shape[1]), BFLOAT) for _ in inner]
    outs = pl.pallas_call(
        functools.partial(collect_kernel, masks, len(gathered)),
        in_specs=[fast] * (1 + len(gathered) + len(inner)),
        out_specs=[fast] * len(out_shape),
        out_shape=out_shape,
        compiler_params=pltpu.CompilerParams(vmem_limit_bytes=DENSE_BYTES),
        cost_estimate=estimate(
            flops=4 * len(masks) * rows * half * values.shape[1],
            bytes_accessed=2 * len(masks) * rows * (values.shape[1] + 4 * half),
            transcendentals=0,
        ),
        name="collect_blocks",
    )(values, *gathered, *inner)
    return [tuple(outs[2 * at : 2 * at + 2]) for at in range(len(masks))] + list(outs[2 * len(masks) :])


def root_mean(values):
    return lax.rsqrt(jnp.mean(values * values, axis=1, keepdims=True) + EPSILON)


def packed_grad(narrow, values, choose):
    half = LANES // 2
    chosen = dot(narrow, choose, (1, 0)).astype(BFLOAT)
    grad = dot(chosen, values, (0, 0))
    low = lax.broadcasted_iota(jnp.int32, (8, LANES), 1) < half
    devices = []
    for start in range(0, grad.shape[1], LANES):
        own = grad[:, start : start + LANES]
        turned_own = pltpu.roll(own, half, 1)
        for first, second in ((own, turned_own), (turned_own, own)):
            devices.append(
                jnp.concatenate(
                    [jnp.where(low, first[at : at + 8], second[at + 8 : at + 16]) for at in (0, 16)], axis=1
                )
            )
    return jnp.concatenate(devices, axis=0).astype(BFLOAT)


def finish_kernel(kind, first_own, first_near, first_far, second_own, second_near, second_far, lower_ref, chosen_ref,
                  *refs):
    half = second_own.shape[1]
    model = HALVES * half
    wide = lambda ref: ref[...].astype(FLOAT)
    first = wide(first_own) + wide(first_near) + wide(first_far)
    second = wide(second_own) + wide(second_near) + wide(second_far)
    inner = (chosen_ref[...] * first[:, half:]).astype(BFLOAT)
    summed = jnp.concatenate([first[:, :half], second], axis=1) + dot(
        inner, matrix_rows(lower_ref[...]), (1, 1)
    )
    if kind == "output":
        residual_ref, place_ref, choose_ref, branch_ref, early_ref, out_ref = refs
        result = (residual_ref[...] + summed).astype(BFLOAT)
        out_ref[:, :model] = dot(place_ref[...], result, (0, 0)).astype(BFLOAT)
        out_ref[:, model : model + 2 * LANES] = packed_grad(inner, branch_ref[...], choose_ref[...])
        out_ref[:, model + 2 * LANES :] = early_ref[...]
        return
    if kind == "forward":
        residual_ref, gain_ref, out_ref, inner_ref, left_ref, right_ref = refs
        hidden = residual_ref[...] + summed
        normed = (hidden * root_mean(hidden) * gain_ref[0:1, :]).astype(BFLOAT)
    else:
        values_ref, upstream_ref, gain_ref, choose_ref, normed_left, normed_right = refs[:6]
        values = values_ref[...]
        scale = root_mean(values)
        weighted = summed * gain_ref[0:1, :]
        mean = jnp.mean(weighted * values, axis=1, keepdims=True)
        hidden = upstream_ref[...].astype(FLOAT) + scale * weighted - values * (scale * scale * scale * mean)
        normed = hidden.astype(BFLOAT)
        packed = packed_grad(
            inner, jnp.concatenate([normed_left[...], normed_right[...]], axis=1), choose_ref[...]
        )
        if kind == "input":
            place_ref, out_ref = refs[6:]
            out_ref[:, :model] = dot(place_ref[...], normed, (0, 0)).astype(BFLOAT)
            out_ref[:, model:] = packed
            return
        given_ref, out_ref, inner_ref, left_ref, right_ref, packed_ref = refs[6:]
        packed_ref[:, : 2 * LANES] = packed
        packed_ref[:, 2 * LANES :] = packed_grad(given_ref[...], normed, choose_ref[...])
    out_ref[...] = hidden
    inner_ref[...] = inner
    left_ref[...] = normed[:, :half]
    right_ref[...] = normed[:, half:]


def finish(kind, parts, gathered, own_selector, *operands):
    rows = own_selector.shape[0]
    half = parts[3].shape[1]
    shards = gathered[-1].shape[0]
    model = HALVES * half
    lower = gathered[-1][:, : model // shards, -LANES:]
    shaped = jax.ShapeDtypeStruct
    if kind in ("output", "input"):
        out_shape = shaped((rows, model + 2 * LANES * (3 if kind == "output" else 1)), BFLOAT)
        out_specs = whole(out_shape.shape)
    else:
        out_shape = [shaped((rows, model), FLOAT), shaped((rows, LANES), BFLOAT)]
        out_shape += [shaped((rows, half), BFLOAT)] * 2
        out_shape += [shaped((rows, 4 * LANES), BFLOAT)] * (kind == "backward")
        out_specs = [whole(shape.shape) for shape in out_shape]
    given = [*parts, lower, own_selector, *operands]
    return pl.pallas_call(
        functools.partial(finish_kernel, kind),
        grid=(1,),
        in_specs=[whole(value.shape) for value in given],
        out_specs=out_specs,
        out_shape=out_shape,
        compiler_params=pltpu.CompilerParams(vmem_limit_bytes=FINISH_BYTES),
        cost_estimate=estimate(
            flops=2 * rows * model * LANES, bytes_accessed=rows * model * 20, transcendentals=0
        ),
        name="finish_" + kind,
    )(*given)


def onward_kernel(first_kept, first_part, second_kept, second_part, first_ref, second_ref):
    first_ref[...] = (first_kept[...] + first_part[...].astype(FLOAT)).astype(BFLOAT)
    second_ref[...] = (second_kept[...] + second_part[...].astype(FLOAT)).astype(BFLOAT)


def sum_onward(first_kept, first_part, second_kept, second_part):
    return pl.pallas_call(
        onward_kernel,
        in_specs=[pl.BlockSpec(memory_space=pltpu.VMEM)] * 4,
        out_specs=[pl.BlockSpec(memory_space=pltpu.VMEM)] * 2,
        out_shape=[jax.ShapeDtypeStruct(part.shape, BFLOAT) for part in (first_part, second_part)],
        compiler_params=pltpu.CompilerParams(vmem_limit_bytes=DENSE_BYTES),
        name="sum_onward",
    )(first_kept, first_part, second_kept, second_part)


def send_kernel(target_column, target_row, tokens_ref, adapter_ref, sent_ref, matrix_ref):
    rows = tokens_ref.shape[0]
    model = tokens_ref.shape[1]
    peer = adapter_ref.shape[0]
    column, row = target_column[:, 0:1], target_row[0:1, :]
    earlier = lax.broadcasted_iota(jnp.int32, (rows, rows), 0) < lax.broadcasted_iota(jnp.int32, (rows, rows), 1)
    same = jnp.where((column // rows == row // rows) & earlier, 1.0, 0.0)
    place = (row // rows) * peer + jnp.sum(same, axis=0, keepdims=True).astype(jnp.int32)
    matrix = (lax.broadcasted_iota(jnp.int32, (rows, rows), 0) == place).astype(BFLOAT)
    matrix_ref[...] = matrix
    sent_ref[:, :model] = dot(matrix, tokens_ref[...], (1, 0)).astype(BFLOAT)
    lane = lax.broadcasted_iota(jnp.int32, (rows, LANES), 1)
    slots = jnp.where(lane == 0, column % rows, 0).astype(FLOAT).astype(BFLOAT)
    notes = dot(matrix, slots, (1, 0))
    sent_ref[:, model:] = jnp.where(lane == 0, notes, adapter_ref[0:1, :]).astype(BFLOAT)


def send_tokens(target, tokens, adapters, peer):
    rows, model = tokens.shape
    notes = jnp.pad(adapters.astype(FLOAT), (1, LANES - 1 - adapters.shape[0]))
    return pl.pallas_call(
        send_kernel,
        in_specs=[pl.BlockSpec(memory_space=pltpu.VMEM)] * 4,
        out_specs=[pl.BlockSpec(memory_space=pltpu.VMEM)] * 2,
        out_shape=[
            jax.ShapeDtypeStruct((rows, model + LANES), BFLOAT),
            jax.ShapeDtypeStruct((rows, rows), BFLOAT),
        ],
        compiler_params=pltpu.CompilerParams(vmem_limit_bytes=DENSE_BYTES),
        name="send_tokens",
    )(
        jnp.broadcast_to(target[:, None], (rows, LANES)),
        jnp.broadcast_to(target[None, :], (8, rows)),
        tokens,
        jnp.broadcast_to(notes[None, :], (peer, LANES)),
    )


def shards_kernel(given_ref, lower_ref, taps_ref, own_ref, shared_ref):
    half = LANES // 2
    given = given_ref[...].astype(FLOAT)
    tall, width = given.shape
    second = pltpu.roll(given, width - UNIT_IN, 1)
    gate = DSSM // QUERY_HEADS
    pair_at = 2 * gate + HEAD_SIZE
    start = 0
    for low, high in ((0, gate), (gate, 2 * gate), (2 * gate, pair_at)):
        for unit in (given, second):
            own_ref[:, start : start + high - low] = unit[:, low:high].astype(BFLOAT)
            start += high - low
    lane = lax.broadcasted_iota(jnp.int32, (tall, LANES), 1)
    heads = NH // QUERY_HEADS
    steps_at = pair_at + LANES
    other = pltpu.roll(second[:, steps_at : steps_at + LANES], heads, 1)
    steps = jnp.where(lane < heads, given[:, steps_at : steps_at + LANES], jnp.where(lane < 2 * heads, other, 0.0))
    own_ref[:, start : start + LANES] = steps.astype(BFLOAT)
    rows = lower_ref.shape[0]
    own_ref[:rows, start + LANES :] = lower_ref[...]
    own_ref[rows:, start + LANES :] = jnp.zeros((tall - rows, LANES), BFLOAT)
    first_tile, second_tile = given[:, pair_at:steps_at], second[:, pair_at:steps_at]
    shared_ref[:tall, :LANES] = jnp.where(lane < half, first_tile, pltpu.roll(second_tile, half, 1)).astype(BFLOAT)
    shared_ref[:tall, LANES:] = jnp.where(lane < half, pltpu.roll(first_tile, half, 1), second_tile).astype(BFLOAT)
    shared_ref[tall:, :LANES] = jnp.zeros(taps_ref.shape, BFLOAT)
    shared_ref[tall:, LANES:] = taps_ref[...]


def make_shards(given, lower, taps):
    tall = given.shape[0]
    own = 2 * (2 * DSSM // QUERY_HEADS + HEAD_SIZE) + 2 * LANES
    return pl.pallas_call(
        shards_kernel,
        in_specs=[pl.BlockSpec(memory_space=pltpu.VMEM)] * 3,
        out_specs=[pl.BlockSpec(memory_space=pltpu.VMEM)] * 2,
        out_shape=[
            jax.ShapeDtypeStruct((tall, own), BFLOAT),
            jax.ShapeDtypeStruct((tall + taps.shape[0], 2 * LANES), BFLOAT),
        ],
        compiler_params=pltpu.CompilerParams(vmem_limit_bytes=DENSE_BYTES),
        name="make_shards",
    )(given, lower, taps)


def arrive_kernel(arrived_ref, gain_ref, own_ref, matrix_ref, left_ref, right_ref):
    rows, model = own_ref.shape
    slots = arrived_ref[:, model:].astype(FLOAT).T[0:1, :]
    row = lax.broadcasted_iota(jnp.int32, (rows, rows), 0).astype(FLOAT)
    matrix = (row == slots).astype(BFLOAT)
    matrix_ref[...] = matrix
    own = dot(matrix, arrived_ref[:, :model], (1, 0))
    own_ref[...] = own
    normed = (own * root_mean(own) * gain_ref[0:1, :]).astype(BFLOAT)
    left_ref[...] = normed[:, : model // HALVES]
    right_ref[...] = normed[:, model // HALVES :]


def arrive_tokens(arrived, gain):
    rows, model = arrived.shape[0], arrived.shape[1] - LANES
    return pl.pallas_call(
        arrive_kernel,
        in_specs=[pl.BlockSpec(memory_space=pltpu.VMEM)] * 2,
        out_specs=[pl.BlockSpec(memory_space=pltpu.VMEM)] * 4,
        out_shape=[
            jax.ShapeDtypeStruct((rows, model), FLOAT),
            jax.ShapeDtypeStruct((rows, rows), BFLOAT),
            jax.ShapeDtypeStruct((rows, model // HALVES), BFLOAT),
            jax.ShapeDtypeStruct((rows, model // HALVES), BFLOAT),
        ],
        compiler_params=pltpu.CompilerParams(vmem_limit_bytes=DENSE_BYTES),
        name="arrive_tokens",
    )(arrived, gain)


GATE_WIDTH = DSSM // QUERY_HEADS
PAIR_WIDTH = 2 * KEY_VALUE_HEADS * HEAD_SIZE // QUERY_HEADS
STATE_WIDTH = 2 * NSTATE // QUERY_HEADS
STEP_WIDTH = NH // QUERY_HEADS
ALL_AXES = ("row", "col")


def pad_columns(values, width):
    return jnp.pad(values, ((0, 0), (0, width - values.shape[1])))


def after(values, *earlier):
    return lax.optimization_barrier((values, *earlier))[0]


def after_all(values, *earlier):
    return lax.optimization_barrier((*values, *earlier))[: len(values)]


def unit_parts(values, units):
    cuts = [0]
    for width in (GATE_WIDTH, GATE_WIDTH, HEAD_SIZE, PAIR_WIDTH, STATE_WIDTH, STEP_WIDTH):
        cuts.append(cuts[-1] + width)
    return [
        jnp.concatenate(
            [values[:, unit * UNIT_IN + low : unit * UNIT_IN + high] for unit in range(units)], axis=1
        )
        for low, high in zip(cuts[:-1], cuts[1:])
    ]


def restore_units(parts, units):
    ordered = []
    for unit in range(units):
        for part in parts:
            width = part.shape[1] // units
            ordered.append(part[:, unit * width : (unit + 1) * width])
    return jnp.concatenate(ordered, axis=1)


def split_halves(values, units, first, axis):
    block = values.shape[axis] // units
    take = lambda low, high: lax.slice_in_dim(values, low, high, axis=axis)
    parts = [take(unit * block, unit * block + first) for unit in range(units)]
    parts += [take(unit * block + first, (unit + 1) * block) for unit in range(units)]
    return jnp.concatenate(parts, axis=axis)


def join_halves(values, units, first, axis):
    block = values.shape[axis] // units
    rest = block - first
    take = lambda low, high: lax.slice_in_dim(values, low, high, axis=axis)
    parts = []
    for unit in range(units):
        parts.append(take(unit * first, (unit + 1) * first))
        parts.append(take(units * first + unit * rest, units * first + (unit + 1) * rest))
    return jnp.concatenate(parts, axis=axis)


def quick(rows):
    return lax.axis_size("col") == 4 and lax.axis_size("row") == 8 and rows == 256


def spread_early(halves, gathered, selector):
    left, right = halves
    far_left, near_right = flip(left, 2), flip(right, 1)
    near_left, far_right = flip(left, 1), flip(right, 2)
    held = spread_blocks([(0, halves)], gathered, selector, None)
    onward_left, onward_right = after_all((far_left, near_right), held[1])
    corner = flip(onward_left, 1), flip(onward_right, 2)
    held = spread_blocks([(1, (near_left, near_right))], gathered, selector, held)
    held = spread_blocks([(2, (far_left, far_right))], gathered, selector, held)
    return spread_blocks([(3, corner)], gathered, selector, held)


def flip(values, mask):
    return lax.ppermute(values, "col", [(i, i ^ mask) for i in range(4)])


def gather_blocks(halves):
    left, right = halves
    far_left, near_right = flip(left, 2), flip(right, 1)
    near_left, far_right = flip(left, 1), flip(right, 2)
    corner_left, corner_right = flip(far_left, 1), flip(near_right, 2)
    return [
        (0, (left, right)),
        (1, (near_left, near_right)),
        (2, (far_left, far_right)),
        (3, (corner_left, corner_right)),
    ]


def rows_of(values, block, rows):
    return lax.dynamic_slice_in_dim(values, block * rows, rows, 0)


def spread_gathered(blocks, gathered, selector):
    held = None
    for block in blocks:
        held = spread_blocks([block], gathered, selector, held)
    return held


def spread_project(halves, gathered, selector):
    rows = halves[0].shape[0]
    if quick(rows):
        return spread_gathered(gather_blocks(halves), gathered, selector)
    wide, narrow_factor = gathered
    width = narrow_factor.shape[1]
    both = product(lax.all_gather(jnp.concatenate(halves, axis=1), "col", axis=0, tiled=True), wide)
    narrow = (selector * both[:, width:]).astype(BFLOAT)
    return (both[:, :width] + product(narrow, narrow_factor)).astype(BFLOAT), narrow


PIECE_TYPES = [(BFLOAT, BFLOAT), (BFLOAT, FLOAT), (FLOAT, BFLOAT), (FLOAT, FLOAT)]


def collect_pieces(values, gathered, at_once):
    if at_once:
        return collect_blocks([3, 1, 2, 0], values, gathered, PIECE_TYPES)
    (corner,) = collect_blocks([3], values, gathered, PIECE_TYPES[:1])
    values = after(values, corner[0])
    return [corner, *collect_blocks([1, 2, 0], values, gathered, PIECE_TYPES[1:])]


def collect_send(pieces, ordered=True):
    corner, near, far, own = pieces
    arriving = flip(corner[0], 1), flip(corner[1], 2)
    sent_near, sent_far = after_all((near[0], far[1]), *arriving) if ordered else (near[0], far[1])
    return own, flip(sent_near, 1), flip(sent_far, 2), far[0], near[1], arriving


def collect_middle(started):
    own, near_first, far_second, far_first, near_second, arriving = started
    return (own, near_first, far_second), sum_onward(far_first, arriving[0], near_second, arriving[1])


def collect_onward(onward):
    return flip(onward[0], 2), flip(onward[1], 1)


def collect_end(kept, last, kind, gathered, own_selector, *operands):
    own, near_first, far_second = kept
    parts = [own[0], near_first, last[0], own[1], far_second, last[1]]
    return finish(kind, parts, gathered, own_selector, *operands)


def collect_project(values, gathered, kind, own_selector, *operands):
    rows, model = own_selector.shape[0], operands[0].shape[1]
    if quick(rows):
        kept, onward = collect_middle(collect_send(collect_pieces(values, gathered, False)))
        return collect_end(kept, collect_onward(onward), kind, gathered, own_selector, *operands)
    wide, narrow_factor = gathered
    width = narrow_factor.shape[1]
    partial = jnp.concatenate(
        [contract_last(values, wide[:, :width]), contract_last(values, narrow_factor)], axis=1
    ).astype(BFLOAT)
    summed = lax.psum_scatter(partial, "col", scatter_dimension=0, tiled=True).astype(FLOAT)
    inner = (own_selector * summed[:, model:]).astype(BFLOAT)
    summed = summed[:, :model] + contract_last(inner, wide[:, width:])
    if kind == "output":
        return (operands[0] + summed).astype(BFLOAT), inner
    if kind == "forward":
        residual, gain = operands
        hidden = residual + summed
        return hidden, inner, *cut_halves(rms_norm(hidden, gain[0]).astype(BFLOAT))
    values, upstream, gain = operands
    _, back = jax.vjp(lambda given: rms_norm(given, gain[0]), values)
    hidden = upstream.astype(FLOAT) + back(summed)[0]
    if kind == "input":
        return hidden.astype(BFLOAT), inner
    return hidden, inner, *cut_halves(hidden.astype(BFLOAT))


def cut_halves(values):
    half = values.shape[1] // HALVES
    return values[:, :half], values[:, half:]


def local(
    tokens_in,
    cotangent,
    target,
    sequence_lengths,
    sequence_adapter,
    norm_gains,
    weight_in,
    conv_values,
    conv_states,
    scan_params,
    weight_mix,
    weight_feed,
    weight_down,
    in_lower,
    in_raise,
    mix_lower,
    mix_raise,
    feed_lower,
    feed_raise,
    down_lower,
    down_raise,
):
    cols = lax.axis_size("col")
    rows_axis = lax.axis_size("row")
    col = lax.axis_index("col")
    devices = cols * rows_axis
    rows = tokens_in.shape[0]
    model = tokens_in.shape[1]
    total = rows * cols
    units = QUERY_HEADS // cols
    channels = units * GATE_WIDTH
    peer = rows // devices
    lengths, adapters = sequence_lengths[0], sequence_adapter[0]
    sequences = lengths.shape[0]
    fast = quick(rows)
    key_head = col * units // (QUERY_HEADS // KEY_VALUE_HEADS)
    exchange = lambda values: lax.all_to_all(values, ALL_AXES, split_axis=0, concat_axis=0, tiled=True)

    sent, send_matrix = send_tokens(target, tokens_in, adapters, peer)
    shards = []

    def gather_weight(weight, lower, raised):
        top = jnp.concatenate([weight, lower], axis=1)
        if fast:
            bottom = pad_columns(raised, top.shape[1])
            shards.append(jnp.concatenate([top, bottom], axis=0))
            return (lax.all_gather(shards[-1], "row", axis=0),)
        wide = lax.all_gather(top, "row", axis=0, tiled=True)
        return wide, lax.all_gather(raised, "row", axis=0, tiled=True)

    depth = weight_in.shape[0]
    height = depth + in_raise.shape[0]
    given = after(jnp.concatenate([weight_in, in_raise], axis=0), send_matrix)
    pair_width, state_width = units * PAIR_WIDTH, units * STATE_WIDTH
    taps = jnp.pad(conv_states, ((0, 16 - KCONV - 1), (0, 0)))
    if fast:
        full = -(-given.shape[1] // LANES) * LANES
        own_shard, shared_shard = make_shards(pad_columns(given, full), in_lower, taps)
        shared = lax.all_gather(shared_shard, "row", axis=0)
        shards.append(own_shard)
        weights_own = (lax.all_gather(own_shard, "row", axis=0),)
    else:
        gates, convs, queries, pairs, states, steps = unit_parts(given, units)
        taps = jnp.concatenate([jnp.zeros((taps.shape[0], pair_width), BFLOAT), taps], axis=1)
        shared = jnp.concatenate([jnp.concatenate([pairs, states], axis=1), taps], axis=0)
        own_columns = jnp.concatenate([gates, convs, queries, pad_columns(steps, LANES)], axis=1)
    arrived = exchange(after(sent, shared) if fast else sent)
    gains = jnp.broadcast_to(norm_gains.astype(FLOAT)[:, None, :], (2, 8, model))
    if fast:
        near, far = flip(shared, 1), flip(shared, 2)
        arrived = after(arrived, near, far, shards[0])
    own_input, place_matrix, *normed_one = arrive_tokens(arrived.reshape(rows, model + LANES), gains[0])
    blocks_one = gather_blocks(normed_one) if fast else normed_one
    if fast:
        held = jnp.zeros((cols,) + shared.shape, BFLOAT)
        for block, values in ((col, shared), (col ^ 1, near), (col ^ 2, far)):
            held = lax.dynamic_update_index_in_dim(held, values, block, 0)
        split = shared.shape[0] // 2
        corner = jnp.concatenate([flip(near[:split], 2), flip(far[split:], 1)], axis=0)
        held = lax.dynamic_update_index_in_dim(held, corner, col ^ 3, 0)
    else:
        held = lax.all_gather(shared, "col", axis=0)
    all_pairs = jnp.concatenate([held[at, ..., :height, :pair_width] for at in range(cols)], axis=-1)
    pick = lambda start: lax.select_n(
        key_head,
        *[all_pairs[..., start + at * HEAD_SIZE : start + (at + 1) * HEAD_SIZE] for at in range(KEY_VALUE_HEADS)],
    )
    shared_columns = jnp.concatenate(
        [held[at, ..., :height, pair_width:] for at in range(cols)]
        + [pick(0), pick(KEY_VALUE_HEADS * HEAD_SIZE)],
        axis=-1,
    )
    tap_rows = held[:, 0] if fast else held
    all_taps = jnp.concatenate(
        [tap_rows[at, height : height + KCONV + 1, pair_width:] for at in range(cols)], axis=1
    )
    if fast:
        weights_in = (shared_columns, *weights_own)
    else:
        columns = jnp.concatenate([shared_columns, own_columns], axis=1)
        weights_in = gather_weight(columns[:depth], in_lower, columns[depth:])
    weights_mix = gather_weight(
        after(split_halves(weight_mix, units, GATE_WIDTH, 0).T, sent),
        mix_raise.T,
        split_halves(mix_lower, units, GATE_WIDTH, 0).T,
    )
    weights_feed = gather_weight(
        after(split_halves(weight_feed, units, UNIT_FF, 1), arrived),
        feed_lower,
        split_halves(feed_raise, units, UNIT_FF, 1),
    )

    source_adapters = arrived.reshape(rows, model + LANES)[::peer, model + 1 : model + 1 + sequences].astype(jnp.int32)
    segment, position, selector = sequence_tables(lengths, adapters, total)
    own_selector = rows_of(selector, col, rows)
    own_segment = rows_of(segment, col, rows)
    tables = mixer_tables(lengths, segment, position, conv_values, all_taps, scan_params)

    def compact_grad(narrow, values):
        parts = [
            lax.dynamic_slice_in_dim(narrow, adapters[at] * RANK, RANK, 1)
            * (own_segment == at).astype(BFLOAT)[:, None]
            for at in range(sequences)
        ]
        grad = contract_first(jnp.concatenate(parts, axis=1), values).astype(BFLOAT)
        kept = sequences * RANK
        grad = grad.reshape(kept, devices, model // devices).transpose(1, 0, 2)
        return grad.reshape(devices, peer, kept * model // devices // peer)

    def expand_grad(dealt):
        kept = sequences * RANK
        dealt = dealt.reshape(devices * kept, model // devices)
        adapter_row = (source_adapters[:, :, None] * RANK + jnp.arange(RANK, dtype=jnp.int32)).reshape(-1)
        chosen = (jnp.arange(NADAPT * RANK, dtype=jnp.int32)[:, None] == adapter_row[None, :]).astype(BFLOAT)
        return product(chosen, dealt)

    def send_back(values, grads):
        back = contract_first(place_matrix, values).astype(BFLOAT).reshape(devices, peer, model)
        return exchange(jnp.concatenate([back, *grads], axis=2))

    def expand_packed(dealt, count):
        slots = dealt.shape[0] * peer
        block = jnp.arange(2 * LANES // (model // devices), dtype=jnp.int32)[:, None, None]
        row = jnp.arange(peer, dtype=jnp.int32)[None, None, :]
        place = block * peer + row
        adapter = jnp.where(place < RANK, source_adapters[None, :, 0:1], source_adapters[None, :, 1:2])
        adapter_row = (adapter * RANK + place % RANK).reshape(block.shape[0], 1, slots)
        chosen = (jnp.arange(NADAPT * RANK, dtype=jnp.int32)[None, :, None] == adapter_row).astype(BFLOAT)
        sums = product(chosen.reshape(-1, slots), dealt.reshape(slots, dealt.shape[2]))
        sums = sums.reshape(block.shape[0], NADAPT * RANK, dealt.shape[2])
        width = model // devices
        return [
            sum(
                sums[at, :, grad * 2 * LANES + at * width : grad * 2 * LANES + (at + 1) * width]
                for at in range(block.shape[0])
            )
            for grad in range(count)
        ]

    def take_back(dealt, count):
        returned = contract_first(send_matrix, dealt[:, :, :model].reshape(rows, model)).astype(BFLOAT)
        if fast:
            return returned, expand_packed(dealt[:, :, model:], count)
        width = (dealt.shape[2] - model) // count
        return returned, [
            expand_grad(dealt[:, :, model + at * width : model + (at + 1) * width]) for at in range(count)
        ]

    projected, inner_in = (spread_gathered if fast else spread_project)(blocks_one, weights_in, selector)

    sent_grad = product(send_matrix, cotangent).astype(BFLOAT).reshape(devices, peer, model)
    arrived_grad = exchange(after(sent_grad, normed_one[0])).reshape(rows, model)
    branch_two = product(place_matrix, arrived_grad).astype(BFLOAT)
    weights_down = gather_weight(after(weight_down.T, projected), down_raise.T, down_lower.T)

    mixed_out = attention_forward(projected, tables)
    mixed_out, scanned, carried = scan_forward(projected, tables, mixed_out)
    hidden, inner_out, *normed_two = collect_project(mixed_out, weights_mix, "forward", own_selector, own_input, gains[1])
    gate_up, inner_feed = spread_project(normed_two, weights_feed, selector)
    branch_halves = cut_halves(after(branch_two, projected))
    if fast:
        act_grad, narrow_two = spread_blocks(gather_blocks(branch_halves), weights_down, selector, None)
    else:
        act_grad, narrow_two = spread_project(branch_halves, weights_down, selector)
    half_feed = units * UNIT_FF
    gate_part, up_part = gate_up[:, :half_feed].astype(FLOAT), gate_up[:, half_feed:].astype(FLOAT)
    gate = jax.nn.sigmoid(gate_part)
    silu = gate_part * gate
    activated = (silu * up_part).astype(BFLOAT)
    wide_grad = act_grad.astype(FLOAT)
    feed_grad = jnp.concatenate(
        [wide_grad * up_part * (gate * (1.0 + gate_part * (1.0 - gate))), wide_grad * silu], axis=1
    ).astype(BFLOAT)
    choose = (
        jnp.arange(NADAPT * RANK, dtype=jnp.int32)[:, None]
        == (adapters[:, None] * RANK + jnp.arange(RANK, dtype=jnp.int32)[None, :]).reshape(1, -1)
    ).astype(BFLOAT)
    if fast:
        pieces = collect_pieces(after(activated, feed_grad), weights_down, True)
        kept, onward = collect_middle(collect_send(collect_pieces(feed_grad, weights_feed, False)))
        hidden_grad, narrow_three, left, right, early_grads = collect_end(
            kept,
            collect_onward(onward),
            "backward",
            weights_feed,
            own_selector,
            after(hidden, pieces[3][0]),
            branch_two,
            gains[1],
            choose,
            *normed_two,
            inner_out,
        )
        mixed_grad, narrow_one = spread_early((left, right), weights_mix, selector)
    else:
        hidden_grad, narrow_three, *branch_one = collect_project(
            feed_grad, weights_feed, "backward", own_selector, hidden, branch_two, gains[1]
        )
        mixed_grad, narrow_one = spread_project(branch_one, weights_mix, selector)

    if fast:
        near_parts = after_all((*pieces[0], pieces[1][0], pieces[2][1]), mixed_grad)
        started = collect_send(
            [near_parts[:2], (near_parts[2], pieces[1][1]), (pieces[2][0], near_parts[3]), pieces[3]], False
        )
        attended_grads = attention_backward(projected, tables, after(mixed_grad, near_parts[0]))
        kept, onward = collect_middle((*started[:5], after_all(started[5], attended_grads[1])))
        scan_inputs = (projected, tables, scanned, carried, after(mixed_grad, *onward), attended_grads)
        scan_part = list(scan_backward(*scan_inputs, 0, 2, None))
        payload = collect_end(
            kept,
            collect_onward(onward),
            "output",
            weights_down,
            own_selector,
            after(hidden, scan_part[2]),
            place_matrix,
            choose,
            branch_two,
            early_grads,
        )
        dealt_out = exchange(payload.reshape(devices, peer, -1))
        scan_part[2] = after(scan_part[2], payload)
        projected_grad = scan_backward(*scan_inputs, 1, 2, scan_part)[0]
        *pieces_in, raise_grad = collect_blocks([3, 1, 2, 0], projected_grad, weights_in, PIECE_TYPES, [inner_in])
        started_in = collect_send(pieces_in)
        kept_in, onward_in = collect_middle(started_in)
    else:
        block_out, inner_down = collect_project(activated, weights_down, "output", own_selector, hidden)
        attended_grads = attention_backward(projected, tables, mixed_grad)
        projected_grad = scan_backward(
            projected, tables, scanned, carried, mixed_grad, attended_grads, 0, 1, None
        )[0]
        dealt_out = send_back(
            block_out,
            [
                compact_grad(inner_down, branch_two),
                compact_grad(narrow_three, jnp.concatenate(normed_two, axis=1)),
                compact_grad(inner_out, jnp.concatenate(branch_one, axis=1)),
            ],
        )

    def sum_rows(values):
        return lax.psum_scatter(values.astype(BFLOAT), "row", scatter_dimension=0, tiled=True).astype(FLOAT)

    early_parts = [
        contract_first(narrow_one, mixed_out),
        contract_first(inner_feed, feed_grad),
        contract_first(narrow_two, activated),
    ]
    early = sum_rows(jnp.concatenate(early_parts, axis=1))

    late = sum_rows(raise_grad if fast else contract_first(inner_in, projected_grad))

    if fast:
        payload = collect_end(
            kept_in,
            collect_onward(onward_in),
            "input",
            weights_in,
            own_selector,
            own_input,
            after(hidden_grad, dealt_out),
            gains[0],
            choose,
            *normed_one,
            place_matrix,
        )
        dealt_grad = exchange(payload.reshape(devices, peer, -1))
    else:
        input_grad, narrow_four = collect_project(
            projected_grad, weights_in, "input", own_selector, own_input, hidden_grad, gains[0]
        )
        dealt_grad = send_back(input_grad, [compact_grad(narrow_four, jnp.concatenate(normed_one, axis=1))])
        payload = input_grad
    dealt_out, early, late = after_all((dealt_out, early, late), payload)
    early_cuts = [0, early_parts[0].shape[1]]
    early_cuts.append(early_cuts[1] + early_parts[1].shape[1])
    grad_mix_lower = join_halves(early[:, : early_cuts[1]], units, GATE_WIDTH, 1).T
    grad_feed_raise = join_halves(early[:, early_cuts[1] : early_cuts[2]], units, UNIT_FF, 1)
    grad_down_lower = early[:, early_cuts[2] :].T

    key_columns = late[:, STATES : STATES + HEAD_SIZE]
    value_columns = late[:, STATES + HEAD_SIZE : STATES + PAIR]
    mine = [(key_head == at).astype(FLOAT) for at in range(KEY_VALUE_HEADS)]
    pair_grad = jnp.concatenate([part * here for part in (key_columns, value_columns) for here in mine], axis=1)
    stacked = jnp.stack(
        [
            jnp.concatenate(
                [
                    pair_grad[:, at * pair_width : (at + 1) * pair_width],
                    late[:, at * state_width : (at + 1) * state_width],
                ],
                axis=1,
            )
            for at in range(cols)
        ]
    )
    if fast:
        piece = lambda mask: lax.dynamic_index_in_dim(stacked, col ^ mask, 0, False)
        shared_sum = piece(0) + flip(piece(1), 1) + flip(piece(2), 2) + flip(piece(3), 3)
    else:
        shared_sum = lax.psum_scatter(
            stacked.reshape(stacked.shape[0] * stacked.shape[1], -1), "col", scatter_dimension=0, tiled=True
        )
    late = jnp.concatenate([shared_sum, late[:, STATES + PAIR :]], axis=1)
    shared_width = pair_width + state_width
    cuts = [shared_width]
    for width in (channels, channels, units * HEAD_SIZE, units * STEP_WIDTH):
        cuts.append(cuts[-1] + width)
    gate_columns, conv_columns, query_columns, step_columns = [
        late[:, low:high] for low, high in zip(cuts[:-1], cuts[1:])
    ]
    grad_in_raise = restore_units(
        [
            gate_columns,
            conv_columns,
            query_columns,
            late[:, :pair_width],
            late[:, pair_width:shared_width],
            step_columns,
        ],
        units,
    )

    returned_out, (grad_down_raise, grad_feed_lower, grad_mix_raise) = take_back(dealt_out, 3)
    returned_grad, (grad_in_lower,) = take_back(dealt_grad, 1)
    return (
        returned_out,
        returned_grad,
        grad_in_lower.T,
        grad_in_raise,
        grad_mix_lower,
        grad_mix_raise,
        grad_feed_lower.T,
        grad_feed_raise,
        grad_down_lower,
        grad_down_raise,
    )


def solution(mesh):
    in_specs = (
        P(("row", "col"), None),
        P(("row", "col"), None),
        P(("row", "col")),
        P("row", None),
        P("row", None),
        P(),
        P("row", "col"),
        P(None, "col"),
        P(None, "col"),
        P(None, "col"),
        P("col", "row"),
        P("row", "col"),
        P("col", "row"),
        P("row", None),
        P("row", "col"),
        P("col", "row"),
        P(None, "row"),
        P("row", None),
        P("row", "col"),
        P("col", "row"),
        P(None, "row"),
    )
    out_specs = (
        P(("row", "col"), None),
        P(("row", "col"), None),
        P(("row", "col"), None),
        P("row", "col"),
        P("col", "row"),
        P(None, ("row", "col")),
        P(("row", "col"), None),
        P("row", "col"),
        P("col", "row"),
        P(None, ("row", "col")),
    )
    return jax.shard_map(local, mesh=mesh, in_specs=in_specs, out_specs=out_specs, check_vma=False)
```

```python
import functools
import math

import jax
import jax.numpy as jnp
from jax import lax
from jax.experimental import pallas as pl
from jax.experimental.pallas import tpu as pltpu
from jax.sharding import PartitionSpec as P

NH = 48
HP = 64
NSTATE = 256
KCONV = 4
QUERY_HEADS = 8
KEY_VALUE_HEADS = 2
HEAD_SIZE = 128
RANK = 16
NADAPT = 8
SSD_BLOCK = 256
DSSM = 3072
UNIT_IN = 1030
UNIT_FF = 512


EPSILON = 1e-05
ROPE_BASE = 10000.0
NEGATIVE = -1e30
FLOAT = jnp.float32
BFLOAT = jnp.bfloat16


def product(left, right):
    return jnp.dot(left, right, preferred_element_type=FLOAT)


def contract_last(left, right):
    return lax.dot_general(left, right, (((1,), (1,)), ((), ())), preferred_element_type=FLOAT)


def contract_first(left, right):
    return lax.dot_general(left, right, (((0,), (0,)), ((), ())), preferred_element_type=FLOAT)


def rms_norm(values, gain):
    return values * lax.rsqrt(jnp.mean(values * values, axis=-1, keepdims=True) + EPSILON) * gain


def sequence_tables(lengths, adapters, sequence_length):
    sequence_count = lengths.shape[0]
    boundary = jnp.cumsum(lengths)
    token_index = jnp.arange(sequence_length, dtype=jnp.int32)
    passed = (token_index[:, None] >= boundary[None, :]).astype(jnp.int32)
    segment = jnp.sum(passed, axis=1)
    segment_start = jnp.sum(passed * lengths[None, :], axis=1)
    position = token_index - segment_start
    member = (segment[:, None] == jnp.arange(sequence_count, dtype=jnp.int32)[None, :]).astype(
        jnp.int32
    )
    chosen = jnp.sum(member * adapters[None, :], axis=1)
    column = jnp.arange(NADAPT * RANK, dtype=jnp.int32) // RANK
    selector = (chosen[:, None] == column[None, :]).astype(FLOAT)
    return (segment, position, selector)


ESTIMATE = 16
SCAN_BYTES = 32 * 1024 * 1024
ALONE_BYTES = 44 * 1024 * 1024
DENSE_BYTES = 16 * 1024 * 1024
FINISH_BYTES = 32 * 1024 * 1024
LANES = 128


def whole(shape):
    return pl.BlockSpec(shape, lambda *_: (0,) * len(shape))


def estimate(flops, bytes_accessed, transcendentals):
    return pl.CostEstimate(
        flops=flops // ESTIMATE,
        bytes_accessed=bytes_accessed // ESTIMATE,
        transcendentals=transcendentals // ESTIMATE,
    )


def dot(left, right, contract):
    return lax.dot_general(left, right, ((contract[:1], contract[1:]), ((), ())), preferred_element_type=FLOAT)


def parts_of(values, count):
    parts = []
    for _ in range(count):
        part = values.astype(BFLOAT)
        parts.append(part)
        values = values - part.astype(FLOAT)
    return parts


def running_sum(values, triangle, contract):
    width = values.shape[1]
    split = dot(triangle, jnp.concatenate(parts_of(values, 3), axis=1), contract)
    return split[:, :width] + split[:, width : 2 * width] + split[:, 2 * width :]


def head_spread(values, expand):
    return dot(jnp.concatenate(parts_of(values, 2), axis=1), expand, (1, 0))


def head_sum(values, expand):
    high, low = parts_of(values, 2)
    single = expand[:LANES]
    return dot(high, single, (1, 1)) + dot(low, single, (1, 1))


def silu_parts(values):
    gate = 1.0 / (1.0 + jnp.exp(-values))
    return values * gate, gate


def expand_table(channels):
    row = lax.broadcasted_iota(jnp.int32, (2 * LANES, channels), 0) % LANES
    channel = lax.broadcasted_iota(jnp.int32, (2 * LANES, channels), 1) // HP
    return (row == channel).astype(BFLOAT)


def conv_sum(current_ref, before_ref, taps_ref, meta):
    rows = SSD_BLOCK
    current = current_ref[...].astype(FLOAT)
    window = jnp.concatenate([before_ref[...].astype(FLOAT)[8:16], current], axis=0)
    summed = taps_ref[KCONV : KCONV + 1, :] + current * taps_ref[0:1, :]
    for lag in range(1, KCONV):
        shifted = window[8 - lag : 8 - lag + rows]
        summed = summed + jnp.where(meta[:, 1:2] >= lag, shifted, 0.0) * taps_ref[lag : lag + 1, :]
    return summed


def conv_back(summed_grad, later, taps_ref, meta):
    rows = SSD_BLOCK
    window = jnp.concatenate([summed_grad, later[...]], axis=0)
    grad = summed_grad * taps_ref[0:1, :]
    for lag in range(1, KCONV):
        grad = grad + jnp.where(meta[:, 2:3] >= lag, window[lag : lag + rows], 0.0) * taps_ref[lag : lag + 1, :]
    later[...] = summed_grad[:8]
    return grad


def silu_slope(values, gate):
    return gate * (1.0 + values * (1.0 - gate))


def scan_block(
    conv_ref, before_ref, state_ref, state_before_ref, step_ref, meta_ref, segment_ref, taps_ref, state_taps_ref, head_ref,
    turned_over,
):
    rows = SSD_BLOCK
    channels = conv_ref.shape[1]
    meta = meta_ref[...]
    summed = conv_sum(conv_ref, before_ref, taps_ref, meta)
    activated, conv_gate = silu_parts(summed)
    wide_inputs = activated.astype(BFLOAT).astype(FLOAT)
    state_summed = conv_sum(state_ref, state_before_ref, state_taps_ref, meta)
    state_values, state_gate = silu_parts(state_summed)
    write = state_values[:, :NSTATE].astype(BFLOAT)
    read = state_values[:, NSTATE:].astype(BFLOAT)
    raw = step_ref[...].astype(FLOAT) + head_ref[0:1, :]
    steps = jnp.maximum(raw, 0.0) + jnp.log1p(jnp.exp(-jnp.abs(raw)))
    row = lax.broadcasted_iota(jnp.int32, (rows, rows), 0)
    column = lax.broadcasted_iota(jnp.int32, (rows, rows), 1)
    triangle = (row >= column).astype(BFLOAT)
    total = running_sum(steps * head_ref[1:2, :], triangle, (1, 0))
    entered = jnp.exp(total) * meta[:, 3:4]
    leaving = jnp.exp(total[rows - 1 : rows] - total) * meta[:, 4:5]
    expand = expand_table(channels)
    spread = head_spread(jnp.concatenate([steps, entered, leaving * steps], axis=0), expand)
    ordered = row <= column if turned_over else row >= column
    blocked = jnp.where(ordered & (meta[:, 0:1] == segment_ref[0:1, :]), 0.0, NEGATIVE)
    return dict(
        summed=summed,
        conv_gate=conv_gate,
        state_summed=state_summed,
        state_gate=state_gate,
        write=write,
        read=read,
        wide_inputs=wide_inputs,
        raw=raw,
        steps=steps,
        triangle=triangle,
        total=total,
        total_rows=total.T,
        leaving=leaving,
        expand=expand,
        steps_wide=spread[:rows],
        entered_wide=spread[rows : 2 * rows],
        tail_wide=spread[2 * rows :],
        stepped=(wide_inputs * spread[:rows]).astype(BFLOAT),
        tailed=(wide_inputs * spread[2 * rows :]).astype(BFLOAT),
        blocked=blocked,
        crossing=dot(write, read, (1, 1)) if turned_over else dot(read, write, (1, 1)),
    )


def decay_of(block, head):
    difference = block["total"][:, head : head + 1] - block["total_rows"][head : head + 1, :]
    return jnp.exp(difference + block["blocked"])


def turned_decay_of(block, head):
    difference = block["total_rows"][head : head + 1, :] - block["total"][:, head : head + 1]
    return jnp.exp(difference + block["blocked"])


def scan_forward_kernel(
    gate_ref, conv_ref, before_ref, state_ref, state_before_ref, step_ref, meta_ref, segment_ref, taps_ref,
    state_taps_ref, head_ref, skip_ref, mixed_ref, out_ref, scanned_ref, states_ref, state,
):
    del mixed_ref

    @pl.when(pl.program_id(0) == 0)
    def _():
        state[...] = jnp.zeros_like(state)

    block = scan_block(
        conv_ref, before_ref, state_ref, state_before_ref, step_ref, meta_ref, segment_ref, taps_ref, state_taps_ref,
        head_ref, False,
    )
    heads = conv_ref.shape[1] // HP
    carried = state[...].astype(BFLOAT)
    states_ref[0] = carried
    across = dot(block["read"], carried, (1, 0)) * block["entered_wide"]
    within = []
    for head in range(heads):
        weights = (block["crossing"] * decay_of(block, head)).astype(BFLOAT)
        within.append(dot(weights, block["stepped"][:, head * HP : (head + 1) * HP], (1, 0)))
    scanned = across + jnp.concatenate(within, axis=1)
    scanned_ref[...] = scanned
    gated, _ = silu_parts(gate_ref[...].astype(FLOAT))
    out_ref[...] = ((scanned + skip_ref[0:1, :] * block["wide_inputs"]) * gated).astype(BFLOAT)
    state[...] = state[...] * block["entered_wide"][SSD_BLOCK - 1 : SSD_BLOCK, :] + dot(
        block["write"], block["tailed"], (0, 0)
    )


def scan_backward_kernel(
    gate_ref, conv_ref, before_ref, state_ref, state_before_ref, step_ref, meta_ref, segment_ref, taps_ref,
    state_taps_ref, head_ref, skip_ref, scanned_ref, states_ref, grad_ref, query_grad_ref, shared_grad_ref, *rest,
):
    out_ref, *running = rest[-4:]
    state_grad, later, state_later = running

    @pl.when(pl.program_id(0) == 0)
    def _():
        for at, ref in enumerate(running):
            ref[...] = rest[1 + at][...] if len(rest) > 4 else jnp.zeros_like(ref)

    block = scan_block(
        conv_ref, before_ref, state_ref, state_before_ref, step_ref, meta_ref, segment_ref, taps_ref, state_taps_ref,
        head_ref, True,
    )
    rows = SSD_BLOCK
    channels = conv_ref.shape[1]
    heads = channels // HP
    meta = meta_ref[...]
    read, write = block["read"], block["write"]
    inputs = block["wide_inputs"]
    scanned = scanned_ref[...]
    skip = skip_ref[0:1, :]
    gate_values = gate_ref[...].astype(FLOAT)
    gated, gate = silu_parts(gate_values)
    grad = grad_ref[...].astype(FLOAT)
    gate_grad = grad * (scanned + skip * inputs) * silu_slope(gate_values, gate)
    out_grad = grad * gated
    inputs_grad = skip * out_grad
    rounded = out_grad.astype(BFLOAT)
    wide_rounded = rounded.astype(FLOAT)
    carried = states_ref[0]
    after = state_grad[...]
    after_rounded = after.astype(BFLOAT)

    from_state = dot(write, after_rounded, (1, 0))
    entering = (wide_rounded * block["entered_wide"]).astype(BFLOAT)
    write_grad = dot(block["tailed"], after_rounded, (1, 1))
    read_grad = dot(entering, carried, (1, 1))
    last_entered = block["entered_wide"][rows - 1 : rows, :]
    through = jnp.sum(after * carried.astype(FLOAT), axis=0, keepdims=True) * last_entered
    state_grad[...] = after * last_entered + dot(read, entering, (0, 0))

    crossing_grad = jnp.zeros((rows, rows), FLOAT)
    pulled = []
    for head in range(heads):
        span = slice(head * HP, (head + 1) * HP)
        decay = turned_decay_of(block, head)
        weights = (block["crossing"] * decay).astype(BFLOAT)
        pulled.append(dot(weights, rounded[:, span], (1, 0)))
        crossing_grad = crossing_grad + dot(block["stepped"][:, span], rounded[:, span], (1, 1)) * decay
    pulled = jnp.concatenate(pulled, axis=1)
    crossing_rounded = crossing_grad.astype(BFLOAT)
    read_grad = read_grad + dot(crossing_rounded, write, (0, 0))
    write_grad = write_grad + dot(crossing_rounded, read, (1, 0))

    inputs_grad = inputs_grad + block["steps_wide"] * pulled + block["tail_wide"] * from_state
    sums = head_sum(
        jnp.concatenate(
            [
                wide_rounded * scanned - block["stepped"].astype(FLOAT) * pulled,
                inputs * pulled,
                inputs * from_state,
                jnp.broadcast_to(through, (8, channels)),
            ],
            axis=0,
        ),
        block["expand"],
    )
    leaving_grad = sums[2 * rows : 3 * rows] * block["leaving"]
    leaving_total = leaving_grad * block["steps"]
    last = sums[3 * rows : 3 * rows + 1] + jnp.sum(leaving_total, axis=0, keepdims=True)
    total_grad = sums[:rows] - leaving_total
    total_grad = total_grad + jnp.where(
        lax.broadcasted_iota(jnp.int32, total_grad.shape, 0) == rows - 1, last, 0.0
    )
    decay_grad = running_sum(total_grad, block["triangle"], (0, 0))
    steps_grad = sums[rows : 2 * rows] + leaving_grad + decay_grad * head_ref[1:2, :]
    raw_grad = steps_grad / (1.0 + jnp.exp(-block["raw"]))
    raw_grad = jnp.where(lax.broadcasted_iota(jnp.int32, raw_grad.shape, 1) < heads, raw_grad, 0.0)

    state_slope = silu_slope(block["state_summed"], block["state_gate"])
    state_pre = conv_back(
        jnp.concatenate([write_grad, read_grad], axis=1) * state_slope, state_later, state_taps_ref, meta
    )
    conv_pre = conv_back(inputs_grad * silu_slope(block["summed"], block["conv_gate"]), later, taps_ref, meta)
    out_ref[:, : 2 * NSTATE] = state_pre.astype(BFLOAT)
    start = 2 * NSTATE + 2 * HEAD_SIZE
    end = out_ref.shape[1] - LANES
    out_ref[:, 2 * NSTATE : start] = shared_grad_ref[...]
    out_ref[:, start + 2 * channels : end] = query_grad_ref[...]
    out_ref[:, start : start + channels] = gate_grad.astype(BFLOAT)
    out_ref[:, start + channels : start + 2 * channels] = conv_pre.astype(BFLOAT)
    out_ref[:, end:] = raw_grad.astype(BFLOAT)


STATES = 2 * NSTATE
PAIR = 2 * HEAD_SIZE


def scan_specs(channels, order):
    half = SSD_BLOCK // 16
    before = lambda i: jnp.maximum(order(i) * half - 1, 0)
    gate_at = (STATES + PAIR) // channels
    step_at = (STATES + PAIR + 2 * channels + channels * QUERY_HEADS // DSSM * HEAD_SIZE) // LANES
    return [
        pl.BlockSpec((SSD_BLOCK, channels), lambda i: (order(i), gate_at)),
        pl.BlockSpec((SSD_BLOCK, channels), lambda i: (order(i), gate_at + 1)),
        pl.BlockSpec((16, channels), lambda i: (before(i), gate_at + 1)),
        pl.BlockSpec((SSD_BLOCK, STATES), lambda i: (order(i), 0)),
        pl.BlockSpec((16, STATES), lambda i: (before(i), 0)),
        pl.BlockSpec((SSD_BLOCK, LANES), lambda i: (order(i), step_at)),
        pl.BlockSpec((SSD_BLOCK, LANES), lambda i: (order(i), 0)),
        pl.BlockSpec((8, SSD_BLOCK), lambda i: (0, order(i))),
        whole((8, channels)),
        whole((8, STATES)),
        whole((8, LANES)),
        whole((8, channels)),
    ]


def scan_operands(projected, tables):
    return [projected] * 6 + [
        tables[name] for name in ("meta", "segment_row", "taps", "state_taps", "head", "skip")
    ]


def scan_cost(tokens, channels, factor):
    heads = channels // HP
    return estimate(
        flops=factor * 2 * tokens * SSD_BLOCK * (3 * channels + NSTATE),
        bytes_accessed=factor * tokens * channels * 12,
        transcendentals=tokens * SSD_BLOCK * heads,
    )


def scan_forward(projected, tables, mixed):
    tokens = projected.shape[0]
    channels = tables["taps"].shape[1]
    blocks = tokens // SSD_BLOCK
    return pl.pallas_call(
        scan_forward_kernel,
        grid=(blocks,),
        in_specs=scan_specs(channels, lambda i: i) + [pl.BlockSpec(memory_space=pl.ANY)],
        out_specs=[
            pl.BlockSpec((SSD_BLOCK, channels), lambda i: (i, 0)),
            pl.BlockSpec((SSD_BLOCK, channels), lambda i: (i, 0)),
            pl.BlockSpec((1, NSTATE, channels), lambda i: (i, 0, 0)),
        ],
        out_shape=[
            jax.ShapeDtypeStruct(mixed.shape, BFLOAT),
            jax.ShapeDtypeStruct((tokens, channels), FLOAT),
            jax.ShapeDtypeStruct((blocks, NSTATE, channels), BFLOAT),
        ],
        scratch_shapes=[pltpu.VMEM((NSTATE, channels), FLOAT)],
        input_output_aliases={12: 0},
        compiler_params=pltpu.CompilerParams(vmem_limit_bytes=SCAN_BYTES),
        cost_estimate=scan_cost(tokens, channels, 1),
        name="scan_forward",
    )(*scan_operands(projected, tables), mixed)


def scan_backward(projected, tables, scanned, carried, mixed_grad, attended_grads, part, parts, before):
    tokens, width = projected.shape
    channels = tables["taps"].shape[1]
    blocks = tokens // SSD_BLOCK
    last = blocks - 1 - part * (blocks // parts)
    back = lambda i: (last - i, 0)
    running = [(NSTATE, channels), (8, channels), (8, STATES)]
    query_grad, shared_grad = attended_grads
    operands = [*scan_operands(projected, tables), scanned, carried, mixed_grad, query_grad, shared_grad]
    in_specs = scan_specs(channels, lambda i: last - i) + [
        pl.BlockSpec((SSD_BLOCK, channels), back),
        pl.BlockSpec((1, NSTATE, channels), lambda i: (last - i, 0, 0)),
        pl.BlockSpec((SSD_BLOCK, channels), back),
        pl.BlockSpec((SSD_BLOCK, query_grad.shape[1]), back),
        pl.BlockSpec((SSD_BLOCK, PAIR), back),
    ]
    aliases = {}
    if before is not None:
        aliases = {len(operands): 0}
        operands += list(before)
        in_specs += [pl.BlockSpec(memory_space=pl.ANY), *[whole(shape) for shape in running]]
    return pl.pallas_call(
        scan_backward_kernel,
        grid=(blocks // parts,),
        in_specs=in_specs,
        out_specs=[pl.BlockSpec((SSD_BLOCK, width), back), *[whole(shape) for shape in running]],
        out_shape=[
            jax.ShapeDtypeStruct((tokens, width), BFLOAT),
            *[jax.ShapeDtypeStruct(shape, FLOAT) for shape in running],
        ],
        input_output_aliases=aliases,
        compiler_params=pltpu.CompilerParams(vmem_limit_bytes=ALONE_BYTES),
        cost_estimate=scan_cost(tokens, channels, 2),
        name="scan_backward",
    )(*operands)


def turned(values, cosine, sine):
    return (values * cosine + pltpu.roll(values, HEAD_SIZE // 2, 1) * sine).astype(BFLOAT)


def turned_back(values, cosine, sine):
    return values * cosine + pltpu.roll(values * sine, HEAD_SIZE // 2, 1)


ATT_ROWS = 256


def attention_mask(meta_ref, segment_ref, start, extent):
    row = start + lax.broadcasted_iota(jnp.int32, (ATT_ROWS, extent), 0)
    column = lax.broadcasted_iota(jnp.int32, (ATT_ROWS, extent), 1)
    return (row >= column) & (meta_ref[start : start + ATT_ROWS, 0:1] == segment_ref[0:1, :extent])


def probabilities(query, keys, allowed):
    score = dot(query, keys, (1, 1)) * (1.0 / math.sqrt(HEAD_SIZE))
    score = jnp.where(allowed, score, NEGATIVE)
    exponent = jnp.exp(score - jnp.max(score, axis=1, keepdims=True))
    return exponent / jnp.sum(exponent, axis=1, keepdims=True)


def attention_forward_kernel(query_ref, key_ref, value_ref, cosine_ref, sine_ref, meta_ref, segment_ref, out_ref, keys):
    tokens = key_ref.shape[0]
    keys[...] = turned(key_ref[...].astype(FLOAT), cosine_ref[...], sine_ref[...])
    for start in range(0, tokens, ATT_ROWS):
        extent = start + ATT_ROWS
        here = slice(start, extent)
        allowed = attention_mask(meta_ref, segment_ref, start, extent)
        for unit in range(query_ref.shape[1] // HEAD_SIZE):
            span = slice(unit * HEAD_SIZE, (unit + 1) * HEAD_SIZE)
            query = turned(query_ref[here, span].astype(FLOAT), cosine_ref[here], sine_ref[here])
            weights = probabilities(query, keys[:extent], allowed).astype(BFLOAT)
            out_ref[here, span] = dot(weights, value_ref[:extent], (1, 0)).astype(BFLOAT)


def attention_backward_kernel(
    query_ref, key_ref, value_ref, cosine_ref, sine_ref, meta_ref, segment_ref, grad_ref,
    query_grad_ref, shared_grad_ref, keys, key_sum, value_sum,
):
    tokens = key_ref.shape[0]
    scale = 1.0 / math.sqrt(HEAD_SIZE)
    keys[...] = turned(key_ref[...].astype(FLOAT), cosine_ref[...], sine_ref[...])
    key_sum[...] = jnp.zeros_like(key_sum)
    value_sum[...] = jnp.zeros_like(value_sum)
    for start in range(0, tokens, ATT_ROWS):
        extent = start + ATT_ROWS
        here = slice(start, extent)
        allowed = attention_mask(meta_ref, segment_ref, start, extent)
        for unit in range(query_ref.shape[1] // HEAD_SIZE):
            span = slice(unit * HEAD_SIZE, (unit + 1) * HEAD_SIZE)
            query = turned(query_ref[here, span].astype(FLOAT), cosine_ref[here], sine_ref[here])
            weights = probabilities(query, keys[:extent], allowed)
            grad = grad_ref[here, span]
            weights_grad = dot(grad, value_ref[:extent], (1, 1))
            value_sum[:extent] += dot(weights.astype(BFLOAT), grad, (0, 0))
            mean_grad = jnp.sum(weights * weights_grad, axis=1, keepdims=True)
            score_grad = (weights * (weights_grad - mean_grad) * scale).astype(BFLOAT)
            query_grad = dot(score_grad, keys[:extent], (1, 0))
            key_sum[:extent] += dot(score_grad, query, (0, 0))
            query_grad_ref[here, span] = turned_back(query_grad, cosine_ref[here], sine_ref[here]).astype(BFLOAT)
    shared_grad_ref[:, :HEAD_SIZE] = turned_back(key_sum[...], cosine_ref[...], sine_ref[...]).astype(BFLOAT)
    shared_grad_ref[:, HEAD_SIZE:] = value_sum[...].astype(BFLOAT)


def attention_cost(tokens, width, factor):
    return estimate(
        flops=factor * 2 * tokens * tokens * width,
        bytes_accessed=factor * tokens * width * 8,
        transcendentals=tokens * tokens * width // (2 * HEAD_SIZE),
    )


def attention_specs(tokens, channels):
    width = channels * QUERY_HEADS // DSSM * HEAD_SIZE
    narrow = whole((tokens, HEAD_SIZE))
    return [
        pl.BlockSpec((tokens, width), lambda *_: (0, (STATES + PAIR + 2 * channels) // width)),
        pl.BlockSpec((tokens, HEAD_SIZE), lambda *_: (0, STATES // HEAD_SIZE)),
        pl.BlockSpec((tokens, HEAD_SIZE), lambda *_: (0, STATES // HEAD_SIZE + 1)),
        narrow,
        narrow,
        whole((tokens, LANES)),
        whole((8, tokens)),
    ]


def attention_operands(projected, tables):
    return [projected] * 3 + [tables[name] for name in ("cosine", "sine", "meta", "segment_row")]


def attention_forward(projected, tables):
    tokens = projected.shape[0]
    channels = tables["taps"].shape[1]
    width = channels * QUERY_HEADS // DSSM * HEAD_SIZE
    return pl.pallas_call(
        attention_forward_kernel,
        grid=(1,),
        in_specs=attention_specs(tokens, channels),
        out_specs=pl.BlockSpec((tokens, width), lambda *_: (0, channels // width)),
        out_shape=jax.ShapeDtypeStruct((tokens, channels + width), BFLOAT),
        scratch_shapes=[pltpu.VMEM((tokens, HEAD_SIZE), BFLOAT)],
        compiler_params=pltpu.CompilerParams(vmem_limit_bytes=SCAN_BYTES),
        cost_estimate=attention_cost(tokens, width, 1),
        name="attention_forward",
    )(*attention_operands(projected, tables))


def attention_backward(projected, tables, mixed_grad):
    tokens = projected.shape[0]
    channels = tables["taps"].shape[1]
    width = channels * QUERY_HEADS // DSSM * HEAD_SIZE
    return pl.pallas_call(
        attention_backward_kernel,
        grid=(1,),
        in_specs=attention_specs(tokens, channels)
        + [pl.BlockSpec((tokens, width), lambda *_: (0, channels // width))],
        out_specs=[whole((tokens, width)), whole((tokens, PAIR))],
        out_shape=[jax.ShapeDtypeStruct((tokens, width), BFLOAT), jax.ShapeDtypeStruct((tokens, PAIR), BFLOAT)],
        scratch_shapes=[
            pltpu.VMEM((tokens, HEAD_SIZE), BFLOAT),
            pltpu.VMEM((tokens, HEAD_SIZE), FLOAT),
            pltpu.VMEM((tokens, HEAD_SIZE), FLOAT),
        ],
        compiler_params=pltpu.CompilerParams(vmem_limit_bytes=ALONE_BYTES),
        cost_estimate=attention_cost(tokens, width, 3),
        name="attention_backward",
    )(*attention_operands(projected, tables), mixed_grad)


def mixer_tables(lengths, segment, position, conv_values, conv_states, scan_params):
    tokens = segment.shape[0]
    block = jnp.arange(tokens, dtype=jnp.int32) // SSD_BLOCK
    previous = jnp.concatenate([jnp.full((1,), -1, jnp.int32), segment[:-1]])
    first_previous = jnp.repeat(previous[::SSD_BLOCK], SSD_BLOCK)
    last_segment = jnp.repeat(segment[SSD_BLOCK - 1 :: SSD_BLOCK], SSD_BLOCK)
    length = jnp.sum(
        jnp.where(segment[:, None] == jnp.arange(lengths.shape[0], dtype=jnp.int32)[None, :], lengths[None, :], 0),
        axis=1,
    )
    columns = [
        segment,
        position,
        length - 1 - position,
        segment == first_previous,
        segment == last_segment,
    ]
    meta = jnp.stack([column.astype(FLOAT) for column in columns], axis=1)
    half_width = HEAD_SIZE // 2
    frequency = ROPE_BASE ** (-2.0 * jnp.arange(half_width, dtype=FLOAT) / HEAD_SIZE)
    angle = position.astype(FLOAT)[:, None] * frequency[None, :]
    cosine, sine = jnp.cos(angle), jnp.sin(angle)
    heads = scan_params.shape[1]
    head = jnp.stack([scan_params[0], -jnp.exp(scan_params[1]), scan_params[2]])
    return dict(
        meta=jnp.pad(meta, ((0, 0), (0, LANES - meta.shape[1]))),
        segment_row=jnp.broadcast_to(segment.astype(FLOAT)[None, :], (8, tokens)),
        taps=jnp.pad(conv_values.astype(FLOAT), ((0, 3), (0, 0))),
        state_taps=jnp.pad(conv_states.astype(FLOAT), ((0, 3), (0, 0))),
        head=jnp.pad(head, ((0, 5), (0, LANES - heads))),
        skip=jnp.broadcast_to(jnp.repeat(scan_params[2], HP)[None, :], (8, heads * HP)),
        cosine=jnp.concatenate([cosine, cosine], axis=1),
        sine=jnp.concatenate([-sine, sine], axis=1),
    )


HALVES = 2
DENSE_TILE = 1024


def matrix_rows(values):
    return values.reshape(values.shape[0] * values.shape[1], values.shape[2])


def cut_tiles(width, tile):
    return [(low, min(low + tile, width)) for low in range(0, width, tile)]


def spread_kernel(masks, count, chosen_ref, *rest):
    halves, weights = rest[: 2 * len(masks)], rest[2 * len(masks) : 2 * len(masks) + count]
    out_ref, narrow_ref, out_tile, narrow, sems = rest[-5:]
    rows = halves[0].shape[0]
    shards = weights[0].shape[0]
    depth = shards // HALVES
    lower = weights[-1].shape[2] - LANES
    copies = []
    for at, mask in enumerate(masks):
        left_ref, right_ref = halves[2 * at : 2 * at + 2]
        here = pl.ds(pl.multiple_of((lax.axis_index("col") ^ mask) * rows, rows), rows)

        def through(ref, low, high):
            return dot(left_ref[...], matrix_rows(ref[:depth, :rows, low:high]), (1, 0)) + dot(
                right_ref[...], matrix_rows(ref[depth:, :rows, low:high]), (1, 0)
            )

        def send(tile, target):
            copies.append(pltpu.make_async_copy(tile, target, sems.at[len(copies)]))
            copies[-1].start()

        narrow[at] = (chosen_ref[here, :] * through(weights[-1], lower, lower + LANES)).astype(BFLOAT)
        send(narrow.at[at], narrow_ref.at[here, :])
        column = 0
        for ref in weights:
            for low, high in cut_tiles(ref.shape[2] - (LANES if ref is weights[-1] else 0), DENSE_TILE):
                span = slice(column, column + high - low)
                column += high - low
                raised = matrix_rows(ref[:, rows : rows + NADAPT * RANK // shards, low:high])
                out_tile[at, :, span] = (through(ref, low, high) + dot(narrow[at], raised, (1, 0))).astype(BFLOAT)
                send(out_tile.at[at, :, span], out_ref.at[here, span])
    for copy in copies:
        copy.wait()


def weights_width(gathered):
    return sum(part.shape[2] for part in gathered) - LANES


def spread_blocks(blocks, gathered, selector, held):
    masks = [mask for mask, _ in blocks]
    rows, half = blocks[0][1][0].shape
    width = weights_width(gathered)
    total = selector.shape[0]
    fast, free = pl.BlockSpec(memory_space=pltpu.VMEM), pl.BlockSpec(memory_space=pl.ANY)
    operands = [selector, *[part for _, halves in blocks for part in halves], *gathered]
    in_specs = [fast] * len(operands)
    aliases = {}
    if held is not None:
        aliases = {len(operands): 0, len(operands) + 1: 1}
        operands += list(held)
        in_specs += [free] * 2
    copies = len(masks) * (1 + sum(-(-part.shape[2] // DENSE_TILE) for part in gathered))
    return pl.pallas_call(
        functools.partial(spread_kernel, masks, len(gathered)),
        in_specs=in_specs,
        out_specs=[free] * 2,
        out_shape=[
            jax.ShapeDtypeStruct((total, width), BFLOAT),
            jax.ShapeDtypeStruct((total, LANES), BFLOAT),
        ],
        scratch_shapes=[
            pltpu.VMEM((len(masks), rows, width), BFLOAT),
            pltpu.VMEM((len(masks), rows, LANES), BFLOAT),
            pltpu.SemaphoreType.DMA((copies,)),
        ],
        input_output_aliases=aliases,
        compiler_params=pltpu.CompilerParams(vmem_limit_bytes=DENSE_BYTES),
        cost_estimate=estimate(
            flops=4 * len(masks) * rows * half * (width + LANES),
            bytes_accessed=2 * len(masks) * rows * (2 * half + width),
            transcendentals=0,
        ),
        name="spread_blocks",
    )(*operands)


def collect_kernel(masks, count, values_ref, *refs):
    weights, outs = refs[:count], refs[count:]
    if len(outs) > 2 * len(masks):
        inner_ref, *outs, raise_ref = outs
        raise_ref[...] = dot(inner_ref[...], values_ref[...], (0, 0)).astype(BFLOAT)
    rows = values_ref.shape[0] // 4
    shards = weights[0].shape[0]
    half = shards // HALVES * rows
    width = values_ref.shape[1]
    starts, column = [], 0
    for ref in weights:
        high = min(column + ref.shape[2], width)
        starts.append((column, high))
        column = high
    for at, mask in enumerate(masks):
        here = pl.ds(pl.multiple_of((lax.axis_index("col") ^ mask) * rows, rows), rows)
        first, second = outs[2 * at], outs[2 * at + 1]

        def through(cut):
            total = None
            for (low, high), ref in zip(starts, weights):
                part = dot(values_ref[here, low:high], cut(ref, high - low), (1, 1))
                total = part if total is None else total + part
            return total

        for shard in range(shards):
            out_ref = first if shard < shards // HALVES else second
            column = shard * rows % half
            out_ref[:, column : column + rows] = through(lambda ref, wide: ref[shard, :rows, :wide]).astype(
                out_ref.dtype
            )
        first[:, half:] = through(
            lambda ref, wide: matrix_rows(ref[:, rows : rows + NADAPT * RANK // shards, :wide])
        ).astype(first.dtype)


def collect_blocks(masks, values, gathered, types, inner=()):
    rows = values.shape[0] // 4
    half = gathered[0].shape[0] // HALVES * rows
    fast = pl.BlockSpec(memory_space=pltpu.VMEM)
    out_shape = []
    for pair in types:
        out_shape.append(jax.ShapeDtypeStruct((rows, half + LANES), pair[0]))
        out_shape.append(jax.ShapeDtypeStruct((rows, half), pair[1]))
    out_shape += [jax.ShapeDtypeStruct((LANES, values.shape[1]), BFLOAT) for _ in inner]
    outs = pl.pallas_call(
        functools.partial(collect_kernel, masks, len(gathered)),
        in_specs=[fast] * (1 + len(gathered) + len(inner)),
        out_specs=[fast] * len(out_shape),
        out_shape=out_shape,
        compiler_params=pltpu.CompilerParams(vmem_limit_bytes=DENSE_BYTES),
        cost_estimate=estimate(
            flops=4 * len(masks) * rows * half * values.shape[1],
            bytes_accessed=2 * len(masks) * rows * (values.shape[1] + 4 * half),
            transcendentals=0,
        ),
        name="collect_blocks",
    )(values, *gathered, *inner)
    return [tuple(outs[2 * at : 2 * at + 2]) for at in range(len(masks))] + list(outs[2 * len(masks) :])


def root_mean(values):
    return lax.rsqrt(jnp.mean(values * values, axis=1, keepdims=True) + EPSILON)


def packed_grad(narrow, values, choose):
    half = LANES // 2
    chosen = dot(narrow, choose, (1, 0)).astype(BFLOAT)
    grad = dot(chosen, values, (0, 0))
    low = lax.broadcasted_iota(jnp.int32, (8, LANES), 1) < half
    devices = []
    for start in range(0, grad.shape[1], LANES):
        own = grad[:, start : start + LANES]
        turned_own = pltpu.roll(own, half, 1)
        for first, second in ((own, turned_own), (turned_own, own)):
            devices.append(
                jnp.concatenate(
                    [jnp.where(low, first[at : at + 8], second[at + 8 : at + 16]) for at in (0, 16)], axis=1
                )
            )
    return jnp.concatenate(devices, axis=0).astype(BFLOAT)


def finish_kernel(kind, first_own, first_near, first_far, second_own, second_near, second_far, lower_ref, chosen_ref,
                  *refs):
    half = second_own.shape[1]
    model = HALVES * half
    wide = lambda ref: ref[...].astype(FLOAT)
    first = wide(first_own) + wide(first_near) + wide(first_far)
    second = wide(second_own) + wide(second_near) + wide(second_far)
    inner = (chosen_ref[...] * first[:, half:]).astype(BFLOAT)
    summed = jnp.concatenate([first[:, :half], second], axis=1) + dot(
        inner, matrix_rows(lower_ref[...]), (1, 1)
    )
    if kind == "output":
        residual_ref, place_ref, choose_ref, branch_ref, early_ref, out_ref = refs
        result = (residual_ref[...] + summed).astype(BFLOAT)
        out_ref[:, :model] = dot(place_ref[...], result, (0, 0)).astype(BFLOAT)
        out_ref[:, model : model + 2 * LANES] = packed_grad(inner, branch_ref[...], choose_ref[...])
        out_ref[:, model + 2 * LANES :] = early_ref[...]
        return
    if kind == "forward":
        residual_ref, gain_ref, out_ref, inner_ref, left_ref, right_ref = refs
        hidden = residual_ref[...] + summed
        normed = (hidden * root_mean(hidden) * gain_ref[0:1, :]).astype(BFLOAT)
    else:
        values_ref, upstream_ref, gain_ref, choose_ref, normed_left, normed_right = refs[:6]
        values = values_ref[...]
        scale = root_mean(values)
        weighted = summed * gain_ref[0:1, :]
        mean = jnp.mean(weighted * values, axis=1, keepdims=True)
        hidden = upstream_ref[...].astype(FLOAT) + scale * weighted - values * (scale * scale * scale * mean)
        normed = hidden.astype(BFLOAT)
        packed = packed_grad(
            inner, jnp.concatenate([normed_left[...], normed_right[...]], axis=1), choose_ref[...]
        )
        if kind == "input":
            place_ref, out_ref = refs[6:]
            out_ref[:, :model] = dot(place_ref[...], normed, (0, 0)).astype(BFLOAT)
            out_ref[:, model:] = packed
            return
        given_ref, out_ref, inner_ref, left_ref, right_ref, packed_ref = refs[6:]
        packed_ref[:, : 2 * LANES] = packed
        packed_ref[:, 2 * LANES :] = packed_grad(given_ref[...], normed, choose_ref[...])
    out_ref[...] = hidden
    inner_ref[...] = inner
    left_ref[...] = normed[:, :half]
    right_ref[...] = normed[:, half:]


def finish(kind, parts, gathered, own_selector, *operands):
    rows = own_selector.shape[0]
    half = parts[3].shape[1]
    shards = gathered[-1].shape[0]
    model = HALVES * half
    lower = gathered[-1][:, : model // shards, -LANES:]
    shaped = jax.ShapeDtypeStruct
    if kind in ("output", "input"):
        out_shape = shaped((rows, model + 2 * LANES * (3 if kind == "output" else 1)), BFLOAT)
        out_specs = whole(out_shape.shape)
    else:
        out_shape = [shaped((rows, model), FLOAT), shaped((rows, LANES), BFLOAT)]
        out_shape += [shaped((rows, half), BFLOAT)] * 2
        out_shape += [shaped((rows, 4 * LANES), BFLOAT)] * (kind == "backward")
        out_specs = [whole(shape.shape) for shape in out_shape]
    given = [*parts, lower, own_selector, *operands]
    return pl.pallas_call(
        functools.partial(finish_kernel, kind),
        grid=(1,),
        in_specs=[whole(value.shape) for value in given],
        out_specs=out_specs,
        out_shape=out_shape,
        compiler_params=pltpu.CompilerParams(vmem_limit_bytes=FINISH_BYTES),
        cost_estimate=estimate(
            flops=2 * rows * model * LANES, bytes_accessed=rows * model * 20, transcendentals=0
        ),
        name="finish_" + kind,
    )(*given)


def onward_kernel(first_kept, first_part, second_kept, second_part, first_ref, second_ref):
    first_ref[...] = (first_kept[...] + first_part[...].astype(FLOAT)).astype(BFLOAT)
    second_ref[...] = (second_kept[...] + second_part[...].astype(FLOAT)).astype(BFLOAT)


def sum_onward(first_kept, first_part, second_kept, second_part):
    return pl.pallas_call(
        onward_kernel,
        in_specs=[pl.BlockSpec(memory_space=pltpu.VMEM)] * 4,
        out_specs=[pl.BlockSpec(memory_space=pltpu.VMEM)] * 2,
        out_shape=[jax.ShapeDtypeStruct(part.shape, BFLOAT) for part in (first_part, second_part)],
        compiler_params=pltpu.CompilerParams(vmem_limit_bytes=DENSE_BYTES),
        name="sum_onward",
    )(first_kept, first_part, second_kept, second_part)


def send_kernel(target_column, target_row, tokens_ref, adapter_ref, sent_ref, matrix_ref):
    rows = tokens_ref.shape[0]
    model = tokens_ref.shape[1]
    peer = adapter_ref.shape[0]
    column, row = target_column[:, 0:1], target_row[0:1, :]
    earlier = lax.broadcasted_iota(jnp.int32, (rows, rows), 0) < lax.broadcasted_iota(jnp.int32, (rows, rows), 1)
    same = jnp.where((column // rows == row // rows) & earlier, 1.0, 0.0)
    place = (row // rows) * peer + jnp.sum(same, axis=0, keepdims=True).astype(jnp.int32)
    matrix = (lax.broadcasted_iota(jnp.int32, (rows, rows), 0) == place).astype(BFLOAT)
    matrix_ref[...] = matrix
    sent_ref[:, :model] = dot(matrix, tokens_ref[...], (1, 0)).astype(BFLOAT)
    lane = lax.broadcasted_iota(jnp.int32, (rows, LANES), 1)
    slots = jnp.where(lane == 0, column % rows, 0).astype(FLOAT).astype(BFLOAT)
    notes = dot(matrix, slots, (1, 0))
    sent_ref[:, model:] = jnp.where(lane == 0, notes, adapter_ref[0:1, :]).astype(BFLOAT)


def send_tokens(target, tokens, adapters, peer):
    rows, model = tokens.shape
    notes = jnp.pad(adapters.astype(FLOAT), (1, LANES - 1 - adapters.shape[0]))
    return pl.pallas_call(
        send_kernel,
        in_specs=[pl.BlockSpec(memory_space=pltpu.VMEM)] * 4,
        out_specs=[pl.BlockSpec(memory_space=pltpu.VMEM)] * 2,
        out_shape=[
            jax.ShapeDtypeStruct((rows, model + LANES), BFLOAT),
            jax.ShapeDtypeStruct((rows, rows), BFLOAT),
        ],
        compiler_params=pltpu.CompilerParams(vmem_limit_bytes=DENSE_BYTES),
        name="send_tokens",
    )(
        jnp.broadcast_to(target[:, None], (rows, LANES)),
        jnp.broadcast_to(target[None, :], (8, rows)),
        tokens,
        jnp.broadcast_to(notes[None, :], (peer, LANES)),
    )


def arrive_kernel(arrived_ref, gain_ref, own_ref, matrix_ref, left_ref, right_ref):
    rows, model = own_ref.shape
    slots = arrived_ref[:, model:].astype(FLOAT).T[0:1, :]
    row = lax.broadcasted_iota(jnp.int32, (rows, rows), 0).astype(FLOAT)
    matrix = (row == slots).astype(BFLOAT)
    matrix_ref[...] = matrix
    own = dot(matrix, arrived_ref[:, :model], (1, 0))
    own_ref[...] = own
    normed = (own * root_mean(own) * gain_ref[0:1, :]).astype(BFLOAT)
    left_ref[...] = normed[:, : model // HALVES]
    right_ref[...] = normed[:, model // HALVES :]


def arrive_tokens(arrived, gain):
    rows, model = arrived.shape[0], arrived.shape[1] - LANES
    return pl.pallas_call(
        arrive_kernel,
        in_specs=[pl.BlockSpec(memory_space=pltpu.VMEM)] * 2,
        out_specs=[pl.BlockSpec(memory_space=pltpu.VMEM)] * 4,
        out_shape=[
            jax.ShapeDtypeStruct((rows, model), FLOAT),
            jax.ShapeDtypeStruct((rows, rows), BFLOAT),
            jax.ShapeDtypeStruct((rows, model // HALVES), BFLOAT),
            jax.ShapeDtypeStruct((rows, model // HALVES), BFLOAT),
        ],
        compiler_params=pltpu.CompilerParams(vmem_limit_bytes=DENSE_BYTES),
        name="arrive_tokens",
    )(arrived, gain)


GATE_WIDTH = DSSM // QUERY_HEADS
PAIR_WIDTH = 2 * KEY_VALUE_HEADS * HEAD_SIZE // QUERY_HEADS
STATE_WIDTH = 2 * NSTATE // QUERY_HEADS
STEP_WIDTH = NH // QUERY_HEADS
ALL_AXES = ("row", "col")


def pad_columns(values, width):
    return jnp.pad(values, ((0, 0), (0, width - values.shape[1])))


def after(values, *earlier):
    return lax.optimization_barrier((values, *earlier))[0]


def after_all(values, *earlier):
    return lax.optimization_barrier((*values, *earlier))[: len(values)]


def unit_parts(values, units):
    cuts = [0]
    for width in (GATE_WIDTH, GATE_WIDTH, HEAD_SIZE, PAIR_WIDTH, STATE_WIDTH, STEP_WIDTH):
        cuts.append(cuts[-1] + width)
    return [
        jnp.concatenate(
            [values[:, unit * UNIT_IN + low : unit * UNIT_IN + high] for unit in range(units)], axis=1
        )
        for low, high in zip(cuts[:-1], cuts[1:])
    ]


def restore_units(parts, units):
    ordered = []
    for unit in range(units):
        for part in parts:
            width = part.shape[1] // units
            ordered.append(part[:, unit * width : (unit + 1) * width])
    return jnp.concatenate(ordered, axis=1)


def split_halves(values, units, first, axis):
    block = values.shape[axis] // units
    take = lambda low, high: lax.slice_in_dim(values, low, high, axis=axis)
    parts = [take(unit * block, unit * block + first) for unit in range(units)]
    parts += [take(unit * block + first, (unit + 1) * block) for unit in range(units)]
    return jnp.concatenate(parts, axis=axis)


def join_halves(values, units, first, axis):
    block = values.shape[axis] // units
    rest = block - first
    take = lambda low, high: lax.slice_in_dim(values, low, high, axis=axis)
    parts = []
    for unit in range(units):
        parts.append(take(unit * first, (unit + 1) * first))
        parts.append(take(units * first + unit * rest, units * first + (unit + 1) * rest))
    return jnp.concatenate(parts, axis=axis)


def quick(rows):
    return lax.axis_size("col") == 4 and lax.axis_size("row") == 8 and rows == 256


def spread_early(halves, gathered, selector):
    left, right = halves
    far_left, near_right = flip(left, 2), flip(right, 1)
    near_left, far_right = flip(left, 1), flip(right, 2)
    held = spread_blocks([(0, halves)], gathered, selector, None)
    onward_left, onward_right = after_all((far_left, near_right), held[1])
    corner = flip(onward_left, 1), flip(onward_right, 2)
    held = spread_blocks([(1, (near_left, near_right))], gathered, selector, held)
    held = spread_blocks([(2, (far_left, far_right))], gathered, selector, held)
    return spread_blocks([(3, corner)], gathered, selector, held)


def flip(values, mask):
    return lax.ppermute(values, "col", [(i, i ^ mask) for i in range(4)])


def gather_blocks(halves):
    left, right = halves
    far_left, near_right = flip(left, 2), flip(right, 1)
    near_left, far_right = flip(left, 1), flip(right, 2)
    corner_left, corner_right = flip(far_left, 1), flip(near_right, 2)
    return [
        (0, (left, right)),
        (1, (near_left, near_right)),
        (2, (far_left, far_right)),
        (3, (corner_left, corner_right)),
    ]


def rows_of(values, block, rows):
    return lax.dynamic_slice_in_dim(values, block * rows, rows, 0)


def spread_gathered(blocks, gathered, selector):
    held = None
    for block in blocks:
        held = spread_blocks([block], gathered, selector, held)
    return held


def spread_project(halves, gathered, selector):
    rows = halves[0].shape[0]
    if quick(rows):
        return spread_gathered(gather_blocks(halves), gathered, selector)
    wide, narrow_factor = gathered
    width = narrow_factor.shape[1]
    both = product(lax.all_gather(jnp.concatenate(halves, axis=1), "col", axis=0, tiled=True), wide)
    narrow = (selector * both[:, width:]).astype(BFLOAT)
    return (both[:, :width] + product(narrow, narrow_factor)).astype(BFLOAT), narrow


PIECE_TYPES = [(BFLOAT, BFLOAT), (BFLOAT, FLOAT), (FLOAT, BFLOAT), (FLOAT, FLOAT)]


def collect_pieces(values, gathered, at_once):
    if at_once:
        return collect_blocks([3, 1, 2, 0], values, gathered, PIECE_TYPES)
    (corner,) = collect_blocks([3], values, gathered, PIECE_TYPES[:1])
    values = after(values, corner[0])
    return [corner, *collect_blocks([1, 2, 0], values, gathered, PIECE_TYPES[1:])]


def collect_send(pieces, ordered=True):
    corner, near, far, own = pieces
    arriving = flip(corner[0], 1), flip(corner[1], 2)
    sent_near, sent_far = after_all((near[0], far[1]), *arriving) if ordered else (near[0], far[1])
    return own, flip(sent_near, 1), flip(sent_far, 2), far[0], near[1], arriving


def collect_middle(started):
    own, near_first, far_second, far_first, near_second, arriving = started
    return (own, near_first, far_second), sum_onward(far_first, arriving[0], near_second, arriving[1])


def collect_onward(onward):
    return flip(onward[0], 2), flip(onward[1], 1)


def collect_end(kept, last, kind, gathered, own_selector, *operands):
    own, near_first, far_second = kept
    parts = [own[0], near_first, last[0], own[1], far_second, last[1]]
    return finish(kind, parts, gathered, own_selector, *operands)


def collect_project(values, gathered, kind, own_selector, *operands):
    rows, model = own_selector.shape[0], operands[0].shape[1]
    if quick(rows):
        kept, onward = collect_middle(collect_send(collect_pieces(values, gathered, False)))
        return collect_end(kept, collect_onward(onward), kind, gathered, own_selector, *operands)
    wide, narrow_factor = gathered
    width = narrow_factor.shape[1]
    partial = jnp.concatenate(
        [contract_last(values, wide[:, :width]), contract_last(values, narrow_factor)], axis=1
    ).astype(BFLOAT)
    summed = lax.psum_scatter(partial, "col", scatter_dimension=0, tiled=True).astype(FLOAT)
    inner = (own_selector * summed[:, model:]).astype(BFLOAT)
    summed = summed[:, :model] + contract_last(inner, wide[:, width:])
    if kind == "output":
        return (operands[0] + summed).astype(BFLOAT), inner
    if kind == "forward":
        residual, gain = operands
        hidden = residual + summed
        return hidden, inner, *cut_halves(rms_norm(hidden, gain[0]).astype(BFLOAT))
    values, upstream, gain = operands
    _, back = jax.vjp(lambda given: rms_norm(given, gain[0]), values)
    hidden = upstream.astype(FLOAT) + back(summed)[0]
    if kind == "input":
        return hidden.astype(BFLOAT), inner
    return hidden, inner, *cut_halves(hidden.astype(BFLOAT))


def cut_halves(values):
    half = values.shape[1] // HALVES
    return values[:, :half], values[:, half:]


def local(
    tokens_in,
    cotangent,
    target,
    sequence_lengths,
    sequence_adapter,
    norm_gains,
    weight_in,
    conv_values,
    conv_states,
    scan_params,
    weight_mix,
    weight_feed,
    weight_down,
    in_lower,
    in_raise,
    mix_lower,
    mix_raise,
    feed_lower,
    feed_raise,
    down_lower,
    down_raise,
):
    cols = lax.axis_size("col")
    rows_axis = lax.axis_size("row")
    col = lax.axis_index("col")
    devices = cols * rows_axis
    rows = tokens_in.shape[0]
    model = tokens_in.shape[1]
    total = rows * cols
    units = QUERY_HEADS // cols
    channels = units * GATE_WIDTH
    peer = rows // devices
    lengths, adapters = sequence_lengths[0], sequence_adapter[0]
    sequences = lengths.shape[0]
    fast = quick(rows)
    key_head = col * units // (QUERY_HEADS // KEY_VALUE_HEADS)
    exchange = lambda values: lax.all_to_all(values, ALL_AXES, split_axis=0, concat_axis=0, tiled=True)

    sent, send_matrix = send_tokens(target, tokens_in, adapters, peer)
    shards = []

    def gather_weight(weight, lower, raised):
        top = jnp.concatenate([weight, lower], axis=1)
        if fast:
            bottom = pad_columns(raised, top.shape[1])
            shards.append(jnp.concatenate([top, bottom], axis=0))
            return (lax.all_gather(shards[-1], "row", axis=0),)
        wide = lax.all_gather(top, "row", axis=0, tiled=True)
        return wide, lax.all_gather(raised, "row", axis=0, tiled=True)

    depth = weight_in.shape[0]
    height = depth + in_raise.shape[0]
    given = after(jnp.concatenate([weight_in, in_raise], axis=0), send_matrix)
    gates, convs, queries, pairs, states, steps = unit_parts(given, units)
    pair_width, state_width = pairs.shape[1], states.shape[1]
    taps = jnp.concatenate([jnp.zeros((KCONV + 1, pair_width), BFLOAT), conv_states], axis=1)
    taps = jnp.pad(taps, ((0, 16 - KCONV - 1), (0, 0)))
    shared = jnp.concatenate([jnp.concatenate([pairs, states], axis=1), taps], axis=0)
    own_columns = jnp.concatenate([gates, convs, queries, pad_columns(steps, LANES)], axis=1)
    if fast:
        shared_shard = shared
        shared = lax.all_gather(shared_shard, "row", axis=0)
        weights_own = gather_weight(own_columns[:depth], in_lower, own_columns[depth:])
    arrived = exchange(sent)
    gains = jnp.broadcast_to(norm_gains.astype(FLOAT)[:, None, :], (2, 8, model))
    if fast:
        near, far = flip(shared, 1), flip(shared, 2)
        arrived = after(arrived, near, far, shards[0])
    own_input, place_matrix, *normed_one = arrive_tokens(arrived.reshape(rows, model + LANES), gains[0])
    blocks_one = gather_blocks(normed_one) if fast else normed_one
    if fast:
        held = jnp.zeros((cols,) + shared.shape, BFLOAT)
        for block, values in ((col, shared), (col ^ 1, near), (col ^ 2, far)):
            held = lax.dynamic_update_index_in_dim(held, values, block, 0)
        split = shared.shape[0] // 2
        corner = jnp.concatenate([flip(near[:split], 2), flip(far[split:], 1)], axis=0)
        held = lax.dynamic_update_index_in_dim(held, corner, col ^ 3, 0)
    else:
        held = lax.all_gather(shared, "col", axis=0)
    all_pairs = jnp.concatenate([held[at, ..., :height, :pair_width] for at in range(cols)], axis=-1)
    pick = lambda start: lax.select_n(
        key_head,
        *[all_pairs[..., start + at * HEAD_SIZE : start + (at + 1) * HEAD_SIZE] for at in range(KEY_VALUE_HEADS)],
    )
    shared_columns = jnp.concatenate(
        [held[at, ..., :height, pair_width:] for at in range(cols)]
        + [pick(0), pick(KEY_VALUE_HEADS * HEAD_SIZE)],
        axis=-1,
    )
    tap_rows = held[:, 0] if fast else held
    all_taps = jnp.concatenate(
        [tap_rows[at, height : height + KCONV + 1, pair_width:] for at in range(cols)], axis=1
    )
    if fast:
        weights_in = (shared_columns, *weights_own)
    else:
        columns = jnp.concatenate([shared_columns, own_columns], axis=1)
        weights_in = gather_weight(columns[:depth], in_lower, columns[depth:])
    weights_mix = gather_weight(
        after(split_halves(weight_mix, units, GATE_WIDTH, 0).T, sent),
        mix_raise.T,
        split_halves(mix_lower, units, GATE_WIDTH, 0).T,
    )
    weights_feed = gather_weight(
        after(split_halves(weight_feed, units, UNIT_FF, 1), arrived),
        feed_lower,
        split_halves(feed_raise, units, UNIT_FF, 1),
    )

    source_adapters = arrived.reshape(rows, model + LANES)[::peer, model + 1 : model + 1 + sequences].astype(jnp.int32)
    segment, position, selector = sequence_tables(lengths, adapters, total)
    own_selector = rows_of(selector, col, rows)
    own_segment = rows_of(segment, col, rows)
    tables = mixer_tables(lengths, segment, position, conv_values, all_taps, scan_params)

    def compact_grad(narrow, values):
        parts = [
            lax.dynamic_slice_in_dim(narrow, adapters[at] * RANK, RANK, 1)
            * (own_segment == at).astype(BFLOAT)[:, None]
            for at in range(sequences)
        ]
        grad = contract_first(jnp.concatenate(parts, axis=1), values).astype(BFLOAT)
        kept = sequences * RANK
        grad = grad.reshape(kept, devices, model // devices).transpose(1, 0, 2)
        return grad.reshape(devices, peer, kept * model // devices // peer)

    def expand_grad(dealt):
        kept = sequences * RANK
        dealt = dealt.reshape(devices * kept, model // devices)
        adapter_row = (source_adapters[:, :, None] * RANK + jnp.arange(RANK, dtype=jnp.int32)).reshape(-1)
        chosen = (jnp.arange(NADAPT * RANK, dtype=jnp.int32)[:, None] == adapter_row[None, :]).astype(BFLOAT)
        return product(chosen, dealt)

    def send_back(values, grads):
        back = contract_first(place_matrix, values).astype(BFLOAT).reshape(devices, peer, model)
        return exchange(jnp.concatenate([back, *grads], axis=2))

    def expand_packed(dealt, count):
        slots = dealt.shape[0] * peer
        block = jnp.arange(2 * LANES // (model // devices), dtype=jnp.int32)[:, None, None]
        row = jnp.arange(peer, dtype=jnp.int32)[None, None, :]
        place = block * peer + row
        adapter = jnp.where(place < RANK, source_adapters[None, :, 0:1], source_adapters[None, :, 1:2])
        adapter_row = (adapter * RANK + place % RANK).reshape(block.shape[0], 1, slots)
        chosen = (jnp.arange(NADAPT * RANK, dtype=jnp.int32)[None, :, None] == adapter_row).astype(BFLOAT)
        sums = product(chosen.reshape(-1, slots), dealt.reshape(slots, dealt.shape[2]))
        sums = sums.reshape(block.shape[0], NADAPT * RANK, dealt.shape[2])
        width = model // devices
        return [
            sum(
                sums[at, :, grad * 2 * LANES + at * width : grad * 2 * LANES + (at + 1) * width]
                for at in range(block.shape[0])
            )
            for grad in range(count)
        ]

    def take_back(dealt, count):
        returned = contract_first(send_matrix, dealt[:, :, :model].reshape(rows, model)).astype(BFLOAT)
        if fast:
            return returned, expand_packed(dealt[:, :, model:], count)
        width = (dealt.shape[2] - model) // count
        return returned, [
            expand_grad(dealt[:, :, model + at * width : model + (at + 1) * width]) for at in range(count)
        ]

    projected, inner_in = (spread_gathered if fast else spread_project)(blocks_one, weights_in, selector)

    sent_grad = product(send_matrix, cotangent).astype(BFLOAT).reshape(devices, peer, model)
    arrived_grad = exchange(after(sent_grad, normed_one[0])).reshape(rows, model)
    branch_two = product(place_matrix, arrived_grad).astype(BFLOAT)
    weights_down = gather_weight(after(weight_down.T, projected), down_raise.T, down_lower.T)

    mixed_out = attention_forward(projected, tables)
    mixed_out, scanned, carried = scan_forward(projected, tables, mixed_out)
    hidden, inner_out, *normed_two = collect_project(mixed_out, weights_mix, "forward", own_selector, own_input, gains[1])
    gate_up, inner_feed = spread_project(normed_two, weights_feed, selector)
    branch_halves = cut_halves(after(branch_two, projected))
    if fast:
        act_grad, narrow_two = spread_blocks(gather_blocks(branch_halves), weights_down, selector, None)
    else:
        act_grad, narrow_two = spread_project(branch_halves, weights_down, selector)
    half_feed = units * UNIT_FF
    gate_part, up_part = gate_up[:, :half_feed].astype(FLOAT), gate_up[:, half_feed:].astype(FLOAT)
    gate = jax.nn.sigmoid(gate_part)
    silu = gate_part * gate
    activated = (silu * up_part).astype(BFLOAT)
    wide_grad = act_grad.astype(FLOAT)
    feed_grad = jnp.concatenate(
        [wide_grad * up_part * (gate * (1.0 + gate_part * (1.0 - gate))), wide_grad * silu], axis=1
    ).astype(BFLOAT)
    choose = (
        jnp.arange(NADAPT * RANK, dtype=jnp.int32)[:, None]
        == (adapters[:, None] * RANK + jnp.arange(RANK, dtype=jnp.int32)[None, :]).reshape(1, -1)
    ).astype(BFLOAT)
    if fast:
        pieces = collect_pieces(after(activated, feed_grad), weights_down, True)
        kept, onward = collect_middle(collect_send(collect_pieces(feed_grad, weights_feed, False)))
        hidden_grad, narrow_three, left, right, early_grads = collect_end(
            kept,
            collect_onward(onward),
            "backward",
            weights_feed,
            own_selector,
            after(hidden, pieces[3][0]),
            branch_two,
            gains[1],
            choose,
            *normed_two,
            inner_out,
        )
        mixed_grad, narrow_one = spread_early((left, right), weights_mix, selector)
    else:
        hidden_grad, narrow_three, *branch_one = collect_project(
            feed_grad, weights_feed, "backward", own_selector, hidden, branch_two, gains[1]
        )
        mixed_grad, narrow_one = spread_project(branch_one, weights_mix, selector)

    if fast:
        near_parts = after_all((*pieces[0], pieces[1][0], pieces[2][1]), mixed_grad)
        started = collect_send(
            [near_parts[:2], (near_parts[2], pieces[1][1]), (pieces[2][0], near_parts[3]), pieces[3]], False
        )
        attended_grads = attention_backward(projected, tables, after(mixed_grad, near_parts[0]))
        kept, onward = collect_middle((*started[:5], after_all(started[5], attended_grads[1])))
        scan_inputs = (projected, tables, scanned, carried, after(mixed_grad, *onward), attended_grads)
        scan_part = list(scan_backward(*scan_inputs, 0, 2, None))
        payload = collect_end(
            kept,
            collect_onward(onward),
            "output",
            weights_down,
            own_selector,
            after(hidden, scan_part[2]),
            place_matrix,
            choose,
            branch_two,
            early_grads,
        )
        dealt_out = exchange(payload.reshape(devices, peer, -1))
        scan_part[2] = after(scan_part[2], payload)
        projected_grad = scan_backward(*scan_inputs, 1, 2, scan_part)[0]
        *pieces_in, raise_grad = collect_blocks([3, 1, 2, 0], projected_grad, weights_in, PIECE_TYPES, [inner_in])
        started_in = collect_send(pieces_in)
        kept_in, onward_in = collect_middle(started_in)
    else:
        block_out, inner_down = collect_project(activated, weights_down, "output", own_selector, hidden)
        attended_grads = attention_backward(projected, tables, mixed_grad)
        projected_grad = scan_backward(
            projected, tables, scanned, carried, mixed_grad, attended_grads, 0, 1, None
        )[0]
        dealt_out = send_back(
            block_out,
            [
                compact_grad(inner_down, branch_two),
                compact_grad(narrow_three, jnp.concatenate(normed_two, axis=1)),
                compact_grad(inner_out, jnp.concatenate(branch_one, axis=1)),
            ],
        )

    def sum_rows(values):
        return lax.psum_scatter(values.astype(BFLOAT), "row", scatter_dimension=0, tiled=True).astype(FLOAT)

    early_parts = [
        contract_first(narrow_one, mixed_out),
        contract_first(inner_feed, feed_grad),
        contract_first(narrow_two, activated),
    ]
    early = sum_rows(jnp.concatenate(early_parts, axis=1))

    late = sum_rows(raise_grad if fast else contract_first(inner_in, projected_grad))

    if fast:
        payload = collect_end(
            kept_in,
            collect_onward(onward_in),
            "input",
            weights_in,
            own_selector,
            own_input,
            after(hidden_grad, dealt_out),
            gains[0],
            choose,
            *normed_one,
            place_matrix,
        )
        dealt_grad = exchange(payload.reshape(devices, peer, -1))
    else:
        input_grad, narrow_four = collect_project(
            projected_grad, weights_in, "input", own_selector, own_input, hidden_grad, gains[0]
        )
        dealt_grad = send_back(input_grad, [compact_grad(narrow_four, jnp.concatenate(normed_one, axis=1))])
        payload = input_grad
    dealt_out, early, late = after_all((dealt_out, early, late), payload)
    early_cuts = [0, early_parts[0].shape[1]]
    early_cuts.append(early_cuts[1] + early_parts[1].shape[1])
    grad_mix_lower = join_halves(early[:, : early_cuts[1]], units, GATE_WIDTH, 1).T
    grad_feed_raise = join_halves(early[:, early_cuts[1] : early_cuts[2]], units, UNIT_FF, 1)
    grad_down_lower = early[:, early_cuts[2] :].T

    key_columns = late[:, STATES : STATES + HEAD_SIZE]
    value_columns = late[:, STATES + HEAD_SIZE : STATES + PAIR]
    mine = [(key_head == at).astype(FLOAT) for at in range(KEY_VALUE_HEADS)]
    pair_grad = jnp.concatenate([part * here for part in (key_columns, value_columns) for here in mine], axis=1)
    stacked = jnp.stack(
        [
            jnp.concatenate(
                [
                    pair_grad[:, at * pair_width : (at + 1) * pair_width],
                    late[:, at * state_width : (at + 1) * state_width],
                ],
                axis=1,
            )
            for at in range(cols)
        ]
    )
    if fast:
        piece = lambda mask: lax.dynamic_index_in_dim(stacked, col ^ mask, 0, False)
        shared_sum = piece(0) + flip(piece(1), 1) + flip(piece(2), 2) + flip(piece(3), 3)
    else:
        shared_sum = lax.psum_scatter(
            stacked.reshape(stacked.shape[0] * stacked.shape[1], -1), "col", scatter_dimension=0, tiled=True
        )
    late = jnp.concatenate([shared_sum, late[:, STATES + PAIR :]], axis=1)
    shared_width = pair_width + state_width
    cuts = [shared_width]
    for width in (channels, channels, units * HEAD_SIZE, units * STEP_WIDTH):
        cuts.append(cuts[-1] + width)
    gate_columns, conv_columns, query_columns, step_columns = [
        late[:, low:high] for low, high in zip(cuts[:-1], cuts[1:])
    ]
    grad_in_raise = restore_units(
        [
            gate_columns,
            conv_columns,
            query_columns,
            late[:, :pair_width],
            late[:, pair_width:shared_width],
            step_columns,
        ],
        units,
    )

    returned_out, (grad_down_raise, grad_feed_lower, grad_mix_raise) = take_back(dealt_out, 3)
    returned_grad, (grad_in_lower,) = take_back(dealt_grad, 1)
    return (
        returned_out,
        returned_grad,
        grad_in_lower.T,
        grad_in_raise,
        grad_mix_lower,
        grad_mix_raise,
        grad_feed_lower.T,
        grad_feed_raise,
        grad_down_lower,
        grad_down_raise,
    )


def solution(mesh):
    in_specs = (
        P(("row", "col"), None),
        P(("row", "col"), None),
        P(("row", "col")),
        P("row", None),
        P("row", None),
        P(),
        P("row", "col"),
        P(None, "col"),
        P(None, "col"),
        P(None, "col"),
        P("col", "row"),
        P("row", "col"),
        P("col", "row"),
        P("row", None),
        P("row", "col"),
        P("col", "row"),
        P(None, "row"),
        P("row", None),
        P("row", "col"),
        P("col", "row"),
        P(None, "row"),
    )
    out_specs = (
        P(("row", "col"), None),
        P(("row", "col"), None),
        P(("row", "col"), None),
        P("row", "col"),
        P("col", "row"),
        P(None, ("row", "col")),
        P(("row", "col"), None),
        P("row", "col"),
        P("col", "row"),
        P(None, ("row", "col")),
    )
    return jax.shard_map(local, mesh=mesh, in_specs=in_specs, out_specs=out_specs, check_vma=False)
```
